32 devices in a mesh: dp: 4 (over z), rows: 2 (over core), tensor: 4 (over y, x).
Axes of the slice: x: 2, y: 2, z: 4, core: 2. Of those that a mesh axis runs over, the one named last changes fastest.
Arguments:
- section_input: bfloat16 [4, 36, 24576], P('dp', 'rows', 'tensor'), may hold values from -6 to 6
- conv_weights: bfloat16 [6, 512, 4608], P(None, 'tensor'), may hold values from -0.09375 to 0.09375
- norm_gains: float32 [6, 512], P(None, 'tensor'), may hold values from 0.25 to 1.75
- norm_shifts: float32 [6, 512], P(None, 'tensor'), may hold values from -0.5 to 0.5
- out_grad: bfloat16 [4, 36, 24576], P('dp', 'rows', 'tensor'), may hold values from -6 to 6
- out_mask: int32 [4, 36, 48], P('dp', 'rows'), may hold values from 0 to 1, as said below
Outputs:
- section_output: bfloat16 [4, 36, 24576], P('dp', 'rows', 'tensor')
- input_grad: float32 [4, 36, 24576], P('dp', 'rows', 'tensor')
- conv_grads: float32 [6, 512, 4608], P(None, 'tensor')
- gain_grads: float32 [6, 512], P(None, 'tensor')
- shift_grads: float32 [6, 512], P(None, 'tensor')
The draws below stay inside these ranges and needn't reach their ends.
Inputs may be any that keep to these rules, and one draw needn't show every extreme that they name: `out_mask`: 0 or 1; the share of ones differs from image to image, one of 1, 1/2, 1/4 or 1/8 in law.
All inputs are finite; a program needn't handle non-finite values.
Results may differ from the reference program's by a relative error of at most 0.034.
Values may be sent and summed in bfloat16 or wider, within the bound.
No kernel may reach another device: no remote copies, remote signals or barrier semaphores. Data moves between devices by JAX's collectives and lax.ppermute only.
A program may use at most 128 MiB of HBM per device.

```python
import jax
import jax.numpy as jnp
from jax import lax

C = 512
HEIGHT = 36
WIDTH = 48
LAYERS = 6
IMAGES = 4


def draw_out_mask(key, part):
    key = jax.random.fold_in(key, 7)
    key_level, key_bits = jax.random.split(key)
    level = jax.random.randint(key_level, (IMAGES, 1, 1), 0, 4)
    limit = jnp.right_shift(jnp.int32(1024), level)
    bits = jax.random.randint(key_bits, (IMAGES, HEIGHT, WIDTH), 0, 1024)
    return (bits < limit).astype(jnp.int32)


def block_levels(rng, extent, cuts, low, high):
    def one(position, blocks):
        draws = jax.random.uniform(jax.random.fold_in(jax.random.fold_in(rng, 6), position), (blocks,), jnp.float32, low / len(cuts), high / len(cuts))
        return jnp.repeat(jnp.exp(draws), extent[position] // blocks).reshape((-1,) + (1,) * (len(extent) - position - 1))

    loudness = one(*cuts[0])
    for cut in cuts[1:]:
        loudness = loudness * one(*cut)
    return loudness


def bell_draw(rng, dims, scale, most, cuts=(), held_as=jnp.bfloat16):
    values = jax.random.normal(rng, dims, jnp.float32) * scale
    if len(cuts) > 0:
        values = block_levels(rng, dims, cuts, -0.22, 0.18) * values
    return jnp.clip(values, min=-most, max=most).astype(held_as)


def setup_inputs(seed: int = 0) -> dict:
    key_of = jax.random.split(jax.random.key(seed), 7)
    section_input = bell_draw(key_of[0], (IMAGES, HEIGHT, C * WIDTH), 1.0, 6.0, ((0, 4), (1, 2), (2, 4)))
    conv_weights = bell_draw(key_of[1], (LAYERS, C, 9 * C), (9 * C) ** -0.5, 0.09375, ((1, 4),))
    norm_gains = jnp.clip(1.0 + 0.15 * jax.random.normal(key_of[2], (LAYERS, C), jnp.float32), 0.25, 1.75)
    norm_shifts = jnp.clip(jax.random.uniform(key_of[3], (LAYERS, C), jnp.float32, -0.5, 0.5) * block_levels(key_of[3], (LAYERS, C), ((1, 4),), -0.4, 0.0), -0.5, 0.5)
    out_grad = bell_draw(key_of[4], (IMAGES, HEIGHT, C * WIDTH), 1.0, 6.0, ((0, 4), (1, 2), (2, 4)))
    out_mask = draw_out_mask(jax.random.fold_in(key_of[6], 71), 0)
    return {"section_input": section_input, "conv_weights": conv_weights, "norm_gains": norm_gains, "norm_shifts": norm_shifts, "out_grad": out_grad, "out_mask": out_mask}


@jax.custom_vjp
def low(v):
    return lax.optimization_barrier(v.astype(jnp.bfloat16)).astype(jnp.float32)

@jax.custom_vjp
def low_back(v):
    return v

def low_keep(v):
    return (low(v), None)

def low_pass(kept, grad):
    return (grad,)

def back_keep(v):
    return (v, None)

def back_low(kept, grad):
    return (low(grad),)
low.defvjp(low_keep, low_pass)
low_back.defvjp(back_keep, back_low)
EPS = 1e-05

def to_maps(flat):
    count, high, merged = flat.shape
    return flat.reshape(count, high, merged // WIDTH, WIDTH).transpose(0, 1, 3, 2)

def from_maps(maps):
    count, high, wide, chans = maps.shape
    return maps.transpose(0, 1, 3, 2).reshape(count, high, chans * wide)

def convolve(image, kernel):
    return lax.conv_general_dilated(image, kernel, (1, 1), ((1, 1), (1, 1)), dimension_numbers=('NHWC', 'HWIO', 'NHWC'), precision=lax.Precision.HIGHEST)

def pool_unpool(values):
    count, high, wide, chans = values.shape
    blocks = values.reshape(count, high // 2, 2, wide // 2, 2, chans)
    pooled = jax.nn.logsumexp(blocks, axis=(2, 4), keepdims=True)
    return (jnp.exp(blocks - pooled) * pooled).reshape(values.shape)

def layer(hidden, kernel, gain, shift):
    conv_out = low_back(convolve(low(hidden), kernel))
    mean = lax.optimization_barrier(jnp.mean(conv_out, axis=(0, 1, 2)))
    var = lax.optimization_barrier(jnp.mean(jnp.square(conv_out - mean), axis=(0, 1, 2)))
    normed = (conv_out - mean) * lax.rsqrt(var + EPS) * gain + shift
    return jax.nn.silu(normed)

def section(inputs, kernels, gains, shifts):
    hidden = inputs
    for index in range(LAYERS):
        if index == LAYERS // 2:
            hidden = pool_unpool(hidden)
        hidden = layer(hidden, kernels[index], gains[index], shifts[index])
    return hidden

def reference(section_input, conv_weights, norm_gains, norm_shifts, out_grad, out_mask):
    inputs = to_maps(section_input.astype(jnp.float32))
    kernels = conv_weights.astype(jnp.float32).reshape(LAYERS, C, 3, 3, C).transpose(0, 2, 3, 4, 1)
    result, pull = jax.vjp(section, inputs, kernels, norm_gains, norm_shifts)
    cotangent = to_maps(out_grad.astype(jnp.float32)) * out_mask[..., None].astype(jnp.float32)
    d_input, d_kernels, d_gains, d_shifts = pull(cotangent)
    flat_kernels = d_kernels.transpose(0, 4, 1, 2, 3).reshape(LAYERS, C, 9 * C)
    return (from_maps(result).astype(jnp.bfloat16), from_maps(d_input), flat_kernels, d_gains, d_shifts)
```

```python
import functools

import jax
import jax.numpy as jnp
from jax import lax
from jax.experimental import pallas as pl
from jax.experimental.pallas import tpu as pltpu
from jax.sharding import PartitionSpec as P

EPS = 1e-05


def padded_2(cells, sides, width):
    for axis, dim in sides:
        count = lax.axis_size(axis)
        ends = count - 1
        head = lax.slice_in_dim(cells, 0, width, axis=dim)
        tail = lax.slice_in_dim(cells, cells.shape[dim] - width, cells.shape[dim], axis=dim)
        cells = jnp.concatenate(
            [
                lax.ppermute(tail, axis, [(i, (i + 1) % count) for i in range(ends)]),
                cells,
                lax.ppermute(head, axis, [((i + 1) % count, i) for i in range(ends)]),
            ],
            axis=dim,
        )
    return cells


def to_maps(flat, width):
    count, high, merged = flat.shape
    return flat.reshape(count, high, merged // width, width).transpose(0, 1, 3, 2)


def from_maps(maps):
    count, high, wide, chans = maps.shape
    return maps.transpose(0, 1, 3, 2).reshape(count, high, chans * wide)


def spatial_conv(padded, kernel):
    return lax.conv_general_dilated(
        padded,
        kernel,
        (1, 1),
        ((0, 0), (1, 1)),
        dimension_numbers=("NHWC", "HWIO", "NHWC"),
        preferred_element_type=jnp.float32,
    )


def flipped(kernel):
    return jnp.transpose(kernel[::-1, ::-1], (0, 1, 3, 2))


def pool_unpool(values):
    count, high, wide, chans = values.shape
    blocks = values.reshape(count, high // 2, 2, wide // 2, 2, chans)
    pooled = jax.nn.logsumexp(blocks, axis=(2, 4), keepdims=True)
    return (jnp.exp(blocks - pooled) * pooled).reshape(values.shape)


def moments(conv_out, total_pixels):
    summed = lax.psum(jnp.sum(conv_out, axis=(0, 1, 2)), ("dp", "rows"))
    mean = summed / total_pixels
    spread = lax.psum(jnp.sum(jnp.square(conv_out - mean), axis=(0, 1, 2)), ("dp", "rows"))
    var = spread / total_pixels
    return (mean, lax.rsqrt(var + EPS))


def kernel_grad(whole, dconv):
    images, rows_here, width, chans = dconv.shape
    widened = jnp.pad(whole, ((0, 0), (0, 0), (1, 1), (0, 0)))
    stacked = []
    for row_off in range(3):
        line = []
        for col_off in range(3):
            window = widened[:, row_off : row_off + rows_here, col_off : col_off + width, :]
            line.append(
                jnp.einsum("bhwc,bhwo->co", window, dconv, preferred_element_type=jnp.float32)
            )
        stacked.append(jnp.stack(line))
    return jnp.stack(stacked)


def generic_local(section_input, conv_weights, norm_gains, norm_shifts, out_grad, out_mask):
    width = out_mask.shape[2]
    images, rows_here = (out_mask.shape[0], out_mask.shape[1])
    total_pixels = float(images * rows_here * width * lax.axis_size("dp") * lax.axis_size("rows"))
    layers, out_here, flat_in = conv_weights.shape
    chans_in = flat_in // 9
    kernels_hwio = conv_weights.reshape(layers, out_here, 3, 3, chans_in).transpose(0, 2, 3, 4, 1)
    middle = layers // 2
    kept = []
    acting = to_maps(section_input, width)
    current = acting.astype(jnp.float32)
    pre_pool = current
    for index in range(layers):
        if index == middle:
            pre_pool = current
            acting = pool_unpool(pre_pool).astype(jnp.bfloat16)
        padded = padded_2(acting, (("rows", 1),), 1)
        whole = lax.all_gather(padded, "tensor", axis=3, tiled=True)
        conv_out = spatial_conv(whole, kernels_hwio[index])
        mean, rstd = moments(conv_out, total_pixels)
        normed = (conv_out - mean) * rstd
        shifted = normed * norm_gains[index] + norm_shifts[index]
        current = jax.nn.silu(shifted)
        acting = current.astype(jnp.bfloat16)
        kept.append((whole, normed, shifted, rstd))
    grad = to_maps(out_grad, width).astype(jnp.float32) * out_mask[..., None].astype(jnp.float32)
    kernel_list = [None] * layers
    gain_list = [None] * layers
    shift_list = [None] * layers
    for index in range(layers - 1, -1, -1):
        whole, normed, shifted, rstd = kept[index]
        unused, pull_silu = jax.vjp(jax.nn.silu, shifted)
        dshift = pull_silu(grad)[0]
        gain_sum, shift_sum = lax.psum(
            (jnp.sum(dshift * normed, axis=(0, 1, 2)), jnp.sum(dshift, axis=(0, 1, 2))),
            ("dp", "rows"),
        )
        gain_list[index] = gain_sum
        shift_list[index] = shift_sum
        dconv = (
            norm_gains[index]
            * rstd
            * (dshift - shift_sum / total_pixels - normed * gain_sum / total_pixels)
        ).astype(jnp.bfloat16)
        summed_kernel = lax.psum(
            kernel_grad(whole, dconv).astype(jnp.bfloat16), ("dp", "rows")
        ).astype(jnp.float32)
        kernel_list[index] = summed_kernel.transpose(3, 0, 1, 2).reshape(out_here, flat_in)
        grad_rim = padded_2(dconv, (("rows", 1),), 1)
        partial_terms = spatial_conv(grad_rim, flipped(kernels_hwio[index]))
        grad_in = lax.psum_scatter(
            partial_terms.astype(jnp.bfloat16), "tensor", scatter_dimension=3, tiled=True
        ).astype(jnp.float32)
        if index == middle:
            unused, pull_pool = jax.vjp(pool_unpool, pre_pool)
            grad = pull_pool(grad_in)[0]
        else:
            grad = grad_in
    return (
        from_maps(acting),
        from_maps(grad),
        jnp.stack(kernel_list),
        jnp.stack(gain_list),
        jnp.stack(shift_list),
    )


GROUPS = 4
LANES = 128
WIDE = 48
CHANS = GROUPS * LANES
F32 = jnp.float32
BF16 = jnp.bfloat16
VMEM = pl.BlockSpec(memory_space=pltpu.VMEM)
SMEM = pl.BlockSpec(memory_space=pltpu.SMEM)
ANY = pl.BlockSpec(memory_space=pl.ANY)
PARAMS = pltpu.CompilerParams(vmem_limit_bytes=24 * 1024 * 1024)


def fits_kernels(mesh):
    return mesh.shape["tensor"] == GROUPS and mesh.shape["rows"] == 2


def sigmoid(v):
    return 0.5 * jnp.tanh(0.5 * v) + 0.5


def swap_columns(v):
    column = lax.broadcasted_iota(jnp.int32, v.shape, 0)
    return jnp.where(column % 2 == 0, pltpu.roll(v, WIDE - 1, 0), pltpu.roll(v, 1, 0))


def soft_parts(h):
    top = jnp.maximum(h[0], h[1])
    top = jnp.maximum(top, swap_columns(top))
    e0, e1 = jnp.exp(h[0] - top), jnp.exp(h[1] - top)
    total = e0 + e1
    total = total + swap_columns(total)
    pooled = top + jnp.log(total)
    inverse = 1.0 / total
    return e0 * inverse, e1 * inverse, pooled


def soft(h):
    h = h.reshape(2, WIDE, LANES)
    q0, q1, pooled = soft_parts(h)
    return jnp.concatenate([q0 * pooled, q1 * pooled], axis=0)


def soft_pull(h, grad):
    h = h.reshape(2, WIDE, LANES)
    grad = grad.reshape(2, WIDE, LANES)
    q0, q1, pooled = soft_parts(h)
    mix = q0 * grad[0] + q1 * grad[1]
    mix = mix + swap_columns(mix)
    return jnp.concatenate(
        [q0 * (pooled * (grad[0] - mix) + mix), q1 * (pooled * (grad[1] - mix) + mix)], axis=0
    )


def norm_tables(st_ref, i_own, i_oth, n_local, total):
    groups = st_ref.shape[0]
    blocks = [st_ref[i] for i in range(groups)]
    summed = functools.reduce(jnp.add, blocks)
    mean = summed / groups
    apart = functools.reduce(jnp.add, [jnp.square(b - mean) for b in blocks])
    var = (pltpu.roll(summed, 7, 0) + n_local * apart) / total
    rstd = lax.rsqrt(var + EPS)
    own = (st_ref[i_own] - mean) * rstd
    oth = (st_ref[i_oth] - mean) * rstd
    return rstd, own, oth


def left_right(y0, y1, y2):
    rows = y0.shape[0]
    column = lax.broadcasted_iota(jnp.int32, y0.shape, 0) % WIDE
    before = jnp.where(column == 0, 0.0, pltpu.roll(y0, 1, 0))
    after = jnp.where(column == WIDE - 1, 0.0, pltpu.roll(y2, rows - 1, 0))
    return before + y1 + after


def lane_of(group):
    return pl.multiple_of(group * LANES, LANES)


def fwd_kernel(first, pool, layer, total, *refs):
    if first:
        pos, z0, z1, z2, z3, halo, w_hbm, hb, zc_out, st_out, w, y, z, tab, hs, sem = refs
    else:
        pos, z0, z1, z2, z3, halo, st, gain, shift, w_hbm, hb, zc_out, st_out, w, y, z, tab, hs, sem = refs
    zs = (z0, z1, z2, z3)
    load = pltpu.make_async_copy(w_hbm.at[layer], w, sem)
    load.start()
    t, r, i_own, i_oth = pos[0], pos[1], pos[2], pos[3]
    n_own = z0.shape[0]
    halo_at = pl.multiple_of((1 - r) * (n_own + WIDE), WIDE)
    zero_at = pl.multiple_of(r * (n_own + WIDE), WIDE)
    hb[pl.ds(zero_at, WIDE), :] = jnp.zeros((WIDE, CHANS), BF16)
    edge = halo.shape[0] // GROUPS
    if not first:
        rstd, own, oth = norm_tables(st, i_own, i_oth, float(n_own), total)
        tab[0] = rstd * gain[...]
        tab[1] = own * gain[...] + shift[...]
        tab[2] = oth * gain[...] + shift[...]

    def act(values, k, which):
        if first:
            return values
        at = 2 * (t ^ k)
        n = values.astype(F32) * tab[0, pl.ds(at, 1), :] + tab[which, pl.ds(at, 1), :]
        h = n * sigmoid(n)
        return soft(h) if pool else h

    def body(j, carry):
        at = pl.multiple_of(j * 2 * WIDE, 2 * WIDE)
        for k in range(GROUPS):
            h = act(zs[k][pl.ds(at, 2 * WIDE), :], k, 1)
            hb[pl.ds(pl.multiple_of(at + WIDE, WIDE), 2 * WIDE), pl.ds(lane_of(t ^ k), LANES)] = h.astype(BF16)
        return carry

    lax.fori_loop(0, n_own // (2 * WIDE), body, 0)
    for k in range(GROUPS):
        h = act(halo[pl.ds(k * edge, edge), :], k, 2)
        if edge > WIDE:
            hs[...] = h
            h = hs[pl.ds(pl.multiple_of(r * WIDE, WIDE), WIDE), :]
        hb[pl.ds(halo_at, WIDE), pl.ds(lane_of(t ^ k), LANES)] = h.astype(BF16)
    load.wait()
    lhs = jnp.concatenate([hb[i * WIDE : i * WIDE + n_own, :] for i in range(3)], axis=1)
    rhs = jnp.concatenate(
        [
            jnp.concatenate([w[:, (3 * i + s) * CHANS : (3 * i + s + 1) * CHANS] for i in range(3)], axis=1)
            for s in range(3)
        ],
        axis=0,
    )
    y[...] = lax.dot_general(lhs, rhs, (((1,), (1,)), ((), ())), preferred_element_type=F32)

    def add_up(j, acc):
        at = pl.multiple_of(j * 2 * WIDE, 2 * WIDE)
        rows = pl.ds(at, 2 * WIDE)
        v = left_right(y[rows, 0:128], y[rows, 128:256], y[rows, 256:384])
        z[rows, :] = v
        return acc + jnp.sum(v.reshape(12, 8, LANES), axis=0)

    steps = n_own // (2 * WIDE)
    summed = lax.fori_loop(0, steps, add_up, jnp.zeros((8, LANES), F32))
    mean = jnp.sum(summed, axis=0, keepdims=True) / n_own

    def centre(j, acc):
        rows = pl.ds(pl.multiple_of(j * 2 * WIDE, 2 * WIDE), 2 * WIDE)
        v = z[rows, :] - mean
        zc_out[rows, :] = v.astype(BF16)
        return acc + jnp.sum(jnp.square(v).reshape(12, 8, LANES), axis=0)

    apart = lax.fori_loop(0, steps, centre, jnp.zeros((8, LANES), F32))
    st_out[...] = jnp.concatenate([mean, jnp.sum(apart, axis=0, keepdims=True)], axis=0)


def fwd_step(layer, pool, total, pos, slots, halo, norms, weights):
    n_own = slots[0].shape[0]
    first = norms is None
    extra = () if first else norms
    return pl.pallas_call(
        functools.partial(fwd_kernel, first, pool, layer, total),
        out_shape=(
            jax.ShapeDtypeStruct((n_own + 2 * WIDE, CHANS), BF16),
            jax.ShapeDtypeStruct((n_own, LANES), BF16),
            jax.ShapeDtypeStruct((2, LANES), F32),
        ),
        in_specs=[SMEM] + [VMEM] * (5 + len(extra)) + [ANY],
        out_specs=(VMEM, VMEM, VMEM),
        scratch_shapes=[
            pltpu.VMEM((LANES, 9 * CHANS), BF16),
            pltpu.VMEM((n_own, 3 * LANES), F32),
            pltpu.VMEM((n_own, LANES), F32),
            pltpu.VMEM((3, 8, LANES), F32),
            pltpu.VMEM((2 * WIDE, LANES), F32),
            pltpu.SemaphoreType.DMA,
        ],
        compiler_params=PARAMS,
        cost_estimate=pl.CostEstimate(
            flops=2 * n_own * 9 * CHANS * LANES, bytes_accessed=4 * 1024 * 1024, transcendentals=n_own * CHANS
        ),
        name="conv_forward",
    )(pos, *slots, halo, *extra, weights)


def below_sums(pos, zc, st, gain, shift, grad_ref, n_own, total, tab, emit):
    rstd, own, oth = norm_tables(st, pos[2], pos[3], float(n_own), total)
    tab[0], tab[1] = rstd, own
    tab[2], tab[3] = jnp.broadcast_to(gain[...], tab[2].shape), jnp.broadcast_to(shift[...], tab[3].shape)
    row = pl.ds(2 * pos[0], 1)

    def body(j, accs):
        rows = pl.ds(pl.multiple_of(j * 2 * WIDE, 2 * WIDE), 2 * WIDE)
        xhat = zc[rows, :].astype(F32) * tab[0, row, :] + tab[1, row, :]
        n = xhat * tab[2, row, :] + tab[3, row, :]
        sig = sigmoid(n)
        h = n * sig
        g = emit(rows, h, grad_ref[rows, :].astype(F32))
        dn = g * (sig * (1.0 + n - h))
        return (
            accs[0] + jnp.sum(dn.reshape(12, 8, LANES), axis=0),
            accs[1] + jnp.sum((dn * xhat).reshape(12, 8, LANES), axis=0),
        )

    zero = jnp.zeros((8, LANES), F32)
    sums = lax.fori_loop(0, n_own // (2 * WIDE), body, (zero, zero))
    return jnp.concatenate([jnp.sum(s, axis=0, keepdims=True) for s in sums], axis=0)


def top_kernel(total, pos, zc, st, gain, shift, grad, h_out, sums_out, tab):
    def emit(rows, h, g):
        h_out[rows, :] = h.astype(BF16)
        return g

    sums_out[...] = below_sums(pos, zc, st, gain, shift, grad, zc.shape[0], total, tab, emit)


def top_step(total, pos, zc, norms, grad):
    n_own = zc.shape[0]
    return pl.pallas_call(
        functools.partial(top_kernel, total),
        out_shape=(
            jax.ShapeDtypeStruct((n_own, LANES), BF16),
            jax.ShapeDtypeStruct((2, LANES), F32),
        ),
        in_specs=[SMEM] + [VMEM] * 5,
        out_specs=(VMEM, VMEM),
        scratch_shapes=[pltpu.VMEM((4, 8, LANES), F32)],
        compiler_params=PARAMS,
        name="top_sums",
    )(pos, zc, *norms, grad)


def bwd_kernel(last, pool, layer, total, *refs):
    pos, z0, z1, z2, z3, zhalo, st, gain, shift, g0, g1, g2, g3, ghalo, sums = refs[:15]
    rest = refs[15:]
    if last:
        w_hbms, (g_out, dz_out) = rest[:4], rest[4:6]
        dz, w, y, g, tab, tab2, sem = rest[6:]
    else:
        zb, stb, gainb, shiftb = rest[:4]
        w_hbms, (g_out, dz_out, sums_out) = rest[4:8], rest[8:11]
        dz, w, y, g, tab, tab2, sem = rest[11:]
    zs, gs = (z0, z1, z2, z3), (g0, g1, g2, g3)
    loads = [
        pltpu.make_async_copy(w_hbms[k].at[layer], w.at[pl.ds(k * LANES, LANES)], sem.at[k]) for k in range(GROUPS)
    ]
    for load in loads:
        load.start()
    t, r, i_own, i_oth = pos[0], pos[1], pos[2], pos[3]
    n_own = z0.shape[0]
    halo_at = pl.multiple_of((1 - r) * (n_own + WIDE), WIDE)
    zero_at = pl.multiple_of(r * (n_own + WIDE), WIDE)
    dz[pl.ds(zero_at, WIDE), :] = jnp.zeros((WIDE, CHANS), BF16)
    rstd, own, oth = norm_tables(st, i_own, i_oth, float(n_own), total)
    summed = functools.reduce(jnp.add, [sums[i] for i in range(sums.shape[0])]) / total
    scale = gain[...] * rstd
    tab[0], tab[1], tab[2] = rstd, own, oth
    tab[3], tab[4] = gain[...], shift[...]
    tab[5] = scale
    tab[6] = scale * summed
    tab[7] = scale * pltpu.roll(summed, 7, 0)

    def back(values, grad, k, which):
        at = pl.ds(2 * (t ^ k), 1)
        xhat = values.astype(F32) * tab[0, at, :] + tab[which, at, :]
        n = xhat * tab[3, at, :] + tab[4, at, :]
        sig = sigmoid(n)
        dn = grad.astype(F32) * (sig * (1.0 + n - n * sig))
        return (dn * tab[5, at, :] - tab[6, at, :] - xhat * tab[7, at, :]).astype(BF16)

    def body(j, carry):
        at = pl.multiple_of(j * 2 * WIDE, 2 * WIDE)
        rows = pl.ds(at, 2 * WIDE)
        for k in range(GROUPS):
            d = back(zs[k][rows, :], gs[k][rows, :], k, 1)
            dz[pl.ds(pl.multiple_of(at + WIDE, WIDE), 2 * WIDE), k * LANES : (k + 1) * LANES] = d
            if k == 0:
                dz_out[rows, :] = d
        return carry

    lax.fori_loop(0, n_own // (2 * WIDE), body, 0)
    zedge = zhalo.shape[0] // GROUPS
    for k in range(GROUPS):
        if zedge > WIDE:
            values = zhalo[pl.ds(pl.multiple_of(k * zedge + r * WIDE, WIDE), WIDE), :]
        else:
            values = zhalo[pl.ds(k * WIDE, WIDE), :]
        dz[pl.ds(halo_at, WIDE), k * LANES : (k + 1) * LANES] = back(values, ghalo[pl.ds(k * WIDE, WIDE), :], k, 2)
    for load in loads:
        load.wait()
    lhs = jnp.concatenate([dz[(2 - i) * WIDE : (2 - i) * WIDE + n_own, :] for i in range(3)], axis=1)
    rhs = jnp.concatenate([w[:, 384 * i : 384 * (i + 1)] for i in range(3)], axis=0)
    y[...] = jnp.dot(lhs, rhs, preferred_element_type=F32)

    def add_up(j, carry):
        rows = pl.ds(pl.multiple_of(j * 2 * WIDE, 2 * WIDE), 2 * WIDE)
        g[rows, :] = left_right(y[rows, 256:384], y[rows, 128:256], y[rows, 0:128])
        return carry

    if last:
        def finish(j, carry):
            rows = pl.ds(pl.multiple_of(j * 2 * WIDE, 2 * WIDE), 2 * WIDE)
            g_out[rows, :] = left_right(y[rows, 256:384], y[rows, 128:256], y[rows, 0:128])
            return carry

        lax.fori_loop(0, n_own // (2 * WIDE), finish, 0)
    else:
        lax.fori_loop(0, n_own // (2 * WIDE), add_up, 0)

        def emit(rows, h, grad):
            if pool:
                grad = soft_pull(h, grad)
            g_out[rows, :] = grad.astype(BF16)
            return grad

        sums_out[...] = below_sums(pos, zb, stb, gainb, shiftb, g, n_own, total, tab2, emit)


def bwd_step(layer, pool, total, pos, zslots, zhalo, norms, gslots, ghalo, sums, below, weights):
    n_own = zslots[0].shape[0]
    last = below is None
    extra = () if last else below
    out_shape = [
        jax.ShapeDtypeStruct((n_own, LANES), F32 if last else BF16),
        jax.ShapeDtypeStruct((n_own, LANES), BF16),
    ]
    if not last:
        out_shape.append(jax.ShapeDtypeStruct((2, LANES), F32))
    return pl.pallas_call(
        functools.partial(bwd_kernel, last, pool, layer, total),
        out_shape=tuple(out_shape),
        in_specs=[SMEM] + [VMEM] * (14 + len(extra)) + [ANY] * GROUPS,
        out_specs=(VMEM,) * len(out_shape),
        scratch_shapes=[
            pltpu.VMEM((n_own + 2 * WIDE, CHANS), BF16),
            pltpu.VMEM((CHANS, 9 * LANES), BF16),
            pltpu.VMEM((n_own, 3 * LANES), F32),
            pltpu.VMEM((n_own, LANES), F32),
            pltpu.VMEM((8, 8, LANES), F32),
            pltpu.VMEM((4, 8, LANES), F32),
            pltpu.SemaphoreType.DMA((GROUPS,)),
        ],
        compiler_params=PARAMS,
        cost_estimate=pl.CostEstimate(
            flops=2 * n_own * 9 * CHANS * LANES, bytes_accessed=4 * 1024 * 1024, transcendentals=n_own * CHANS
        ),
        name="conv_backward",
    )(pos, *zslots, zhalo, *norms, *gslots, ghalo, sums, *extra, *weights)


def wgrad_kernel(dz, hb, out, d):
    n_own = dz.shape[0]

    def body(j, carry):
        rows = pl.ds(pl.multiple_of(j * 2 * WIDE, 2 * WIDE), 2 * WIDE)
        v = dz[rows, :].astype(F32)
        column = lax.broadcasted_iota(jnp.int32, v.shape, 0) % WIDE
        ahead = jnp.where(column == WIDE - 1, 0.0, pltpu.roll(v, 2 * WIDE - 1, 0))
        behind = jnp.where(column == 0, 0.0, pltpu.roll(v, 1, 0))
        d[rows, 0:128] = ahead.astype(BF16)
        d[rows, 128:256] = v.astype(BF16)
        d[rows, 256:384] = behind.astype(BF16)
        return carry

    lax.fori_loop(0, n_own // (2 * WIDE), body, 0)
    lhs = d[...]
    for i in range(3):
        part = lax.dot_general(
            lhs, hb[i * WIDE : i * WIDE + n_own, :], (((0,), (0,)), ((), ())), preferred_element_type=F32
        ).astype(BF16)
        for s in range(3):
            out[:, (3 * i + s) * CHANS : (3 * i + s + 1) * CHANS] = part[s * LANES : (s + 1) * LANES]


def wgrad_step(dz, hb):
    n_own = dz.shape[0]
    return pl.pallas_call(
        wgrad_kernel,
        out_shape=jax.ShapeDtypeStruct((LANES, 9 * CHANS), BF16),
        in_specs=[VMEM] * 2,
        out_specs=VMEM,
        scratch_shapes=[pltpu.VMEM((n_own, 3 * LANES), BF16)],
        compiler_params=PARAMS,
        cost_estimate=pl.CostEstimate(
            flops=2 * n_own * 9 * CHANS * LANES, bytes_accessed=3 * 1024 * 1024, transcendentals=0
        ),
        name="kernel_gradient",
    )(dz, hb)


def turn_kernel(pos, w, o0, o1, o2, o3):
    for k, out in enumerate((o0, o1, o2, o3)):
        for i in range(9):
            at = pl.multiple_of(i * CHANS + (pos[0] ^ k) * LANES, LANES)
            out[0, :, i * LANES : (i + 1) * LANES] = w[0, :, pl.ds(at, LANES)]


def turn_step(pos, weights):
    layers = weights.shape[0]
    block = pl.BlockSpec((1, LANES, 9 * LANES), lambda i: (i, 0, 0))
    return pl.pallas_call(
        turn_kernel,
        grid=(layers,),
        out_shape=(jax.ShapeDtypeStruct((layers, LANES, 9 * LANES), BF16),) * GROUPS,
        in_specs=[SMEM, pl.BlockSpec((1, LANES, 9 * CHANS), lambda i: (i, 0, 0))],
        out_specs=(block,) * GROUPS,
        compiler_params=PARAMS,
        name="kernels_by_group",
    )(pos, weights)


def swap_with(value, k):
    return lax.ppermute(value, "tensor", [(i, i ^ k) for i in range(GROUPS)])


def spread(own):
    return [own] + [swap_with(own, k) for k in range(1, GROUPS)]


def edges(slots, half, rows):
    n_own = slots[0].shape[0]
    start = (1 - half) * (n_own - rows * WIDE)
    cut = jnp.concatenate([lax.dynamic_slice_in_dim(s, start, rows * WIDE, axis=0) for s in slots], axis=0)
    return lax.ppermute(cut, "rows", [(0, 1), (1, 0)])


def share_sums(sums):
    everywhere = lax.all_gather(sums.reshape(2 * LANES), ("dp", "rows", "tensor"), tiled=True)
    return everywhere.reshape(-1, 2 * GROUPS, LANES)


def fast_local(section_input, conv_weights, norm_gains, norm_shifts, out_grad, out_mask):
    images, rows_here, width = out_mask.shape
    layers = conv_weights.shape[0]
    n_own = rows_here * width
    parts = lax.axis_size("dp") * lax.axis_size("rows")
    total = float(n_own * parts)
    t, half, d = lax.axis_index("tensor"), lax.axis_index("rows"), lax.axis_index("dp")
    pos = jnp.stack([t, half, 2 * d + half, 2 * d + 1 - half]).astype(jnp.int32)
    middle = layers // 2
    x = to_maps(section_input, width).reshape(n_own, LANES)
    tables = lax.all_gather(jnp.stack([norm_gains, norm_shifts]), "tensor", axis=0)
    tables = jnp.repeat(tables.transpose(1, 2, 0, 3), 2, axis=2)
    gains, shifts = tables[0], tables[1]
    turned = turn_step(pos, conv_weights)
    turned = [turned[0]] + [swap_with(turned[k], k) for k in range(1, GROUPS)]
    top_grad = (
        to_maps(out_grad, width) * out_mask[..., None].astype(BF16)
    ).reshape(n_own, LANES)

    slots = spread(x)
    halo = edges(slots, half, 1)
    norms = None
    kept_h, kept_z, kept_norms = [], [], []
    for layer in range(layers):
        hb, zc, local_sums = fwd_step(layer, layer == middle, total, pos, slots, halo, norms, conv_weights)
        slots = spread(zc)
        norms = (share_sums(local_sums), gains[layer], shifts[layer])
        halo = edges(slots, half, 2 if layer + 1 == middle else 1)
        kept_h.append(hb)
        kept_z.append((slots, halo))
        kept_norms.append(norms)
    h_last, local_sums = top_step(total, pos, kept_z[-1][0][0], kept_norms[-1], top_grad)
    gslots = spread(top_grad)
    ghalo = edges(gslots, half, 1)
    kernel_list, sum_list = [None] * layers, [None] * layers
    done = None
    for layer in range(layers - 1, -1, -1):
        sums = share_sums(local_sums)
        sum_list[layer] = sums
        zslots, zhalo = kept_z[layer]
        below = None
        if layer > 0:
            below = (kept_z[layer - 1][0][0],) + kept_norms[layer - 1]
        outs = bwd_step(
            layer, layer == middle, total, pos, zslots, zhalo, kept_norms[layer], gslots, ghalo, sums, below, turned
        )
        grad, dz = outs[0], outs[1]
        if layer > 0:
            local_sums = outs[2]
            gslots = spread(grad)
            ghalo = edges(gslots, half, 1)
        kernel = wgrad_step(dz, kept_h[layer])
        if done is not None:
            kernel, done = lax.optimization_barrier((kernel, done))
        done = lax.psum(kernel, ("dp", "rows"))
        kernel_list[layer] = done
    sums = jnp.sum(jnp.stack(sum_list).reshape(layers, parts, GROUPS, 2, LANES), axis=1)
    sums = lax.dynamic_index_in_dim(sums, t, axis=1, keepdims=False)
    shape = (images, rows_here, width, LANES)
    return (
        from_maps(h_last.reshape(shape)),
        from_maps(grad.reshape(shape)),
        jnp.stack([k.astype(F32) for k in kernel_list]),
        sums[:, 1],
        sums[:, 0],
    )


def solution(mesh):
    in_specs = (
        P("dp", "rows", "tensor"),
        P(None, "tensor", None),
        P(None, "tensor"),
        P(None, "tensor"),
        P("dp", "rows", "tensor"),
        P("dp", "rows", None),
    )
    out_specs = (
        P("dp", "rows", "tensor"),
        P("dp", "rows", "tensor"),
        P(None, "tensor", None),
        P(None, "tensor"),
        P(None, "tensor"),
    )
    local = fast_local if fits_kernels(mesh) else generic_local
    return jax.shard_map(local, mesh=mesh, in_specs=in_specs, out_specs=out_specs, check_vma=False)
```

```python
import functools

import jax
import jax.numpy as jnp
from jax import lax
from jax.experimental import pallas as pl
from jax.experimental.pallas import tpu as pltpu
from jax.sharding import PartitionSpec as P

EPS = 1e-05


def padded_2(cells, sides, width):
    for axis, dim in sides:
        count = lax.axis_size(axis)
        ends = count - 1
        head = lax.slice_in_dim(cells, 0, width, axis=dim)
        tail = lax.slice_in_dim(cells, cells.shape[dim] - width, cells.shape[dim], axis=dim)
        cells = jnp.concatenate(
            [
                lax.ppermute(tail, axis, [(i, (i + 1) % count) for i in range(ends)]),
                cells,
                lax.ppermute(head, axis, [((i + 1) % count, i) for i in range(ends)]),
            ],
            axis=dim,
        )
    return cells


def to_maps(flat, width):
    count, high, merged = flat.shape
    return flat.reshape(count, high, merged // width, width).transpose(0, 1, 3, 2)


def from_maps(maps):
    count, high, wide, chans = maps.shape
    return maps.transpose(0, 1, 3, 2).reshape(count, high, chans * wide)


def spatial_conv(padded, kernel):
    return lax.conv_general_dilated(
        padded,
        kernel,
        (1, 1),
        ((0, 0), (1, 1)),
        dimension_numbers=("NHWC", "HWIO", "NHWC"),
        preferred_element_type=jnp.float32,
    )


def flipped(kernel):
    return jnp.transpose(kernel[::-1, ::-1], (0, 1, 3, 2))


def pool_unpool(values):
    count, high, wide, chans = values.shape
    blocks = values.reshape(count, high // 2, 2, wide // 2, 2, chans)
    pooled = jax.nn.logsumexp(blocks, axis=(2, 4), keepdims=True)
    return (jnp.exp(blocks - pooled) * pooled).reshape(values.shape)


def moments(conv_out, total_pixels):
    summed = lax.psum(jnp.sum(conv_out, axis=(0, 1, 2)), ("dp", "rows"))
    mean = summed / total_pixels
    spread = lax.psum(jnp.sum(jnp.square(conv_out - mean), axis=(0, 1, 2)), ("dp", "rows"))
    var = spread / total_pixels
    return (mean, lax.rsqrt(var + EPS))


def kernel_grad(whole, dconv):
    images, rows_here, width, chans = dconv.shape
    widened = jnp.pad(whole, ((0, 0), (0, 0), (1, 1), (0, 0)))
    stacked = []
    for row_off in range(3):
        line = []
        for col_off in range(3):
            window = widened[:, row_off : row_off + rows_here, col_off : col_off + width, :]
            line.append(
                jnp.einsum("bhwc,bhwo->co", window, dconv, preferred_element_type=jnp.float32)
            )
        stacked.append(jnp.stack(line))
    return jnp.stack(stacked)


def generic_local(section_input, conv_weights, norm_gains, norm_shifts, out_grad, out_mask):
    width = out_mask.shape[2]
    images, rows_here = (out_mask.shape[0], out_mask.shape[1])
    total_pixels = float(images * rows_here * width * lax.axis_size("dp") * lax.axis_size("rows"))
    layers, out_here, flat_in = conv_weights.shape
    chans_in = flat_in // 9
    kernels_hwio = conv_weights.reshape(layers, out_here, 3, 3, chans_in).transpose(0, 2, 3, 4, 1)
    middle = layers // 2
    kept = []
    acting = to_maps(section_input, width)
    current = acting.astype(jnp.float32)
    pre_pool = current
    for index in range(layers):
        if index == middle:
            pre_pool = current
            acting = pool_unpool(pre_pool).astype(jnp.bfloat16)
        padded = padded_2(acting, (("rows", 1),), 1)
        whole = lax.all_gather(padded, "tensor", axis=3, tiled=True)
        conv_out = spatial_conv(whole, kernels_hwio[index])
        mean, rstd = moments(conv_out, total_pixels)
        normed = (conv_out - mean) * rstd
        shifted = normed * norm_gains[index] + norm_shifts[index]
        current = jax.nn.silu(shifted)
        acting = current.astype(jnp.bfloat16)
        kept.append((whole, normed, shifted, rstd))
    grad = to_maps(out_grad, width).astype(jnp.float32) * out_mask[..., None].astype(jnp.float32)
    kernel_list = [None] * layers
    gain_list = [None] * layers
    shift_list = [None] * layers
    for index in range(layers - 1, -1, -1):
        whole, normed, shifted, rstd = kept[index]
        unused, pull_silu = jax.vjp(jax.nn.silu, shifted)
        dshift = pull_silu(grad)[0]
        gain_sum, shift_sum = lax.psum(
            (jnp.sum(dshift * normed, axis=(0, 1, 2)), jnp.sum(dshift, axis=(0, 1, 2))),
            ("dp", "rows"),
        )
        gain_list[index] = gain_sum
        shift_list[index] = shift_sum
        dconv = (
            norm_gains[index]
            * rstd
            * (dshift - shift_sum / total_pixels - normed * gain_sum / total_pixels)
        ).astype(jnp.bfloat16)
        summed_kernel = lax.psum(
            kernel_grad(whole, dconv).astype(jnp.bfloat16), ("dp", "rows")
        ).astype(jnp.float32)
        kernel_list[index] = summed_kernel.transpose(3, 0, 1, 2).reshape(out_here, flat_in)
        grad_rim = padded_2(dconv, (("rows", 1),), 1)
        partial_terms = spatial_conv(grad_rim, flipped(kernels_hwio[index]))
        grad_in = lax.psum_scatter(
            partial_terms.astype(jnp.bfloat16), "tensor", scatter_dimension=3, tiled=True
        ).astype(jnp.float32)
        if index == middle:
            unused, pull_pool = jax.vjp(pool_unpool, pre_pool)
            grad = pull_pool(grad_in)[0]
        else:
            grad = grad_in
    return (
        from_maps(acting),
        from_maps(grad),
        jnp.stack(kernel_list),
        jnp.stack(gain_list),
        jnp.stack(shift_list),
    )


GROUPS = 4
LANES = 128
WIDE = 48
CHANS = GROUPS * LANES
F32 = jnp.float32
BF16 = jnp.bfloat16
VMEM = pl.BlockSpec(memory_space=pltpu.VMEM)
SMEM = pl.BlockSpec(memory_space=pltpu.SMEM)
ANY = pl.BlockSpec(memory_space=pl.ANY)
PARAMS = pltpu.CompilerParams(vmem_limit_bytes=24 * 1024 * 1024)


def fits_kernels(mesh):
    return mesh.shape["tensor"] == GROUPS and mesh.shape["rows"] == 2 and mesh.shape["dp"] == 4


def sigmoid(v):
    return 0.5 * jnp.tanh(0.5 * v) + 0.5


def swap_columns(v):
    column = lax.broadcasted_iota(jnp.int32, v.shape, 0)
    return jnp.where(column % 2 == 0, pltpu.roll(v, WIDE - 1, 0), pltpu.roll(v, 1, 0))


def soft_parts(h):
    top = jnp.maximum(h[0], h[1])
    top = jnp.maximum(top, swap_columns(top))
    e0, e1 = jnp.exp(h[0] - top), jnp.exp(h[1] - top)
    total = e0 + e1
    total = total + swap_columns(total)
    pooled = top + jnp.log(total)
    inverse = 1.0 / total
    return e0 * inverse, e1 * inverse, pooled


def soft(h):
    h = h.reshape(2, WIDE, LANES)
    q0, q1, pooled = soft_parts(h)
    return jnp.concatenate([q0 * pooled, q1 * pooled], axis=0)


def soft_pull(h, grad):
    h = h.reshape(2, WIDE, LANES)
    grad = grad.reshape(2, WIDE, LANES)
    q0, q1, pooled = soft_parts(h)
    mix = q0 * grad[0] + q1 * grad[1]
    mix = mix + swap_columns(mix)
    return jnp.concatenate(
        [q0 * (pooled * (grad[0] - mix) + mix), q1 * (pooled * (grad[1] - mix) + mix)], axis=0
    )


def norm_tables(st_ref, n_local, total):
    st = st_ref[...]
    row = lax.broadcasted_iota(jnp.int32, st.shape, 0) % 8
    is_mean = (row == 0) | (row == 2)
    parts = st.shape[0] // 4
    mean = jnp.sum(jnp.where(is_mean, st, 0.0), axis=0, keepdims=True) / parts
    inside = jnp.sum(jnp.where(is_mean, 0.0, st), axis=0, keepdims=True)
    apart = jnp.sum(jnp.where(is_mean, jnp.square(st - mean), 0.0), axis=0, keepdims=True)
    rstd = lax.rsqrt((inside + n_local * apart) / total + EPS)
    return rstd, (st_ref[0:1, :] - mean) * rstd, (st_ref[2:3, :] - mean) * rstd


def grad_tables(sums_ref):
    sums = sums_ref[...]
    row = lax.broadcasted_iota(jnp.int32, sums.shape, 0) % 2
    first = jnp.sum(jnp.where(row == 0, sums, 0.0), axis=0, keepdims=True)
    second = jnp.sum(jnp.where(row == 1, sums, 0.0), axis=0, keepdims=True)
    return first, second


def left_right(y0, y1, y2):
    rows = y0.shape[0]
    column = lax.broadcasted_iota(jnp.int32, y0.shape, 0) % WIDE
    before = jnp.where(column == 0, 0.0, pltpu.roll(y0, 1, 0))
    after = jnp.where(column == WIDE - 1, 0.0, pltpu.roll(y2, rows - 1, 0))
    return before + y1 + after


def lane_of(group):
    return pl.multiple_of(group * LANES, LANES)


def write_message(msg, own, sums, edge, half):
    n_own = own.shape[0]
    start = pl.multiple_of((1 - half) * (n_own - edge), WIDE)
    msg[0:edge, :] = own[pl.ds(start, edge), :].astype(F32)
    msg[edge : edge + 8, :] = jnp.concatenate([sums, jnp.zeros((6, LANES), F32)], axis=0)


def fwd_kernel(first, pool, layer, total, edge_out, *refs):
    if first:
        pos, z0, z1, z2, z3, w_hbm = refs[:6]
        rest = refs[6:]
    else:
        pos, z0, z1, z2, z3, st0, st1, st2, st3, gs0, gs1, gs2, gs3, w_hbm = refs[:14]
        sts, gss = (st0, st1, st2, st3), (gs0, gs1, gs2, gs3)
        rest = refs[14:]
    hb_out, zc_out, msg, hb, w, y, z, tab, hs, sem = rest
    zs = (z0, z1, z2, z3)
    load = pltpu.make_async_copy(w_hbm.at[layer], w, sem.at[0])
    load.start()
    save = pltpu.make_async_copy(hb, hb_out, sem.at[1])
    t, r = pos[0], pos[1]
    n_own = z.shape[0]
    edge = z0.shape[0] - n_own
    halo_at = pl.multiple_of((1 - r) * (n_own + WIDE), WIDE)
    zero_at = pl.multiple_of(r * (n_own + WIDE), WIDE)
    hb[pl.ds(zero_at, WIDE), :] = jnp.zeros((WIDE, CHANS), BF16)
    if not first:
        for k in range(GROUPS):
            rstd, own, oth = norm_tables(sts[k], float(n_own), total)
            gain, shift = gss[k][layer - 1 : layer, :], gss[k][layer + 7 : layer + 8, :]
            tab[k, 0:1] = rstd * gain
            tab[k, 1:2] = own * gain + shift
            tab[k, 2:3] = oth * gain + shift

    def act(values, k, which):
        if first:
            return values
        n = values.astype(F32) * tab[k, 0:1, :] + tab[k, which : which + 1, :]
        h = n * sigmoid(n)
        return soft(h) if pool else h

    def body(j, carry):
        at = pl.multiple_of(j * 2 * WIDE, 2 * WIDE)
        for k in range(GROUPS):
            h = act(zs[k][pl.ds(at, 2 * WIDE), :], k, 1)
            hb[pl.ds(pl.multiple_of(at + WIDE, WIDE), 2 * WIDE), pl.ds(lane_of(t ^ k), LANES)] = h.astype(BF16)
        return carry

    lax.fori_loop(0, n_own // (2 * WIDE), body, 0)
    for k in range(GROUPS):
        h = act(zs[k][n_own : n_own + edge, :], k, 2)
        if edge > WIDE:
            hs[...] = h
            h = hs[pl.ds(pl.multiple_of(r * WIDE, WIDE), WIDE), :]
        hb[pl.ds(halo_at, WIDE), pl.ds(lane_of(t ^ k), LANES)] = h.astype(BF16)
    save.start()
    load.wait()
    lhs = jnp.concatenate([hb[i * WIDE : i * WIDE + n_own, :] for i in range(3)], axis=1)
    rhs = jnp.concatenate(
        [
            jnp.concatenate([w[:, (3 * i + s) * CHANS : (3 * i + s + 1) * CHANS] for i in range(3)], axis=1)
            for s in range(3)
        ],
        axis=0,
    )
    y[...] = lax.dot_general(lhs, rhs, (((1,), (1,)), ((), ())), preferred_element_type=F32)

    def add_up(j, acc):
        at = pl.multiple_of(j * 2 * WIDE, 2 * WIDE)
        rows = pl.ds(at, 2 * WIDE)
        v = left_right(y[rows, 0:128], y[rows, 128:256], y[rows, 256:384])
        z[rows, :] = v
        return acc + jnp.sum(v.reshape(12, 8, LANES), axis=0)

    steps = n_own // (2 * WIDE)
    summed = lax.fori_loop(0, steps, add_up, jnp.zeros((8, LANES), F32))
    mean = jnp.sum(summed, axis=0, keepdims=True) / n_own

    def centre(j, acc):
        rows = pl.ds(pl.multiple_of(j * 2 * WIDE, 2 * WIDE), 2 * WIDE)
        v = z[rows, :] - mean
        z[rows, :] = v
        zc_out[rows, :] = v.astype(BF16)
        return acc + jnp.sum(jnp.square(v).reshape(12, 8, LANES), axis=0)

    apart = lax.fori_loop(0, steps, centre, jnp.zeros((8, LANES), F32))
    write_message(msg, z, jnp.concatenate([mean, jnp.sum(apart, axis=0, keepdims=True)], axis=0), edge_out, r)
    save.wait()


def fwd_step(layer, pool, edge_out, total, pos, slots, stats, tables, weights, n_own):
    first = stats is None
    extra = () if first else (*stats, *tables)
    return pl.pallas_call(
        functools.partial(fwd_kernel, first, pool, layer, total, edge_out),
        out_shape=(
            jax.ShapeDtypeStruct((n_own + 2 * WIDE, CHANS), BF16),
            jax.ShapeDtypeStruct((n_own + edge_out, LANES), BF16),
            jax.ShapeDtypeStruct((edge_out + 8, LANES), F32),
        ),
        in_specs=[SMEM] + [VMEM] * (4 + len(extra)) + [ANY],
        out_specs=(ANY, VMEM, VMEM),
        scratch_shapes=[
            pltpu.VMEM((n_own + 2 * WIDE, CHANS), BF16),
            pltpu.VMEM((LANES, 9 * CHANS), BF16),
            pltpu.VMEM((n_own, 3 * LANES), F32),
            pltpu.VMEM((n_own, LANES), F32),
            pltpu.VMEM((GROUPS, 8, LANES), F32),
            pltpu.VMEM((2 * WIDE, LANES), F32),
            pltpu.SemaphoreType.DMA((2,)),
        ],
        compiler_params=PARAMS,
        cost_estimate=pl.CostEstimate(
            flops=2 * n_own * 9 * CHANS * LANES, bytes_accessed=4 * 1024 * 1024, transcendentals=n_own * CHANS
        ),
        name="conv_forward",
    )(pos, *slots, *extra, weights)


def below_sums(zc, st, gs, layer, grad_ref, n_own, total, tab, emit):
    rstd, own, oth = norm_tables(st, float(n_own), total)
    tab[0:1], tab[1:2] = rstd, own
    tab[2:3], tab[3:4] = gs[layer : layer + 1, :], gs[layer + 8 : layer + 9, :]

    def body(j, accs):
        rows = pl.ds(pl.multiple_of(j * 2 * WIDE, 2 * WIDE), 2 * WIDE)
        xhat = zc[rows, :].astype(F32) * tab[0:1, :] + tab[1:2, :]
        n = xhat * tab[2:3, :] + tab[3:4, :]
        sig = sigmoid(n)
        h = n * sig
        g = emit(rows, h, grad_ref[rows, :].astype(F32))
        dn = g * (sig * (1.0 + n - h))
        return (
            accs[0] + jnp.sum(dn.reshape(12, 8, LANES), axis=0),
            accs[1] + jnp.sum((dn * xhat).reshape(12, 8, LANES), axis=0),
        )

    zero = jnp.zeros((8, LANES), F32)
    sums = lax.fori_loop(0, n_own // (2 * WIDE), body, (zero, zero))
    return jnp.concatenate([jnp.sum(s, axis=0, keepdims=True) for s in sums], axis=0)


def top_kernel(layer, total, zc, st, gs, grad, h_out, msg, tab):
    def emit(rows, h, g):
        h_out[rows, :] = h.astype(BF16)
        return g

    sums = below_sums(zc, st, gs, layer, grad, h_out.shape[0], total, tab, emit)
    msg[...] = jnp.concatenate([sums, jnp.zeros((6, LANES), F32)], axis=0)


def top_step(layer, total, zc, st, gs, grad, n_own):
    return pl.pallas_call(
        functools.partial(top_kernel, layer, total),
        out_shape=(
            jax.ShapeDtypeStruct((n_own, LANES), BF16),
            jax.ShapeDtypeStruct((8, LANES), F32),
        ),
        in_specs=[VMEM] * 4,
        out_specs=(VMEM, VMEM),
        scratch_shapes=[pltpu.VMEM((8, LANES), F32)],
        compiler_params=PARAMS,
        name="top_sums",
    )(zc, st, gs, grad)


def bwd_kernel(last, pool, layer, total, *refs):
    pos = refs[0]
    zs, sts, gss, gs, sums = refs[1:5], refs[5:9], refs[9:13], refs[13:17], refs[17:21]
    rest = refs[21:]
    if last:
        w_hbms, (g_out, dz_out) = rest[:4], rest[4:6]
        dz, zv, w, y, g, tab, tab2, sem = rest[6:]
    else:
        zb, stb = rest[:2]
        w_hbms, (g_out, dz_out, msg) = rest[2:6], rest[6:9]
        dz, zv, w, y, g, tab, tab2, sem = rest[9:]
    n_own = dz_out.shape[0]
    edge = zv.shape[1] - n_own
    zloads = [pltpu.make_async_copy(zs[k], zv.at[k], sem.at[k]) for k in range(GROUPS)]
    loads = [
        pltpu.make_async_copy(w_hbms[k].at[layer], w.at[pl.ds(k * LANES, LANES)], sem.at[GROUPS + k])
        for k in range(GROUPS)
    ]
    for load in zloads + loads:
        load.start()
    r = pos[1]
    halo_at = pl.multiple_of((1 - r) * (n_own + WIDE), WIDE)
    zero_at = pl.multiple_of(r * (n_own + WIDE), WIDE)
    dz[pl.ds(zero_at, WIDE), :] = jnp.zeros((WIDE, CHANS), BF16)
    for k in range(GROUPS):
        rstd, own, oth = norm_tables(sts[k], float(n_own), total)
        shift_sum, gain_sum = grad_tables(sums[k])
        gain, shift = gss[k][layer : layer + 1, :], gss[k][layer + 8 : layer + 9, :]
        scale = gain * rstd
        tab[k, 0:1], tab[k, 1:2], tab[k, 2:3] = rstd, own, oth
        tab[k, 3:4], tab[k, 4:5], tab[k, 5:6] = gain, shift, scale
        tab[k, 6:7], tab[k, 7:8] = scale * shift_sum / total, scale * gain_sum / total

    def back(values, grad, k, which):
        xhat = values.astype(F32) * tab[k, 0:1, :] + tab[k, which : which + 1, :]
        n = xhat * tab[k, 3:4, :] + tab[k, 4:5, :]
        sig = sigmoid(n)
        dn = grad.astype(F32) * (sig * (1.0 + n - n * sig))
        return (dn * tab[k, 5:6, :] - tab[k, 6:7, :] - xhat * tab[k, 7:8, :]).astype(BF16)

    for k in range(GROUPS):
        zloads[k].wait()

        def body(j, carry):
            at = pl.multiple_of(j * 2 * WIDE, 2 * WIDE)
            rows = pl.ds(at, 2 * WIDE)
            d = back(zv[k, rows, :], gs[k][rows, :], k, 1)
            dz[pl.ds(pl.multiple_of(at + WIDE, WIDE), 2 * WIDE), k * LANES : (k + 1) * LANES] = d
            if k == 0:
                dz_out[rows, :] = d
            return carry

        lax.fori_loop(0, n_own // (2 * WIDE), body, 0)
        z_at = n_own if edge == WIDE else pl.multiple_of(n_own + r * WIDE, WIDE)
        dz[pl.ds(halo_at, WIDE), k * LANES : (k + 1) * LANES] = back(
            zv[k, pl.ds(z_at, WIDE), :], gs[k][n_own : n_own + WIDE, :], k, 2
        )
    for load in loads:
        load.wait()
    lhs = jnp.concatenate([dz[(2 - i) * WIDE : (2 - i) * WIDE + n_own, :] for i in range(3)], axis=1)
    rhs = jnp.concatenate([w[:, 384 * i : 384 * (i + 1)] for i in range(3)], axis=0)
    y[...] = jnp.dot(lhs, rhs, preferred_element_type=F32)

    def shifted(rows):
        return left_right(y[rows, 256:384], y[rows, 128:256], y[rows, 0:128])

    def add_up(j, carry):
        rows = pl.ds(pl.multiple_of(j * 2 * WIDE, 2 * WIDE), 2 * WIDE)
        out = g_out if last else g
        out[rows, :] = shifted(rows)
        return carry

    lax.fori_loop(0, n_own // (2 * WIDE), add_up, 0)
    if not last:

        def emit(rows, h, grad):
            if pool:
                grad = soft_pull(h, grad)
                g[rows, :] = grad
            g_out[rows, :] = grad.astype(BF16)
            return grad

        below = below_sums(zb, stb, gss[0], layer - 1, g, n_own, total, tab2, emit)
        write_message(msg, g, below, WIDE, r)


def bwd_step(layer, pool, total, pos, zslots, stats, tables, gslots, sums, below, weights, n_own):
    last = below is None
    extra = () if last else below
    if last:
        out_shape = [jax.ShapeDtypeStruct((n_own, LANES), F32), jax.ShapeDtypeStruct((n_own, LANES), BF16)]
    else:
        out_shape = [
            jax.ShapeDtypeStruct((n_own + WIDE, LANES), BF16),
            jax.ShapeDtypeStruct((n_own, LANES), BF16),
            jax.ShapeDtypeStruct((WIDE + 8, LANES), F32),
        ]
    return pl.pallas_call(
        functools.partial(bwd_kernel, last, pool, layer, total),
        out_shape=tuple(out_shape),
        in_specs=[SMEM] + [ANY] * 4 + [VMEM] * (16 + len(extra)) + [ANY] * GROUPS,
        out_specs=(VMEM,) * len(out_shape),
        scratch_shapes=[
            pltpu.VMEM((n_own + 2 * WIDE, CHANS), BF16),
            pltpu.VMEM((GROUPS,) + zslots[0].shape, BF16),
            pltpu.VMEM((CHANS, 9 * LANES), BF16),
            pltpu.VMEM((n_own, 3 * LANES), F32),
            pltpu.VMEM((n_own, LANES), F32),
            pltpu.VMEM((GROUPS, 8, LANES), F32),
            pltpu.VMEM((8, LANES), F32),
            pltpu.SemaphoreType.DMA((2 * GROUPS,)),
        ],
        compiler_params=PARAMS,
        cost_estimate=pl.CostEstimate(
            flops=2 * n_own * 9 * CHANS * LANES, bytes_accessed=4 * 1024 * 1024, transcendentals=n_own * CHANS
        ),
        name="conv_backward",
    )(pos, *zslots, *stats, *tables, *gslots, *sums, *extra, *weights)


def wgrad_kernel(dz, hb_hbm, out, d, hb, sem):
    n_own = dz.shape[0]
    load = pltpu.make_async_copy(hb_hbm, hb, sem)
    load.start()

    def body(j, carry):
        rows = pl.ds(pl.multiple_of(j * 2 * WIDE, 2 * WIDE), 2 * WIDE)
        v = dz[rows, :].astype(F32)
        column = lax.broadcasted_iota(jnp.int32, v.shape, 0) % WIDE
        ahead = jnp.where(column == WIDE - 1, 0.0, pltpu.roll(v, 2 * WIDE - 1, 0))
        behind = jnp.where(column == 0, 0.0, pltpu.roll(v, 1, 0))
        d[rows, 0:128] = ahead.astype(BF16)
        d[rows, 128:256] = v.astype(BF16)
        d[rows, 256:384] = behind.astype(BF16)
        return carry

    lax.fori_loop(0, n_own // (2 * WIDE), body, 0)
    load.wait()
    lhs = d[...]
    for i in range(3):
        part = lax.dot_general(
            lhs, hb[i * WIDE : i * WIDE + n_own, :], (((0,), (0,)), ((), ())), preferred_element_type=F32
        ).astype(BF16)
        for s in range(3):
            out[:, (3 * i + s) * CHANS : (3 * i + s + 1) * CHANS] = part[s * LANES : (s + 1) * LANES]


def wgrad_step(dz, hb):
    n_own = dz.shape[0]
    return pl.pallas_call(
        wgrad_kernel,
        out_shape=jax.ShapeDtypeStruct((LANES, 9 * CHANS), BF16),
        in_specs=[VMEM, ANY],
        out_specs=VMEM,
        scratch_shapes=[
            pltpu.VMEM((n_own, 3 * LANES), BF16),
            pltpu.VMEM(hb.shape, BF16),
            pltpu.SemaphoreType.DMA,
        ],
        compiler_params=PARAMS,
        cost_estimate=pl.CostEstimate(
            flops=2 * n_own * 9 * CHANS * LANES, bytes_accessed=3 * 1024 * 1024, transcendentals=0
        ),
        name="kernel_gradient",
    )(dz, hb)


def turn_kernel(pos, w, o0, o1, o2, o3):
    for k, out in enumerate((o0, o1, o2, o3)):
        for i in range(9):
            at = pl.multiple_of(i * CHANS + (pos[0] ^ k) * LANES, LANES)
            out[0, :, i * LANES : (i + 1) * LANES] = w[0, :, pl.ds(at, LANES)]


def turn_step(pos, weights):
    layers = weights.shape[0]
    block = pl.BlockSpec((1, LANES, 9 * LANES), lambda i: (i, 0, 0))
    return pl.pallas_call(
        turn_kernel,
        grid=(layers,),
        out_shape=(jax.ShapeDtypeStruct((layers, LANES, 9 * LANES), BF16),) * GROUPS,
        in_specs=[SMEM, pl.BlockSpec((1, LANES, 9 * CHANS), lambda i: (i, 0, 0))],
        out_specs=(block,) * GROUPS,
        compiler_params=PARAMS,
        name="kernels_by_group",
    )(pos, weights)


def swap_with(value, axis, k):
    return lax.ppermute(value, axis, [(i, i ^ k) for i in range(lax.axis_size(axis))])


def spread(own):
    return (own, *[swap_with(own, "tensor", k) for k in range(1, GROUPS)])


def meet(own, msg, edge):
    got = swap_with(msg, "rows", 1)
    if edge > 0:
        own = lax.dynamic_update_slice_in_dim(own, got[:edge].astype(BF16), own.shape[0] - edge, axis=0)
    sums = jnp.concatenate([msg[edge : edge + 2], got[edge : edge + 2], jnp.zeros((4, LANES), F32)], axis=0)
    return own, sums


def share_images(sums):
    return jnp.concatenate([sums] + [swap_with(sums, "dp", k) for k in range(1, 4)], axis=0)


def halo_of_input(x, half):
    n_own = x.shape[0]
    edge = jnp.where(half == 0, x[n_own - WIDE :], x[:WIDE])
    return jnp.concatenate([x, swap_with(edge, "rows", 1)], axis=0)


def fast_local(section_input, conv_weights, norm_gains, norm_shifts, out_grad, out_mask):
    images, rows_here, width = out_mask.shape
    layers = conv_weights.shape[0]
    n_own = rows_here * width
    parts = lax.axis_size("dp") * lax.axis_size("rows")
    total = float(n_own * parts)
    t, half = lax.axis_index("tensor"), lax.axis_index("rows")
    pos = jnp.stack([t, half]).astype(jnp.int32)
    middle = layers // 2
    x = to_maps(section_input, width).reshape(n_own, LANES)
    slots = spread(halo_of_input(x, half))
    pad = jnp.zeros((8 - layers, LANES), F32)
    tables = spread(jnp.concatenate([norm_gains, pad, norm_shifts, pad], axis=0))
    turned = turn_step(pos, conv_weights)
    turned = (turned[0], *[swap_with(turned[k], "tensor", k) for k in range(1, GROUPS)])
    top_grad = (to_maps(out_grad, width) * out_mask[..., None].astype(BF16)).reshape(n_own, LANES)
    gslots = spread(halo_of_input(top_grad, half))

    stats = None
    kept_h, kept_z, kept_stats = [], [], []
    for layer in range(layers):
        edge = 2 * WIDE if layer + 1 == middle else WIDE
        hb, own, msg = fwd_step(
            layer, layer == middle, edge, total, pos, slots, stats, tables, conv_weights, n_own
        )
        own, sums = meet(own, msg, edge)
        slots = spread(own)
        shared = share_images(sums)
        stats = spread(shared)
        kept_h.append(hb)
        kept_z.append(slots)
        kept_stats.append(stats)
    h_last, msg = top_step(layers - 1, total, own, shared, tables[0], top_grad, n_own)
    unused, sums = meet(None, msg, 0)
    kernel_list, sum_list = [None] * layers, [None] * layers
    for layer in range(layers - 1, -1, -1):
        shared = share_images(sums)
        sum_list[layer] = shared
        sum_slots = spread(shared)
        below = (kept_z[layer - 1][0], kept_stats[layer - 1][0]) if layer > 0 else None
        outs = bwd_step(
            layer,
            layer == middle,
            total,
            pos,
            kept_z[layer],
            kept_stats[layer],
            tables,
            gslots,
            sum_slots,
            below,
            turned,
            n_own,
        )
        grad, dz = outs[0], outs[1]
        if layer > 0:
            grad, sums = meet(grad, outs[2], WIDE)
            gslots = spread(grad)
        kernel_list[layer] = wgrad_step(dz, kept_h[layer])
    upper = lax.psum(tuple(kernel_list[middle:]), ("dp", "rows"))
    tied = lax.optimization_barrier((tuple(kernel_list[:middle]), upper))
    lower = lax.psum(tied[0], ("dp", "rows"))
    kernel_list = list(lower) + list(tied[1])
    sums = jnp.sum(jnp.stack(sum_list).reshape(layers, 4, 8, LANES)[:, :, :4], axis=1)
    sums = sums[:, :2] + sums[:, 2:]
    shape = (images, rows_here, width, LANES)
    return (
        from_maps(h_last.reshape(shape)),
        from_maps(grad.reshape(shape)),
        jnp.stack([k.astype(F32) for k in kernel_list]),
        sums[:, 1],
        sums[:, 0],
    )


def solution(mesh):
    in_specs = (
        P("dp", "rows", "tensor"),
        P(None, "tensor", None),
        P(None, "tensor"),
        P(None, "tensor"),
        P("dp", "rows", "tensor"),
        P("dp", "rows", None),
    )
    out_specs = (
        P("dp", "rows", "tensor"),
        P("dp", "rows", "tensor"),
        P(None, "tensor", None),
        P(None, "tensor"),
        P(None, "tensor"),
    )
    local = fast_local if fits_kernels(mesh) else generic_local
    return jax.shard_map(local, mesh=mesh, in_specs=in_specs, out_specs=out_specs, check_vma=False)
```

```python
import functools

import jax
import jax.numpy as jnp
from jax import lax
from jax.experimental import pallas as pl
from jax.experimental.pallas import tpu as pltpu
from jax.sharding import PartitionSpec as P

EPS = 1e-05


def padded_2(cells, sides, width):
    for axis, dim in sides:
        count = lax.axis_size(axis)
        ends = count - 1
        head = lax.slice_in_dim(cells, 0, width, axis=dim)
        tail = lax.slice_in_dim(cells, cells.shape[dim] - width, cells.shape[dim], axis=dim)
        cells = jnp.concatenate(
            [
                lax.ppermute(tail, axis, [(i, (i + 1) % count) for i in range(ends)]),
                cells,
                lax.ppermute(head, axis, [((i + 1) % count, i) for i in range(ends)]),
            ],
            axis=dim,
        )
    return cells


def to_maps(flat, width):
    count, high, merged = flat.shape
    return flat.reshape(count, high, merged // width, width).transpose(0, 1, 3, 2)


def from_maps(maps):
    count, high, wide, chans = maps.shape
    return maps.transpose(0, 1, 3, 2).reshape(count, high, chans * wide)


def spatial_conv(padded, kernel):
    return lax.conv_general_dilated(
        padded,
        kernel,
        (1, 1),
        ((0, 0), (1, 1)),
        dimension_numbers=("NHWC", "HWIO", "NHWC"),
        preferred_element_type=jnp.float32,
    )


def flipped(kernel):
    return jnp.transpose(kernel[::-1, ::-1], (0, 1, 3, 2))


def pool_unpool(values):
    count, high, wide, chans = values.shape
    blocks = values.reshape(count, high // 2, 2, wide // 2, 2, chans)
    pooled = jax.nn.logsumexp(blocks, axis=(2, 4), keepdims=True)
    return (jnp.exp(blocks - pooled) * pooled).reshape(values.shape)


def moments(conv_out, total_pixels):
    summed = lax.psum(jnp.sum(conv_out, axis=(0, 1, 2)), ("dp", "rows"))
    mean = summed / total_pixels
    spread = lax.psum(jnp.sum(jnp.square(conv_out - mean), axis=(0, 1, 2)), ("dp", "rows"))
    var = spread / total_pixels
    return (mean, lax.rsqrt(var + EPS))


def kernel_grad(whole, dconv):
    images, rows_here, width, chans = dconv.shape
    widened = jnp.pad(whole, ((0, 0), (0, 0), (1, 1), (0, 0)))
    stacked = []
    for row_off in range(3):
        line = []
        for col_off in range(3):
            window = widened[:, row_off : row_off + rows_here, col_off : col_off + width, :]
            line.append(
                jnp.einsum("bhwc,bhwo->co", window, dconv, preferred_element_type=jnp.float32)
            )
        stacked.append(jnp.stack(line))
    return jnp.stack(stacked)


def generic_local(section_input, conv_weights, norm_gains, norm_shifts, out_grad, out_mask):
    width = out_mask.shape[2]
    images, rows_here = (out_mask.shape[0], out_mask.shape[1])
    total_pixels = float(images * rows_here * width * lax.axis_size("dp") * lax.axis_size("rows"))
    layers, out_here, flat_in = conv_weights.shape
    chans_in = flat_in // 9
    kernels_hwio = conv_weights.reshape(layers, out_here, 3, 3, chans_in).transpose(0, 2, 3, 4, 1)
    middle = layers // 2
    kept = []
    acting = to_maps(section_input, width)
    current = acting.astype(jnp.float32)
    pre_pool = current
    for index in range(layers):
        if index == middle:
            pre_pool = current
            acting = pool_unpool(pre_pool).astype(jnp.bfloat16)
        padded = padded_2(acting, (("rows", 1),), 1)
        whole = lax.all_gather(padded, "tensor", axis=3, tiled=True)
        conv_out = spatial_conv(whole, kernels_hwio[index])
        mean, rstd = moments(conv_out, total_pixels)
        normed = (conv_out - mean) * rstd
        shifted = normed * norm_gains[index] + norm_shifts[index]
        current = jax.nn.silu(shifted)
        acting = current.astype(jnp.bfloat16)
        kept.append((whole, normed, shifted, rstd))
    grad = to_maps(out_grad, width).astype(jnp.float32) * out_mask[..., None].astype(jnp.float32)
    kernel_list = [None] * layers
    gain_list = [None] * layers
    shift_list = [None] * layers
    for index in range(layers - 1, -1, -1):
        whole, normed, shifted, rstd = kept[index]
        unused, pull_silu = jax.vjp(jax.nn.silu, shifted)
        dshift = pull_silu(grad)[0]
        gain_sum, shift_sum = lax.psum(
            (jnp.sum(dshift * normed, axis=(0, 1, 2)), jnp.sum(dshift, axis=(0, 1, 2))),
            ("dp", "rows"),
        )
        gain_list[index] = gain_sum
        shift_list[index] = shift_sum
        dconv = (
            norm_gains[index]
            * rstd
            * (dshift - shift_sum / total_pixels - normed * gain_sum / total_pixels)
        ).astype(jnp.bfloat16)
        summed_kernel = lax.psum(
            kernel_grad(whole, dconv).astype(jnp.bfloat16), ("dp", "rows")
        ).astype(jnp.float32)
        kernel_list[index] = summed_kernel.transpose(3, 0, 1, 2).reshape(out_here, flat_in)
        grad_rim = padded_2(dconv, (("rows", 1),), 1)
        partial_terms = spatial_conv(grad_rim, flipped(kernels_hwio[index]))
        grad_in = lax.psum_scatter(
            partial_terms.astype(jnp.bfloat16), "tensor", scatter_dimension=3, tiled=True
        ).astype(jnp.float32)
        if index == middle:
            unused, pull_pool = jax.vjp(pool_unpool, pre_pool)
            grad = pull_pool(grad_in)[0]
        else:
            grad = grad_in
    return (
        from_maps(acting),
        from_maps(grad),
        jnp.stack(kernel_list),
        jnp.stack(gain_list),
        jnp.stack(shift_list),
    )


GROUPS = 4
LANES = 128
WIDE = 48
CHANS = GROUPS * LANES
F32 = jnp.float32
BF16 = jnp.bfloat16
VMEM = pl.BlockSpec(memory_space=pltpu.VMEM)
SMEM = pl.BlockSpec(memory_space=pltpu.SMEM)
ANY = pl.BlockSpec(memory_space=pltpu.HBM)
PARAMS = pltpu.CompilerParams(vmem_limit_bytes=24 * 1024 * 1024)


def fits_kernels(mesh):
    return mesh.shape["tensor"] == GROUPS and mesh.shape["rows"] == 2 and mesh.shape["dp"] == 4


def sigmoid(v):
    return 0.5 * jnp.tanh(0.5 * v) + 0.5


def swap_columns(v):
    column = lax.broadcasted_iota(jnp.int32, v.shape, 0)
    return jnp.where(column % 2 == 0, pltpu.roll(v, WIDE - 1, 0), pltpu.roll(v, 1, 0))


def soft_parts(h):
    top = jnp.maximum(h[0], h[1])
    top = jnp.maximum(top, swap_columns(top))
    e0, e1 = jnp.exp(h[0] - top), jnp.exp(h[1] - top)
    total = e0 + e1
    total = total + swap_columns(total)
    pooled = top + jnp.log(total)
    inverse = 1.0 / total
    return e0 * inverse, e1 * inverse, pooled


def soft(h):
    h = h.reshape(2, WIDE, LANES)
    q0, q1, pooled = soft_parts(h)
    return jnp.concatenate([q0 * pooled, q1 * pooled], axis=0)


def soft_pull(h, grad):
    h = h.reshape(2, WIDE, LANES)
    grad = grad.reshape(2, WIDE, LANES)
    q0, q1, pooled = soft_parts(h)
    mix = q0 * grad[0] + q1 * grad[1]
    mix = mix + swap_columns(mix)
    return jnp.concatenate(
        [q0 * (pooled * (grad[0] - mix) + mix), q1 * (pooled * (grad[1] - mix) + mix)], axis=0
    )


def norm_tables(st_ref, at, total):
    mean, spread, own, oth = (st_ref[at + i : at + i + 1, :] for i in range(4))
    rstd = lax.rsqrt(spread / total + EPS)
    return rstd, (own - mean) * rstd, (oth - mean) * rstd


def left_right(y0, y1, y2):
    rows = y0.shape[0]
    column = lax.broadcasted_iota(jnp.int32, y0.shape, 0) % WIDE
    before = jnp.where(column == 0, 0.0, pltpu.roll(y0, 1, 0))
    after = jnp.where(column == WIDE - 1, 0.0, pltpu.roll(y2, rows - 1, 0))
    return before + y1 + after


def lane_of(group):
    return pl.multiple_of(group * LANES, LANES)


def write_message(msg, own, sums, edge, half):
    n_own = own.shape[0]
    start = pl.multiple_of((1 - half) * (n_own - edge), WIDE)
    msg[0:edge, :] = own[pl.ds(start, edge), :].astype(F32)
    msg[edge : edge + 8, :] = jnp.concatenate([sums, jnp.zeros((8 - sums.shape[0], LANES), F32)], axis=0)


def fwd_kernel(first, pool, layer, total, edge_out, ties, *refs):
    if first:
        pos, z0, z1, z2, z3, w_hbm = refs[:6]
        rest = refs[6:]
    else:
        pos, z0, z1, z2, z3, st0, st1, st2, gs0, gs1, gs2, gs3, w_hbm = refs[:13]
        sts, gss = ((st0, 0), (st1, 0), (st2, 0), (st2, 8)), (gs0, gs1, gs2, gs3)
        rest = refs[13:]
    hb_out, zc_out, msg = rest[ties : ties + 3]
    hb, w, y, z, tab, hs, sem = rest[-7:]
    zs = (z0, z1, z2, z3)
    load = pltpu.make_async_copy(w_hbm.at[layer], w, sem.at[0])
    load.start()
    save = pltpu.make_async_copy(hb, hb_out, sem.at[1])
    t, r = pos[0], pos[1]
    n_own = z.shape[0]
    edge = z0.shape[0] - n_own
    halo_at = pl.multiple_of((1 - r) * (n_own + WIDE), WIDE)
    zero_at = pl.multiple_of(r * (n_own + WIDE), WIDE)
    hb[pl.ds(zero_at, WIDE), :] = jnp.zeros((WIDE, CHANS), BF16)
    if not first:
        for k in range(GROUPS):
            rstd, own, oth = norm_tables(*sts[k], total)
            gain, shift = gss[k][layer - 1 : layer, :], gss[k][layer + 7 : layer + 8, :]
            tab[k, 0:1] = rstd * gain
            tab[k, 1:2] = own * gain + shift
            tab[k, 2:3] = oth * gain + shift

    def act(values, k, which):
        if first:
            return values
        n = values.astype(F32) * tab[k, 0:1, :] + tab[k, which : which + 1, :]
        h = n * sigmoid(n)
        return soft(h) if pool else h

    def body(j, carry):
        at = pl.multiple_of(j * 2 * WIDE, 2 * WIDE)
        for k in range(GROUPS):
            h = act(zs[k][pl.ds(at, 2 * WIDE), :], k, 1)
            hb[pl.ds(pl.multiple_of(at + WIDE, WIDE), 2 * WIDE), pl.ds(lane_of(t ^ k), LANES)] = h.astype(BF16)
        return carry

    lax.fori_loop(0, n_own // (2 * WIDE), body, 0)
    for k in range(GROUPS):
        h = act(zs[k][n_own : n_own + edge, :], k, 2)
        if edge > WIDE:
            hs[...] = h
            h = hs[pl.ds(pl.multiple_of(r * WIDE, WIDE), WIDE), :]
        hb[pl.ds(halo_at, WIDE), pl.ds(lane_of(t ^ k), LANES)] = h.astype(BF16)
    save.start()
    load.wait()
    lhs = jnp.concatenate([hb[i * WIDE : i * WIDE + n_own, :] for i in range(3)], axis=1)
    rhs = jnp.concatenate(
        [
            jnp.concatenate([w[:, (3 * i + s) * CHANS : (3 * i + s + 1) * CHANS] for i in range(3)], axis=1)
            for s in range(3)
        ],
        axis=0,
    )
    y[...] = lax.dot_general(lhs, rhs, (((1,), (1,)), ((), ())), preferred_element_type=F32)

    def add_up(j, acc):
        at = pl.multiple_of(j * 2 * WIDE, 2 * WIDE)
        rows = pl.ds(at, 2 * WIDE)
        v = left_right(y[rows, 0:128], y[rows, 128:256], y[rows, 256:384])
        z[rows, :] = v
        return acc + jnp.sum(v.reshape(12, 8, LANES), axis=0)

    steps = n_own // (2 * WIDE)
    summed = lax.fori_loop(0, steps, add_up, jnp.zeros((8, LANES), F32))
    mean = jnp.sum(summed, axis=0, keepdims=True) / n_own

    def centre(j, acc):
        rows = pl.ds(pl.multiple_of(j * 2 * WIDE, 2 * WIDE), 2 * WIDE)
        v = z[rows, :] - mean
        z[rows, :] = v
        zc_out[rows, :] = v.astype(BF16)
        return acc + jnp.sum(jnp.square(v).reshape(12, 8, LANES), axis=0)

    apart = lax.fori_loop(0, steps, centre, jnp.zeros((8, LANES), F32))
    sums = [mean, jnp.sum(apart, axis=0, keepdims=True), mean, jnp.zeros((1, LANES), F32)]
    write_message(msg, z, jnp.concatenate(sums, axis=0), edge_out, r)
    save.wait()


def fwd_step(layer, pool, edge_out, total, pos, slots, stats, tables, weights, n_own, passed, need):
    first = stats is None
    extra = () if first else (*stats, *tables)
    passes = [] if passed is None else [jax.ShapeDtypeStruct(passed.shape, passed.dtype)]
    ties = [v for v in (passed, need) if v is not None]
    return pl.pallas_call(
        functools.partial(fwd_kernel, first, pool, layer, total, edge_out, len(ties)),
        out_shape=(
            jax.ShapeDtypeStruct((n_own + 2 * WIDE, CHANS), BF16),
            jax.ShapeDtypeStruct((n_own + edge_out, LANES), BF16),
            jax.ShapeDtypeStruct((edge_out + 8, LANES), F32),
            *passes,
        ),
        in_specs=[SMEM] + [VMEM] * (4 + len(extra)) + [ANY] * (1 + len(ties)),
        out_specs=(ANY, VMEM, VMEM) + (ANY,) * len(passes),
        input_output_aliases={6 + len(extra): 3} if passes else {},
        scratch_shapes=[
            pltpu.VMEM((n_own + 2 * WIDE, CHANS), BF16),
            pltpu.VMEM((LANES, 9 * CHANS), BF16),
            pltpu.VMEM((n_own, 3 * LANES), F32),
            pltpu.VMEM((n_own, LANES), F32),
            pltpu.VMEM((GROUPS, 8, LANES), F32),
            pltpu.VMEM((2 * WIDE, LANES), F32),
            pltpu.SemaphoreType.DMA((2,)),
        ],
        compiler_params=PARAMS,
        cost_estimate=pl.CostEstimate(
            flops=2 * n_own * 9 * CHANS * LANES, bytes_accessed=4 * 1024 * 1024, transcendentals=n_own * CHANS
        ),
        name="conv_forward",
    )(pos, *slots, *extra, weights, *ties)


def below_sums(zc, st, gs, layer, grad_ref, n_own, total, tab, emit):
    rstd, own, oth = norm_tables(st, 0, total)
    tab[0:1], tab[1:2] = rstd, own
    tab[2:3], tab[3:4] = gs[layer : layer + 1, :], gs[layer + 8 : layer + 9, :]

    def body(j, accs):
        rows = pl.ds(pl.multiple_of(j * 2 * WIDE, 2 * WIDE), 2 * WIDE)
        xhat = zc[rows, :].astype(F32) * tab[0:1, :] + tab[1:2, :]
        n = xhat * tab[2:3, :] + tab[3:4, :]
        sig = sigmoid(n)
        h = n * sig
        g = emit(rows, h, grad_ref[rows, :].astype(F32))
        dn = g * (sig * (1.0 + n - h))
        return (
            accs[0] + jnp.sum(dn.reshape(12, 8, LANES), axis=0),
            accs[1] + jnp.sum((dn * xhat).reshape(12, 8, LANES), axis=0),
        )

    zero = jnp.zeros((8, LANES), F32)
    sums = lax.fori_loop(0, n_own // (2 * WIDE), body, (zero, zero))
    return jnp.concatenate([jnp.sum(s, axis=0, keepdims=True) for s in sums], axis=0)


def top_kernel(layer, total, zc, st, gs, grad, h_out, msg, tab):
    def emit(rows, h, g):
        h_out[rows, :] = h.astype(BF16)
        return g

    sums = below_sums(zc, st, gs, layer, grad, h_out.shape[0], total, tab, emit)
    msg[...] = jnp.concatenate([sums, jnp.zeros((6, LANES), F32)], axis=0)


def top_step(layer, total, zc, st, gs, grad, n_own):
    return pl.pallas_call(
        functools.partial(top_kernel, layer, total),
        out_shape=(
            jax.ShapeDtypeStruct((n_own, LANES), BF16),
            jax.ShapeDtypeStruct((8, LANES), F32),
        ),
        in_specs=[VMEM] * 4,
        out_specs=(VMEM, VMEM),
        scratch_shapes=[pltpu.VMEM((8, LANES), F32)],
        compiler_params=PARAMS,
        name="top_sums",
    )(zc, st, gs, grad)


def bwd_kernel(last, pool, layer, total, *refs):
    pos = refs[0]
    zs, sts, gss, gs, sums = refs[1:5], refs[5:8], refs[8:12], refs[12:16], refs[16:19]
    sts = ((sts[0], 0), (sts[1], 0), (sts[2], 0), (sts[2], 8))
    sums = ((sums[0], 0), (sums[1], 0), (sums[2], 0), (sums[2], 8))
    rest = refs[19:]
    if last:
        w_hbms, (g_out, dz_out) = rest[:7], rest[7:9]
        dz, zv, w, y, g, tab, tab2, sem = rest[9:]
    else:
        zb, stb = rest[:2]
        w_hbms, (g_out, dz_out, msg) = rest[2:9], rest[9:12]
        dz, zv, w, y, g, tab, tab2, sem = rest[12:]
    n_own = dz_out.shape[0]
    edge = zv.shape[1] - n_own
    zloads = [pltpu.make_async_copy(zs[k], zv.at[k], sem.at[k]) for k in range(GROUPS)]
    r = pos[1]
    for load in zloads:
        load.start()
    third = layer % 3
    w_own = pltpu.make_async_copy(w_hbms[0].at[layer], w.at[pl.ds(0, LANES)], sem.at[GROUPS])
    w_own.start()
    near = [
        pltpu.make_async_copy(w_hbms[k].at[third], w.at[pl.ds(k * LANES, LANES)], sem.at[GROUPS + k])
        for k in range(1, GROUPS)
    ]
    far = [
        pltpu.make_async_copy(w_hbms[3 + k].at[third], w.at[pl.ds(k * LANES, LANES)], sem.at[GROUPS + k])
        for k in range(1, GROUPS)
    ]
    direct = r == (0 if layer >= 3 else 1)

    @pl.when(direct)
    def _():
        for load in near:
            load.start()

    @pl.when(jnp.logical_not(direct))
    def _():
        for load in far:
            load.start()
    halo_at = pl.multiple_of((1 - r) * (n_own + WIDE), WIDE)
    zero_at = pl.multiple_of(r * (n_own + WIDE), WIDE)
    dz[pl.ds(zero_at, WIDE), :] = jnp.zeros((WIDE, CHANS), BF16)
    for k in range(GROUPS):
        rstd, own, oth = norm_tables(*sts[k], total)
        sums_ref, at = sums[k]
        shift_sum, gain_sum = sums_ref[at : at + 1, :], sums_ref[at + 1 : at + 2, :]
        gain, shift = gss[k][layer : layer + 1, :], gss[k][layer + 8 : layer + 9, :]
        scale = gain * rstd
        tab[k, 0:1], tab[k, 1:2], tab[k, 2:3] = rstd, own, oth
        tab[k, 3:4], tab[k, 4:5], tab[k, 5:6] = gain, shift, scale
        tab[k, 6:7], tab[k, 7:8] = scale * shift_sum / total, scale * gain_sum / total

    def back(values, grad, k, which):
        xhat = values.astype(F32) * tab[k, 0:1, :] + tab[k, which : which + 1, :]
        n = xhat * tab[k, 3:4, :] + tab[k, 4:5, :]
        sig = sigmoid(n)
        dn = grad.astype(F32) * (sig * (1.0 + n - n * sig))
        return (dn * tab[k, 5:6, :] - tab[k, 6:7, :] - xhat * tab[k, 7:8, :]).astype(BF16)

    for k in range(GROUPS):
        zloads[k].wait()

        def body(j, carry):
            at = pl.multiple_of(j * 2 * WIDE, 2 * WIDE)
            rows = pl.ds(at, 2 * WIDE)
            d = back(zv[k, rows, :], gs[k][rows, :], k, 1)
            dz[pl.ds(pl.multiple_of(at + WIDE, WIDE), 2 * WIDE), k * LANES : (k + 1) * LANES] = d
            if k == 0:
                dz_out[rows, :] = d
            return carry

        lax.fori_loop(0, n_own // (2 * WIDE), body, 0)
        z_at = n_own if edge == WIDE else pl.multiple_of(n_own + r * WIDE, WIDE)
        dz[pl.ds(halo_at, WIDE), k * LANES : (k + 1) * LANES] = back(
            zv[k, pl.ds(z_at, WIDE), :], gs[k][n_own : n_own + WIDE, :], k, 2
        )
    w_own.wait()
    for load in near:
        load.wait()
    lhs = jnp.concatenate([dz[(2 - i) * WIDE : (2 - i) * WIDE + n_own, :] for i in range(3)], axis=1)
    rhs = jnp.concatenate([w[:, 384 * i : 384 * (i + 1)] for i in range(3)], axis=0)
    y[...] = jnp.dot(lhs, rhs, preferred_element_type=F32)

    def shifted(rows):
        return left_right(y[rows, 256:384], y[rows, 128:256], y[rows, 0:128])

    def add_up(j, carry):
        rows = pl.ds(pl.multiple_of(j * 2 * WIDE, 2 * WIDE), 2 * WIDE)
        out = g_out if last else g
        out[rows, :] = shifted(rows)
        return carry

    lax.fori_loop(0, n_own // (2 * WIDE), add_up, 0)
    if not last:

        def emit(rows, h, grad):
            if pool:
                grad = soft_pull(h, grad)
                g[rows, :] = grad
            g_out[rows, :] = grad.astype(BF16)
            return grad

        below = below_sums(zb, stb, gss[0], layer - 1, g, n_own, total, tab2, emit)
        write_message(msg, g, below, WIDE, r)


def bwd_step(layer, pool, total, pos, zslots, stats, tables, gslots, sums, below, weights, n_own):
    last = below is None
    extra = () if last else below
    if last:
        out_shape = [jax.ShapeDtypeStruct((n_own, LANES), F32), jax.ShapeDtypeStruct((n_own, LANES), BF16)]
    else:
        out_shape = [
            jax.ShapeDtypeStruct((n_own + WIDE, LANES), BF16),
            jax.ShapeDtypeStruct((n_own, LANES), BF16),
            jax.ShapeDtypeStruct((WIDE + 8, LANES), F32),
        ]
    return pl.pallas_call(
        functools.partial(bwd_kernel, last, pool, layer, total),
        out_shape=tuple(out_shape),
        in_specs=[SMEM] + [ANY] * 4 + [VMEM] * (14 + len(extra)) + [ANY] * 7,
        out_specs=(VMEM,) * len(out_shape),
        scratch_shapes=[
            pltpu.VMEM((n_own + 2 * WIDE, CHANS), BF16),
            pltpu.VMEM((GROUPS,) + zslots[0].shape, BF16),
            pltpu.VMEM((CHANS, 9 * LANES), BF16),
            pltpu.VMEM((n_own, 3 * LANES), F32),
            pltpu.VMEM((n_own, LANES), F32),
            pltpu.VMEM((GROUPS, 8, LANES), F32),
            pltpu.VMEM((8, LANES), F32),
            pltpu.SemaphoreType.DMA((2 * GROUPS,)),
        ],
        compiler_params=PARAMS,
        cost_estimate=pl.CostEstimate(
            flops=2 * n_own * 9 * CHANS * LANES, bytes_accessed=4 * 1024 * 1024, transcendentals=n_own * CHANS
        ),
        name="conv_backward",
    )(pos, *zslots, *stats, *tables, *gslots, *sums, *extra, *weights)


def wgrad_kernel(dz, hb_hbm, out, d, hb, sem):
    n_own = dz.shape[0]
    load = pltpu.make_async_copy(hb_hbm, hb, sem)
    load.start()

    def body(j, carry):
        rows = pl.ds(pl.multiple_of(j * 2 * WIDE, 2 * WIDE), 2 * WIDE)
        v = dz[rows, :].astype(F32)
        column = lax.broadcasted_iota(jnp.int32, v.shape, 0) % WIDE
        ahead = jnp.where(column == WIDE - 1, 0.0, pltpu.roll(v, 2 * WIDE - 1, 0))
        behind = jnp.where(column == 0, 0.0, pltpu.roll(v, 1, 0))
        d[rows, 0:128] = ahead.astype(BF16)
        d[rows, 128:256] = v.astype(BF16)
        d[rows, 256:384] = behind.astype(BF16)
        return carry

    lax.fori_loop(0, n_own // (2 * WIDE), body, 0)
    load.wait()
    lhs = d[...]
    for i in range(3):
        part = lax.dot_general(
            lhs, hb[i * WIDE : i * WIDE + n_own, :], (((0,), (0,)), ((), ())), preferred_element_type=F32
        ).astype(BF16)
        for s in range(3):
            out[:, (3 * i + s) * CHANS : (3 * i + s + 1) * CHANS] = part[s * LANES : (s + 1) * LANES]


def wgrad_step(dz, hb):
    n_own = dz.shape[0]
    return pl.pallas_call(
        wgrad_kernel,
        out_shape=jax.ShapeDtypeStruct((LANES, 9 * CHANS), BF16),
        in_specs=[VMEM, ANY],
        out_specs=VMEM,
        scratch_shapes=[
            pltpu.VMEM((n_own, 3 * LANES), BF16),
            pltpu.VMEM(hb.shape, BF16),
            pltpu.SemaphoreType.DMA,
        ],
        compiler_params=PARAMS,
        cost_estimate=pl.CostEstimate(
            flops=2 * n_own * 9 * CHANS * LANES, bytes_accessed=3 * 1024 * 1024, transcendentals=0
        ),
        name="kernel_gradient",
    )(dz, hb)


def turn_kernel(pos, w, own, o1, o2, o3, sem):
    t, r = pos[0], pos[1]
    base = 3 * (1 - r)
    copies = []
    for i in range(9):
        lanes = pl.ds(pl.multiple_of(i * CHANS + t * LANES, LANES), LANES)
        copies.append(pltpu.make_async_copy(w.at[:, :, lanes], own.at[:, :, i * LANES : (i + 1) * LANES], sem.at[i]))
    for k, out in enumerate((o1, o2, o3), 1):
        for i in range(9):
            lanes = pl.ds(pl.multiple_of(i * CHANS + (t ^ k) * LANES, LANES), LANES)
            copies.append(
                pltpu.make_async_copy(
                    w.at[pl.ds(base, 3), :, lanes], out.at[:, :, i * LANES : (i + 1) * LANES], sem.at[9 * k + i]
                )
            )
    for copy in copies:
        copy.start()
    for copy in copies:
        copy.wait()


def turn_step(pos, weights):
    layers = weights.shape[0]
    third = jax.ShapeDtypeStruct((3, LANES, 9 * LANES), BF16)
    return pl.pallas_call(
        turn_kernel,
        out_shape=(jax.ShapeDtypeStruct((layers, LANES, 9 * LANES), BF16), third, third, third),
        in_specs=[SMEM, ANY],
        out_specs=(ANY,) * 4,
        scratch_shapes=[pltpu.SemaphoreType.DMA((36,))],
        compiler_params=PARAMS,
        cost_estimate=pl.CostEstimate(flops=0, bytes_accessed=10 * 1024 * 1024, transcendentals=0),
        name="kernels_by_group",
    )(pos, weights)


def place_kernel(value, *refs):
    refs[-1][0] = value[...].astype(F32)


def place_step(layer, value, whole, layers):
    rows = 32
    return pl.pallas_call(
        place_kernel,
        grid=(LANES // rows,),
        out_shape=jax.ShapeDtypeStruct((layers, LANES, 9 * CHANS), F32),
        in_specs=[pl.BlockSpec((rows, 9 * CHANS), lambda i: (i, 0))] + ([] if whole is None else [ANY]),
        out_specs=pl.BlockSpec((1, rows, 9 * CHANS), lambda i: (layer, i, 0)),
        input_output_aliases={} if whole is None else {1: 0},
        compiler_params=PARAMS,
        cost_estimate=pl.CostEstimate(flops=0, bytes_accessed=4 * 1024 * 1024, transcendentals=0),
        name="place_gradient",
    )(value, *(() if whole is None else (whole,)))


def swap_with(value, axis, k):
    return lax.ppermute(value, axis, [(i, i ^ k) for i in range(lax.axis_size(axis))])


def spread(own):
    return (own, *[swap_with(own, "tensor", k) for k in range(1, GROUPS)])


def pair_moments(mine, got, count):
    mean = 0.5 * (mine[0:1] + got[0:1])
    apart = mine[1:2] + got[1:2] + (0.5 * count) * jnp.square(got[0:1] - mine[0:1])
    return mean, apart


def meet(own, msg, edge, count):
    got = swap_with(msg, "rows", 1)
    if own is not None:
        own = lax.dynamic_update_slice_in_dim(own, got[:edge].astype(BF16), own.shape[0] - edge, axis=0)
    mine, got = msg[edge:], got[edge:]
    if count is None:
        return own, mine + got
    mean, apart = pair_moments(mine, got, count)
    return own, jnp.concatenate([mean, apart, mine[2:3], got[2:3], mine[4:]], axis=0)


def share_images(sums, count):
    for k in (1, 2):
        got = swap_with(sums, "dp", k)
        if count is None:
            sums = sums + got
        else:
            mean, apart = pair_moments(sums, got, 2 * k * count)
            sums = jnp.concatenate([mean, apart, sums[2:]], axis=0)
    return sums


def share_groups(sums):
    one = swap_with(sums, "tensor", 1)
    return sums, one, swap_with(jnp.concatenate([sums, one], axis=0), "tensor", 2)


def halo_of_input(x, half):
    n_own = x.shape[0]
    edge = jnp.where(half == 0, x[n_own - WIDE :], x[:WIDE])
    return jnp.concatenate([x, swap_with(edge, "rows", 1)], axis=0)


def fast_local(section_input, conv_weights, norm_gains, norm_shifts, out_grad, out_mask):
    images, rows_here, width = out_mask.shape
    layers = conv_weights.shape[0]
    n_own = rows_here * width
    parts = lax.axis_size("dp") * lax.axis_size("rows")
    total = float(n_own * parts)
    t, half = lax.axis_index("tensor"), lax.axis_index("rows")
    pos = jnp.stack([t, half]).astype(jnp.int32)
    middle = layers // 2
    x = to_maps(section_input, width).reshape(n_own, LANES)
    slots = spread(halo_of_input(x, half))
    pad = jnp.zeros((8 - layers, LANES), F32)
    tables = spread(jnp.concatenate([norm_gains, pad, norm_shifts, pad], axis=0))
    turned = turn_step(pos, conv_weights)
    top_grad = (to_maps(out_grad, width) * out_mask[..., None].astype(BF16)).reshape(n_own, LANES)

    stats = None
    kept_h, kept_z, kept_stats = [], [], []
    sent = {0: 1, 1: 2, 3: 3}
    due = {2: 1, 3: 2, 5: 3}
    near, far = {}, {}
    for layer in range(layers):
        edge = 2 * WIDE if layer + 1 == middle else WIDE
        peer = sent.get(layer)
        passed = turned[peer] if peer else None
        need = near[due[layer]] if layer in due else None
        hb, own, msg, *passed = fwd_step(
            layer,
            layer == middle,
            edge,
            total,
            pos,
            slots,
            stats,
            tables,
            conv_weights,
            n_own,
            passed,
            need,
        )
        if peer:
            near[peer] = swap_with(passed[0], "tensor", peer)
        if layer in due:
            far[due[layer]] = swap_with(need, "rows", 1)
        own, sums = meet(own, msg, edge, float(n_own))
        slots = spread(own)
        shared = share_images(sums, float(n_own))
        stats = share_groups(shared)
        kept_h.append(hb)
        kept_z.append(slots)
        kept_stats.append(stats)
    kernels = (turned[0], near[1], near[2], near[3], far[1], far[2], far[3])
    gslots = spread(halo_of_input(top_grad, half))
    h_last, msg = top_step(layers - 1, total, own, shared, tables[0], top_grad, n_own)
    unused, sums = meet(None, msg, 0, None)
    kernel_list, sum_list = [None] * layers, [None] * layers
    for layer in range(layers - 1, -1, -1):
        shared = share_images(sums, None)
        sum_list[layer] = shared
        sum_slots = share_groups(shared)
        below = (kept_z[layer - 1][0], kept_stats[layer - 1][0]) if layer > 0 else None
        outs = bwd_step(
            layer,
            layer == middle,
            total,
            pos,
            kept_z[layer],
            kept_stats[layer],
            tables,
            gslots,
            sum_slots,
            below,
            kernels,
            n_own,
        )
        grad, dz = outs[0], outs[1]
        if layer > 0:
            grad, sums = meet(grad, outs[2], WIDE, None)
            gslots = spread(grad)
        kernel_list[layer] = wgrad_step(dz, kept_h[layer])
    upper = lax.psum(tuple(kernel_list[middle:]), ("dp", "rows"))
    tied = lax.optimization_barrier((tuple(kernel_list[:middle]), upper))
    lower = lax.psum(tied[0], ("dp", "rows"))
    whole = None
    for layer in range(layers - 1, -1, -1):
        whole = place_step(layer, (list(lower) + list(tied[1]))[layer], whole, layers)
    sums = jnp.stack(sum_list)
    shape = (images, rows_here, width, LANES)
    return (
        from_maps(h_last.reshape(shape)),
        from_maps(grad.reshape(shape)),
        whole,
        sums[:, 1],
        sums[:, 0],
    )


def solution(mesh):
    in_specs = (
        P("dp", "rows", "tensor"),
        P(None, "tensor", None),
        P(None, "tensor"),
        P(None, "tensor"),
        P("dp", "rows", "tensor"),
        P("dp", "rows", None),
    )
    out_specs = (
        P("dp", "rows", "tensor"),
        P("dp", "rows", "tensor"),
        P(None, "tensor", None),
        P(None, "tensor"),
        P(None, "tensor"),
    )
    local = fast_local if fits_kernels(mesh) else generic_local
    return jax.shard_map(local, mesh=mesh, in_specs=in_specs, out_specs=out_specs, check_vma=False)
```

```python
import functools

import jax
import jax.numpy as jnp
from jax import lax
from jax.experimental import pallas as pl
from jax.experimental.pallas import tpu as pltpu
from jax.sharding import PartitionSpec as P

EPS = 1e-05


def padded_2(cells, sides, width):
    for axis, dim in sides:
        count = lax.axis_size(axis)
        ends = count - 1
        head = lax.slice_in_dim(cells, 0, width, axis=dim)
        tail = lax.slice_in_dim(cells, cells.shape[dim] - width, cells.shape[dim], axis=dim)
        cells = jnp.concatenate(
            [
                lax.ppermute(tail, axis, [(i, (i + 1) % count) for i in range(ends)]),
                cells,
                lax.ppermute(head, axis, [((i + 1) % count, i) for i in range(ends)]),
            ],
            axis=dim,
        )
    return cells


def to_maps(flat, width):
    count, high, merged = flat.shape
    return flat.reshape(count, high, merged // width, width).transpose(0, 1, 3, 2)


def from_maps(maps):
    count, high, wide, chans = maps.shape
    return maps.transpose(0, 1, 3, 2).reshape(count, high, chans * wide)


def spatial_conv(padded, kernel):
    return lax.conv_general_dilated(
        padded,
        kernel,
        (1, 1),
        ((0, 0), (1, 1)),
        dimension_numbers=("NHWC", "HWIO", "NHWC"),
        preferred_element_type=jnp.float32,
    )


def flipped(kernel):
    return jnp.transpose(kernel[::-1, ::-1], (0, 1, 3, 2))


def pool_unpool(values):
    count, high, wide, chans = values.shape
    blocks = values.reshape(count, high // 2, 2, wide // 2, 2, chans)
    pooled = jax.nn.logsumexp(blocks, axis=(2, 4), keepdims=True)
    return (jnp.exp(blocks - pooled) * pooled).reshape(values.shape)


def moments(conv_out, total_pixels):
    summed = lax.psum(jnp.sum(conv_out, axis=(0, 1, 2)), ("dp", "rows"))
    mean = summed / total_pixels
    spread = lax.psum(jnp.sum(jnp.square(conv_out - mean), axis=(0, 1, 2)), ("dp", "rows"))
    var = spread / total_pixels
    return (mean, lax.rsqrt(var + EPS))


def kernel_grad(whole, dconv):
    images, rows_here, width, chans = dconv.shape
    widened = jnp.pad(whole, ((0, 0), (0, 0), (1, 1), (0, 0)))
    stacked = []
    for row_off in range(3):
        line = []
        for col_off in range(3):
            window = widened[:, row_off : row_off + rows_here, col_off : col_off + width, :]
            line.append(
                jnp.einsum("bhwc,bhwo->co", window, dconv, preferred_element_type=jnp.float32)
            )
        stacked.append(jnp.stack(line))
    return jnp.stack(stacked)


def generic_local(section_input, conv_weights, norm_gains, norm_shifts, out_grad, out_mask):
    width = out_mask.shape[2]
    images, rows_here = (out_mask.shape[0], out_mask.shape[1])
    total_pixels = float(images * rows_here * width * lax.axis_size("dp") * lax.axis_size("rows"))
    layers, out_here, flat_in = conv_weights.shape
    chans_in = flat_in // 9
    kernels_hwio = conv_weights.reshape(layers, out_here, 3, 3, chans_in).transpose(0, 2, 3, 4, 1)
    middle = layers // 2
    kept = []
    acting = to_maps(section_input, width)
    current = acting.astype(jnp.float32)
    pre_pool = current
    for index in range(layers):
        if index == middle:
            pre_pool = current
            acting = pool_unpool(pre_pool).astype(jnp.bfloat16)
        padded = padded_2(acting, (("rows", 1),), 1)
        whole = lax.all_gather(padded, "tensor", axis=3, tiled=True)
        conv_out = spatial_conv(whole, kernels_hwio[index])
        mean, rstd = moments(conv_out, total_pixels)
        normed = (conv_out - mean) * rstd
        shifted = normed * norm_gains[index] + norm_shifts[index]
        current = jax.nn.silu(shifted)
        acting = current.astype(jnp.bfloat16)
        kept.append((whole, normed, shifted, rstd))
    grad = to_maps(out_grad, width).astype(jnp.float32) * out_mask[..., None].astype(jnp.float32)
    kernel_list = [None] * layers
    gain_list = [None] * layers
    shift_list = [None] * layers
    for index in range(layers - 1, -1, -1):
        whole, normed, shifted, rstd = kept[index]
        unused, pull_silu = jax.vjp(jax.nn.silu, shifted)
        dshift = pull_silu(grad)[0]
        gain_sum, shift_sum = lax.psum(
            (jnp.sum(dshift * normed, axis=(0, 1, 2)), jnp.sum(dshift, axis=(0, 1, 2))),
            ("dp", "rows"),
        )
        gain_list[index] = gain_sum
        shift_list[index] = shift_sum
        dconv = (
            norm_gains[index]
            * rstd
            * (dshift - shift_sum / total_pixels - normed * gain_sum / total_pixels)
        ).astype(jnp.bfloat16)
        summed_kernel = lax.psum(
            kernel_grad(whole, dconv).astype(jnp.bfloat16), ("dp", "rows")
        ).astype(jnp.float32)
        kernel_list[index] = summed_kernel.transpose(3, 0, 1, 2).reshape(out_here, flat_in)
        grad_rim = padded_2(dconv, (("rows", 1),), 1)
        partial_terms = spatial_conv(grad_rim, flipped(kernels_hwio[index]))
        grad_in = lax.psum_scatter(
            partial_terms.astype(jnp.bfloat16), "tensor", scatter_dimension=3, tiled=True
        ).astype(jnp.float32)
        if index == middle:
            unused, pull_pool = jax.vjp(pool_unpool, pre_pool)
            grad = pull_pool(grad_in)[0]
        else:
            grad = grad_in
    return (
        from_maps(acting),
        from_maps(grad),
        jnp.stack(kernel_list),
        jnp.stack(gain_list),
        jnp.stack(shift_list),
    )


GROUPS = 4
LANES = 128
WIDE = 48
CHANS = GROUPS * LANES
F32 = jnp.float32
BF16 = jnp.bfloat16
VMEM = pl.BlockSpec(memory_space=pltpu.VMEM)
SMEM = pl.BlockSpec(memory_space=pltpu.SMEM)
ANY = pl.BlockSpec(memory_space=pltpu.HBM)
PARAMS = pltpu.CompilerParams(vmem_limit_bytes=46 * 1024 * 1024)


def fits_kernels(mesh):
    return mesh.shape["tensor"] == GROUPS and mesh.shape["rows"] == 2 and mesh.shape["dp"] == 4


def sigmoid(v):
    return 0.5 * jnp.tanh(0.5 * v) + 0.5


def swap_columns(v):
    column = lax.broadcasted_iota(jnp.int32, v.shape, 0)
    return jnp.where(column % 2 == 0, pltpu.roll(v, WIDE - 1, 0), pltpu.roll(v, 1, 0))


def soft_parts(h):
    top = jnp.maximum(h[0], h[1])
    top = jnp.maximum(top, swap_columns(top))
    e0, e1 = jnp.exp(h[0] - top), jnp.exp(h[1] - top)
    total = e0 + e1
    total = total + swap_columns(total)
    pooled = top + jnp.log(total)
    inverse = 1.0 / total
    return e0 * inverse, e1 * inverse, pooled


def soft(h):
    h = h.reshape(2, WIDE, LANES)
    q0, q1, pooled = soft_parts(h)
    return jnp.concatenate([q0 * pooled, q1 * pooled], axis=0)


def soft_pull(h, grad):
    h = h.reshape(2, WIDE, LANES)
    grad = grad.reshape(2, WIDE, LANES)
    q0, q1, pooled = soft_parts(h)
    mix = q0 * grad[0] + q1 * grad[1]
    mix = mix + swap_columns(mix)
    return jnp.concatenate(
        [q0 * (pooled * (grad[0] - mix) + mix), q1 * (pooled * (grad[1] - mix) + mix)], axis=0
    )


def norm_tables(st_ref, at, total):
    mean, spread, own, oth = (st_ref[at + i : at + i + 1, :] for i in range(4))
    rstd = lax.rsqrt(spread / total + EPS)
    return rstd, (own - mean) * rstd, (oth - mean) * rstd


def left_right(y0, y1, y2):
    rows = y0.shape[0]
    column = lax.broadcasted_iota(jnp.int32, y0.shape, 0) % WIDE
    before = jnp.where(column == 0, 0.0, pltpu.roll(y0, 1, 0))
    after = jnp.where(column == WIDE - 1, 0.0, pltpu.roll(y2, rows - 1, 0))
    return before + y1 + after


def lane_of(group):
    return pl.multiple_of(group * LANES, LANES)


def write_message(msg, own, sums, edge, half):
    n_own = own.shape[0]
    start = pl.multiple_of((1 - half) * (n_own - edge), WIDE)
    msg[0:edge, :] = own[pl.ds(start, edge), :].astype(F32)
    msg[edge : edge + 8, :] = jnp.concatenate([sums, jnp.zeros((8 - sums.shape[0], LANES), F32)], axis=0)


def pair_rows(j):
    return pl.ds(pl.multiple_of(j * 2 * WIDE, 2 * WIDE), 2 * WIDE)


def fold(v):
    return jnp.sum(v.reshape(v.shape[0] // 8, 8, LANES), axis=0)


def fwd_kernel(first, pool, layer, total, edge_out, *refs):
    pos, zs = refs[0], refs[1:5]
    if first:
        w_hbm, rest = refs[5], refs[6:]
    else:
        sides, gss, w_hbm, rest = refs[5:9], refs[9:13], refs[13], refs[15:]
    hb_out, zc_out, msg, hb, w, y, z, tab, hs, sem = rest
    load = pltpu.make_async_copy(w_hbm.at[layer], w, sem.at[0])
    load.start()
    save = pltpu.make_async_copy(hb, hb_out.at[layer], sem.at[1])
    t, r = pos[0], pos[1]
    n_own = z.shape[0]
    halo_at = pl.multiple_of((1 - r) * (n_own + WIDE), WIDE)
    zero_at = pl.multiple_of(r * (n_own + WIDE), WIDE)
    hb[pl.ds(zero_at, WIDE), :] = jnp.zeros((WIDE, CHANS), BF16)
    if not first:
        edge = sides[0].shape[0] - 8
        for k in range(GROUPS):
            rstd, own, oth = norm_tables(sides[k], edge, total)
            gain, shift = gss[k][layer - 1 : layer, :], gss[k][layer + 7 : layer + 8, :]
            tab[k, 0:1] = rstd * gain
            tab[k, 1:2] = own * gain + shift
            tab[k, 2:3] = oth * gain + shift

    def act(values, k, which):
        if first:
            return values
        n = values.astype(F32) * tab[k, 0:1, :] + tab[k, which : which + 1, :]
        h = n * sigmoid(n)
        return soft(h) if pool else h

    def body(j, carry):
        at = pl.multiple_of(j * 2 * WIDE, 2 * WIDE)
        for k in range(GROUPS):
            h = act(zs[k][pl.ds(at, 2 * WIDE), :], k, 1)
            hb[pl.ds(pl.multiple_of(at + WIDE, WIDE), 2 * WIDE), pl.ds(lane_of(t ^ k), LANES)] = h.astype(BF16)
        return carry

    lax.fori_loop(0, n_own // (2 * WIDE), body, 0)
    for k in range(GROUPS):
        if first:
            h = zs[k][n_own : n_own + WIDE, :]
        else:
            h = act(sides[k][0:edge, :], k, 2)
            if edge > WIDE:
                hs[...] = h
                h = hs[pl.ds(pl.multiple_of(r * WIDE, WIDE), WIDE), :]
        hb[pl.ds(halo_at, WIDE), pl.ds(lane_of(t ^ k), LANES)] = h.astype(BF16)
    save.start()
    load.wait()
    lhs = jnp.concatenate([hb[i * WIDE : i * WIDE + n_own, :] for i in range(3)], axis=1)
    rhs = jnp.concatenate(
        [
            jnp.concatenate([w[:, (3 * i + s) * CHANS : (3 * i + s + 1) * CHANS] for i in range(3)], axis=1)
            for s in range(3)
        ],
        axis=0,
    )
    y[...] = lax.dot_general(lhs, rhs, (((1,), (1,)), ((), ())), preferred_element_type=F32)

    def add_up(j, acc):
        rows = pair_rows(j)
        v = left_right(y[rows, 0:128], y[rows, 128:256], y[rows, 256:384])
        z[rows, :] = v
        return acc + fold(v)

    steps = n_own // (2 * WIDE)
    summed = lax.fori_loop(0, steps, add_up, jnp.zeros((8, LANES), F32))
    mean = jnp.sum(summed, axis=0, keepdims=True) / n_own

    def centre(j, acc):
        rows = pair_rows(j)
        v = z[rows, :] - mean
        z[rows, :] = v
        zc_out[rows, :] = v.astype(BF16)
        return acc + fold(jnp.square(v))

    apart = lax.fori_loop(0, steps, centre, jnp.zeros((8, LANES), F32))
    sums = [mean, jnp.sum(apart, axis=0, keepdims=True), mean, jnp.zeros((1, LANES), F32)]
    write_message(msg, z, jnp.concatenate(sums, axis=0), edge_out, r)
    save.wait()


def fwd_step(layer, pool, edge_out, total, pos, slots, sides, tables, weights, kept, n_own):
    first = sides is None
    layers = weights.shape[0]
    extra = () if first else (*sides, *tables)
    return pl.pallas_call(
        functools.partial(fwd_kernel, first, pool, layer, total, edge_out),
        out_shape=(
            jax.ShapeDtypeStruct((layers, n_own + 2 * WIDE, CHANS), BF16),
            jax.ShapeDtypeStruct((n_own, LANES), BF16),
            jax.ShapeDtypeStruct((edge_out + 8, LANES), F32),
        ),
        in_specs=[SMEM] + [VMEM] * (4 + len(extra)) + [ANY] * (1 if first else 2),
        out_specs=(ANY, VMEM, VMEM),
        input_output_aliases={} if first else {6 + len(extra): 0},
        scratch_shapes=[
            pltpu.VMEM((n_own + 2 * WIDE, CHANS), BF16),
            pltpu.VMEM((LANES, 9 * CHANS), BF16),
            pltpu.VMEM((n_own, 3 * LANES), F32),
            pltpu.VMEM((n_own, LANES), F32),
            pltpu.VMEM((GROUPS, 8, LANES), F32),
            pltpu.VMEM((2 * WIDE, LANES), F32),
            pltpu.SemaphoreType.DMA((2,)),
        ],
        compiler_params=PARAMS,
        cost_estimate=pl.CostEstimate(
            flops=2 * n_own * 9 * CHANS * LANES, bytes_accessed=4 * 1024 * 1024, transcendentals=n_own * CHANS
        ),
        name="conv_forward",
    )(pos, *slots, *extra, weights, *(() if first else (kept,)))


def below_kernel(layer, pool, total, count, *refs):
    pos, terms = refs[0], refs[1 : 1 + count]
    zc, side, gs = refs[1 + count : 4 + count]
    outs = refs[4 + count :]
    top = count == 1
    if top:
        h_out, dn_out, msg, tab = outs
    else:
        dn_out, msg, tab = outs
    n_own = zc.shape[0]
    rstd, own, oth = norm_tables(side, side.shape[0] - 8, total)
    tab[0:1], tab[1:2] = rstd, own
    tab[2:3], tab[3:4] = gs[layer : layer + 1, :], gs[layer + 8 : layer + 9, :]

    def body(j, accs):
        rows = pair_rows(j)
        xhat = zc[rows, :].astype(F32) * tab[0:1, :] + tab[1:2, :]
        n = xhat * tab[2:3, :] + tab[3:4, :]
        sig = sigmoid(n)
        h = n * sig
        g = functools.reduce(jnp.add, [term[rows, :].astype(F32) for term in terms])
        if pool:
            g = soft_pull(h, g)
        if top:
            h_out[rows, :] = h.astype(BF16)
        dn = g * (sig * (1.0 + n - h))
        dn_out[rows, :] = dn
        return accs[0] + fold(dn), accs[1] + fold(dn * xhat)

    zero = jnp.zeros((8, LANES), F32)
    sums = lax.fori_loop(0, n_own // (2 * WIDE), body, (zero, zero))
    sums = jnp.concatenate([jnp.sum(s, axis=0, keepdims=True) for s in sums], axis=0)
    write_message(msg, dn_out, sums, WIDE, pos[1])


def below_step(layer, pool, total, pos, terms, zc, side, gs):
    n_own = zc.shape[0]
    top = len(terms) == 1
    out_shape = [jax.ShapeDtypeStruct((n_own, LANES), F32), jax.ShapeDtypeStruct((WIDE + 8, LANES), F32)]
    if top:
        out_shape = [jax.ShapeDtypeStruct((n_own, LANES), BF16)] + out_shape
    return pl.pallas_call(
        functools.partial(below_kernel, layer, pool, total, len(terms)),
        out_shape=tuple(out_shape),
        in_specs=[SMEM] + [VMEM] * (3 + len(terms)),
        out_specs=(VMEM,) * len(out_shape),
        scratch_shapes=[pltpu.VMEM((8, LANES), F32)],
        compiler_params=PARAMS,
        cost_estimate=pl.CostEstimate(flops=40 * n_own * LANES, bytes_accessed=1024 * 1024, transcendentals=n_own * LANES),
        name="silu_backward",
    )(pos, *terms, zc, side, gs)


def bwd_kernel(layer, total, *refs):
    pos, dn, dside, zc, zside, gs, w_hbm = refs[:7]
    outs, d_out, d, w, y, tab, sem = refs[7:11], *refs[11:]
    load = pltpu.make_async_copy(w_hbm.at[layer], w, sem)
    load.start()
    t, r = pos[0], pos[1]
    n_own = dn.shape[0]
    halo_at = pl.multiple_of((1 - r) * (n_own + WIDE), WIDE)
    zero_at = pl.multiple_of(r * (n_own + WIDE), WIDE)
    edge = zside.shape[0] - 8
    d[pl.ds(zero_at, WIDE), :] = jnp.zeros((WIDE, 3 * LANES), BF16)
    rstd, own, oth = norm_tables(zside, edge, total)
    scale = gs[layer : layer + 1, :] * rstd
    shift_sum, gain_sum = dside[WIDE : WIDE + 1, :], dside[WIDE + 1 : WIDE + 2, :]
    slope = scale * gain_sum / total
    tab[0:1] = scale
    tab[1:2] = slope * rstd
    tab[2:3] = scale * shift_sum / total + slope * own
    tab[3:4] = scale * shift_sum / total + slope * oth

    def spread_columns(v, at):
        rows = v.shape[0]
        column = lax.broadcasted_iota(jnp.int32, v.shape, 0) % WIDE
        ahead = jnp.where(column == WIDE - 1, 0.0, pltpu.roll(v, rows - 1, 0))
        behind = jnp.where(column == 0, 0.0, pltpu.roll(v, 1, 0))
        d[pl.ds(at, rows), 0:128] = ahead.astype(BF16)
        d[pl.ds(at, rows), 128:256] = v.astype(BF16)
        d[pl.ds(at, rows), 256:384] = behind.astype(BF16)

    def body(j, carry):
        rows = pair_rows(j)
        v = dn[rows, :] * tab[0:1, :] - tab[2:3, :] - zc[rows, :].astype(F32) * tab[1:2, :]
        spread_columns(v, pl.multiple_of(j * 2 * WIDE + WIDE, WIDE))
        return carry

    lax.fori_loop(0, n_own // (2 * WIDE), body, 0)
    near = zside[0:WIDE, :] if edge == WIDE else zside[pl.ds(pl.multiple_of(r * WIDE, WIDE), WIDE), :]
    spread_columns(dside[0:WIDE, :] * tab[0:1, :] - tab[3:4, :] - near * tab[1:2, :], halo_at)
    d_out[...] = d[WIDE : WIDE + n_own, :]
    load.wait()
    lhs = jnp.concatenate([d[(2 - i) * WIDE : (2 - i) * WIDE + n_own, :] for i in range(3)], axis=1)
    rhs = jnp.concatenate([w[:, i * CHANS : (i + 1) * CHANS] for i in range(9)], axis=0)
    y[...] = jnp.dot(lhs, rhs, preferred_element_type=F32)

    def share(j, carry):
        rows = pair_rows(j)
        for k in range(GROUPS):
            outs[k][rows, :] = y[rows, pl.ds(lane_of(t ^ k), LANES)].astype(outs[k].dtype)
        return carry

    lax.fori_loop(0, n_own // (2 * WIDE), share, 0)


def bwd_step(layer, total, pos, dn, dside, zc, zside, gs, weights):
    n_own = dn.shape[0]
    part = jax.ShapeDtypeStruct((n_own, LANES), BF16)
    return pl.pallas_call(
        functools.partial(bwd_kernel, layer, total),
        out_shape=(
            jax.ShapeDtypeStruct((n_own, LANES), F32),
            part,
            part,
            part,
            jax.ShapeDtypeStruct((n_own, 3 * LANES), BF16),
        ),
        in_specs=[SMEM] + [VMEM] * 5 + [ANY],
        out_specs=(VMEM,) * 5,
        scratch_shapes=[
            pltpu.VMEM((n_own + 2 * WIDE, 3 * LANES), BF16),
            pltpu.VMEM((LANES, 9 * CHANS), BF16),
            pltpu.VMEM((n_own, CHANS), F32),
            pltpu.VMEM((8, LANES), F32),
            pltpu.SemaphoreType.DMA,
        ],
        compiler_params=PARAMS,
        cost_estimate=pl.CostEstimate(
            flops=2 * n_own * 9 * CHANS * LANES, bytes_accessed=4 * 1024 * 1024, transcendentals=0
        ),
        name="conv_backward",
    )(pos, dn, dside, zc, zside, gs, weights)


def last_kernel(*refs):
    terms, out = refs[:-1], refs[-1]

    def body(j, carry):
        rows = pair_rows(j)
        out[rows, :] = functools.reduce(jnp.add, [term[rows, :].astype(F32) for term in terms])
        return carry

    lax.fori_loop(0, out.shape[0] // (2 * WIDE), body, 0)


def last_step(terms):
    return pl.pallas_call(
        last_kernel,
        out_shape=jax.ShapeDtypeStruct(terms[0].shape, F32),
        in_specs=[VMEM] * len(terms),
        out_specs=VMEM,
        compiler_params=PARAMS,
        name="add_terms",
    )(*terms)


def wgrad_kernel(layer, pos, d, hb_hbm, keep, send, hb, grad, sem):
    load = pltpu.make_async_copy(hb_hbm.at[layer], hb, sem)
    load.start()
    n_own = d.shape[0]
    lhs = d[...]
    load.wait()
    for i in range(3):
        part = lax.dot_general(
            lhs, hb[i * WIDE : i * WIDE + n_own, :], (((0,), (0,)), ((), ())), preferred_element_type=F32
        ).astype(BF16)
        for s in range(3):
            grad[:, (3 * i + s) * CHANS : (3 * i + s + 1) * CHANS] = part[s * LANES : (s + 1) * LANES]
    half = LANES // 2
    keep[...] = grad[pl.ds(pl.multiple_of(pos[1] * half, half), half), :]
    send[...] = grad[pl.ds(pl.multiple_of((1 - pos[1]) * half, half), half), :]


def wgrad_step(layer, pos, d, kept):
    half = jax.ShapeDtypeStruct((LANES // 2, 9 * CHANS), BF16)
    return pl.pallas_call(
        functools.partial(wgrad_kernel, layer),
        out_shape=(half, half),
        in_specs=[SMEM, VMEM, ANY],
        out_specs=(VMEM, VMEM),
        scratch_shapes=[
            pltpu.VMEM(kept.shape[1:], BF16),
            pltpu.VMEM((LANES, 9 * CHANS), BF16),
            pltpu.SemaphoreType.DMA,
        ],
        compiler_params=PARAMS,
        cost_estimate=pl.CostEstimate(
            flops=2 * d.shape[0] * 9 * CHANS * LANES, bytes_accessed=3 * 1024 * 1024, transcendentals=0
        ),
        name="kernel_gradient",
    )(pos, d, kept)


def place_kernel(pos, mine, other, *refs):
    refs[-1][0] = jnp.where(pl.program_id(0) == pos[1], mine[...], other[...]).astype(F32)


def place_step(layer, pos, mine, other, whole, layers):
    half = LANES // 2
    block = pl.BlockSpec((half, 9 * CHANS), lambda i: (0, 0))
    return pl.pallas_call(
        place_kernel,
        grid=(2,),
        out_shape=jax.ShapeDtypeStruct((layers, LANES, 9 * CHANS), F32),
        in_specs=[SMEM, block, block] + ([] if whole is None else [ANY]),
        out_specs=pl.BlockSpec((1, half, 9 * CHANS), lambda i: (layer, i, 0)),
        input_output_aliases={} if whole is None else {3: 0},
        compiler_params=PARAMS,
        cost_estimate=pl.CostEstimate(flops=0, bytes_accessed=4 * 1024 * 1024, transcendentals=0),
        name="place_gradient",
    )(pos, mine, other, *(() if whole is None else (whole,)))


def swap_with(value, axis, k):
    return lax.ppermute(value, axis, [(i, i ^ k) for i in range(lax.axis_size(axis))])


def spread(own):
    return (own, *[swap_with(own, "tensor", k) for k in range(1, GROUPS)])


def pair_moments(mine, got, count):
    mean = 0.5 * (mine[0:1] + got[0:1])
    apart = mine[1:2] + got[1:2] + (0.5 * count) * jnp.square(got[0:1] - mine[0:1])
    return mean, apart


def share_moments(msg, edge, count):
    got = swap_with(msg, "rows", 1)
    mine, other = msg[edge:], got[edge:]
    mean, apart = pair_moments(mine, other, count)
    sums = jnp.concatenate([mean, apart, mine[2:3], other[2:3], mine[4:]], axis=0)
    for k in (1, 2):
        other = swap_with(sums, "dp", k)
        mean, apart = pair_moments(sums, other, 2 * k * count)
        sums = jnp.concatenate([mean, apart, sums[2:]], axis=0)
    return jnp.concatenate([got[:edge], sums], axis=0)


def share_sums(msg, edge):
    got = swap_with(msg, "rows", 1)
    sums = lax.psum(msg[edge:] + got[edge:], "dp")
    return jnp.concatenate([got[:edge], sums], axis=0)


def halo_of_input(x, half):
    n_own = x.shape[0]
    edge = jnp.where(half == 0, x[n_own - WIDE :], x[:WIDE])
    return jnp.concatenate([x, swap_with(edge, "rows", 1)], axis=0)


def fast_local(section_input, conv_weights, norm_gains, norm_shifts, out_grad, out_mask):
    images, rows_here, width = out_mask.shape
    layers = conv_weights.shape[0]
    n_own = rows_here * width
    parts = lax.axis_size("dp") * lax.axis_size("rows")
    total = float(n_own * parts)
    t, half = lax.axis_index("tensor"), lax.axis_index("rows")
    pos = jnp.stack([t, half]).astype(jnp.int32)
    middle = layers // 2
    x = to_maps(section_input, width).reshape(n_own, LANES)
    slots = spread(halo_of_input(x, half))
    pad = jnp.zeros((8 - layers, LANES), F32)
    tables = spread(jnp.concatenate([norm_gains, pad, norm_shifts, pad], axis=0))
    top_grad = (to_maps(out_grad, width) * out_mask[..., None].astype(BF16)).reshape(n_own, LANES)

    sides, kept = None, None
    kept_z, kept_side = [], []
    for layer in range(layers):
        edge = 2 * WIDE if layer + 1 == middle else WIDE
        kept, zc, msg = fwd_step(
            layer, layer == middle, edge, total, pos, slots, sides, tables, conv_weights, kept, n_own
        )
        side = share_moments(msg, edge, float(n_own))
        kept_z.append(zc)
        kept_side.append(side)
        if layer + 1 < layers:
            slots = spread(zc)
            sides = spread(side)
    top = layers - 1
    h_last, dn, msg = below_step(top, False, total, pos, (top_grad,), kept_z[top], kept_side[top], tables[0])
    sum_list = [None] * layers
    whole, before = None, None
    for layer in range(layers - 1, -1, -1):
        dside = share_sums(msg, WIDE)
        sum_list[layer] = dside[WIDE : WIDE + 2]
        *terms, d = bwd_step(
            layer, total, pos, dn, dside, kept_z[layer], kept_side[layer], tables[0], conv_weights
        )
        terms = (terms[0], *[swap_with(terms[k], "tensor", k) for k in range(1, GROUPS)])
        if layer > 0:
            dn, msg = below_step(
                layer - 1, layer == middle, total, pos, terms, kept_z[layer - 1], kept_side[layer - 1], tables[0]
            )
        else:
            grad = last_step(terms)
        keep, send = wgrad_step(layer, pos, d, kept)
        pair = keep + swap_with(send, "rows", 1)
        if before is not None:
            pair, before = lax.optimization_barrier((pair, before))
            whole = place_step(layer + 1, pos, before, swap_with(before, "rows", 1), whole, layers)
        before = lax.psum(pair, "dp")
    whole = place_step(0, pos, before, swap_with(before, "rows", 1), whole, layers)
    sums = jnp.stack(sum_list)
    shape = (images, rows_here, width, LANES)
    return (
        from_maps(h_last.reshape(shape)),
        from_maps(grad.reshape(shape)),
        whole,
        sums[:, 1],
        sums[:, 0],
    )


def solution(mesh):
    in_specs = (
        P("dp", "rows", "tensor"),
        P(None, "tensor", None),
        P(None, "tensor"),
        P(None, "tensor"),
        P("dp", "rows", "tensor"),
        P("dp", "rows", None),
    )
    out_specs = (
        P("dp", "rows", "tensor"),
        P("dp", "rows", "tensor"),
        P(None, "tensor", None),
        P(None, "tensor"),
        P(None, "tensor"),
    )
    local = fast_local if fits_kernels(mesh) else generic_local
    return jax.shard_map(local, mesh=mesh, in_specs=in_specs, out_specs=out_specs, check_vma=False)
```

```python
import functools

import jax
import jax.numpy as jnp
from jax import lax
from jax.experimental import pallas as pl
from jax.experimental.pallas import tpu as pltpu
from jax.sharding import PartitionSpec as P

EPS = 1e-05


def padded_2(cells, sides, width):
    for axis, dim in sides:
        count = lax.axis_size(axis)
        ends = count - 1
        head = lax.slice_in_dim(cells, 0, width, axis=dim)
        tail = lax.slice_in_dim(cells, cells.shape[dim] - width, cells.shape[dim], axis=dim)
        cells = jnp.concatenate(
            [
                lax.ppermute(tail, axis, [(i, (i + 1) % count) for i in range(ends)]),
                cells,
                lax.ppermute(head, axis, [((i + 1) % count, i) for i in range(ends)]),
            ],
            axis=dim,
        )
    return cells


def to_maps(flat, width):
    count, high, merged = flat.shape
    return flat.reshape(count, high, merged // width, width).transpose(0, 1, 3, 2)


def from_maps(maps):
    count, high, wide, chans = maps.shape
    return maps.transpose(0, 1, 3, 2).reshape(count, high, chans * wide)


def spatial_conv(padded, kernel):
    return lax.conv_general_dilated(
        padded,
        kernel,
        (1, 1),
        ((0, 0), (1, 1)),
        dimension_numbers=("NHWC", "HWIO", "NHWC"),
        preferred_element_type=jnp.float32,
    )


def flipped(kernel):
    return jnp.transpose(kernel[::-1, ::-1], (0, 1, 3, 2))


def pool_unpool(values):
    count, high, wide, chans = values.shape
    blocks = values.reshape(count, high // 2, 2, wide // 2, 2, chans)
    pooled = jax.nn.logsumexp(blocks, axis=(2, 4), keepdims=True)
    return (jnp.exp(blocks - pooled) * pooled).reshape(values.shape)


def moments(conv_out, total_pixels):
    summed = lax.psum(jnp.sum(conv_out, axis=(0, 1, 2)), ("dp", "rows"))
    mean = summed / total_pixels
    spread = lax.psum(jnp.sum(jnp.square(conv_out - mean), axis=(0, 1, 2)), ("dp", "rows"))
    var = spread / total_pixels
    return (mean, lax.rsqrt(var + EPS))


def kernel_grad(whole, dconv):
    images, rows_here, width, chans = dconv.shape
    widened = jnp.pad(whole, ((0, 0), (0, 0), (1, 1), (0, 0)))
    stacked = []
    for row_off in range(3):
        line = []
        for col_off in range(3):
            window = widened[:, row_off : row_off + rows_here, col_off : col_off + width, :]
            line.append(
                jnp.einsum("bhwc,bhwo->co", window, dconv, preferred_element_type=jnp.float32)
            )
        stacked.append(jnp.stack(line))
    return jnp.stack(stacked)


def generic_local(section_input, conv_weights, norm_gains, norm_shifts, out_grad, out_mask):
    width = out_mask.shape[2]
    images, rows_here = (out_mask.shape[0], out_mask.shape[1])
    total_pixels = float(images * rows_here * width * lax.axis_size("dp") * lax.axis_size("rows"))
    layers, out_here, flat_in = conv_weights.shape
    chans_in = flat_in // 9
    kernels_hwio = conv_weights.reshape(layers, out_here, 3, 3, chans_in).transpose(0, 2, 3, 4, 1)
    middle = layers // 2
    kept = []
    acting = to_maps(section_input, width)
    current = acting.astype(jnp.float32)
    pre_pool = current
    for index in range(layers):
        if index == middle:
            pre_pool = current
            acting = pool_unpool(pre_pool).astype(jnp.bfloat16)
        padded = padded_2(acting, (("rows", 1),), 1)
        whole = lax.all_gather(padded, "tensor", axis=3, tiled=True)
        conv_out = spatial_conv(whole, kernels_hwio[index])
        mean, rstd = moments(conv_out, total_pixels)
        normed = (conv_out - mean) * rstd
        shifted = normed * norm_gains[index] + norm_shifts[index]
        current = jax.nn.silu(shifted)
        acting = current.astype(jnp.bfloat16)
        kept.append((whole, normed, shifted, rstd))
    grad = to_maps(out_grad, width).astype(jnp.float32) * out_mask[..., None].astype(jnp.float32)
    kernel_list = [None] * layers
    gain_list = [None] * layers
    shift_list = [None] * layers
    for index in range(layers - 1, -1, -1):
        whole, normed, shifted, rstd = kept[index]
        unused, pull_silu = jax.vjp(jax.nn.silu, shifted)
        dshift = pull_silu(grad)[0]
        gain_sum, shift_sum = lax.psum(
            (jnp.sum(dshift * normed, axis=(0, 1, 2)), jnp.sum(dshift, axis=(0, 1, 2))),
            ("dp", "rows"),
        )
        gain_list[index] = gain_sum
        shift_list[index] = shift_sum
        dconv = (
            norm_gains[index]
            * rstd
            * (dshift - shift_sum / total_pixels - normed * gain_sum / total_pixels)
        ).astype(jnp.bfloat16)
        summed_kernel = lax.psum(
            kernel_grad(whole, dconv).astype(jnp.bfloat16), ("dp", "rows")
        ).astype(jnp.float32)
        kernel_list[index] = summed_kernel.transpose(3, 0, 1, 2).reshape(out_here, flat_in)
        grad_rim = padded_2(dconv, (("rows", 1),), 1)
        partial_terms = spatial_conv(grad_rim, flipped(kernels_hwio[index]))
        grad_in = lax.psum_scatter(
            partial_terms.astype(jnp.bfloat16), "tensor", scatter_dimension=3, tiled=True
        ).astype(jnp.float32)
        if index == middle:
            unused, pull_pool = jax.vjp(pool_unpool, pre_pool)
            grad = pull_pool(grad_in)[0]
        else:
            grad = grad_in
    return (
        from_maps(acting),
        from_maps(grad),
        jnp.stack(kernel_list),
        jnp.stack(gain_list),
        jnp.stack(shift_list),
    )


GROUPS = 4
LANES = 128
WIDE = 48
CHANS = GROUPS * LANES
F32 = jnp.float32
BF16 = jnp.bfloat16
VMEM = pl.BlockSpec(memory_space=pltpu.VMEM)
SMEM = pl.BlockSpec(memory_space=pltpu.SMEM)
ANY = pl.BlockSpec(memory_space=pltpu.HBM)
PARAMS = pltpu.CompilerParams(vmem_limit_bytes=20 * 1024 * 1024)


def in_hbm(value):
    return pltpu.with_memory_space_constraint(value, pltpu.HBM)


def fits_kernels(mesh):
    return mesh.shape["tensor"] == GROUPS and mesh.shape["rows"] == 2 and mesh.shape["dp"] == 4


def sigmoid(v):
    return 0.5 * jnp.tanh(0.5 * v) + 0.5


def swap_columns(v):
    column = lax.broadcasted_iota(jnp.int32, v.shape, 0)
    return jnp.where(column % 2 == 0, pltpu.roll(v, WIDE - 1, 0), pltpu.roll(v, 1, 0))


def soft_parts(h):
    top = jnp.maximum(h[0], h[1])
    top = jnp.maximum(top, swap_columns(top))
    e0, e1 = jnp.exp(h[0] - top), jnp.exp(h[1] - top)
    total = e0 + e1
    total = total + swap_columns(total)
    pooled = top + jnp.log(total)
    inverse = 1.0 / total
    return e0 * inverse, e1 * inverse, pooled


def soft(h):
    h = h.reshape(2, WIDE, LANES)
    q0, q1, pooled = soft_parts(h)
    return jnp.concatenate([q0 * pooled, q1 * pooled], axis=0)


def soft_pull(h, grad):
    h = h.reshape(2, WIDE, LANES)
    grad = grad.reshape(2, WIDE, LANES)
    q0, q1, pooled = soft_parts(h)
    mix = q0 * grad[0] + q1 * grad[1]
    mix = mix + swap_columns(mix)
    return jnp.concatenate(
        [q0 * (pooled * (grad[0] - mix) + mix), q1 * (pooled * (grad[1] - mix) + mix)], axis=0
    )


def norm_tables(st_ref, at, total):
    mean, spread, own, oth = (st_ref[at + i : at + i + 1, :] for i in range(4))
    rstd = lax.rsqrt(spread / total + EPS)
    return rstd, (own - mean) * rstd, (oth - mean) * rstd


def left_right(y0, y1, y2):
    rows = y0.shape[0]
    column = lax.broadcasted_iota(jnp.int32, y0.shape, 0) % WIDE
    before = jnp.where(column == 0, 0.0, pltpu.roll(y0, 1, 0))
    after = jnp.where(column == WIDE - 1, 0.0, pltpu.roll(y2, rows - 1, 0))
    return before + y1 + after


def lane_of(group):
    return pl.multiple_of(group * LANES, LANES)


def write_message(msg, own, sums, edge, half):
    n_own = own.shape[0]
    start = pl.multiple_of((1 - half) * (n_own - edge), WIDE)
    msg[0:edge, :] = own[pl.ds(start, edge), :].astype(F32)
    msg[edge : edge + 8, :] = jnp.concatenate([sums, jnp.zeros((8 - sums.shape[0], LANES), F32)], axis=0)


def pair_rows(j):
    return pl.ds(pl.multiple_of(j * 2 * WIDE, 2 * WIDE), 2 * WIDE)


def fold(v):
    return jnp.sum(v.reshape(v.shape[0] // 8, 8, LANES), axis=0)


def fwd_kernel(first, pool, layer, total, edge_out, *refs):
    pos, zs = refs[0], refs[1:5]
    if first:
        w_hbm, rest = refs[5], refs[6:]
    else:
        sides, gss, w_hbm, rest = refs[5:9], refs[9:13], refs[13], refs[15:]
    hb_out, zc_out, msg, hb, w, y, z, tab, hs, sem = rest
    load = pltpu.make_async_copy(w_hbm.at[layer], w, sem.at[0])
    load.start()
    save = pltpu.make_async_copy(hb, hb_out.at[layer], sem.at[1])
    t, r = pos[0], pos[1]
    n_own = z.shape[0]
    halo_at = pl.multiple_of((1 - r) * (n_own + WIDE), WIDE)
    zero_at = pl.multiple_of(r * (n_own + WIDE), WIDE)
    hb[pl.ds(zero_at, WIDE), :] = jnp.zeros((WIDE, CHANS), BF16)
    if not first:
        edge = sides[0].shape[0] - 8
        for k in range(GROUPS):
            rstd, own, oth = norm_tables(sides[k], edge, total)
            gain, shift = gss[k][layer - 1 : layer, :], gss[k][layer + 7 : layer + 8, :]
            tab[k, 0:1] = rstd * gain
            tab[k, 1:2] = own * gain + shift
            tab[k, 2:3] = oth * gain + shift

    def act(values, k, which):
        if first:
            return values
        n = values.astype(F32) * tab[k, 0:1, :] + tab[k, which : which + 1, :]
        h = n * sigmoid(n)
        return soft(h) if pool else h

    def body(j, carry):
        at = pl.multiple_of(j * 2 * WIDE, 2 * WIDE)
        for k in range(GROUPS):
            h = act(zs[k][pl.ds(at, 2 * WIDE), :], k, 1)
            hb[pl.ds(pl.multiple_of(at + WIDE, WIDE), 2 * WIDE), pl.ds(lane_of(t ^ k), LANES)] = h.astype(BF16)
        return carry

    lax.fori_loop(0, n_own // (2 * WIDE), body, 0)
    for k in range(GROUPS):
        if first:
            h = zs[k][n_own : n_own + WIDE, :]
        else:
            h = act(sides[k][0:edge, :], k, 2)
            if edge > WIDE:
                hs[...] = h
                h = hs[pl.ds(pl.multiple_of(r * WIDE, WIDE), WIDE), :]
        hb[pl.ds(halo_at, WIDE), pl.ds(lane_of(t ^ k), LANES)] = h.astype(BF16)
    save.start()
    load.wait()
    lhs = jnp.concatenate([hb[i * WIDE : i * WIDE + n_own, :] for i in range(3)], axis=1)
    rhs = jnp.concatenate(
        [
            jnp.concatenate([w[:, (3 * i + s) * CHANS : (3 * i + s + 1) * CHANS] for i in range(3)], axis=1)
            for s in range(3)
        ],
        axis=0,
    )
    y[...] = lax.dot_general(lhs, rhs, (((1,), (1,)), ((), ())), preferred_element_type=F32)

    def add_up(j, acc):
        rows = pair_rows(j)
        v = left_right(y[rows, 0:128], y[rows, 128:256], y[rows, 256:384])
        z[rows, :] = v
        return acc + fold(v)

    steps = n_own // (2 * WIDE)
    summed = lax.fori_loop(0, steps, add_up, jnp.zeros((8, LANES), F32))
    mean = jnp.sum(summed, axis=0, keepdims=True) / n_own

    def centre(j, acc):
        rows = pair_rows(j)
        v = z[rows, :] - mean
        z[rows, :] = v
        zc_out[rows, :] = v.astype(BF16)
        return acc + fold(jnp.square(v))

    apart = lax.fori_loop(0, steps, centre, jnp.zeros((8, LANES), F32))
    sums = [mean, jnp.sum(apart, axis=0, keepdims=True), mean, jnp.zeros((1, LANES), F32)]
    write_message(msg, z, jnp.concatenate(sums, axis=0), edge_out, r)
    save.wait()


def fwd_step(layer, pool, edge_out, total, pos, slots, sides, tables, weights, kept, n_own):
    first = sides is None
    layers = weights.shape[0]
    extra = () if first else (*sides, *tables)
    return pl.pallas_call(
        functools.partial(fwd_kernel, first, pool, layer, total, edge_out),
        out_shape=(
            pltpu.HBM((layers, n_own + 2 * WIDE, CHANS), BF16),
            pltpu.VMEM((n_own, LANES), BF16),
            pltpu.VMEM((edge_out + 8, LANES), F32),
        ),
        in_specs=[SMEM] + [VMEM] * (4 + len(extra)) + [ANY] * (1 if first else 2),
        out_specs=(ANY, VMEM, VMEM),
        input_output_aliases={} if first else {6 + len(extra): 0},
        scratch_shapes=[
            pltpu.VMEM((n_own + 2 * WIDE, CHANS), BF16),
            pltpu.VMEM((LANES, 9 * CHANS), BF16),
            pltpu.VMEM((n_own, 3 * LANES), F32),
            pltpu.VMEM((n_own, LANES), F32),
            pltpu.VMEM((GROUPS, 8, LANES), F32),
            pltpu.VMEM((2 * WIDE, LANES), F32),
            pltpu.SemaphoreType.DMA((2,)),
        ],
        compiler_params=PARAMS,
        cost_estimate=pl.CostEstimate(
            flops=2 * n_own * 9 * CHANS * LANES, bytes_accessed=4 * 1024 * 1024, transcendentals=n_own * CHANS
        ),
        name="conv_forward",
    )(pos, *slots, *extra, in_hbm(weights), *(() if first else (in_hbm(kept),)))


def below_kernel(layer, pool, total, count, *refs):
    pos, terms = refs[0], refs[1 : 1 + count]
    zc, side, gs = refs[1 + count : 4 + count]
    top = count == 1
    if top:
        h_out, dn_out, msg, tab = refs[4 + count :]
    else:
        keep, got, dn_out, msg, pair, tab = refs[4 + count :]
        pair[...] = (keep[...].astype(F32) + got[...].astype(F32)).astype(BF16)
    n_own = zc.shape[0]
    rstd, own, oth = norm_tables(side, side.shape[0] - 8, total)
    tab[0:1], tab[1:2] = rstd, own
    tab[2:3], tab[3:4] = gs[layer : layer + 1, :], gs[layer + 8 : layer + 9, :]

    def body(j, accs):
        rows = pair_rows(j)
        xhat = zc[rows, :].astype(F32) * tab[0:1, :] + tab[1:2, :]
        n = xhat * tab[2:3, :] + tab[3:4, :]
        sig = sigmoid(n)
        h = n * sig
        g = functools.reduce(jnp.add, [term[rows, :].astype(F32) for term in terms])
        if pool:
            g = soft_pull(h, g)
        if top:
            h_out[rows, :] = h.astype(BF16)
        dn = g * (sig * (1.0 + n - h))
        dn_out[rows, :] = dn
        return accs[0] + fold(dn), accs[1] + fold(dn * xhat)

    zero = jnp.zeros((8, LANES), F32)
    sums = lax.fori_loop(0, n_own // (2 * WIDE), body, (zero, zero))
    sums = jnp.concatenate([jnp.sum(s, axis=0, keepdims=True) for s in sums], axis=0)
    write_message(msg, dn_out, sums, WIDE, pos[1])


def below_step(layer, pool, total, pos, terms, zc, side, gs, halves=()):
    n_own = zc.shape[0]
    top = len(terms) == 1
    out_shape = [pltpu.VMEM((n_own, LANES), F32), pltpu.VMEM((WIDE + 8, LANES), F32)]
    if top:
        out_shape = [jax.ShapeDtypeStruct((n_own, LANES), BF16)] + out_shape
    else:
        out_shape = out_shape + [jax.ShapeDtypeStruct(halves[0].shape, BF16)]
    return pl.pallas_call(
        functools.partial(below_kernel, layer, pool, total, len(terms)),
        out_shape=tuple(out_shape),
        in_specs=[SMEM] + [VMEM] * (3 + len(terms) + len(halves)),
        out_specs=(VMEM,) * len(out_shape),
        scratch_shapes=[pltpu.VMEM((8, LANES), F32)],
        compiler_params=PARAMS,
        cost_estimate=pl.CostEstimate(flops=40 * n_own * LANES, bytes_accessed=1024 * 1024, transcendentals=n_own * LANES),
        name="silu_backward",
    )(pos, *terms, zc, side, gs, *halves)


def bwd_kernel(layer, total, *refs):
    pos, dn, dside, zc, zside, gs, w_hbm = refs[:7]
    outs, d_out, d, w, y, tab, sem = refs[7:11], *refs[11:]
    load = pltpu.make_async_copy(w_hbm.at[layer], w, sem)
    load.start()
    t, r = pos[0], pos[1]
    n_own = dn.shape[0]
    halo_at = pl.multiple_of((1 - r) * (n_own + WIDE), WIDE)
    zero_at = pl.multiple_of(r * (n_own + WIDE), WIDE)
    edge = zside.shape[0] - 8
    d[pl.ds(zero_at, WIDE), :] = jnp.zeros((WIDE, 3 * LANES), BF16)
    rstd, own, oth = norm_tables(zside, edge, total)
    scale = gs[layer : layer + 1, :] * rstd
    shift_sum, gain_sum = dside[WIDE : WIDE + 1, :], dside[WIDE + 1 : WIDE + 2, :]
    slope = scale * gain_sum / total
    tab[0:1] = scale
    tab[1:2] = slope * rstd
    tab[2:3] = scale * shift_sum / total + slope * own
    tab[3:4] = scale * shift_sum / total + slope * oth

    def spread_columns(v, at):
        rows = v.shape[0]
        column = lax.broadcasted_iota(jnp.int32, v.shape, 0) % WIDE
        ahead = jnp.where(column == WIDE - 1, 0.0, pltpu.roll(v, rows - 1, 0))
        behind = jnp.where(column == 0, 0.0, pltpu.roll(v, 1, 0))
        d[pl.ds(at, rows), 0:128] = ahead.astype(BF16)
        d[pl.ds(at, rows), 128:256] = v.astype(BF16)
        d[pl.ds(at, rows), 256:384] = behind.astype(BF16)

    def body(j, carry):
        rows = pair_rows(j)
        v = dn[rows, :] * tab[0:1, :] - tab[2:3, :] - zc[rows, :].astype(F32) * tab[1:2, :]
        spread_columns(v, pl.multiple_of(j * 2 * WIDE + WIDE, WIDE))
        return carry

    lax.fori_loop(0, n_own // (2 * WIDE), body, 0)
    near = zside[0:WIDE, :] if edge == WIDE else zside[pl.ds(pl.multiple_of(r * WIDE, WIDE), WIDE), :]
    spread_columns(dside[0:WIDE, :] * tab[0:1, :] - tab[3:4, :] - near * tab[1:2, :], halo_at)
    d_out[...] = d[WIDE : WIDE + n_own, :]
    load.wait()
    lhs = jnp.concatenate([d[(2 - i) * WIDE : (2 - i) * WIDE + n_own, :] for i in range(3)], axis=1)
    rhs = jnp.concatenate([w[:, i * CHANS : (i + 1) * CHANS] for i in range(9)], axis=0)
    y[...] = jnp.dot(lhs, rhs, preferred_element_type=F32)

    def share(j, carry):
        rows = pair_rows(j)
        for k in range(GROUPS):
            outs[k][rows, :] = y[rows, pl.ds(lane_of(t ^ k), LANES)].astype(outs[k].dtype)
        return carry

    lax.fori_loop(0, n_own // (2 * WIDE), share, 0)


def bwd_step(layer, total, pos, dn, dside, zc, zside, gs, weights):
    n_own = dn.shape[0]
    part = pltpu.VMEM((n_own, LANES), BF16)
    return pl.pallas_call(
        functools.partial(bwd_kernel, layer, total),
        out_shape=(
            pltpu.VMEM((n_own, LANES), F32),
            part,
            part,
            part,
            pltpu.VMEM((n_own, 3 * LANES), BF16),
        ),
        in_specs=[SMEM] + [VMEM] * 5 + [ANY],
        out_specs=(VMEM,) * 5,
        scratch_shapes=[
            pltpu.VMEM((n_own + 2 * WIDE, 3 * LANES), BF16),
            pltpu.VMEM((LANES, 9 * CHANS), BF16),
            pltpu.VMEM((n_own, CHANS), F32),
            pltpu.VMEM((8, LANES), F32),
            pltpu.SemaphoreType.DMA,
        ],
        compiler_params=PARAMS,
        cost_estimate=pl.CostEstimate(
            flops=2 * n_own * 9 * CHANS * LANES, bytes_accessed=4 * 1024 * 1024, transcendentals=0
        ),
        name="conv_backward",
    )(pos, dn, dside, zc, zside, gs, in_hbm(weights))


def last_kernel(*refs):
    terms, (keep, got, out, pair) = refs[:-4], refs[-4:]
    pair[...] = (keep[...].astype(F32) + got[...].astype(F32)).astype(BF16)

    def body(j, carry):
        rows = pair_rows(j)
        out[rows, :] = functools.reduce(jnp.add, [term[rows, :].astype(F32) for term in terms])
        return carry

    lax.fori_loop(0, out.shape[0] // (2 * WIDE), body, 0)


def last_step(terms, halves):
    return pl.pallas_call(
        last_kernel,
        out_shape=(jax.ShapeDtypeStruct(terms[0].shape, F32), jax.ShapeDtypeStruct(halves[0].shape, BF16)),
        in_specs=[VMEM] * (len(terms) + 2),
        out_specs=(VMEM, VMEM),
        compiler_params=PARAMS,
        name="add_terms",
    )(*terms, *halves)


def wgrad_kernel(layer, pos, d, hb_hbm, keep, send, hb, grad, sem):
    load = pltpu.make_async_copy(hb_hbm.at[layer], hb, sem)
    load.start()
    n_own = d.shape[0]
    lhs = d[...]
    load.wait()
    for i in range(3):
        part = lax.dot_general(
            lhs, hb[i * WIDE : i * WIDE + n_own, :], (((0,), (0,)), ((), ())), preferred_element_type=F32
        ).astype(BF16)
        for s in range(3):
            grad[:, (3 * i + s) * CHANS : (3 * i + s + 1) * CHANS] = part[s * LANES : (s + 1) * LANES]
    half = LANES // 2
    keep[...] = grad[pl.ds(pl.multiple_of(pos[1] * half, half), half), :]
    send[...] = grad[pl.ds(pl.multiple_of((1 - pos[1]) * half, half), half), :]


def wgrad_step(layer, pos, d, kept):
    half = pltpu.VMEM((LANES // 2, 9 * CHANS), BF16)
    return pl.pallas_call(
        functools.partial(wgrad_kernel, layer),
        out_shape=(half, half),
        in_specs=[SMEM, VMEM, ANY],
        out_specs=(VMEM, VMEM),
        scratch_shapes=[
            pltpu.VMEM(kept.shape[1:], BF16),
            pltpu.VMEM((LANES, 9 * CHANS), BF16),
            pltpu.SemaphoreType.DMA,
        ],
        compiler_params=PARAMS,
        cost_estimate=pl.CostEstimate(
            flops=2 * d.shape[0] * 9 * CHANS * LANES, bytes_accessed=3 * 1024 * 1024, transcendentals=0
        ),
        name="kernel_gradient",
    )(pos, d, in_hbm(kept))


def place_kernel(pos, mine, other, *refs):
    refs[-1][0] = jnp.where(pl.program_id(0) == pos[1], mine[...], other[...]).astype(F32)


def place_step(layer, pos, mine, other, whole, layers):
    half = LANES // 2
    block = pl.BlockSpec((half, 9 * CHANS), lambda i: (0, 0))
    return pl.pallas_call(
        place_kernel,
        grid=(2,),
        out_shape=jax.ShapeDtypeStruct((layers, LANES, 9 * CHANS), F32),
        in_specs=[SMEM, block, block] + ([] if whole is None else [ANY]),
        out_specs=pl.BlockSpec((1, half, 9 * CHANS), lambda i: (layer, i, 0)),
        input_output_aliases={} if whole is None else {3: 0},
        compiler_params=PARAMS,
        cost_estimate=pl.CostEstimate(flops=0, bytes_accessed=4 * 1024 * 1024, transcendentals=0),
        name="place_gradient",
    )(pos, mine, other, *(() if whole is None else (whole,)))


def swap_with(value, axis, k):
    return lax.ppermute(value, axis, [(i, i ^ k) for i in range(lax.axis_size(axis))])


def spread(own):
    return (own, *[swap_with(own, "tensor", k) for k in range(1, GROUPS)])


def pair_moments(mine, got, count):
    mean = 0.5 * (mine[0:1] + got[0:1])
    apart = mine[1:2] + got[1:2] + (0.5 * count) * jnp.square(got[0:1] - mine[0:1])
    return mean, apart


def share_moments(msg, edge, count):
    got = swap_with(msg, "rows", 1)
    mine, other = msg[edge:], got[edge:]
    mean, apart = pair_moments(mine, other, count)
    sums = jnp.concatenate([mean, apart, mine[2:3], other[2:3], mine[4:]], axis=0)
    for k in (1, 2):
        other = swap_with(sums, "dp", k)
        mean, apart = pair_moments(sums, other, 2 * k * count)
        sums = jnp.concatenate([mean, apart, sums[2:]], axis=0)
    return jnp.concatenate([got[:edge], sums], axis=0)


def share_sums(msg, edge):
    got = swap_with(msg, "rows", 1)
    sums = msg[edge:] + got[edge:]
    for k in (1, 2):
        sums = sums + swap_with(sums, "dp", k)
    return jnp.concatenate([got[:edge], sums], axis=0)


def halo_of_input(x, half):
    n_own = x.shape[0]
    edge = jnp.where(half == 0, x[n_own - WIDE :], x[:WIDE])
    return jnp.concatenate([x, swap_with(edge, "rows", 1)], axis=0)


def fast_local(section_input, conv_weights, norm_gains, norm_shifts, out_grad, out_mask):
    images, rows_here, width = out_mask.shape
    layers = conv_weights.shape[0]
    n_own = rows_here * width
    parts = lax.axis_size("dp") * lax.axis_size("rows")
    total = float(n_own * parts)
    t, half = lax.axis_index("tensor"), lax.axis_index("rows")
    pos = jnp.stack([t, half]).astype(jnp.int32)
    middle = layers // 2
    x = to_maps(section_input, width).reshape(n_own, LANES)
    slots = spread(halo_of_input(x, half))
    pad = jnp.zeros((8 - layers, LANES), F32)
    tables = spread(jnp.concatenate([norm_gains, pad, norm_shifts, pad], axis=0))
    top_grad = (to_maps(out_grad, width) * out_mask[..., None].astype(BF16)).reshape(n_own, LANES)

    sides, kept = None, None
    kept_z, kept_side = [], []
    for layer in range(layers):
        edge = 2 * WIDE if layer + 1 == middle else WIDE
        kept, zc, msg = fwd_step(
            layer, layer == middle, edge, total, pos, slots, sides, tables, conv_weights, kept, n_own
        )
        side = share_moments(msg, edge, float(n_own))
        kept_z.append(zc)
        kept_side.append(side)
        if layer + 1 < layers:
            slots = spread(zc)
            sides = spread(side)
    top = layers - 1
    h_last, dn, msg = below_step(top, False, total, pos, (top_grad,), kept_z[top], kept_side[top], tables[0])
    sum_list = [None] * layers
    pairs = [None] * layers
    for layer in range(layers - 1, -1, -1):
        dside = share_sums(msg, WIDE)
        sum_list[layer] = dside[WIDE : WIDE + 2]
        *terms, d = bwd_step(
            layer, total, pos, dn, dside, kept_z[layer], kept_side[layer], tables[0], conv_weights
        )
        terms = (terms[0], *[swap_with(terms[k], "tensor", k) for k in range(1, GROUPS)])
        keep, send = wgrad_step(layer, pos, d, kept)
        halves = (keep, swap_with(send, "rows", 1))
        if layer > 0:
            below = layer - 1
            dn, msg, pairs[layer] = below_step(
                below, layer == middle, total, pos, terms, kept_z[below], kept_side[below], tables[0], halves
            )
        else:
            grad, pairs[layer] = last_step(terms, halves)
    ahead, back = [[0, 1, 2, 3]], [[3, 2, 1, 0]]
    upper = lax.psum((pairs[5], pairs[4]), "dp", axis_index_groups=ahead)
    mid = lax.psum((pairs[3], pairs[2]), "dp", axis_index_groups=back)
    tied, upper = lax.optimization_barrier(((pairs[1], pairs[0]), upper))
    lower = lax.psum(tied, "dp", axis_index_groups=ahead)
    whole = None
    for layer, mine in zip((5, 4, 3, 2, 1, 0), (*upper, *mid, *lower)):
        whole = place_step(layer, pos, mine, swap_with(mine, "rows", 1), whole, layers)
    sums = jnp.stack(sum_list)
    shape = (images, rows_here, width, LANES)
    return (
        from_maps(h_last.reshape(shape)),
        from_maps(grad.reshape(shape)),
        whole,
        sums[:, 1],
        sums[:, 0],
    )


def solution(mesh):
    in_specs = (
        P("dp", "rows", "tensor"),
        P(None, "tensor", None),
        P(None, "tensor"),
        P(None, "tensor"),
        P("dp", "rows", "tensor"),
        P("dp", "rows", None),
    )
    out_specs = (
        P("dp", "rows", "tensor"),
        P("dp", "rows", "tensor"),
        P(None, "tensor", None),
        P(None, "tensor"),
        P(None, "tensor"),
    )
    local = fast_local if fits_kernels(mesh) else generic_local
    return jax.shard_map(local, mesh=mesh, in_specs=in_specs, out_specs=out_specs, check_vma=False)
```

```python
import functools

import jax
import jax.numpy as jnp
from jax import lax
from jax.experimental import pallas as pl
from jax.experimental.pallas import tpu as pltpu
from jax.sharding import PartitionSpec as P

EPS = 1e-05


def padded_2(cells, sides, width):
    for axis, dim in sides:
        count = lax.axis_size(axis)
        ends = count - 1
        head = lax.slice_in_dim(cells, 0, width, axis=dim)
        tail = lax.slice_in_dim(cells, cells.shape[dim] - width, cells.shape[dim], axis=dim)
        cells = jnp.concatenate(
            [
                lax.ppermute(tail, axis, [(i, (i + 1) % count) for i in range(ends)]),
                cells,
                lax.ppermute(head, axis, [((i + 1) % count, i) for i in range(ends)]),
            ],
            axis=dim,
        )
    return cells


def to_maps(flat, width):
    count, high, merged = flat.shape
    return flat.reshape(count, high, merged // width, width).transpose(0, 1, 3, 2)


def from_maps(maps):
    count, high, wide, chans = maps.shape
    return maps.transpose(0, 1, 3, 2).reshape(count, high, chans * wide)


def spatial_conv(padded, kernel):
    return lax.conv_general_dilated(
        padded,
        kernel,
        (1, 1),
        ((0, 0), (1, 1)),
        dimension_numbers=("NHWC", "HWIO", "NHWC"),
        preferred_element_type=jnp.float32,
    )


def flipped(kernel):
    return jnp.transpose(kernel[::-1, ::-1], (0, 1, 3, 2))


def pool_unpool(values):
    count, high, wide, chans = values.shape
    blocks = values.reshape(count, high // 2, 2, wide // 2, 2, chans)
    pooled = jax.nn.logsumexp(blocks, axis=(2, 4), keepdims=True)
    return (jnp.exp(blocks - pooled) * pooled).reshape(values.shape)


def moments(conv_out, total_pixels):
    summed = lax.psum(jnp.sum(conv_out, axis=(0, 1, 2)), ("dp", "rows"))
    mean = summed / total_pixels
    spread = lax.psum(jnp.sum(jnp.square(conv_out - mean), axis=(0, 1, 2)), ("dp", "rows"))
    var = spread / total_pixels
    return (mean, lax.rsqrt(var + EPS))


def kernel_grad(whole, dconv):
    images, rows_here, width, chans = dconv.shape
    widened = jnp.pad(whole, ((0, 0), (0, 0), (1, 1), (0, 0)))
    stacked = []
    for row_off in range(3):
        line = []
        for col_off in range(3):
            window = widened[:, row_off : row_off + rows_here, col_off : col_off + width, :]
            line.append(
                jnp.einsum("bhwc,bhwo->co", window, dconv, preferred_element_type=jnp.float32)
            )
        stacked.append(jnp.stack(line))
    return jnp.stack(stacked)


def generic_local(section_input, conv_weights, norm_gains, norm_shifts, out_grad, out_mask):
    width = out_mask.shape[2]
    images, rows_here = (out_mask.shape[0], out_mask.shape[1])
    total_pixels = float(images * rows_here * width * lax.axis_size("dp") * lax.axis_size("rows"))
    layers, out_here, flat_in = conv_weights.shape
    chans_in = flat_in // 9
    kernels_hwio = conv_weights.reshape(layers, out_here, 3, 3, chans_in).transpose(0, 2, 3, 4, 1)
    middle = layers // 2
    kept = []
    acting = to_maps(section_input, width)
    current = acting.astype(jnp.float32)
    pre_pool = current
    for index in range(layers):
        if index == middle:
            pre_pool = current
            acting = pool_unpool(pre_pool).astype(jnp.bfloat16)
        padded = padded_2(acting, (("rows", 1),), 1)
        whole = lax.all_gather(padded, "tensor", axis=3, tiled=True)
        conv_out = spatial_conv(whole, kernels_hwio[index])
        mean, rstd = moments(conv_out, total_pixels)
        normed = (conv_out - mean) * rstd
        shifted = normed * norm_gains[index] + norm_shifts[index]
        current = jax.nn.silu(shifted)
        acting = current.astype(jnp.bfloat16)
        kept.append((whole, normed, shifted, rstd))
    grad = to_maps(out_grad, width).astype(jnp.float32) * out_mask[..., None].astype(jnp.float32)
    kernel_list = [None] * layers
    gain_list = [None] * layers
    shift_list = [None] * layers
    for index in range(layers - 1, -1, -1):
        whole, normed, shifted, rstd = kept[index]
        unused, pull_silu = jax.vjp(jax.nn.silu, shifted)
        dshift = pull_silu(grad)[0]
        gain_sum, shift_sum = lax.psum(
            (jnp.sum(dshift * normed, axis=(0, 1, 2)), jnp.sum(dshift, axis=(0, 1, 2))),
            ("dp", "rows"),
        )
        gain_list[index] = gain_sum
        shift_list[index] = shift_sum
        dconv = (
            norm_gains[index]
            * rstd
            * (dshift - shift_sum / total_pixels - normed * gain_sum / total_pixels)
        ).astype(jnp.bfloat16)
        summed_kernel = lax.psum(
            kernel_grad(whole, dconv).astype(jnp.bfloat16), ("dp", "rows")
        ).astype(jnp.float32)
        kernel_list[index] = summed_kernel.transpose(3, 0, 1, 2).reshape(out_here, flat_in)
        grad_rim = padded_2(dconv, (("rows", 1),), 1)
        partial_terms = spatial_conv(grad_rim, flipped(kernels_hwio[index]))
        grad_in = lax.psum_scatter(
            partial_terms.astype(jnp.bfloat16), "tensor", scatter_dimension=3, tiled=True
        ).astype(jnp.float32)
        if index == middle:
            unused, pull_pool = jax.vjp(pool_unpool, pre_pool)
            grad = pull_pool(grad_in)[0]
        else:
            grad = grad_in
    return (
        from_maps(acting),
        from_maps(grad),
        jnp.stack(kernel_list),
        jnp.stack(gain_list),
        jnp.stack(shift_list),
    )


GROUPS = 4
LANES = 128
WIDE = 48
CHANS = GROUPS * LANES
F32 = jnp.float32
BF16 = jnp.bfloat16
VMEM = pl.BlockSpec(memory_space=pltpu.VMEM)
SMEM = pl.BlockSpec(memory_space=pltpu.SMEM)
ANY = pl.BlockSpec(memory_space=pltpu.HBM)
PARAMS = pltpu.CompilerParams(vmem_limit_bytes=20 * 1024 * 1024)


def in_hbm(value):
    return pltpu.with_memory_space_constraint(value, pltpu.HBM)


def fits_kernels(mesh):
    return mesh.shape["tensor"] == GROUPS and mesh.shape["rows"] == 2 and mesh.shape["dp"] == 4


def sigmoid(v):
    return 0.5 * jnp.tanh(0.5 * v) + 0.5


def swap_columns(v):
    column = lax.broadcasted_iota(jnp.int32, v.shape, 0)
    return jnp.where(column % 2 == 0, pltpu.roll(v, WIDE - 1, 0), pltpu.roll(v, 1, 0))


def soft_parts(h):
    top = jnp.maximum(h[0], h[1])
    top = jnp.maximum(top, swap_columns(top))
    e0, e1 = jnp.exp(h[0] - top), jnp.exp(h[1] - top)
    total = e0 + e1
    total = total + swap_columns(total)
    pooled = top + jnp.log(total)
    inverse = 1.0 / total
    return e0 * inverse, e1 * inverse, pooled


def soft(h):
    h = h.reshape(2, WIDE, LANES)
    q0, q1, pooled = soft_parts(h)
    return jnp.concatenate([q0 * pooled, q1 * pooled], axis=0)


def soft_pull(h, grad):
    h = h.reshape(2, WIDE, LANES)
    grad = grad.reshape(2, WIDE, LANES)
    q0, q1, pooled = soft_parts(h)
    mix = q0 * grad[0] + q1 * grad[1]
    mix = mix + swap_columns(mix)
    return jnp.concatenate(
        [q0 * (pooled * (grad[0] - mix) + mix), q1 * (pooled * (grad[1] - mix) + mix)], axis=0
    )


def norm_tables(st_ref, at, total):
    mean, spread, own, oth = (st_ref[at + i : at + i + 1, :] for i in range(4))
    rstd = lax.rsqrt(spread / total + EPS)
    return rstd, (own - mean) * rstd, (oth - mean) * rstd


def left_right(y0, y1, y2):
    rows = y0.shape[0]
    column = lax.broadcasted_iota(jnp.int32, y0.shape, 0) % WIDE
    before = jnp.where(column == 0, 0.0, pltpu.roll(y0, 1, 0))
    after = jnp.where(column == WIDE - 1, 0.0, pltpu.roll(y2, rows - 1, 0))
    return before + y1 + after


def lane_of(group):
    return pl.multiple_of(group * LANES, LANES)


def write_message(msg, own, sums, edge, half):
    n_own = own.shape[0]
    start = pl.multiple_of((1 - half) * (n_own - edge), WIDE)
    msg[0:edge, :] = own[pl.ds(start, edge), :].astype(F32)
    msg[edge : edge + 8, :] = jnp.concatenate([sums, jnp.zeros((8 - sums.shape[0], LANES), F32)], axis=0)


def pair_rows(j):
    return pl.ds(pl.multiple_of(j * 2 * WIDE, 2 * WIDE), 2 * WIDE)


def fold(v):
    return jnp.sum(v.reshape(v.shape[0] // 8, 8, LANES), axis=0)


def fwd_kernel(first, pool, layer, total, edge_out, *refs):
    pos, zs = refs[0], refs[1:5]
    if first:
        w_hbm, rest = refs[5], refs[6:]
    else:
        sides, gss, w_hbm, rest = refs[5:9], refs[9:13], refs[13], refs[15:]
    hb_out, zc_out, msg, hb, w, y, z, tab, hs, sem = rest
    load = pltpu.make_async_copy(w_hbm.at[layer], w, sem.at[0])
    load.start()
    save = pltpu.make_async_copy(hb, hb_out.at[layer], sem.at[1])
    t, r = pos[0], pos[1]
    n_own = z.shape[0]
    halo_at = pl.multiple_of((1 - r) * (n_own + WIDE), WIDE)
    zero_at = pl.multiple_of(r * (n_own + WIDE), WIDE)
    hb[pl.ds(zero_at, WIDE), :] = jnp.zeros((WIDE, CHANS), BF16)
    if not first:
        edge = sides[0].shape[0] - 8
        for k in range(GROUPS):
            rstd, own, oth = norm_tables(sides[k], edge, total)
            gain, shift = gss[k][layer - 1 : layer, :], gss[k][layer + 7 : layer + 8, :]
            tab[k, 0:1] = rstd * gain
            tab[k, 1:2] = own * gain + shift
            tab[k, 2:3] = oth * gain + shift

    def act(values, k, which):
        if first:
            return values
        n = values.astype(F32) * tab[k, 0:1, :] + tab[k, which : which + 1, :]
        h = n * sigmoid(n)
        return soft(h) if pool else h

    def body(j, carry):
        at = pl.multiple_of(j * 2 * WIDE, 2 * WIDE)
        for k in range(GROUPS):
            h = act(zs[k][pl.ds(at, 2 * WIDE), :], k, 1)
            hb[pl.ds(pl.multiple_of(at + WIDE, WIDE), 2 * WIDE), pl.ds(lane_of(t ^ k), LANES)] = h.astype(BF16)
        return carry

    lax.fori_loop(0, n_own // (2 * WIDE), body, 0)
    for k in range(GROUPS):
        if first:
            h = zs[k][n_own : n_own + WIDE, :]
        else:
            h = act(sides[k][0:edge, :], k, 2)
            if edge > WIDE:
                hs[...] = h
                h = hs[pl.ds(pl.multiple_of(r * WIDE, WIDE), WIDE), :]
        hb[pl.ds(halo_at, WIDE), pl.ds(lane_of(t ^ k), LANES)] = h.astype(BF16)
    save.start()
    load.wait()
    lhs = jnp.concatenate([hb[i * WIDE : i * WIDE + n_own, :] for i in range(3)], axis=1)
    rhs = jnp.concatenate(
        [
            jnp.concatenate([w[:, (3 * i + s) * CHANS : (3 * i + s + 1) * CHANS] for i in range(3)], axis=1)
            for s in range(3)
        ],
        axis=0,
    )
    y[...] = lax.dot_general(lhs, rhs, (((1,), (1,)), ((), ())), preferred_element_type=F32)

    def add_up(j, acc):
        rows = pair_rows(j)
        v = left_right(y[rows, 0:128], y[rows, 128:256], y[rows, 256:384])
        z[rows, :] = v
        return acc + fold(v)

    steps = n_own // (2 * WIDE)
    summed = lax.fori_loop(0, steps, add_up, jnp.zeros((8, LANES), F32))
    mean = jnp.sum(summed, axis=0, keepdims=True) / n_own

    def centre(j, acc):
        rows = pair_rows(j)
        v = z[rows, :] - mean
        z[rows, :] = v
        zc_out[rows, :] = v.astype(BF16)
        return acc + fold(jnp.square(v))

    apart = lax.fori_loop(0, steps, centre, jnp.zeros((8, LANES), F32))
    sums = [mean, jnp.sum(apart, axis=0, keepdims=True), mean, jnp.zeros((1, LANES), F32)]
    write_message(msg, z, jnp.concatenate(sums, axis=0), edge_out, r)
    save.wait()


def fwd_step(layer, pool, edge_out, total, pos, slots, sides, tables, weights, kept, n_own):
    first = sides is None
    layers = weights.shape[0]
    extra = () if first else (*sides, *tables)
    return pl.pallas_call(
        functools.partial(fwd_kernel, first, pool, layer, total, edge_out),
        out_shape=(
            pltpu.HBM((layers, n_own + 2 * WIDE, CHANS), BF16),
            pltpu.VMEM((n_own, LANES), BF16),
            pltpu.VMEM((edge_out + 8, LANES), F32),
        ),
        in_specs=[SMEM] + [VMEM] * (4 + len(extra)) + [ANY] * (1 if first else 2),
        out_specs=(ANY, VMEM, VMEM),
        input_output_aliases={} if first else {6 + len(extra): 0},
        scratch_shapes=[
            pltpu.VMEM((n_own + 2 * WIDE, CHANS), BF16),
            pltpu.VMEM((LANES, 9 * CHANS), BF16),
            pltpu.VMEM((n_own, 3 * LANES), F32),
            pltpu.VMEM((n_own, LANES), F32),
            pltpu.VMEM((GROUPS, 8, LANES), F32),
            pltpu.VMEM((2 * WIDE, LANES), F32),
            pltpu.SemaphoreType.DMA((2,)),
        ],
        compiler_params=PARAMS,
        cost_estimate=pl.CostEstimate(
            flops=2 * n_own * 9 * CHANS * LANES, bytes_accessed=4 * 1024 * 1024, transcendentals=n_own * CHANS
        ),
        name="conv_forward",
    )(pos, *slots, *extra, in_hbm(weights), *(() if first else (in_hbm(kept),)))


def below_kernel(layer, pool, total, top, *refs):
    pos, terms, zc, side, gs = refs[:5]
    if top:
        h_out, dn_out, edge_out, sums_out, tab = refs[5:]
    else:
        dn_out, edge_out, sums_out, tab = refs[5:]
    n_own = zc.shape[0]
    rstd, own, oth = norm_tables(side, side.shape[0] - 8, total)
    tab[0:1], tab[1:2] = rstd, own
    tab[2:3], tab[3:4] = gs[layer : layer + 1, :], gs[layer + 8 : layer + 9, :]

    def body(j, accs):
        rows = pair_rows(j)
        xhat = zc[rows, :].astype(F32) * tab[0:1, :] + tab[1:2, :]
        n = xhat * tab[2:3, :] + tab[3:4, :]
        sig = sigmoid(n)
        h = n * sig
        if top:
            g = terms[rows, :].astype(F32)
            h_out[rows, :] = h.astype(BF16)
        else:
            g = functools.reduce(jnp.add, [terms[k, rows, :].astype(F32) for k in range(GROUPS)])
        if pool:
            g = soft_pull(h, g)
        dn = g * (sig * (1.0 + n - h))
        dn_out[rows, :] = dn
        return accs[0] + fold(dn), accs[1] + fold(dn * xhat)

    zero = jnp.zeros((8, LANES), F32)
    sums = lax.fori_loop(0, n_own // (2 * WIDE), body, (zero, zero))
    sums = [jnp.sum(v, axis=0, keepdims=True) for v in sums]
    sums = jnp.concatenate(sums + [jnp.zeros((6, LANES), F32)], axis=0)
    for i in range(sums_out.shape[0]):
        sums_out[i] = sums
    start = pl.multiple_of((1 - pos[1]) * (n_own - WIDE), WIDE)
    edge_out[...] = dn_out[pl.ds(start, WIDE), :]


def below_step(layer, pool, total, pos, terms, zc, side, gs, parts):
    n_own = zc.shape[0]
    top = len(terms.shape) == 2
    out_shape = [
        pltpu.VMEM((n_own, LANES), F32),
        pltpu.VMEM((WIDE, LANES), F32),
        pltpu.VMEM((parts, 8, LANES), F32),
    ]
    if top:
        out_shape = [jax.ShapeDtypeStruct((n_own, LANES), BF16)] + out_shape
    return pl.pallas_call(
        functools.partial(below_kernel, layer, pool, total, top),
        out_shape=tuple(out_shape),
        in_specs=[SMEM] + [VMEM] * 4,
        out_specs=(VMEM,) * len(out_shape),
        scratch_shapes=[pltpu.VMEM((8, LANES), F32)],
        compiler_params=PARAMS,
        cost_estimate=pl.CostEstimate(flops=40 * n_own * LANES, bytes_accessed=1024 * 1024, transcendentals=n_own * LANES),
        name="silu_backward",
    )(pos, terms, zc, side, gs)


def bwd_kernel(layer, total, *refs):
    pos, dn, dedge, sums, zc, zside, gs, w_hbm, out, d_out, d, w, y, tab, sem = refs
    load = pltpu.make_async_copy(w_hbm.at[layer], w, sem)
    load.start()
    t, r = pos[0], pos[1]
    n_own = dn.shape[0]
    halo_at = pl.multiple_of((1 - r) * (n_own + WIDE), WIDE)
    zero_at = pl.multiple_of(r * (n_own + WIDE), WIDE)
    edge = zside.shape[0] - 8
    d[pl.ds(zero_at, WIDE), :] = jnp.zeros((WIDE, 3 * LANES), BF16)
    rstd, own, oth = norm_tables(zside, edge, total)
    scale = gs[layer : layer + 1, :] * rstd
    added = functools.reduce(jnp.add, [sums[i] for i in range(sums.shape[0])])
    shift_sum, gain_sum = added[0:1], added[1:2]
    slope = scale * gain_sum / total
    tab[0:1] = scale
    tab[1:2] = slope * rstd
    tab[2:3] = scale * shift_sum / total + slope * own
    tab[3:4] = scale * shift_sum / total + slope * oth

    def spread_columns(v, at):
        rows = v.shape[0]
        column = lax.broadcasted_iota(jnp.int32, v.shape, 0) % WIDE
        ahead = jnp.where(column == WIDE - 1, 0.0, pltpu.roll(v, rows - 1, 0))
        behind = jnp.where(column == 0, 0.0, pltpu.roll(v, 1, 0))
        d[pl.ds(at, rows), 0:128] = ahead.astype(BF16)
        d[pl.ds(at, rows), 128:256] = v.astype(BF16)
        d[pl.ds(at, rows), 256:384] = behind.astype(BF16)

    def body(j, carry):
        rows = pair_rows(j)
        v = dn[rows, :] * tab[0:1, :] - tab[2:3, :] - zc[rows, :].astype(F32) * tab[1:2, :]
        spread_columns(v, pl.multiple_of(j * 2 * WIDE + WIDE, WIDE))
        return carry

    lax.fori_loop(0, n_own // (2 * WIDE), body, 0)
    near = zside[0:WIDE, :] if edge == WIDE else zside[pl.ds(pl.multiple_of(r * WIDE, WIDE), WIDE), :]
    spread_columns(dedge[...] * tab[0:1, :] - tab[3:4, :] - near * tab[1:2, :], halo_at)
    d_out[...] = d[WIDE : WIDE + n_own, :]
    load.wait()
    lhs = jnp.concatenate([d[(2 - i) * WIDE : (2 - i) * WIDE + n_own, :] for i in range(3)], axis=1)
    rhs = jnp.concatenate([w[:, i * CHANS : (i + 1) * CHANS] for i in range(9)], axis=0)
    y[...] = jnp.dot(lhs, rhs, preferred_element_type=F32)

    def share(j, carry):
        rows = pair_rows(j)
        for k in range(GROUPS):
            out[k, rows, :] = y[rows, k * LANES : (k + 1) * LANES].astype(BF16)
        return carry

    lax.fori_loop(0, n_own // (2 * WIDE), share, 0)


def bwd_step(layer, total, pos, dn, dedge, sums, zc, zside, gs, weights):
    n_own = dn.shape[0]
    return pl.pallas_call(
        functools.partial(bwd_kernel, layer, total),
        out_shape=(
            pltpu.VMEM((GROUPS, n_own, LANES), BF16),
            pltpu.VMEM((n_own, 3 * LANES), BF16),
        ),
        in_specs=[SMEM] + [VMEM] * 6 + [ANY],
        out_specs=(VMEM,) * 2,
        scratch_shapes=[
            pltpu.VMEM((n_own + 2 * WIDE, 3 * LANES), BF16),
            pltpu.VMEM((LANES, 9 * CHANS), BF16),
            pltpu.VMEM((n_own, CHANS), F32),
            pltpu.VMEM((8, LANES), F32),
            pltpu.SemaphoreType.DMA,
        ],
        compiler_params=PARAMS,
        cost_estimate=pl.CostEstimate(
            flops=2 * n_own * 9 * CHANS * LANES, bytes_accessed=4 * 1024 * 1024, transcendentals=0
        ),
        name="conv_backward",
    )(pos, dn, dedge, sums, zc, zside, gs, in_hbm(weights))


def last_kernel(terms, out):
    def body(j, carry):
        rows = pair_rows(j)
        out[rows, :] = functools.reduce(jnp.add, [terms[k, rows, :].astype(F32) for k in range(GROUPS)])
        return carry

    lax.fori_loop(0, out.shape[0] // (2 * WIDE), body, 0)


def last_step(terms):
    return pl.pallas_call(
        last_kernel,
        out_shape=jax.ShapeDtypeStruct(terms.shape[1:], F32),
        in_specs=[VMEM],
        out_specs=VMEM,
        compiler_params=PARAMS,
        name="add_terms",
    )(terms)


def halves_kernel(keep, got, out):
    out[...] = (keep[...].astype(F32) + got[...].astype(F32)).astype(BF16)


def add_halves(keep, got):
    return pl.pallas_call(
        halves_kernel,
        out_shape=jax.ShapeDtypeStruct(keep.shape, BF16),
        in_specs=[VMEM] * 2,
        out_specs=VMEM,
        compiler_params=PARAMS,
        cost_estimate=pl.CostEstimate(flops=keep.size, bytes_accessed=6 * keep.size, transcendentals=0),
        name="add_halves",
    )(keep, got)


def wgrad_kernel(layer, pos, d, hb_hbm, keep, send, hb, grad, sem):
    load = pltpu.make_async_copy(hb_hbm.at[layer], hb, sem)
    load.start()
    n_own = d.shape[0]
    lhs = d[...]
    load.wait()
    for i in range(3):
        part = lax.dot_general(
            lhs, hb[i * WIDE : i * WIDE + n_own, :], (((0,), (0,)), ((), ())), preferred_element_type=F32
        ).astype(BF16)
        for s in range(3):
            grad[:, (3 * i + s) * CHANS : (3 * i + s + 1) * CHANS] = part[s * LANES : (s + 1) * LANES]
    half = LANES // 2
    keep[...] = grad[pl.ds(pl.multiple_of(pos[1] * half, half), half), :]
    send[...] = grad[pl.ds(pl.multiple_of((1 - pos[1]) * half, half), half), :]


def wgrad_step(layer, pos, d, kept):
    half = pltpu.VMEM((LANES // 2, 9 * CHANS), BF16)
    return pl.pallas_call(
        functools.partial(wgrad_kernel, layer),
        out_shape=(half, half),
        in_specs=[SMEM, VMEM, ANY],
        out_specs=(VMEM, VMEM),
        scratch_shapes=[
            pltpu.VMEM(kept.shape[1:], BF16),
            pltpu.VMEM((LANES, 9 * CHANS), BF16),
            pltpu.SemaphoreType.DMA,
        ],
        compiler_params=PARAMS,
        cost_estimate=pl.CostEstimate(
            flops=2 * d.shape[0] * 9 * CHANS * LANES, bytes_accessed=3 * 1024 * 1024, transcendentals=0
        ),
        name="kernel_gradient",
    )(pos, d, in_hbm(kept))


def place_kernel(pos, mine, other, *refs):
    refs[-1][0] = jnp.where(pl.program_id(0) == pos[1], mine[...], other[...]).astype(F32)


def place_step(layer, pos, mine, other, whole, layers):
    half = LANES // 2
    block = pl.BlockSpec((half, 9 * CHANS), lambda i: (0, 0))
    return pl.pallas_call(
        place_kernel,
        grid=(2,),
        out_shape=jax.ShapeDtypeStruct((layers, LANES, 9 * CHANS), F32),
        in_specs=[SMEM, block, block] + ([] if whole is None else [ANY]),
        out_specs=pl.BlockSpec((1, half, 9 * CHANS), lambda i: (layer, i, 0)),
        input_output_aliases={} if whole is None else {3: 0},
        compiler_params=PARAMS,
        cost_estimate=pl.CostEstimate(flops=0, bytes_accessed=4 * 1024 * 1024, transcendentals=0),
        name="place_gradient",
    )(pos, mine, other, *(() if whole is None else (whole,)))


def swap_with(value, axis, k):
    return lax.ppermute(value, axis, [(i, i ^ k) for i in range(lax.axis_size(axis))])


def spread(own):
    return (own, *[swap_with(own, "tensor", k) for k in range(1, GROUPS)])


def pair_moments(mine, got, count):
    mean = 0.5 * (mine[0:1] + got[0:1])
    apart = mine[1:2] + got[1:2] + (0.5 * count) * jnp.square(got[0:1] - mine[0:1])
    return mean, apart


def share_moments(msg, edge, count):
    got = swap_with(msg, "rows", 1)
    mine, other = msg[edge:], got[edge:]
    mean, apart = pair_moments(mine, other, count)
    sums = jnp.concatenate([mean, apart, mine[2:3], other[2:3], mine[4:]], axis=0)
    for k in (1, 2):
        other = swap_with(sums, "dp", k)
        mean, apart = pair_moments(sums, other, 2 * k * count)
        sums = jnp.concatenate([mean, apart, sums[2:]], axis=0)
    return jnp.concatenate([got[:edge], sums], axis=0)


def halo_of_input(x, half):
    n_own = x.shape[0]
    edge = jnp.where(half == 0, x[n_own - WIDE :], x[:WIDE])
    return jnp.concatenate([x, swap_with(edge, "rows", 1)], axis=0)


def fast_local(section_input, conv_weights, norm_gains, norm_shifts, out_grad, out_mask):
    images, rows_here, width = out_mask.shape
    layers = conv_weights.shape[0]
    n_own = rows_here * width
    parts = lax.axis_size("dp") * lax.axis_size("rows")
    total = float(n_own * parts)
    t, half = lax.axis_index("tensor"), lax.axis_index("rows")
    pos = jnp.stack([t, half]).astype(jnp.int32)
    middle = layers // 2
    x = to_maps(section_input, width).reshape(n_own, LANES)
    slots = spread(halo_of_input(x, half))
    pad = jnp.zeros((8 - layers, LANES), F32)
    tables = spread(jnp.concatenate([norm_gains, pad, norm_shifts, pad], axis=0))
    top_grad = (to_maps(out_grad, width) * out_mask[..., None].astype(BF16)).reshape(n_own, LANES)

    sides, kept = None, None
    kept_z, kept_side = [], []
    for layer in range(layers):
        edge = 2 * WIDE if layer + 1 == middle else WIDE
        kept, zc, msg = fwd_step(
            layer, layer == middle, edge, total, pos, slots, sides, tables, conv_weights, kept, n_own
        )
        side = share_moments(msg, edge, float(n_own))
        kept_z.append(zc)
        kept_side.append(side)
        if layer + 1 < layers:
            slots = spread(zc)
            sides = spread(side)
    top = layers - 1
    h_last, dn, edge, sums = below_step(
        top, False, total, pos, top_grad, kept_z[top], kept_side[top], tables[0], parts
    )
    sum_list = [None] * layers
    pairs = [None] * layers
    for layer in range(layers - 1, -1, -1):
        edge = swap_with(edge, "rows", 1)
        sums = lax.all_to_all(sums, ("dp", "rows"), split_axis=0, concat_axis=0, tiled=True)
        sum_list[layer] = sums
        terms, d = bwd_step(
            layer, total, pos, dn, edge, sums, kept_z[layer], kept_side[layer], tables[0], conv_weights
        )
        terms = lax.all_to_all(terms, "tensor", split_axis=0, concat_axis=0, tiled=True)
        keep, send = wgrad_step(layer, pos, d, kept)
        pairs[layer] = add_halves(keep, swap_with(send, "rows", 1))
        if layer > 0:
            below = layer - 1
            dn, edge, sums = below_step(
                below, layer == middle, total, pos, terms, kept_z[below], kept_side[below], tables[0], parts
            )
        else:
            grad = last_step(terms)
    ahead, back = [[0, 1, 2, 3]], [[3, 2, 1, 0]]
    upper = lax.psum((pairs[5], pairs[4]), "dp", axis_index_groups=ahead)
    mid = lax.psum((pairs[3], pairs[2]), "dp", axis_index_groups=back)
    tied, upper = lax.optimization_barrier(((pairs[1], pairs[0]), upper))
    lower = lax.psum(tied, "dp", axis_index_groups=ahead)
    whole = None
    for layer, mine in zip((5, 4, 3, 2, 1, 0), (*upper, *mid, *lower)):
        whole = place_step(layer, pos, mine, swap_with(mine, "rows", 1), whole, layers)
    sums = jnp.sum(jnp.stack(sum_list), axis=1)
    shape = (images, rows_here, width, LANES)
    return (
        from_maps(h_last.reshape(shape)),
        from_maps(grad.reshape(shape)),
        whole,
        sums[:, 1],
        sums[:, 0],
    )


def solution(mesh):
    in_specs = (
        P("dp", "rows", "tensor"),
        P(None, "tensor", None),
        P(None, "tensor"),
        P(None, "tensor"),
        P("dp", "rows", "tensor"),
        P("dp", "rows", None),
    )
    out_specs = (
        P("dp", "rows", "tensor"),
        P("dp", "rows", "tensor"),
        P(None, "tensor", None),
        P(None, "tensor"),
        P(None, "tensor"),
    )
    local = fast_local if fits_kernels(mesh) else generic_local
    return jax.shard_map(local, mesh=mesh, in_specs=in_specs, out_specs=out_specs, check_vma=False)
```

```python
import functools

import jax
import jax.numpy as jnp
from jax import lax
from jax.experimental import pallas as pl
from jax.experimental.pallas import tpu as pltpu
from jax.sharding import PartitionSpec as P

EPS = 1e-05


def padded_2(cells, sides, width):
    for axis, dim in sides:
        count = lax.axis_size(axis)
        ends = count - 1
        head = lax.slice_in_dim(cells, 0, width, axis=dim)
        tail = lax.slice_in_dim(cells, cells.shape[dim] - width, cells.shape[dim], axis=dim)
        cells = jnp.concatenate(
            [
                lax.ppermute(tail, axis, [(i, (i + 1) % count) for i in range(ends)]),
                cells,
                lax.ppermute(head, axis, [((i + 1) % count, i) for i in range(ends)]),
            ],
            axis=dim,
        )
    return cells


def to_maps(flat, width):
    count, high, merged = flat.shape
    return flat.reshape(count, high, merged // width, width).transpose(0, 1, 3, 2)


def from_maps(maps):
    count, high, wide, chans = maps.shape
    return maps.transpose(0, 1, 3, 2).reshape(count, high, chans * wide)


def spatial_conv(padded, kernel):
    return lax.conv_general_dilated(
        padded,
        kernel,
        (1, 1),
        ((0, 0), (1, 1)),
        dimension_numbers=("NHWC", "HWIO", "NHWC"),
        preferred_element_type=jnp.float32,
    )


def flipped(kernel):
    return jnp.transpose(kernel[::-1, ::-1], (0, 1, 3, 2))


def pool_unpool(values):
    count, high, wide, chans = values.shape
    blocks = values.reshape(count, high // 2, 2, wide // 2, 2, chans)
    pooled = jax.nn.logsumexp(blocks, axis=(2, 4), keepdims=True)
    return (jnp.exp(blocks - pooled) * pooled).reshape(values.shape)


def moments(conv_out, total_pixels):
    summed = lax.psum(jnp.sum(conv_out, axis=(0, 1, 2)), ("dp", "rows"))
    mean = summed / total_pixels
    spread = lax.psum(jnp.sum(jnp.square(conv_out - mean), axis=(0, 1, 2)), ("dp", "rows"))
    var = spread / total_pixels
    return (mean, lax.rsqrt(var + EPS))


def kernel_grad(whole, dconv):
    images, rows_here, width, chans = dconv.shape
    widened = jnp.pad(whole, ((0, 0), (0, 0), (1, 1), (0, 0)))
    stacked = []
    for row_off in range(3):
        line = []
        for col_off in range(3):
            window = widened[:, row_off : row_off + rows_here, col_off : col_off + width, :]
            line.append(
                jnp.einsum("bhwc,bhwo->co", window, dconv, preferred_element_type=jnp.float32)
            )
        stacked.append(jnp.stack(line))
    return jnp.stack(stacked)


def generic_local(section_input, conv_weights, norm_gains, norm_shifts, out_grad, out_mask):
    width = out_mask.shape[2]
    images, rows_here = (out_mask.shape[0], out_mask.shape[1])
    total_pixels = float(images * rows_here * width * lax.axis_size("dp") * lax.axis_size("rows"))
    layers, out_here, flat_in = conv_weights.shape
    chans_in = flat_in // 9
    kernels_hwio = conv_weights.reshape(layers, out_here, 3, 3, chans_in).transpose(0, 2, 3, 4, 1)
    middle = layers // 2
    kept = []
    acting = to_maps(section_input, width)
    current = acting.astype(jnp.float32)
    pre_pool = current
    for index in range(layers):
        if index == middle:
            pre_pool = current
            acting = pool_unpool(pre_pool).astype(jnp.bfloat16)
        padded = padded_2(acting, (("rows", 1),), 1)
        whole = lax.all_gather(padded, "tensor", axis=3, tiled=True)
        conv_out = spatial_conv(whole, kernels_hwio[index])
        mean, rstd = moments(conv_out, total_pixels)
        normed = (conv_out - mean) * rstd
        shifted = normed * norm_gains[index] + norm_shifts[index]
        current = jax.nn.silu(shifted)
        acting = current.astype(jnp.bfloat16)
        kept.append((whole, normed, shifted, rstd))
    grad = to_maps(out_grad, width).astype(jnp.float32) * out_mask[..., None].astype(jnp.float32)
    kernel_list = [None] * layers
    gain_list = [None] * layers
    shift_list = [None] * layers
    for index in range(layers - 1, -1, -1):
        whole, normed, shifted, rstd = kept[index]
        unused, pull_silu = jax.vjp(jax.nn.silu, shifted)
        dshift = pull_silu(grad)[0]
        gain_sum, shift_sum = lax.psum(
            (jnp.sum(dshift * normed, axis=(0, 1, 2)), jnp.sum(dshift, axis=(0, 1, 2))),
            ("dp", "rows"),
        )
        gain_list[index] = gain_sum
        shift_list[index] = shift_sum
        dconv = (
            norm_gains[index]
            * rstd
            * (dshift - shift_sum / total_pixels - normed * gain_sum / total_pixels)
        ).astype(jnp.bfloat16)
        summed_kernel = lax.psum(
            kernel_grad(whole, dconv).astype(jnp.bfloat16), ("dp", "rows")
        ).astype(jnp.float32)
        kernel_list[index] = summed_kernel.transpose(3, 0, 1, 2).reshape(out_here, flat_in)
        grad_rim = padded_2(dconv, (("rows", 1),), 1)
        partial_terms = spatial_conv(grad_rim, flipped(kernels_hwio[index]))
        grad_in = lax.psum_scatter(
            partial_terms.astype(jnp.bfloat16), "tensor", scatter_dimension=3, tiled=True
        ).astype(jnp.float32)
        if index == middle:
            unused, pull_pool = jax.vjp(pool_unpool, pre_pool)
            grad = pull_pool(grad_in)[0]
        else:
            grad = grad_in
    return (
        from_maps(acting),
        from_maps(grad),
        jnp.stack(kernel_list),
        jnp.stack(gain_list),
        jnp.stack(shift_list),
    )


GROUPS = 4
LANES = 128
WIDE = 48
CHANS = GROUPS * LANES
F32 = jnp.float32
BF16 = jnp.bfloat16
VMEM = pl.BlockSpec(memory_space=pltpu.VMEM)
SMEM = pl.BlockSpec(memory_space=pltpu.SMEM)
ANY = pl.BlockSpec(memory_space=pltpu.HBM)
FREE = pl.BlockSpec(memory_space=pl.ANY)
PARAMS = pltpu.CompilerParams(vmem_limit_bytes=20 * 1024 * 1024)


def in_hbm(value):
    return pltpu.with_memory_space_constraint(value, pltpu.HBM)


def fits_kernels(mesh):
    return mesh.shape["tensor"] == GROUPS and mesh.shape["rows"] == 2 and mesh.shape["dp"] == 4


def sigmoid(v):
    return 0.5 * jnp.tanh(0.5 * v) + 0.5


def swap_columns(v):
    column = lax.broadcasted_iota(jnp.int32, v.shape, 0)
    return jnp.where(column % 2 == 0, pltpu.roll(v, WIDE - 1, 0), pltpu.roll(v, 1, 0))


def soft_parts(h):
    top = jnp.maximum(h[0], h[1])
    top = jnp.maximum(top, swap_columns(top))
    e0, e1 = jnp.exp(h[0] - top), jnp.exp(h[1] - top)
    total = e0 + e1
    total = total + swap_columns(total)
    pooled = top + jnp.log(total)
    inverse = 1.0 / total
    return e0 * inverse, e1 * inverse, pooled


def soft(h):
    h = h.reshape(2, WIDE, LANES)
    q0, q1, pooled = soft_parts(h)
    return jnp.concatenate([q0 * pooled, q1 * pooled], axis=0)


def soft_pull(h, grad):
    h = h.reshape(2, WIDE, LANES)
    grad = grad.reshape(2, WIDE, LANES)
    q0, q1, pooled = soft_parts(h)
    mix = q0 * grad[0] + q1 * grad[1]
    mix = mix + swap_columns(mix)
    return jnp.concatenate(
        [q0 * (pooled * (grad[0] - mix) + mix), q1 * (pooled * (grad[1] - mix) + mix)], axis=0
    )


def norm_tables(st, group, i_own, i_oth, n_local, total):
    parts = st.shape[0]
    blocks = [st[i, group] for i in range(parts)]
    summed = functools.reduce(jnp.add, blocks)
    mean = summed[0:1] / parts
    apart = functools.reduce(jnp.add, [jnp.square(b - mean) for b in blocks])
    rstd = lax.rsqrt((summed[1:2] + n_local * apart[0:1]) / total + EPS)
    return rstd, (st[i_own, group, 0:1] - mean) * rstd, (st[i_oth, group, 0:1] - mean) * rstd


def left_right(y0, y1, y2):
    rows = y0.shape[0]
    column = lax.broadcasted_iota(jnp.int32, y0.shape, 0) % WIDE
    before = jnp.where(column == 0, 0.0, pltpu.roll(y0, 1, 0))
    after = jnp.where(column == WIDE - 1, 0.0, pltpu.roll(y2, rows - 1, 0))
    return before + y1 + after


def lane_of(group):
    return pl.multiple_of(group * LANES, LANES)


def edge_start(n_own, edge, half):
    return pl.multiple_of((1 - half) * (n_own - edge), WIDE)


def pair_rows(j):
    return pl.ds(pl.multiple_of(j * 2 * WIDE, 2 * WIDE), 2 * WIDE)


def fold(v):
    return jnp.sum(v.reshape(v.shape[0] // 8, 8, LANES), axis=0)


def fwd_kernel(first, pool, layer, total, edge_out, *refs):
    pos, zs = refs[0], refs[1:5]
    if first:
        w_hbm, rest = refs[5], refs[6:]
    else:
        st, gss, w_hbm, rest = refs[5], refs[6:10], refs[10], refs[12:]
    hb_out, zc_out, edge_ref, st_out, hb, w, y, z, tab, hs, sem = rest
    load = pltpu.make_async_copy(w_hbm.at[layer], w, sem.at[0])
    load.start()
    save = pltpu.make_async_copy(hb, hb_out.at[layer], sem.at[1])
    t, r = pos[0], pos[1]
    n_own = z.shape[0]
    halo_at = pl.multiple_of((1 - r) * (n_own + WIDE), WIDE)
    zero_at = pl.multiple_of(r * (n_own + WIDE), WIDE)
    hb[pl.ds(zero_at, WIDE), :] = jnp.zeros((WIDE, CHANS), BF16)
    edge = zs[0].shape[0] - n_own
    if not first:
        for k in range(GROUPS):
            rstd, own, oth = norm_tables(st, t ^ k, pos[2], pos[3], float(n_own), total)
            gain, shift = gss[k][layer - 1 : layer, :], gss[k][layer + 7 : layer + 8, :]
            tab[k, 0:1] = rstd * gain
            tab[k, 1:2] = own * gain + shift
            tab[k, 2:3] = oth * gain + shift

    def act(values, k, which):
        if first:
            return values
        n = values.astype(F32) * tab[k, 0:1, :] + tab[k, which : which + 1, :]
        h = n * sigmoid(n)
        return soft(h) if pool else h

    def body(j, carry):
        at = pl.multiple_of(j * 2 * WIDE, 2 * WIDE)
        for k in range(GROUPS):
            h = act(zs[k][pl.ds(at, 2 * WIDE), :], k, 1)
            hb[pl.ds(pl.multiple_of(at + WIDE, WIDE), 2 * WIDE), pl.ds(lane_of(t ^ k), LANES)] = h.astype(BF16)
        return carry

    lax.fori_loop(0, n_own // (2 * WIDE), body, 0)
    for k in range(GROUPS):
        h = act(zs[k][n_own : n_own + edge, :], k, 2)
        if edge > WIDE:
            hs[...] = h
            h = hs[pl.ds(pl.multiple_of(r * WIDE, WIDE), WIDE), :]
        hb[pl.ds(halo_at, WIDE), pl.ds(lane_of(t ^ k), LANES)] = h.astype(BF16)
    save.start()
    load.wait()
    lhs = jnp.concatenate([hb[i * WIDE : i * WIDE + n_own, :] for i in range(3)], axis=1)
    rhs = jnp.concatenate(
        [
            jnp.concatenate([w[:, (3 * i + s) * CHANS : (3 * i + s + 1) * CHANS] for i in range(3)], axis=1)
            for s in range(3)
        ],
        axis=0,
    )
    y[...] = lax.dot_general(lhs, rhs, (((1,), (1,)), ((), ())), preferred_element_type=F32)

    def add_up(j, acc):
        rows = pair_rows(j)
        v = left_right(y[rows, 0:128], y[rows, 128:256], y[rows, 256:384])
        z[rows, :] = v
        return acc + fold(v)

    steps = n_own // (2 * WIDE)
    summed = lax.fori_loop(0, steps, add_up, jnp.zeros((8, LANES), F32))
    mean = jnp.sum(summed, axis=0, keepdims=True) / n_own

    def centre(j, acc):
        rows = pair_rows(j)
        v = z[rows, :] - mean
        z[rows, :] = v
        zc_out[rows, :] = v.astype(BF16)
        return acc + fold(jnp.square(v))

    apart = lax.fori_loop(0, steps, centre, jnp.zeros((8, LANES), F32))
    sums = [mean, jnp.sum(apart, axis=0, keepdims=True), jnp.zeros((6, LANES), F32)]
    sums = jnp.concatenate(sums, axis=0)
    for i in range(st_out.shape[0]):
        st_out[i] = sums
    edge_ref[...] = zc_out[pl.ds(edge_start(n_own, edge_out, r), edge_out), :]
    zc_out[n_own : n_own + edge_out, :] = jnp.zeros((edge_out, LANES), BF16)
    save.wait()


def fwd_step(layer, pool, edge_out, total, pos, slots, st, tables, weights, kept, n_own, devices):
    first = st is None
    layers = weights.shape[0]
    extra = () if first else (st, *tables)
    return pl.pallas_call(
        functools.partial(fwd_kernel, first, pool, layer, total, edge_out),
        out_shape=(
            pltpu.HBM((layers, n_own + 2 * WIDE, CHANS), BF16),
            pltpu.VMEM((n_own + edge_out, LANES), BF16),
            pltpu.VMEM((edge_out, LANES), BF16),
            pltpu.VMEM((devices, 8, LANES), F32),
        ),
        in_specs=[SMEM] + [VMEM] * (4 + len(extra)) + [ANY] * (1 if first else 2),
        out_specs=(ANY, VMEM, VMEM, VMEM),
        input_output_aliases={} if first else {6 + len(extra): 0},
        scratch_shapes=[
            pltpu.VMEM((n_own + 2 * WIDE, CHANS), BF16),
            pltpu.VMEM((LANES, 9 * CHANS), BF16),
            pltpu.VMEM((n_own, 3 * LANES), F32),
            pltpu.VMEM((n_own, LANES), F32),
            pltpu.VMEM((GROUPS, 8, LANES), F32),
            pltpu.VMEM((2 * WIDE, LANES), F32),
            pltpu.SemaphoreType.DMA((2,)),
        ],
        compiler_params=PARAMS,
        cost_estimate=pl.CostEstimate(
            flops=2 * n_own * 9 * CHANS * LANES, bytes_accessed=4 * 1024 * 1024, transcendentals=n_own * CHANS
        ),
        name="conv_forward",
    )(pos, *slots, *extra, in_hbm(weights), *(() if first else (in_hbm(kept),)))


def below_kernel(layer, pool, total, top, *refs):
    pos, zc, st, gs = refs[:4]
    if top:
        terms, h_out, dn_out, edge_out, sums_out, tab = refs[4:]
    else:
        terms, (dn_out, edge_out, sums_out, tab) = refs[4:8], refs[9:]
    n_own = dn_out.shape[0]
    rstd, own, oth = norm_tables(st, pos[0], pos[2], pos[3], float(n_own), total)
    tab[0:1], tab[1:2] = rstd, own
    tab[2:3], tab[3:4] = gs[layer : layer + 1, :], gs[layer + 8 : layer + 9, :]

    def body(j, accs):
        rows = pair_rows(j)
        xhat = zc[rows, :].astype(F32) * tab[0:1, :] + tab[1:2, :]
        n = xhat * tab[2:3, :] + tab[3:4, :]
        sig = sigmoid(n)
        h = n * sig
        if top:
            g = terms[rows, :].astype(F32)
            h_out[rows, :] = h.astype(BF16)
        else:
            g = functools.reduce(jnp.add, [term[rows, :].astype(F32) for term in terms])
        if pool:
            g = soft_pull(h, g)
        dn = g * (sig * (1.0 + n - h))
        dn_out[rows, :] = dn
        return accs[0] + fold(dn), accs[1] + fold(dn * xhat)

    zero = jnp.zeros((8, LANES), F32)
    sums = lax.fori_loop(0, n_own // (2 * WIDE), body, (zero, zero))
    sums = [jnp.sum(v, axis=0, keepdims=True) for v in sums]
    sums = jnp.concatenate(sums + [jnp.zeros((6, LANES), F32)], axis=0)
    for i in range(sums_out.shape[0]):
        sums_out[i] = sums
    edge_out[...] = dn_out[pl.ds(edge_start(n_own, WIDE, pos[1]), WIDE), :]


def below_step(layer, pool, total, pos, zc, st, gs, terms, parts, tie=None):
    n_own = terms[0].shape[0]
    top = len(terms) == 1
    ties = () if tie is None else (tie,)
    out_shape = [
        pltpu.VMEM((n_own, LANES), F32),
        pltpu.VMEM((WIDE, LANES), F32),
        pltpu.VMEM((parts, 8, LANES), F32),
    ]
    if top:
        out_shape = [jax.ShapeDtypeStruct((n_own, LANES), BF16)] + out_shape
    return pl.pallas_call(
        functools.partial(below_kernel, layer, pool, total, top),
        out_shape=tuple(out_shape),
        in_specs=[SMEM] + [VMEM] * (3 + len(terms)) + [FREE] * len(ties),
        out_specs=(VMEM,) * len(out_shape),
        scratch_shapes=[pltpu.VMEM((8, LANES), F32)],
        compiler_params=PARAMS,
        cost_estimate=pl.CostEstimate(flops=40 * n_own * LANES, bytes_accessed=1024 * 1024, transcendentals=n_own * LANES),
        name="silu_backward",
    )(pos, zc, st, gs, *terms, *ties)


def bwd_kernel(layer, total, *refs):
    pos, dn, dedge, sums, zc, st, gs, w_hbm = refs[:8]
    outs, d_out, d, w, y, tab, sem = refs[-10:-6], *refs[-6:]
    load = pltpu.make_async_copy(w_hbm.at[layer], w, sem)
    load.start()
    t, r = pos[0], pos[1]
    n_own = dn.shape[0]
    halo_at = pl.multiple_of((1 - r) * (n_own + WIDE), WIDE)
    zero_at = pl.multiple_of(r * (n_own + WIDE), WIDE)
    edge = zc.shape[0] - n_own
    d[pl.ds(zero_at, WIDE), :] = jnp.zeros((WIDE, 3 * LANES), BF16)
    rstd, own, oth = norm_tables(st, t, pos[2], pos[3], float(n_own), total)
    scale = gs[layer : layer + 1, :] * rstd
    added = functools.reduce(jnp.add, [sums[i] for i in range(sums.shape[0])])
    shift_sum, gain_sum = added[0:1], added[1:2]
    slope = scale * gain_sum / total
    tab[0:1] = scale
    tab[1:2] = slope * rstd
    tab[2:3] = scale * shift_sum / total + slope * own
    tab[3:4] = scale * shift_sum / total + slope * oth

    def spread_columns(v, at):
        rows = v.shape[0]
        column = lax.broadcasted_iota(jnp.int32, v.shape, 0) % WIDE
        ahead = jnp.where(column == WIDE - 1, 0.0, pltpu.roll(v, rows - 1, 0))
        behind = jnp.where(column == 0, 0.0, pltpu.roll(v, 1, 0))
        d[pl.ds(at, rows), 0:128] = ahead.astype(BF16)
        d[pl.ds(at, rows), 128:256] = v.astype(BF16)
        d[pl.ds(at, rows), 256:384] = behind.astype(BF16)

    def body(j, carry):
        rows = pair_rows(j)
        v = dn[rows, :] * tab[0:1, :] - tab[2:3, :] - zc[rows, :].astype(F32) * tab[1:2, :]
        spread_columns(v, pl.multiple_of(j * 2 * WIDE + WIDE, WIDE))
        return carry

    lax.fori_loop(0, n_own // (2 * WIDE), body, 0)
    near = n_own if edge == WIDE else pl.multiple_of(n_own + r * WIDE, WIDE)
    near = zc[pl.ds(near, WIDE), :].astype(F32)
    spread_columns(dedge[...] * tab[0:1, :] - tab[3:4, :] - near * tab[1:2, :], halo_at)
    d_out[...] = d[WIDE : WIDE + n_own, :]
    load.wait()
    lhs = jnp.concatenate([d[(2 - i) * WIDE : (2 - i) * WIDE + n_own, :] for i in range(3)], axis=1)
    rhs = jnp.concatenate([w[:, i * CHANS : (i + 1) * CHANS] for i in range(9)], axis=0)
    y[...] = jnp.dot(lhs, rhs, preferred_element_type=F32)

    def share(j, carry):
        rows = pair_rows(j)
        for k in range(GROUPS):
            outs[k][rows, :] = y[rows, pl.ds(lane_of(t ^ k), LANES)].astype(BF16)
        return carry

    lax.fori_loop(0, n_own // (2 * WIDE), share, 0)


def bwd_step(layer, total, pos, dn, dedge, sums, zc, st, gs, weights, ties):
    n_own = dn.shape[0]
    part = pltpu.VMEM((n_own, LANES), BF16)
    return pl.pallas_call(
        functools.partial(bwd_kernel, layer, total),
        out_shape=(
            part,
            part,
            part,
            part,
            pltpu.VMEM((n_own, 3 * LANES), BF16),
        ),
        in_specs=[SMEM] + [VMEM] * 6 + [ANY] + [FREE] * len(ties),
        out_specs=(VMEM,) * 5,
        scratch_shapes=[
            pltpu.VMEM((n_own + 2 * WIDE, 3 * LANES), BF16),
            pltpu.VMEM((LANES, 9 * CHANS), BF16),
            pltpu.VMEM((n_own, CHANS), F32),
            pltpu.VMEM((8, LANES), F32),
            pltpu.SemaphoreType.DMA,
        ],
        compiler_params=PARAMS,
        cost_estimate=pl.CostEstimate(
            flops=2 * n_own * 9 * CHANS * LANES, bytes_accessed=4 * 1024 * 1024, transcendentals=0
        ),
        name="conv_backward",
    )(pos, dn, dedge, sums, zc, st, gs, in_hbm(weights), *ties)


def last_kernel(t0, t1, t2, t3, tie, out):
    def body(j, carry):
        rows = pair_rows(j)
        out[rows, :] = functools.reduce(jnp.add, [term[rows, :].astype(F32) for term in (t0, t1, t2, t3)])
        return carry

    lax.fori_loop(0, out.shape[0] // (2 * WIDE), body, 0)


def last_step(terms, tie):
    return pl.pallas_call(
        last_kernel,
        out_shape=jax.ShapeDtypeStruct(terms[0].shape, F32),
        in_specs=[VMEM] * 4 + [FREE],
        out_specs=VMEM,
        compiler_params=PARAMS,
        name="add_terms",
    )(*terms, tie)


def quarters_kernel(parts, *refs):
    out = refs[-1]
    total = functools.reduce(jnp.add, [parts[i].astype(F32) for i in range(4)]).astype(BF16)
    for i in range(4):
        out[i] = total


def add_quarters(parts, ties):
    return pl.pallas_call(
        quarters_kernel,
        out_shape=pltpu.VMEM(parts.shape, BF16),
        in_specs=[VMEM] + [FREE] * len(ties),
        out_specs=VMEM,
        compiler_params=PARAMS,
        cost_estimate=pl.CostEstimate(flops=parts.size, bytes_accessed=4 * parts.size, transcendentals=0),
        name="add_quarters",
    )(parts, *ties)


def halves_kernel(keep, got, out):
    out[...] = (keep[...].astype(F32) + got[...].astype(F32)).astype(BF16)


def add_halves(keep, got):
    return pl.pallas_call(
        halves_kernel,
        out_shape=jax.ShapeDtypeStruct(keep.shape, BF16),
        in_specs=[VMEM] * 2,
        out_specs=VMEM,
        compiler_params=PARAMS,
        cost_estimate=pl.CostEstimate(flops=keep.size, bytes_accessed=6 * keep.size, transcendentals=0),
        name="add_halves",
    )(keep, got)


def wgrad_kernel(layer, pos, d, hb_hbm, tie, keep, send, hb, grad, sem):
    load = pltpu.make_async_copy(hb_hbm.at[layer], hb, sem)
    load.start()
    n_own = d.shape[0]
    lhs = d[...]
    load.wait()
    for i in range(3):
        part = lax.dot_general(
            lhs, hb[i * WIDE : i * WIDE + n_own, :], (((0,), (0,)), ((), ())), preferred_element_type=F32
        ).astype(BF16)
        for s in range(3):
            grad[:, (3 * i + s) * CHANS : (3 * i + s + 1) * CHANS] = part[s * LANES : (s + 1) * LANES]
    half = LANES // 2
    keep[...] = grad[pl.ds(pl.multiple_of(pos[1] * half, half), half), :]
    send[...] = grad[pl.ds(pl.multiple_of((1 - pos[1]) * half, half), half), :]


def wgrad_step(layer, pos, d, kept, tie):
    half = pltpu.VMEM((LANES // 2, 9 * CHANS), BF16)
    return pl.pallas_call(
        functools.partial(wgrad_kernel, layer),
        out_shape=(half, half),
        in_specs=[SMEM, VMEM, ANY, FREE],
        out_specs=(VMEM, VMEM),
        scratch_shapes=[
            pltpu.VMEM(kept.shape[1:], BF16),
            pltpu.VMEM((LANES, 9 * CHANS), BF16),
            pltpu.SemaphoreType.DMA,
        ],
        compiler_params=PARAMS,
        cost_estimate=pl.CostEstimate(
            flops=2 * d.shape[0] * 9 * CHANS * LANES, bytes_accessed=3 * 1024 * 1024, transcendentals=0
        ),
        name="kernel_gradient",
    )(pos, d, in_hbm(kept), tie)


def place_kernel(pos, mine, other, *refs):
    refs[-1][0] = jnp.where(pl.program_id(0) == pos[1], mine[...], other[...]).astype(F32)


def place_step(layer, pos, mine, other, whole, layers):
    half = LANES // 2
    block = pl.BlockSpec((half, 9 * CHANS), lambda i: (0, 0))
    return pl.pallas_call(
        place_kernel,
        grid=(2,),
        out_shape=jax.ShapeDtypeStruct((layers, LANES, 9 * CHANS), F32),
        in_specs=[SMEM, block, block] + ([] if whole is None else [ANY]),
        out_specs=pl.BlockSpec((1, half, 9 * CHANS), lambda i: (layer, i, 0)),
        input_output_aliases={} if whole is None else {3: 0},
        compiler_params=PARAMS,
        cost_estimate=pl.CostEstimate(flops=0, bytes_accessed=4 * 1024 * 1024, transcendentals=0),
        name="place_gradient",
    )(pos, mine, other, *(() if whole is None else (whole,)))


def swap_with(value, axis, k):
    return lax.ppermute(value, axis, [(i, i ^ k) for i in range(lax.axis_size(axis))])


def spread(own):
    return (own, *[swap_with(own, "tensor", k) for k in range(1, GROUPS)])


def halo_of_input(x, half):
    n_own = x.shape[0]
    edge = jnp.where(half == 0, x[n_own - WIDE :], x[:WIDE])
    return jnp.concatenate([x, swap_with(edge, "rows", 1)], axis=0)


def fast_local(section_input, conv_weights, norm_gains, norm_shifts, out_grad, out_mask):
    images, rows_here, width = out_mask.shape
    layers = conv_weights.shape[0]
    n_own = rows_here * width
    parts = lax.axis_size("dp") * lax.axis_size("rows")
    total = float(n_own * parts)
    t, half = lax.axis_index("tensor"), lax.axis_index("rows")
    image = lax.axis_index("dp")
    pos = jnp.stack([t, half, 2 * image + half, 2 * image + 1 - half]).astype(jnp.int32)
    middle = layers // 2
    x = to_maps(section_input, width).reshape(n_own, LANES)
    slots = spread(halo_of_input(x, half))
    pad = jnp.zeros((8 - layers, LANES), F32)
    tables = spread(jnp.concatenate([norm_gains, pad, norm_shifts, pad], axis=0))
    top_grad = (to_maps(out_grad, width) * out_mask[..., None].astype(BF16)).reshape(n_own, LANES)

    st, kept = None, None
    everyone = ("dp", "rows", "tensor")
    devices = parts * GROUPS
    kept_z, kept_st = [], []
    for layer in range(layers):
        edge = 2 * WIDE if layer + 1 == middle else WIDE
        kept, zc, rim, local = fwd_step(
            layer, layer == middle, edge, total, pos, slots, st, tables, conv_weights, kept, n_own, devices
        )
        rim = swap_with(rim, "rows", 1)
        st = lax.all_to_all(local, everyone, split_axis=0, concat_axis=0, tiled=True)
        st = st.reshape(parts, GROUPS, 8, LANES)
        zc = lax.dynamic_update_slice_in_dim(zc, rim, n_own, axis=0)
        kept_z.append(zc)
        kept_st.append(st)
        if layer + 1 < layers:
            slots = spread(zc)
    top = layers - 1
    h_last, dn, rim, sums = below_step(
        top, False, total, pos, kept_z[top], kept_st[top], tables[0], (top_grad,), parts
    )
    sum_list, pairs = [None] * layers, [None] * layers
    ties = ()
    for layer in range(layers - 1, -1, -1):
        rim = swap_with(rim, "rows", 1)
        sums = lax.all_to_all(sums, ("dp", "rows"), split_axis=0, concat_axis=0, tiled=True)
        sum_list[layer] = sums
        *terms, d = bwd_step(
            layer, total, pos, dn, rim, sums, kept_z[layer], kept_st[layer], tables[0], conv_weights, ties
        )
        terms = (terms[0], *[swap_with(terms[k], "tensor", k) for k in range(1, GROUPS)])
        keep, send = wgrad_step(layer, pos, d, kept, terms[1])
        pairs[layer] = add_halves(keep, swap_with(send, "rows", 1))
        ties = (pairs[layer],)
        if layer > 0:
            below = layer - 1
            dn, rim, sums = below_step(
                below, layer == middle, total, pos, kept_z[below], kept_st[below], tables[0], terms, parts, keep
            )
        else:
            grad = last_step(terms, keep)
    ahead, back = [[0, 1, 2, 3]], [[3, 2, 1, 0]]
    upper = lax.psum((pairs[5], pairs[4]), "dp", axis_index_groups=ahead)
    mid = lax.psum((pairs[3], pairs[2]), "dp", axis_index_groups=back)

    def reduce_images(pair, ties):
        rows = pair.shape[0] // 4
        parts = lax.all_to_all(pair.reshape(4, rows, -1), "dp", split_axis=0, concat_axis=0, tiled=True)
        parts = lax.all_to_all(add_quarters(parts, ties), "dp", split_axis=0, concat_axis=0, tiled=True)
        return parts.reshape(pair.shape)

    done = {5: upper[0], 4: upper[1], 3: mid[0], 2: mid[1], 1: reduce_images(pairs[1], ())}
    whole = None
    for layer in range(layers - 1, -1, -1):
        if layer == 0:
            done[0] = reduce_images(pairs[0], (in_hbm(whole),))
        whole = place_step(layer, pos, done[layer], swap_with(done[layer], "rows", 1), whole, layers)
    sums = jnp.sum(jnp.stack(sum_list), axis=1)
    shape = (images, rows_here, width, LANES)
    return (
        from_maps(h_last.reshape(shape)),
        from_maps(grad.reshape(shape)),
        whole,
        sums[:, 1],
        sums[:, 0],
    )


def solution(mesh):
    in_specs = (
        P("dp", "rows", "tensor"),
        P(None, "tensor", None),
        P(None, "tensor"),
        P(None, "tensor"),
        P("dp", "rows", "tensor"),
        P("dp", "rows", None),
    )
    out_specs = (
        P("dp", "rows", "tensor"),
        P("dp", "rows", "tensor"),
        P(None, "tensor", None),
        P(None, "tensor"),
        P(None, "tensor"),
    )
    local = fast_local if fits_kernels(mesh) else generic_local
    return jax.shard_map(local, mesh=mesh, in_specs=in_specs, out_specs=out_specs, check_vma=False)
```

```python
import functools

import jax
import jax.numpy as jnp
from jax import lax
from jax.experimental import pallas as pl
from jax.experimental.pallas import tpu as pltpu
from jax.sharding import PartitionSpec as P

EPS = 1e-05


def padded_2(cells, sides, width):
    for axis, dim in sides:
        count = lax.axis_size(axis)
        ends = count - 1
        head = lax.slice_in_dim(cells, 0, width, axis=dim)
        tail = lax.slice_in_dim(cells, cells.shape[dim] - width, cells.shape[dim], axis=dim)
        cells = jnp.concatenate(
            [
                lax.ppermute(tail, axis, [(i, (i + 1) % count) for i in range(ends)]),
                cells,
                lax.ppermute(head, axis, [((i + 1) % count, i) for i in range(ends)]),
            ],
            axis=dim,
        )
    return cells


def to_maps(flat, width):
    count, high, merged = flat.shape
    return flat.reshape(count, high, merged // width, width).transpose(0, 1, 3, 2)


def from_maps(maps):
    count, high, wide, chans = maps.shape
    return maps.transpose(0, 1, 3, 2).reshape(count, high, chans * wide)


def spatial_conv(padded, kernel):
    return lax.conv_general_dilated(
        padded,
        kernel,
        (1, 1),
        ((0, 0), (1, 1)),
        dimension_numbers=("NHWC", "HWIO", "NHWC"),
        preferred_element_type=jnp.float32,
    )


def flipped(kernel):
    return jnp.transpose(kernel[::-1, ::-1], (0, 1, 3, 2))


def pool_unpool(values):
    count, high, wide, chans = values.shape
    blocks = values.reshape(count, high // 2, 2, wide // 2, 2, chans)
    pooled = jax.nn.logsumexp(blocks, axis=(2, 4), keepdims=True)
    return (jnp.exp(blocks - pooled) * pooled).reshape(values.shape)


def moments(conv_out, total_pixels):
    summed = lax.psum(jnp.sum(conv_out, axis=(0, 1, 2)), ("dp", "rows"))
    mean = summed / total_pixels
    spread = lax.psum(jnp.sum(jnp.square(conv_out - mean), axis=(0, 1, 2)), ("dp", "rows"))
    var = spread / total_pixels
    return (mean, lax.rsqrt(var + EPS))


def kernel_grad(whole, dconv):
    images, rows_here, width, chans = dconv.shape
    widened = jnp.pad(whole, ((0, 0), (0, 0), (1, 1), (0, 0)))
    stacked = []
    for row_off in range(3):
        line = []
        for col_off in range(3):
            window = widened[:, row_off : row_off + rows_here, col_off : col_off + width, :]
            line.append(
                jnp.einsum("bhwc,bhwo->co", window, dconv, preferred_element_type=jnp.float32)
            )
        stacked.append(jnp.stack(line))
    return jnp.stack(stacked)


def generic_local(section_input, conv_weights, norm_gains, norm_shifts, out_grad, out_mask):
    width = out_mask.shape[2]
    images, rows_here = (out_mask.shape[0], out_mask.shape[1])
    total_pixels = float(images * rows_here * width * lax.axis_size("dp") * lax.axis_size("rows"))
    layers, out_here, flat_in = conv_weights.shape
    chans_in = flat_in // 9
    kernels_hwio = conv_weights.reshape(layers, out_here, 3, 3, chans_in).transpose(0, 2, 3, 4, 1)
    middle = layers // 2
    kept = []
    acting = to_maps(section_input, width)
    current = acting.astype(jnp.float32)
    pre_pool = current
    for index in range(layers):
        if index == middle:
            pre_pool = current
            acting = pool_unpool(pre_pool).astype(jnp.bfloat16)
        padded = padded_2(acting, (("rows", 1),), 1)
        whole = lax.all_gather(padded, "tensor", axis=3, tiled=True)
        conv_out = spatial_conv(whole, kernels_hwio[index])
        mean, rstd = moments(conv_out, total_pixels)
        normed = (conv_out - mean) * rstd
        shifted = normed * norm_gains[index] + norm_shifts[index]
        current = jax.nn.silu(shifted)
        acting = current.astype(jnp.bfloat16)
        kept.append((whole, normed, shifted, rstd))
    grad = to_maps(out_grad, width).astype(jnp.float32) * out_mask[..., None].astype(jnp.float32)
    kernel_list = [None] * layers
    gain_list = [None] * layers
    shift_list = [None] * layers
    for index in range(layers - 1, -1, -1):
        whole, normed, shifted, rstd = kept[index]
        unused, pull_silu = jax.vjp(jax.nn.silu, shifted)
        dshift = pull_silu(grad)[0]
        gain_sum, shift_sum = lax.psum(
            (jnp.sum(dshift * normed, axis=(0, 1, 2)), jnp.sum(dshift, axis=(0, 1, 2))),
            ("dp", "rows"),
        )
        gain_list[index] = gain_sum
        shift_list[index] = shift_sum
        dconv = (
            norm_gains[index]
            * rstd
            * (dshift - shift_sum / total_pixels - normed * gain_sum / total_pixels)
        ).astype(jnp.bfloat16)
        summed_kernel = lax.psum(
            kernel_grad(whole, dconv).astype(jnp.bfloat16), ("dp", "rows")
        ).astype(jnp.float32)
        kernel_list[index] = summed_kernel.transpose(3, 0, 1, 2).reshape(out_here, flat_in)
        grad_rim = padded_2(dconv, (("rows", 1),), 1)
        partial_terms = spatial_conv(grad_rim, flipped(kernels_hwio[index]))
        grad_in = lax.psum_scatter(
            partial_terms.astype(jnp.bfloat16), "tensor", scatter_dimension=3, tiled=True
        ).astype(jnp.float32)
        if index == middle:
            unused, pull_pool = jax.vjp(pool_unpool, pre_pool)
            grad = pull_pool(grad_in)[0]
        else:
            grad = grad_in
    return (
        from_maps(acting),
        from_maps(grad),
        jnp.stack(kernel_list),
        jnp.stack(gain_list),
        jnp.stack(shift_list),
    )


GROUPS = 4
LANES = 128
WIDE = 48
CHANS = GROUPS * LANES
F32 = jnp.float32
BF16 = jnp.bfloat16
VMEM = pl.BlockSpec(memory_space=pltpu.VMEM)
SMEM = pl.BlockSpec(memory_space=pltpu.SMEM)
ANY = pl.BlockSpec(memory_space=pltpu.HBM)
FREE = pl.BlockSpec(memory_space=pl.ANY)
PARAMS = pltpu.CompilerParams(vmem_limit_bytes=20 * 1024 * 1024)


def in_hbm(value):
    return pltpu.with_memory_space_constraint(value, pltpu.HBM)


def fits_kernels(mesh):
    return mesh.shape["tensor"] == GROUPS and mesh.shape["rows"] == 2 and mesh.shape["dp"] == 4


def sigmoid(v):
    return 0.5 * jnp.tanh(0.5 * v) + 0.5


def swap_columns(v):
    column = lax.broadcasted_iota(jnp.int32, v.shape, 0)
    return jnp.where(column % 2 == 0, pltpu.roll(v, WIDE - 1, 0), pltpu.roll(v, 1, 0))


def soft_parts(h):
    top = jnp.maximum(h[0], h[1])
    top = jnp.maximum(top, swap_columns(top))
    e0, e1 = jnp.exp(h[0] - top), jnp.exp(h[1] - top)
    total = e0 + e1
    total = total + swap_columns(total)
    pooled = top + jnp.log(total)
    inverse = 1.0 / total
    return e0 * inverse, e1 * inverse, pooled


def soft(h):
    h = h.reshape(2, WIDE, LANES)
    q0, q1, pooled = soft_parts(h)
    return jnp.concatenate([q0 * pooled, q1 * pooled], axis=0)


def soft_pull(h, grad):
    h = h.reshape(2, WIDE, LANES)
    grad = grad.reshape(2, WIDE, LANES)
    q0, q1, pooled = soft_parts(h)
    mix = q0 * grad[0] + q1 * grad[1]
    mix = mix + swap_columns(mix)
    return jnp.concatenate(
        [q0 * (pooled * (grad[0] - mix) + mix), q1 * (pooled * (grad[1] - mix) + mix)], axis=0
    )


def norm_tables(st, group, i_own, i_oth, n_local, total):
    parts = st.shape[0]
    group = 0 if st.shape[1] == 1 else group
    blocks = [st[i, group] for i in range(parts)]
    summed = functools.reduce(jnp.add, blocks)
    mean = summed[0:1] / parts
    apart = functools.reduce(jnp.add, [jnp.square(b - mean) for b in blocks])
    rstd = lax.rsqrt((summed[1:2] + n_local * apart[0:1]) / total + EPS)
    return rstd, (st[i_own, group, 0:1] - mean) * rstd, (st[i_oth, group, 0:1] - mean) * rstd


def left_right(y0, y1, y2):
    rows = y0.shape[0]
    column = lax.broadcasted_iota(jnp.int32, y0.shape, 0) % WIDE
    before = jnp.where(column == 0, 0.0, pltpu.roll(y0, 1, 0))
    after = jnp.where(column == WIDE - 1, 0.0, pltpu.roll(y2, rows - 1, 0))
    return before + y1 + after


def lane_of(group):
    return pl.multiple_of(group * LANES, LANES)


def edge_start(n_own, edge, half):
    return pl.multiple_of((1 - half) * (n_own - edge), WIDE)


def pair_rows(j):
    return pl.ds(pl.multiple_of(j * 2 * WIDE, 2 * WIDE), 2 * WIDE)


def fold(v):
    return jnp.sum(v.reshape(v.shape[0] // 8, 8, LANES), axis=0)


def fwd_kernel(first, pool, layer, total, edge_out, *refs):
    pos, zs = refs[0], refs[1:5]
    if first:
        w_hbm, rest = refs[5], refs[6:]
    else:
        rims, st, gss, w_hbm, rest = refs[5], refs[6], refs[7:11], refs[11], refs[13:]
    hb_out, zc_out, edge_ref, st_out, hb, w, y, z, tab, hs, sem = rest
    load = pltpu.make_async_copy(w_hbm.at[layer], w, sem.at[0])
    load.start()
    save = pltpu.make_async_copy(hb, hb_out.at[layer], sem.at[1])
    t, r = pos[0], pos[1]
    n_own = z.shape[0]
    halo_at = pl.multiple_of((1 - r) * (n_own + WIDE), WIDE)
    zero_at = pl.multiple_of(r * (n_own + WIDE), WIDE)
    hb[pl.ds(zero_at, WIDE), :] = jnp.zeros((WIDE, CHANS), BF16)
    edge = WIDE if first else rims.shape[1]
    if not first:
        for k in range(GROUPS):
            rstd, own, oth = norm_tables(st, t ^ k, pos[2], pos[3], float(n_own), total)
            gain, shift = gss[k][layer - 1 : layer, :], gss[k][layer + 7 : layer + 8, :]
            tab[k, 0:1] = rstd * gain
            tab[k, 1:2] = own * gain + shift
            tab[k, 2:3] = oth * gain + shift

    def act(values, k, which):
        if first:
            return values
        n = values.astype(F32) * tab[k, 0:1, :] + tab[k, which : which + 1, :]
        h = n * sigmoid(n)
        return soft(h) if pool else h

    def body(j, carry):
        at = pl.multiple_of(j * 2 * WIDE, 2 * WIDE)
        for k in range(GROUPS):
            h = act(zs[k][pl.ds(at, 2 * WIDE), :], k, 1)
            hb[pl.ds(pl.multiple_of(at + WIDE, WIDE), 2 * WIDE), pl.ds(lane_of(t ^ k), LANES)] = h.astype(BF16)
        return carry

    lax.fori_loop(0, n_own // (2 * WIDE), body, 0)
    for k in range(GROUPS):
        h = act(zs[k][n_own : n_own + edge, :] if first else rims[t ^ k], k, 2)
        if edge > WIDE:
            hs[...] = h
            h = hs[pl.ds(pl.multiple_of(r * WIDE, WIDE), WIDE), :]
        hb[pl.ds(halo_at, WIDE), pl.ds(lane_of(t ^ k), LANES)] = h.astype(BF16)
    save.start()
    load.wait()
    lhs = jnp.concatenate([hb[i * WIDE : i * WIDE + n_own, :] for i in range(3)], axis=1)
    rhs = jnp.concatenate(
        [
            jnp.concatenate([w[:, (3 * i + s) * CHANS : (3 * i + s + 1) * CHANS] for i in range(3)], axis=1)
            for s in range(3)
        ],
        axis=0,
    )
    y[...] = lax.dot_general(lhs, rhs, (((1,), (1,)), ((), ())), preferred_element_type=F32)

    def add_up(j, acc):
        rows = pair_rows(j)
        v = left_right(y[rows, 0:128], y[rows, 128:256], y[rows, 256:384])
        z[rows, :] = v
        return acc + fold(v)

    steps = n_own // (2 * WIDE)
    summed = lax.fori_loop(0, steps, add_up, jnp.zeros((8, LANES), F32))
    mean = jnp.sum(summed, axis=0, keepdims=True) / n_own

    def centre(j, acc):
        rows = pair_rows(j)
        v = z[rows, :] - mean
        z[rows, :] = v
        zc_out[rows, :] = v.astype(BF16)
        return acc + fold(jnp.square(v))

    apart = lax.fori_loop(0, steps, centre, jnp.zeros((8, LANES), F32))
    sums = [mean, jnp.sum(apart, axis=0, keepdims=True), jnp.zeros((6, LANES), F32)]
    sums = jnp.concatenate(sums, axis=0)
    for i in range(st_out.shape[0]):
        st_out[i] = sums
    edge_ref[...] = zc_out[pl.ds(edge_start(n_own, edge_out, r), edge_out), :]
    save.wait()


def fwd_step(layer, pool, edge_out, total, pos, slots, rims, st, tables, weights, kept, n_own, devices):
    first = st is None
    layers = weights.shape[0]
    extra = () if first else (rims, st, *tables)
    return pl.pallas_call(
        functools.partial(fwd_kernel, first, pool, layer, total, edge_out),
        out_shape=(
            pltpu.HBM((layers, n_own + 2 * WIDE, CHANS), BF16),
            pltpu.VMEM((n_own, LANES), BF16),
            pltpu.VMEM((edge_out, LANES), BF16),
            pltpu.VMEM((devices, 8, LANES), F32),
        ),
        in_specs=[SMEM] + [VMEM] * (4 + len(extra)) + [ANY] * (1 if first else 2),
        out_specs=(ANY, VMEM, VMEM, VMEM),
        input_output_aliases={} if first else {6 + len(extra): 0},
        scratch_shapes=[
            pltpu.VMEM((n_own + 2 * WIDE, CHANS), BF16),
            pltpu.VMEM((LANES, 9 * CHANS), BF16),
            pltpu.VMEM((n_own, 3 * LANES), F32),
            pltpu.VMEM((n_own, LANES), F32),
            pltpu.VMEM((GROUPS, 8, LANES), F32),
            pltpu.VMEM((2 * WIDE, LANES), F32),
            pltpu.SemaphoreType.DMA((2,)),
        ],
        compiler_params=PARAMS,
        cost_estimate=pl.CostEstimate(
            flops=2 * n_own * 9 * CHANS * LANES, bytes_accessed=4 * 1024 * 1024, transcendentals=n_own * CHANS
        ),
        name="conv_forward",
    )(pos, *slots, *extra, in_hbm(weights), *(() if first else (in_hbm(kept),)))


def below_kernel(layer, pool, total, top, *refs):
    pos, zc, st, gs = refs[:4]
    if top:
        terms, h_out, dn_out, edge_out, sums_out, tab = refs[4:]
    else:
        terms, (dn_out, edge_out, sums_out, tab) = refs[4:8], refs[9:]
    n_own = dn_out.shape[0]
    rstd, own, oth = norm_tables(st, pos[0], pos[2], pos[3], float(n_own), total)
    tab[0:1], tab[1:2] = rstd, own
    tab[2:3], tab[3:4] = gs[layer : layer + 1, :], gs[layer + 8 : layer + 9, :]

    def body(j, accs):
        rows = pair_rows(j)
        xhat = zc[rows, :].astype(F32) * tab[0:1, :] + tab[1:2, :]
        n = xhat * tab[2:3, :] + tab[3:4, :]
        sig = sigmoid(n)
        h = n * sig
        if top:
            g = terms[rows, :].astype(F32)
            h_out[rows, :] = h.astype(BF16)
        else:
            g = functools.reduce(jnp.add, [term[rows, :].astype(F32) for term in terms])
        if pool:
            g = soft_pull(h, g)
        dn = g * (sig * (1.0 + n - h))
        dn_out[rows, :] = dn
        return accs[0] + fold(dn), accs[1] + fold(dn * xhat)

    zero = jnp.zeros((8, LANES), F32)
    sums = lax.fori_loop(0, n_own // (2 * WIDE), body, (zero, zero))
    sums = [jnp.sum(v, axis=0, keepdims=True) for v in sums]
    sums = jnp.concatenate(sums + [jnp.zeros((6, LANES), F32)], axis=0)
    for i in range(sums_out.shape[0]):
        sums_out[i] = sums
    edge_out[...] = dn_out[pl.ds(edge_start(n_own, WIDE, pos[1]), WIDE), :]


def below_step(layer, pool, total, pos, zc, st, gs, terms, parts, tie=None):
    n_own = terms[0].shape[0]
    top = len(terms) == 1
    ties = () if tie is None else (tie,)
    out_shape = [
        pltpu.VMEM((n_own, LANES), F32),
        pltpu.VMEM((WIDE, LANES), F32),
        pltpu.VMEM((parts, 8, LANES), F32),
    ]
    if top:
        out_shape = [jax.ShapeDtypeStruct((n_own, LANES), BF16)] + out_shape
    return pl.pallas_call(
        functools.partial(below_kernel, layer, pool, total, top),
        out_shape=tuple(out_shape),
        in_specs=[SMEM] + [VMEM] * (3 + len(terms)) + [FREE] * len(ties),
        out_specs=(VMEM,) * len(out_shape),
        scratch_shapes=[pltpu.VMEM((8, LANES), F32)],
        compiler_params=PARAMS,
        cost_estimate=pl.CostEstimate(flops=40 * n_own * LANES, bytes_accessed=1024 * 1024, transcendentals=n_own * LANES),
        name="silu_backward",
    )(pos, zc, st, gs, *terms, *ties)


def bwd_kernel(layer, total, *refs):
    pos, dn, dedge, sums, zc, zrim, st, gs, w_hbm = refs[:9]
    outs, d_out, d, w, y, tab, sem = refs[-10:-6], *refs[-6:]
    load = pltpu.make_async_copy(w_hbm.at[layer], w, sem)
    load.start()
    t, r = pos[0], pos[1]
    n_own = dn.shape[0]
    halo_at = pl.multiple_of((1 - r) * (n_own + WIDE), WIDE)
    zero_at = pl.multiple_of(r * (n_own + WIDE), WIDE)
    edge = zrim.shape[0]
    d[pl.ds(zero_at, WIDE), :] = jnp.zeros((WIDE, 3 * LANES), BF16)
    rstd, own, oth = norm_tables(st, t, pos[2], pos[3], float(n_own), total)
    scale = gs[layer : layer + 1, :] * rstd
    added = functools.reduce(jnp.add, [sums[i] for i in range(sums.shape[0])])
    shift_sum, gain_sum = added[0:1], added[1:2]
    slope = scale * gain_sum / total
    tab[0:1] = scale
    tab[1:2] = slope * rstd
    tab[2:3] = scale * shift_sum / total + slope * own
    tab[3:4] = scale * shift_sum / total + slope * oth

    def spread_columns(v, at):
        rows = v.shape[0]
        column = lax.broadcasted_iota(jnp.int32, v.shape, 0) % WIDE
        ahead = jnp.where(column == WIDE - 1, 0.0, pltpu.roll(v, rows - 1, 0))
        behind = jnp.where(column == 0, 0.0, pltpu.roll(v, 1, 0))
        d[pl.ds(at, rows), 0:128] = ahead.astype(BF16)
        d[pl.ds(at, rows), 128:256] = v.astype(BF16)
        d[pl.ds(at, rows), 256:384] = behind.astype(BF16)

    def body(j, carry):
        rows = pair_rows(j)
        v = dn[rows, :] * tab[0:1, :] - tab[2:3, :] - zc[rows, :].astype(F32) * tab[1:2, :]
        spread_columns(v, pl.multiple_of(j * 2 * WIDE + WIDE, WIDE))
        return carry

    lax.fori_loop(0, n_own // (2 * WIDE), body, 0)
    near = 0 if edge == WIDE else pl.multiple_of(r * WIDE, WIDE)
    near = zrim[pl.ds(near, WIDE), :].astype(F32)
    spread_columns(dedge[...] * tab[0:1, :] - tab[3:4, :] - near * tab[1:2, :], halo_at)
    d_out[...] = d[WIDE : WIDE + n_own, :]
    load.wait()
    lhs = jnp.concatenate([d[(2 - i) * WIDE : (2 - i) * WIDE + n_own, :] for i in range(3)], axis=1)
    rhs = jnp.concatenate([w[:, i * CHANS : (i + 1) * CHANS] for i in range(9)], axis=0)
    y[...] = jnp.dot(lhs, rhs, preferred_element_type=F32)

    def share(j, carry):
        rows = pair_rows(j)
        for k in range(GROUPS):
            outs[k][rows, :] = y[rows, pl.ds(lane_of(t ^ k), LANES)].astype(BF16)
        return carry

    lax.fori_loop(0, n_own // (2 * WIDE), share, 0)


def bwd_step(layer, total, pos, dn, dedge, sums, zc, zrim, st, gs, weights, ties):
    n_own = dn.shape[0]
    part = pltpu.VMEM((n_own, LANES), BF16)
    return pl.pallas_call(
        functools.partial(bwd_kernel, layer, total),
        out_shape=(
            part,
            part,
            part,
            part,
            pltpu.VMEM((n_own, 3 * LANES), BF16),
        ),
        in_specs=[SMEM] + [VMEM] * 7 + [ANY] + [FREE] * len(ties),
        out_specs=(VMEM,) * 5,
        scratch_shapes=[
            pltpu.VMEM((n_own + 2 * WIDE, 3 * LANES), BF16),
            pltpu.VMEM((LANES, 9 * CHANS), BF16),
            pltpu.VMEM((n_own, CHANS), F32),
            pltpu.VMEM((8, LANES), F32),
            pltpu.SemaphoreType.DMA,
        ],
        compiler_params=PARAMS,
        cost_estimate=pl.CostEstimate(
            flops=2 * n_own * 9 * CHANS * LANES, bytes_accessed=4 * 1024 * 1024, transcendentals=0
        ),
        name="conv_backward",
    )(pos, dn, dedge, sums, zc, zrim, st, gs, in_hbm(weights), *ties)


def last_kernel(t0, t1, t2, t3, *refs):
    out = refs[-1]

    def body(j, carry):
        rows = pair_rows(j)
        out[rows, :] = functools.reduce(jnp.add, [term[rows, :].astype(F32) for term in (t0, t1, t2, t3)])
        return carry

    lax.fori_loop(0, out.shape[0] // (2 * WIDE), body, 0)


def last_step(terms, ties):
    return pl.pallas_call(
        last_kernel,
        out_shape=jax.ShapeDtypeStruct(terms[0].shape, F32),
        in_specs=[VMEM] * 4 + [FREE] * len(ties),
        out_specs=VMEM,
        compiler_params=PARAMS,
        name="add_terms",
    )(*terms, *ties)


def quarters_kernel(parts, *refs):
    out = refs[-1]
    total = functools.reduce(jnp.add, [parts[i].astype(F32) for i in range(4)]).astype(BF16)
    for i in range(4):
        out[i] = total


def add_quarters(parts, ties):
    return pl.pallas_call(
        quarters_kernel,
        out_shape=pltpu.VMEM(parts.shape, BF16),
        in_specs=[VMEM] + [FREE] * len(ties),
        out_specs=VMEM,
        compiler_params=PARAMS,
        cost_estimate=pl.CostEstimate(flops=parts.size, bytes_accessed=4 * parts.size, transcendentals=0),
        name="add_quarters",
    )(parts, *ties)


def halves_kernel(keep, got, out):
    out[...] = (keep[...].astype(F32) + got[...].astype(F32)).astype(BF16)


def add_halves(keep, got):
    return pl.pallas_call(
        halves_kernel,
        out_shape=jax.ShapeDtypeStruct(keep.shape, BF16),
        in_specs=[VMEM] * 2,
        out_specs=VMEM,
        compiler_params=PARAMS,
        cost_estimate=pl.CostEstimate(flops=keep.size, bytes_accessed=6 * keep.size, transcendentals=0),
        name="add_halves",
    )(keep, got)


def wgrad_kernel(layer, pos, d, hb_hbm, tie, keep, send, hb, grad, sem):
    load = pltpu.make_async_copy(hb_hbm.at[layer], hb, sem)
    load.start()
    n_own = d.shape[0]
    lhs = d[...]
    load.wait()
    for i in range(3):
        part = lax.dot_general(
            lhs, hb[i * WIDE : i * WIDE + n_own, :], (((0,), (0,)), ((), ())), preferred_element_type=F32
        ).astype(BF16)
        for s in range(3):
            grad[:, (3 * i + s) * CHANS : (3 * i + s + 1) * CHANS] = part[s * LANES : (s + 1) * LANES]
    half = LANES // 2
    keep[...] = grad[pl.ds(pl.multiple_of(pos[1] * half, half), half), :]
    send[...] = grad[pl.ds(pl.multiple_of((1 - pos[1]) * half, half), half), :]


def wgrad_step(layer, pos, d, kept, tie):
    half = pltpu.VMEM((LANES // 2, 9 * CHANS), BF16)
    return pl.pallas_call(
        functools.partial(wgrad_kernel, layer),
        out_shape=(half, half),
        in_specs=[SMEM, VMEM, ANY, FREE],
        out_specs=(VMEM, VMEM),
        scratch_shapes=[
            pltpu.VMEM(kept.shape[1:], BF16),
            pltpu.VMEM((LANES, 9 * CHANS), BF16),
            pltpu.SemaphoreType.DMA,
        ],
        compiler_params=PARAMS,
        cost_estimate=pl.CostEstimate(flops=1024, bytes_accessed=1024, transcendentals=0),
        name="kernel_gradient",
    )(pos, d, in_hbm(kept), tie)


def place_kernel(pos, mine, other, *refs):
    refs[-1][0] = jnp.where(pl.program_id(0) == pos[1], mine[...], other[...]).astype(F32)


def place_step(layer, pos, mine, other, whole, layers):
    half = LANES // 2
    block = pl.BlockSpec((half, 9 * CHANS), lambda i: (0, 0))
    return pl.pallas_call(
        place_kernel,
        grid=(2,),
        out_shape=jax.ShapeDtypeStruct((layers, LANES, 9 * CHANS), F32),
        in_specs=[SMEM, block, block] + ([] if whole is None else [ANY]),
        out_specs=pl.BlockSpec((1, half, 9 * CHANS), lambda i: (layer, i, 0)),
        input_output_aliases={} if whole is None else {3: 0},
        compiler_params=PARAMS,
        cost_estimate=pl.CostEstimate(flops=0, bytes_accessed=4 * 1024 * 1024, transcendentals=0),
        name="place_gradient",
    )(pos, mine, other, *(() if whole is None else (whole,)))


def swap_with(value, axis, k):
    return lax.ppermute(value, axis, [(i, i ^ k) for i in range(lax.axis_size(axis))])


def spread(own):
    return (own, *[swap_with(own, "tensor", k) for k in range(1, GROUPS)])


def halo_of_input(x, half):
    n_own = x.shape[0]
    edge = jnp.where(half == 0, x[n_own - WIDE :], x[:WIDE])
    return jnp.concatenate([x, swap_with(edge, "rows", 1)], axis=0)


def fast_local(section_input, conv_weights, norm_gains, norm_shifts, out_grad, out_mask):
    images, rows_here, width = out_mask.shape
    layers = conv_weights.shape[0]
    n_own = rows_here * width
    parts = lax.axis_size("dp") * lax.axis_size("rows")
    total = float(n_own * parts)
    t, half = lax.axis_index("tensor"), lax.axis_index("rows")
    image = lax.axis_index("dp")
    pos = jnp.stack([t, half, 2 * image + half, 2 * image + 1 - half]).astype(jnp.int32)
    middle = layers // 2
    x = to_maps(section_input, width).reshape(n_own, LANES)
    slots = spread(halo_of_input(x, half))
    pad = jnp.zeros((8 - layers, LANES), F32)
    tables = spread(jnp.concatenate([norm_gains, pad, norm_shifts, pad], axis=0))
    top_grad = (to_maps(out_grad, width) * out_mask[..., None].astype(BF16)).reshape(n_own, LANES)

    rims, st, kept = None, None, None
    halves = ("dp", "rows")
    kept_z, kept_rim, kept_st = [], [], []
    for layer in range(layers):
        last = layer + 1 == layers
        edge = 2 * WIDE if layer + 1 == middle else WIDE
        everyone = halves if last else (*halves, "tensor")
        devices = parts if last else parts * GROUPS
        kept, zc, rim, local = fwd_step(
            layer, layer == middle, edge, total, pos, slots, rims, st, tables, conv_weights, kept, n_own, devices
        )
        rim = swap_with(rim, "rows", 1)
        if not last:
            slots = spread(zc)
            rim, local = lax.optimization_barrier((rim, local))
            rims = jnp.broadcast_to(rim, (GROUPS, edge, LANES))
            rims = lax.all_to_all(rims, "tensor", split_axis=0, concat_axis=0, tiled=True)
        st = lax.all_to_all(local, everyone, split_axis=0, concat_axis=0, tiled=True)
        st = st.reshape(parts, devices // parts, 8, LANES)
        kept_z.append(zc)
        kept_rim.append(rim)
        kept_st.append(st)
    top = layers - 1
    h_last, dn, rim, sums = below_step(
        top, False, total, pos, kept_z[top], kept_st[top], tables[0], (top_grad,), parts
    )

    def reduce_images(pair, ties):
        rows = pair.shape[0] // 4
        pieces = lax.all_to_all(pair.reshape(4, rows, -1), "dp", split_axis=0, concat_axis=0, tiled=True)
        pieces = lax.all_to_all(add_quarters(pieces, ties), "dp", split_axis=0, concat_axis=0, tiled=True)
        return pieces.reshape(pair.shape)

    def place(layer, mine, whole):
        return place_step(layer, pos, mine, swap_with(mine, "rows", 1), whole, layers)

    sum_list, pairs = [None] * layers, [None] * layers
    ahead, back = [[0, 1, 2, 3]], [[3, 2, 1, 0]]
    ties, whole = (), None
    for layer in range(layers - 1, -1, -1):
        rim = swap_with(rim, "rows", 1)
        sums = lax.all_to_all(sums, halves, split_axis=0, concat_axis=0, tiled=True)
        sum_list[layer] = sums
        *terms, d = bwd_step(
            layer,
            total,
            pos,
            dn,
            rim,
            sums,
            kept_z[layer],
            kept_rim[layer],
            kept_st[layer],
            tables[0],
            conv_weights,
            ties,
        )
        terms = (terms[0], *[swap_with(terms[k], "tensor", k) for k in range(1, GROUPS)])
        keep, send = wgrad_step(layer, pos, d, kept, terms[1])
        pairs[layer] = add_halves(keep, swap_with(send, "rows", 1))
        ties = (pairs[layer],)
        if layer == 4:
            upper = lax.psum((pairs[5], pairs[4]), "dp", axis_index_groups=ahead)
        if layer == 2:
            mid = lax.psum((pairs[3], pairs[2]), "dp", axis_index_groups=back)
            whole = place(4, upper[1], place(5, upper[0], None))
            ties = (pairs[2], in_hbm(whole))
        if layer > 0:
            below = layer - 1
            dn, rim, sums = below_step(
                below, layer == middle, total, pos, kept_z[below], kept_st[below], tables[0], terms, parts, keep
            )
        else:
            grad = last_step(terms, (keep,))
    whole = place(1, reduce_images(pairs[1], ()), whole)
    whole = place(2, mid[1], place(3, mid[0], whole))
    whole = place(0, reduce_images(pairs[0], (in_hbm(whole),)), whole)
    sums = jnp.sum(jnp.stack(sum_list), axis=1)
    shape = (images, rows_here, width, LANES)
    return (
        from_maps(h_last.reshape(shape)),
        from_maps(grad.reshape(shape)),
        whole,
        sums[:, 1],
        sums[:, 0],
    )


def solution(mesh):
    in_specs = (
        P("dp", "rows", "tensor"),
        P(None, "tensor", None),
        P(None, "tensor"),
        P(None, "tensor"),
        P("dp", "rows", "tensor"),
        P("dp", "rows", None),
    )
    out_specs = (
        P("dp", "rows", "tensor"),
        P("dp", "rows", "tensor"),
        P(None, "tensor", None),
        P(None, "tensor"),
        P(None, "tensor"),
    )
    local = fast_local if fits_kernels(mesh) else generic_local
    return jax.shard_map(local, mesh=mesh, in_specs=in_specs, out_specs=out_specs, check_vma=False)
```

```python
import functools

import jax
import jax.numpy as jnp
from jax import lax
from jax.experimental import pallas as pl
from jax.experimental.pallas import tpu as pltpu
from jax.sharding import PartitionSpec as P

EPS = 1e-05


def padded_2(cells, sides, width):
    for axis, dim in sides:
        count = lax.axis_size(axis)
        ends = count - 1
        head = lax.slice_in_dim(cells, 0, width, axis=dim)
        tail = lax.slice_in_dim(cells, cells.shape[dim] - width, cells.shape[dim], axis=dim)
        cells = jnp.concatenate(
            [
                lax.ppermute(tail, axis, [(i, (i + 1) % count) for i in range(ends)]),
                cells,
                lax.ppermute(head, axis, [((i + 1) % count, i) for i in range(ends)]),
            ],
            axis=dim,
        )
    return cells


def to_maps(flat, width):
    count, high, merged = flat.shape
    return flat.reshape(count, high, merged // width, width).transpose(0, 1, 3, 2)


def from_maps(maps):
    count, high, wide, chans = maps.shape
    return maps.transpose(0, 1, 3, 2).reshape(count, high, chans * wide)


def spatial_conv(padded, kernel):
    return lax.conv_general_dilated(
        padded,
        kernel,
        (1, 1),
        ((0, 0), (1, 1)),
        dimension_numbers=("NHWC", "HWIO", "NHWC"),
        preferred_element_type=jnp.float32,
    )


def flipped(kernel):
    return jnp.transpose(kernel[::-1, ::-1], (0, 1, 3, 2))


def pool_unpool(values):
    count, high, wide, chans = values.shape
    blocks = values.reshape(count, high // 2, 2, wide // 2, 2, chans)
    pooled = jax.nn.logsumexp(blocks, axis=(2, 4), keepdims=True)
    return (jnp.exp(blocks - pooled) * pooled).reshape(values.shape)


def moments(conv_out, total_pixels):
    summed = lax.psum(jnp.sum(conv_out, axis=(0, 1, 2)), ("dp", "rows"))
    mean = summed / total_pixels
    spread = lax.psum(jnp.sum(jnp.square(conv_out - mean), axis=(0, 1, 2)), ("dp", "rows"))
    var = spread / total_pixels
    return (mean, lax.rsqrt(var + EPS))


def kernel_grad(whole, dconv):
    images, rows_here, width, chans = dconv.shape
    widened = jnp.pad(whole, ((0, 0), (0, 0), (1, 1), (0, 0)))
    stacked = []
    for row_off in range(3):
        line = []
        for col_off in range(3):
            window = widened[:, row_off : row_off + rows_here, col_off : col_off + width, :]
            line.append(
                jnp.einsum("bhwc,bhwo->co", window, dconv, preferred_element_type=jnp.float32)
            )
        stacked.append(jnp.stack(line))
    return jnp.stack(stacked)


def generic_local(section_input, conv_weights, norm_gains, norm_shifts, out_grad, out_mask):
    width = out_mask.shape[2]
    images, rows_here = (out_mask.shape[0], out_mask.shape[1])
    total_pixels = float(images * rows_here * width * lax.axis_size("dp") * lax.axis_size("rows"))
    layers, out_here, flat_in = conv_weights.shape
    chans_in = flat_in // 9
    kernels_hwio = conv_weights.reshape(layers, out_here, 3, 3, chans_in).transpose(0, 2, 3, 4, 1)
    middle = layers // 2
    kept = []
    acting = to_maps(section_input, width)
    current = acting.astype(jnp.float32)
    pre_pool = current
    for index in range(layers):
        if index == middle:
            pre_pool = current
            acting = pool_unpool(pre_pool).astype(jnp.bfloat16)
        padded = padded_2(acting, (("rows", 1),), 1)
        whole = lax.all_gather(padded, "tensor", axis=3, tiled=True)
        conv_out = spatial_conv(whole, kernels_hwio[index])
        mean, rstd = moments(conv_out, total_pixels)
        normed = (conv_out - mean) * rstd
        shifted = normed * norm_gains[index] + norm_shifts[index]
        current = jax.nn.silu(shifted)
        acting = current.astype(jnp.bfloat16)
        kept.append((whole, normed, shifted, rstd))
    grad = to_maps(out_grad, width).astype(jnp.float32) * out_mask[..., None].astype(jnp.float32)
    kernel_list = [None] * layers
    gain_list = [None] * layers
    shift_list = [None] * layers
    for index in range(layers - 1, -1, -1):
        whole, normed, shifted, rstd = kept[index]
        unused, pull_silu = jax.vjp(jax.nn.silu, shifted)
        dshift = pull_silu(grad)[0]
        gain_sum, shift_sum = lax.psum(
            (jnp.sum(dshift * normed, axis=(0, 1, 2)), jnp.sum(dshift, axis=(0, 1, 2))),
            ("dp", "rows"),
        )
        gain_list[index] = gain_sum
        shift_list[index] = shift_sum
        dconv = (
            norm_gains[index]
            * rstd
            * (dshift - shift_sum / total_pixels - normed * gain_sum / total_pixels)
        ).astype(jnp.bfloat16)
        summed_kernel = lax.psum(
            kernel_grad(whole, dconv).astype(jnp.bfloat16), ("dp", "rows")
        ).astype(jnp.float32)
        kernel_list[index] = summed_kernel.transpose(3, 0, 1, 2).reshape(out_here, flat_in)
        grad_rim = padded_2(dconv, (("rows", 1),), 1)
        partial_terms = spatial_conv(grad_rim, flipped(kernels_hwio[index]))
        grad_in = lax.psum_scatter(
            partial_terms.astype(jnp.bfloat16), "tensor", scatter_dimension=3, tiled=True
        ).astype(jnp.float32)
        if index == middle:
            unused, pull_pool = jax.vjp(pool_unpool, pre_pool)
            grad = pull_pool(grad_in)[0]
        else:
            grad = grad_in
    return (
        from_maps(acting),
        from_maps(grad),
        jnp.stack(kernel_list),
        jnp.stack(gain_list),
        jnp.stack(shift_list),
    )


GROUPS = 4
LANES = 128
WIDE = 48
CHANS = GROUPS * LANES
F32 = jnp.float32
BF16 = jnp.bfloat16
VMEM = pl.BlockSpec(memory_space=pltpu.VMEM)
SMEM = pl.BlockSpec(memory_space=pltpu.SMEM)
ANY = pl.BlockSpec(memory_space=pltpu.HBM)
FREE = pl.BlockSpec(memory_space=pl.ANY)
PARAMS = pltpu.CompilerParams(vmem_limit_bytes=20 * 1024 * 1024)


def in_hbm(value):
    return pltpu.with_memory_space_constraint(value, pltpu.HBM)


def fits_kernels(mesh):
    return mesh.shape["tensor"] == GROUPS and mesh.shape["rows"] == 2 and mesh.shape["dp"] == 4


def sigmoid(v):
    return 0.5 * jnp.tanh(0.5 * v) + 0.5


def swap_columns(v):
    column = lax.broadcasted_iota(jnp.int32, v.shape, 0)
    return jnp.where(column % 2 == 0, pltpu.roll(v, WIDE - 1, 0), pltpu.roll(v, 1, 0))


def soft_parts(h):
    top = jnp.maximum(h[0], h[1])
    top = jnp.maximum(top, swap_columns(top))
    e0, e1 = jnp.exp(h[0] - top), jnp.exp(h[1] - top)
    total = e0 + e1
    total = total + swap_columns(total)
    pooled = top + jnp.log(total)
    inverse = 1.0 / total
    return e0 * inverse, e1 * inverse, pooled


def soft(h):
    h = h.reshape(2, WIDE, LANES)
    q0, q1, pooled = soft_parts(h)
    return jnp.concatenate([q0 * pooled, q1 * pooled], axis=0)


def soft_pull(h, grad):
    h = h.reshape(2, WIDE, LANES)
    grad = grad.reshape(2, WIDE, LANES)
    q0, q1, pooled = soft_parts(h)
    mix = q0 * grad[0] + q1 * grad[1]
    mix = mix + swap_columns(mix)
    return jnp.concatenate(
        [q0 * (pooled * (grad[0] - mix) + mix), q1 * (pooled * (grad[1] - mix) + mix)], axis=0
    )


def norm_tables(st, group, i_own, i_oth, n_local, total):
    parts = st.shape[0]
    group = 0 if st.shape[1] == 1 else group
    blocks = [st[i, group] for i in range(parts)]
    summed = functools.reduce(jnp.add, blocks)
    mean = summed[0:1] / parts
    apart = functools.reduce(jnp.add, [jnp.square(b - mean) for b in blocks])
    rstd = lax.rsqrt((summed[1:2] + n_local * apart[0:1]) / total + EPS)
    return rstd, (st[i_own, group, 0:1] - mean) * rstd, (st[i_oth, group, 0:1] - mean) * rstd


def left_right(y0, y1, y2):
    rows = y0.shape[0]
    column = lax.broadcasted_iota(jnp.int32, y0.shape, 0) % WIDE
    before = jnp.where(column == 0, 0.0, pltpu.roll(y0, 1, 0))
    after = jnp.where(column == WIDE - 1, 0.0, pltpu.roll(y2, rows - 1, 0))
    return before + y1 + after


def lane_of(group):
    return pl.multiple_of(group * LANES, LANES)


def edge_start(n_own, edge, half):
    return pl.multiple_of((1 - half) * (n_own - edge), WIDE)


def pair_rows(j):
    return pl.ds(pl.multiple_of(j * 2 * WIDE, 2 * WIDE), 2 * WIDE)


def fold(v):
    return jnp.sum(v.reshape(v.shape[0] // 8, 8, LANES), axis=0)


def fwd_kernel(first, last, pool, layer, total, edge_out, *refs):
    pos = refs[0]
    if first:
        zs, w_hbm, rest = refs[1:5], refs[5], refs[6:]
    else:
        zall, rims, st, gss, w_hbm, rest = refs[1], refs[2:6], refs[6], refs[7:11], refs[11], refs[13:]
    if last:
        hb_out, zc_out, edge_ref, st_out, hb, w, y, z, tab, hs, sem = rest
    else:
        hb_out, zc_out, copies, edge_ref, st_out, hb, w, y, z, tab, hs, sem = rest
    load = pltpu.make_async_copy(w_hbm.at[layer], w, sem.at[0])
    load.start()
    save = pltpu.make_async_copy(hb, hb_out.at[layer], sem.at[1])
    t, r = pos[0], pos[1]
    n_own = z.shape[0]
    halo_at = pl.multiple_of((1 - r) * (n_own + WIDE), WIDE)
    zero_at = pl.multiple_of(r * (n_own + WIDE), WIDE)
    hb[pl.ds(zero_at, WIDE), :] = jnp.zeros((WIDE, CHANS), BF16)
    if first:
        for k in range(GROUPS):
            lanes = pl.ds(lane_of(t ^ k), LANES)
            hb[WIDE : WIDE + n_own, lanes] = zs[k][0:n_own, :]
            hb[pl.ds(halo_at, WIDE), lanes] = zs[k][n_own : n_own + WIDE, :]
    else:
        edge = rims[0].shape[0]
        for k in range(GROUPS):
            group = t ^ k
            rstd, own, oth = norm_tables(st, group, pos[2], pos[3], float(n_own), total)
            gain, shift = gss[k][layer - 1 : layer, :], gss[k][layer + 7 : layer + 8, :]
            tab[group, 0:1] = rstd * gain
            tab[group, 1:2] = own * gain + shift
            tab[group, 2:3] = oth * gain + shift

        def act(values, group, which):
            n = values.astype(F32) * tab[group, 0:1, :] + tab[group, which : which + 1, :]
            h = n * sigmoid(n)
            return soft(h) if pool else h

        def body(j, carry):
            at = pl.multiple_of(j * 2 * WIDE, 2 * WIDE)
            for group in range(GROUPS):
                h = act(zall[group, pl.ds(at, 2 * WIDE), :], group, 1)
                lanes = slice(group * LANES, (group + 1) * LANES)
                hb[pl.ds(pl.multiple_of(at + WIDE, WIDE), 2 * WIDE), lanes] = h.astype(BF16)
            return carry

        lax.fori_loop(0, n_own // (2 * WIDE), body, 0)
        for k in range(GROUPS):
            h = act(rims[k][...], t ^ k, 2)
            if edge > WIDE:
                hs[...] = h
                h = hs[pl.ds(pl.multiple_of(r * WIDE, WIDE), WIDE), :]
            hb[pl.ds(halo_at, WIDE), pl.ds(lane_of(t ^ k), LANES)] = h.astype(BF16)
    save.start()
    load.wait()
    lhs = jnp.concatenate([hb[i * WIDE : i * WIDE + n_own, :] for i in range(3)], axis=1)
    rhs = jnp.concatenate(
        [
            jnp.concatenate([w[:, (3 * i + s) * CHANS : (3 * i + s + 1) * CHANS] for i in range(3)], axis=1)
            for s in range(3)
        ],
        axis=0,
    )
    y[...] = lax.dot_general(lhs, rhs, (((1,), (1,)), ((), ())), preferred_element_type=F32)

    def add_up(j, acc):
        rows = pair_rows(j)
        v = left_right(y[rows, 0:128], y[rows, 128:256], y[rows, 256:384])
        z[rows, :] = v
        return acc + fold(v)

    steps = n_own // (2 * WIDE)
    summed = lax.fori_loop(0, steps, add_up, jnp.zeros((8, LANES), F32))
    mean = jnp.sum(summed, axis=0, keepdims=True) / n_own

    def centre(j, acc):
        rows = pair_rows(j)
        v = z[rows, :] - mean
        z[rows, :] = v
        low = v.astype(BF16)
        zc_out[rows, :] = low
        if not last:
            for i in range(GROUPS):
                copies[i, rows, :] = low
        return acc + fold(jnp.square(v))

    apart = lax.fori_loop(0, steps, centre, jnp.zeros((8, LANES), F32))
    sums = [mean, jnp.sum(apart, axis=0, keepdims=True), jnp.zeros((6, LANES), F32)]
    sums = jnp.concatenate(sums, axis=0)
    for i in range(st_out.shape[0]):
        st_out[i] = sums
    edge_ref[...] = zc_out[pl.ds(edge_start(n_own, edge_out, r), edge_out), :]
    save.wait()


def fwd_step(layer, pool, edge_out, total, pos, slots, rims, st, tables, weights, kept, n_own, devices):
    first = st is None
    layers = weights.shape[0]
    last = layer + 1 == layers
    inputs = slots if first else (slots, *rims, st, *tables)
    copies = () if last else (pltpu.VMEM((GROUPS, n_own, LANES), BF16),)
    return pl.pallas_call(
        functools.partial(fwd_kernel, first, last, pool, layer, total, edge_out),
        out_shape=(
            pltpu.HBM((layers, n_own + 2 * WIDE, CHANS), BF16),
            pltpu.VMEM((n_own, LANES), BF16),
            *copies,
            pltpu.VMEM((edge_out, LANES), BF16),
            pltpu.VMEM((devices, 8, LANES), F32),
        ),
        in_specs=[SMEM] + [VMEM] * len(inputs) + [ANY] * (1 if first else 2),
        out_specs=(ANY,) + (VMEM,) * (3 + len(copies)),
        input_output_aliases={} if first else {2 + len(inputs): 0},
        scratch_shapes=[
            pltpu.VMEM((n_own + 2 * WIDE, CHANS), BF16),
            pltpu.VMEM((LANES, 9 * CHANS), BF16),
            pltpu.VMEM((n_own, 3 * LANES), F32),
            pltpu.VMEM((n_own, LANES), F32),
            pltpu.VMEM((GROUPS, 8, LANES), F32),
            pltpu.VMEM((2 * WIDE, LANES), F32),
            pltpu.SemaphoreType.DMA((2,)),
        ],
        compiler_params=PARAMS,
        cost_estimate=pl.CostEstimate(
            flops=2 * n_own * 9 * CHANS * LANES, bytes_accessed=4 * 1024 * 1024, transcendentals=n_own * CHANS
        ),
        name="conv_forward",
    )(pos, *inputs, in_hbm(weights), *(() if first else (in_hbm(kept),)))


def below_kernel(layer, pool, total, top, *refs):
    pos, zc, st, gs = refs[:4]
    if top:
        terms, h_out, dn_out, edge_out, sums_out, tab = refs[4:]
    else:
        terms, (dn_out, edge_out, sums_out, tab) = refs[4:8], refs[-4:]
    n_own = dn_out.shape[0]
    rstd, own, oth = norm_tables(st, pos[0], pos[2], pos[3], float(n_own), total)
    tab[0:1], tab[1:2] = rstd, own
    tab[2:3], tab[3:4] = gs[layer : layer + 1, :], gs[layer + 8 : layer + 9, :]

    def body(j, accs):
        rows = pair_rows(j)
        xhat = zc[rows, :].astype(F32) * tab[0:1, :] + tab[1:2, :]
        n = xhat * tab[2:3, :] + tab[3:4, :]
        sig = sigmoid(n)
        h = n * sig
        if top:
            g = terms[rows, :].astype(F32)
            h_out[rows, :] = h.astype(BF16)
        else:
            g = functools.reduce(jnp.add, [term[rows, :].astype(F32) for term in terms])
        if pool:
            g = soft_pull(h, g)
        dn = g * (sig * (1.0 + n - h))
        dn_out[rows, :] = dn
        return accs[0] + fold(dn), accs[1] + fold(dn * xhat)

    zero = jnp.zeros((8, LANES), F32)
    sums = lax.fori_loop(0, n_own // (2 * WIDE), body, (zero, zero))
    sums = [jnp.sum(v, axis=0, keepdims=True) for v in sums]
    sums = jnp.concatenate(sums + [jnp.zeros((6, LANES), F32)], axis=0)
    for i in range(sums_out.shape[0]):
        sums_out[i] = sums
    edge_out[...] = dn_out[pl.ds(edge_start(n_own, WIDE, pos[1]), WIDE), :]


def below_step(layer, pool, total, pos, zc, st, gs, terms, parts, ties=()):
    n_own = terms[0].shape[0]
    top = len(terms) == 1
    out_shape = [
        pltpu.VMEM((n_own, LANES), F32),
        pltpu.VMEM((WIDE, LANES), F32),
        pltpu.VMEM((parts, 8, LANES), F32),
    ]
    if top:
        out_shape = [jax.ShapeDtypeStruct((n_own, LANES), BF16)] + out_shape
    return pl.pallas_call(
        functools.partial(below_kernel, layer, pool, total, top),
        out_shape=tuple(out_shape),
        in_specs=[SMEM] + [VMEM] * (3 + len(terms)) + [FREE] * len(ties),
        out_specs=(VMEM,) * len(out_shape),
        scratch_shapes=[pltpu.VMEM((8, LANES), F32)],
        compiler_params=PARAMS,
        cost_estimate=pl.CostEstimate(flops=40 * n_own * LANES, bytes_accessed=1024 * 1024, transcendentals=n_own * LANES),
        name="silu_backward",
    )(pos, zc, st, gs, *terms, *ties)


def bwd_kernel(layer, total, *refs):
    pos, dn, dedge, sums, zc, zrim, st, gs, w_hbm = refs[:9]
    outs, d_out, d, w, y, tab, sem = refs[-10:-6], *refs[-6:]
    load = pltpu.make_async_copy(w_hbm.at[layer], w, sem)
    load.start()
    t, r = pos[0], pos[1]
    n_own = dn.shape[0]
    halo_at = pl.multiple_of((1 - r) * (n_own + WIDE), WIDE)
    zero_at = pl.multiple_of(r * (n_own + WIDE), WIDE)
    edge = zrim.shape[0]
    d[pl.ds(zero_at, WIDE), :] = jnp.zeros((WIDE, 3 * LANES), BF16)
    rstd, own, oth = norm_tables(st, t, pos[2], pos[3], float(n_own), total)
    scale = gs[layer : layer + 1, :] * rstd
    added = functools.reduce(jnp.add, [sums[i] for i in range(sums.shape[0])])
    shift_sum, gain_sum = added[0:1], added[1:2]
    slope = scale * gain_sum / total
    tab[0:1] = scale
    tab[1:2] = slope * rstd
    tab[2:3] = scale * shift_sum / total + slope * own
    tab[3:4] = scale * shift_sum / total + slope * oth

    def spread_columns(v, at):
        rows = v.shape[0]
        column = lax.broadcasted_iota(jnp.int32, v.shape, 0) % WIDE
        ahead = jnp.where(column == WIDE - 1, 0.0, pltpu.roll(v, rows - 1, 0))
        behind = jnp.where(column == 0, 0.0, pltpu.roll(v, 1, 0))
        d[pl.ds(at, rows), 0:128] = ahead.astype(BF16)
        d[pl.ds(at, rows), 128:256] = v.astype(BF16)
        d[pl.ds(at, rows), 256:384] = behind.astype(BF16)

    def body(j, carry):
        rows = pair_rows(j)
        v = dn[rows, :] * tab[0:1, :] - tab[2:3, :] - zc[rows, :].astype(F32) * tab[1:2, :]
        spread_columns(v, pl.multiple_of(j * 2 * WIDE + WIDE, WIDE))
        return carry

    lax.fori_loop(0, n_own // (2 * WIDE), body, 0)
    near = 0 if edge == WIDE else pl.multiple_of(r * WIDE, WIDE)
    near = zrim[pl.ds(near, WIDE), :].astype(F32)
    spread_columns(dedge[...] * tab[0:1, :] - tab[3:4, :] - near * tab[1:2, :], halo_at)
    d_out[...] = d[WIDE : WIDE + n_own, :]
    load.wait()
    lhs = jnp.concatenate([d[(2 - i) * WIDE : (2 - i) * WIDE + n_own, :] for i in range(3)], axis=1)
    rhs = jnp.concatenate([w[:, i * CHANS : (i + 1) * CHANS] for i in range(9)], axis=0)
    y[...] = jnp.dot(lhs, rhs, preferred_element_type=F32)

    def share(j, carry):
        rows = pair_rows(j)
        for k in range(GROUPS):
            outs[k][rows, :] = y[rows, pl.ds(lane_of(t ^ k), LANES)].astype(BF16)
        return carry

    lax.fori_loop(0, n_own // (2 * WIDE), share, 0)


def bwd_step(layer, total, pos, dn, dedge, sums, zc, zrim, st, gs, weights, ties):
    n_own = dn.shape[0]
    part = pltpu.VMEM((n_own, LANES), BF16)
    return pl.pallas_call(
        functools.partial(bwd_kernel, layer, total),
        out_shape=(
            part,
            part,
            part,
            part,
            pltpu.VMEM((n_own, 3 * LANES), BF16),
        ),
        in_specs=[SMEM] + [VMEM] * 7 + [ANY] + [FREE] * len(ties),
        out_specs=(VMEM,) * 5,
        scratch_shapes=[
            pltpu.VMEM((n_own + 2 * WIDE, 3 * LANES), BF16),
            pltpu.VMEM((LANES, 9 * CHANS), BF16),
            pltpu.VMEM((n_own, CHANS), F32),
            pltpu.VMEM((8, LANES), F32),
            pltpu.SemaphoreType.DMA,
        ],
        compiler_params=PARAMS,
        cost_estimate=pl.CostEstimate(
            flops=2 * n_own * 9 * CHANS * LANES, bytes_accessed=4 * 1024 * 1024, transcendentals=0
        ),
        name="conv_backward",
    )(pos, dn, dedge, sums, zc, zrim, st, gs, in_hbm(weights), *ties)


def last_kernel(t0, t1, t2, t3, *refs):
    out = refs[-1]

    def body(j, carry):
        rows = pair_rows(j)
        out[rows, :] = functools.reduce(jnp.add, [term[rows, :].astype(F32) for term in (t0, t1, t2, t3)])
        return carry

    lax.fori_loop(0, out.shape[0] // (2 * WIDE), body, 0)


def last_step(terms, ties):
    return pl.pallas_call(
        last_kernel,
        out_shape=jax.ShapeDtypeStruct(terms[0].shape, F32),
        in_specs=[VMEM] * 4 + [FREE] * len(ties),
        out_specs=VMEM,
        compiler_params=PARAMS,
        name="add_terms",
    )(*terms, *ties)


def quarters_kernel(parts, *refs):
    out = refs[-1]
    total = functools.reduce(jnp.add, [parts[i].astype(F32) for i in range(4)]).astype(BF16)
    for i in range(4):
        out[i] = total


def add_quarters(parts, ties):
    return pl.pallas_call(
        quarters_kernel,
        out_shape=pltpu.VMEM(parts.shape, BF16),
        in_specs=[VMEM] + [FREE] * len(ties),
        out_specs=VMEM,
        compiler_params=PARAMS,
        cost_estimate=pl.CostEstimate(flops=parts.size, bytes_accessed=4 * parts.size, transcendentals=0),
        name="add_quarters",
    )(parts, *ties)


def halves_kernel(keep, got, out):
    out[...] = (keep[...].astype(F32) + got[...].astype(F32)).astype(BF16)


def add_halves(keep, got):
    return pl.pallas_call(
        halves_kernel,
        out_shape=jax.ShapeDtypeStruct(keep.shape, BF16),
        in_specs=[VMEM] * 2,
        out_specs=VMEM,
        compiler_params=PARAMS,
        cost_estimate=pl.CostEstimate(flops=keep.size, bytes_accessed=6 * keep.size, transcendentals=0),
        name="add_halves",
    )(keep, got)


def wgrad_kernel(layer, pos, d, hb_hbm, *refs):
    keep, send, hb, grad, sem = refs[-5:]
    load = pltpu.make_async_copy(hb_hbm.at[layer], hb, sem)
    load.start()
    n_own = d.shape[0]
    lhs = d[...]
    load.wait()
    for i in range(3):
        part = lax.dot_general(
            lhs, hb[i * WIDE : i * WIDE + n_own, :], (((0,), (0,)), ((), ())), preferred_element_type=F32
        ).astype(BF16)
        for s in range(3):
            grad[:, (3 * i + s) * CHANS : (3 * i + s + 1) * CHANS] = part[s * LANES : (s + 1) * LANES]
    half = LANES // 2
    keep[...] = grad[pl.ds(pl.multiple_of(pos[1] * half, half), half), :]
    send[...] = grad[pl.ds(pl.multiple_of((1 - pos[1]) * half, half), half), :]


def wgrad_step(layer, pos, d, kept, ties):
    half = pltpu.VMEM((LANES // 2, 9 * CHANS), BF16)
    return pl.pallas_call(
        functools.partial(wgrad_kernel, layer),
        out_shape=(half, half),
        in_specs=[SMEM, VMEM, ANY] + [FREE] * len(ties),
        out_specs=(VMEM, VMEM),
        scratch_shapes=[
            pltpu.VMEM(kept.shape[1:], BF16),
            pltpu.VMEM((LANES, 9 * CHANS), BF16),
            pltpu.SemaphoreType.DMA,
        ],
        compiler_params=PARAMS,
        cost_estimate=pl.CostEstimate(
            flops=2 * d.shape[0] * 9 * CHANS * LANES, bytes_accessed=3 * 1024 * 1024, transcendentals=0
        ),
        name="kernel_gradient",
    )(pos, d, in_hbm(kept), *ties)


def place_kernel(pos, mine, other, *refs):
    refs[-1][0] = jnp.where(pl.program_id(0) == pos[1], mine[...], other[...]).astype(F32)


def place_step(layer, pos, mine, other, whole, layers):
    half = LANES // 2
    block = pl.BlockSpec((half, 9 * CHANS), lambda i: (0, 0))
    return pl.pallas_call(
        place_kernel,
        grid=(2,),
        out_shape=jax.ShapeDtypeStruct((layers, LANES, 9 * CHANS), F32),
        in_specs=[SMEM, block, block] + ([] if whole is None else [ANY]),
        out_specs=pl.BlockSpec((1, half, 9 * CHANS), lambda i: (layer, i, 0)),
        input_output_aliases={} if whole is None else {3: 0},
        compiler_params=PARAMS,
        cost_estimate=pl.CostEstimate(flops=0, bytes_accessed=4 * 1024 * 1024, transcendentals=0),
        name="place_gradient",
    )(pos, mine, other, *(() if whole is None else (whole,)))


def swap_with(value, axis, k):
    return lax.ppermute(value, axis, [(i, i ^ k) for i in range(lax.axis_size(axis))])


def spread(own):
    return (own, *[swap_with(own, "tensor", k) for k in range(1, GROUPS)])


def halo_of_input(x, half):
    n_own = x.shape[0]
    edge = jnp.where(half == 0, x[n_own - WIDE :], x[:WIDE])
    return jnp.concatenate([x, swap_with(edge, "rows", 1)], axis=0)


def fast_local(section_input, conv_weights, norm_gains, norm_shifts, out_grad, out_mask):
    images, rows_here, width = out_mask.shape
    layers = conv_weights.shape[0]
    n_own = rows_here * width
    parts = lax.axis_size("dp") * lax.axis_size("rows")
    total = float(n_own * parts)
    t, half = lax.axis_index("tensor"), lax.axis_index("rows")
    image = lax.axis_index("dp")
    pos = jnp.stack([t, half, 2 * image + half, 2 * image + 1 - half]).astype(jnp.int32)
    middle = layers // 2
    x = to_maps(section_input, width).reshape(n_own, LANES)
    slots = spread(halo_of_input(x, half))
    pad = jnp.zeros((8 - layers, LANES), F32)
    tables = spread(jnp.concatenate([norm_gains, pad, norm_shifts, pad], axis=0))
    top_grad = (to_maps(out_grad, width) * out_mask[..., None].astype(BF16)).reshape(n_own, LANES)

    rims, st, kept = None, None, None
    halves = ("dp", "rows")
    kept_z, kept_rim, kept_st = [], [], []
    for layer in range(layers):
        last = layer + 1 == layers
        edge = 2 * WIDE if layer + 1 == middle else WIDE
        everyone = halves if last else (*halves, "tensor")
        devices = parts if last else parts * GROUPS
        kept, zc, *copies, rim, local = fwd_step(
            layer, layer == middle, edge, total, pos, slots, rims, st, tables, conv_weights, kept, n_own, devices
        )
        rim = swap_with(rim, "rows", 1)
        if not last:
            slots = lax.all_to_all(copies[0], "tensor", split_axis=0, concat_axis=0, tiled=True)
            rims = spread(rim)
        st = lax.all_to_all(local, everyone, split_axis=0, concat_axis=0, tiled=True)
        st = st.reshape(parts, devices // parts, 8, LANES)
        kept_z.append(zc)
        kept_rim.append(rim)
        kept_st.append(st)
    top = layers - 1
    h_last, dn, rim, sums = below_step(
        top, False, total, pos, kept_z[top], kept_st[top], tables[0], (top_grad,), parts
    )

    def reduce_images(pair, ties):
        rows = pair.shape[0] // 4
        pieces = lax.all_to_all(pair.reshape(4, rows, -1), "dp", split_axis=0, concat_axis=0, tiled=True)
        pieces = lax.all_to_all(add_quarters(pieces, ties), "dp", split_axis=0, concat_axis=0, tiled=True)
        return pieces.reshape(pair.shape)

    def place(layer, mine, whole):
        return place_step(layer, pos, mine, swap_with(mine, "rows", 1), whole, layers)

    sum_list, pairs = [None] * layers, [None] * layers
    ahead, back = [[0, 1, 2, 3]], [[3, 2, 1, 0]]
    ties, whole = (), None
    for layer in range(layers - 1, -1, -1):
        rim = swap_with(rim, "rows", 1)
        sums = lax.all_to_all(sums, halves, split_axis=0, concat_axis=0, tiled=True)
        sum_list[layer] = sums
        *terms, d = bwd_step(
            layer,
            total,
            pos,
            dn,
            rim,
            sums,
            kept_z[layer],
            kept_rim[layer],
            kept_st[layer],
            tables[0],
            conv_weights,
            (),
        )
        terms = (terms[0], *[swap_with(terms[k], "tensor", k) for k in range(1, GROUPS)])
        if layer > 0:
            below = layer - 1
            dn, rim, sums = below_step(
                below, layer == middle, total, pos, kept_z[below], kept_st[below], tables[0], terms, parts, ties
            )
            keep, send = wgrad_step(layer, pos, d, kept, (dn,))
        else:
            grad = last_step(terms, ())
            keep, send = wgrad_step(layer, pos, d, kept, ())
        pairs[layer] = add_halves(keep, swap_with(send, "rows", 1))
        ties = (pairs[layer],)
        if layer == 4:
            upper = lax.psum((pairs[5], pairs[4]), "dp", axis_index_groups=ahead)
        if layer == 2:
            mid = lax.psum((pairs[3], pairs[2]), "dp", axis_index_groups=back)
            whole = place(4, upper[1], place(5, upper[0], None))
            ties = (pairs[2], in_hbm(whole))
    whole = place(1, reduce_images(pairs[1], ()), whole)
    last_pair = reduce_images(pairs[0], (in_hbm(whole),))
    whole = place(2, mid[1], place(3, mid[0], whole))
    whole = place(0, last_pair, whole)
    sums = jnp.sum(jnp.stack(sum_list), axis=1)
    shape = (images, rows_here, width, LANES)
    return (
        from_maps(h_last.reshape(shape)),
        from_maps(grad.reshape(shape)),
        whole,
        sums[:, 1],
        sums[:, 0],
    )


def solution(mesh):
    in_specs = (
        P("dp", "rows", "tensor"),
        P(None, "tensor", None),
        P(None, "tensor"),
        P(None, "tensor"),
        P("dp", "rows", "tensor"),
        P("dp", "rows", None),
    )
    out_specs = (
        P("dp", "rows", "tensor"),
        P("dp", "rows", "tensor"),
        P(None, "tensor", None),
        P(None, "tensor"),
        P(None, "tensor"),
    )
    local = fast_local if fits_kernels(mesh) else generic_local
    return jax.shard_map(local, mesh=mesh, in_specs=in_specs, out_specs=out_specs, check_vma=False)
```

```python
import functools

import jax
import jax.numpy as jnp
from jax import lax
from jax.experimental import pallas as pl
from jax.experimental.pallas import tpu as pltpu
from jax.sharding import PartitionSpec as P

EPS = 1e-05


def padded_2(cells, sides, width):
    for axis, dim in sides:
        count = lax.axis_size(axis)
        ends = count - 1
        head = lax.slice_in_dim(cells, 0, width, axis=dim)
        tail = lax.slice_in_dim(cells, cells.shape[dim] - width, cells.shape[dim], axis=dim)
        cells = jnp.concatenate(
            [
                lax.ppermute(tail, axis, [(i, (i + 1) % count) for i in range(ends)]),
                cells,
                lax.ppermute(head, axis, [((i + 1) % count, i) for i in range(ends)]),
            ],
            axis=dim,
        )
    return cells


def to_maps(flat, width):
    count, high, merged = flat.shape
    return flat.reshape(count, high, merged // width, width).transpose(0, 1, 3, 2)


def from_maps(maps):
    count, high, wide, chans = maps.shape
    return maps.transpose(0, 1, 3, 2).reshape(count, high, chans * wide)


def spatial_conv(padded, kernel):
    return lax.conv_general_dilated(
        padded,
        kernel,
        (1, 1),
        ((0, 0), (1, 1)),
        dimension_numbers=("NHWC", "HWIO", "NHWC"),
        preferred_element_type=jnp.float32,
    )


def flipped(kernel):
    return jnp.transpose(kernel[::-1, ::-1], (0, 1, 3, 2))


def pool_unpool(values):
    count, high, wide, chans = values.shape
    blocks = values.reshape(count, high // 2, 2, wide // 2, 2, chans)
    pooled = jax.nn.logsumexp(blocks, axis=(2, 4), keepdims=True)
    return (jnp.exp(blocks - pooled) * pooled).reshape(values.shape)


def moments(conv_out, total_pixels):
    summed = lax.psum(jnp.sum(conv_out, axis=(0, 1, 2)), ("dp", "rows"))
    mean = summed / total_pixels
    spread = lax.psum(jnp.sum(jnp.square(conv_out - mean), axis=(0, 1, 2)), ("dp", "rows"))
    var = spread / total_pixels
    return (mean, lax.rsqrt(var + EPS))


def kernel_grad(whole, dconv):
    images, rows_here, width, chans = dconv.shape
    widened = jnp.pad(whole, ((0, 0), (0, 0), (1, 1), (0, 0)))
    stacked = []
    for row_off in range(3):
        line = []
        for col_off in range(3):
            window = widened[:, row_off : row_off + rows_here, col_off : col_off + width, :]
            line.append(
                jnp.einsum("bhwc,bhwo->co", window, dconv, preferred_element_type=jnp.float32)
            )
        stacked.append(jnp.stack(line))
    return jnp.stack(stacked)


def generic_local(section_input, conv_weights, norm_gains, norm_shifts, out_grad, out_mask):
    width = out_mask.shape[2]
    images, rows_here = (out_mask.shape[0], out_mask.shape[1])
    total_pixels = float(images * rows_here * width * lax.axis_size("dp") * lax.axis_size("rows"))
    layers, out_here, flat_in = conv_weights.shape
    chans_in = flat_in // 9
    kernels_hwio = conv_weights.reshape(layers, out_here, 3, 3, chans_in).transpose(0, 2, 3, 4, 1)
    middle = layers // 2
    kept = []
    acting = to_maps(section_input, width)
    current = acting.astype(jnp.float32)
    pre_pool = current
    for index in range(layers):
        if index == middle:
            pre_pool = current
            acting = pool_unpool(pre_pool).astype(jnp.bfloat16)
        padded = padded_2(acting, (("rows", 1),), 1)
        whole = lax.all_gather(padded, "tensor", axis=3, tiled=True)
        conv_out = spatial_conv(whole, kernels_hwio[index])
        mean, rstd = moments(conv_out, total_pixels)
        normed = (conv_out - mean) * rstd
        shifted = normed * norm_gains[index] + norm_shifts[index]
        current = jax.nn.silu(shifted)
        acting = current.astype(jnp.bfloat16)
        kept.append((whole, normed, shifted, rstd))
    grad = to_maps(out_grad, width).astype(jnp.float32) * out_mask[..., None].astype(jnp.float32)
    kernel_list = [None] * layers
    gain_list = [None] * layers
    shift_list = [None] * layers
    for index in range(layers - 1, -1, -1):
        whole, normed, shifted, rstd = kept[index]
        unused, pull_silu = jax.vjp(jax.nn.silu, shifted)
        dshift = pull_silu(grad)[0]
        gain_sum, shift_sum = lax.psum(
            (jnp.sum(dshift * normed, axis=(0, 1, 2)), jnp.sum(dshift, axis=(0, 1, 2))),
            ("dp", "rows"),
        )
        gain_list[index] = gain_sum
        shift_list[index] = shift_sum
        dconv = (
            norm_gains[index]
            * rstd
            * (dshift - shift_sum / total_pixels - normed * gain_sum / total_pixels)
        ).astype(jnp.bfloat16)
        summed_kernel = lax.psum(
            kernel_grad(whole, dconv).astype(jnp.bfloat16), ("dp", "rows")
        ).astype(jnp.float32)
        kernel_list[index] = summed_kernel.transpose(3, 0, 1, 2).reshape(out_here, flat_in)
        grad_rim = padded_2(dconv, (("rows", 1),), 1)
        partial_terms = spatial_conv(grad_rim, flipped(kernels_hwio[index]))
        grad_in = lax.psum_scatter(
            partial_terms.astype(jnp.bfloat16), "tensor", scatter_dimension=3, tiled=True
        ).astype(jnp.float32)
        if index == middle:
            unused, pull_pool = jax.vjp(pool_unpool, pre_pool)
            grad = pull_pool(grad_in)[0]
        else:
            grad = grad_in
    return (
        from_maps(acting),
        from_maps(grad),
        jnp.stack(kernel_list),
        jnp.stack(gain_list),
        jnp.stack(shift_list),
    )


GROUPS = 4
LANES = 128
WIDE = 48
CHANS = GROUPS * LANES
F32 = jnp.float32
BF16 = jnp.bfloat16
VMEM = pl.BlockSpec(memory_space=pltpu.VMEM)
SMEM = pl.BlockSpec(memory_space=pltpu.SMEM)
ANY = pl.BlockSpec(memory_space=pltpu.HBM)
FREE = pl.BlockSpec(memory_space=pl.ANY)
PARAMS = pltpu.CompilerParams(vmem_limit_bytes=20 * 1024 * 1024)


def in_hbm(value):
    return pltpu.with_memory_space_constraint(value, pltpu.HBM)


def fits_kernels(mesh):
    return mesh.shape["tensor"] == GROUPS and mesh.shape["rows"] == 2 and mesh.shape["dp"] == 4


def sigmoid(v):
    return 0.5 * jnp.tanh(0.5 * v) + 0.5


def swap_columns(v):
    column = lax.broadcasted_iota(jnp.int32, v.shape, 0)
    return jnp.where(column % 2 == 0, pltpu.roll(v, WIDE - 1, 0), pltpu.roll(v, 1, 0))


def soft_parts(h):
    top = jnp.maximum(h[0], h[1])
    top = jnp.maximum(top, swap_columns(top))
    e0, e1 = jnp.exp(h[0] - top), jnp.exp(h[1] - top)
    total = e0 + e1
    total = total + swap_columns(total)
    pooled = top + jnp.log(total)
    inverse = 1.0 / total
    return e0 * inverse, e1 * inverse, pooled


def soft(h):
    h = h.reshape(2, WIDE, LANES)
    q0, q1, pooled = soft_parts(h)
    return jnp.concatenate([q0 * pooled, q1 * pooled], axis=0)


def soft_pull(h, grad):
    h = h.reshape(2, WIDE, LANES)
    grad = grad.reshape(2, WIDE, LANES)
    q0, q1, pooled = soft_parts(h)
    mix = q0 * grad[0] + q1 * grad[1]
    mix = mix + swap_columns(mix)
    return jnp.concatenate(
        [q0 * (pooled * (grad[0] - mix) + mix), q1 * (pooled * (grad[1] - mix) + mix)], axis=0
    )


def norm_tables(st, group, i_own, i_oth, n_local, total):
    parts = st.shape[0]
    group = 0 if st.shape[1] == 1 else group
    blocks = [st[i, group] for i in range(parts)]
    summed = functools.reduce(jnp.add, blocks)
    mean = summed[0:1] / parts
    apart = functools.reduce(jnp.add, [jnp.square(b - mean) for b in blocks])
    rstd = lax.rsqrt((summed[1:2] + n_local * apart[0:1]) / total + EPS)
    return rstd, (st[i_own, group, 0:1] - mean) * rstd, (st[i_oth, group, 0:1] - mean) * rstd


def left_right(y0, y1, y2):
    rows = y0.shape[0]
    column = lax.broadcasted_iota(jnp.int32, y0.shape, 0) % WIDE
    before = jnp.where(column == 0, 0.0, pltpu.roll(y0, 1, 0))
    after = jnp.where(column == WIDE - 1, 0.0, pltpu.roll(y2, rows - 1, 0))
    return before + y1 + after


def lane_of(group):
    return pl.multiple_of(group * LANES, LANES)


def edge_start(n_own, edge, half):
    return pl.multiple_of((1 - half) * (n_own - edge), WIDE)


def pair_rows(j):
    return pl.ds(pl.multiple_of(j * 2 * WIDE, 2 * WIDE), 2 * WIDE)


def fold(v):
    return jnp.sum(v.reshape(v.shape[0] // 8, 8, LANES), axis=0)


def fwd_kernel(first, pool, layer, total, edge_out, *refs):
    pos, zs = refs[0], refs[1:5]
    if first:
        w_hbm, rest = refs[5], refs[6:]
    else:
        st, gss, w_hbm, rest = refs[5], refs[6:10], refs[10], refs[12:]
    hb_out, zc_out, edge_ref, st_out, hb, w, y, z, tab, hs, sem = rest
    load = pltpu.make_async_copy(w_hbm.at[layer], w, sem.at[0])
    load.start()
    save = pltpu.make_async_copy(hb, hb_out.at[layer], sem.at[1])
    t, r = pos[0], pos[1]
    n_own = z.shape[0]
    halo_at = pl.multiple_of((1 - r) * (n_own + WIDE), WIDE)
    zero_at = pl.multiple_of(r * (n_own + WIDE), WIDE)
    hb[pl.ds(zero_at, WIDE), :] = jnp.zeros((WIDE, CHANS), BF16)
    edge = zs[0].shape[0] - n_own
    if not first:
        for k in range(GROUPS):
            rstd, own, oth = norm_tables(st, t ^ k, pos[2], pos[3], float(n_own), total)
            gain, shift = gss[k][layer - 1 : layer, :], gss[k][layer + 7 : layer + 8, :]
            tab[k, 0:1] = rstd * gain
            tab[k, 1:2] = own * gain + shift
            tab[k, 2:3] = oth * gain + shift

    def act(values, k, which):
        if first:
            return values
        n = values.astype(F32) * tab[k, 0:1, :] + tab[k, which : which + 1, :]
        h = n * sigmoid(n)
        return soft(h) if pool else h

    def body(j, carry):
        at = pl.multiple_of(j * 2 * WIDE, 2 * WIDE)
        for k in range(GROUPS):
            h = act(zs[k][pl.ds(at, 2 * WIDE), :], k, 1)
            hb[pl.ds(pl.multiple_of(at + WIDE, WIDE), 2 * WIDE), pl.ds(lane_of(t ^ k), LANES)] = h.astype(BF16)
        return carry

    lax.fori_loop(0, n_own // (2 * WIDE), body, 0)
    for k in range(GROUPS):
        h = act(zs[k][n_own : n_own + edge, :], k, 2)
        if edge > WIDE:
            hs[...] = h
            h = hs[pl.ds(pl.multiple_of(r * WIDE, WIDE), WIDE), :]
        hb[pl.ds(halo_at, WIDE), pl.ds(lane_of(t ^ k), LANES)] = h.astype(BF16)
    save.start()
    load.wait()
    lhs = jnp.concatenate([hb[i * WIDE : i * WIDE + n_own, :] for i in range(3)], axis=1)
    rhs = jnp.concatenate(
        [
            jnp.concatenate([w[:, (3 * i + s) * CHANS : (3 * i + s + 1) * CHANS] for i in range(3)], axis=1)
            for s in range(3)
        ],
        axis=0,
    )
    y[...] = lax.dot_general(lhs, rhs, (((1,), (1,)), ((), ())), preferred_element_type=F32)

    def add_up(j, acc):
        rows = pair_rows(j)
        v = left_right(y[rows, 0:128], y[rows, 128:256], y[rows, 256:384])
        z[rows, :] = v
        return acc + fold(v)

    steps = n_own // (2 * WIDE)
    summed = lax.fori_loop(0, steps, add_up, jnp.zeros((8, LANES), F32))
    mean = jnp.sum(summed, axis=0, keepdims=True) / n_own

    def centre(j, acc):
        rows = pair_rows(j)
        v = z[rows, :] - mean
        z[rows, :] = v
        zc_out[rows, :] = v.astype(BF16)
        return acc + fold(jnp.square(v))

    apart = lax.fori_loop(0, steps, centre, jnp.zeros((8, LANES), F32))
    sums = [mean, jnp.sum(apart, axis=0, keepdims=True), jnp.zeros((6, LANES), F32)]
    sums = jnp.concatenate(sums, axis=0)
    for i in range(st_out.shape[0]):
        st_out[i] = sums
    edge_ref[...] = zc_out[pl.ds(edge_start(n_own, edge_out, r), edge_out), :]
    zc_out[n_own : n_own + edge_out, :] = jnp.zeros((edge_out, LANES), BF16)
    save.wait()


def fwd_step(layer, pool, edge_out, total, pos, slots, st, tables, weights, kept, n_own, devices):
    first = st is None
    layers = weights.shape[0]
    extra = () if first else (st, *tables)
    return pl.pallas_call(
        functools.partial(fwd_kernel, first, pool, layer, total, edge_out),
        out_shape=(
            pltpu.HBM((layers, n_own + 2 * WIDE, CHANS), BF16),
            pltpu.VMEM((n_own + edge_out, LANES), BF16),
            pltpu.VMEM((edge_out, LANES), BF16),
            pltpu.VMEM((devices, 8, LANES), F32),
        ),
        in_specs=[SMEM] + [VMEM] * (4 + len(extra)) + [ANY] * (1 if first else 2),
        out_specs=(ANY, VMEM, VMEM, VMEM),
        input_output_aliases={} if first else {6 + len(extra): 0},
        scratch_shapes=[
            pltpu.VMEM((n_own + 2 * WIDE, CHANS), BF16),
            pltpu.VMEM((LANES, 9 * CHANS), BF16),
            pltpu.VMEM((n_own, 3 * LANES), F32),
            pltpu.VMEM((n_own, LANES), F32),
            pltpu.VMEM((GROUPS, 8, LANES), F32),
            pltpu.VMEM((2 * WIDE, LANES), F32),
            pltpu.SemaphoreType.DMA((2,)),
        ],
        compiler_params=PARAMS,
        cost_estimate=pl.CostEstimate(
            flops=2 * n_own * 9 * CHANS * LANES, bytes_accessed=4 * 1024 * 1024, transcendentals=n_own * CHANS
        ),
        name="conv_forward",
    )(pos, *slots, *extra, in_hbm(weights), *(() if first else (in_hbm(kept),)))


def below_kernel(layer, pool, total, top, *refs):
    pos, zc, st, gs = refs[:4]
    if top:
        terms, h_out, dn_out, msg, tab = refs[4:]
    else:
        terms, (dn_out, msg, tab) = refs[4:8], refs[-3:]
    n_own = dn_out.shape[0]
    rstd, own, oth = norm_tables(st, pos[0], pos[2], pos[3], float(n_own), total)
    tab[0:1], tab[1:2] = rstd, own
    tab[2:3], tab[3:4] = gs[layer : layer + 1, :], gs[layer + 8 : layer + 9, :]

    def body(j, accs):
        rows = pair_rows(j)
        xhat = zc[rows, :].astype(F32) * tab[0:1, :] + tab[1:2, :]
        n = xhat * tab[2:3, :] + tab[3:4, :]
        sig = sigmoid(n)
        h = n * sig
        if top:
            g = terms[rows, :].astype(F32)
            h_out[rows, :] = h.astype(BF16)
        else:
            g = functools.reduce(jnp.add, [term[rows, :].astype(F32) for term in terms])
        if pool:
            g = soft_pull(h, g)
        dn = g * (sig * (1.0 + n - h))
        dn_out[rows, :] = dn
        return accs[0] + fold(dn), accs[1] + fold(dn * xhat)

    zero = jnp.zeros((8, LANES), F32)
    sums = lax.fori_loop(0, n_own // (2 * WIDE), body, (zero, zero))
    sums = [jnp.sum(v, axis=0, keepdims=True) for v in sums]
    msg[0:WIDE, :] = dn_out[pl.ds(edge_start(n_own, WIDE, pos[1]), WIDE), :]
    msg[WIDE : WIDE + 8, :] = jnp.concatenate(sums + [jnp.zeros((6, LANES), F32)], axis=0)


def below_step(layer, pool, total, pos, zc, st, gs, terms, ties=()):
    n_own = terms[0].shape[0]
    top = len(terms) == 1
    out_shape = [
        pltpu.VMEM((n_own, LANES), F32),
        pltpu.VMEM((WIDE + 8, LANES), F32),
    ]
    if top:
        out_shape = [jax.ShapeDtypeStruct((n_own, LANES), BF16)] + out_shape
    return pl.pallas_call(
        functools.partial(below_kernel, layer, pool, total, top),
        out_shape=tuple(out_shape),
        in_specs=[SMEM] + [VMEM] * (3 + len(terms)) + [FREE] * len(ties),
        out_specs=(VMEM,) * len(out_shape),
        scratch_shapes=[pltpu.VMEM((8, LANES), F32)],
        compiler_params=PARAMS,
        cost_estimate=pl.CostEstimate(flops=40 * n_own * LANES, bytes_accessed=1024 * 1024, transcendentals=n_own * LANES),
        name="silu_backward",
    )(pos, zc, st, gs, *terms, *ties)


def bwd_kernel(layer, total, *refs):
    pos, dn, dedge, sums, zc, st, gs, w_hbm = refs[:8]
    outs, d_out, d, w, y, tab, sem = refs[-10:-6], *refs[-6:]
    load = pltpu.make_async_copy(w_hbm.at[layer], w, sem)
    load.start()
    t, r = pos[0], pos[1]
    n_own = dn.shape[0]
    halo_at = pl.multiple_of((1 - r) * (n_own + WIDE), WIDE)
    zero_at = pl.multiple_of(r * (n_own + WIDE), WIDE)
    edge = zc.shape[0] - n_own
    d[pl.ds(zero_at, WIDE), :] = jnp.zeros((WIDE, 3 * LANES), BF16)
    rstd, own, oth = norm_tables(st, t, pos[2], pos[3], float(n_own), total)
    scale = gs[layer : layer + 1, :] * rstd
    shift_sum, gain_sum = sums[0:1, :], sums[1:2, :]
    slope = scale * gain_sum / total
    tab[0:1] = scale
    tab[1:2] = slope * rstd
    tab[2:3] = scale * shift_sum / total + slope * own
    tab[3:4] = scale * shift_sum / total + slope * oth

    def spread_columns(v, at):
        rows = v.shape[0]
        column = lax.broadcasted_iota(jnp.int32, v.shape, 0) % WIDE
        ahead = jnp.where(column == WIDE - 1, 0.0, pltpu.roll(v, rows - 1, 0))
        behind = jnp.where(column == 0, 0.0, pltpu.roll(v, 1, 0))
        d[pl.ds(at, rows), 0:128] = ahead.astype(BF16)
        d[pl.ds(at, rows), 128:256] = v.astype(BF16)
        d[pl.ds(at, rows), 256:384] = behind.astype(BF16)

    def body(j, carry):
        rows = pair_rows(j)
        v = dn[rows, :] * tab[0:1, :] - tab[2:3, :] - zc[rows, :].astype(F32) * tab[1:2, :]
        spread_columns(v, pl.multiple_of(j * 2 * WIDE + WIDE, WIDE))
        return carry

    lax.fori_loop(0, n_own // (2 * WIDE), body, 0)
    near = n_own if edge == WIDE else pl.multiple_of(n_own + r * WIDE, WIDE)
    near = zc[pl.ds(near, WIDE), :].astype(F32)
    spread_columns(dedge[0:WIDE, :] * tab[0:1, :] - tab[3:4, :] - near * tab[1:2, :], halo_at)
    d_out[...] = d[WIDE : WIDE + n_own, :]
    load.wait()
    lhs = jnp.concatenate([d[(2 - i) * WIDE : (2 - i) * WIDE + n_own, :] for i in range(3)], axis=1)
    rhs = jnp.concatenate([w[:, i * CHANS : (i + 1) * CHANS] for i in range(9)], axis=0)
    y[...] = jnp.dot(lhs, rhs, preferred_element_type=F32)

    def share(j, carry):
        rows = pair_rows(j)
        for k in range(GROUPS):
            outs[k][rows, :] = y[rows, pl.ds(lane_of(t ^ k), LANES)].astype(BF16)
        return carry

    lax.fori_loop(0, n_own // (2 * WIDE), share, 0)


def bwd_step(layer, total, pos, dn, dedge, sums, zc, st, gs, weights, ties):
    n_own = dn.shape[0]
    part = pltpu.VMEM((n_own, LANES), BF16)
    return pl.pallas_call(
        functools.partial(bwd_kernel, layer, total),
        out_shape=(
            part,
            part,
            part,
            part,
            pltpu.VMEM((n_own, 3 * LANES), BF16),
        ),
        in_specs=[SMEM] + [VMEM] * 6 + [ANY] + [FREE] * len(ties),
        out_specs=(VMEM,) * 5,
        scratch_shapes=[
            pltpu.VMEM((n_own + 2 * WIDE, 3 * LANES), BF16),
            pltpu.VMEM((LANES, 9 * CHANS), BF16),
            pltpu.VMEM((n_own, CHANS), F32),
            pltpu.VMEM((8, LANES), F32),
            pltpu.SemaphoreType.DMA,
        ],
        compiler_params=PARAMS,
        cost_estimate=pl.CostEstimate(
            flops=2 * n_own * 9 * CHANS * LANES, bytes_accessed=4 * 1024 * 1024, transcendentals=0
        ),
        name="conv_backward",
    )(pos, dn, dedge, sums, zc, st, gs, in_hbm(weights), *ties)


def last_kernel(t0, t1, t2, t3, *refs):
    out = refs[-1]

    def body(j, carry):
        rows = pair_rows(j)
        out[rows, :] = functools.reduce(jnp.add, [term[rows, :].astype(F32) for term in (t0, t1, t2, t3)])
        return carry

    lax.fori_loop(0, out.shape[0] // (2 * WIDE), body, 0)


def last_step(terms, ties):
    return pl.pallas_call(
        last_kernel,
        out_shape=jax.ShapeDtypeStruct(terms[0].shape, F32),
        in_specs=[VMEM] * 4 + [FREE] * len(ties),
        out_specs=VMEM,
        compiler_params=PARAMS,
        name="add_terms",
    )(*terms, *ties)


def halves_kernel(keep, got, out):
    out[...] = (keep[...].astype(F32) + got[...].astype(F32)).astype(BF16)


def add_halves(keep, got):
    return pl.pallas_call(
        halves_kernel,
        out_shape=jax.ShapeDtypeStruct(keep.shape, BF16),
        in_specs=[VMEM] * 2,
        out_specs=VMEM,
        compiler_params=PARAMS,
        cost_estimate=pl.CostEstimate(flops=keep.size, bytes_accessed=6 * keep.size, transcendentals=0),
        name="add_halves",
    )(keep, got)


def wgrad_kernel(layer, pos, d, hb_hbm, *refs):
    keep, send, hb, grad, sem = refs[-5:]
    load = pltpu.make_async_copy(hb_hbm.at[layer], hb, sem)
    load.start()
    n_own = d.shape[0]
    lhs = d[...]
    load.wait()
    for i in range(3):
        part = lax.dot_general(
            lhs, hb[i * WIDE : i * WIDE + n_own, :], (((0,), (0,)), ((), ())), preferred_element_type=F32
        ).astype(BF16)
        for s in range(3):
            grad[:, (3 * i + s) * CHANS : (3 * i + s + 1) * CHANS] = part[s * LANES : (s + 1) * LANES]
    half = LANES // 2
    keep[...] = grad[pl.ds(pl.multiple_of(pos[1] * half, half), half), :]
    send[...] = grad[pl.ds(pl.multiple_of((1 - pos[1]) * half, half), half), :]


def wgrad_step(layer, pos, d, kept, ties):
    half = pltpu.VMEM((LANES // 2, 9 * CHANS), BF16)
    return pl.pallas_call(
        functools.partial(wgrad_kernel, layer),
        out_shape=(half, half),
        in_specs=[SMEM, VMEM, ANY] + [FREE] * len(ties),
        out_specs=(VMEM, VMEM),
        scratch_shapes=[
            pltpu.VMEM(kept.shape[1:], BF16),
            pltpu.VMEM((LANES, 9 * CHANS), BF16),
            pltpu.SemaphoreType.DMA,
        ],
        compiler_params=PARAMS,
        cost_estimate=pl.CostEstimate(
            flops=2 * d.shape[0] * 9 * CHANS * LANES, bytes_accessed=3 * 1024 * 1024, transcendentals=0
        ),
        name="kernel_gradient",
    )(pos, d, in_hbm(kept), *ties)


def place_kernel(pos, mine, other, *refs):
    refs[-1][0] = jnp.where(pl.program_id(0) == pos[1], mine[...], other[...]).astype(F32)


def place_step(layer, pos, mine, other, whole, layers):
    half = LANES // 2
    block = pl.BlockSpec((half, 9 * CHANS), lambda i: (0, 0))
    return pl.pallas_call(
        place_kernel,
        grid=(2,),
        out_shape=jax.ShapeDtypeStruct((layers, LANES, 9 * CHANS), F32),
        in_specs=[SMEM, block, block] + ([] if whole is None else [ANY]),
        out_specs=pl.BlockSpec((1, half, 9 * CHANS), lambda i: (layer, i, 0)),
        input_output_aliases={} if whole is None else {3: 0},
        compiler_params=PARAMS,
        cost_estimate=pl.CostEstimate(flops=0, bytes_accessed=4 * 1024 * 1024, transcendentals=0),
        name="place_gradient",
    )(pos, mine, other, *(() if whole is None else (whole,)))


def swap_with(value, axis, k):
    return lax.ppermute(value, axis, [(i, i ^ k) for i in range(lax.axis_size(axis))])


def spread(own):
    return (own, *[swap_with(own, "tensor", k) for k in range(1, GROUPS)])


def halo_of_input(x, half):
    n_own = x.shape[0]
    edge = jnp.where(half == 0, x[n_own - WIDE :], x[:WIDE])
    return jnp.concatenate([x, swap_with(edge, "rows", 1)], axis=0)


def fast_local(section_input, conv_weights, norm_gains, norm_shifts, out_grad, out_mask):
    images, rows_here, width = out_mask.shape
    layers = conv_weights.shape[0]
    n_own = rows_here * width
    parts = lax.axis_size("dp") * lax.axis_size("rows")
    total = float(n_own * parts)
    t, half = lax.axis_index("tensor"), lax.axis_index("rows")
    image = lax.axis_index("dp")
    pos = jnp.stack([t, half, 2 * image + half, 2 * image + 1 - half]).astype(jnp.int32)
    middle = layers // 2
    x = to_maps(section_input, width).reshape(n_own, LANES)
    slots = spread(halo_of_input(x, half))
    pad = jnp.zeros((8 - layers, LANES), F32)
    tables = spread(jnp.concatenate([norm_gains, pad, norm_shifts, pad], axis=0))
    top_grad = (to_maps(out_grad, width) * out_mask[..., None].astype(BF16)).reshape(n_own, LANES)

    st, kept = None, None
    halves = ("dp", "rows")
    kept_z, kept_st = [], []
    for layer in range(layers):
        last = layer + 1 == layers
        edge = 2 * WIDE if layer + 1 == middle else WIDE
        everyone = halves if last else (*halves, "tensor")
        devices = parts if last else parts * GROUPS
        kept, zc, rim, local = fwd_step(
            layer, layer == middle, edge, total, pos, slots, st, tables, conv_weights, kept, n_own, devices
        )
        rim = swap_with(rim, "rows", 1)
        st = lax.all_to_all(local, everyone, split_axis=0, concat_axis=0, tiled=True)
        st = st.reshape(parts, devices // parts, 8, LANES)
        zc = lax.dynamic_update_slice_in_dim(zc, rim, n_own, axis=0)
        kept_z.append(zc)
        kept_st.append(st)
        if not last:
            slots = spread(zc)
    top = layers - 1
    h_last, dn, msg = below_step(top, False, total, pos, kept_z[top], kept_st[top], tables[0], (top_grad,))

    def place(layer, mine, whole):
        return place_step(layer, pos, mine, swap_with(mine, "rows", 1), whole, layers)

    sum_list, pairs = [None] * layers, [None] * layers
    ahead, back = [[0, 1, 2, 3]], [[3, 2, 1, 0]]
    ties, whole = (), None
    for layer in range(layers - 1, -1, -1):
        got = swap_with(msg, "rows", 1)
        sums = msg[WIDE:] + got[WIDE:]
        for k in (1, 2):
            sums = sums + swap_with(sums, "dp", k)
        sum_list[layer] = sums
        *terms, d = bwd_step(
            layer, total, pos, dn, got, sums, kept_z[layer], kept_st[layer], tables[0], conv_weights, ()
        )
        terms = (terms[0], *[swap_with(terms[k], "tensor", k) for k in range(1, GROUPS)])
        if layer > 0:
            below = layer - 1
            dn, msg = below_step(
                below, layer == middle, total, pos, kept_z[below], kept_st[below], tables[0], terms, ties
            )
            keep, send = wgrad_step(layer, pos, d, kept, (dn,))
        else:
            grad = last_step(terms, ties)
            keep, send = wgrad_step(layer, pos, d, kept, ())
        pairs[layer] = add_halves(keep, swap_with(send, "rows", 1))
        ties = (pairs[layer],)
        if layer == 4:
            upper = lax.psum((pairs[5], pairs[4]), "dp", axis_index_groups=ahead)
        if layer == 2:
            mid = lax.psum((pairs[3], pairs[2]), "dp", axis_index_groups=back)
        if layer == 1:
            whole = place(4, upper[1], place(5, upper[0], None))
            ties = (pairs[1], in_hbm(whole))
    tied, upper = lax.optimization_barrier(((pairs[1], pairs[0]), upper))
    lower = lax.psum(tied, "dp", axis_index_groups=ahead)
    whole = place(2, mid[1], place(3, mid[0], whole))
    whole = place(0, lower[1], place(1, lower[0], whole))
    sums = jnp.stack(sum_list)
    shape = (images, rows_here, width, LANES)
    return (
        from_maps(h_last.reshape(shape)),
        from_maps(grad.reshape(shape)),
        whole,
        sums[:, 1],
        sums[:, 0],
    )


def solution(mesh):
    in_specs = (
        P("dp", "rows", "tensor"),
        P(None, "tensor", None),
        P(None, "tensor"),
        P(None, "tensor"),
        P("dp", "rows", "tensor"),
        P("dp", "rows", None),
    )
    out_specs = (
        P("dp", "rows", "tensor"),
        P("dp", "rows", "tensor"),
        P(None, "tensor", None),
        P(None, "tensor"),
        P(None, "tensor"),
    )
    local = fast_local if fits_kernels(mesh) else generic_local
    return jax.shard_map(local, mesh=mesh, in_specs=in_specs, out_specs=out_specs, check_vma=False)
```

```python
import functools

import jax
import jax.numpy as jnp
from jax import lax
from jax.experimental import pallas as pl
from jax.experimental.pallas import tpu as pltpu
from jax.sharding import PartitionSpec as P

EPS = 1e-05


def padded_2(cells, sides, width):
    for axis, dim in sides:
        count = lax.axis_size(axis)
        ends = count - 1
        head = lax.slice_in_dim(cells, 0, width, axis=dim)
        tail = lax.slice_in_dim(cells, cells.shape[dim] - width, cells.shape[dim], axis=dim)
        cells = jnp.concatenate(
            [
                lax.ppermute(tail, axis, [(i, (i + 1) % count) for i in range(ends)]),
                cells,
                lax.ppermute(head, axis, [((i + 1) % count, i) for i in range(ends)]),
            ],
            axis=dim,
        )
    return cells


def to_maps(flat, width):
    count, high, merged = flat.shape
    return flat.reshape(count, high, merged // width, width).transpose(0, 1, 3, 2)


def from_maps(maps):
    count, high, wide, chans = maps.shape
    return maps.transpose(0, 1, 3, 2).reshape(count, high, chans * wide)


def spatial_conv(padded, kernel):
    return lax.conv_general_dilated(
        padded,
        kernel,
        (1, 1),
        ((0, 0), (1, 1)),
        dimension_numbers=("NHWC", "HWIO", "NHWC"),
        preferred_element_type=jnp.float32,
    )


def flipped(kernel):
    return jnp.transpose(kernel[::-1, ::-1], (0, 1, 3, 2))


def pool_unpool(values):
    count, high, wide, chans = values.shape
    blocks = values.reshape(count, high // 2, 2, wide // 2, 2, chans)
    pooled = jax.nn.logsumexp(blocks, axis=(2, 4), keepdims=True)
    return (jnp.exp(blocks - pooled) * pooled).reshape(values.shape)


def moments(conv_out, total_pixels):
    summed = lax.psum(jnp.sum(conv_out, axis=(0, 1, 2)), ("dp", "rows"))
    mean = summed / total_pixels
    spread = lax.psum(jnp.sum(jnp.square(conv_out - mean), axis=(0, 1, 2)), ("dp", "rows"))
    var = spread / total_pixels
    return (mean, lax.rsqrt(var + EPS))


def kernel_grad(whole, dconv):
    images, rows_here, width, chans = dconv.shape
    widened = jnp.pad(whole, ((0, 0), (0, 0), (1, 1), (0, 0)))
    stacked = []
    for row_off in range(3):
        line = []
        for col_off in range(3):
            window = widened[:, row_off : row_off + rows_here, col_off : col_off + width, :]
            line.append(
                jnp.einsum("bhwc,bhwo->co", window, dconv, preferred_element_type=jnp.float32)
            )
        stacked.append(jnp.stack(line))
    return jnp.stack(stacked)


def generic_local(section_input, conv_weights, norm_gains, norm_shifts, out_grad, out_mask):
    width = out_mask.shape[2]
    images, rows_here = (out_mask.shape[0], out_mask.shape[1])
    total_pixels = float(images * rows_here * width * lax.axis_size("dp") * lax.axis_size("rows"))
    layers, out_here, flat_in = conv_weights.shape
    chans_in = flat_in // 9
    kernels_hwio = conv_weights.reshape(layers, out_here, 3, 3, chans_in).transpose(0, 2, 3, 4, 1)
    middle = layers // 2
    kept = []
    acting = to_maps(section_input, width)
    current = acting.astype(jnp.float32)
    pre_pool = current
    for index in range(layers):
        if index == middle:
            pre_pool = current
            acting = pool_unpool(pre_pool).astype(jnp.bfloat16)
        padded = padded_2(acting, (("rows", 1),), 1)
        whole = lax.all_gather(padded, "tensor", axis=3, tiled=True)
        conv_out = spatial_conv(whole, kernels_hwio[index])
        mean, rstd = moments(conv_out, total_pixels)
        normed = (conv_out - mean) * rstd
        shifted = normed * norm_gains[index] + norm_shifts[index]
        current = jax.nn.silu(shifted)
        acting = current.astype(jnp.bfloat16)
        kept.append((whole, normed, shifted, rstd))
    grad = to_maps(out_grad, width).astype(jnp.float32) * out_mask[..., None].astype(jnp.float32)
    kernel_list = [None] * layers
    gain_list = [None] * layers
    shift_list = [None] * layers
    for index in range(layers - 1, -1, -1):
        whole, normed, shifted, rstd = kept[index]
        unused, pull_silu = jax.vjp(jax.nn.silu, shifted)
        dshift = pull_silu(grad)[0]
        gain_sum, shift_sum = lax.psum(
            (jnp.sum(dshift * normed, axis=(0, 1, 2)), jnp.sum(dshift, axis=(0, 1, 2))),
            ("dp", "rows"),
        )
        gain_list[index] = gain_sum
        shift_list[index] = shift_sum
        dconv = (
            norm_gains[index]
            * rstd
            * (dshift - shift_sum / total_pixels - normed * gain_sum / total_pixels)
        ).astype(jnp.bfloat16)
        summed_kernel = lax.psum(
            kernel_grad(whole, dconv).astype(jnp.bfloat16), ("dp", "rows")
        ).astype(jnp.float32)
        kernel_list[index] = summed_kernel.transpose(3, 0, 1, 2).reshape(out_here, flat_in)
        grad_rim = padded_2(dconv, (("rows", 1),), 1)
        partial_terms = spatial_conv(grad_rim, flipped(kernels_hwio[index]))
        grad_in = lax.psum_scatter(
            partial_terms.astype(jnp.bfloat16), "tensor", scatter_dimension=3, tiled=True
        ).astype(jnp.float32)
        if index == middle:
            unused, pull_pool = jax.vjp(pool_unpool, pre_pool)
            grad = pull_pool(grad_in)[0]
        else:
            grad = grad_in
    return (
        from_maps(acting),
        from_maps(grad),
        jnp.stack(kernel_list),
        jnp.stack(gain_list),
        jnp.stack(shift_list),
    )


GROUPS = 4
LANES = 128
WIDE = 48
CHANS = GROUPS * LANES
F32 = jnp.float32
BF16 = jnp.bfloat16
VMEM = pl.BlockSpec(memory_space=pltpu.VMEM)
SMEM = pl.BlockSpec(memory_space=pltpu.SMEM)
ANY = pl.BlockSpec(memory_space=pltpu.HBM)
FREE = pl.BlockSpec(memory_space=pl.ANY)
PARAMS = pltpu.CompilerParams(vmem_limit_bytes=20 * 1024 * 1024)


def in_hbm(value):
    return pltpu.with_memory_space_constraint(value, pltpu.HBM)


def fits_kernels(mesh):
    return mesh.shape["tensor"] == GROUPS and mesh.shape["rows"] == 2 and mesh.shape["dp"] == 4


def sigmoid(v):
    return 0.5 * jnp.tanh(0.5 * v) + 0.5


def swap_columns(v):
    column = lax.broadcasted_iota(jnp.int32, v.shape, 0)
    return jnp.where(column % 2 == 0, pltpu.roll(v, WIDE - 1, 0), pltpu.roll(v, 1, 0))


def soft_parts(h):
    top = jnp.maximum(h[0], h[1])
    top = jnp.maximum(top, swap_columns(top))
    e0, e1 = jnp.exp(h[0] - top), jnp.exp(h[1] - top)
    total = e0 + e1
    total = total + swap_columns(total)
    pooled = top + jnp.log(total)
    inverse = 1.0 / total
    return e0 * inverse, e1 * inverse, pooled


def soft(h):
    h = h.reshape(2, WIDE, LANES)
    q0, q1, pooled = soft_parts(h)
    return jnp.concatenate([q0 * pooled, q1 * pooled], axis=0)


def soft_pull(h, grad):
    h = h.reshape(2, WIDE, LANES)
    grad = grad.reshape(2, WIDE, LANES)
    q0, q1, pooled = soft_parts(h)
    mix = q0 * grad[0] + q1 * grad[1]
    mix = mix + swap_columns(mix)
    return jnp.concatenate(
        [q0 * (pooled * (grad[0] - mix) + mix), q1 * (pooled * (grad[1] - mix) + mix)], axis=0
    )


def norm_tables(st, group, i_own, i_oth, n_local, total):
    parts = st.shape[0]
    group = 0 if st.shape[1] == 1 else group
    blocks = [st[i, group] for i in range(parts)]
    summed = functools.reduce(jnp.add, blocks)
    mean = summed[0:1] / parts
    apart = functools.reduce(jnp.add, [jnp.square(b - mean) for b in blocks])
    rstd = lax.rsqrt((summed[1:2] + n_local * apart[0:1]) / total + EPS)
    return rstd, (st[i_own, group, 0:1] - mean) * rstd, (st[i_oth, group, 0:1] - mean) * rstd


def left_right(y0, y1, y2):
    rows = y0.shape[0]
    column = lax.broadcasted_iota(jnp.int32, y0.shape, 0) % WIDE
    before = jnp.where(column == 0, 0.0, pltpu.roll(y0, 1, 0))
    after = jnp.where(column == WIDE - 1, 0.0, pltpu.roll(y2, rows - 1, 0))
    return before + y1 + after


def lane_of(group):
    return pl.multiple_of(group * LANES, LANES)


def edge_start(n_own, edge, half):
    return pl.multiple_of((1 - half) * (n_own - edge), WIDE)


def pair_rows(j):
    return pl.ds(pl.multiple_of(j * 2 * WIDE, 2 * WIDE), 2 * WIDE)


def fold(v):
    return jnp.sum(v.reshape(v.shape[0] // 8, 8, LANES), axis=0)


def fwd_kernel(first, pool, layer, total, edge_out, *refs):
    pos, zs = refs[0], refs[1:5]
    if first:
        w_hbm, rest = refs[5], refs[6:]
    else:
        st, gss, w_hbm, rest = refs[5], refs[6:10], refs[10], refs[12:]
    hb_out, zc_out, edge_ref, st_out, hb, w, y, z, tab, hs, sem = rest[-11:]
    load = pltpu.make_async_copy(w_hbm.at[layer], w, sem.at[0])
    load.start()
    save = pltpu.make_async_copy(hb, hb_out.at[layer], sem.at[1])
    t, r = pos[0], pos[1]
    n_own = z.shape[0]
    halo_at = pl.multiple_of((1 - r) * (n_own + WIDE), WIDE)
    zero_at = pl.multiple_of(r * (n_own + WIDE), WIDE)
    hb[pl.ds(zero_at, WIDE), :] = jnp.zeros((WIDE, CHANS), BF16)
    edge = zs[0].shape[0] - n_own
    if not first:
        for k in range(GROUPS):
            rstd, own, oth = norm_tables(st, t ^ k, pos[2], pos[3], float(n_own), total)
            gain, shift = gss[k][layer - 1 : layer, :], gss[k][layer + 7 : layer + 8, :]
            tab[k, 0:1] = rstd * gain
            tab[k, 1:2] = own * gain + shift
            tab[k, 2:3] = oth * gain + shift

    def act(values, k, which):
        if first:
            return values
        n = values.astype(F32) * tab[k, 0:1, :] + tab[k, which : which + 1, :]
        h = n * sigmoid(n)
        return soft(h) if pool else h

    def body(j, carry):
        at = pl.multiple_of(j * 2 * WIDE, 2 * WIDE)
        for k in range(GROUPS):
            h = act(zs[k][pl.ds(at, 2 * WIDE), :], k, 1)
            hb[pl.ds(pl.multiple_of(at + WIDE, WIDE), 2 * WIDE), pl.ds(lane_of(t ^ k), LANES)] = h.astype(BF16)
        return carry

    lax.fori_loop(0, n_own // (2 * WIDE), body, 0)
    for k in range(GROUPS):
        h = act(zs[k][n_own : n_own + edge, :], k, 2)
        if edge > WIDE:
            hs[...] = h
            h = hs[pl.ds(pl.multiple_of(r * WIDE, WIDE), WIDE), :]
        hb[pl.ds(halo_at, WIDE), pl.ds(lane_of(t ^ k), LANES)] = h.astype(BF16)
    save.start()
    load.wait()
    lhs = jnp.concatenate([hb[i * WIDE : i * WIDE + n_own, :] for i in range(3)], axis=1)
    rhs = jnp.concatenate(
        [
            jnp.concatenate([w[:, (3 * i + s) * CHANS : (3 * i + s + 1) * CHANS] for i in range(3)], axis=1)
            for s in range(3)
        ],
        axis=0,
    )
    y[...] = lax.dot_general(lhs, rhs, (((1,), (1,)), ((), ())), preferred_element_type=F32)

    def add_up(j, acc):
        rows = pair_rows(j)
        v = left_right(y[rows, 0:128], y[rows, 128:256], y[rows, 256:384])
        z[rows, :] = v
        return acc + fold(v)

    steps = n_own // (2 * WIDE)
    summed = lax.fori_loop(0, steps, add_up, jnp.zeros((8, LANES), F32))
    mean = jnp.sum(summed, axis=0, keepdims=True) / n_own

    def centre(j, acc):
        rows = pair_rows(j)
        v = z[rows, :] - mean
        z[rows, :] = v
        zc_out[rows, :] = v.astype(BF16)
        return acc + fold(jnp.square(v))

    apart = lax.fori_loop(0, steps, centre, jnp.zeros((8, LANES), F32))
    sums = [mean, jnp.sum(apart, axis=0, keepdims=True), jnp.zeros((6, LANES), F32)]
    sums = jnp.concatenate(sums, axis=0)
    for i in range(st_out.shape[0]):
        st_out[i] = sums
    edge_ref[...] = zc_out[pl.ds(edge_start(n_own, edge_out, r), edge_out), :]
    zc_out[n_own : n_own + edge_out, :] = jnp.zeros((edge_out, LANES), BF16)
    save.wait()


def fwd_step(layer, pool, edge_out, total, pos, slots, st, tables, weights, kept, n_own, devices, ties):
    first = st is None
    layers = weights.shape[0]
    extra = () if first else (st, *tables)
    return pl.pallas_call(
        functools.partial(fwd_kernel, first, pool, layer, total, edge_out),
        out_shape=(
            pltpu.HBM((layers, n_own + 2 * WIDE, CHANS), BF16),
            pltpu.VMEM((n_own + edge_out, LANES), BF16),
            pltpu.VMEM((edge_out, LANES), BF16),
            pltpu.VMEM((devices, 8, LANES), F32),
        ),
        in_specs=[SMEM] + [VMEM] * (4 + len(extra)) + [ANY] * (1 if first else 2) + [FREE] * len(ties),
        out_specs=(ANY, VMEM, VMEM, VMEM),
        input_output_aliases={} if first else {6 + len(extra): 0},
        scratch_shapes=[
            pltpu.VMEM((n_own + 2 * WIDE, CHANS), BF16),
            pltpu.VMEM((LANES, 9 * CHANS), BF16),
            pltpu.VMEM((n_own, 3 * LANES), F32),
            pltpu.VMEM((n_own, LANES), F32),
            pltpu.VMEM((GROUPS, 8, LANES), F32),
            pltpu.VMEM((2 * WIDE, LANES), F32),
            pltpu.SemaphoreType.DMA((2,)),
        ],
        compiler_params=PARAMS,
        cost_estimate=pl.CostEstimate(
            flops=2 * n_own * 9 * CHANS * LANES, bytes_accessed=4 * 1024 * 1024, transcendentals=n_own * CHANS
        ),
        name="conv_forward",
    )(pos, *slots, *extra, in_hbm(weights), *(() if first else (in_hbm(kept),)), *ties)


def below_kernel(layer, pool, total, top, *refs):
    pos, zc, st, gs = refs[:4]
    if top:
        terms, h_out, dn_out, msg, tab = refs[4:]
    else:
        terms, (dn_out, msg, tab) = refs[4:8], refs[-3:]
    n_own = dn_out.shape[0]
    rstd, own, oth = norm_tables(st, pos[0], pos[2], pos[3], float(n_own), total)
    tab[0:1], tab[1:2] = rstd, own
    tab[2:3], tab[3:4] = gs[layer : layer + 1, :], gs[layer + 8 : layer + 9, :]

    def body(j, accs):
        rows = pair_rows(j)
        xhat = zc[rows, :].astype(F32) * tab[0:1, :] + tab[1:2, :]
        n = xhat * tab[2:3, :] + tab[3:4, :]
        sig = sigmoid(n)
        h = n * sig
        if top:
            g = terms[rows, :].astype(F32)
            h_out[rows, :] = h.astype(BF16)
        else:
            g = functools.reduce(jnp.add, [term[rows, :].astype(F32) for term in terms])
        if pool:
            g = soft_pull(h, g)
        dn = g * (sig * (1.0 + n - h))
        dn_out[rows, :] = dn
        return accs[0] + fold(dn), accs[1] + fold(dn * xhat)

    zero = jnp.zeros((8, LANES), F32)
    sums = lax.fori_loop(0, n_own // (2 * WIDE), body, (zero, zero))
    sums = [jnp.sum(v, axis=0, keepdims=True) for v in sums]
    msg[0:WIDE, :] = dn_out[pl.ds(edge_start(n_own, WIDE, pos[1]), WIDE), :]
    msg[WIDE : WIDE + 8, :] = jnp.concatenate(sums + [jnp.zeros((6, LANES), F32)], axis=0)


def below_step(layer, pool, total, pos, zc, st, gs, terms, ties=()):
    n_own = terms[0].shape[0]
    top = len(terms) == 1
    out_shape = [
        pltpu.VMEM((n_own, LANES), F32),
        pltpu.VMEM((WIDE + 8, LANES), F32),
    ]
    if top:
        out_shape = [jax.ShapeDtypeStruct((n_own, LANES), BF16)] + out_shape
    return pl.pallas_call(
        functools.partial(below_kernel, layer, pool, total, top),
        out_shape=tuple(out_shape),
        in_specs=[SMEM] + [VMEM] * (3 + len(terms)) + [FREE] * len(ties),
        out_specs=(VMEM,) * len(out_shape),
        scratch_shapes=[pltpu.VMEM((8, LANES), F32)],
        compiler_params=PARAMS,
        cost_estimate=pl.CostEstimate(flops=40 * n_own * LANES, bytes_accessed=1024 * 1024, transcendentals=n_own * LANES),
        name="silu_backward",
    )(pos, zc, st, gs, *terms, *ties)


def bwd_kernel(layer, total, *refs):
    pos, dn, dedge, sums, zc, st, gs, w_hbm = refs[:8]
    outs, d_out, d, w, y, tab, sem = refs[-10:-6], *refs[-6:]
    load = pltpu.make_async_copy(w_hbm.at[layer], w, sem)
    load.start()
    t, r = pos[0], pos[1]
    n_own = dn.shape[0]
    halo_at = pl.multiple_of((1 - r) * (n_own + WIDE), WIDE)
    zero_at = pl.multiple_of(r * (n_own + WIDE), WIDE)
    edge = zc.shape[0] - n_own
    d[pl.ds(zero_at, WIDE), :] = jnp.zeros((WIDE, 3 * LANES), BF16)
    rstd, own, oth = norm_tables(st, t, pos[2], pos[3], float(n_own), total)
    scale = gs[layer : layer + 1, :] * rstd
    shift_sum, gain_sum = sums[0:1, :], sums[1:2, :]
    slope = scale * gain_sum / total
    tab[0:1] = scale
    tab[1:2] = slope * rstd
    tab[2:3] = scale * shift_sum / total + slope * own
    tab[3:4] = scale * shift_sum / total + slope * oth

    def spread_columns(v, at):
        rows = v.shape[0]
        column = lax.broadcasted_iota(jnp.int32, v.shape, 0) % WIDE
        ahead = jnp.where(column == WIDE - 1, 0.0, pltpu.roll(v, rows - 1, 0))
        behind = jnp.where(column == 0, 0.0, pltpu.roll(v, 1, 0))
        d[pl.ds(at, rows), 0:128] = ahead.astype(BF16)
        d[pl.ds(at, rows), 128:256] = v.astype(BF16)
        d[pl.ds(at, rows), 256:384] = behind.astype(BF16)

    def body(j, carry):
        rows = pair_rows(j)
        v = dn[rows, :] * tab[0:1, :] - tab[2:3, :] - zc[rows, :].astype(F32) * tab[1:2, :]
        spread_columns(v, pl.multiple_of(j * 2 * WIDE + WIDE, WIDE))
        return carry

    lax.fori_loop(0, n_own // (2 * WIDE), body, 0)
    near = n_own if edge == WIDE else pl.multiple_of(n_own + r * WIDE, WIDE)
    near = zc[pl.ds(near, WIDE), :].astype(F32)
    spread_columns(dedge[0:WIDE, :] * tab[0:1, :] - tab[3:4, :] - near * tab[1:2, :], halo_at)
    d_out[...] = d[WIDE : WIDE + n_own, :]
    load.wait()
    lhs = jnp.concatenate([d[(2 - i) * WIDE : (2 - i) * WIDE + n_own, :] for i in range(3)], axis=1)
    rhs = jnp.concatenate([w[:, i * CHANS : (i + 1) * CHANS] for i in range(9)], axis=0)
    y[...] = jnp.dot(lhs, rhs, preferred_element_type=F32)

    def share(j, carry):
        rows = pair_rows(j)
        for k in range(GROUPS):
            outs[k][rows, :] = y[rows, pl.ds(lane_of(t ^ k), LANES)].astype(BF16)
        return carry

    lax.fori_loop(0, n_own // (2 * WIDE), share, 0)


def bwd_step(layer, total, pos, dn, dedge, sums, zc, st, gs, weights, ties):
    n_own = dn.shape[0]
    part = pltpu.VMEM((n_own, LANES), BF16)
    return pl.pallas_call(
        functools.partial(bwd_kernel, layer, total),
        out_shape=(
            part,
            part,
            part,
            part,
            pltpu.VMEM((n_own, 3 * LANES), BF16),
        ),
        in_specs=[SMEM] + [VMEM] * 6 + [ANY] + [FREE] * len(ties),
        out_specs=(VMEM,) * 5,
        scratch_shapes=[
            pltpu.VMEM((n_own + 2 * WIDE, 3 * LANES), BF16),
            pltpu.VMEM((LANES, 9 * CHANS), BF16),
            pltpu.VMEM((n_own, CHANS), F32),
            pltpu.VMEM((8, LANES), F32),
            pltpu.SemaphoreType.DMA,
        ],
        compiler_params=PARAMS,
        cost_estimate=pl.CostEstimate(
            flops=2 * n_own * 9 * CHANS * LANES, bytes_accessed=4 * 1024 * 1024, transcendentals=0
        ),
        name="conv_backward",
    )(pos, dn, dedge, sums, zc, st, gs, in_hbm(weights), *ties)


def last_kernel(t0, t1, t2, t3, *refs):
    out = refs[-1]

    def body(j, carry):
        rows = pair_rows(j)
        out[rows, :] = functools.reduce(jnp.add, [term[rows, :].astype(F32) for term in (t0, t1, t2, t3)])
        return carry

    lax.fori_loop(0, out.shape[0] // (2 * WIDE), body, 0)


def last_step(terms, ties):
    return pl.pallas_call(
        last_kernel,
        out_shape=jax.ShapeDtypeStruct(terms[0].shape, F32),
        in_specs=[VMEM] * 4 + [FREE] * len(ties),
        out_specs=VMEM,
        compiler_params=PARAMS,
        name="add_terms",
    )(*terms, *ties)


def quarters_kernel(parts, *refs):
    out = refs[-1]
    total = functools.reduce(jnp.add, [parts[i].astype(F32) for i in range(4)]).astype(BF16)
    for i in range(4):
        out[i] = total


def add_quarters(parts, ties):
    return pl.pallas_call(
        quarters_kernel,
        out_shape=pltpu.VMEM(parts.shape, BF16),
        in_specs=[VMEM] + [FREE] * len(ties),
        out_specs=VMEM,
        compiler_params=PARAMS,
        cost_estimate=pl.CostEstimate(flops=parts.size, bytes_accessed=4 * parts.size, transcendentals=0),
        name="add_quarters",
    )(parts, *ties)


def halves_kernel(keep, got, out):
    out[...] = (keep[...].astype(F32) + got[...].astype(F32)).astype(BF16)


def add_halves(keep, got):
    return pl.pallas_call(
        halves_kernel,
        out_shape=jax.ShapeDtypeStruct(keep.shape, BF16),
        in_specs=[VMEM] * 2,
        out_specs=VMEM,
        compiler_params=PARAMS,
        cost_estimate=pl.CostEstimate(flops=keep.size, bytes_accessed=6 * keep.size, transcendentals=0),
        name="add_halves",
    )(keep, got)


def wgrad_kernel(layer, pos, d, hb_hbm, *refs):
    keep, send, hb, grad, sem = refs[-5:]
    load = pltpu.make_async_copy(hb_hbm.at[layer], hb, sem)
    load.start()
    n_own = d.shape[0]
    lhs = d[...]
    load.wait()
    for i in range(3):
        part = lax.dot_general(
            lhs, hb[i * WIDE : i * WIDE + n_own, :], (((0,), (0,)), ((), ())), preferred_element_type=F32
        ).astype(BF16)
        for s in range(3):
            grad[:, (3 * i + s) * CHANS : (3 * i + s + 1) * CHANS] = part[s * LANES : (s + 1) * LANES]
    half = LANES // 2
    keep[...] = grad[pl.ds(pl.multiple_of(pos[1] * half, half), half), :]
    send[...] = grad[pl.ds(pl.multiple_of((1 - pos[1]) * half, half), half), :]


def wgrad_step(layer, pos, d, kept, ties):
    half = pltpu.VMEM((LANES // 2, 9 * CHANS), BF16)
    return pl.pallas_call(
        functools.partial(wgrad_kernel, layer),
        out_shape=(half, half),
        in_specs=[SMEM, VMEM, ANY] + [FREE] * len(ties),
        out_specs=(VMEM, VMEM),
        scratch_shapes=[
            pltpu.VMEM(kept.shape[1:], BF16),
            pltpu.VMEM((LANES, 9 * CHANS), BF16),
            pltpu.SemaphoreType.DMA,
        ],
        compiler_params=PARAMS,
        cost_estimate=pl.CostEstimate(
            flops=2 * d.shape[0] * 9 * CHANS * LANES, bytes_accessed=3 * 1024 * 1024, transcendentals=0
        ),
        name="kernel_gradient",
    )(pos, d, in_hbm(kept), *ties)


def place_kernel(pos, mine, other, *refs):
    refs[-1][0] = jnp.where(pl.program_id(0) // 4 == pos[1], mine[...], other[...]).astype(F32)


def place_step(layer, pos, mine, other, whole, layers):
    rows = LANES // 8
    block = pl.BlockSpec((rows, 9 * CHANS), lambda i: (i % 4, 0))
    return pl.pallas_call(
        place_kernel,
        grid=(8,),
        out_shape=jax.ShapeDtypeStruct((layers, LANES, 9 * CHANS), F32),
        in_specs=[SMEM, block, block] + ([] if whole is None else [ANY]),
        out_specs=pl.BlockSpec((1, rows, 9 * CHANS), lambda i: (layer, i, 0)),
        input_output_aliases={} if whole is None else {3: 0},
        compiler_params=PARAMS,
        cost_estimate=pl.CostEstimate(flops=0, bytes_accessed=4 * 1024 * 1024, transcendentals=0),
        name="place_gradient",
    )(pos, mine, other, *(() if whole is None else (whole,)))


def swap_with(value, axis, k):
    return lax.ppermute(value, axis, [(i, i ^ k) for i in range(lax.axis_size(axis))])


def spread(own):
    return (own, *[swap_with(own, "tensor", k) for k in range(1, GROUPS)])


def halo_of_input(x, half):
    n_own = x.shape[0]
    edge = jnp.where(half == 0, x[n_own - WIDE :], x[:WIDE])
    return jnp.concatenate([x, swap_with(edge, "rows", 1)], axis=0)


def fast_local(section_input, conv_weights, norm_gains, norm_shifts, out_grad, out_mask):
    images, rows_here, width = out_mask.shape
    layers = conv_weights.shape[0]
    n_own = rows_here * width
    parts = lax.axis_size("dp") * lax.axis_size("rows")
    total = float(n_own * parts)
    t, half = lax.axis_index("tensor"), lax.axis_index("rows")
    image = lax.axis_index("dp")
    pos = jnp.stack([t, half, 2 * image + half, 2 * image + 1 - half]).astype(jnp.int32)
    middle = layers // 2
    x = to_maps(section_input, width).reshape(n_own, LANES)
    slots = spread(halo_of_input(x, half))
    pad = jnp.zeros((8 - layers, LANES), F32)
    tables = spread(jnp.concatenate([norm_gains, pad, norm_shifts, pad], axis=0))
    top_grad = (to_maps(out_grad, width) * out_mask[..., None].astype(BF16)).reshape(n_own, LANES)

    st, kept = None, None
    halves = ("dp", "rows")
    kept_z, kept_st = [], []
    for layer in range(layers):
        last = layer + 1 == layers
        edge = 2 * WIDE if layer + 1 == middle else WIDE
        everyone = halves if last else (*halves, "tensor")
        devices = parts if last else parts * GROUPS
        kept, zc, rim, local = fwd_step(
            layer,
            layer == middle,
            edge,
            total,
            pos,
            slots,
            st,
            tables,
            conv_weights,
            kept,
            n_own,
            devices,
            (top_grad,) if layer == 2 else (),
        )
        rim = swap_with(rim, "rows", 1)
        st = lax.all_to_all(local, everyone, split_axis=0, concat_axis=0, tiled=True)
        st = st.reshape(parts, devices // parts, 8, LANES)
        zc = lax.dynamic_update_slice_in_dim(zc, rim, n_own, axis=0)
        kept_z.append(zc)
        kept_st.append(st)
        if not last:
            slots = spread(zc)
    top = layers - 1
    h_last, dn, msg = below_step(top, False, total, pos, kept_z[top], kept_st[top], tables[0], (top_grad,))

    def place(layer, mine, whole):
        return place_step(layer, pos, mine, swap_with(mine, "rows", 1), whole, layers)

    sum_list, pairs = [None] * layers, [None] * layers
    ahead, back = [[0, 1, 2, 3]], [[3, 2, 1, 0]]
    ties, whole = (), None
    for layer in range(layers - 1, -1, -1):
        got = swap_with(msg, "rows", 1)
        sums = msg[WIDE:] + got[WIDE:]
        for k in (1, 2):
            sums = sums + swap_with(sums, "dp", k)
        sum_list[layer] = sums
        *terms, d = bwd_step(
            layer, total, pos, dn, got, sums, kept_z[layer], kept_st[layer], tables[0], conv_weights, ()
        )
        terms = (terms[0], *[swap_with(terms[k], "tensor", k) for k in range(1, GROUPS)])
        keep, send = wgrad_step(layer, pos, d, kept, ())
        if layer > 0:
            below = layer - 1
            dn, msg = below_step(
                below, layer == middle, total, pos, kept_z[below], kept_st[below], tables[0], terms, (keep, *ties)
            )
        else:
            grad = last_step(terms, (keep, *ties))
        pairs[layer] = add_halves(keep, swap_with(send, "rows", 1))
        ties = (pairs[layer],)
        if layer == 5:
            first = lax.psum(pairs[5], "dp", axis_index_groups=ahead)
        if layer == 3:
            mid = lax.psum((pairs[4], pairs[3]), "dp", axis_index_groups=back)
            whole = place(5, first, None)
            ties = (pairs[3], in_hbm(whole))
        if layer == 1:
            whole = place(3, mid[1], place(4, mid[0], whole))
            ties = (pairs[1], in_hbm(whole))
    tied, first = lax.optimization_barrier(((pairs[2], pairs[1]), first))
    lower = lax.psum(tied, "dp", axis_index_groups=ahead)
    shape = (images, rows_here, width, LANES)
    outputs = (from_maps(h_last.reshape(shape)), from_maps(grad.reshape(shape)))
    rows = LANES // 8
    pieces = lax.all_to_all(pairs[0].reshape(4, rows, -1), "dp", split_axis=0, concat_axis=0, tiled=True)
    pieces = add_quarters(pieces, tuple(in_hbm(v) for v in outputs))
    pieces = lax.all_to_all(pieces, "dp", split_axis=0, concat_axis=0, tiled=True)
    whole = place(0, pieces.reshape(pairs[0].shape), whole)
    whole = place(1, lower[1], place(2, lower[0], whole))
    sums = jnp.stack(sum_list)
    return (*outputs, whole, sums[:, 1], sums[:, 0])


def solution(mesh):
    in_specs = (
        P("dp", "rows", "tensor"),
        P(None, "tensor", None),
        P(None, "tensor"),
        P(None, "tensor"),
        P("dp", "rows", "tensor"),
        P("dp", "rows", None),
    )
    out_specs = (
        P("dp", "rows", "tensor"),
        P("dp", "rows", "tensor"),
        P(None, "tensor", None),
        P(None, "tensor"),
        P(None, "tensor"),
    )
    local = fast_local if fits_kernels(mesh) else generic_local
    return jax.shard_map(local, mesh=mesh, in_specs=in_specs, out_specs=out_specs, check_vma=False)
```

```python
import functools

import jax
import jax.numpy as jnp
from jax import lax
from jax.experimental import pallas as pl
from jax.experimental.pallas import tpu as pltpu
from jax.sharding import PartitionSpec as P

EPS = 1e-05


def padded_2(cells, sides, width):
    for axis, dim in sides:
        count = lax.axis_size(axis)
        ends = count - 1
        head = lax.slice_in_dim(cells, 0, width, axis=dim)
        tail = lax.slice_in_dim(cells, cells.shape[dim] - width, cells.shape[dim], axis=dim)
        cells = jnp.concatenate(
            [
                lax.ppermute(tail, axis, [(i, (i + 1) % count) for i in range(ends)]),
                cells,
                lax.ppermute(head, axis, [((i + 1) % count, i) for i in range(ends)]),
            ],
            axis=dim,
        )
    return cells


def to_maps(flat, width):
    count, high, merged = flat.shape
    return flat.reshape(count, high, merged // width, width).transpose(0, 1, 3, 2)


def from_maps(maps):
    count, high, wide, chans = maps.shape
    return maps.transpose(0, 1, 3, 2).reshape(count, high, chans * wide)


def spatial_conv(padded, kernel):
    return lax.conv_general_dilated(
        padded,
        kernel,
        (1, 1),
        ((0, 0), (1, 1)),
        dimension_numbers=("NHWC", "HWIO", "NHWC"),
        preferred_element_type=jnp.float32,
    )


def flipped(kernel):
    return jnp.transpose(kernel[::-1, ::-1], (0, 1, 3, 2))


def pool_unpool(values):
    count, high, wide, chans = values.shape
    blocks = values.reshape(count, high // 2, 2, wide // 2, 2, chans)
    pooled = jax.nn.logsumexp(blocks, axis=(2, 4), keepdims=True)
    return (jnp.exp(blocks - pooled) * pooled).reshape(values.shape)


def moments(conv_out, total_pixels):
    summed = lax.psum(jnp.sum(conv_out, axis=(0, 1, 2)), ("dp", "rows"))
    mean = summed / total_pixels
    spread = lax.psum(jnp.sum(jnp.square(conv_out - mean), axis=(0, 1, 2)), ("dp", "rows"))
    var = spread / total_pixels
    return (mean, lax.rsqrt(var + EPS))


def kernel_grad(whole, dconv):
    images, rows_here, width, chans = dconv.shape
    widened = jnp.pad(whole, ((0, 0), (0, 0), (1, 1), (0, 0)))
    stacked = []
    for row_off in range(3):
        line = []
        for col_off in range(3):
            window = widened[:, row_off : row_off + rows_here, col_off : col_off + width, :]
            line.append(
                jnp.einsum("bhwc,bhwo->co", window, dconv, preferred_element_type=jnp.float32)
            )
        stacked.append(jnp.stack(line))
    return jnp.stack(stacked)


def generic_local(section_input, conv_weights, norm_gains, norm_shifts, out_grad, out_mask):
    width = out_mask.shape[2]
    images, rows_here = (out_mask.shape[0], out_mask.shape[1])
    total_pixels = float(images * rows_here * width * lax.axis_size("dp") * lax.axis_size("rows"))
    layers, out_here, flat_in = conv_weights.shape
    chans_in = flat_in // 9
    kernels_hwio = conv_weights.reshape(layers, out_here, 3, 3, chans_in).transpose(0, 2, 3, 4, 1)
    middle = layers // 2
    kept = []
    acting = to_maps(section_input, width)
    current = acting.astype(jnp.float32)
    pre_pool = current
    for index in range(layers):
        if index == middle:
            pre_pool = current
            acting = pool_unpool(pre_pool).astype(jnp.bfloat16)
        padded = padded_2(acting, (("rows", 1),), 1)
        whole = lax.all_gather(padded, "tensor", axis=3, tiled=True)
        conv_out = spatial_conv(whole, kernels_hwio[index])
        mean, rstd = moments(conv_out, total_pixels)
        normed = (conv_out - mean) * rstd
        shifted = normed * norm_gains[index] + norm_shifts[index]
        current = jax.nn.silu(shifted)
        acting = current.astype(jnp.bfloat16)
        kept.append((whole, normed, shifted, rstd))
    grad = to_maps(out_grad, width).astype(jnp.float32) * out_mask[..., None].astype(jnp.float32)
    kernel_list = [None] * layers
    gain_list = [None] * layers
    shift_list = [None] * layers
    for index in range(layers - 1, -1, -1):
        whole, normed, shifted, rstd = kept[index]
        unused, pull_silu = jax.vjp(jax.nn.silu, shifted)
        dshift = pull_silu(grad)[0]
        gain_sum, shift_sum = lax.psum(
            (jnp.sum(dshift * normed, axis=(0, 1, 2)), jnp.sum(dshift, axis=(0, 1, 2))),
            ("dp", "rows"),
        )
        gain_list[index] = gain_sum
        shift_list[index] = shift_sum
        dconv = (
            norm_gains[index]
            * rstd
            * (dshift - shift_sum / total_pixels - normed * gain_sum / total_pixels)
        ).astype(jnp.bfloat16)
        summed_kernel = lax.psum(
            kernel_grad(whole, dconv).astype(jnp.bfloat16), ("dp", "rows")
        ).astype(jnp.float32)
        kernel_list[index] = summed_kernel.transpose(3, 0, 1, 2).reshape(out_here, flat_in)
        grad_rim = padded_2(dconv, (("rows", 1),), 1)
        partial_terms = spatial_conv(grad_rim, flipped(kernels_hwio[index]))
        grad_in = lax.psum_scatter(
            partial_terms.astype(jnp.bfloat16), "tensor", scatter_dimension=3, tiled=True
        ).astype(jnp.float32)
        if index == middle:
            unused, pull_pool = jax.vjp(pool_unpool, pre_pool)
            grad = pull_pool(grad_in)[0]
        else:
            grad = grad_in
    return (
        from_maps(acting),
        from_maps(grad),
        jnp.stack(kernel_list),
        jnp.stack(gain_list),
        jnp.stack(shift_list),
    )


GROUPS = 4
LANES = 128
WIDE = 48
CHANS = GROUPS * LANES
F32 = jnp.float32
BF16 = jnp.bfloat16
VMEM = pl.BlockSpec(memory_space=pltpu.VMEM)
SMEM = pl.BlockSpec(memory_space=pltpu.SMEM)
ANY = pl.BlockSpec(memory_space=pltpu.HBM)
FREE = pl.BlockSpec(memory_space=pl.ANY)
PARAMS = pltpu.CompilerParams(vmem_limit_bytes=20 * 1024 * 1024)


def in_hbm(value):
    return pltpu.with_memory_space_constraint(value, pltpu.HBM)


def fits_kernels(mesh):
    return mesh.shape["tensor"] == GROUPS and mesh.shape["rows"] == 2 and mesh.shape["dp"] == 4


def sigmoid(v):
    return 0.5 * jnp.tanh(0.5 * v) + 0.5


def swap_columns(v):
    column = lax.broadcasted_iota(jnp.int32, v.shape, 0)
    return jnp.where(column % 2 == 0, pltpu.roll(v, WIDE - 1, 0), pltpu.roll(v, 1, 0))


def soft_parts(h):
    top = jnp.maximum(h[0], h[1])
    top = jnp.maximum(top, swap_columns(top))
    e0, e1 = jnp.exp(h[0] - top), jnp.exp(h[1] - top)
    total = e0 + e1
    total = total + swap_columns(total)
    pooled = top + jnp.log(total)
    inverse = 1.0 / total
    return e0 * inverse, e1 * inverse, pooled


def soft(h):
    h = h.reshape(2, WIDE, LANES)
    q0, q1, pooled = soft_parts(h)
    return jnp.concatenate([q0 * pooled, q1 * pooled], axis=0)


def soft_pull(h, grad):
    h = h.reshape(2, WIDE, LANES)
    grad = grad.reshape(2, WIDE, LANES)
    q0, q1, pooled = soft_parts(h)
    mix = q0 * grad[0] + q1 * grad[1]
    mix = mix + swap_columns(mix)
    return jnp.concatenate(
        [q0 * (pooled * (grad[0] - mix) + mix), q1 * (pooled * (grad[1] - mix) + mix)], axis=0
    )


def moments_kernel(layer, n_local, total, pos, st, gs, out):
    parts = st.shape[0]
    blocks = [st[i] for i in range(parts)]
    summed = functools.reduce(jnp.add, blocks)
    mean = summed[0:1] / parts
    apart = functools.reduce(jnp.add, [jnp.square(b - mean) for b in blocks])
    rstd = lax.rsqrt((summed[1:2] + n_local * apart[0:1]) / total + EPS)
    own, oth = (st[pos[2], 0:1] - mean) * rstd, (st[pos[3], 0:1] - mean) * rstd
    gain, shift = gs[layer : layer + 1, :], gs[layer + 8 : layer + 9, :]
    rows = [rstd * gain, own * gain + shift, oth * gain + shift, rstd, own, oth]
    out[...] = jnp.concatenate(rows + [jnp.zeros((2, LANES), F32)], axis=0)


def moments_step(layer, n_local, total, pos, st, gs):
    return pl.pallas_call(
        functools.partial(moments_kernel, layer, n_local, total),
        out_shape=pltpu.VMEM((8, LANES), F32),
        in_specs=[SMEM, VMEM, VMEM],
        out_specs=VMEM,
        compiler_params=PARAMS,
        cost_estimate=pl.CostEstimate(flops=1024, bytes_accessed=64 * 1024, transcendentals=128),
        name="moments",
    )(pos, st, gs)


def left_right(y0, y1, y2):
    rows = y0.shape[0]
    column = lax.broadcasted_iota(jnp.int32, y0.shape, 0) % WIDE
    before = jnp.where(column == 0, 0.0, pltpu.roll(y0, 1, 0))
    after = jnp.where(column == WIDE - 1, 0.0, pltpu.roll(y2, rows - 1, 0))
    return before + y1 + after


def lane_of(group):
    return pl.multiple_of(group * LANES, LANES)


def edge_start(n_own, edge, half):
    return pl.multiple_of((1 - half) * (n_own - edge), WIDE)


def pair_rows(j):
    return pl.ds(pl.multiple_of(j * 2 * WIDE, 2 * WIDE), 2 * WIDE)


def fold(v):
    return jnp.sum(v.reshape(v.shape[0] // 8, 8, LANES), axis=0)


def fwd_kernel(first, pool, layer, total, edge_out, *refs):
    pos, zs = refs[0], refs[1:5]
    if first:
        w_hbm, rest = refs[5], refs[6:]
    else:
        tabs, w_hbm, rest = refs[5:9], refs[9], refs[11:]
    hb_out, zc_out, edge_ref, st_out, hb, w, y, z, hs, sem = rest[-10:]
    load = pltpu.make_async_copy(w_hbm.at[layer], w, sem.at[0])
    load.start()
    save = pltpu.make_async_copy(hb, hb_out.at[layer], sem.at[1])
    t, r = pos[0], pos[1]
    n_own = z.shape[0]
    halo_at = pl.multiple_of((1 - r) * (n_own + WIDE), WIDE)
    zero_at = pl.multiple_of(r * (n_own + WIDE), WIDE)
    hb[pl.ds(zero_at, WIDE), :] = jnp.zeros((WIDE, CHANS), BF16)
    edge = zs[0].shape[0] - n_own
    def act(values, k, which):
        if first:
            return values
        n = values.astype(F32) * tabs[k][0:1, :] + tabs[k][which : which + 1, :]
        h = n * sigmoid(n)
        return soft(h) if pool else h

    def body(j, carry):
        at = pl.multiple_of(j * 2 * WIDE, 2 * WIDE)
        for k in range(GROUPS):
            h = act(zs[k][pl.ds(at, 2 * WIDE), :], k, 1)
            hb[pl.ds(pl.multiple_of(at + WIDE, WIDE), 2 * WIDE), pl.ds(lane_of(t ^ k), LANES)] = h.astype(BF16)
        return carry

    lax.fori_loop(0, n_own // (2 * WIDE), body, 0)
    for k in range(GROUPS):
        h = act(zs[k][n_own : n_own + edge, :], k, 2)
        if edge > WIDE:
            hs[...] = h
            h = hs[pl.ds(pl.multiple_of(r * WIDE, WIDE), WIDE), :]
        hb[pl.ds(halo_at, WIDE), pl.ds(lane_of(t ^ k), LANES)] = h.astype(BF16)
    save.start()
    load.wait()
    lhs = jnp.concatenate([hb[i * WIDE : i * WIDE + n_own, :] for i in range(3)], axis=1)
    rhs = jnp.concatenate(
        [
            jnp.concatenate([w[:, (3 * i + s) * CHANS : (3 * i + s + 1) * CHANS] for i in range(3)], axis=1)
            for s in range(3)
        ],
        axis=0,
    )
    y[...] = lax.dot_general(lhs, rhs, (((1,), (1,)), ((), ())), preferred_element_type=F32)

    def add_up(j, acc):
        rows = pair_rows(j)
        v = left_right(y[rows, 0:128], y[rows, 128:256], y[rows, 256:384])
        z[rows, :] = v
        return acc + fold(v)

    steps = n_own // (2 * WIDE)
    summed = lax.fori_loop(0, steps, add_up, jnp.zeros((8, LANES), F32))
    mean = jnp.sum(summed, axis=0, keepdims=True) / n_own

    def centre(j, acc):
        rows = pair_rows(j)
        v = z[rows, :] - mean
        z[rows, :] = v
        zc_out[rows, :] = v.astype(BF16)
        return acc + fold(jnp.square(v))

    apart = lax.fori_loop(0, steps, centre, jnp.zeros((8, LANES), F32))
    sums = [mean, jnp.sum(apart, axis=0, keepdims=True), jnp.zeros((6, LANES), F32)]
    sums = jnp.concatenate(sums, axis=0)
    for i in range(st_out.shape[0]):
        st_out[i] = sums
    edge_ref[...] = zc_out[pl.ds(edge_start(n_own, edge_out, r), edge_out), :]
    zc_out[n_own : n_own + edge_out, :] = jnp.zeros((edge_out, LANES), BF16)
    save.wait()


def fwd_step(layer, pool, edge_out, total, pos, slots, tabs, weights, kept, n_own, parts, ties):
    first = tabs is None
    layers = weights.shape[0]
    extra = () if first else tabs
    return pl.pallas_call(
        functools.partial(fwd_kernel, first, pool, layer, total, edge_out),
        out_shape=(
            pltpu.HBM((layers, n_own + 2 * WIDE, CHANS), BF16),
            pltpu.VMEM((n_own + edge_out, LANES), BF16),
            pltpu.VMEM((edge_out, LANES), BF16),
            pltpu.VMEM((parts, 8, LANES), F32),
        ),
        in_specs=[SMEM] + [VMEM] * (4 + len(extra)) + [ANY] * (1 if first else 2) + [FREE] * len(ties),
        out_specs=(ANY, VMEM, VMEM, VMEM),
        input_output_aliases={} if first else {6 + len(extra): 0},
        scratch_shapes=[
            pltpu.VMEM((n_own + 2 * WIDE, CHANS), BF16),
            pltpu.VMEM((LANES, 9 * CHANS), BF16),
            pltpu.VMEM((n_own, 3 * LANES), F32),
            pltpu.VMEM((n_own, LANES), F32),
            pltpu.VMEM((2 * WIDE, LANES), F32),
            pltpu.SemaphoreType.DMA((2,)),
        ],
        compiler_params=PARAMS,
        cost_estimate=pl.CostEstimate(
            flops=2 * n_own * 9 * CHANS * LANES, bytes_accessed=4 * 1024 * 1024, transcendentals=n_own * CHANS
        ),
        name="conv_forward",
    )(pos, *slots, *extra, in_hbm(weights), *(() if first else (in_hbm(kept),)), *ties)


def below_kernel(layer, pool, total, top, *refs):
    pos, zc, mo, gs = refs[:4]
    if top:
        terms, h_out, dn_out, msg, tab = refs[4:]
    else:
        terms, (dn_out, msg, tab) = refs[4:8], refs[-3:]
    n_own = dn_out.shape[0]
    tab[0:1], tab[1:2] = mo[3:4, :], mo[4:5, :]
    tab[2:3], tab[3:4] = gs[layer : layer + 1, :], gs[layer + 8 : layer + 9, :]

    def body(j, accs):
        rows = pair_rows(j)
        xhat = zc[rows, :].astype(F32) * tab[0:1, :] + tab[1:2, :]
        n = xhat * tab[2:3, :] + tab[3:4, :]
        sig = sigmoid(n)
        h = n * sig
        if top:
            g = terms[rows, :].astype(F32)
            h_out[rows, :] = h.astype(BF16)
        else:
            g = functools.reduce(jnp.add, [term[rows, :].astype(F32) for term in terms])
        if pool:
            g = soft_pull(h, g)
        dn = g * (sig * (1.0 + n - h))
        dn_out[rows, :] = dn
        return accs[0] + fold(dn), accs[1] + fold(dn * xhat)

    zero = jnp.zeros((8, LANES), F32)
    sums = lax.fori_loop(0, n_own // (2 * WIDE), body, (zero, zero))
    sums = [jnp.sum(v, axis=0, keepdims=True) for v in sums]
    msg[0:WIDE, :] = dn_out[pl.ds(edge_start(n_own, WIDE, pos[1]), WIDE), :]
    msg[WIDE : WIDE + 8, :] = jnp.concatenate(sums + [jnp.zeros((6, LANES), F32)], axis=0)


def below_step(layer, pool, total, pos, zc, mo, gs, terms, ties=()):
    n_own = terms[0].shape[0]
    top = len(terms) == 1
    out_shape = [
        pltpu.VMEM((n_own, LANES), F32),
        pltpu.VMEM((WIDE + 8, LANES), F32),
    ]
    if top:
        out_shape = [jax.ShapeDtypeStruct((n_own, LANES), BF16)] + out_shape
    return pl.pallas_call(
        functools.partial(below_kernel, layer, pool, total, top),
        out_shape=tuple(out_shape),
        in_specs=[SMEM] + [VMEM] * (3 + len(terms)) + [FREE] * len(ties),
        out_specs=(VMEM,) * len(out_shape),
        scratch_shapes=[pltpu.VMEM((8, LANES), F32)],
        compiler_params=PARAMS,
        cost_estimate=pl.CostEstimate(flops=40 * n_own * LANES, bytes_accessed=1024 * 1024, transcendentals=n_own * LANES),
        name="silu_backward",
    )(pos, zc, mo, gs, *terms, *ties)


def bwd_kernel(layer, total, halves, *refs):
    pos, dn, dedge, sums, zc, mo, gs, w_hbm = refs[:8]
    if halves:
        keep, got, pair = refs[8], refs[9], refs[-6]
        outs, d_out = refs[-11:-7], refs[-7]
    else:
        outs, d_out = refs[-10:-6], refs[-6]
    d, w, y, tab, sem = refs[-5:]
    load = pltpu.make_async_copy(w_hbm.at[layer], w, sem)
    load.start()
    t, r = pos[0], pos[1]
    n_own = dn.shape[0]
    if halves:
        pair[...] = (keep[...].astype(F32) + got[...].astype(F32)).astype(BF16)
    halo_at = pl.multiple_of((1 - r) * (n_own + WIDE), WIDE)
    zero_at = pl.multiple_of(r * (n_own + WIDE), WIDE)
    edge = zc.shape[0] - n_own
    d[pl.ds(zero_at, WIDE), :] = jnp.zeros((WIDE, 3 * LANES), BF16)
    scale, rstd, own, oth = mo[0:1, :], mo[3:4, :], mo[4:5, :], mo[5:6, :]
    shift_sum, gain_sum = sums[0:1, :], sums[1:2, :]
    slope = scale * gain_sum / total
    tab[0:1] = scale
    tab[1:2] = slope * rstd
    tab[2:3] = scale * shift_sum / total + slope * own
    tab[3:4] = scale * shift_sum / total + slope * oth

    def spread_columns(v, at):
        rows = v.shape[0]
        column = lax.broadcasted_iota(jnp.int32, v.shape, 0) % WIDE
        ahead = jnp.where(column == WIDE - 1, 0.0, pltpu.roll(v, rows - 1, 0))
        behind = jnp.where(column == 0, 0.0, pltpu.roll(v, 1, 0))
        d[pl.ds(at, rows), 0:128] = ahead.astype(BF16)
        d[pl.ds(at, rows), 128:256] = v.astype(BF16)
        d[pl.ds(at, rows), 256:384] = behind.astype(BF16)

    def body(j, carry):
        rows = pair_rows(j)
        v = dn[rows, :] * tab[0:1, :] - tab[2:3, :] - zc[rows, :].astype(F32) * tab[1:2, :]
        spread_columns(v, pl.multiple_of(j * 2 * WIDE + WIDE, WIDE))
        return carry

    lax.fori_loop(0, n_own // (2 * WIDE), body, 0)
    near = n_own if edge == WIDE else pl.multiple_of(n_own + r * WIDE, WIDE)
    near = zc[pl.ds(near, WIDE), :].astype(F32)
    spread_columns(dedge[0:WIDE, :] * tab[0:1, :] - tab[3:4, :] - near * tab[1:2, :], halo_at)
    d_out[...] = d[WIDE : WIDE + n_own, :]
    load.wait()
    lhs = jnp.concatenate([d[(2 - i) * WIDE : (2 - i) * WIDE + n_own, :] for i in range(3)], axis=1)
    rhs = jnp.concatenate([w[:, i * CHANS : (i + 1) * CHANS] for i in range(9)], axis=0)
    y[...] = jnp.dot(lhs, rhs, preferred_element_type=F32)

    def share(j, carry):
        rows = pair_rows(j)
        for k in range(GROUPS):
            outs[k][rows, :] = y[rows, pl.ds(lane_of(t ^ k), LANES)].astype(BF16)
        return carry

    lax.fori_loop(0, n_own // (2 * WIDE), share, 0)


def bwd_step(layer, total, pos, dn, dedge, sums, zc, mo, gs, weights, halves):
    n_own = dn.shape[0]
    part = pltpu.VMEM((n_own, LANES), BF16)
    pair = tuple(pltpu.VMEM(v.shape, BF16) for v in halves[:1])
    return pl.pallas_call(
        functools.partial(bwd_kernel, layer, total, len(halves)),
        out_shape=(part, part, part, part, pltpu.VMEM((n_own, 3 * LANES), BF16), *pair),
        in_specs=[SMEM] + [VMEM] * 6 + [ANY] + [VMEM] * len(halves),
        out_specs=(VMEM,) * (5 + len(pair)),
        scratch_shapes=[
            pltpu.VMEM((n_own + 2 * WIDE, 3 * LANES), BF16),
            pltpu.VMEM((LANES, 9 * CHANS), BF16),
            pltpu.VMEM((n_own, CHANS), F32),
            pltpu.VMEM((8, LANES), F32),
            pltpu.SemaphoreType.DMA,
        ],
        compiler_params=PARAMS,
        cost_estimate=pl.CostEstimate(
            flops=2 * n_own * 9 * CHANS * LANES, bytes_accessed=4 * 1024 * 1024, transcendentals=0
        ),
        name="conv_backward",
    )(pos, dn, dedge, sums, zc, mo, gs, in_hbm(weights), *halves)


def last_kernel(t0, t1, t2, t3, *refs):
    out = refs[-1]

    def body(j, carry):
        rows = pair_rows(j)
        out[rows, :] = functools.reduce(jnp.add, [term[rows, :].astype(F32) for term in (t0, t1, t2, t3)])
        return carry

    lax.fori_loop(0, out.shape[0] // (2 * WIDE), body, 0)


def last_step(terms, ties):
    return pl.pallas_call(
        last_kernel,
        out_shape=jax.ShapeDtypeStruct(terms[0].shape, F32),
        in_specs=[VMEM] * 4 + [FREE] * len(ties),
        out_specs=VMEM,
        compiler_params=PARAMS,
        name="add_terms",
    )(*terms, *ties)


def halves_kernel(keep, got, out):
    out[...] = (keep[...].astype(F32) + got[...].astype(F32)).astype(BF16)


def add_halves(keep, got):
    return pl.pallas_call(
        halves_kernel,
        out_shape=jax.ShapeDtypeStruct(keep.shape, BF16),
        in_specs=[VMEM] * 2,
        out_specs=VMEM,
        compiler_params=PARAMS,
        cost_estimate=pl.CostEstimate(flops=keep.size, bytes_accessed=6 * keep.size, transcendentals=0),
        name="add_halves",
    )(keep, got)


def wgrad_kernel(layer, pos, d, hb_hbm, *refs):
    keep, send, hb, grad, sem = refs[-5:]
    load = pltpu.make_async_copy(hb_hbm.at[layer], hb, sem)
    load.start()
    n_own = d.shape[0]
    lhs = d[...]
    load.wait()
    for i in range(3):
        part = lax.dot_general(
            lhs, hb[i * WIDE : i * WIDE + n_own, :], (((0,), (0,)), ((), ())), preferred_element_type=F32
        ).astype(BF16)
        for s in range(3):
            grad[:, (3 * i + s) * CHANS : (3 * i + s + 1) * CHANS] = part[s * LANES : (s + 1) * LANES]
    half = LANES // 2
    keep[...] = grad[pl.ds(pl.multiple_of(pos[1] * half, half), half), :]
    send[...] = grad[pl.ds(pl.multiple_of((1 - pos[1]) * half, half), half), :]


def wgrad_step(layer, pos, d, kept, ties):
    half = pltpu.VMEM((LANES // 2, 9 * CHANS), BF16)
    return pl.pallas_call(
        functools.partial(wgrad_kernel, layer),
        out_shape=(half, half),
        in_specs=[SMEM, VMEM, ANY] + [FREE] * len(ties),
        out_specs=(VMEM, VMEM),
        scratch_shapes=[
            pltpu.VMEM(kept.shape[1:], BF16),
            pltpu.VMEM((LANES, 9 * CHANS), BF16),
            pltpu.SemaphoreType.DMA,
        ],
        compiler_params=PARAMS,
        cost_estimate=pl.CostEstimate(
            flops=2 * d.shape[0] * 9 * CHANS * LANES, bytes_accessed=3 * 1024 * 1024, transcendentals=0
        ),
        name="kernel_gradient",
    )(pos, d, in_hbm(kept), *ties)


def place_kernel(layers, fresh, pos, *refs):
    count = 2 * len(layers)
    sources = refs[:count]
    out, held, wide, sem = refs[-4:]
    half = LANES // 2
    r = pos[1]
    loads = [pltpu.make_async_copy(sources[j], held.at[j], sem.at[j]) for j in range(count)]
    for load in loads:
        load.start()
    stores = []
    for j in range(count):
        at = pl.multiple_of((r if j % 2 == 0 else 1 - r) * half, half)
        if j >= 2:
            stores[j - 2].wait()
        loads[j].wait()
        wide[j % 2] = held[j].astype(F32)
        store = pltpu.make_async_copy(wide.at[j % 2], out.at[layers[j // 2], pl.ds(at, half)], sem.at[count + j])
        store.start()
        stores.append(store)
    for store in stores[-2:]:
        store.wait()


def place_step(layers, pos, sources, whole, count):
    half = LANES // 2
    jobs = len(sources)
    return pl.pallas_call(
        functools.partial(place_kernel, layers, whole is None),
        out_shape=pltpu.HBM((count, LANES, 9 * CHANS), F32),
        in_specs=[SMEM] + [ANY] * jobs + ([] if whole is None else [ANY]),
        out_specs=ANY,
        input_output_aliases={} if whole is None else {1 + jobs: 0},
        scratch_shapes=[
            pltpu.VMEM((jobs, half, 9 * CHANS), BF16),
            pltpu.VMEM((2, half, 9 * CHANS), F32),
            pltpu.SemaphoreType.DMA((2 * jobs,)),
        ],
        compiler_params=PARAMS,
        cost_estimate=pl.CostEstimate(flops=0, bytes_accessed=jobs * 2 * 1024 * 1024, transcendentals=0),
        name="place_gradients",
    )(pos, *[in_hbm(v) for v in sources], *(() if whole is None else (in_hbm(whole),)))


def swap_with(value, axis, k):
    return lax.ppermute(value, axis, [(i, i ^ k) for i in range(lax.axis_size(axis))])


def spread(own):
    return (own, *[swap_with(own, "tensor", k) for k in range(1, GROUPS)])


def halo_of_input(x, half):
    n_own = x.shape[0]
    edge = jnp.where(half == 0, x[n_own - WIDE :], x[:WIDE])
    return jnp.concatenate([x, swap_with(edge, "rows", 1)], axis=0)


def fast_local(section_input, conv_weights, norm_gains, norm_shifts, out_grad, out_mask):
    images, rows_here, width = out_mask.shape
    layers = conv_weights.shape[0]
    n_own = rows_here * width
    parts = lax.axis_size("dp") * lax.axis_size("rows")
    total = float(n_own * parts)
    t, half = lax.axis_index("tensor"), lax.axis_index("rows")
    image = lax.axis_index("dp")
    pos = jnp.stack([t, half, 2 * image + half, 2 * image + 1 - half]).astype(jnp.int32)
    middle = layers // 2
    x = to_maps(section_input, width).reshape(n_own, LANES)
    slots = spread(halo_of_input(x, half))
    pad = jnp.zeros((8 - layers, LANES), F32)
    gains = jnp.concatenate([norm_gains, pad, norm_shifts, pad], axis=0)
    top_grad = (to_maps(out_grad, width) * out_mask[..., None].astype(BF16)).reshape(n_own, LANES)

    tabs, kept = None, None
    halves = ("dp", "rows")
    kept_z, kept_mo = [], []
    for layer in range(layers):
        edge = 2 * WIDE if layer + 1 == middle else WIDE
        tie = (top_grad,) if layer == 2 else ()
        kept, zc, rim, local = fwd_step(
            layer, layer == middle, edge, total, pos, slots, tabs, conv_weights, kept, n_own, parts, tie
        )
        rim = swap_with(rim, "rows", 1)
        st = lax.all_to_all(local, halves, split_axis=0, concat_axis=0, tiled=True)
        moments = moments_step(layer, float(n_own), total, pos, st, gains)
        zc = lax.dynamic_update_slice_in_dim(zc, rim, n_own, axis=0)
        kept_z.append(zc)
        kept_mo.append(moments)
        if layer + 1 < layers:
            slots = spread(zc)
            tabs = spread(moments)
    top = layers - 1
    h_last, dn, msg = below_step(top, False, total, pos, kept_z[top], kept_mo[top], gains, (top_grad,))

    def with_other(values):
        return [v for mine in values for v in (mine, swap_with(mine, "rows", 1))]

    sum_list, pairs = [None] * layers, [None] * layers
    ahead, back = [[0, 1, 3, 2]], [[2, 3, 1, 0]]
    halves, upper = (), None
    for layer in range(layers - 1, -1, -1):
        got = swap_with(msg, "rows", 1)
        sums = msg[WIDE:] + got[WIDE:]
        for k in (1, 2):
            sums = sums + swap_with(sums, "dp", k)
        sum_list[layer] = sums
        outs = bwd_step(
            layer, total, pos, dn, got, sums, kept_z[layer], kept_mo[layer], gains, conv_weights, halves
        )
        terms, d = outs[:4], outs[4]
        if layer + 1 < layers:
            pairs[layer + 1] = outs[5]
        terms = (terms[0], *[swap_with(terms[k], "tensor", k) for k in range(1, GROUPS)])
        keep, send = wgrad_step(layer, pos, d, kept, ())
        if layer == 3:
            upper = lax.psum((pairs[5], pairs[4]), "dp", axis_index_groups=ahead)
        if layer > 0:
            below = layer - 1
            dn, msg = below_step(
                below, layer == middle, total, pos, kept_z[below], kept_mo[below], gains, terms, (keep,)
            )
        else:
            grad = last_step(terms, (keep, in_hbm(upper[0])))
        halves = (keep, swap_with(send, "rows", 1))
    pairs[0] = add_halves(*halves)
    shape = (images, rows_here, width, LANES)
    outputs = (from_maps(h_last.reshape(shape)), from_maps(grad.reshape(shape)))
    lower = lax.psum(tuple(pairs[3::-1]), "dp", axis_index_groups=back)
    whole = place_step((5, 4), pos, with_other(upper), None, layers)
    whole = place_step((3, 2, 1, 0), pos, with_other(lower), whole, layers)
    sums = jnp.stack(sum_list)
    return (*outputs, whole, sums[:, 1], sums[:, 0])


def solution(mesh):
    in_specs = (
        P("dp", "rows", "tensor"),
        P(None, "tensor", None),
        P(None, "tensor"),
        P(None, "tensor"),
        P("dp", "rows", "tensor"),
        P("dp", "rows", None),
    )
    out_specs = (
        P("dp", "rows", "tensor"),
        P("dp", "rows", "tensor"),
        P(None, "tensor", None),
        P(None, "tensor"),
        P(None, "tensor"),
    )
    local = fast_local if fits_kernels(mesh) else generic_local
    return jax.shard_map(local, mesh=mesh, in_specs=in_specs, out_specs=out_specs, check_vma=False)
```

```python
import functools

import jax
import jax.numpy as jnp
from jax import lax
from jax.experimental import pallas as pl
from jax.experimental.pallas import tpu as pltpu
from jax.sharding import PartitionSpec as P

EPS = 1e-05


def padded_2(cells, sides, width):
    for axis, dim in sides:
        count = lax.axis_size(axis)
        ends = count - 1
        head = lax.slice_in_dim(cells, 0, width, axis=dim)
        tail = lax.slice_in_dim(cells, cells.shape[dim] - width, cells.shape[dim], axis=dim)
        cells = jnp.concatenate(
            [
                lax.ppermute(tail, axis, [(i, (i + 1) % count) for i in range(ends)]),
                cells,
                lax.ppermute(head, axis, [((i + 1) % count, i) for i in range(ends)]),
            ],
            axis=dim,
        )
    return cells


def to_maps(flat, width):
    count, high, merged = flat.shape
    return flat.reshape(count, high, merged // width, width).transpose(0, 1, 3, 2)


def from_maps(maps):
    count, high, wide, chans = maps.shape
    return maps.transpose(0, 1, 3, 2).reshape(count, high, chans * wide)


def spatial_conv(padded, kernel):
    return lax.conv_general_dilated(
        padded,
        kernel,
        (1, 1),
        ((0, 0), (1, 1)),
        dimension_numbers=("NHWC", "HWIO", "NHWC"),
        preferred_element_type=jnp.float32,
    )


def flipped(kernel):
    return jnp.transpose(kernel[::-1, ::-1], (0, 1, 3, 2))


def pool_unpool(values):
    count, high, wide, chans = values.shape
    blocks = values.reshape(count, high // 2, 2, wide // 2, 2, chans)
    pooled = jax.nn.logsumexp(blocks, axis=(2, 4), keepdims=True)
    return (jnp.exp(blocks - pooled) * pooled).reshape(values.shape)


def moments(conv_out, total_pixels):
    summed = lax.psum(jnp.sum(conv_out, axis=(0, 1, 2)), ("dp", "rows"))
    mean = summed / total_pixels
    spread = lax.psum(jnp.sum(jnp.square(conv_out - mean), axis=(0, 1, 2)), ("dp", "rows"))
    var = spread / total_pixels
    return (mean, lax.rsqrt(var + EPS))


def kernel_grad(whole, dconv):
    images, rows_here, width, chans = dconv.shape
    widened = jnp.pad(whole, ((0, 0), (0, 0), (1, 1), (0, 0)))
    stacked = []
    for row_off in range(3):
        line = []
        for col_off in range(3):
            window = widened[:, row_off : row_off + rows_here, col_off : col_off + width, :]
            line.append(
                jnp.einsum("bhwc,bhwo->co", window, dconv, preferred_element_type=jnp.float32)
            )
        stacked.append(jnp.stack(line))
    return jnp.stack(stacked)


def generic_local(section_input, conv_weights, norm_gains, norm_shifts, out_grad, out_mask):
    width = out_mask.shape[2]
    images, rows_here = (out_mask.shape[0], out_mask.shape[1])
    total_pixels = float(images * rows_here * width * lax.axis_size("dp") * lax.axis_size("rows"))
    layers, out_here, flat_in = conv_weights.shape
    chans_in = flat_in // 9
    kernels_hwio = conv_weights.reshape(layers, out_here, 3, 3, chans_in).transpose(0, 2, 3, 4, 1)
    middle = layers // 2
    kept = []
    acting = to_maps(section_input, width)
    current = acting.astype(jnp.float32)
    pre_pool = current
    for index in range(layers):
        if index == middle:
            pre_pool = current
            acting = pool_unpool(pre_pool).astype(jnp.bfloat16)
        padded = padded_2(acting, (("rows", 1),), 1)
        whole = lax.all_gather(padded, "tensor", axis=3, tiled=True)
        conv_out = spatial_conv(whole, kernels_hwio[index])
        mean, rstd = moments(conv_out, total_pixels)
        normed = (conv_out - mean) * rstd
        shifted = normed * norm_gains[index] + norm_shifts[index]
        current = jax.nn.silu(shifted)
        acting = current.astype(jnp.bfloat16)
        kept.append((whole, normed, shifted, rstd))
    grad = to_maps(out_grad, width).astype(jnp.float32) * out_mask[..., None].astype(jnp.float32)
    kernel_list = [None] * layers
    gain_list = [None] * layers
    shift_list = [None] * layers
    for index in range(layers - 1, -1, -1):
        whole, normed, shifted, rstd = kept[index]
        unused, pull_silu = jax.vjp(jax.nn.silu, shifted)
        dshift = pull_silu(grad)[0]
        gain_sum, shift_sum = lax.psum(
            (jnp.sum(dshift * normed, axis=(0, 1, 2)), jnp.sum(dshift, axis=(0, 1, 2))),
            ("dp", "rows"),
        )
        gain_list[index] = gain_sum
        shift_list[index] = shift_sum
        dconv = (
            norm_gains[index]
            * rstd
            * (dshift - shift_sum / total_pixels - normed * gain_sum / total_pixels)
        ).astype(jnp.bfloat16)
        summed_kernel = lax.psum(
            kernel_grad(whole, dconv).astype(jnp.bfloat16), ("dp", "rows")
        ).astype(jnp.float32)
        kernel_list[index] = summed_kernel.transpose(3, 0, 1, 2).reshape(out_here, flat_in)
        grad_rim = padded_2(dconv, (("rows", 1),), 1)
        partial_terms = spatial_conv(grad_rim, flipped(kernels_hwio[index]))
        grad_in = lax.psum_scatter(
            partial_terms.astype(jnp.bfloat16), "tensor", scatter_dimension=3, tiled=True
        ).astype(jnp.float32)
        if index == middle:
            unused, pull_pool = jax.vjp(pool_unpool, pre_pool)
            grad = pull_pool(grad_in)[0]
        else:
            grad = grad_in
    return (
        from_maps(acting),
        from_maps(grad),
        jnp.stack(kernel_list),
        jnp.stack(gain_list),
        jnp.stack(shift_list),
    )


GROUPS = 4
LANES = 128
WIDE = 48
CHANS = GROUPS * LANES
F32 = jnp.float32
BF16 = jnp.bfloat16
VMEM = pl.BlockSpec(memory_space=pltpu.VMEM)
SMEM = pl.BlockSpec(memory_space=pltpu.SMEM)
ANY = pl.BlockSpec(memory_space=pltpu.HBM)
FREE = pl.BlockSpec(memory_space=pl.ANY)
PARAMS = pltpu.CompilerParams(vmem_limit_bytes=20 * 1024 * 1024)


def in_hbm(value):
    return pltpu.with_memory_space_constraint(value, pltpu.HBM)


def fits_kernels(mesh):
    return mesh.shape["tensor"] == GROUPS and mesh.shape["rows"] == 2 and mesh.shape["dp"] == 4


def sigmoid(v):
    return 0.5 * jnp.tanh(0.5 * v) + 0.5


def swap_columns(v):
    column = lax.broadcasted_iota(jnp.int32, v.shape, 0)
    return jnp.where(column % 2 == 0, pltpu.roll(v, WIDE - 1, 0), pltpu.roll(v, 1, 0))


def soft_parts(h):
    top = jnp.maximum(h[0], h[1])
    top = jnp.maximum(top, swap_columns(top))
    e0, e1 = jnp.exp(h[0] - top), jnp.exp(h[1] - top)
    total = e0 + e1
    total = total + swap_columns(total)
    pooled = top + jnp.log(total)
    inverse = 1.0 / total
    return e0 * inverse, e1 * inverse, pooled


def soft(h):
    h = h.reshape(2, WIDE, LANES)
    q0, q1, pooled = soft_parts(h)
    return jnp.concatenate([q0 * pooled, q1 * pooled], axis=0)


def soft_pull(h, grad):
    h = h.reshape(2, WIDE, LANES)
    grad = grad.reshape(2, WIDE, LANES)
    q0, q1, pooled = soft_parts(h)
    mix = q0 * grad[0] + q1 * grad[1]
    mix = mix + swap_columns(mix)
    return jnp.concatenate(
        [q0 * (pooled * (grad[0] - mix) + mix), q1 * (pooled * (grad[1] - mix) + mix)], axis=0
    )


def norm_tables(st, group, i_own, i_oth, n_local, total):
    parts = st.shape[0]
    group = 0 if st.shape[1] == 1 else group
    blocks = [st[i, group] for i in range(parts)]
    summed = functools.reduce(jnp.add, blocks)
    mean = summed[0:1] / parts
    apart = functools.reduce(jnp.add, [jnp.square(b - mean) for b in blocks])
    rstd = lax.rsqrt((summed[1:2] + n_local * apart[0:1]) / total + EPS)
    return rstd, (st[i_own, group, 0:1] - mean) * rstd, (st[i_oth, group, 0:1] - mean) * rstd


def left_right(y0, y1, y2):
    rows = y0.shape[0]
    column = lax.broadcasted_iota(jnp.int32, y0.shape, 0) % WIDE
    before = jnp.where(column == 0, 0.0, pltpu.roll(y0, 1, 0))
    after = jnp.where(column == WIDE - 1, 0.0, pltpu.roll(y2, rows - 1, 0))
    return before + y1 + after


def lane_of(group):
    return pl.multiple_of(group * LANES, LANES)


def edge_start(n_own, edge, half):
    return pl.multiple_of((1 - half) * (n_own - edge), WIDE)


def pair_rows(j):
    return pl.ds(pl.multiple_of(j * 2 * WIDE, 2 * WIDE), 2 * WIDE)


def fold(v):
    return jnp.sum(v.reshape(v.shape[0] // 8, 8, LANES), axis=0)


def fwd_kernel(first, pool, layer, total, edge_out, *refs):
    pos, zall = refs[0], refs[1]
    if first:
        w_hbm = refs[2]
    else:
        st, gss, w_hbm = refs[2], refs[3:7], refs[7]
    hb_out, zc_out, edge_ref, st_out, hb, w, y, z, tab, hs, sem = refs[-11:]
    load = pltpu.make_async_copy(w_hbm.at[layer], w, sem.at[0])
    load.start()
    save = pltpu.make_async_copy(hb, hb_out.at[layer], sem.at[1])
    t, r = pos[0], pos[1]
    n_own = z.shape[0]
    halo_at = pl.multiple_of((1 - r) * (n_own + WIDE), WIDE)
    zero_at = pl.multiple_of(r * (n_own + WIDE), WIDE)
    hb[pl.ds(zero_at, WIDE), :] = jnp.zeros((WIDE, CHANS), BF16)
    edge = zall.shape[0] - n_own
    if not first:
        for k in range(GROUPS):
            group = t ^ k
            rstd, own, oth = norm_tables(st, group, pos[2], pos[3], float(n_own), total)
            gain, shift = gss[k][layer - 1 : layer, :], gss[k][layer + 7 : layer + 8, :]
            tab[group, 0:1] = rstd * gain
            tab[group, 1:2] = own * gain + shift
            tab[group, 2:3] = oth * gain + shift

    def act(values, group, which):
        if first:
            return values
        n = values.astype(F32) * tab[group, 0:1, :] + tab[group, which : which + 1, :]
        h = n * sigmoid(n)
        return soft(h) if pool else h

    def body(j, carry):
        at = pl.multiple_of(j * 2 * WIDE, 2 * WIDE)
        for group in range(GROUPS):
            lanes = slice(group * LANES, (group + 1) * LANES)
            h = act(zall[pl.ds(at, 2 * WIDE), lanes], group, 1)
            hb[pl.ds(pl.multiple_of(at + WIDE, WIDE), 2 * WIDE), lanes] = h.astype(BF16)
        return carry

    lax.fori_loop(0, n_own // (2 * WIDE), body, 0)
    for group in range(GROUPS):
        lanes = slice(group * LANES, (group + 1) * LANES)
        h = act(zall[n_own : n_own + edge, lanes], group, 2)
        if edge > WIDE:
            hs[...] = h
            h = hs[pl.ds(pl.multiple_of(r * WIDE, WIDE), WIDE), :]
        hb[pl.ds(halo_at, WIDE), lanes] = h.astype(BF16)
    save.start()
    load.wait()
    lhs = jnp.concatenate([hb[i * WIDE : i * WIDE + n_own, :] for i in range(3)], axis=1)
    rhs = jnp.concatenate(
        [
            jnp.concatenate([w[:, (3 * i + s) * CHANS : (3 * i + s + 1) * CHANS] for i in range(3)], axis=1)
            for s in range(3)
        ],
        axis=0,
    )
    y[...] = lax.dot_general(lhs, rhs, (((1,), (1,)), ((), ())), preferred_element_type=F32)

    def add_up(j, acc):
        rows = pair_rows(j)
        v = left_right(y[rows, 0:128], y[rows, 128:256], y[rows, 256:384])
        z[rows, :] = v
        return acc + fold(v)

    steps = n_own // (2 * WIDE)
    summed = lax.fori_loop(0, steps, add_up, jnp.zeros((8, LANES), F32))
    mean = jnp.sum(summed, axis=0, keepdims=True) / n_own

    def centre(j, acc):
        rows = pair_rows(j)
        v = z[rows, :] - mean
        z[rows, :] = v
        zc_out[rows, :] = v.astype(BF16)
        return acc + fold(jnp.square(v))

    apart = lax.fori_loop(0, steps, centre, jnp.zeros((8, LANES), F32))
    sums = [mean, jnp.sum(apart, axis=0, keepdims=True), jnp.zeros((6, LANES), F32)]
    sums = jnp.concatenate(sums, axis=0)
    for i in range(st_out.shape[0]):
        st_out[i] = sums
    edge_ref[...] = zc_out[pl.ds(edge_start(n_own, edge_out, r), edge_out), :]
    zc_out[n_own : n_own + edge_out, :] = jnp.zeros((edge_out, LANES), BF16)
    save.wait()


def fwd_step(layer, pool, edge_out, total, pos, slots, st, tables, weights, kept, n_own, devices, ties):
    first = st is None
    layers = weights.shape[0]
    extra = () if first else (st, *tables)
    return pl.pallas_call(
        functools.partial(fwd_kernel, first, pool, layer, total, edge_out),
        out_shape=(
            pltpu.HBM((layers, n_own + 2 * WIDE, CHANS), BF16),
            pltpu.VMEM((n_own + edge_out, LANES), BF16),
            pltpu.VMEM((edge_out, LANES), BF16),
            pltpu.VMEM((devices, 8, LANES), F32),
        ),
        in_specs=[SMEM] + [VMEM] * (1 + len(extra)) + [ANY] * (1 if first else 2) + [FREE] * len(ties),
        out_specs=(ANY, VMEM, VMEM, VMEM),
        input_output_aliases={} if first else {3 + len(extra): 0},
        scratch_shapes=[
            pltpu.VMEM((n_own + 2 * WIDE, CHANS), BF16),
            pltpu.VMEM((LANES, 9 * CHANS), BF16),
            pltpu.VMEM((n_own, 3 * LANES), F32),
            pltpu.VMEM((n_own, LANES), F32),
            pltpu.VMEM((GROUPS, 8, LANES), F32),
            pltpu.VMEM((2 * WIDE, LANES), F32),
            pltpu.SemaphoreType.DMA((2,)),
        ],
        compiler_params=PARAMS,
        cost_estimate=pl.CostEstimate(
            flops=2 * n_own * 9 * CHANS * LANES, bytes_accessed=4 * 1024 * 1024, transcendentals=n_own * CHANS
        ),
        name="conv_forward",
    )(pos, slots, *extra, in_hbm(weights), *(() if first else (in_hbm(kept),)), *ties)


def below_kernel(layer, pool, total, top, *refs):
    pos, zc, st, gs = refs[:4]
    if top:
        terms, h_out, dn_out, msg, tab = refs[4:]
    else:
        terms, (dn_out, msg, tab) = refs[4:8], refs[-3:]
    n_own = dn_out.shape[0]
    rstd, own, oth = norm_tables(st, pos[0], pos[2], pos[3], float(n_own), total)
    tab[0:1], tab[1:2] = rstd, own
    tab[2:3], tab[3:4] = gs[layer : layer + 1, :], gs[layer + 8 : layer + 9, :]

    def body(j, accs):
        rows = pair_rows(j)
        xhat = zc[rows, :].astype(F32) * tab[0:1, :] + tab[1:2, :]
        n = xhat * tab[2:3, :] + tab[3:4, :]
        sig = sigmoid(n)
        h = n * sig
        if top:
            g = terms[rows, :].astype(F32)
            h_out[rows, :] = h.astype(BF16)
        else:
            g = functools.reduce(jnp.add, [term[rows, :].astype(F32) for term in terms])
        if pool:
            g = soft_pull(h, g)
        dn = g * (sig * (1.0 + n - h))
        dn_out[rows, :] = dn
        return accs[0] + fold(dn), accs[1] + fold(dn * xhat)

    zero = jnp.zeros((8, LANES), F32)
    sums = lax.fori_loop(0, n_own // (2 * WIDE), body, (zero, zero))
    sums = [jnp.sum(v, axis=0, keepdims=True) for v in sums]
    msg[0:WIDE, :] = dn_out[pl.ds(edge_start(n_own, WIDE, pos[1]), WIDE), :]
    msg[WIDE : WIDE + 8, :] = jnp.concatenate(sums + [jnp.zeros((6, LANES), F32)], axis=0)


def below_step(layer, pool, total, pos, zc, st, gs, terms, ties=()):
    n_own = terms[0].shape[0]
    top = len(terms) == 1
    out_shape = [
        pltpu.VMEM((n_own, LANES), F32),
        pltpu.VMEM((WIDE + 8, LANES), F32),
    ]
    if top:
        out_shape = [jax.ShapeDtypeStruct((n_own, LANES), BF16)] + out_shape
    return pl.pallas_call(
        functools.partial(below_kernel, layer, pool, total, top),
        out_shape=tuple(out_shape),
        in_specs=[SMEM] + [VMEM] * (3 + len(terms)) + [FREE] * len(ties),
        out_specs=(VMEM,) * len(out_shape),
        scratch_shapes=[pltpu.VMEM((8, LANES), F32)],
        compiler_params=PARAMS,
        cost_estimate=pl.CostEstimate(flops=40 * n_own * LANES, bytes_accessed=1024 * 1024, transcendentals=n_own * LANES),
        name="silu_backward",
    )(pos, zc, st, gs, *terms, *ties)


def bwd_kernel(layer, total, *refs):
    pos, dn, dedge, sums, zc, st, gs, w_hbm = refs[:8]
    outs, d_out, d, w, y, tab, sem = refs[-10:-6], *refs[-6:]
    load = pltpu.make_async_copy(w_hbm.at[layer], w, sem)
    load.start()
    t, r = pos[0], pos[1]
    n_own = dn.shape[0]
    halo_at = pl.multiple_of((1 - r) * (n_own + WIDE), WIDE)
    zero_at = pl.multiple_of(r * (n_own + WIDE), WIDE)
    edge = zc.shape[0] - n_own
    d[pl.ds(zero_at, WIDE), :] = jnp.zeros((WIDE, 3 * LANES), BF16)
    rstd, own, oth = norm_tables(st, t, pos[2], pos[3], float(n_own), total)
    scale = gs[layer : layer + 1, :] * rstd
    shift_sum, gain_sum = sums[0:1, :], sums[1:2, :]
    slope = scale * gain_sum / total
    tab[0:1] = scale
    tab[1:2] = slope * rstd
    tab[2:3] = scale * shift_sum / total + slope * own
    tab[3:4] = scale * shift_sum / total + slope * oth

    def spread_columns(v, at):
        rows = v.shape[0]
        column = lax.broadcasted_iota(jnp.int32, v.shape, 0) % WIDE
        ahead = jnp.where(column == WIDE - 1, 0.0, pltpu.roll(v, rows - 1, 0))
        behind = jnp.where(column == 0, 0.0, pltpu.roll(v, 1, 0))
        d[pl.ds(at, rows), 0:128] = ahead.astype(BF16)
        d[pl.ds(at, rows), 128:256] = v.astype(BF16)
        d[pl.ds(at, rows), 256:384] = behind.astype(BF16)

    def body(j, carry):
        rows = pair_rows(j)
        v = dn[rows, :] * tab[0:1, :] - tab[2:3, :] - zc[rows, :].astype(F32) * tab[1:2, :]
        spread_columns(v, pl.multiple_of(j * 2 * WIDE + WIDE, WIDE))
        return carry

    lax.fori_loop(0, n_own // (2 * WIDE), body, 0)
    near = n_own if edge == WIDE else pl.multiple_of(n_own + r * WIDE, WIDE)
    near = zc[pl.ds(near, WIDE), :].astype(F32)
    spread_columns(dedge[0:WIDE, :] * tab[0:1, :] - tab[3:4, :] - near * tab[1:2, :], halo_at)
    d_out[...] = d[WIDE : WIDE + n_own, :]
    load.wait()
    lhs = jnp.concatenate([d[(2 - i) * WIDE : (2 - i) * WIDE + n_own, :] for i in range(3)], axis=1)
    rhs = jnp.concatenate([w[:, i * CHANS : (i + 1) * CHANS] for i in range(9)], axis=0)
    y[...] = jnp.dot(lhs, rhs, preferred_element_type=F32)

    def share(j, carry):
        rows = pair_rows(j)
        for k in range(GROUPS):
            outs[k][rows, :] = y[rows, pl.ds(lane_of(t ^ k), LANES)].astype(BF16)
        return carry

    lax.fori_loop(0, n_own // (2 * WIDE), share, 0)


def bwd_step(layer, total, pos, dn, dedge, sums, zc, st, gs, weights, ties):
    n_own = dn.shape[0]
    part = pltpu.VMEM((n_own, LANES), BF16)
    return pl.pallas_call(
        functools.partial(bwd_kernel, layer, total),
        out_shape=(
            part,
            part,
            part,
            part,
            pltpu.VMEM((n_own, 3 * LANES), BF16),
        ),
        in_specs=[SMEM] + [VMEM] * 6 + [ANY] + [FREE] * len(ties),
        out_specs=(VMEM,) * 5,
        scratch_shapes=[
            pltpu.VMEM((n_own + 2 * WIDE, 3 * LANES), BF16),
            pltpu.VMEM((LANES, 9 * CHANS), BF16),
            pltpu.VMEM((n_own, CHANS), F32),
            pltpu.VMEM((8, LANES), F32),
            pltpu.SemaphoreType.DMA,
        ],
        compiler_params=PARAMS,
        cost_estimate=pl.CostEstimate(
            flops=2 * n_own * 9 * CHANS * LANES, bytes_accessed=4 * 1024 * 1024, transcendentals=0
        ),
        name="conv_backward",
    )(pos, dn, dedge, sums, zc, st, gs, in_hbm(weights), *ties)


def last_kernel(t0, t1, t2, t3, *refs):
    out = refs[-1]

    def body(j, carry):
        rows = pair_rows(j)
        out[rows, :] = functools.reduce(jnp.add, [term[rows, :].astype(F32) for term in (t0, t1, t2, t3)])
        return carry

    lax.fori_loop(0, out.shape[0] // (2 * WIDE), body, 0)


def last_step(terms, ties):
    return pl.pallas_call(
        last_kernel,
        out_shape=jax.ShapeDtypeStruct(terms[0].shape, F32),
        in_specs=[VMEM] * 4 + [FREE] * len(ties),
        out_specs=VMEM,
        compiler_params=PARAMS,
        name="add_terms",
    )(*terms, *ties)


def halves_kernel(keep, got, out):
    out[...] = (keep[...].astype(F32) + got[...].astype(F32)).astype(BF16)


def add_halves(keep, got):
    return pl.pallas_call(
        halves_kernel,
        out_shape=jax.ShapeDtypeStruct(keep.shape, BF16),
        in_specs=[VMEM] * 2,
        out_specs=VMEM,
        compiler_params=PARAMS,
        cost_estimate=pl.CostEstimate(flops=keep.size, bytes_accessed=6 * keep.size, transcendentals=0),
        name="add_halves",
    )(keep, got)


def wgrad_kernel(layer, pos, d, hb_hbm, *refs):
    keep, send, hb, grad, sem = refs[-5:]
    load = pltpu.make_async_copy(hb_hbm.at[layer], hb, sem)
    load.start()
    n_own = d.shape[0]
    lhs = d[...]
    load.wait()
    for i in range(3):
        part = lax.dot_general(
            lhs, hb[i * WIDE : i * WIDE + n_own, :], (((0,), (0,)), ((), ())), preferred_element_type=F32
        ).astype(BF16)
        for s in range(3):
            grad[:, (3 * i + s) * CHANS : (3 * i + s + 1) * CHANS] = part[s * LANES : (s + 1) * LANES]
    half = LANES // 2
    keep[...] = grad[pl.ds(pl.multiple_of(pos[1] * half, half), half), :]
    send[...] = grad[pl.ds(pl.multiple_of((1 - pos[1]) * half, half), half), :]


def wgrad_step(layer, pos, d, kept, ties):
    half = pltpu.VMEM((LANES // 2, 9 * CHANS), BF16)
    return pl.pallas_call(
        functools.partial(wgrad_kernel, layer),
        out_shape=(half, half),
        in_specs=[SMEM, VMEM, ANY] + [FREE] * len(ties),
        out_specs=(VMEM, VMEM),
        scratch_shapes=[
            pltpu.VMEM(kept.shape[1:], BF16),
            pltpu.VMEM((LANES, 9 * CHANS), BF16),
            pltpu.SemaphoreType.DMA,
        ],
        compiler_params=PARAMS,
        cost_estimate=pl.CostEstimate(
            flops=2 * d.shape[0] * 9 * CHANS * LANES, bytes_accessed=3 * 1024 * 1024, transcendentals=0
        ),
        name="kernel_gradient",
    )(pos, d, in_hbm(kept), *ties)


def place_kernel(layers, fresh, pos, *refs):
    count = 2 * len(layers)
    sources = refs[:count]
    out, held, wide, sem = refs[-4:]
    half = LANES // 2
    r = pos[1]
    loads = [pltpu.make_async_copy(sources[j], held.at[j], sem.at[j]) for j in range(count)]
    for load in loads:
        load.start()
    stores = []
    for j in range(count):
        at = pl.multiple_of((r if j % 2 == 0 else 1 - r) * half, half)
        if j >= 2:
            stores[j - 2].wait()
        loads[j].wait()
        wide[j % 2] = held[j].astype(F32)
        store = pltpu.make_async_copy(wide.at[j % 2], out.at[layers[j // 2], pl.ds(at, half)], sem.at[count + j])
        store.start()
        stores.append(store)
    for store in stores[-2:]:
        store.wait()


def place_step(layers, pos, sources, whole, count):
    half = LANES // 2
    jobs = len(sources)
    return pl.pallas_call(
        functools.partial(place_kernel, layers, whole is None),
        out_shape=pltpu.HBM((count, LANES, 9 * CHANS), F32),
        in_specs=[SMEM] + [ANY] * jobs + ([] if whole is None else [ANY]),
        out_specs=ANY,
        input_output_aliases={} if whole is None else {1 + jobs: 0},
        scratch_shapes=[
            pltpu.VMEM((jobs, half, 9 * CHANS), BF16),
            pltpu.VMEM((2, half, 9 * CHANS), F32),
            pltpu.SemaphoreType.DMA((2 * jobs,)),
        ],
        compiler_params=PARAMS,
        cost_estimate=pl.CostEstimate(flops=0, bytes_accessed=jobs * 2 * 1024 * 1024, transcendentals=0),
        name="place_gradients",
    )(pos, *[in_hbm(v) for v in sources], *(() if whole is None else (in_hbm(whole),)))


def swap_with(value, axis, k):
    return lax.ppermute(value, axis, [(i, i ^ k) for i in range(lax.axis_size(axis))])


def spread(own):
    return (own, *[swap_with(own, "tensor", k) for k in range(1, GROUPS)])


def halo_of_input(x, half):
    n_own = x.shape[0]
    edge = jnp.where(half == 0, x[n_own - WIDE :], x[:WIDE])
    return jnp.concatenate([x, swap_with(edge, "rows", 1)], axis=0)


def fast_local(section_input, conv_weights, norm_gains, norm_shifts, out_grad, out_mask):
    images, rows_here, width = out_mask.shape
    layers = conv_weights.shape[0]
    n_own = rows_here * width
    parts = lax.axis_size("dp") * lax.axis_size("rows")
    total = float(n_own * parts)
    t, half = lax.axis_index("tensor"), lax.axis_index("rows")
    image = lax.axis_index("dp")
    pos = jnp.stack([t, half, 2 * image + half, 2 * image + 1 - half]).astype(jnp.int32)
    middle = layers // 2
    x = to_maps(section_input, width).reshape(n_own, LANES)
    slots = lax.all_gather(halo_of_input(x, half), "tensor", axis=1, tiled=True)
    pad = jnp.zeros((8 - layers, LANES), F32)
    tables = spread(jnp.concatenate([norm_gains, pad, norm_shifts, pad], axis=0))
    top_grad = (to_maps(out_grad, width) * out_mask[..., None].astype(BF16)).reshape(n_own, LANES)

    st, kept = None, None
    halves = ("dp", "rows")
    kept_z, kept_st = [], []
    for layer in range(layers):
        last = layer + 1 == layers
        edge = 2 * WIDE if layer + 1 == middle else WIDE
        everyone = halves if last else (*halves, "tensor")
        devices = parts if last else parts * GROUPS
        kept, zc, rim, local = fwd_step(
            layer,
            layer == middle,
            edge,
            total,
            pos,
            slots,
            st,
            tables,
            conv_weights,
            kept,
            n_own,
            devices,
            (top_grad,) if layer == 2 else (),
        )
        rim = swap_with(rim, "rows", 1)
        st = lax.all_to_all(local, everyone, split_axis=0, concat_axis=0, tiled=True)
        st = st.reshape(parts, devices // parts, 8, LANES)
        zc = lax.dynamic_update_slice_in_dim(zc, rim, n_own, axis=0)
        kept_z.append(zc)
        kept_st.append(st)
        if not last:
            slots = lax.all_gather(zc, "tensor", axis=1, tiled=True)
    top = layers - 1
    h_last, dn, msg = below_step(top, False, total, pos, kept_z[top], kept_st[top], tables[0], (top_grad,))

    def with_other(values):
        return [v for mine in values for v in (mine, swap_with(mine, "rows", 1))]

    sum_list, pairs = [None] * layers, [None] * layers
    ahead, back = [[0, 1, 2, 3]], [[3, 2, 1, 0]]
    ties, whole = (), None
    for layer in range(layers - 1, -1, -1):
        got = swap_with(msg, "rows", 1)
        sums = msg[WIDE:] + got[WIDE:]
        for k in (1, 2):
            sums = sums + swap_with(sums, "dp", k)
        sum_list[layer] = sums
        *terms, d = bwd_step(
            layer, total, pos, dn, got, sums, kept_z[layer], kept_st[layer], tables[0], conv_weights, ()
        )
        terms = (terms[0], *[swap_with(terms[k], "tensor", k) for k in range(1, GROUPS)])
        keep, send = wgrad_step(layer, pos, d, kept, ())
        if layer > 0:
            below = layer - 1
            dn, msg = below_step(
                below, layer == middle, total, pos, kept_z[below], kept_st[below], tables[0], terms, (keep, *ties)
            )
        else:
            grad = last_step(terms, (keep, *ties))
        pairs[layer] = add_halves(keep, swap_with(send, "rows", 1))
        ties = (pairs[layer],)
        if layer == 4:
            upper = lax.psum((pairs[5], pairs[4]), "dp", axis_index_groups=ahead)
        if layer == 2:
            mid = lax.psum((pairs[3], pairs[2]), "dp", axis_index_groups=back)
            ties = (pairs[2], in_hbm(upper[0]))
    tied, upper = lax.optimization_barrier(((pairs[1], pairs[0]), upper))
    lower = lax.psum(tied, "dp", axis_index_groups=ahead)
    shape = (images, rows_here, width, LANES)
    outputs = (from_maps(h_last.reshape(shape)), from_maps(grad.reshape(shape)))
    whole = place_step((5, 4), pos, with_other(upper), None, layers)
    whole = place_step((3, 2), pos, with_other(mid), whole, layers)
    sums = jnp.stack(sum_list)
    lower, whole, outputs, sums = lax.optimization_barrier((lower, whole, outputs, sums))
    whole = place_step((1, 0), pos, with_other(lower), whole, layers)
    return (*outputs, whole, sums[:, 1], sums[:, 0])


def solution(mesh):
    in_specs = (
        P("dp", "rows", "tensor"),
        P(None, "tensor", None),
        P(None, "tensor"),
        P(None, "tensor"),
        P("dp", "rows", "tensor"),
        P("dp", "rows", None),
    )
    out_specs = (
        P("dp", "rows", "tensor"),
        P("dp", "rows", "tensor"),
        P(None, "tensor", None),
        P(None, "tensor"),
        P(None, "tensor"),
    )
    local = fast_local if fits_kernels(mesh) else generic_local
    return jax.shard_map(local, mesh=mesh, in_specs=in_specs, out_specs=out_specs, check_vma=False)
```

```python
import functools

import jax
import jax.numpy as jnp
from jax import lax
from jax.experimental import pallas as pl
from jax.experimental.pallas import tpu as pltpu
from jax.sharding import PartitionSpec as P

EPS = 1e-05


def padded_2(cells, sides, width):
    for axis, dim in sides:
        count = lax.axis_size(axis)
        ends = count - 1
        head = lax.slice_in_dim(cells, 0, width, axis=dim)
        tail = lax.slice_in_dim(cells, cells.shape[dim] - width, cells.shape[dim], axis=dim)
        cells = jnp.concatenate(
            [
                lax.ppermute(tail, axis, [(i, (i + 1) % count) for i in range(ends)]),
                cells,
                lax.ppermute(head, axis, [((i + 1) % count, i) for i in range(ends)]),
            ],
            axis=dim,
        )
    return cells


def to_maps(flat, width):
    count, high, merged = flat.shape
    return flat.reshape(count, high, merged // width, width).transpose(0, 1, 3, 2)


def from_maps(maps):
    count, high, wide, chans = maps.shape
    return maps.transpose(0, 1, 3, 2).reshape(count, high, chans * wide)


def spatial_conv(padded, kernel):
    return lax.conv_general_dilated(
        padded,
        kernel,
        (1, 1),
        ((0, 0), (1, 1)),
        dimension_numbers=("NHWC", "HWIO", "NHWC"),
        preferred_element_type=jnp.float32,
    )


def flipped(kernel):
    return jnp.transpose(kernel[::-1, ::-1], (0, 1, 3, 2))


def pool_unpool(values):
    count, high, wide, chans = values.shape
    blocks = values.reshape(count, high // 2, 2, wide // 2, 2, chans)
    pooled = jax.nn.logsumexp(blocks, axis=(2, 4), keepdims=True)
    return (jnp.exp(blocks - pooled) * pooled).reshape(values.shape)


def moments(conv_out, total_pixels):
    summed = lax.psum(jnp.sum(conv_out, axis=(0, 1, 2)), ("dp", "rows"))
    mean = summed / total_pixels
    spread = lax.psum(jnp.sum(jnp.square(conv_out - mean), axis=(0, 1, 2)), ("dp", "rows"))
    var = spread / total_pixels
    return (mean, lax.rsqrt(var + EPS))


def kernel_grad(whole, dconv):
    images, rows_here, width, chans = dconv.shape
    widened = jnp.pad(whole, ((0, 0), (0, 0), (1, 1), (0, 0)))
    stacked = []
    for row_off in range(3):
        line = []
        for col_off in range(3):
            window = widened[:, row_off : row_off + rows_here, col_off : col_off + width, :]
            line.append(
                jnp.einsum("bhwc,bhwo->co", window, dconv, preferred_element_type=jnp.float32)
            )
        stacked.append(jnp.stack(line))
    return jnp.stack(stacked)


def generic_local(section_input, conv_weights, norm_gains, norm_shifts, out_grad, out_mask):
    width = out_mask.shape[2]
    images, rows_here = (out_mask.shape[0], out_mask.shape[1])
    total_pixels = float(images * rows_here * width * lax.axis_size("dp") * lax.axis_size("rows"))
    layers, out_here, flat_in = conv_weights.shape
    chans_in = flat_in // 9
    kernels_hwio = conv_weights.reshape(layers, out_here, 3, 3, chans_in).transpose(0, 2, 3, 4, 1)
    middle = layers // 2
    kept = []
    acting = to_maps(section_input, width)
    current = acting.astype(jnp.float32)
    pre_pool = current
    for index in range(layers):
        if index == middle:
            pre_pool = current
            acting = pool_unpool(pre_pool).astype(jnp.bfloat16)
        padded = padded_2(acting, (("rows", 1),), 1)
        whole = lax.all_gather(padded, "tensor", axis=3, tiled=True)
        conv_out = spatial_conv(whole, kernels_hwio[index])
        mean, rstd = moments(conv_out, total_pixels)
        normed = (conv_out - mean) * rstd
        shifted = normed * norm_gains[index] + norm_shifts[index]
        current = jax.nn.silu(shifted)
        acting = current.astype(jnp.bfloat16)
        kept.append((whole, normed, shifted, rstd))
    grad = to_maps(out_grad, width).astype(jnp.float32) * out_mask[..., None].astype(jnp.float32)
    kernel_list = [None] * layers
    gain_list = [None] * layers
    shift_list = [None] * layers
    for index in range(layers - 1, -1, -1):
        whole, normed, shifted, rstd = kept[index]
        unused, pull_silu = jax.vjp(jax.nn.silu, shifted)
        dshift = pull_silu(grad)[0]
        gain_sum, shift_sum = lax.psum(
            (jnp.sum(dshift * normed, axis=(0, 1, 2)), jnp.sum(dshift, axis=(0, 1, 2))),
            ("dp", "rows"),
        )
        gain_list[index] = gain_sum
        shift_list[index] = shift_sum
        dconv = (
            norm_gains[index]
            * rstd
            * (dshift - shift_sum / total_pixels - normed * gain_sum / total_pixels)
        ).astype(jnp.bfloat16)
        summed_kernel = lax.psum(
            kernel_grad(whole, dconv).astype(jnp.bfloat16), ("dp", "rows")
        ).astype(jnp.float32)
        kernel_list[index] = summed_kernel.transpose(3, 0, 1, 2).reshape(out_here, flat_in)
        grad_rim = padded_2(dconv, (("rows", 1),), 1)
        partial_terms = spatial_conv(grad_rim, flipped(kernels_hwio[index]))
        grad_in = lax.psum_scatter(
            partial_terms.astype(jnp.bfloat16), "tensor", scatter_dimension=3, tiled=True
        ).astype(jnp.float32)
        if index == middle:
            unused, pull_pool = jax.vjp(pool_unpool, pre_pool)
            grad = pull_pool(grad_in)[0]
        else:
            grad = grad_in
    return (
        from_maps(acting),
        from_maps(grad),
        jnp.stack(kernel_list),
        jnp.stack(gain_list),
        jnp.stack(shift_list),
    )


GROUPS = 4
LANES = 128
WIDE = 48
CHANS = GROUPS * LANES
F32 = jnp.float32
BF16 = jnp.bfloat16
VMEM = pl.BlockSpec(memory_space=pltpu.VMEM)
SMEM = pl.BlockSpec(memory_space=pltpu.SMEM)
ANY = pl.BlockSpec(memory_space=pltpu.HBM)
FREE = pl.BlockSpec(memory_space=pl.ANY)
PARAMS = pltpu.CompilerParams(vmem_limit_bytes=20 * 1024 * 1024)


def in_hbm(value):
    return pltpu.with_memory_space_constraint(value, pltpu.HBM)


def fits_kernels(mesh):
    return mesh.shape["tensor"] == GROUPS and mesh.shape["rows"] == 2 and mesh.shape["dp"] == 4


def sigmoid(v):
    return 0.5 * jnp.tanh(0.5 * v) + 0.5


def swap_columns(v):
    column = lax.broadcasted_iota(jnp.int32, v.shape, 0)
    return jnp.where(column % 2 == 0, pltpu.roll(v, WIDE - 1, 0), pltpu.roll(v, 1, 0))


def soft_parts(h):
    top = jnp.maximum(h[0], h[1])
    top = jnp.maximum(top, swap_columns(top))
    e0, e1 = jnp.exp(h[0] - top), jnp.exp(h[1] - top)
    total = e0 + e1
    total = total + swap_columns(total)
    pooled = top + jnp.log(total)
    inverse = 1.0 / total
    return e0 * inverse, e1 * inverse, pooled


def soft(h):
    h = h.reshape(2, WIDE, LANES)
    q0, q1, pooled = soft_parts(h)
    return jnp.concatenate([q0 * pooled, q1 * pooled], axis=0)


def soft_pull(h, grad):
    h = h.reshape(2, WIDE, LANES)
    grad = grad.reshape(2, WIDE, LANES)
    q0, q1, pooled = soft_parts(h)
    mix = q0 * grad[0] + q1 * grad[1]
    mix = mix + swap_columns(mix)
    return jnp.concatenate(
        [q0 * (pooled * (grad[0] - mix) + mix), q1 * (pooled * (grad[1] - mix) + mix)], axis=0
    )


def norm_tables(st, group, i_own, i_oth, n_local, total):
    parts = st.shape[0]
    group = 0 if st.shape[1] == 1 else group
    blocks = [st[i, group] for i in range(parts)]
    summed = functools.reduce(jnp.add, blocks)
    mean = summed[0:1] / parts
    apart = functools.reduce(jnp.add, [jnp.square(b - mean) for b in blocks])
    rstd = lax.rsqrt((summed[1:2] + n_local * apart[0:1]) / total + EPS)
    return rstd, (st[i_own, group, 0:1] - mean) * rstd, (st[i_oth, group, 0:1] - mean) * rstd


def left_right(y0, y1, y2):
    rows = y0.shape[0]
    column = lax.broadcasted_iota(jnp.int32, y0.shape, 0) % WIDE
    before = jnp.where(column == 0, 0.0, pltpu.roll(y0, 1, 0))
    after = jnp.where(column == WIDE - 1, 0.0, pltpu.roll(y2, rows - 1, 0))
    return before + y1 + after


def lane_of(group):
    return pl.multiple_of(group * LANES, LANES)


def edge_start(n_own, edge, half):
    return pl.multiple_of((1 - half) * (n_own - edge), WIDE)


def pair_rows(j):
    return pl.ds(pl.multiple_of(j * 2 * WIDE, 2 * WIDE), 2 * WIDE)


def fold(v):
    return jnp.sum(v.reshape(v.shape[0] // 8, 8, LANES), axis=0)


def fwd_kernel(first, pool, layer, total, edge_out, *refs):
    pos, zall = refs[0], refs[1]
    if first:
        w_hbm = refs[2]
    else:
        st, gss, w_hbm = refs[2], refs[3:7], refs[7]
    hb_out, zc_out, edge_ref, st_out, hb, w, y, z, tab, hs, sem = refs[-11:]
    load = pltpu.make_async_copy(w_hbm.at[layer], w, sem.at[0])
    load.start()
    save = pltpu.make_async_copy(hb, hb_out.at[layer], sem.at[1])
    t, r = pos[0], pos[1]
    n_own = z.shape[0]
    halo_at = pl.multiple_of((1 - r) * (n_own + WIDE), WIDE)
    zero_at = pl.multiple_of(r * (n_own + WIDE), WIDE)
    hb[pl.ds(zero_at, WIDE), :] = jnp.zeros((WIDE, CHANS), BF16)
    edge = zall.shape[0] - n_own
    if not first:
        for k in range(GROUPS):
            group = t ^ k
            rstd, own, oth = norm_tables(st, group, pos[2], pos[3], float(n_own), total)
            gain, shift = gss[k][layer - 1 : layer, :], gss[k][layer + 7 : layer + 8, :]
            tab[group, 0:1] = rstd * gain
            tab[group, 1:2] = own * gain + shift
            tab[group, 2:3] = oth * gain + shift

    def act(values, group, which):
        if first:
            return values
        n = values.astype(F32) * tab[group, 0:1, :] + tab[group, which : which + 1, :]
        h = n * sigmoid(n)
        return soft(h) if pool else h

    def body(j, carry):
        at = pl.multiple_of(j * 2 * WIDE, 2 * WIDE)
        for group in range(GROUPS):
            lanes = slice(group * LANES, (group + 1) * LANES)
            h = act(zall[pl.ds(at, 2 * WIDE), lanes], group, 1)
            hb[pl.ds(pl.multiple_of(at + WIDE, WIDE), 2 * WIDE), lanes] = h.astype(BF16)
        return carry

    lax.fori_loop(0, n_own // (2 * WIDE), body, 0)
    for group in range(GROUPS):
        lanes = slice(group * LANES, (group + 1) * LANES)
        h = act(zall[n_own : n_own + edge, lanes], group, 2)
        if edge > WIDE:
            hs[...] = h
            h = hs[pl.ds(pl.multiple_of(r * WIDE, WIDE), WIDE), :]
        hb[pl.ds(halo_at, WIDE), lanes] = h.astype(BF16)
    save.start()
    load.wait()
    lhs = jnp.concatenate([hb[i * WIDE : i * WIDE + n_own, :] for i in range(3)], axis=1)
    rhs = jnp.concatenate(
        [
            jnp.concatenate([w[:, (3 * i + s) * CHANS : (3 * i + s + 1) * CHANS] for i in range(3)], axis=1)
            for s in range(3)
        ],
        axis=0,
    )
    y[...] = lax.dot_general(lhs, rhs, (((1,), (1,)), ((), ())), preferred_element_type=F32)

    def add_up(j, acc):
        rows = pair_rows(j)
        v = left_right(y[rows, 0:128], y[rows, 128:256], y[rows, 256:384])
        z[rows, :] = v
        return acc + fold(v)

    steps = n_own // (2 * WIDE)
    summed = lax.fori_loop(0, steps, add_up, jnp.zeros((8, LANES), F32))
    mean = jnp.sum(summed, axis=0, keepdims=True) / n_own

    def centre(j, acc):
        rows = pair_rows(j)
        v = z[rows, :] - mean
        z[rows, :] = v
        zc_out[rows, :] = v.astype(BF16)
        return acc + fold(jnp.square(v))

    apart = lax.fori_loop(0, steps, centre, jnp.zeros((8, LANES), F32))
    sums = [mean, jnp.sum(apart, axis=0, keepdims=True), jnp.zeros((6, LANES), F32)]
    sums = jnp.concatenate(sums, axis=0)
    for i in range(st_out.shape[0]):
        st_out[i] = sums
    edge_ref[...] = zc_out[pl.ds(edge_start(n_own, edge_out, r), edge_out), :]
    zc_out[n_own : n_own + edge_out, :] = jnp.zeros((edge_out, LANES), BF16)
    save.wait()


def fwd_step(layer, pool, edge_out, total, pos, slots, st, tables, weights, kept, n_own, devices, ties):
    first = st is None
    layers = weights.shape[0]
    extra = () if first else (st, *tables)
    return pl.pallas_call(
        functools.partial(fwd_kernel, first, pool, layer, total, edge_out),
        out_shape=(
            pltpu.HBM((layers, n_own + 2 * WIDE, CHANS), BF16),
            pltpu.VMEM((n_own + edge_out, LANES), BF16),
            pltpu.VMEM((edge_out, LANES), BF16),
            pltpu.VMEM((devices, 8, LANES), F32),
        ),
        in_specs=[SMEM] + [VMEM] * (1 + len(extra)) + [ANY] * (1 if first else 2) + [FREE] * len(ties),
        out_specs=(ANY, VMEM, VMEM, VMEM),
        input_output_aliases={} if first else {3 + len(extra): 0},
        scratch_shapes=[
            pltpu.VMEM((n_own + 2 * WIDE, CHANS), BF16),
            pltpu.VMEM((LANES, 9 * CHANS), BF16),
            pltpu.VMEM((n_own, 3 * LANES), F32),
            pltpu.VMEM((n_own, LANES), F32),
            pltpu.VMEM((GROUPS, 8, LANES), F32),
            pltpu.VMEM((2 * WIDE, LANES), F32),
            pltpu.SemaphoreType.DMA((2,)),
        ],
        compiler_params=PARAMS,
        cost_estimate=pl.CostEstimate(
            flops=2 * n_own * 9 * CHANS * LANES, bytes_accessed=4 * 1024 * 1024, transcendentals=n_own * CHANS
        ),
        name="conv_forward",
    )(pos, slots, *extra, in_hbm(weights), *(() if first else (in_hbm(kept),)), *ties)


def below_kernel(layer, pool, total, top, *refs):
    pos, zc, st, gs = refs[:4]
    if top:
        terms, h_out, dn_out, msg, tab = refs[4:]
    else:
        terms, (dn_out, msg, tab) = refs[4:8], refs[-3:]
    n_own = dn_out.shape[0]
    rstd, own, oth = norm_tables(st, pos[0], pos[2], pos[3], float(n_own), total)
    tab[0:1], tab[1:2] = rstd, own
    tab[2:3], tab[3:4] = gs[layer : layer + 1, :], gs[layer + 8 : layer + 9, :]

    def body(j, accs):
        rows = pair_rows(j)
        xhat = zc[rows, :].astype(F32) * tab[0:1, :] + tab[1:2, :]
        n = xhat * tab[2:3, :] + tab[3:4, :]
        sig = sigmoid(n)
        h = n * sig
        if top:
            g = terms[rows, :].astype(F32)
            h_out[rows, :] = h.astype(BF16)
        else:
            g = functools.reduce(jnp.add, [term[rows, :].astype(F32) for term in terms])
        if pool:
            g = soft_pull(h, g)
        dn = g * (sig * (1.0 + n - h))
        dn_out[rows, :] = dn
        return accs[0] + fold(dn), accs[1] + fold(dn * xhat)

    zero = jnp.zeros((8, LANES), F32)
    sums = lax.fori_loop(0, n_own // (2 * WIDE), body, (zero, zero))
    sums = [jnp.sum(v, axis=0, keepdims=True) for v in sums]
    msg[0:WIDE, :] = dn_out[pl.ds(edge_start(n_own, WIDE, pos[1]), WIDE), :]
    msg[WIDE : WIDE + 8, :] = jnp.concatenate(sums + [jnp.zeros((6, LANES), F32)], axis=0)


def below_step(layer, pool, total, pos, zc, st, gs, terms, ties=()):
    n_own = terms[0].shape[0]
    top = len(terms) == 1
    out_shape = [
        pltpu.VMEM((n_own, LANES), F32),
        pltpu.VMEM((WIDE + 8, LANES), F32),
    ]
    if top:
        out_shape = [jax.ShapeDtypeStruct((n_own, LANES), BF16)] + out_shape
    return pl.pallas_call(
        functools.partial(below_kernel, layer, pool, total, top),
        out_shape=tuple(out_shape),
        in_specs=[SMEM] + [VMEM] * (3 + len(terms)) + [FREE] * len(ties),
        out_specs=(VMEM,) * len(out_shape),
        scratch_shapes=[pltpu.VMEM((8, LANES), F32)],
        compiler_params=PARAMS,
        cost_estimate=pl.CostEstimate(flops=40 * n_own * LANES, bytes_accessed=1024 * 1024, transcendentals=n_own * LANES),
        name="silu_backward",
    )(pos, zc, st, gs, *terms, *ties)


def bwd_kernel(layer, total, *refs):
    pos, dn, dedge, sums, zc, st, gs, w_hbm = refs[:8]
    outs, d_out, d, w, y, tab, sem = refs[-10:-6], *refs[-6:]
    load = pltpu.make_async_copy(w_hbm.at[layer], w, sem)
    load.start()
    t, r = pos[0], pos[1]
    n_own = dn.shape[0]
    halo_at = pl.multiple_of((1 - r) * (n_own + WIDE), WIDE)
    zero_at = pl.multiple_of(r * (n_own + WIDE), WIDE)
    edge = zc.shape[0] - n_own
    d[pl.ds(zero_at, WIDE), :] = jnp.zeros((WIDE, 3 * LANES), BF16)
    rstd, own, oth = norm_tables(st, t, pos[2], pos[3], float(n_own), total)
    scale = gs[layer : layer + 1, :] * rstd
    shift_sum, gain_sum = sums[0:1, :], sums[1:2, :]
    slope = scale * gain_sum / total
    tab[0:1] = scale
    tab[1:2] = slope * rstd
    tab[2:3] = scale * shift_sum / total + slope * own
    tab[3:4] = scale * shift_sum / total + slope * oth

    def spread_columns(v, at):
        rows = v.shape[0]
        column = lax.broadcasted_iota(jnp.int32, v.shape, 0) % WIDE
        ahead = jnp.where(column == WIDE - 1, 0.0, pltpu.roll(v, rows - 1, 0))
        behind = jnp.where(column == 0, 0.0, pltpu.roll(v, 1, 0))
        d[pl.ds(at, rows), 0:128] = ahead.astype(BF16)
        d[pl.ds(at, rows), 128:256] = v.astype(BF16)
        d[pl.ds(at, rows), 256:384] = behind.astype(BF16)

    def body(j, carry):
        rows = pair_rows(j)
        v = dn[rows, :] * tab[0:1, :] - tab[2:3, :] - zc[rows, :].astype(F32) * tab[1:2, :]
        spread_columns(v, pl.multiple_of(j * 2 * WIDE + WIDE, WIDE))
        return carry

    lax.fori_loop(0, n_own // (2 * WIDE), body, 0)
    near = n_own if edge == WIDE else pl.multiple_of(n_own + r * WIDE, WIDE)
    near = zc[pl.ds(near, WIDE), :].astype(F32)
    spread_columns(dedge[0:WIDE, :] * tab[0:1, :] - tab[3:4, :] - near * tab[1:2, :], halo_at)
    d_out[...] = d[WIDE : WIDE + n_own, :]
    load.wait()
    lhs = jnp.concatenate([d[(2 - i) * WIDE : (2 - i) * WIDE + n_own, :] for i in range(3)], axis=1)
    rhs = jnp.concatenate([w[:, i * CHANS : (i + 1) * CHANS] for i in range(9)], axis=0)
    y[...] = jnp.dot(lhs, rhs, preferred_element_type=F32)

    def share(j, carry):
        rows = pair_rows(j)
        for k in range(GROUPS):
            outs[k][rows, :] = y[rows, pl.ds(lane_of(t ^ k), LANES)].astype(BF16)
        return carry

    lax.fori_loop(0, n_own // (2 * WIDE), share, 0)


def bwd_step(layer, total, pos, dn, dedge, sums, zc, st, gs, weights, ties):
    n_own = dn.shape[0]
    part = pltpu.VMEM((n_own, LANES), BF16)
    return pl.pallas_call(
        functools.partial(bwd_kernel, layer, total),
        out_shape=(
            part,
            part,
            part,
            part,
            pltpu.VMEM((n_own, 3 * LANES), BF16),
        ),
        in_specs=[SMEM] + [VMEM] * 6 + [ANY] + [FREE] * len(ties),
        out_specs=(VMEM,) * 5,
        scratch_shapes=[
            pltpu.VMEM((n_own + 2 * WIDE, 3 * LANES), BF16),
            pltpu.VMEM((LANES, 9 * CHANS), BF16),
            pltpu.VMEM((n_own, CHANS), F32),
            pltpu.VMEM((8, LANES), F32),
            pltpu.SemaphoreType.DMA,
        ],
        compiler_params=PARAMS,
        cost_estimate=pl.CostEstimate(
            flops=2 * n_own * 9 * CHANS * LANES, bytes_accessed=4 * 1024 * 1024, transcendentals=0
        ),
        name="conv_backward",
    )(pos, dn, dedge, sums, zc, st, gs, in_hbm(weights), *ties)


def last_kernel(t0, t1, t2, t3, *refs):
    out = refs[-1]

    def body(j, carry):
        rows = pair_rows(j)
        out[rows, :] = functools.reduce(jnp.add, [term[rows, :].astype(F32) for term in (t0, t1, t2, t3)])
        return carry

    lax.fori_loop(0, out.shape[0] // (2 * WIDE), body, 0)


def last_step(terms, ties):
    return pl.pallas_call(
        last_kernel,
        out_shape=jax.ShapeDtypeStruct(terms[0].shape, F32),
        in_specs=[VMEM] * 4 + [FREE] * len(ties),
        out_specs=VMEM,
        compiler_params=PARAMS,
        name="add_terms",
    )(*terms, *ties)


def halves_kernel(keep, got, out):
    out[...] = (keep[...].astype(F32) + got[...].astype(F32)).astype(BF16)


def add_halves(keep, got):
    return pl.pallas_call(
        halves_kernel,
        out_shape=jax.ShapeDtypeStruct(keep.shape, BF16),
        in_specs=[VMEM] * 2,
        out_specs=VMEM,
        compiler_params=PARAMS,
        cost_estimate=pl.CostEstimate(flops=keep.size, bytes_accessed=6 * keep.size, transcendentals=0),
        name="add_halves",
    )(keep, got)


def wgrad_kernel(layer, pos, d, hb_hbm, *refs):
    keep, send, hb, grad, sem = refs[-5:]
    load = pltpu.make_async_copy(hb_hbm.at[layer], hb, sem)
    load.start()
    n_own = d.shape[0]
    lhs = d[...]
    load.wait()
    for i in range(3):
        part = lax.dot_general(
            lhs, hb[i * WIDE : i * WIDE + n_own, :], (((0,), (0,)), ((), ())), preferred_element_type=F32
        ).astype(BF16)
        for s in range(3):
            grad[:, (3 * i + s) * CHANS : (3 * i + s + 1) * CHANS] = part[s * LANES : (s + 1) * LANES]
    half = LANES // 2
    keep[...] = grad[pl.ds(pl.multiple_of(pos[1] * half, half), half), :]
    send[...] = grad[pl.ds(pl.multiple_of((1 - pos[1]) * half, half), half), :]


def wgrad_step(layer, pos, d, kept, ties):
    half = pltpu.VMEM((LANES // 2, 9 * CHANS), BF16)
    return pl.pallas_call(
        functools.partial(wgrad_kernel, layer),
        out_shape=(half, half),
        in_specs=[SMEM, VMEM, ANY] + [FREE] * len(ties),
        out_specs=(VMEM, VMEM),
        scratch_shapes=[
            pltpu.VMEM(kept.shape[1:], BF16),
            pltpu.VMEM((LANES, 9 * CHANS), BF16),
            pltpu.SemaphoreType.DMA,
        ],
        compiler_params=PARAMS,
        cost_estimate=pl.CostEstimate(
            flops=2 * d.shape[0] * 9 * CHANS * LANES, bytes_accessed=3 * 1024 * 1024, transcendentals=0
        ),
        name="kernel_gradient",
    )(pos, d, in_hbm(kept), *ties)


def place_kernel(layers, fresh, pos, *refs):
    count = 2 * len(layers)
    sources = refs[:count]
    out, held, wide, sem = refs[-4:]
    half = LANES // 2
    r = pos[1]
    loads = [pltpu.make_async_copy(sources[j], held.at[j], sem.at[j]) for j in range(count)]
    for load in loads:
        load.start()
    stores = []
    for j in range(count):
        at = pl.multiple_of((r if j % 2 == 0 else 1 - r) * half, half)
        if j >= 2:
            stores[j - 2].wait()
        loads[j].wait()
        wide[j % 2] = held[j].astype(F32)
        store = pltpu.make_async_copy(wide.at[j % 2], out.at[layers[j // 2], pl.ds(at, half)], sem.at[count + j])
        store.start()
        stores.append(store)
    for store in stores[-2:]:
        store.wait()


def place_step(layers, pos, sources, whole, count):
    half = LANES // 2
    jobs = len(sources)
    return pl.pallas_call(
        functools.partial(place_kernel, layers, whole is None),
        out_shape=pltpu.HBM((count, LANES, 9 * CHANS), F32),
        in_specs=[SMEM] + [ANY] * jobs + ([] if whole is None else [ANY]),
        out_specs=ANY,
        input_output_aliases={} if whole is None else {1 + jobs: 0},
        scratch_shapes=[
            pltpu.VMEM((jobs, half, 9 * CHANS), BF16),
            pltpu.VMEM((2, half, 9 * CHANS), F32),
            pltpu.SemaphoreType.DMA((2 * jobs,)),
        ],
        compiler_params=PARAMS,
        cost_estimate=pl.CostEstimate(flops=0, bytes_accessed=jobs * 2 * 1024 * 1024, transcendentals=0),
        name="place_gradients",
    )(pos, *[in_hbm(v) for v in sources], *(() if whole is None else (in_hbm(whole),)))


def swap_with(value, axis, k):
    return lax.ppermute(value, axis, [(i, i ^ k) for i in range(lax.axis_size(axis))])


def spread(own):
    return (own, *[swap_with(own, "tensor", k) for k in range(1, GROUPS)])


def halo_of_input(x, half):
    n_own = x.shape[0]
    edge = jnp.where(half == 0, x[n_own - WIDE :], x[:WIDE])
    return jnp.concatenate([x, swap_with(edge, "rows", 1)], axis=0)


def fast_local(section_input, conv_weights, norm_gains, norm_shifts, out_grad, out_mask):
    images, rows_here, width = out_mask.shape
    layers = conv_weights.shape[0]
    n_own = rows_here * width
    parts = lax.axis_size("dp") * lax.axis_size("rows")
    total = float(n_own * parts)
    t, half = lax.axis_index("tensor"), lax.axis_index("rows")
    image = lax.axis_index("dp")
    pos = jnp.stack([t, half, 2 * image + half, 2 * image + 1 - half]).astype(jnp.int32)
    middle = layers // 2
    x = to_maps(section_input, width).reshape(n_own, LANES)
    slots = lax.all_gather(halo_of_input(x, half), "tensor", axis=1, tiled=True)
    pad = jnp.zeros((8 - layers, LANES), F32)
    tables = spread(jnp.concatenate([norm_gains, pad, norm_shifts, pad], axis=0))
    top_grad = (to_maps(out_grad, width) * out_mask[..., None].astype(BF16)).reshape(n_own, LANES)

    st, kept = None, None
    halves = ("dp", "rows")
    kept_z, kept_st = [], []
    for layer in range(layers):
        last = layer + 1 == layers
        edge = 2 * WIDE if layer + 1 == middle else WIDE
        everyone = halves if last else (*halves, "tensor")
        devices = parts if last else parts * GROUPS
        kept, zc, rim, local = fwd_step(
            layer,
            layer == middle,
            edge,
            total,
            pos,
            slots,
            st,
            tables,
            conv_weights,
            kept,
            n_own,
            devices,
            (top_grad,) if layer == 2 else (),
        )
        rim = swap_with(rim, "rows", 1)
        st = lax.all_to_all(local, everyone, split_axis=0, concat_axis=0, tiled=True)
        st = st.reshape(parts, devices // parts, 8, LANES)
        zc = lax.dynamic_update_slice_in_dim(zc, rim, n_own, axis=0)
        kept_z.append(zc)
        kept_st.append(st)
        if not last:
            slots = lax.all_gather(zc, "tensor", axis=1, tiled=True)
    top = layers - 1
    h_last, dn, msg = below_step(top, False, total, pos, kept_z[top], kept_st[top], tables[0], (top_grad,))

    def with_other(values):
        return [v for mine in values for v in (mine, swap_with(mine, "rows", 1))]

    sum_list, pairs = [None] * layers, [None] * layers
    ahead, back = [[0, 1, 2, 3]], [[3, 2, 1, 0]]
    ties, urgent, whole = (), (), None
    for layer in range(layers - 1, -1, -1):
        got = swap_with(msg, "rows", 1)
        sums = msg[WIDE:] + got[WIDE:]
        one, two, three = (swap_with(sums, "dp", k) for k in (1, 2, 3))
        sums = (sums + one) + (two + three)
        sum_list[layer] = sums
        *terms, d = bwd_step(
            layer, total, pos, dn, got, sums, kept_z[layer], kept_st[layer], tables[0], conv_weights, urgent
        )
        terms = (terms[0], *[swap_with(terms[k], "tensor", k) for k in range(1, GROUPS)])
        keep, send = wgrad_step(layer, pos, d, kept, ())
        pairs[layer] = add_halves(keep, swap_with(send, "rows", 1))
        if layer > 0:
            below = layer - 1
            dn, msg = below_step(
                below, layer == middle, total, pos, kept_z[below], kept_st[below], tables[0], terms, (keep, *ties)
            )
        else:
            grad = last_step(terms, (pairs[0], *ties))
        ties, urgent = ((), (pairs[layer],)) if layer % 2 == 0 else ((pairs[layer],), ())
        if layer == 4:
            upper = lax.psum((pairs[5], pairs[4]), "dp", axis_index_groups=ahead)
        if layer == 2:
            mid = lax.psum((pairs[3], pairs[2]), "dp", axis_index_groups=back)
            urgent = (pairs[2], in_hbm(upper[0]))
    tied, upper = lax.optimization_barrier(((pairs[1], pairs[0]), upper))
    lower = lax.psum(tied, "dp", axis_index_groups=ahead)
    shape = (images, rows_here, width, LANES)
    grad, mid = lax.optimization_barrier((grad, mid))
    outputs = (from_maps(h_last.reshape(shape)), from_maps(grad.reshape(shape)))
    whole = place_step((5, 4), pos, with_other(upper), None, layers)
    whole = place_step((3, 2), pos, with_other(mid), whole, layers)
    sums = jnp.stack(sum_list)
    lower, whole, outputs, sums = lax.optimization_barrier((lower, whole, outputs, sums))
    whole = place_step((1, 0), pos, with_other(lower), whole, layers)
    return (*outputs, whole, sums[:, 1], sums[:, 0])


def solution(mesh):
    in_specs = (
        P("dp", "rows", "tensor"),
        P(None, "tensor", None),
        P(None, "tensor"),
        P(None, "tensor"),
        P("dp", "rows", "tensor"),
        P("dp", "rows", None),
    )
    out_specs = (
        P("dp", "rows", "tensor"),
        P("dp", "rows", "tensor"),
        P(None, "tensor", None),
        P(None, "tensor"),
        P(None, "tensor"),
    )
    local = fast_local if fits_kernels(mesh) else generic_local
    return jax.shard_map(local, mesh=mesh, in_specs=in_specs, out_specs=out_specs, check_vma=False)
```

```python
import functools

import jax
import jax.numpy as jnp
from jax import lax
from jax.experimental import pallas as pl
from jax.experimental.pallas import tpu as pltpu
from jax.sharding import PartitionSpec as P

EPS = 1e-05


def padded_2(cells, sides, width):
    for axis, dim in sides:
        count = lax.axis_size(axis)
        ends = count - 1
        head = lax.slice_in_dim(cells, 0, width, axis=dim)
        tail = lax.slice_in_dim(cells, cells.shape[dim] - width, cells.shape[dim], axis=dim)
        cells = jnp.concatenate(
            [
                lax.ppermute(tail, axis, [(i, (i + 1) % count) for i in range(ends)]),
                cells,
                lax.ppermute(head, axis, [((i + 1) % count, i) for i in range(ends)]),
            ],
            axis=dim,
        )
    return cells


def to_maps(flat, width):
    count, high, merged = flat.shape
    return flat.reshape(count, high, merged // width, width).transpose(0, 1, 3, 2)


def from_maps(maps):
    count, high, wide, chans = maps.shape
    return maps.transpose(0, 1, 3, 2).reshape(count, high, chans * wide)


def spatial_conv(padded, kernel):
    return lax.conv_general_dilated(
        padded,
        kernel,
        (1, 1),
        ((0, 0), (1, 1)),
        dimension_numbers=("NHWC", "HWIO", "NHWC"),
        preferred_element_type=jnp.float32,
    )


def flipped(kernel):
    return jnp.transpose(kernel[::-1, ::-1], (0, 1, 3, 2))


def pool_unpool(values):
    count, high, wide, chans = values.shape
    blocks = values.reshape(count, high // 2, 2, wide // 2, 2, chans)
    pooled = jax.nn.logsumexp(blocks, axis=(2, 4), keepdims=True)
    return (jnp.exp(blocks - pooled) * pooled).reshape(values.shape)


def moments(conv_out, total_pixels):
    summed = lax.psum(jnp.sum(conv_out, axis=(0, 1, 2)), ("dp", "rows"))
    mean = summed / total_pixels
    spread = lax.psum(jnp.sum(jnp.square(conv_out - mean), axis=(0, 1, 2)), ("dp", "rows"))
    var = spread / total_pixels
    return (mean, lax.rsqrt(var + EPS))


def kernel_grad(whole, dconv):
    images, rows_here, width, chans = dconv.shape
    widened = jnp.pad(whole, ((0, 0), (0, 0), (1, 1), (0, 0)))
    stacked = []
    for row_off in range(3):
        line = []
        for col_off in range(3):
            window = widened[:, row_off : row_off + rows_here, col_off : col_off + width, :]
            line.append(
                jnp.einsum("bhwc,bhwo->co", window, dconv, preferred_element_type=jnp.float32)
            )
        stacked.append(jnp.stack(line))
    return jnp.stack(stacked)


def generic_local(section_input, conv_weights, norm_gains, norm_shifts, out_grad, out_mask):
    width = out_mask.shape[2]
    images, rows_here = (out_mask.shape[0], out_mask.shape[1])
    total_pixels = float(images * rows_here * width * lax.axis_size("dp") * lax.axis_size("rows"))
    layers, out_here, flat_in = conv_weights.shape
    chans_in = flat_in // 9
    kernels_hwio = conv_weights.reshape(layers, out_here, 3, 3, chans_in).transpose(0, 2, 3, 4, 1)
    middle = layers // 2
    kept = []
    acting = to_maps(section_input, width)
    current = acting.astype(jnp.float32)
    pre_pool = current
    for index in range(layers):
        if index == middle:
            pre_pool = current
            acting = pool_unpool(pre_pool).astype(jnp.bfloat16)
        padded = padded_2(acting, (("rows", 1),), 1)
        whole = lax.all_gather(padded, "tensor", axis=3, tiled=True)
        conv_out = spatial_conv(whole, kernels_hwio[index])
        mean, rstd = moments(conv_out, total_pixels)
        normed = (conv_out - mean) * rstd
        shifted = normed * norm_gains[index] + norm_shifts[index]
        current = jax.nn.silu(shifted)
        acting = current.astype(jnp.bfloat16)
        kept.append((whole, normed, shifted, rstd))
    grad = to_maps(out_grad, width).astype(jnp.float32) * out_mask[..., None].astype(jnp.float32)
    kernel_list = [None] * layers
    gain_list = [None] * layers
    shift_list = [None] * layers
    for index in range(layers - 1, -1, -1):
        whole, normed, shifted, rstd = kept[index]
        unused, pull_silu = jax.vjp(jax.nn.silu, shifted)
        dshift = pull_silu(grad)[0]
        gain_sum, shift_sum = lax.psum(
            (jnp.sum(dshift * normed, axis=(0, 1, 2)), jnp.sum(dshift, axis=(0, 1, 2))),
            ("dp", "rows"),
        )
        gain_list[index] = gain_sum
        shift_list[index] = shift_sum
        dconv = (
            norm_gains[index]
            * rstd
            * (dshift - shift_sum / total_pixels - normed * gain_sum / total_pixels)
        ).astype(jnp.bfloat16)
        summed_kernel = lax.psum(
            kernel_grad(whole, dconv).astype(jnp.bfloat16), ("dp", "rows")
        ).astype(jnp.float32)
        kernel_list[index] = summed_kernel.transpose(3, 0, 1, 2).reshape(out_here, flat_in)
        grad_rim = padded_2(dconv, (("rows", 1),), 1)
        partial_terms = spatial_conv(grad_rim, flipped(kernels_hwio[index]))
        grad_in = lax.psum_scatter(
            partial_terms.astype(jnp.bfloat16), "tensor", scatter_dimension=3, tiled=True
        ).astype(jnp.float32)
        if index == middle:
            unused, pull_pool = jax.vjp(pool_unpool, pre_pool)
            grad = pull_pool(grad_in)[0]
        else:
            grad = grad_in
    return (
        from_maps(acting),
        from_maps(grad),
        jnp.stack(kernel_list),
        jnp.stack(gain_list),
        jnp.stack(shift_list),
    )


GROUPS = 4
LANES = 128
WIDE = 48
CHANS = GROUPS * LANES
F32 = jnp.float32
BF16 = jnp.bfloat16
VMEM = pl.BlockSpec(memory_space=pltpu.VMEM)
SMEM = pl.BlockSpec(memory_space=pltpu.SMEM)
ANY = pl.BlockSpec(memory_space=pltpu.HBM)
FREE = pl.BlockSpec(memory_space=pl.ANY)
LITTLE = pl.CostEstimate(flops=1024, bytes_accessed=1024, transcendentals=0)
PARAMS = pltpu.CompilerParams(vmem_limit_bytes=20 * 1024 * 1024)


def in_hbm(value):
    return pltpu.with_memory_space_constraint(value, pltpu.HBM)


def fits_kernels(mesh):
    return mesh.shape["tensor"] == GROUPS and mesh.shape["rows"] == 2 and mesh.shape["dp"] == 4


def sigmoid(v):
    return 0.5 * jnp.tanh(0.5 * v) + 0.5


def swap_columns(v):
    column = lax.broadcasted_iota(jnp.int32, v.shape, 0)
    return jnp.where(column % 2 == 0, pltpu.roll(v, WIDE - 1, 0), pltpu.roll(v, 1, 0))


def soft_parts(h):
    top = jnp.maximum(h[0], h[1])
    top = jnp.maximum(top, swap_columns(top))
    e0, e1 = jnp.exp(h[0] - top), jnp.exp(h[1] - top)
    total = e0 + e1
    total = total + swap_columns(total)
    pooled = top + jnp.log(total)
    inverse = 1.0 / total
    return e0 * inverse, e1 * inverse, pooled


def soft(h):
    h = h.reshape(2, WIDE, LANES)
    q0, q1, pooled = soft_parts(h)
    return jnp.concatenate([q0 * pooled, q1 * pooled], axis=0)


def soft_pull(h, grad):
    h = h.reshape(2, WIDE, LANES)
    grad = grad.reshape(2, WIDE, LANES)
    q0, q1, pooled = soft_parts(h)
    mix = q0 * grad[0] + q1 * grad[1]
    mix = mix + swap_columns(mix)
    return jnp.concatenate(
        [q0 * (pooled * (grad[0] - mix) + mix), q1 * (pooled * (grad[1] - mix) + mix)], axis=0
    )


def norm_tables(st, group, i_own, i_oth, n_local, total):
    parts = st.shape[0]
    group = 0 if st.shape[1] == 1 else group
    blocks = [st[i, group] for i in range(parts)]
    summed = functools.reduce(jnp.add, blocks)
    mean = summed[0:1] / parts
    apart = functools.reduce(jnp.add, [jnp.square(b - mean) for b in blocks])
    rstd = lax.rsqrt((summed[1:2] + n_local * apart[0:1]) / total + EPS)
    return rstd, (st[i_own, group, 0:1] - mean) * rstd, (st[i_oth, group, 0:1] - mean) * rstd


def left_right(y0, y1, y2):
    rows = y0.shape[0]
    column = lax.broadcasted_iota(jnp.int32, y0.shape, 0) % WIDE
    before = jnp.where(column == 0, 0.0, pltpu.roll(y0, 1, 0))
    after = jnp.where(column == WIDE - 1, 0.0, pltpu.roll(y2, rows - 1, 0))
    return before + y1 + after


def lane_of(group):
    return pl.multiple_of(group * LANES, LANES)


def edge_start(n_own, edge, half):
    return pl.multiple_of((1 - half) * (n_own - edge), WIDE)


def pair_rows(j):
    return pl.ds(pl.multiple_of(j * 2 * WIDE, 2 * WIDE), 2 * WIDE)


def fold(v):
    return jnp.sum(v.reshape(v.shape[0] // 8, 8, LANES), axis=0)


def fwd_kernel(first, pool, layer, total, edge_out, *refs):
    pos, zall = refs[0], refs[1]
    if first:
        w_hbm = refs[2]
    else:
        st, gss, w_hbm = refs[2], refs[3:7], refs[7]
    hb_out, zc_out, edge_ref, st_out, hb, w, y, z, tab, hs, sem = refs[-11:]
    load = pltpu.make_async_copy(w_hbm.at[layer], w, sem.at[0])
    load.start()
    save = pltpu.make_async_copy(hb, hb_out.at[layer], sem.at[1])
    t, r = pos[0], pos[1]
    n_own = z.shape[0]
    halo_at = pl.multiple_of((1 - r) * (n_own + WIDE), WIDE)
    zero_at = pl.multiple_of(r * (n_own + WIDE), WIDE)
    hb[pl.ds(zero_at, WIDE), :] = jnp.zeros((WIDE, CHANS), BF16)
    edge = zall.shape[0] - n_own
    if not first:
        for k in range(GROUPS):
            group = t ^ k
            rstd, own, oth = norm_tables(st, group, pos[2], pos[3], float(n_own), total)
            gain, shift = gss[k][layer - 1 : layer, :], gss[k][layer + 7 : layer + 8, :]
            tab[group, 0:1] = rstd * gain
            tab[group, 1:2] = own * gain + shift
            tab[group, 2:3] = oth * gain + shift

    def act(values, group, which):
        if first:
            return values
        n = values.astype(F32) * tab[group, 0:1, :] + tab[group, which : which + 1, :]
        h = n * sigmoid(n)
        return soft(h) if pool else h

    def body(j, carry):
        at = pl.multiple_of(j * 2 * WIDE, 2 * WIDE)
        for group in range(GROUPS):
            lanes = slice(group * LANES, (group + 1) * LANES)
            h = act(zall[pl.ds(at, 2 * WIDE), lanes], group, 1)
            hb[pl.ds(pl.multiple_of(at + WIDE, WIDE), 2 * WIDE), lanes] = h.astype(BF16)
        return carry

    lax.fori_loop(0, n_own // (2 * WIDE), body, 0)
    for group in range(GROUPS):
        lanes = slice(group * LANES, (group + 1) * LANES)
        h = act(zall[n_own : n_own + edge, lanes], group, 2)
        if edge > WIDE:
            hs[...] = h
            h = hs[pl.ds(pl.multiple_of(r * WIDE, WIDE), WIDE), :]
        hb[pl.ds(halo_at, WIDE), lanes] = h.astype(BF16)
    save.start()
    load.wait()
    lhs = jnp.concatenate([hb[i * WIDE : i * WIDE + n_own, :] for i in range(3)], axis=1)
    rhs = jnp.concatenate(
        [
            jnp.concatenate([w[:, (3 * i + s) * CHANS : (3 * i + s + 1) * CHANS] for i in range(3)], axis=1)
            for s in range(3)
        ],
        axis=0,
    )
    y[...] = lax.dot_general(lhs, rhs, (((1,), (1,)), ((), ())), preferred_element_type=F32)

    def add_up(j, acc):
        rows = pair_rows(j)
        v = left_right(y[rows, 0:128], y[rows, 128:256], y[rows, 256:384])
        z[rows, :] = v
        return acc + fold(v)

    steps = n_own // (2 * WIDE)
    summed = lax.fori_loop(0, steps, add_up, jnp.zeros((8, LANES), F32))
    mean = jnp.sum(summed, axis=0, keepdims=True) / n_own

    def centre(j, acc):
        rows = pair_rows(j)
        v = z[rows, :] - mean
        z[rows, :] = v
        zc_out[rows, :] = v.astype(BF16)
        return acc + fold(jnp.square(v))

    apart = lax.fori_loop(0, steps, centre, jnp.zeros((8, LANES), F32))
    sums = [mean, jnp.sum(apart, axis=0, keepdims=True), jnp.zeros((6, LANES), F32)]
    sums = jnp.concatenate(sums, axis=0)
    for i in range(st_out.shape[0]):
        st_out[i] = sums
    edge_ref[...] = zc_out[pl.ds(edge_start(n_own, edge_out, r), edge_out), :]
    zc_out[n_own : n_own + edge_out, :] = jnp.zeros((edge_out, LANES), BF16)
    save.wait()


def fwd_step(layer, pool, edge_out, total, pos, slots, st, tables, weights, kept, n_own, devices, ties):
    first = st is None
    layers = weights.shape[0]
    extra = () if first else (st, *tables)
    return pl.pallas_call(
        functools.partial(fwd_kernel, first, pool, layer, total, edge_out),
        out_shape=(
            pltpu.HBM((layers, n_own + 2 * WIDE, CHANS), BF16),
            pltpu.VMEM((n_own + edge_out, LANES), BF16),
            pltpu.VMEM((edge_out, LANES), BF16),
            pltpu.VMEM((devices, 8, LANES), F32),
        ),
        in_specs=[SMEM] + [VMEM] * (1 + len(extra)) + [ANY] * (1 if first else 2) + [FREE] * len(ties),
        out_specs=(ANY, VMEM, VMEM, VMEM),
        input_output_aliases={} if first else {3 + len(extra): 0},
        scratch_shapes=[
            pltpu.VMEM((n_own + 2 * WIDE, CHANS), BF16),
            pltpu.VMEM((LANES, 9 * CHANS), BF16),
            pltpu.VMEM((n_own, 3 * LANES), F32),
            pltpu.VMEM((n_own, LANES), F32),
            pltpu.VMEM((GROUPS, 8, LANES), F32),
            pltpu.VMEM((2 * WIDE, LANES), F32),
            pltpu.SemaphoreType.DMA((2,)),
        ],
        compiler_params=PARAMS,
        cost_estimate=pl.CostEstimate(
            flops=2 * n_own * 9 * CHANS * LANES, bytes_accessed=4 * 1024 * 1024, transcendentals=n_own * CHANS
        ),
        name="conv_forward",
    )(pos, slots, *extra, in_hbm(weights), *(() if first else (in_hbm(kept),)), *ties)


def below_kernel(layer, pool, total, top, *refs):
    pos, zc, st, gs = refs[:4]
    if top:
        terms, h_out, dn_out, msg, tab = refs[4:]
    else:
        terms, (dn_out, msg, tab) = refs[4:8], refs[-3:]
    n_own = dn_out.shape[0]
    rstd, own, oth = norm_tables(st, pos[0], pos[2], pos[3], float(n_own), total)
    tab[0:1], tab[1:2] = rstd, own
    tab[2:3], tab[3:4] = gs[layer : layer + 1, :], gs[layer + 8 : layer + 9, :]

    def body(j, accs):
        rows = pair_rows(j)
        xhat = zc[rows, :].astype(F32) * tab[0:1, :] + tab[1:2, :]
        n = xhat * tab[2:3, :] + tab[3:4, :]
        sig = sigmoid(n)
        h = n * sig
        if top:
            g = terms[rows, :].astype(F32)
            h_out[rows, :] = h.astype(BF16)
        else:
            g = functools.reduce(jnp.add, [term[rows, :].astype(F32) for term in terms])
        if pool:
            g = soft_pull(h, g)
        dn = g * (sig * (1.0 + n - h))
        dn_out[rows, :] = dn
        return accs[0] + fold(dn), accs[1] + fold(dn * xhat)

    zero = jnp.zeros((8, LANES), F32)
    sums = lax.fori_loop(0, n_own // (2 * WIDE), body, (zero, zero))
    sums = [jnp.sum(v, axis=0, keepdims=True) for v in sums]
    msg[0:WIDE, :] = dn_out[pl.ds(edge_start(n_own, WIDE, pos[1]), WIDE), :]
    msg[WIDE : WIDE + 8, :] = jnp.concatenate(sums + [jnp.zeros((6, LANES), F32)], axis=0)


def below_step(layer, pool, total, pos, zc, st, gs, terms, ties=()):
    n_own = terms[0].shape[0]
    top = len(terms) == 1
    out_shape = [
        pltpu.VMEM((n_own, LANES), F32),
        pltpu.VMEM((WIDE + 8, LANES), F32),
    ]
    if top:
        out_shape = [jax.ShapeDtypeStruct((n_own, LANES), BF16)] + out_shape
    return pl.pallas_call(
        functools.partial(below_kernel, layer, pool, total, top),
        out_shape=tuple(out_shape),
        in_specs=[SMEM] + [VMEM] * (3 + len(terms)) + [FREE] * len(ties),
        out_specs=(VMEM,) * len(out_shape),
        scratch_shapes=[pltpu.VMEM((8, LANES), F32)],
        compiler_params=PARAMS,
        cost_estimate=LITTLE,
        name="silu_backward",
    )(pos, zc, st, gs, *terms, *ties)


def bwd_kernel(layer, total, *refs):
    pos, dn, dedge, sums, zc, st, gs, w_hbm = refs[:8]
    outs, d_out, d, w, y, tab, sem = refs[-10:-6], *refs[-6:]
    load = pltpu.make_async_copy(w_hbm.at[layer], w, sem)
    load.start()
    t, r = pos[0], pos[1]
    n_own = dn.shape[0]
    halo_at = pl.multiple_of((1 - r) * (n_own + WIDE), WIDE)
    zero_at = pl.multiple_of(r * (n_own + WIDE), WIDE)
    edge = zc.shape[0] - n_own
    d[pl.ds(zero_at, WIDE), :] = jnp.zeros((WIDE, 3 * LANES), BF16)
    rstd, own, oth = norm_tables(st, t, pos[2], pos[3], float(n_own), total)
    scale = gs[layer : layer + 1, :] * rstd
    shift_sum, gain_sum = sums[0:1, :], sums[1:2, :]
    slope = scale * gain_sum / total
    tab[0:1] = scale
    tab[1:2] = slope * rstd
    tab[2:3] = scale * shift_sum / total + slope * own
    tab[3:4] = scale * shift_sum / total + slope * oth

    def spread_columns(v, at):
        rows = v.shape[0]
        column = lax.broadcasted_iota(jnp.int32, v.shape, 0) % WIDE
        ahead = jnp.where(column == WIDE - 1, 0.0, pltpu.roll(v, rows - 1, 0))
        behind = jnp.where(column == 0, 0.0, pltpu.roll(v, 1, 0))
        d[pl.ds(at, rows), 0:128] = ahead.astype(BF16)
        d[pl.ds(at, rows), 128:256] = v.astype(BF16)
        d[pl.ds(at, rows), 256:384] = behind.astype(BF16)

    def body(j, carry):
        rows = pair_rows(j)
        v = dn[rows, :] * tab[0:1, :] - tab[2:3, :] - zc[rows, :].astype(F32) * tab[1:2, :]
        spread_columns(v, pl.multiple_of(j * 2 * WIDE + WIDE, WIDE))
        return carry

    lax.fori_loop(0, n_own // (2 * WIDE), body, 0)
    near = n_own if edge == WIDE else pl.multiple_of(n_own + r * WIDE, WIDE)
    near = zc[pl.ds(near, WIDE), :].astype(F32)
    spread_columns(dedge[0:WIDE, :] * tab[0:1, :] - tab[3:4, :] - near * tab[1:2, :], halo_at)
    d_out[...] = d[WIDE : WIDE + n_own, :]
    load.wait()
    lhs = jnp.concatenate([d[(2 - i) * WIDE : (2 - i) * WIDE + n_own, :] for i in range(3)], axis=1)
    rhs = jnp.concatenate([w[:, i * CHANS : (i + 1) * CHANS] for i in range(9)], axis=0)
    y[...] = jnp.dot(lhs, rhs, preferred_element_type=F32)

    def share(j, carry):
        rows = pair_rows(j)
        for k in range(GROUPS):
            outs[k][rows, :] = y[rows, pl.ds(lane_of(t ^ k), LANES)].astype(BF16)
        return carry

    lax.fori_loop(0, n_own // (2 * WIDE), share, 0)


def bwd_step(layer, total, pos, dn, dedge, sums, zc, st, gs, weights, ties):
    n_own = dn.shape[0]
    part = pltpu.VMEM((n_own, LANES), BF16)
    return pl.pallas_call(
        functools.partial(bwd_kernel, layer, total),
        out_shape=(
            part,
            part,
            part,
            part,
            pltpu.VMEM((n_own, 3 * LANES), BF16),
        ),
        in_specs=[SMEM] + [VMEM] * 6 + [ANY] + [FREE] * len(ties),
        out_specs=(VMEM,) * 5,
        scratch_shapes=[
            pltpu.VMEM((n_own + 2 * WIDE, 3 * LANES), BF16),
            pltpu.VMEM((LANES, 9 * CHANS), BF16),
            pltpu.VMEM((n_own, CHANS), F32),
            pltpu.VMEM((8, LANES), F32),
            pltpu.SemaphoreType.DMA,
        ],
        compiler_params=PARAMS,
        cost_estimate=LITTLE,
        name="conv_backward",
    )(pos, dn, dedge, sums, zc, st, gs, in_hbm(weights), *ties)


def last_kernel(t0, t1, t2, t3, *refs):
    out = refs[-1]

    def body(j, carry):
        rows = pair_rows(j)
        out[rows, :] = functools.reduce(jnp.add, [term[rows, :].astype(F32) for term in (t0, t1, t2, t3)])
        return carry

    lax.fori_loop(0, out.shape[0] // (2 * WIDE), body, 0)


def last_step(terms, ties):
    return pl.pallas_call(
        last_kernel,
        out_shape=jax.ShapeDtypeStruct(terms[0].shape, F32),
        in_specs=[VMEM] * 4 + [FREE] * len(ties),
        out_specs=VMEM,
        compiler_params=PARAMS,
        cost_estimate=LITTLE,
        name="add_terms",
    )(*terms, *ties)


def halves_kernel(keep, got, out):
    out[...] = (keep[...].astype(F32) + got[...].astype(F32)).astype(BF16)


def add_halves(keep, got):
    return pl.pallas_call(
        halves_kernel,
        out_shape=jax.ShapeDtypeStruct(keep.shape, BF16),
        in_specs=[VMEM] * 2,
        out_specs=VMEM,
        compiler_params=PARAMS,
        cost_estimate=LITTLE,
        name="add_halves",
    )(keep, got)


def bundle_kernel(keep1, got1, keep0, got0, out):
    rows = LANES // 8
    for i in range(4):
        at = slice(i * rows, (i + 1) * rows)
        out[i, 0:rows] = (keep1[at, :].astype(F32) + got1[at, :].astype(F32)).astype(BF16)
        out[i, rows : 2 * rows] = (keep0[at, :].astype(F32) + got0[at, :].astype(F32)).astype(BF16)


def bundle_halves(upper, lower):
    return pl.pallas_call(
        bundle_kernel,
        out_shape=pltpu.VMEM((4, LANES // 4, 9 * CHANS), BF16),
        in_specs=[VMEM] * 4,
        out_specs=VMEM,
        compiler_params=PARAMS,
        cost_estimate=LITTLE,
        name="bundle_halves",
    )(*upper, *lower)


def quarters_kernel(pieces, *refs):
    out = refs[-1]
    rows = LANES // 8
    for j in range(2):
        at = slice(j * rows, (j + 1) * rows)
        total = functools.reduce(jnp.add, [pieces[i, at].astype(F32) for i in range(4)]).astype(BF16)
        for i in range(4):
            out[i, at] = total


def add_quarters(pieces, ties):
    return pl.pallas_call(
        quarters_kernel,
        out_shape=pltpu.VMEM(pieces.shape, BF16),
        in_specs=[VMEM] + [FREE] * len(ties),
        out_specs=VMEM,
        compiler_params=PARAMS,
        cost_estimate=LITTLE,
        name="add_quarters",
    )(pieces, *ties)


def wgrad_kernel(layer, pos, d, hb_hbm, *refs):
    keep, send, hb, grad, sem = refs[-5:]
    load = pltpu.make_async_copy(hb_hbm.at[layer], hb, sem)
    load.start()
    n_own = d.shape[0]
    lhs = d[...]
    load.wait()
    for i in range(3):
        part = lax.dot_general(
            lhs, hb[i * WIDE : i * WIDE + n_own, :], (((0,), (0,)), ((), ())), preferred_element_type=F32
        ).astype(BF16)
        for s in range(3):
            grad[:, (3 * i + s) * CHANS : (3 * i + s + 1) * CHANS] = part[s * LANES : (s + 1) * LANES]
    half = LANES // 2
    keep[...] = grad[pl.ds(pl.multiple_of(pos[1] * half, half), half), :]
    send[...] = grad[pl.ds(pl.multiple_of((1 - pos[1]) * half, half), half), :]


def wgrad_step(layer, pos, d, kept, ties):
    half = pltpu.VMEM((LANES // 2, 9 * CHANS), BF16)
    return pl.pallas_call(
        functools.partial(wgrad_kernel, layer),
        out_shape=(half, half),
        in_specs=[SMEM, VMEM, ANY] + [FREE] * len(ties),
        out_specs=(VMEM, VMEM),
        scratch_shapes=[
            pltpu.VMEM(kept.shape[1:], BF16),
            pltpu.VMEM((LANES, 9 * CHANS), BF16),
            pltpu.SemaphoreType.DMA,
        ],
        compiler_params=PARAMS,
        cost_estimate=LITTLE,
        name="kernel_gradient",
    )(pos, d, in_hbm(kept), *ties)


def place_kernel(layers, fresh, pos, *refs):
    count = 2 * len(layers)
    sources = refs[:count]
    out, held, wide, sem = refs[-4:]
    half = LANES // 2
    r = pos[1]
    loads = [pltpu.make_async_copy(sources[j], held.at[j], sem.at[j]) for j in range(count)]
    for load in loads:
        load.start()
    stores = []
    for j in range(count):
        at = pl.multiple_of((r if j % 2 == 0 else 1 - r) * half, half)
        if j >= 2:
            stores[j - 2].wait()
        loads[j].wait()
        wide[j % 2] = held[j].astype(F32)
        store = pltpu.make_async_copy(wide.at[j % 2], out.at[layers[j // 2], pl.ds(at, half)], sem.at[count + j])
        store.start()
        stores.append(store)
    for store in stores[-2:]:
        store.wait()


def place_step(layers, pos, sources, whole, count):
    half = LANES // 2
    jobs = len(sources)
    return pl.pallas_call(
        functools.partial(place_kernel, layers, whole is None),
        out_shape=pltpu.HBM((count, LANES, 9 * CHANS), F32),
        in_specs=[SMEM] + [ANY] * jobs + ([] if whole is None else [ANY]),
        out_specs=ANY,
        input_output_aliases={} if whole is None else {1 + jobs: 0},
        scratch_shapes=[
            pltpu.VMEM((jobs, half, 9 * CHANS), BF16),
            pltpu.VMEM((2, half, 9 * CHANS), F32),
            pltpu.SemaphoreType.DMA((2 * jobs,)),
        ],
        compiler_params=PARAMS,
        cost_estimate=LITTLE,
        name="place_gradients",
    )(pos, *[in_hbm(v) for v in sources], *(() if whole is None else (in_hbm(whole),)))


def unbundle_kernel(pos, mine, other, whole, out, held, wide, sem):
    rows, half = LANES // 8, LANES // 2
    r = pos[1]
    loads = [pltpu.make_async_copy(v, held.at[j], sem.at[j]) for j, v in enumerate((mine, other))]
    for load in loads:
        load.start()
    stores = []
    for j in range(2):
        loads[j].wait()
        base = (r if j == 0 else 1 - r) * half
        for layer in (1, 0):
            slot = 2 * j + layer
            for i in range(4):
                at = slice((1 - layer) * rows, (2 - layer) * rows)
                wide[slot, i * rows : (i + 1) * rows] = held[j, i, at].astype(F32)
            store = pltpu.make_async_copy(
                wide.at[slot], out.at[layer, pl.ds(pl.multiple_of(base, half), half)], sem.at[2 + slot]
            )
            store.start()
            stores.append(store)
    for store in stores:
        store.wait()


def unbundle_step(pos, mine, other, whole):
    half = LANES // 2
    return pl.pallas_call(
        unbundle_kernel,
        out_shape=pltpu.HBM(whole.shape, F32),
        in_specs=[SMEM, FREE, FREE, ANY],
        out_specs=ANY,
        input_output_aliases={3: 0},
        scratch_shapes=[
            pltpu.VMEM((2,) + mine.shape, BF16),
            pltpu.VMEM((4, half, 9 * CHANS), F32),
            pltpu.SemaphoreType.DMA((6,)),
        ],
        compiler_params=PARAMS,
        cost_estimate=LITTLE,
        name="unbundle_gradients",
    )(pos, mine, other, in_hbm(whole))


def swap_with(value, axis, k):
    return lax.ppermute(value, axis, [(i, i ^ k) for i in range(lax.axis_size(axis))])


def spread(own):
    return (own, *[swap_with(own, "tensor", k) for k in range(1, GROUPS)])


def halo_of_input(x, half):
    n_own = x.shape[0]
    edge = jnp.where(half == 0, x[n_own - WIDE :], x[:WIDE])
    return jnp.concatenate([x, swap_with(edge, "rows", 1)], axis=0)


def fast_local(section_input, conv_weights, norm_gains, norm_shifts, out_grad, out_mask):
    images, rows_here, width = out_mask.shape
    layers = conv_weights.shape[0]
    n_own = rows_here * width
    parts = lax.axis_size("dp") * lax.axis_size("rows")
    total = float(n_own * parts)
    t, half = lax.axis_index("tensor"), lax.axis_index("rows")
    image = lax.axis_index("dp")
    pos = jnp.stack([t, half, 2 * image + half, 2 * image + 1 - half]).astype(jnp.int32)
    middle = layers // 2
    x = to_maps(section_input, width).reshape(n_own, LANES)
    slots = lax.all_gather(halo_of_input(x, half), "tensor", axis=1, tiled=True)
    pad = jnp.zeros((8 - layers, LANES), F32)
    tables = spread(jnp.concatenate([norm_gains, pad, norm_shifts, pad], axis=0))
    top_grad = (to_maps(out_grad, width) * out_mask[..., None].astype(BF16)).reshape(n_own, LANES)

    st, kept = None, None
    halves = ("dp", "rows")
    kept_z, kept_st = [], []
    for layer in range(layers):
        last = layer + 1 == layers
        edge = 2 * WIDE if layer + 1 == middle else WIDE
        everyone = halves if last else (*halves, "tensor")
        devices = parts if last else parts * GROUPS
        kept, zc, rim, local = fwd_step(
            layer,
            layer == middle,
            edge,
            total,
            pos,
            slots,
            st,
            tables,
            conv_weights,
            kept,
            n_own,
            devices,
            (top_grad,) if layer == 2 else (),
        )
        rim = swap_with(rim, "rows", 1)
        st = lax.all_to_all(local, everyone, split_axis=0, concat_axis=0, tiled=True)
        st = st.reshape(parts, devices // parts, 8, LANES)
        zc = lax.dynamic_update_slice_in_dim(zc, rim, n_own, axis=0)
        kept_z.append(zc)
        kept_st.append(st)
        if not last:
            slots = lax.all_gather(zc, "tensor", axis=1, tiled=True)
    top = layers - 1
    h_last, dn, msg = below_step(top, False, total, pos, kept_z[top], kept_st[top], tables[0], (top_grad,))

    def with_other(values):
        return [v for mine in values for v in (mine, swap_with(mine, "rows", 1))]

    sum_list, pairs = [None] * layers, [None] * layers
    ahead, back = [[0, 1, 2, 3]], [[3, 2, 1, 0]]
    split, urgent, whole = [None] * layers, (), None
    for layer in range(layers - 1, -1, -1):
        got = swap_with(msg, "rows", 1)
        sums = msg[WIDE:] + got[WIDE:]
        one, two, three = (swap_with(sums, "dp", k) for k in (1, 2, 3))
        sums = (sums + one) + (two + three)
        sum_list[layer] = sums
        *terms, d = bwd_step(
            layer, total, pos, dn, got, sums, kept_z[layer], kept_st[layer], tables[0], conv_weights, urgent
        )
        terms = (terms[0], *[swap_with(terms[k], "tensor", k) for k in range(1, GROUPS)])
        keep, send = wgrad_step(layer, pos, d, kept, ())
        split[layer] = (keep, swap_with(send, "rows", 1))
        if layer > 1:
            pairs[layer] = add_halves(*split[layer])
            urgent = (pairs[layer],)
        else:
            urgent = ()
        if layer > 0:
            below = layer - 1
            late = (in_hbm(upper[0]),) if layer == 1 else ()
            dn, msg = below_step(
                below, layer == middle, total, pos, kept_z[below], kept_st[below], tables[0], terms, (keep, *late)
            )
        else:
            bundle = bundle_halves(split[1], split[0])
            grad = last_step(terms, (bundle,))
        if layer == 4:
            upper = lax.psum((pairs[5], pairs[4]), "dp", axis_index_groups=ahead)
        if layer == 2:
            mid = lax.psum((pairs[3], pairs[2]), "dp", axis_index_groups=back)
    shape = (images, rows_here, width, LANES)
    bundle = lax.all_to_all(bundle, "dp", split_axis=0, concat_axis=0, tiled=True)
    bundle = add_quarters(bundle, ())
    bundle, mid = lax.optimization_barrier((bundle, mid))
    bundle = lax.all_to_all(bundle, "dp", split_axis=0, concat_axis=0, tiled=True)
    outputs = (from_maps(h_last.reshape(shape)), from_maps(grad.reshape(shape)))
    whole = place_step((5, 4, 3, 2), pos, with_other((*upper, *mid)), None, layers)
    sums = jnp.stack(sum_list)
    bundle, whole, outputs, sums = lax.optimization_barrier((bundle, whole, outputs, sums))
    whole = unbundle_step(pos, bundle, swap_with(bundle, "rows", 1), whole)
    return (*outputs, whole, sums[:, 1], sums[:, 0])


def solution(mesh):
    in_specs = (
        P("dp", "rows", "tensor"),
        P(None, "tensor", None),
        P(None, "tensor"),
        P(None, "tensor"),
        P("dp", "rows", "tensor"),
        P("dp", "rows", None),
    )
    out_specs = (
        P("dp", "rows", "tensor"),
        P("dp", "rows", "tensor"),
        P(None, "tensor", None),
        P(None, "tensor"),
        P(None, "tensor"),
    )
    local = fast_local if fits_kernels(mesh) else generic_local
    return jax.shard_map(local, mesh=mesh, in_specs=in_specs, out_specs=out_specs, check_vma=False)
```

```python
import functools

import jax
import jax.numpy as jnp
from jax import lax
from jax.experimental import pallas as pl
from jax.experimental.pallas import tpu as pltpu
from jax.sharding import PartitionSpec as P

EPS = 1e-05


def padded_2(cells, sides, width):
    for axis, dim in sides:
        count = lax.axis_size(axis)
        ends = count - 1
        head = lax.slice_in_dim(cells, 0, width, axis=dim)
        tail = lax.slice_in_dim(cells, cells.shape[dim] - width, cells.shape[dim], axis=dim)
        cells = jnp.concatenate(
            [
                lax.ppermute(tail, axis, [(i, (i + 1) % count) for i in range(ends)]),
                cells,
                lax.ppermute(head, axis, [((i + 1) % count, i) for i in range(ends)]),
            ],
            axis=dim,
        )
    return cells


def to_maps(flat, width):
    count, high, merged = flat.shape
    return flat.reshape(count, high, merged // width, width).transpose(0, 1, 3, 2)


def from_maps(maps):
    count, high, wide, chans = maps.shape
    return maps.transpose(0, 1, 3, 2).reshape(count, high, chans * wide)


def spatial_conv(padded, kernel):
    return lax.conv_general_dilated(
        padded,
        kernel,
        (1, 1),
        ((0, 0), (1, 1)),
        dimension_numbers=("NHWC", "HWIO", "NHWC"),
        preferred_element_type=jnp.float32,
    )


def flipped(kernel):
    return jnp.transpose(kernel[::-1, ::-1], (0, 1, 3, 2))


def pool_unpool(values):
    count, high, wide, chans = values.shape
    blocks = values.reshape(count, high // 2, 2, wide // 2, 2, chans)
    pooled = jax.nn.logsumexp(blocks, axis=(2, 4), keepdims=True)
    return (jnp.exp(blocks - pooled) * pooled).reshape(values.shape)


def moments(conv_out, total_pixels):
    summed = lax.psum(jnp.sum(conv_out, axis=(0, 1, 2)), ("dp", "rows"))
    mean = summed / total_pixels
    spread = lax.psum(jnp.sum(jnp.square(conv_out - mean), axis=(0, 1, 2)), ("dp", "rows"))
    var = spread / total_pixels
    return (mean, lax.rsqrt(var + EPS))


def kernel_grad(whole, dconv):
    images, rows_here, width, chans = dconv.shape
    widened = jnp.pad(whole, ((0, 0), (0, 0), (1, 1), (0, 0)))
    stacked = []
    for row_off in range(3):
        line = []
        for col_off in range(3):
            window = widened[:, row_off : row_off + rows_here, col_off : col_off + width, :]
            line.append(
                jnp.einsum("bhwc,bhwo->co", window, dconv, preferred_element_type=jnp.float32)
            )
        stacked.append(jnp.stack(line))
    return jnp.stack(stacked)


def generic_local(section_input, conv_weights, norm_gains, norm_shifts, out_grad, out_mask):
    width = out_mask.shape[2]
    images, rows_here = (out_mask.shape[0], out_mask.shape[1])
    total_pixels = float(images * rows_here * width * lax.axis_size("dp") * lax.axis_size("rows"))
    layers, out_here, flat_in = conv_weights.shape
    chans_in = flat_in // 9
    kernels_hwio = conv_weights.reshape(layers, out_here, 3, 3, chans_in).transpose(0, 2, 3, 4, 1)
    middle = layers // 2
    kept = []
    acting = to_maps(section_input, width)
    current = acting.astype(jnp.float32)
    pre_pool = current
    for index in range(layers):
        if index == middle:
            pre_pool = current
            acting = pool_unpool(pre_pool).astype(jnp.bfloat16)
        padded = padded_2(acting, (("rows", 1),), 1)
        whole = lax.all_gather(padded, "tensor", axis=3, tiled=True)
        conv_out = spatial_conv(whole, kernels_hwio[index])
        mean, rstd = moments(conv_out, total_pixels)
        normed = (conv_out - mean) * rstd
        shifted = normed * norm_gains[index] + norm_shifts[index]
        current = jax.nn.silu(shifted)
        acting = current.astype(jnp.bfloat16)
        kept.append((whole, normed, shifted, rstd))
    grad = to_maps(out_grad, width).astype(jnp.float32) * out_mask[..., None].astype(jnp.float32)
    kernel_list = [None] * layers
    gain_list = [None] * layers
    shift_list = [None] * layers
    for index in range(layers - 1, -1, -1):
        whole, normed, shifted, rstd = kept[index]
        unused, pull_silu = jax.vjp(jax.nn.silu, shifted)
        dshift = pull_silu(grad)[0]
        gain_sum, shift_sum = lax.psum(
            (jnp.sum(dshift * normed, axis=(0, 1, 2)), jnp.sum(dshift, axis=(0, 1, 2))),
            ("dp", "rows"),
        )
        gain_list[index] = gain_sum
        shift_list[index] = shift_sum
        dconv = (
            norm_gains[index]
            * rstd
            * (dshift - shift_sum / total_pixels - normed * gain_sum / total_pixels)
        ).astype(jnp.bfloat16)
        summed_kernel = lax.psum(
            kernel_grad(whole, dconv).astype(jnp.bfloat16), ("dp", "rows")
        ).astype(jnp.float32)
        kernel_list[index] = summed_kernel.transpose(3, 0, 1, 2).reshape(out_here, flat_in)
        grad_rim = padded_2(dconv, (("rows", 1),), 1)
        partial_terms = spatial_conv(grad_rim, flipped(kernels_hwio[index]))
        grad_in = lax.psum_scatter(
            partial_terms.astype(jnp.bfloat16), "tensor", scatter_dimension=3, tiled=True
        ).astype(jnp.float32)
        if index == middle:
            unused, pull_pool = jax.vjp(pool_unpool, pre_pool)
            grad = pull_pool(grad_in)[0]
        else:
            grad = grad_in
    return (
        from_maps(acting),
        from_maps(grad),
        jnp.stack(kernel_list),
        jnp.stack(gain_list),
        jnp.stack(shift_list),
    )


GROUPS = 4
LANES = 128
WIDE = 48
CHANS = GROUPS * LANES
F32 = jnp.float32
BF16 = jnp.bfloat16
VMEM = pl.BlockSpec(memory_space=pltpu.VMEM)
SMEM = pl.BlockSpec(memory_space=pltpu.SMEM)
ANY = pl.BlockSpec(memory_space=pltpu.HBM)
FREE = pl.BlockSpec(memory_space=pl.ANY)
LITTLE = pl.CostEstimate(flops=1024, bytes_accessed=1024, transcendentals=0)
PARAMS = pltpu.CompilerParams(vmem_limit_bytes=20 * 1024 * 1024)


def in_hbm(value):
    return pltpu.with_memory_space_constraint(value, pltpu.HBM)


def fits_kernels(mesh):
    return mesh.shape["tensor"] == GROUPS and mesh.shape["rows"] == 2 and mesh.shape["dp"] == 4


def sigmoid(v):
    return 0.5 * jnp.tanh(0.5 * v) + 0.5


def swap_columns(v):
    column = lax.broadcasted_iota(jnp.int32, v.shape, 0)
    return jnp.where(column % 2 == 0, pltpu.roll(v, WIDE - 1, 0), pltpu.roll(v, 1, 0))


def soft_parts(h):
    top = jnp.maximum(h[0], h[1])
    top = jnp.maximum(top, swap_columns(top))
    e0, e1 = jnp.exp(h[0] - top), jnp.exp(h[1] - top)
    total = e0 + e1
    total = total + swap_columns(total)
    pooled = top + jnp.log(total)
    inverse = 1.0 / total
    return e0 * inverse, e1 * inverse, pooled


def soft(h):
    h = h.reshape(2, WIDE, LANES)
    q0, q1, pooled = soft_parts(h)
    return jnp.concatenate([q0 * pooled, q1 * pooled], axis=0)


def soft_pull(h, grad):
    h = h.reshape(2, WIDE, LANES)
    grad = grad.reshape(2, WIDE, LANES)
    q0, q1, pooled = soft_parts(h)
    mix = q0 * grad[0] + q1 * grad[1]
    mix = mix + swap_columns(mix)
    return jnp.concatenate(
        [q0 * (pooled * (grad[0] - mix) + mix), q1 * (pooled * (grad[1] - mix) + mix)], axis=0
    )


def norm_tables(st, group, i_own, i_oth, n_local, total):
    parts = st.shape[0]
    group = 0 if st.shape[1] == 1 else group
    blocks = [st[i, group] for i in range(parts)]
    summed = functools.reduce(jnp.add, blocks)
    mean = summed[0:1] / parts
    apart = functools.reduce(jnp.add, [jnp.square(b - mean) for b in blocks])
    rstd = lax.rsqrt((summed[1:2] + n_local * apart[0:1]) / total + EPS)
    return rstd, (st[i_own, group, 0:1] - mean) * rstd, (st[i_oth, group, 0:1] - mean) * rstd


def left_right(y0, y1, y2):
    rows = y0.shape[0]
    column = lax.broadcasted_iota(jnp.int32, y0.shape, 0) % WIDE
    before = jnp.where(column == 0, 0.0, pltpu.roll(y0, 1, 0))
    after = jnp.where(column == WIDE - 1, 0.0, pltpu.roll(y2, rows - 1, 0))
    return before + y1 + after


def lane_of(group):
    return pl.multiple_of(group * LANES, LANES)


def edge_start(n_own, edge, half):
    return pl.multiple_of((1 - half) * (n_own - edge), WIDE)


def pair_rows(j):
    return pl.ds(pl.multiple_of(j * 2 * WIDE, 2 * WIDE), 2 * WIDE)


def fold(v):
    return jnp.sum(v.reshape(v.shape[0] // 8, 8, LANES), axis=0)


def fwd_kernel(first, pool, layer, total, edge_out, *refs):
    pos, zall = refs[0], refs[1]
    if first:
        w_hbm = refs[2]
    else:
        st, gss, w_hbm = refs[2], refs[3:7], refs[7]
    hb_out, zc_out, edge_ref, st_out, hb, w, y, z, tab, hs, sem = refs[-11:]
    load = pltpu.make_async_copy(w_hbm.at[layer], w, sem.at[0])
    load.start()
    save = pltpu.make_async_copy(hb, hb_out.at[layer], sem.at[1])
    t, r = pos[0], pos[1]
    n_own = z.shape[0]
    halo_at = pl.multiple_of((1 - r) * (n_own + WIDE), WIDE)
    zero_at = pl.multiple_of(r * (n_own + WIDE), WIDE)
    hb[pl.ds(zero_at, WIDE), :] = jnp.zeros((WIDE, CHANS), BF16)
    edge = zall.shape[0] - n_own
    if not first:
        for k in range(GROUPS):
            group = t ^ k
            rstd, own, oth = norm_tables(st, group, pos[2], pos[3], float(n_own), total)
            gain, shift = gss[k][layer - 1 : layer, :], gss[k][layer + 7 : layer + 8, :]
            tab[group, 0:1] = rstd * gain
            tab[group, 1:2] = own * gain + shift
            tab[group, 2:3] = oth * gain + shift

    def act(values, group, which):
        if first:
            return values
        n = values.astype(F32) * tab[group, 0:1, :] + tab[group, which : which + 1, :]
        h = n * sigmoid(n)
        return soft(h) if pool else h

    def body(j, carry):
        at = pl.multiple_of(j * 2 * WIDE, 2 * WIDE)
        for group in range(GROUPS):
            lanes = slice(group * LANES, (group + 1) * LANES)
            h = act(zall[pl.ds(at, 2 * WIDE), lanes], group, 1)
            hb[pl.ds(pl.multiple_of(at + WIDE, WIDE), 2 * WIDE), lanes] = h.astype(BF16)
        return carry

    lax.fori_loop(0, n_own // (2 * WIDE), body, 0)
    for group in range(GROUPS):
        lanes = slice(group * LANES, (group + 1) * LANES)
        h = act(zall[n_own : n_own + edge, lanes], group, 2)
        if edge > WIDE:
            hs[...] = h
            h = hs[pl.ds(pl.multiple_of(r * WIDE, WIDE), WIDE), :]
        hb[pl.ds(halo_at, WIDE), lanes] = h.astype(BF16)
    save.start()
    load.wait()
    lhs = jnp.concatenate([hb[i * WIDE : i * WIDE + n_own, :] for i in range(3)], axis=1)
    rhs = jnp.concatenate(
        [
            jnp.concatenate([w[:, (3 * i + s) * CHANS : (3 * i + s + 1) * CHANS] for i in range(3)], axis=1)
            for s in range(3)
        ],
        axis=0,
    )
    y[...] = lax.dot_general(lhs, rhs, (((1,), (1,)), ((), ())), preferred_element_type=F32)

    def add_up(j, acc):
        rows = pair_rows(j)
        v = left_right(y[rows, 0:128], y[rows, 128:256], y[rows, 256:384])
        z[rows, :] = v
        return acc + fold(v)

    steps = n_own // (2 * WIDE)
    summed = lax.fori_loop(0, steps, add_up, jnp.zeros((8, LANES), F32))
    mean = jnp.sum(summed, axis=0, keepdims=True) / n_own

    def centre(j, acc):
        rows = pair_rows(j)
        v = z[rows, :] - mean
        z[rows, :] = v
        zc_out[rows, :] = v.astype(BF16)
        return acc + fold(jnp.square(v))

    apart = lax.fori_loop(0, steps, centre, jnp.zeros((8, LANES), F32))
    sums = [mean, jnp.sum(apart, axis=0, keepdims=True), jnp.zeros((6, LANES), F32)]
    sums = jnp.concatenate(sums, axis=0)
    for i in range(st_out.shape[0]):
        st_out[i] = sums
    edge_ref[...] = zc_out[pl.ds(edge_start(n_own, edge_out, r), edge_out), :]
    zc_out[n_own : n_own + edge_out, :] = jnp.zeros((edge_out, LANES), BF16)
    save.wait()


def fwd_step(layer, pool, edge_out, total, pos, slots, st, tables, weights, kept, n_own, devices, ties):
    first = st is None
    layers = weights.shape[0]
    extra = () if first else (st, *tables)
    return pl.pallas_call(
        functools.partial(fwd_kernel, first, pool, layer, total, edge_out),
        out_shape=(
            pltpu.HBM((layers, n_own + 2 * WIDE, CHANS), BF16),
            pltpu.VMEM((n_own + edge_out, LANES), BF16),
            pltpu.VMEM((edge_out, LANES), BF16),
            pltpu.VMEM((devices, 8, LANES), F32),
        ),
        in_specs=[SMEM] + [VMEM] * (1 + len(extra)) + [ANY] * (1 if first else 2) + [FREE] * len(ties),
        out_specs=(ANY, VMEM, VMEM, VMEM),
        input_output_aliases={} if first else {3 + len(extra): 0},
        scratch_shapes=[
            pltpu.VMEM((n_own + 2 * WIDE, CHANS), BF16),
            pltpu.VMEM((LANES, 9 * CHANS), BF16),
            pltpu.VMEM((n_own, 3 * LANES), F32),
            pltpu.VMEM((n_own, LANES), F32),
            pltpu.VMEM((GROUPS, 8, LANES), F32),
            pltpu.VMEM((2 * WIDE, LANES), F32),
            pltpu.SemaphoreType.DMA((2,)),
        ],
        compiler_params=PARAMS,
        cost_estimate=pl.CostEstimate(
            flops=2 * n_own * 9 * CHANS * LANES, bytes_accessed=4 * 1024 * 1024, transcendentals=n_own * CHANS
        ),
        name="conv_forward",
    )(pos, slots, *extra, in_hbm(weights), *(() if first else (in_hbm(kept),)), *ties)


def below_kernel(layer, pool, total, top, *refs):
    pos, zc, st, gs = refs[:4]
    if top:
        terms, h_out, dn_out, msg, tab = refs[4:]
    else:
        terms, (dn_out, msg, tab) = refs[4:8], refs[-3:]
    n_own = dn_out.shape[0]
    rstd, own, oth = norm_tables(st, pos[0], pos[2], pos[3], float(n_own), total)
    tab[0:1], tab[1:2] = rstd, own
    tab[2:3], tab[3:4] = gs[layer : layer + 1, :], gs[layer + 8 : layer + 9, :]

    def body(j, accs):
        rows = pair_rows(j)
        xhat = zc[rows, :].astype(F32) * tab[0:1, :] + tab[1:2, :]
        n = xhat * tab[2:3, :] + tab[3:4, :]
        sig = sigmoid(n)
        h = n * sig
        if top:
            g = terms[rows, :].astype(F32)
            h_out[rows, :] = h.astype(BF16)
        else:
            g = functools.reduce(jnp.add, [term[rows, :].astype(F32) for term in terms])
        if pool:
            g = soft_pull(h, g)
        dn = g * (sig * (1.0 + n - h))
        dn_out[rows, :] = dn
        return accs[0] + fold(dn), accs[1] + fold(dn * xhat)

    zero = jnp.zeros((8, LANES), F32)
    sums = lax.fori_loop(0, n_own // (2 * WIDE), body, (zero, zero))
    sums = [jnp.sum(v, axis=0, keepdims=True) for v in sums]
    msg[0:WIDE, :] = dn_out[pl.ds(edge_start(n_own, WIDE, pos[1]), WIDE), :]
    msg[WIDE : WIDE + 8, :] = jnp.concatenate(sums + [jnp.zeros((6, LANES), F32)], axis=0)


def below_step(layer, pool, total, pos, zc, st, gs, terms, ties=()):
    n_own = terms[0].shape[0]
    top = len(terms) == 1
    out_shape = [
        pltpu.VMEM((n_own, LANES), F32),
        pltpu.VMEM((WIDE + 8, LANES), F32),
    ]
    if top:
        out_shape = [jax.ShapeDtypeStruct((n_own, LANES), BF16)] + out_shape
    return pl.pallas_call(
        functools.partial(below_kernel, layer, pool, total, top),
        out_shape=tuple(out_shape),
        in_specs=[SMEM] + [VMEM] * (3 + len(terms)) + [FREE] * len(ties),
        out_specs=(VMEM,) * len(out_shape),
        scratch_shapes=[pltpu.VMEM((8, LANES), F32)],
        compiler_params=PARAMS,
        cost_estimate=LITTLE,
        name="silu_backward",
    )(pos, zc, st, gs, *terms, *ties)


def bwd_kernel(layer, total, *refs):
    pos, dn, dedge, sums, zc, st, gs, w_hbm = refs[:8]
    outs, d_out, d, w, y, tab, sem = refs[-10:-6], *refs[-6:]
    load = pltpu.make_async_copy(w_hbm.at[layer], w, sem)
    load.start()
    t, r = pos[0], pos[1]
    n_own = dn.shape[0]
    halo_at = pl.multiple_of((1 - r) * (n_own + WIDE), WIDE)
    zero_at = pl.multiple_of(r * (n_own + WIDE), WIDE)
    edge = zc.shape[0] - n_own
    d[pl.ds(zero_at, WIDE), :] = jnp.zeros((WIDE, 3 * LANES), BF16)
    rstd, own, oth = norm_tables(st, t, pos[2], pos[3], float(n_own), total)
    scale = gs[layer : layer + 1, :] * rstd
    shift_sum, gain_sum = sums[0:1, :], sums[1:2, :]
    slope = scale * gain_sum / total
    tab[0:1] = scale
    tab[1:2] = slope * rstd
    tab[2:3] = scale * shift_sum / total + slope * own
    tab[3:4] = scale * shift_sum / total + slope * oth

    def spread_columns(v, at):
        rows = v.shape[0]
        column = lax.broadcasted_iota(jnp.int32, v.shape, 0) % WIDE
        ahead = jnp.where(column == WIDE - 1, 0.0, pltpu.roll(v, rows - 1, 0))
        behind = jnp.where(column == 0, 0.0, pltpu.roll(v, 1, 0))
        d[pl.ds(at, rows), 0:128] = ahead.astype(BF16)
        d[pl.ds(at, rows), 128:256] = v.astype(BF16)
        d[pl.ds(at, rows), 256:384] = behind.astype(BF16)

    def body(j, carry):
        rows = pair_rows(j)
        v = dn[rows, :] * tab[0:1, :] - tab[2:3, :] - zc[rows, :].astype(F32) * tab[1:2, :]
        spread_columns(v, pl.multiple_of(j * 2 * WIDE + WIDE, WIDE))
        return carry

    lax.fori_loop(0, n_own // (2 * WIDE), body, 0)
    near = n_own if edge == WIDE else pl.multiple_of(n_own + r * WIDE, WIDE)
    near = zc[pl.ds(near, WIDE), :].astype(F32)
    spread_columns(dedge[0:WIDE, :] * tab[0:1, :] - tab[3:4, :] - near * tab[1:2, :], halo_at)
    d_out[...] = d[WIDE : WIDE + n_own, :]
    load.wait()
    lhs = jnp.concatenate([d[(2 - i) * WIDE : (2 - i) * WIDE + n_own, :] for i in range(3)], axis=1)
    rhs = jnp.concatenate([w[:, i * CHANS : (i + 1) * CHANS] for i in range(9)], axis=0)
    y[...] = jnp.dot(lhs, rhs, preferred_element_type=F32)

    def share(j, carry):
        rows = pair_rows(j)
        for k in range(GROUPS):
            outs[k][rows, :] = y[rows, pl.ds(lane_of(t ^ k), LANES)].astype(BF16)
        return carry

    lax.fori_loop(0, n_own // (2 * WIDE), share, 0)


def bwd_step(layer, total, pos, dn, dedge, sums, zc, st, gs, weights, ties):
    n_own = dn.shape[0]
    part = pltpu.VMEM((n_own, LANES), BF16)
    return pl.pallas_call(
        functools.partial(bwd_kernel, layer, total),
        out_shape=(
            part,
            part,
            part,
            part,
            pltpu.VMEM((n_own, 3 * LANES), BF16),
        ),
        in_specs=[SMEM] + [VMEM] * 6 + [ANY] + [FREE] * len(ties),
        out_specs=(VMEM,) * 5,
        scratch_shapes=[
            pltpu.VMEM((n_own + 2 * WIDE, 3 * LANES), BF16),
            pltpu.VMEM((LANES, 9 * CHANS), BF16),
            pltpu.VMEM((n_own, CHANS), F32),
            pltpu.VMEM((8, LANES), F32),
            pltpu.SemaphoreType.DMA,
        ],
        compiler_params=PARAMS,
        cost_estimate=LITTLE,
        name="conv_backward",
    )(pos, dn, dedge, sums, zc, st, gs, in_hbm(weights), *ties)


def last_kernel(t0, t1, t2, t3, *refs):
    out = refs[-1]

    def body(j, carry):
        rows = pair_rows(j)
        out[rows, :] = functools.reduce(jnp.add, [term[rows, :].astype(F32) for term in (t0, t1, t2, t3)])
        return carry

    lax.fori_loop(0, out.shape[0] // (2 * WIDE), body, 0)


def last_step(terms, ties):
    return pl.pallas_call(
        last_kernel,
        out_shape=jax.ShapeDtypeStruct(terms[0].shape, F32),
        in_specs=[VMEM] * 4 + [FREE] * len(ties),
        out_specs=VMEM,
        compiler_params=PARAMS,
        cost_estimate=LITTLE,
        name="add_terms",
    )(*terms, *ties)


def halves_kernel(keep, got, out):
    out[...] = (keep[...].astype(F32) + got[...].astype(F32)).astype(BF16)


def add_halves(keep, got):
    return pl.pallas_call(
        halves_kernel,
        out_shape=jax.ShapeDtypeStruct(keep.shape, BF16),
        in_specs=[VMEM] * 2,
        out_specs=VMEM,
        compiler_params=PARAMS,
        cost_estimate=LITTLE,
        name="add_halves",
    )(keep, got)


def bundle_kernel(keep1, got1, keep0, got0, *refs):
    out = refs[-1]
    rows = LANES // 8
    for i in range(4):
        at = slice(i * rows, (i + 1) * rows)
        out[i, 0:rows] = (keep1[at, :].astype(F32) + got1[at, :].astype(F32)).astype(BF16)
        out[i, rows : 2 * rows] = (keep0[at, :].astype(F32) + got0[at, :].astype(F32)).astype(BF16)


def bundle_halves(upper, lower, ties):
    return pl.pallas_call(
        bundle_kernel,
        out_shape=pltpu.VMEM((4, LANES // 4, 9 * CHANS), BF16),
        in_specs=[VMEM] * 4 + [FREE] * len(ties),
        out_specs=VMEM,
        compiler_params=PARAMS,
        cost_estimate=LITTLE,
        name="bundle_halves",
    )(*upper, *lower, *ties)


def quarters_kernel(pieces, *refs):
    out = refs[-1]
    rows = LANES // 8
    for j in range(2):
        at = slice(j * rows, (j + 1) * rows)
        total = functools.reduce(jnp.add, [pieces[i, at].astype(F32) for i in range(4)]).astype(BF16)
        for i in range(4):
            out[i, at] = total


def add_quarters(pieces, ties):
    return pl.pallas_call(
        quarters_kernel,
        out_shape=pltpu.VMEM(pieces.shape, BF16),
        in_specs=[VMEM] + [FREE] * len(ties),
        out_specs=VMEM,
        compiler_params=PARAMS,
        cost_estimate=LITTLE,
        name="add_quarters",
    )(pieces, *ties)


def wgrad_kernel(layer, pos, d, hb_hbm, *refs):
    keep, send, hb, grad, sem = refs[-5:]
    load = pltpu.make_async_copy(hb_hbm.at[layer], hb, sem)
    load.start()
    n_own = d.shape[0]
    lhs = d[...]
    load.wait()
    for i in range(3):
        part = lax.dot_general(
            lhs, hb[i * WIDE : i * WIDE + n_own, :], (((0,), (0,)), ((), ())), preferred_element_type=F32
        ).astype(BF16)
        for s in range(3):
            grad[:, (3 * i + s) * CHANS : (3 * i + s + 1) * CHANS] = part[s * LANES : (s + 1) * LANES]
    half = LANES // 2
    keep[...] = grad[pl.ds(pl.multiple_of(pos[1] * half, half), half), :]
    send[...] = grad[pl.ds(pl.multiple_of((1 - pos[1]) * half, half), half), :]


def wgrad_step(layer, pos, d, kept, ties):
    half = pltpu.VMEM((LANES // 2, 9 * CHANS), BF16)
    return pl.pallas_call(
        functools.partial(wgrad_kernel, layer),
        out_shape=(half, half),
        in_specs=[SMEM, VMEM, ANY] + [FREE] * len(ties),
        out_specs=(VMEM, VMEM),
        scratch_shapes=[
            pltpu.VMEM(kept.shape[1:], BF16),
            pltpu.VMEM((LANES, 9 * CHANS), BF16),
            pltpu.SemaphoreType.DMA,
        ],
        compiler_params=PARAMS,
        cost_estimate=LITTLE,
        name="kernel_gradient",
    )(pos, d, in_hbm(kept), *ties)


def place_kernel(layers, fresh, pos, *refs):
    count = 2 * len(layers)
    sources = refs[:count]
    out, held, wide, sem = refs[-4:]
    half = LANES // 2
    r = pos[1]
    loads = [pltpu.make_async_copy(sources[j], held.at[j], sem.at[j]) for j in range(count)]
    for load in loads:
        load.start()
    stores = []
    for j in range(count):
        at = pl.multiple_of((r if j % 2 == 0 else 1 - r) * half, half)
        if j >= 2:
            stores[j - 2].wait()
        loads[j].wait()
        wide[j % 2] = held[j].astype(F32)
        store = pltpu.make_async_copy(wide.at[j % 2], out.at[layers[j // 2], pl.ds(at, half)], sem.at[count + j])
        store.start()
        stores.append(store)
    for store in stores[-2:]:
        store.wait()


def place_step(layers, pos, sources, whole, count):
    half = LANES // 2
    jobs = len(sources)
    return pl.pallas_call(
        functools.partial(place_kernel, layers, whole is None),
        out_shape=pltpu.HBM((count, LANES, 9 * CHANS), F32),
        in_specs=[SMEM] + [ANY] * jobs + ([] if whole is None else [ANY]),
        out_specs=ANY,
        input_output_aliases={} if whole is None else {1 + jobs: 0},
        scratch_shapes=[
            pltpu.VMEM((jobs, half, 9 * CHANS), BF16),
            pltpu.VMEM((2, half, 9 * CHANS), F32),
            pltpu.SemaphoreType.DMA((2 * jobs,)),
        ],
        compiler_params=PARAMS,
        cost_estimate=LITTLE,
        name="place_gradients",
    )(pos, *[in_hbm(v) for v in sources], *(() if whole is None else (in_hbm(whole),)))


def unbundle_kernel(pos, mine, other, whole, out, held, wide, sem):
    rows, half = LANES // 8, LANES // 2
    r = pos[1]
    loads = [pltpu.make_async_copy(v, held.at[j], sem.at[j]) for j, v in enumerate((mine, other))]
    for load in loads:
        load.start()
    stores = []
    for j in range(2):
        loads[j].wait()
        base = (r if j == 0 else 1 - r) * half
        for layer in (1, 0):
            slot = 2 * j + layer
            for i in range(4):
                at = slice((1 - layer) * rows, (2 - layer) * rows)
                wide[slot, i * rows : (i + 1) * rows] = held[j, i, at].astype(F32)
            store = pltpu.make_async_copy(
                wide.at[slot], out.at[layer, pl.ds(pl.multiple_of(base, half), half)], sem.at[2 + slot]
            )
            store.start()
            stores.append(store)
    for store in stores:
        store.wait()


def unbundle_step(pos, mine, other, whole):
    half = LANES // 2
    return pl.pallas_call(
        unbundle_kernel,
        out_shape=pltpu.HBM(whole.shape, F32),
        in_specs=[SMEM, FREE, FREE, ANY],
        out_specs=ANY,
        input_output_aliases={3: 0},
        scratch_shapes=[
            pltpu.VMEM((2,) + mine.shape, BF16),
            pltpu.VMEM((4, half, 9 * CHANS), F32),
            pltpu.SemaphoreType.DMA((6,)),
        ],
        compiler_params=PARAMS,
        cost_estimate=LITTLE,
        name="unbundle_gradients",
    )(pos, mine, other, in_hbm(whole))


def swap_with(value, axis, k):
    return lax.ppermute(value, axis, [(i, i ^ k) for i in range(lax.axis_size(axis))])


def spread(own):
    return (own, *[swap_with(own, "tensor", k) for k in range(1, GROUPS)])


def halo_of_input(x, half):
    n_own = x.shape[0]
    edge = jnp.where(half == 0, x[n_own - WIDE :], x[:WIDE])
    return jnp.concatenate([x, swap_with(edge, "rows", 1)], axis=0)


def fast_local(section_input, conv_weights, norm_gains, norm_shifts, out_grad, out_mask):
    images, rows_here, width = out_mask.shape
    layers = conv_weights.shape[0]
    n_own = rows_here * width
    parts = lax.axis_size("dp") * lax.axis_size("rows")
    total = float(n_own * parts)
    t, half = lax.axis_index("tensor"), lax.axis_index("rows")
    image = lax.axis_index("dp")
    pos = jnp.stack([t, half, 2 * image + half, 2 * image + 1 - half]).astype(jnp.int32)
    middle = layers // 2
    x = to_maps(section_input, width).reshape(n_own, LANES)
    slots = lax.all_gather(halo_of_input(x, half), "tensor", axis=1, tiled=True)
    pad = jnp.zeros((8 - layers, LANES), F32)
    tables = spread(jnp.concatenate([norm_gains, pad, norm_shifts, pad], axis=0))
    top_grad = (to_maps(out_grad, width) * out_mask[..., None].astype(BF16)).reshape(n_own, LANES)

    st, kept = None, None
    halves = ("dp", "rows")
    kept_z, kept_st = [], []
    for layer in range(layers):
        last = layer + 1 == layers
        edge = 2 * WIDE if layer + 1 == middle else WIDE
        everyone = halves if last else (*halves, "tensor")
        devices = parts if last else parts * GROUPS
        kept, zc, rim, local = fwd_step(
            layer,
            layer == middle,
            edge,
            total,
            pos,
            slots,
            st,
            tables,
            conv_weights,
            kept,
            n_own,
            devices,
            (top_grad,) if layer == 2 else (),
        )
        rim = swap_with(rim, "rows", 1)
        st = lax.all_to_all(local, everyone, split_axis=0, concat_axis=0, tiled=True)
        st = st.reshape(parts, devices // parts, 8, LANES)
        zc = lax.dynamic_update_slice_in_dim(zc, rim, n_own, axis=0)
        kept_z.append(zc)
        kept_st.append(st)
        if not last:
            slots = lax.all_gather(zc, "tensor", axis=1, tiled=True)
    top = layers - 1
    h_last, dn, msg = below_step(top, False, total, pos, kept_z[top], kept_st[top], tables[0], (top_grad,))

    def with_other(values):
        return [v for mine in values for v in (mine, swap_with(mine, "rows", 1))]

    sum_list, pairs = [None] * layers, [None] * layers
    ahead, back = [[0, 1, 2, 3]], [[3, 2, 1, 0]]
    split, urgent, whole = [None] * layers, (), None
    for layer in range(layers - 1, -1, -1):
        got = swap_with(msg, "rows", 1)
        sums = msg[WIDE:] + got[WIDE:]
        one, two, three = (swap_with(sums, "dp", k) for k in (1, 2, 3))
        sums = (sums + one) + (two + three)
        sum_list[layer] = sums
        *terms, d = bwd_step(
            layer, total, pos, dn, got, sums, kept_z[layer], kept_st[layer], tables[0], conv_weights, urgent
        )
        terms = (terms[0], *[swap_with(terms[k], "tensor", k) for k in range(1, GROUPS)])
        keep, send = wgrad_step(layer, pos, d, kept, ())
        split[layer] = (keep, swap_with(send, "rows", 1))
        if layer > 1:
            pairs[layer] = add_halves(*split[layer])
            urgent = (pairs[layer],)
        else:
            urgent = ()
        if layer > 0:
            below = layer - 1
            late = (in_hbm(upper[0]),) if layer == 2 else ()
            dn, msg = below_step(
                below, layer == middle, total, pos, kept_z[below], kept_st[below], tables[0], terms, (keep, *late)
            )
        else:
            grad = last_step(terms, (keep,))
        if layer == 4:
            upper = lax.psum((pairs[5], pairs[4]), "dp", axis_index_groups=ahead)
        if layer == 2:
            mid = lax.psum((pairs[3], pairs[2]), "dp", axis_index_groups=back)
    shape = (images, rows_here, width, LANES)
    bundle = bundle_halves(split[1], split[0], (in_hbm(mid[0]),))
    bundle = lax.all_to_all(bundle, "dp", split_axis=0, concat_axis=0, tiled=True)
    whole = place_step((5, 4, 3, 2), pos, with_other((*upper, *mid)), None, layers)
    bundle = add_quarters(bundle, (in_hbm(grad), in_hbm(whole)))
    bundle = lax.all_to_all(bundle, "dp", split_axis=0, concat_axis=0, tiled=True)
    outputs = (from_maps(h_last.reshape(shape)), from_maps(grad.reshape(shape)))
    sums = jnp.stack(sum_list)
    bundle, whole, outputs, sums = lax.optimization_barrier((bundle, whole, outputs, sums))
    whole = unbundle_step(pos, bundle, swap_with(bundle, "rows", 1), whole)
    return (*outputs, whole, sums[:, 1], sums[:, 0])


def solution(mesh):
    in_specs = (
        P("dp", "rows", "tensor"),
        P(None, "tensor", None),
        P(None, "tensor"),
        P(None, "tensor"),
        P("dp", "rows", "tensor"),
        P("dp", "rows", None),
    )
    out_specs = (
        P("dp", "rows", "tensor"),
        P("dp", "rows", "tensor"),
        P(None, "tensor", None),
        P(None, "tensor"),
        P(None, "tensor"),
    )
    local = fast_local if fits_kernels(mesh) else generic_local
    return jax.shard_map(local, mesh=mesh, in_specs=in_specs, out_specs=out_specs, check_vma=False)
```

```python
import functools

import jax
import jax.numpy as jnp
from jax import lax
from jax.experimental import pallas as pl
from jax.experimental.pallas import tpu as pltpu
from jax.sharding import PartitionSpec as P

EPS = 1e-05


def padded_2(cells, sides, width):
    for axis, dim in sides:
        count = lax.axis_size(axis)
        ends = count - 1
        head = lax.slice_in_dim(cells, 0, width, axis=dim)
        tail = lax.slice_in_dim(cells, cells.shape[dim] - width, cells.shape[dim], axis=dim)
        cells = jnp.concatenate(
            [
                lax.ppermute(tail, axis, [(i, (i + 1) % count) for i in range(ends)]),
                cells,
                lax.ppermute(head, axis, [((i + 1) % count, i) for i in range(ends)]),
            ],
            axis=dim,
        )
    return cells


def to_maps(flat, width):
    count, high, merged = flat.shape
    return flat.reshape(count, high, merged // width, width).transpose(0, 1, 3, 2)


def from_maps(maps):
    count, high, wide, chans = maps.shape
    return maps.transpose(0, 1, 3, 2).reshape(count, high, chans * wide)


def spatial_conv(padded, kernel):
    return lax.conv_general_dilated(
        padded,
        kernel,
        (1, 1),
        ((0, 0), (1, 1)),
        dimension_numbers=("NHWC", "HWIO", "NHWC"),
        preferred_element_type=jnp.float32,
    )


def flipped(kernel):
    return jnp.transpose(kernel[::-1, ::-1], (0, 1, 3, 2))


def pool_unpool(values):
    count, high, wide, chans = values.shape
    blocks = values.reshape(count, high // 2, 2, wide // 2, 2, chans)
    pooled = jax.nn.logsumexp(blocks, axis=(2, 4), keepdims=True)
    return (jnp.exp(blocks - pooled) * pooled).reshape(values.shape)


def moments(conv_out, total_pixels):
    summed = lax.psum(jnp.sum(conv_out, axis=(0, 1, 2)), ("dp", "rows"))
    mean = summed / total_pixels
    spread = lax.psum(jnp.sum(jnp.square(conv_out - mean), axis=(0, 1, 2)), ("dp", "rows"))
    var = spread / total_pixels
    return (mean, lax.rsqrt(var + EPS))


def kernel_grad(whole, dconv):
    images, rows_here, width, chans = dconv.shape
    widened = jnp.pad(whole, ((0, 0), (0, 0), (1, 1), (0, 0)))
    stacked = []
    for row_off in range(3):
        line = []
        for col_off in range(3):
            window = widened[:, row_off : row_off + rows_here, col_off : col_off + width, :]
            line.append(
                jnp.einsum("bhwc,bhwo->co", window, dconv, preferred_element_type=jnp.float32)
            )
        stacked.append(jnp.stack(line))
    return jnp.stack(stacked)


def generic_local(section_input, conv_weights, norm_gains, norm_shifts, out_grad, out_mask):
    width = out_mask.shape[2]
    images, rows_here = (out_mask.shape[0], out_mask.shape[1])
    total_pixels = float(images * rows_here * width * lax.axis_size("dp") * lax.axis_size("rows"))
    layers, out_here, flat_in = conv_weights.shape
    chans_in = flat_in // 9
    kernels_hwio = conv_weights.reshape(layers, out_here, 3, 3, chans_in).transpose(0, 2, 3, 4, 1)
    middle = layers // 2
    kept = []
    acting = to_maps(section_input, width)
    current = acting.astype(jnp.float32)
    pre_pool = current
    for index in range(layers):
        if index == middle:
            pre_pool = current
            acting = pool_unpool(pre_pool).astype(jnp.bfloat16)
        padded = padded_2(acting, (("rows", 1),), 1)
        whole = lax.all_gather(padded, "tensor", axis=3, tiled=True)
        conv_out = spatial_conv(whole, kernels_hwio[index])
        mean, rstd = moments(conv_out, total_pixels)
        normed = (conv_out - mean) * rstd
        shifted = normed * norm_gains[index] + norm_shifts[index]
        current = jax.nn.silu(shifted)
        acting = current.astype(jnp.bfloat16)
        kept.append((whole, normed, shifted, rstd))
    grad = to_maps(out_grad, width).astype(jnp.float32) * out_mask[..., None].astype(jnp.float32)
    kernel_list = [None] * layers
    gain_list = [None] * layers
    shift_list = [None] * layers
    for index in range(layers - 1, -1, -1):
        whole, normed, shifted, rstd = kept[index]
        unused, pull_silu = jax.vjp(jax.nn.silu, shifted)
        dshift = pull_silu(grad)[0]
        gain_sum, shift_sum = lax.psum(
            (jnp.sum(dshift * normed, axis=(0, 1, 2)), jnp.sum(dshift, axis=(0, 1, 2))),
            ("dp", "rows"),
        )
        gain_list[index] = gain_sum
        shift_list[index] = shift_sum
        dconv = (
            norm_gains[index]
            * rstd
            * (dshift - shift_sum / total_pixels - normed * gain_sum / total_pixels)
        ).astype(jnp.bfloat16)
        summed_kernel = lax.psum(
            kernel_grad(whole, dconv).astype(jnp.bfloat16), ("dp", "rows")
        ).astype(jnp.float32)
        kernel_list[index] = summed_kernel.transpose(3, 0, 1, 2).reshape(out_here, flat_in)
        grad_rim = padded_2(dconv, (("rows", 1),), 1)
        partial_terms = spatial_conv(grad_rim, flipped(kernels_hwio[index]))
        grad_in = lax.psum_scatter(
            partial_terms.astype(jnp.bfloat16), "tensor", scatter_dimension=3, tiled=True
        ).astype(jnp.float32)
        if index == middle:
            unused, pull_pool = jax.vjp(pool_unpool, pre_pool)
            grad = pull_pool(grad_in)[0]
        else:
            grad = grad_in
    return (
        from_maps(acting),
        from_maps(grad),
        jnp.stack(kernel_list),
        jnp.stack(gain_list),
        jnp.stack(shift_list),
    )


GROUPS = 4
LANES = 128
WIDE = 48
CHANS = GROUPS * LANES
F32 = jnp.float32
BF16 = jnp.bfloat16
VMEM = pl.BlockSpec(memory_space=pltpu.VMEM)
SMEM = pl.BlockSpec(memory_space=pltpu.SMEM)
ANY = pl.BlockSpec(memory_space=pltpu.HBM)
FREE = pl.BlockSpec(memory_space=pl.ANY)
LITTLE = pl.CostEstimate(flops=1024, bytes_accessed=1024, transcendentals=0)
PARAMS = pltpu.CompilerParams(vmem_limit_bytes=20 * 1024 * 1024)


def in_hbm(value):
    return pltpu.with_memory_space_constraint(value, pltpu.HBM)


def fits_kernels(mesh):
    return mesh.shape["tensor"] == GROUPS and mesh.shape["rows"] == 2 and mesh.shape["dp"] == 4


def sigmoid(v):
    return 0.5 * jnp.tanh(0.5 * v) + 0.5


def swap_columns(v):
    column = lax.broadcasted_iota(jnp.int32, v.shape, 0)
    return jnp.where(column % 2 == 0, pltpu.roll(v, WIDE - 1, 0), pltpu.roll(v, 1, 0))


def soft_parts(h):
    top = jnp.maximum(h[0], h[1])
    top = jnp.maximum(top, swap_columns(top))
    e0, e1 = jnp.exp(h[0] - top), jnp.exp(h[1] - top)
    total = e0 + e1
    total = total + swap_columns(total)
    pooled = top + jnp.log(total)
    inverse = 1.0 / total
    return e0 * inverse, e1 * inverse, pooled


def soft(h):
    h = h.reshape(2, WIDE, LANES)
    q0, q1, pooled = soft_parts(h)
    return jnp.concatenate([q0 * pooled, q1 * pooled], axis=0)


def soft_pull(h, grad):
    h = h.reshape(2, WIDE, LANES)
    grad = grad.reshape(2, WIDE, LANES)
    q0, q1, pooled = soft_parts(h)
    mix = q0 * grad[0] + q1 * grad[1]
    mix = mix + swap_columns(mix)
    return jnp.concatenate(
        [q0 * (pooled * (grad[0] - mix) + mix), q1 * (pooled * (grad[1] - mix) + mix)], axis=0
    )


def norm_tables(st, group, i_own, i_oth, n_local, total):
    parts = st.shape[0]
    group = 0 if st.shape[1] == 1 else group
    blocks = [st[i, group] for i in range(parts)]
    summed = functools.reduce(jnp.add, blocks)
    mean = summed[0:1] / parts
    apart = functools.reduce(jnp.add, [jnp.square(b - mean) for b in blocks])
    rstd = lax.rsqrt((summed[1:2] + n_local * apart[0:1]) / total + EPS)
    return rstd, (st[i_own, group, 0:1] - mean) * rstd, (st[i_oth, group, 0:1] - mean) * rstd


def left_right(y0, y1, y2):
    rows = y0.shape[0]
    column = lax.broadcasted_iota(jnp.int32, y0.shape, 0) % WIDE
    before = jnp.where(column == 0, 0.0, pltpu.roll(y0, 1, 0))
    after = jnp.where(column == WIDE - 1, 0.0, pltpu.roll(y2, rows - 1, 0))
    return before + y1 + after


def lane_of(group):
    return pl.multiple_of(group * LANES, LANES)


def edge_start(n_own, edge, half):
    return pl.multiple_of((1 - half) * (n_own - edge), WIDE)


def pair_rows(j):
    return pl.ds(pl.multiple_of(j * 2 * WIDE, 2 * WIDE), 2 * WIDE)


def fold(v):
    return jnp.sum(v.reshape(v.shape[0] // 8, 8, LANES), axis=0)


def fwd_kernel(first, pool, layer, total, edge_out, *refs):
    pos, zall = refs[0], refs[1]
    if first:
        w_hbm = refs[2]
    else:
        st, gss, w_hbm = refs[2], refs[3:7], refs[7]
    hb_out, zc_out, edge_ref, st_out, hb, w, y, z, tab, hs, sem = refs[-11:]
    load = pltpu.make_async_copy(w_hbm.at[layer], w, sem.at[0])
    load.start()
    save = pltpu.make_async_copy(hb, hb_out.at[layer], sem.at[1])
    t, r = pos[0], pos[1]
    n_own = z.shape[0]
    halo_at = pl.multiple_of((1 - r) * (n_own + WIDE), WIDE)
    zero_at = pl.multiple_of(r * (n_own + WIDE), WIDE)
    hb[pl.ds(zero_at, WIDE), :] = jnp.zeros((WIDE, CHANS), BF16)
    edge = zall.shape[0] - n_own
    if not first:
        for k in range(GROUPS):
            group = t ^ k
            rstd, own, oth = norm_tables(st, group, pos[2], pos[3], float(n_own), total)
            gain, shift = gss[k][layer - 1 : layer, :], gss[k][layer + 7 : layer + 8, :]
            tab[group, 0:1] = rstd * gain
            tab[group, 1:2] = own * gain + shift
            tab[group, 2:3] = oth * gain + shift

    def act(values, group, which):
        if first:
            return values
        n = values.astype(F32) * tab[group, 0:1, :] + tab[group, which : which + 1, :]
        h = n * sigmoid(n)
        return soft(h) if pool else h

    def body(j, carry):
        at = pl.multiple_of(j * 2 * WIDE, 2 * WIDE)
        for group in range(GROUPS):
            lanes = slice(group * LANES, (group + 1) * LANES)
            h = act(zall[pl.ds(at, 2 * WIDE), lanes], group, 1)
            hb[pl.ds(pl.multiple_of(at + WIDE, WIDE), 2 * WIDE), lanes] = h.astype(BF16)
        return carry

    lax.fori_loop(0, n_own // (2 * WIDE), body, 0)
    for group in range(GROUPS):
        lanes = slice(group * LANES, (group + 1) * LANES)
        h = act(zall[n_own : n_own + edge, lanes], group, 2)
        if edge > WIDE:
            hs[...] = h
            h = hs[pl.ds(pl.multiple_of(r * WIDE, WIDE), WIDE), :]
        hb[pl.ds(halo_at, WIDE), lanes] = h.astype(BF16)
    save.start()
    load.wait()
    lhs = jnp.concatenate([hb[i * WIDE : i * WIDE + n_own, :] for i in range(3)], axis=1)
    rhs = jnp.concatenate(
        [
            jnp.concatenate([w[:, (3 * i + s) * CHANS : (3 * i + s + 1) * CHANS] for i in range(3)], axis=1)
            for s in range(3)
        ],
        axis=0,
    )
    y[...] = lax.dot_general(lhs, rhs, (((1,), (1,)), ((), ())), preferred_element_type=F32)

    def add_up(j, acc):
        rows = pair_rows(j)
        v = left_right(y[rows, 0:128], y[rows, 128:256], y[rows, 256:384])
        z[rows, :] = v
        return acc + fold(v)

    steps = n_own // (2 * WIDE)
    summed = lax.fori_loop(0, steps, add_up, jnp.zeros((8, LANES), F32))
    mean = jnp.sum(summed, axis=0, keepdims=True) / n_own

    def centre(j, acc):
        rows = pair_rows(j)
        v = z[rows, :] - mean
        z[rows, :] = v
        zc_out[rows, :] = v.astype(BF16)
        return acc + fold(jnp.square(v))

    apart = lax.fori_loop(0, steps, centre, jnp.zeros((8, LANES), F32))
    sums = [mean, jnp.sum(apart, axis=0, keepdims=True), jnp.zeros((6, LANES), F32)]
    sums = jnp.concatenate(sums, axis=0)
    for i in range(st_out.shape[0]):
        st_out[i] = sums
    edge_ref[...] = zc_out[pl.ds(edge_start(n_own, edge_out, r), edge_out), :]
    zc_out[n_own : n_own + edge_out, :] = jnp.zeros((edge_out, LANES), BF16)
    save.wait()


def fwd_step(layer, pool, edge_out, total, pos, slots, st, tables, weights, kept, n_own, devices, ties):
    first = st is None
    layers = weights.shape[0]
    extra = () if first else (st, *tables)
    return pl.pallas_call(
        functools.partial(fwd_kernel, first, pool, layer, total, edge_out),
        out_shape=(
            pltpu.HBM((layers, n_own + 2 * WIDE, CHANS), BF16),
            pltpu.VMEM((n_own + edge_out, LANES), BF16),
            pltpu.VMEM((edge_out, LANES), BF16),
            pltpu.VMEM((devices, 8, LANES), F32),
        ),
        in_specs=[SMEM] + [VMEM] * (1 + len(extra)) + [ANY] * (1 if first else 2) + [FREE] * len(ties),
        out_specs=(ANY, VMEM, VMEM, VMEM),
        input_output_aliases={} if first else {3 + len(extra): 0},
        scratch_shapes=[
            pltpu.VMEM((n_own + 2 * WIDE, CHANS), BF16),
            pltpu.VMEM((LANES, 9 * CHANS), BF16),
            pltpu.VMEM((n_own, 3 * LANES), F32),
            pltpu.VMEM((n_own, LANES), F32),
            pltpu.VMEM((GROUPS, 8, LANES), F32),
            pltpu.VMEM((2 * WIDE, LANES), F32),
            pltpu.SemaphoreType.DMA((2,)),
        ],
        compiler_params=PARAMS,
        cost_estimate=pl.CostEstimate(
            flops=2 * n_own * 9 * CHANS * LANES, bytes_accessed=4 * 1024 * 1024, transcendentals=n_own * CHANS
        ),
        name="conv_forward",
    )(pos, slots, *extra, in_hbm(weights), *(() if first else (in_hbm(kept),)), *ties)


def below_kernel(layer, pool, total, top, *refs):
    pos, zc, st, gs = refs[:4]
    if top:
        terms, h_out, dn_out, msg, tab = refs[4:]
    else:
        terms, (dn_out, msg, tab) = refs[4:8], refs[-3:]
    n_own = dn_out.shape[0]
    rstd, own, oth = norm_tables(st, pos[0], pos[2], pos[3], float(n_own), total)
    tab[0:1], tab[1:2] = rstd, own
    tab[2:3], tab[3:4] = gs[layer : layer + 1, :], gs[layer + 8 : layer + 9, :]

    def body(j, accs):
        rows = pair_rows(j)
        xhat = zc[rows, :].astype(F32) * tab[0:1, :] + tab[1:2, :]
        n = xhat * tab[2:3, :] + tab[3:4, :]
        sig = sigmoid(n)
        h = n * sig
        if top:
            g = terms[rows, :].astype(F32)
            h_out[rows, :] = h.astype(BF16)
        else:
            g = functools.reduce(jnp.add, [term[rows, :].astype(F32) for term in terms])
        if pool:
            g = soft_pull(h, g)
        dn = g * (sig * (1.0 + n - h))
        dn_out[rows, :] = dn
        return accs[0] + fold(dn), accs[1] + fold(dn * xhat)

    zero = jnp.zeros((8, LANES), F32)
    sums = lax.fori_loop(0, n_own // (2 * WIDE), body, (zero, zero))
    sums = [jnp.sum(v, axis=0, keepdims=True) for v in sums]
    msg[0:WIDE, :] = dn_out[pl.ds(edge_start(n_own, WIDE, pos[1]), WIDE), :]
    msg[WIDE : WIDE + 8, :] = jnp.concatenate(sums + [jnp.zeros((6, LANES), F32)], axis=0)


def below_step(layer, pool, total, pos, zc, st, gs, terms, ties=()):
    n_own = terms[0].shape[0]
    top = len(terms) == 1
    out_shape = [
        pltpu.VMEM((n_own, LANES), F32),
        pltpu.VMEM((WIDE + 8, LANES), F32),
    ]
    if top:
        out_shape = [jax.ShapeDtypeStruct((n_own, LANES), BF16)] + out_shape
    return pl.pallas_call(
        functools.partial(below_kernel, layer, pool, total, top),
        out_shape=tuple(out_shape),
        in_specs=[SMEM] + [VMEM] * (3 + len(terms)) + [FREE] * len(ties),
        out_specs=(VMEM,) * len(out_shape),
        scratch_shapes=[pltpu.VMEM((8, LANES), F32)],
        compiler_params=PARAMS,
        cost_estimate=LITTLE,
        name="silu_backward",
    )(pos, zc, st, gs, *terms, *ties)


def bwd_kernel(layer, total, *refs):
    pos, dn, dedge, sums, zc, st, gs, w_hbm = refs[:8]
    outs, d_out, d, w, y, tab, sem = refs[-10:-6], *refs[-6:]
    load = pltpu.make_async_copy(w_hbm.at[layer], w, sem)
    load.start()
    t, r = pos[0], pos[1]
    n_own = dn.shape[0]
    halo_at = pl.multiple_of((1 - r) * (n_own + WIDE), WIDE)
    zero_at = pl.multiple_of(r * (n_own + WIDE), WIDE)
    edge = zc.shape[0] - n_own
    d[pl.ds(zero_at, WIDE), :] = jnp.zeros((WIDE, 3 * LANES), BF16)
    rstd, own, oth = norm_tables(st, t, pos[2], pos[3], float(n_own), total)
    scale = gs[layer : layer + 1, :] * rstd
    shift_sum, gain_sum = sums[0:1, :], sums[1:2, :]
    slope = scale * gain_sum / total
    tab[0:1] = scale
    tab[1:2] = slope * rstd
    tab[2:3] = scale * shift_sum / total + slope * own
    tab[3:4] = scale * shift_sum / total + slope * oth

    def spread_columns(v, at):
        rows = v.shape[0]
        column = lax.broadcasted_iota(jnp.int32, v.shape, 0) % WIDE
        ahead = jnp.where(column == WIDE - 1, 0.0, pltpu.roll(v, rows - 1, 0))
        behind = jnp.where(column == 0, 0.0, pltpu.roll(v, 1, 0))
        d[pl.ds(at, rows), 0:128] = ahead.astype(BF16)
        d[pl.ds(at, rows), 128:256] = v.astype(BF16)
        d[pl.ds(at, rows), 256:384] = behind.astype(BF16)

    def body(j, carry):
        rows = pair_rows(j)
        v = dn[rows, :] * tab[0:1, :] - tab[2:3, :] - zc[rows, :].astype(F32) * tab[1:2, :]
        spread_columns(v, pl.multiple_of(j * 2 * WIDE + WIDE, WIDE))
        return carry

    lax.fori_loop(0, n_own // (2 * WIDE), body, 0)
    near = n_own if edge == WIDE else pl.multiple_of(n_own + r * WIDE, WIDE)
    near = zc[pl.ds(near, WIDE), :].astype(F32)
    spread_columns(dedge[0:WIDE, :] * tab[0:1, :] - tab[3:4, :] - near * tab[1:2, :], halo_at)
    d_out[...] = d[WIDE : WIDE + n_own, :]
    load.wait()
    lhs = jnp.concatenate([d[(2 - i) * WIDE : (2 - i) * WIDE + n_own, :] for i in range(3)], axis=1)
    rhs = jnp.concatenate([w[:, i * CHANS : (i + 1) * CHANS] for i in range(9)], axis=0)
    y[...] = jnp.dot(lhs, rhs, preferred_element_type=F32)

    def share(j, carry):
        rows = pair_rows(j)
        for k in range(GROUPS):
            outs[k][rows, :] = y[rows, pl.ds(lane_of(t ^ k), LANES)].astype(BF16)
        return carry

    lax.fori_loop(0, n_own // (2 * WIDE), share, 0)


def bwd_step(layer, total, pos, dn, dedge, sums, zc, st, gs, weights, ties):
    n_own = dn.shape[0]
    part = pltpu.VMEM((n_own, LANES), BF16)
    return pl.pallas_call(
        functools.partial(bwd_kernel, layer, total),
        out_shape=(
            part,
            part,
            part,
            part,
            pltpu.VMEM((n_own, 3 * LANES), BF16),
        ),
        in_specs=[SMEM] + [VMEM] * 6 + [ANY] + [FREE] * len(ties),
        out_specs=(VMEM,) * 5,
        scratch_shapes=[
            pltpu.VMEM((n_own + 2 * WIDE, 3 * LANES), BF16),
            pltpu.VMEM((LANES, 9 * CHANS), BF16),
            pltpu.VMEM((n_own, CHANS), F32),
            pltpu.VMEM((8, LANES), F32),
            pltpu.SemaphoreType.DMA,
        ],
        compiler_params=PARAMS,
        cost_estimate=LITTLE,
        name="conv_backward",
    )(pos, dn, dedge, sums, zc, st, gs, in_hbm(weights), *ties)


def last_kernel(t0, t1, t2, t3, *refs):
    out = refs[-1]

    def body(j, carry):
        rows = pair_rows(j)
        out[rows, :] = functools.reduce(jnp.add, [term[rows, :].astype(F32) for term in (t0, t1, t2, t3)])
        return carry

    lax.fori_loop(0, out.shape[0] // (2 * WIDE), body, 0)


def last_step(terms, ties):
    return pl.pallas_call(
        last_kernel,
        out_shape=jax.ShapeDtypeStruct(terms[0].shape, F32),
        in_specs=[VMEM] * 4 + [FREE] * len(ties),
        out_specs=VMEM,
        compiler_params=PARAMS,
        cost_estimate=LITTLE,
        name="add_terms",
    )(*terms, *ties)


def halves_kernel(keep, got, out):
    out[...] = (keep[...].astype(F32) + got[...].astype(F32)).astype(BF16)


def add_halves(keep, got):
    return pl.pallas_call(
        halves_kernel,
        out_shape=jax.ShapeDtypeStruct(keep.shape, BF16),
        in_specs=[VMEM] * 2,
        out_specs=VMEM,
        compiler_params=PARAMS,
        cost_estimate=LITTLE,
        name="add_halves",
    )(keep, got)


def wgrad_kernel(layer, pos, d, hb_hbm, *refs):
    keep, send, hb, grad, sem = refs[-5:]
    load = pltpu.make_async_copy(hb_hbm.at[layer], hb, sem)
    load.start()
    n_own = d.shape[0]
    lhs = d[...]
    load.wait()
    for i in range(3):
        part = lax.dot_general(
            lhs, hb[i * WIDE : i * WIDE + n_own, :], (((0,), (0,)), ((), ())), preferred_element_type=F32
        ).astype(BF16)
        for s in range(3):
            grad[:, (3 * i + s) * CHANS : (3 * i + s + 1) * CHANS] = part[s * LANES : (s + 1) * LANES]
    half = LANES // 2
    keep[...] = grad[pl.ds(pl.multiple_of(pos[1] * half, half), half), :]
    send[...] = grad[pl.ds(pl.multiple_of((1 - pos[1]) * half, half), half), :]


def wgrad_step(layer, pos, d, kept, ties):
    half = pltpu.VMEM((LANES // 2, 9 * CHANS), BF16)
    return pl.pallas_call(
        functools.partial(wgrad_kernel, layer),
        out_shape=(half, half),
        in_specs=[SMEM, VMEM, ANY] + [FREE] * len(ties),
        out_specs=(VMEM, VMEM),
        scratch_shapes=[
            pltpu.VMEM(kept.shape[1:], BF16),
            pltpu.VMEM((LANES, 9 * CHANS), BF16),
            pltpu.SemaphoreType.DMA,
        ],
        compiler_params=PARAMS,
        cost_estimate=LITTLE,
        name="kernel_gradient",
    )(pos, d, in_hbm(kept), *ties)


def place_kernel(layers, fresh, pos, *refs):
    count = 2 * len(layers)
    sources = refs[:count]
    out, held, wide, sem = refs[-4:]
    half = LANES // 2
    r = pos[1]
    loads = [pltpu.make_async_copy(sources[j], held.at[j], sem.at[j]) for j in range(count)]
    for load in loads:
        load.start()
    stores = []
    for j in range(count):
        at = pl.multiple_of((r if j % 2 == 0 else 1 - r) * half, half)
        if j >= 2:
            stores[j - 2].wait()
        loads[j].wait()
        wide[j % 2] = held[j].astype(F32)
        store = pltpu.make_async_copy(wide.at[j % 2], out.at[layers[j // 2], pl.ds(at, half)], sem.at[count + j])
        store.start()
        stores.append(store)
    for store in stores[-2:]:
        store.wait()


def place_step(layers, pos, sources, whole, count):
    half = LANES // 2
    jobs = len(sources)
    return pl.pallas_call(
        functools.partial(place_kernel, layers, whole is None),
        out_shape=pltpu.HBM((count, LANES, 9 * CHANS), F32),
        in_specs=[SMEM] + [ANY] * jobs + ([] if whole is None else [ANY]),
        out_specs=ANY,
        input_output_aliases={} if whole is None else {1 + jobs: 0},
        scratch_shapes=[
            pltpu.VMEM((jobs, half, 9 * CHANS), BF16),
            pltpu.VMEM((2, half, 9 * CHANS), F32),
            pltpu.SemaphoreType.DMA((2 * jobs,)),
        ],
        compiler_params=PARAMS,
        cost_estimate=LITTLE,
        name="place_gradients",
    )(pos, *[in_hbm(v) for v in sources], *(() if whole is None else (in_hbm(whole),)))


def swap_with(value, axis, k):
    return lax.ppermute(value, axis, [(i, i ^ k) for i in range(lax.axis_size(axis))])


def spread(own):
    return (own, *[swap_with(own, "tensor", k) for k in range(1, GROUPS)])


def halo_of_input(x, half):
    n_own = x.shape[0]
    edge = jnp.where(half == 0, x[n_own - WIDE :], x[:WIDE])
    return jnp.concatenate([x, swap_with(edge, "rows", 1)], axis=0)


def fast_local(section_input, conv_weights, norm_gains, norm_shifts, out_grad, out_mask):
    images, rows_here, width = out_mask.shape
    layers = conv_weights.shape[0]
    n_own = rows_here * width
    parts = lax.axis_size("dp") * lax.axis_size("rows")
    total = float(n_own * parts)
    t, half = lax.axis_index("tensor"), lax.axis_index("rows")
    image = lax.axis_index("dp")
    pos = jnp.stack([t, half, 2 * image + half, 2 * image + 1 - half]).astype(jnp.int32)
    middle = layers // 2
    x = to_maps(section_input, width).reshape(n_own, LANES)
    slots = lax.all_gather(halo_of_input(x, half), "tensor", axis=1, tiled=True)
    pad = jnp.zeros((8 - layers, LANES), F32)
    tables = spread(jnp.concatenate([norm_gains, pad, norm_shifts, pad], axis=0))
    top_grad = (to_maps(out_grad, width) * out_mask[..., None].astype(BF16)).reshape(n_own, LANES)

    st, kept = None, None
    halves = ("dp", "rows")
    kept_z, kept_st = [], []
    for layer in range(layers):
        last = layer + 1 == layers
        edge = 2 * WIDE if layer + 1 == middle else WIDE
        everyone = halves if last else (*halves, "tensor")
        devices = parts if last else parts * GROUPS
        kept, zc, rim, local = fwd_step(
            layer,
            layer == middle,
            edge,
            total,
            pos,
            slots,
            st,
            tables,
            conv_weights,
            kept,
            n_own,
            devices,
            (top_grad,) if layer == 2 else (),
        )
        rim = swap_with(rim, "rows", 1)
        st = lax.all_to_all(local, everyone, split_axis=0, concat_axis=0, tiled=True)
        st = st.reshape(parts, devices // parts, 8, LANES)
        zc = lax.dynamic_update_slice_in_dim(zc, rim, n_own, axis=0)
        kept_z.append(zc)
        kept_st.append(st)
        if not last:
            slots = lax.all_gather(zc, "tensor", axis=1, tiled=True)
    top = layers - 1
    h_last, dn, msg = below_step(top, False, total, pos, kept_z[top], kept_st[top], tables[0], (top_grad,))

    def with_other(values):
        return [v for mine in values for v in (mine, swap_with(mine, "rows", 1))]

    sum_list, pairs = [None] * layers, [None] * layers
    ahead, back = [[0, 1, 2, 3]], [[3, 2, 1, 0]]
    urgent = ()
    for layer in range(layers - 1, -1, -1):
        got = swap_with(msg, "rows", 1)
        sums = msg[WIDE:] + got[WIDE:]
        one, two, three = (swap_with(sums, "dp", k) for k in (1, 2, 3))
        sums = (sums + one) + (two + three)
        sum_list[layer] = sums
        *terms, d = bwd_step(
            layer, total, pos, dn, got, sums, kept_z[layer], kept_st[layer], tables[0], conv_weights, urgent
        )
        terms = (terms[0], *[swap_with(terms[k], "tensor", k) for k in range(1, GROUPS)])
        keep, send = wgrad_step(layer, pos, d, kept, ())
        pairs[layer] = add_halves(keep, swap_with(send, "rows", 1))
        urgent = (pairs[layer],)
        if layer == middle:
            upper = lax.psum(tuple(pairs[:2:-1]), "dp", axis_index_groups=ahead)
        if layer > 0:
            below = layer - 1
            dn, msg = below_step(
                below, layer == middle, total, pos, kept_z[below], kept_st[below], tables[0], terms, (keep,)
            )
        else:
            grad = last_step(terms, (pairs[0], in_hbm(upper[0])))
    lower = lax.psum(tuple(pairs[2::-1]), "dp", axis_index_groups=back)
    shape = (images, rows_here, width, LANES)
    outputs = (from_maps(h_last.reshape(shape)), from_maps(grad.reshape(shape)))
    whole = place_step((5, 4, 3), pos, with_other(upper), None, layers)
    sums = jnp.stack(sum_list)
    lower, whole, outputs, sums = lax.optimization_barrier((lower, whole, outputs, sums))
    whole = place_step((2, 1, 0), pos, with_other(lower), whole, layers)
    return (*outputs, whole, sums[:, 1], sums[:, 0])


def solution(mesh):
    in_specs = (
        P("dp", "rows", "tensor"),
        P(None, "tensor", None),
        P(None, "tensor"),
        P(None, "tensor"),
        P("dp", "rows", "tensor"),
        P("dp", "rows", None),
    )
    out_specs = (
        P("dp", "rows", "tensor"),
        P("dp", "rows", "tensor"),
        P(None, "tensor", None),
        P(None, "tensor"),
        P(None, "tensor"),
    )
    local = fast_local if fits_kernels(mesh) else generic_local
    return jax.shard_map(local, mesh=mesh, in_specs=in_specs, out_specs=out_specs, check_vma=False)
```

```python
import functools

import jax
import jax.numpy as jnp
from jax import lax
from jax.experimental import pallas as pl
from jax.experimental.pallas import tpu as pltpu
from jax.sharding import PartitionSpec as P

EPS = 1e-05


def padded_2(cells, sides, width):
    for axis, dim in sides:
        count = lax.axis_size(axis)
        ends = count - 1
        head = lax.slice_in_dim(cells, 0, width, axis=dim)
        tail = lax.slice_in_dim(cells, cells.shape[dim] - width, cells.shape[dim], axis=dim)
        cells = jnp.concatenate(
            [
                lax.ppermute(tail, axis, [(i, (i + 1) % count) for i in range(ends)]),
                cells,
                lax.ppermute(head, axis, [((i + 1) % count, i) for i in range(ends)]),
            ],
            axis=dim,
        )
    return cells


def to_maps(flat, width):
    count, high, merged = flat.shape
    return flat.reshape(count, high, merged // width, width).transpose(0, 1, 3, 2)


def from_maps(maps):
    count, high, wide, chans = maps.shape
    return maps.transpose(0, 1, 3, 2).reshape(count, high, chans * wide)


def spatial_conv(padded, kernel):
    return lax.conv_general_dilated(
        padded,
        kernel,
        (1, 1),
        ((0, 0), (1, 1)),
        dimension_numbers=("NHWC", "HWIO", "NHWC"),
        preferred_element_type=jnp.float32,
    )


def flipped(kernel):
    return jnp.transpose(kernel[::-1, ::-1], (0, 1, 3, 2))


def pool_unpool(values):
    count, high, wide, chans = values.shape
    blocks = values.reshape(count, high // 2, 2, wide // 2, 2, chans)
    pooled = jax.nn.logsumexp(blocks, axis=(2, 4), keepdims=True)
    return (jnp.exp(blocks - pooled) * pooled).reshape(values.shape)


def moments(conv_out, total_pixels):
    summed = lax.psum(jnp.sum(conv_out, axis=(0, 1, 2)), ("dp", "rows"))
    mean = summed / total_pixels
    spread = lax.psum(jnp.sum(jnp.square(conv_out - mean), axis=(0, 1, 2)), ("dp", "rows"))
    var = spread / total_pixels
    return (mean, lax.rsqrt(var + EPS))


def kernel_grad(whole, dconv):
    images, rows_here, width, chans = dconv.shape
    widened = jnp.pad(whole, ((0, 0), (0, 0), (1, 1), (0, 0)))
    stacked = []
    for row_off in range(3):
        line = []
        for col_off in range(3):
            window = widened[:, row_off : row_off + rows_here, col_off : col_off + width, :]
            line.append(
                jnp.einsum("bhwc,bhwo->co", window, dconv, preferred_element_type=jnp.float32)
            )
        stacked.append(jnp.stack(line))
    return jnp.stack(stacked)


def generic_local(section_input, conv_weights, norm_gains, norm_shifts, out_grad, out_mask):
    width = out_mask.shape[2]
    images, rows_here = (out_mask.shape[0], out_mask.shape[1])
    total_pixels = float(images * rows_here * width * lax.axis_size("dp") * lax.axis_size("rows"))
    layers, out_here, flat_in = conv_weights.shape
    chans_in = flat_in // 9
    kernels_hwio = conv_weights.reshape(layers, out_here, 3, 3, chans_in).transpose(0, 2, 3, 4, 1)
    middle = layers // 2
    kept = []
    acting = to_maps(section_input, width)
    current = acting.astype(jnp.float32)
    pre_pool = current
    for index in range(layers):
        if index == middle:
            pre_pool = current
            acting = pool_unpool(pre_pool).astype(jnp.bfloat16)
        padded = padded_2(acting, (("rows", 1),), 1)
        whole = lax.all_gather(padded, "tensor", axis=3, tiled=True)
        conv_out = spatial_conv(whole, kernels_hwio[index])
        mean, rstd = moments(conv_out, total_pixels)
        normed = (conv_out - mean) * rstd
        shifted = normed * norm_gains[index] + norm_shifts[index]
        current = jax.nn.silu(shifted)
        acting = current.astype(jnp.bfloat16)
        kept.append((whole, normed, shifted, rstd))
    grad = to_maps(out_grad, width).astype(jnp.float32) * out_mask[..., None].astype(jnp.float32)
    kernel_list = [None] * layers
    gain_list = [None] * layers
    shift_list = [None] * layers
    for index in range(layers - 1, -1, -1):
        whole, normed, shifted, rstd = kept[index]
        unused, pull_silu = jax.vjp(jax.nn.silu, shifted)
        dshift = pull_silu(grad)[0]
        gain_sum, shift_sum = lax.psum(
            (jnp.sum(dshift * normed, axis=(0, 1, 2)), jnp.sum(dshift, axis=(0, 1, 2))),
            ("dp", "rows"),
        )
        gain_list[index] = gain_sum
        shift_list[index] = shift_sum
        dconv = (
            norm_gains[index]
            * rstd
            * (dshift - shift_sum / total_pixels - normed * gain_sum / total_pixels)
        ).astype(jnp.bfloat16)
        summed_kernel = lax.psum(
            kernel_grad(whole, dconv).astype(jnp.bfloat16), ("dp", "rows")
        ).astype(jnp.float32)
        kernel_list[index] = summed_kernel.transpose(3, 0, 1, 2).reshape(out_here, flat_in)
        grad_rim = padded_2(dconv, (("rows", 1),), 1)
        partial_terms = spatial_conv(grad_rim, flipped(kernels_hwio[index]))
        grad_in = lax.psum_scatter(
            partial_terms.astype(jnp.bfloat16), "tensor", scatter_dimension=3, tiled=True
        ).astype(jnp.float32)
        if index == middle:
            unused, pull_pool = jax.vjp(pool_unpool, pre_pool)
            grad = pull_pool(grad_in)[0]
        else:
            grad = grad_in
    return (
        from_maps(acting),
        from_maps(grad),
        jnp.stack(kernel_list),
        jnp.stack(gain_list),
        jnp.stack(shift_list),
    )


GROUPS = 4
LANES = 128
WIDE = 48
CHANS = GROUPS * LANES
F32 = jnp.float32
BF16 = jnp.bfloat16
VMEM = pl.BlockSpec(memory_space=pltpu.VMEM)
SMEM = pl.BlockSpec(memory_space=pltpu.SMEM)
ANY = pl.BlockSpec(memory_space=pltpu.HBM)
FREE = pl.BlockSpec(memory_space=pl.ANY)
LITTLE = pl.CostEstimate(flops=1024, bytes_accessed=1024, transcendentals=0)
PARAMS = pltpu.CompilerParams(vmem_limit_bytes=20 * 1024 * 1024)


def in_hbm(value):
    return pltpu.with_memory_space_constraint(value, pltpu.HBM)


def fits_kernels(mesh):
    return mesh.shape["tensor"] == GROUPS and mesh.shape["rows"] == 2 and mesh.shape["dp"] == 4


def sigmoid(v):
    return 0.5 * jnp.tanh(0.5 * v) + 0.5


def swap_columns(v):
    column = lax.broadcasted_iota(jnp.int32, v.shape, 0)
    return jnp.where(column % 2 == 0, pltpu.roll(v, WIDE - 1, 0), pltpu.roll(v, 1, 0))


def soft_parts(h):
    top = jnp.maximum(h[0], h[1])
    top = jnp.maximum(top, swap_columns(top))
    e0, e1 = jnp.exp(h[0] - top), jnp.exp(h[1] - top)
    total = e0 + e1
    total = total + swap_columns(total)
    pooled = top + jnp.log(total)
    inverse = 1.0 / total
    return e0 * inverse, e1 * inverse, pooled


def soft(h):
    h = h.reshape(2, WIDE, LANES)
    q0, q1, pooled = soft_parts(h)
    return jnp.concatenate([q0 * pooled, q1 * pooled], axis=0)


def soft_pull(h, grad):
    h = h.reshape(2, WIDE, LANES)
    grad = grad.reshape(2, WIDE, LANES)
    q0, q1, pooled = soft_parts(h)
    mix = q0 * grad[0] + q1 * grad[1]
    mix = mix + swap_columns(mix)
    return jnp.concatenate(
        [q0 * (pooled * (grad[0] - mix) + mix), q1 * (pooled * (grad[1] - mix) + mix)], axis=0
    )


def norm_tables(st, group, i_own, i_oth, n_local, total):
    parts = st.shape[0]
    group = 0 if st.shape[1] == 1 else group
    blocks = [st[i, group] for i in range(parts)]
    summed = functools.reduce(jnp.add, blocks)
    mean = summed[0:1] / parts
    apart = functools.reduce(jnp.add, [jnp.square(b - mean) for b in blocks])
    rstd = lax.rsqrt((summed[1:2] + n_local * apart[0:1]) / total + EPS)
    return rstd, (st[i_own, group, 0:1] - mean) * rstd, (st[i_oth, group, 0:1] - mean) * rstd


def left_right(y0, y1, y2):
    rows = y0.shape[0]
    column = lax.broadcasted_iota(jnp.int32, y0.shape, 0) % WIDE
    before = jnp.where(column == 0, 0.0, pltpu.roll(y0, 1, 0))
    after = jnp.where(column == WIDE - 1, 0.0, pltpu.roll(y2, rows - 1, 0))
    return before + y1 + after


def lane_of(group):
    return pl.multiple_of(group * LANES, LANES)


def edge_start(n_own, edge, half):
    return pl.multiple_of((1 - half) * (n_own - edge), WIDE)


def pair_rows(j):
    return pl.ds(pl.multiple_of(j * 2 * WIDE, 2 * WIDE), 2 * WIDE)


def fold(v):
    return jnp.sum(v.reshape(v.shape[0] // 8, 8, LANES), axis=0)


def fwd_kernel(first, pool, layer, total, edge_out, *refs):
    pos, zall = refs[0], refs[1]
    if first:
        w_hbm = refs[2]
    else:
        st, gss, w_hbm = refs[2], refs[3:7], refs[7]
    hb_out, zc_out, edge_ref, st_out, hb, w, y, z, tab, hs, sem = refs[-11:]
    load = pltpu.make_async_copy(w_hbm.at[layer], w, sem.at[0])
    load.start()
    save = pltpu.make_async_copy(hb, hb_out.at[layer], sem.at[1])
    t, r = pos[0], pos[1]
    n_own = z.shape[0]
    halo_at = pl.multiple_of((1 - r) * (n_own + WIDE), WIDE)
    zero_at = pl.multiple_of(r * (n_own + WIDE), WIDE)
    hb[pl.ds(zero_at, WIDE), :] = jnp.zeros((WIDE, CHANS), BF16)
    edge = zall.shape[0] - n_own
    if not first:
        for k in range(GROUPS):
            group = t ^ k
            rstd, own, oth = norm_tables(st, group, pos[2], pos[3], float(n_own), total)
            gain, shift = gss[k][layer - 1 : layer, :], gss[k][layer + 7 : layer + 8, :]
            tab[group, 0:1] = rstd * gain
            tab[group, 1:2] = own * gain + shift
            tab[group, 2:3] = oth * gain + shift

    def act(values, group, which):
        if first:
            return values
        n = values.astype(F32) * tab[group, 0:1, :] + tab[group, which : which + 1, :]
        h = n * sigmoid(n)
        return soft(h) if pool else h

    def body(j, carry):
        at = pl.multiple_of(j * 2 * WIDE, 2 * WIDE)
        for group in range(GROUPS):
            lanes = slice(group * LANES, (group + 1) * LANES)
            h = act(zall[pl.ds(at, 2 * WIDE), lanes], group, 1)
            hb[pl.ds(pl.multiple_of(at + WIDE, WIDE), 2 * WIDE), lanes] = h.astype(BF16)
        return carry

    lax.fori_loop(0, n_own // (2 * WIDE), body, 0)
    for group in range(GROUPS):
        lanes = slice(group * LANES, (group + 1) * LANES)
        h = act(zall[n_own : n_own + edge, lanes], group, 2)
        if edge > WIDE:
            hs[...] = h
            h = hs[pl.ds(pl.multiple_of(r * WIDE, WIDE), WIDE), :]
        hb[pl.ds(halo_at, WIDE), lanes] = h.astype(BF16)
    save.start()
    load.wait()
    lhs = jnp.concatenate([hb[i * WIDE : i * WIDE + n_own, :] for i in range(3)], axis=1)
    rhs = jnp.concatenate(
        [
            jnp.concatenate([w[:, (3 * i + s) * CHANS : (3 * i + s + 1) * CHANS] for i in range(3)], axis=1)
            for s in range(3)
        ],
        axis=0,
    )
    y[...] = lax.dot_general(lhs, rhs, (((1,), (1,)), ((), ())), preferred_element_type=F32)

    def add_up(j, acc):
        rows = pair_rows(j)
        v = left_right(y[rows, 0:128], y[rows, 128:256], y[rows, 256:384])
        z[rows, :] = v
        return acc + fold(v)

    steps = n_own // (2 * WIDE)
    summed = lax.fori_loop(0, steps, add_up, jnp.zeros((8, LANES), F32))
    mean = jnp.sum(summed, axis=0, keepdims=True) / n_own

    def centre(j, acc):
        rows = pair_rows(j)
        v = z[rows, :] - mean
        z[rows, :] = v
        zc_out[rows, :] = v.astype(BF16)
        return acc + fold(jnp.square(v))

    apart = lax.fori_loop(0, steps, centre, jnp.zeros((8, LANES), F32))
    sums = jnp.concatenate([mean, jnp.sum(apart, axis=0, keepdims=True)], axis=0)
    for i in range(st_out.shape[0]):
        st_out[i] = sums
    edge_ref[...] = zc_out[pl.ds(edge_start(n_own, edge_out, r), edge_out), :]
    zc_out[n_own : n_own + edge_out, :] = jnp.zeros((edge_out, LANES), BF16)
    save.wait()


def fwd_step(layer, pool, edge_out, total, pos, slots, st, tables, weights, kept, n_own, devices, ties):
    first = st is None
    layers = weights.shape[0]
    extra = () if first else (st, *tables)
    return pl.pallas_call(
        functools.partial(fwd_kernel, first, pool, layer, total, edge_out),
        out_shape=(
            pltpu.HBM((layers, n_own + 2 * WIDE, CHANS), BF16),
            pltpu.VMEM((n_own + edge_out, LANES), BF16),
            pltpu.VMEM((edge_out, LANES), BF16),
            pltpu.VMEM((devices, 2, LANES), F32),
        ),
        in_specs=[SMEM] + [VMEM] * (1 + len(extra)) + [ANY] * (1 if first else 2) + [FREE] * len(ties),
        out_specs=(ANY, VMEM, VMEM, VMEM),
        input_output_aliases={} if first else {3 + len(extra): 0},
        scratch_shapes=[
            pltpu.VMEM((n_own + 2 * WIDE, CHANS), BF16),
            pltpu.VMEM((LANES, 9 * CHANS), BF16),
            pltpu.VMEM((n_own, 3 * LANES), F32),
            pltpu.VMEM((n_own, LANES), F32),
            pltpu.VMEM((GROUPS, 8, LANES), F32),
            pltpu.VMEM((2 * WIDE, LANES), F32),
            pltpu.SemaphoreType.DMA((2,)),
        ],
        compiler_params=PARAMS,
        cost_estimate=pl.CostEstimate(
            flops=2 * n_own * 9 * CHANS * LANES, bytes_accessed=4 * 1024 * 1024, transcendentals=n_own * CHANS
        ),
        name="conv_forward",
    )(pos, slots, *extra, in_hbm(weights), *(() if first else (in_hbm(kept),)), *ties)


def below_kernel(layer, pool, total, top, *refs):
    pos, zc, st, gs = refs[:4]
    if top:
        terms, h_out, dn_out, msg, tab = refs[4:]
    else:
        terms, (dn_out, msg, tab) = refs[4:8], refs[-3:]
    n_own = dn_out.shape[0]
    rstd, own, oth = norm_tables(st, pos[0], pos[2], pos[3], float(n_own), total)
    tab[0:1], tab[1:2] = rstd, own
    tab[2:3], tab[3:4] = gs[layer : layer + 1, :], gs[layer + 8 : layer + 9, :]

    def body(j, accs):
        rows = pair_rows(j)
        xhat = zc[rows, :].astype(F32) * tab[0:1, :] + tab[1:2, :]
        n = xhat * tab[2:3, :] + tab[3:4, :]
        sig = sigmoid(n)
        h = n * sig
        if top:
            g = terms[rows, :].astype(F32)
            h_out[rows, :] = h.astype(BF16)
        else:
            g = functools.reduce(jnp.add, [term[rows, :].astype(F32) for term in terms])
        if pool:
            g = soft_pull(h, g)
        dn = g * (sig * (1.0 + n - h))
        dn_out[rows, :] = dn
        return accs[0] + fold(dn), accs[1] + fold(dn * xhat)

    zero = jnp.zeros((8, LANES), F32)
    sums = lax.fori_loop(0, n_own // (2 * WIDE), body, (zero, zero))
    sums = [jnp.sum(v, axis=0, keepdims=True) for v in sums]
    msg[0:WIDE, :] = dn_out[pl.ds(edge_start(n_own, WIDE, pos[1]), WIDE), :]
    msg[WIDE : WIDE + 8, :] = jnp.concatenate(sums + [jnp.zeros((6, LANES), F32)], axis=0)


def below_step(layer, pool, total, pos, zc, st, gs, terms, ties=()):
    n_own = terms[0].shape[0]
    top = len(terms) == 1
    out_shape = [
        pltpu.VMEM((n_own, LANES), F32),
        pltpu.VMEM((WIDE + 8, LANES), F32),
    ]
    if top:
        out_shape = [jax.ShapeDtypeStruct((n_own, LANES), BF16)] + out_shape
    return pl.pallas_call(
        functools.partial(below_kernel, layer, pool, total, top),
        out_shape=tuple(out_shape),
        in_specs=[SMEM] + [VMEM] * (3 + len(terms)) + [FREE] * len(ties),
        out_specs=(VMEM,) * len(out_shape),
        scratch_shapes=[pltpu.VMEM((8, LANES), F32)],
        compiler_params=PARAMS,
        cost_estimate=LITTLE,
        name="silu_backward",
    )(pos, zc, st, gs, *terms, *ties)


def bwd_kernel(layer, total, *refs):
    pos, dn, dedge, sums, zc, st, gs, w_hbm = refs[:8]
    outs, d_out, d, w, y, tab, sem = refs[-10:-6], *refs[-6:]
    load = pltpu.make_async_copy(w_hbm.at[layer], w, sem)
    load.start()
    t, r = pos[0], pos[1]
    n_own = dn.shape[0]
    halo_at = pl.multiple_of((1 - r) * (n_own + WIDE), WIDE)
    zero_at = pl.multiple_of(r * (n_own + WIDE), WIDE)
    edge = zc.shape[0] - n_own
    d[pl.ds(zero_at, WIDE), :] = jnp.zeros((WIDE, 3 * LANES), BF16)
    rstd, own, oth = norm_tables(st, t, pos[2], pos[3], float(n_own), total)
    scale = gs[layer : layer + 1, :] * rstd
    shift_sum, gain_sum = sums[0:1, :], sums[1:2, :]
    slope = scale * gain_sum / total
    tab[0:1] = scale
    tab[1:2] = slope * rstd
    tab[2:3] = scale * shift_sum / total + slope * own
    tab[3:4] = scale * shift_sum / total + slope * oth

    def spread_columns(v, at):
        rows = v.shape[0]
        column = lax.broadcasted_iota(jnp.int32, v.shape, 0) % WIDE
        ahead = jnp.where(column == WIDE - 1, 0.0, pltpu.roll(v, rows - 1, 0))
        behind = jnp.where(column == 0, 0.0, pltpu.roll(v, 1, 0))
        d[pl.ds(at, rows), 0:128] = ahead.astype(BF16)
        d[pl.ds(at, rows), 128:256] = v.astype(BF16)
        d[pl.ds(at, rows), 256:384] = behind.astype(BF16)

    def body(j, carry):
        rows = pair_rows(j)
        v = dn[rows, :] * tab[0:1, :] - tab[2:3, :] - zc[rows, :].astype(F32) * tab[1:2, :]
        spread_columns(v, pl.multiple_of(j * 2 * WIDE + WIDE, WIDE))
        return carry

    lax.fori_loop(0, n_own // (2 * WIDE), body, 0)
    near = n_own if edge == WIDE else pl.multiple_of(n_own + r * WIDE, WIDE)
    near = zc[pl.ds(near, WIDE), :].astype(F32)
    spread_columns(dedge[0:WIDE, :] * tab[0:1, :] - tab[3:4, :] - near * tab[1:2, :], halo_at)
    d_out[...] = d[WIDE : WIDE + n_own, :]
    load.wait()
    lhs = jnp.concatenate([d[(2 - i) * WIDE : (2 - i) * WIDE + n_own, :] for i in range(3)], axis=1)
    rhs = jnp.concatenate([w[:, i * CHANS : (i + 1) * CHANS] for i in range(9)], axis=0)
    y[...] = jnp.dot(lhs, rhs, preferred_element_type=F32)

    def share(j, carry):
        rows = pair_rows(j)
        for k in range(GROUPS):
            outs[k][rows, :] = y[rows, pl.ds(lane_of(t ^ k), LANES)].astype(BF16)
        return carry

    lax.fori_loop(0, n_own // (2 * WIDE), share, 0)


def bwd_step(layer, total, pos, dn, dedge, sums, zc, st, gs, weights, ties):
    n_own = dn.shape[0]
    part = pltpu.VMEM((n_own, LANES), BF16)
    return pl.pallas_call(
        functools.partial(bwd_kernel, layer, total),
        out_shape=(
            part,
            part,
            part,
            part,
            pltpu.VMEM((n_own, 3 * LANES), BF16),
        ),
        in_specs=[SMEM] + [VMEM] * 6 + [ANY] + [FREE] * len(ties),
        out_specs=(VMEM,) * 5,
        scratch_shapes=[
            pltpu.VMEM((n_own + 2 * WIDE, 3 * LANES), BF16),
            pltpu.VMEM((LANES, 9 * CHANS), BF16),
            pltpu.VMEM((n_own, CHANS), F32),
            pltpu.VMEM((8, LANES), F32),
            pltpu.SemaphoreType.DMA,
        ],
        compiler_params=PARAMS,
        cost_estimate=LITTLE,
        name="conv_backward",
    )(pos, dn, dedge, sums, zc, st, gs, in_hbm(weights), *ties)


def last_kernel(t0, t1, t2, t3, *refs):
    out = refs[-1]

    def body(j, carry):
        rows = pair_rows(j)
        out[rows, :] = functools.reduce(jnp.add, [term[rows, :].astype(F32) for term in (t0, t1, t2, t3)])
        return carry

    lax.fori_loop(0, out.shape[0] // (2 * WIDE), body, 0)


def last_step(terms, ties):
    return pl.pallas_call(
        last_kernel,
        out_shape=jax.ShapeDtypeStruct(terms[0].shape, F32),
        in_specs=[VMEM] * 4 + [FREE] * len(ties),
        out_specs=VMEM,
        compiler_params=PARAMS,
        cost_estimate=LITTLE,
        name="add_terms",
    )(*terms, *ties)


def halves_kernel(keep, got, out):
    out[...] = (keep[...].astype(F32) + got[...].astype(F32)).astype(BF16)


def add_halves(keep, got):
    return pl.pallas_call(
        halves_kernel,
        out_shape=jax.ShapeDtypeStruct(keep.shape, BF16),
        in_specs=[VMEM] * 2,
        out_specs=VMEM,
        compiler_params=PARAMS,
        cost_estimate=LITTLE,
        name="add_halves",
    )(keep, got)


def wgrad_kernel(layer, pos, d, hb_hbm, *refs):
    keep, send, hb, grad, sem = refs[-5:]
    load = pltpu.make_async_copy(hb_hbm.at[layer], hb, sem)
    load.start()
    n_own = d.shape[0]
    lhs = d[...]
    load.wait()
    for i in range(3):
        part = lax.dot_general(
            lhs, hb[i * WIDE : i * WIDE + n_own, :], (((0,), (0,)), ((), ())), preferred_element_type=F32
        ).astype(BF16)
        for s in range(3):
            grad[:, (3 * i + s) * CHANS : (3 * i + s + 1) * CHANS] = part[s * LANES : (s + 1) * LANES]
    half = LANES // 2
    keep[...] = grad[pl.ds(pl.multiple_of(pos[1] * half, half), half), :]
    send[...] = grad[pl.ds(pl.multiple_of((1 - pos[1]) * half, half), half), :]


def wgrad_step(layer, pos, d, kept, ties):
    half = pltpu.VMEM((LANES // 2, 9 * CHANS), BF16)
    return pl.pallas_call(
        functools.partial(wgrad_kernel, layer),
        out_shape=(half, half),
        in_specs=[SMEM, VMEM, ANY] + [FREE] * len(ties),
        out_specs=(VMEM, VMEM),
        scratch_shapes=[
            pltpu.VMEM(kept.shape[1:], BF16),
            pltpu.VMEM((LANES, 9 * CHANS), BF16),
            pltpu.SemaphoreType.DMA,
        ],
        compiler_params=PARAMS,
        cost_estimate=LITTLE,
        name="kernel_gradient",
    )(pos, d, in_hbm(kept), *ties)


def place_kernel(layers, fresh, pos, *refs):
    count = 2 * len(layers)
    sources = refs[:count]
    out, held, wide, sem = refs[-4:]
    half = LANES // 2
    r = pos[1]
    loads = [pltpu.make_async_copy(sources[j], held.at[j], sem.at[j]) for j in range(count)]
    for load in loads:
        load.start()
    stores = []
    for j in range(count):
        at = pl.multiple_of((r if j % 2 == 0 else 1 - r) * half, half)
        if j >= 2:
            stores[j - 2].wait()
        loads[j].wait()
        wide[j % 2] = held[j].astype(F32)
        store = pltpu.make_async_copy(wide.at[j % 2], out.at[layers[j // 2], pl.ds(at, half)], sem.at[count + j])
        store.start()
        stores.append(store)
    for store in stores[-2:]:
        store.wait()


def place_step(layers, pos, sources, whole, count):
    half = LANES // 2
    jobs = len(sources)
    return pl.pallas_call(
        functools.partial(place_kernel, layers, whole is None),
        out_shape=pltpu.HBM((count, LANES, 9 * CHANS), F32),
        in_specs=[SMEM] + [ANY] * jobs + ([] if whole is None else [ANY]),
        out_specs=ANY,
        input_output_aliases={} if whole is None else {1 + jobs: 0},
        scratch_shapes=[
            pltpu.VMEM((jobs, half, 9 * CHANS), BF16),
            pltpu.VMEM((2, half, 9 * CHANS), F32),
            pltpu.SemaphoreType.DMA((2 * jobs,)),
        ],
        compiler_params=PARAMS,
        cost_estimate=LITTLE,
        name="place_gradients",
    )(pos, *[in_hbm(v) for v in sources], *(() if whole is None else (in_hbm(whole),)))


def swap_with(value, axis, k):
    return lax.ppermute(value, axis, [(i, i ^ k) for i in range(lax.axis_size(axis))])


def spread(own):
    return (own, *[swap_with(own, "tensor", k) for k in range(1, GROUPS)])


def halo_of_input(x, half):
    n_own = x.shape[0]
    edge = jnp.where(half == 0, x[n_own - WIDE :], x[:WIDE])
    return jnp.concatenate([x, swap_with(edge, "rows", 1)], axis=0)


def fast_local(section_input, conv_weights, norm_gains, norm_shifts, out_grad, out_mask):
    images, rows_here, width = out_mask.shape
    layers = conv_weights.shape[0]
    n_own = rows_here * width
    parts = lax.axis_size("dp") * lax.axis_size("rows")
    total = float(n_own * parts)
    t, half = lax.axis_index("tensor"), lax.axis_index("rows")
    image = lax.axis_index("dp")
    pos = jnp.stack([t, half, 2 * image + half, 2 * image + 1 - half]).astype(jnp.int32)
    middle = layers // 2
    x = to_maps(section_input, width).reshape(n_own, LANES)
    slots = lax.all_gather(halo_of_input(x, half), "tensor", axis=1, tiled=True)
    pad = jnp.zeros((8 - layers, LANES), F32)
    tables = spread(jnp.concatenate([norm_gains, pad, norm_shifts, pad], axis=0))
    top_grad = (to_maps(out_grad, width) * out_mask[..., None].astype(BF16)).reshape(n_own, LANES)

    st, kept = None, None
    halves = ("dp", "rows")
    kept_z, kept_st = [], []
    for layer in range(layers):
        last = layer + 1 == layers
        edge = 2 * WIDE if layer + 1 == middle else WIDE
        everyone = halves if last else (*halves, "tensor")
        devices = parts if last else parts * GROUPS
        kept, zc, rim, local = fwd_step(
            layer,
            layer == middle,
            edge,
            total,
            pos,
            slots,
            st,
            tables,
            conv_weights,
            kept,
            n_own,
            devices,
            (top_grad,) if layer == 2 else (),
        )
        rim = swap_with(rim, "rows", 1)
        st = lax.all_to_all(local, everyone, split_axis=0, concat_axis=0, tiled=True)
        st = st.reshape(parts, devices // parts, 2, LANES)
        zc = lax.dynamic_update_slice_in_dim(zc, rim, n_own, axis=0)
        kept_z.append(zc)
        kept_st.append(st)
        if not last:
            slots = lax.all_gather(zc, "tensor", axis=1, tiled=True)
    top = layers - 1
    h_last, dn, msg = below_step(top, False, total, pos, kept_z[top], kept_st[top], tables[0], (top_grad,))

    def with_other(values):
        return [v for mine in values for v in (mine, swap_with(mine, "rows", 1))]

    sum_list, pairs = [None] * layers, [None] * layers
    ahead, back = [[0, 1, 2, 3]], [[3, 2, 1, 0]]
    urgent = ()
    for layer in range(layers - 1, -1, -1):
        got = swap_with(msg, "rows", 1)
        sums = msg[WIDE:] + got[WIDE:]
        one, two, three = (swap_with(sums, "dp", k) for k in (1, 2, 3))
        sums = (sums + one) + (two + three)
        sum_list[layer] = sums
        *terms, d = bwd_step(
            layer, total, pos, dn, got, sums, kept_z[layer], kept_st[layer], tables[0], conv_weights, urgent
        )
        terms = (terms[0], *[swap_with(terms[k], "tensor", k) for k in range(1, GROUPS)])
        keep, send = wgrad_step(layer, pos, d, kept, ())
        other = swap_with(send, "rows", 1)
        pairs[layer] = add_halves(keep, other)
        urgent, settled = (other,), (() if layer + 1 == layers else (pairs[layer + 1],))
        if layer == 4:
            upper = lax.psum((pairs[5], pairs[4]), "dp", axis_index_groups=ahead)
        if layer == 2:
            mid = lax.psum((pairs[3], pairs[2]), "dp", axis_index_groups=back)
        if layer > 0:
            below = layer - 1
            late = (in_hbm(upper[0]),) if layer == 1 else ()
            dn, msg = below_step(
                below, layer == middle, total, pos, kept_z[below], kept_st[below], tables[0], terms, (keep, *settled, *late)
            )
        else:
            grad = last_step(terms, (pairs[0], pairs[1]))
    tied, upper = lax.optimization_barrier(((pairs[1], pairs[0]), upper))
    lower = lax.psum(tied, "dp", axis_index_groups=ahead)
    shape = (images, rows_here, width, LANES)
    grad, mid = lax.optimization_barrier((grad, mid))
    outputs = (from_maps(h_last.reshape(shape)), from_maps(grad.reshape(shape)))
    whole = place_step((5, 4, 3, 2), pos, with_other((*upper, *mid)), None, layers)
    sums = jnp.stack(sum_list)
    lower, whole, outputs, sums = lax.optimization_barrier((lower, whole, outputs, sums))
    whole = place_step((1, 0), pos, with_other(lower), whole, layers)
    return (*outputs, whole, sums[:, 1], sums[:, 0])


def solution(mesh):
    in_specs = (
        P("dp", "rows", "tensor"),
        P(None, "tensor", None),
        P(None, "tensor"),
        P(None, "tensor"),
        P("dp", "rows", "tensor"),
        P("dp", "rows", None),
    )
    out_specs = (
        P("dp", "rows", "tensor"),
        P("dp", "rows", "tensor"),
        P(None, "tensor", None),
        P(None, "tensor"),
        P(None, "tensor"),
    )
    local = fast_local if fits_kernels(mesh) else generic_local
    return jax.shard_map(local, mesh=mesh, in_specs=in_specs, out_specs=out_specs, check_vma=False)
```

```python
import functools

import jax
import jax.numpy as jnp
from jax import lax
from jax.experimental import pallas as pl
from jax.experimental.pallas import tpu as pltpu
from jax.sharding import PartitionSpec as P

EPS = 1e-05


def padded_2(cells, sides, width):
    for axis, dim in sides:
        count = lax.axis_size(axis)
        ends = count - 1
        head = lax.slice_in_dim(cells, 0, width, axis=dim)
        tail = lax.slice_in_dim(cells, cells.shape[dim] - width, cells.shape[dim], axis=dim)
        cells = jnp.concatenate(
            [
                lax.ppermute(tail, axis, [(i, (i + 1) % count) for i in range(ends)]),
                cells,
                lax.ppermute(head, axis, [((i + 1) % count, i) for i in range(ends)]),
            ],
            axis=dim,
        )
    return cells


def to_maps(flat, width):
    count, high, merged = flat.shape
    return flat.reshape(count, high, merged // width, width).transpose(0, 1, 3, 2)


def from_maps(maps):
    count, high, wide, chans = maps.shape
    return maps.transpose(0, 1, 3, 2).reshape(count, high, chans * wide)


def spatial_conv(padded, kernel):
    return lax.conv_general_dilated(
        padded,
        kernel,
        (1, 1),
        ((0, 0), (1, 1)),
        dimension_numbers=("NHWC", "HWIO", "NHWC"),
        preferred_element_type=jnp.float32,
    )


def flipped(kernel):
    return jnp.transpose(kernel[::-1, ::-1], (0, 1, 3, 2))


def pool_unpool(values):
    count, high, wide, chans = values.shape
    blocks = values.reshape(count, high // 2, 2, wide // 2, 2, chans)
    pooled = jax.nn.logsumexp(blocks, axis=(2, 4), keepdims=True)
    return (jnp.exp(blocks - pooled) * pooled).reshape(values.shape)


def moments(conv_out, total_pixels):
    summed = lax.psum(jnp.sum(conv_out, axis=(0, 1, 2)), ("dp", "rows"))
    mean = summed / total_pixels
    spread = lax.psum(jnp.sum(jnp.square(conv_out - mean), axis=(0, 1, 2)), ("dp", "rows"))
    var = spread / total_pixels
    return (mean, lax.rsqrt(var + EPS))


def kernel_grad(whole, dconv):
    images, rows_here, width, chans = dconv.shape
    widened = jnp.pad(whole, ((0, 0), (0, 0), (1, 1), (0, 0)))
    stacked = []
    for row_off in range(3):
        line = []
        for col_off in range(3):
            window = widened[:, row_off : row_off + rows_here, col_off : col_off + width, :]
            line.append(
                jnp.einsum("bhwc,bhwo->co", window, dconv, preferred_element_type=jnp.float32)
            )
        stacked.append(jnp.stack(line))
    return jnp.stack(stacked)


def generic_local(section_input, conv_weights, norm_gains, norm_shifts, out_grad, out_mask):
    width = out_mask.shape[2]
    images, rows_here = (out_mask.shape[0], out_mask.shape[1])
    total_pixels = float(images * rows_here * width * lax.axis_size("dp") * lax.axis_size("rows"))
    layers, out_here, flat_in = conv_weights.shape
    chans_in = flat_in // 9
    kernels_hwio = conv_weights.reshape(layers, out_here, 3, 3, chans_in).transpose(0, 2, 3, 4, 1)
    middle = layers // 2
    kept = []
    acting = to_maps(section_input, width)
    current = acting.astype(jnp.float32)
    pre_pool = current
    for index in range(layers):
        if index == middle:
            pre_pool = current
            acting = pool_unpool(pre_pool).astype(jnp.bfloat16)
        padded = padded_2(acting, (("rows", 1),), 1)
        whole = lax.all_gather(padded, "tensor", axis=3, tiled=True)
        conv_out = spatial_conv(whole, kernels_hwio[index])
        mean, rstd = moments(conv_out, total_pixels)
        normed = (conv_out - mean) * rstd
        shifted = normed * norm_gains[index] + norm_shifts[index]
        current = jax.nn.silu(shifted)
        acting = current.astype(jnp.bfloat16)
        kept.append((whole, normed, shifted, rstd))
    grad = to_maps(out_grad, width).astype(jnp.float32) * out_mask[..., None].astype(jnp.float32)
    kernel_list = [None] * layers
    gain_list = [None] * layers
    shift_list = [None] * layers
    for index in range(layers - 1, -1, -1):
        whole, normed, shifted, rstd = kept[index]
        unused, pull_silu = jax.vjp(jax.nn.silu, shifted)
        dshift = pull_silu(grad)[0]
        gain_sum, shift_sum = lax.psum(
            (jnp.sum(dshift * normed, axis=(0, 1, 2)), jnp.sum(dshift, axis=(0, 1, 2))),
            ("dp", "rows"),
        )
        gain_list[index] = gain_sum
        shift_list[index] = shift_sum
        dconv = (
            norm_gains[index]
            * rstd
            * (dshift - shift_sum / total_pixels - normed * gain_sum / total_pixels)
        ).astype(jnp.bfloat16)
        summed_kernel = lax.psum(
            kernel_grad(whole, dconv).astype(jnp.bfloat16), ("dp", "rows")
        ).astype(jnp.float32)
        kernel_list[index] = summed_kernel.transpose(3, 0, 1, 2).reshape(out_here, flat_in)
        grad_rim = padded_2(dconv, (("rows", 1),), 1)
        partial_terms = spatial_conv(grad_rim, flipped(kernels_hwio[index]))
        grad_in = lax.psum_scatter(
            partial_terms.astype(jnp.bfloat16), "tensor", scatter_dimension=3, tiled=True
        ).astype(jnp.float32)
        if index == middle:
            unused, pull_pool = jax.vjp(pool_unpool, pre_pool)
            grad = pull_pool(grad_in)[0]
        else:
            grad = grad_in
    return (
        from_maps(acting),
        from_maps(grad),
        jnp.stack(kernel_list),
        jnp.stack(gain_list),
        jnp.stack(shift_list),
    )


GROUPS = 4
LANES = 128
WIDE = 48
CHANS = GROUPS * LANES
F32 = jnp.float32
BF16 = jnp.bfloat16
VMEM = pl.BlockSpec(memory_space=pltpu.VMEM)
SMEM = pl.BlockSpec(memory_space=pltpu.SMEM)
ANY = pl.BlockSpec(memory_space=pltpu.HBM)
FREE = pl.BlockSpec(memory_space=pl.ANY)
LITTLE = pl.CostEstimate(flops=1024, bytes_accessed=1024, transcendentals=0)
PARAMS = pltpu.CompilerParams(vmem_limit_bytes=20 * 1024 * 1024)


def in_hbm(value):
    return pltpu.with_memory_space_constraint(value, pltpu.HBM)


def fits_kernels(mesh):
    return mesh.shape["tensor"] == GROUPS and mesh.shape["rows"] == 2 and mesh.shape["dp"] == 4


def sigmoid(v):
    return 0.5 * jnp.tanh(0.5 * v) + 0.5


def swap_columns(v):
    column = lax.broadcasted_iota(jnp.int32, v.shape, 0)
    return jnp.where(column % 2 == 0, pltpu.roll(v, WIDE - 1, 0), pltpu.roll(v, 1, 0))


def soft_parts(h):
    top = jnp.maximum(h[0], h[1])
    top = jnp.maximum(top, swap_columns(top))
    e0, e1 = jnp.exp(h[0] - top), jnp.exp(h[1] - top)
    total = e0 + e1
    total = total + swap_columns(total)
    pooled = top + jnp.log(total)
    inverse = 1.0 / total
    return e0 * inverse, e1 * inverse, pooled


def soft(h):
    h = h.reshape(2, WIDE, LANES)
    q0, q1, pooled = soft_parts(h)
    return jnp.concatenate([q0 * pooled, q1 * pooled], axis=0)


def soft_pull(h, grad):
    h = h.reshape(2, WIDE, LANES)
    grad = grad.reshape(2, WIDE, LANES)
    q0, q1, pooled = soft_parts(h)
    mix = q0 * grad[0] + q1 * grad[1]
    mix = mix + swap_columns(mix)
    return jnp.concatenate(
        [q0 * (pooled * (grad[0] - mix) + mix), q1 * (pooled * (grad[1] - mix) + mix)], axis=0
    )


def norm_tables(st, group, i_own, i_oth, n_local, total):
    parts = st.shape[0]
    group = 0 if st.shape[1] == 1 else group
    blocks = [st[i, group] for i in range(parts)]
    summed = functools.reduce(jnp.add, blocks)
    mean = summed[0:1] / parts
    apart = functools.reduce(jnp.add, [jnp.square(b - mean) for b in blocks])
    rstd = lax.rsqrt((summed[1:2] + n_local * apart[0:1]) / total + EPS)
    return rstd, (st[i_own, group, 0:1] - mean) * rstd, (st[i_oth, group, 0:1] - mean) * rstd


def left_right(y0, y1, y2):
    rows = y0.shape[0]
    column = lax.broadcasted_iota(jnp.int32, y0.shape, 0) % WIDE
    before = jnp.where(column == 0, 0.0, pltpu.roll(y0, 1, 0))
    after = jnp.where(column == WIDE - 1, 0.0, pltpu.roll(y2, rows - 1, 0))
    return before + y1 + after


def lane_of(group):
    return pl.multiple_of(group * LANES, LANES)


def edge_start(n_own, edge, half):
    return pl.multiple_of((1 - half) * (n_own - edge), WIDE)


def pair_rows(j):
    return pl.ds(pl.multiple_of(j * 2 * WIDE, 2 * WIDE), 2 * WIDE)


def fold(v):
    return jnp.sum(v.reshape(v.shape[0] // 8, 8, LANES), axis=0)


def fwd_kernel(first, pool, layer, total, edge_out, *refs):
    pos, zall = refs[0], refs[1]
    if first:
        w_hbm = refs[2]
    else:
        st, gss, w_hbm = refs[2], refs[3:7], refs[7]
    hb_out, zc_out, edge_ref, st_out, hb, w, y, z, tab, hs, sem = refs[-11:]
    load = pltpu.make_async_copy(w_hbm.at[layer], w, sem.at[0])
    load.start()
    save = pltpu.make_async_copy(hb, hb_out.at[layer], sem.at[1])
    t, r = pos[0], pos[1]
    n_own = z.shape[0]
    halo_at = pl.multiple_of((1 - r) * (n_own + WIDE), WIDE)
    zero_at = pl.multiple_of(r * (n_own + WIDE), WIDE)
    hb[pl.ds(zero_at, WIDE), :] = jnp.zeros((WIDE, CHANS), BF16)
    edge = zall.shape[0] - n_own
    if not first:
        for k in range(GROUPS):
            group = t ^ k
            rstd, own, oth = norm_tables(st, group, pos[2], pos[3], float(n_own), total)
            gain, shift = gss[k][layer - 1 : layer, :], gss[k][layer + 7 : layer + 8, :]
            tab[group, 0:1] = rstd * gain
            tab[group, 1:2] = own * gain + shift
            tab[group, 2:3] = oth * gain + shift

    def act(values, group, which):
        if first:
            return values
        n = values.astype(F32) * tab[group, 0:1, :] + tab[group, which : which + 1, :]
        h = n * sigmoid(n)
        return soft(h) if pool else h

    def body(j, carry):
        at = pl.multiple_of(j * 2 * WIDE, 2 * WIDE)
        for group in range(GROUPS):
            lanes = slice(group * LANES, (group + 1) * LANES)
            h = act(zall[pl.ds(at, 2 * WIDE), lanes], group, 1)
            hb[pl.ds(pl.multiple_of(at + WIDE, WIDE), 2 * WIDE), lanes] = h.astype(BF16)
        return carry

    lax.fori_loop(0, n_own // (2 * WIDE), body, 0)
    for group in range(GROUPS):
        lanes = slice(group * LANES, (group + 1) * LANES)
        h = act(zall[n_own : n_own + edge, lanes], group, 2)
        if edge > WIDE:
            hs[...] = h
            h = hs[pl.ds(pl.multiple_of(r * WIDE, WIDE), WIDE), :]
        hb[pl.ds(halo_at, WIDE), lanes] = h.astype(BF16)
    save.start()
    load.wait()
    lhs = jnp.concatenate([hb[i * WIDE : i * WIDE + n_own, :] for i in range(3)], axis=1)
    rhs = jnp.concatenate(
        [
            jnp.concatenate([w[:, (3 * i + s) * CHANS : (3 * i + s + 1) * CHANS] for i in range(3)], axis=1)
            for s in range(3)
        ],
        axis=0,
    )
    y[...] = lax.dot_general(lhs, rhs, (((1,), (1,)), ((), ())), preferred_element_type=F32)

    def add_up(j, acc):
        rows = pair_rows(j)
        v = left_right(y[rows, 0:128], y[rows, 128:256], y[rows, 256:384])
        z[rows, :] = v
        return acc + fold(v)

    steps = n_own // (2 * WIDE)
    summed = lax.fori_loop(0, steps, add_up, jnp.zeros((8, LANES), F32))
    mean = jnp.sum(summed, axis=0, keepdims=True) / n_own

    def centre(j, acc):
        rows = pair_rows(j)
        v = z[rows, :] - mean
        z[rows, :] = v
        zc_out[rows, :] = v.astype(BF16)
        return acc + fold(jnp.square(v))

    apart = lax.fori_loop(0, steps, centre, jnp.zeros((8, LANES), F32))
    sums = jnp.concatenate([mean, jnp.sum(apart, axis=0, keepdims=True)], axis=0)
    for i in range(st_out.shape[0]):
        st_out[i] = sums
    edge_ref[...] = zc_out[pl.ds(edge_start(n_own, edge_out, r), edge_out), :]
    zc_out[n_own : n_own + edge_out, :] = jnp.zeros((edge_out, LANES), BF16)
    save.wait()


def fwd_step(layer, pool, edge_out, total, pos, slots, st, tables, weights, kept, n_own, devices, ties):
    first = st is None
    layers = weights.shape[0]
    extra = () if first else (st, *tables)
    return pl.pallas_call(
        functools.partial(fwd_kernel, first, pool, layer, total, edge_out),
        out_shape=(
            pltpu.HBM((layers, n_own + 2 * WIDE, CHANS), BF16),
            pltpu.VMEM((n_own + edge_out, LANES), BF16),
            pltpu.VMEM((edge_out, LANES), BF16),
            pltpu.VMEM((devices, 2, LANES), F32),
        ),
        in_specs=[SMEM] + [VMEM] * (1 + len(extra)) + [ANY] * (1 if first else 2) + [FREE] * len(ties),
        out_specs=(ANY, VMEM, VMEM, VMEM),
        input_output_aliases={} if first else {3 + len(extra): 0},
        scratch_shapes=[
            pltpu.VMEM((n_own + 2 * WIDE, CHANS), BF16),
            pltpu.VMEM((LANES, 9 * CHANS), BF16),
            pltpu.VMEM((n_own, 3 * LANES), F32),
            pltpu.VMEM((n_own, LANES), F32),
            pltpu.VMEM((GROUPS, 8, LANES), F32),
            pltpu.VMEM((2 * WIDE, LANES), F32),
            pltpu.SemaphoreType.DMA((2,)),
        ],
        compiler_params=PARAMS,
        cost_estimate=pl.CostEstimate(
            flops=2 * n_own * 9 * CHANS * LANES, bytes_accessed=4 * 1024 * 1024, transcendentals=n_own * CHANS
        ),
        name="conv_forward",
    )(pos, slots, *extra, in_hbm(weights), *(() if first else (in_hbm(kept),)), *ties)


def below_kernel(layer, pool, total, top, *refs):
    pos, zc, st, gs = refs[:4]
    if top:
        terms, h_out, dn_out, msg, tab = refs[4:]
    else:
        terms, (dn_out, msg, tab) = refs[4:8], refs[-3:]
    n_own = dn_out.shape[0]
    rstd, own, oth = norm_tables(st, pos[0], pos[2], pos[3], float(n_own), total)
    tab[0:1], tab[1:2] = rstd, own
    tab[2:3], tab[3:4] = gs[layer : layer + 1, :], gs[layer + 8 : layer + 9, :]

    def body(j, accs):
        rows = pair_rows(j)
        xhat = zc[rows, :].astype(F32) * tab[0:1, :] + tab[1:2, :]
        n = xhat * tab[2:3, :] + tab[3:4, :]
        sig = sigmoid(n)
        h = n * sig
        if top:
            g = terms[rows, :].astype(F32)
            h_out[rows, :] = h.astype(BF16)
        else:
            g = functools.reduce(jnp.add, [term[rows, :].astype(F32) for term in terms])
        if pool:
            g = soft_pull(h, g)
        dn = g * (sig * (1.0 + n - h))
        dn_out[rows, :] = dn
        return accs[0] + fold(dn), accs[1] + fold(dn * xhat)

    zero = jnp.zeros((8, LANES), F32)
    sums = lax.fori_loop(0, n_own // (2 * WIDE), body, (zero, zero))
    sums = [jnp.sum(v, axis=0, keepdims=True) for v in sums]
    msg[0:WIDE, :] = dn_out[pl.ds(edge_start(n_own, WIDE, pos[1]), WIDE), :]
    msg[WIDE : WIDE + 8, :] = jnp.concatenate(sums + [jnp.zeros((6, LANES), F32)], axis=0)


def below_step(layer, pool, total, pos, zc, st, gs, terms, ties=()):
    n_own = terms[0].shape[0]
    top = len(terms) == 1
    out_shape = [
        pltpu.VMEM((n_own, LANES), F32),
        pltpu.VMEM((WIDE + 8, LANES), F32),
    ]
    if top:
        out_shape = [jax.ShapeDtypeStruct((n_own, LANES), BF16)] + out_shape
    return pl.pallas_call(
        functools.partial(below_kernel, layer, pool, total, top),
        out_shape=tuple(out_shape),
        in_specs=[SMEM] + [VMEM] * (3 + len(terms)) + [FREE] * len(ties),
        out_specs=(VMEM,) * len(out_shape),
        scratch_shapes=[pltpu.VMEM((8, LANES), F32)],
        compiler_params=PARAMS,
        cost_estimate=LITTLE,
        name="silu_backward",
    )(pos, zc, st, gs, *terms, *ties)


def bwd_kernel(layer, total, *refs):
    pos, dn, dedge, sums, zc, st, gs, w_hbm = refs[:8]
    outs, d_out, d, w, y, tab, sem = refs[-10:-6], *refs[-6:]
    load = pltpu.make_async_copy(w_hbm.at[layer], w, sem)
    load.start()
    t, r = pos[0], pos[1]
    n_own = dn.shape[0]
    halo_at = pl.multiple_of((1 - r) * (n_own + WIDE), WIDE)
    zero_at = pl.multiple_of(r * (n_own + WIDE), WIDE)
    edge = zc.shape[0] - n_own
    d[pl.ds(zero_at, WIDE), :] = jnp.zeros((WIDE, 3 * LANES), BF16)
    rstd, own, oth = norm_tables(st, t, pos[2], pos[3], float(n_own), total)
    scale = gs[layer : layer + 1, :] * rstd
    shift_sum, gain_sum = sums[0:1, :], sums[1:2, :]
    slope = scale * gain_sum / total
    tab[0:1] = scale
    tab[1:2] = slope * rstd
    tab[2:3] = scale * shift_sum / total + slope * own
    tab[3:4] = scale * shift_sum / total + slope * oth

    def spread_columns(v, at):
        rows = v.shape[0]
        column = lax.broadcasted_iota(jnp.int32, v.shape, 0) % WIDE
        ahead = jnp.where(column == WIDE - 1, 0.0, pltpu.roll(v, rows - 1, 0))
        behind = jnp.where(column == 0, 0.0, pltpu.roll(v, 1, 0))
        d[pl.ds(at, rows), 0:128] = ahead.astype(BF16)
        d[pl.ds(at, rows), 128:256] = v.astype(BF16)
        d[pl.ds(at, rows), 256:384] = behind.astype(BF16)

    def body(j, carry):
        rows = pair_rows(j)
        v = dn[rows, :] * tab[0:1, :] - tab[2:3, :] - zc[rows, :].astype(F32) * tab[1:2, :]
        spread_columns(v, pl.multiple_of(j * 2 * WIDE + WIDE, WIDE))
        return carry

    lax.fori_loop(0, n_own // (2 * WIDE), body, 0)
    near = n_own if edge == WIDE else pl.multiple_of(n_own + r * WIDE, WIDE)
    near = zc[pl.ds(near, WIDE), :].astype(F32)
    spread_columns(dedge[0:WIDE, :] * tab[0:1, :] - tab[3:4, :] - near * tab[1:2, :], halo_at)
    d_out[...] = d[WIDE : WIDE + n_own, :]
    load.wait()
    lhs = jnp.concatenate([d[(2 - i) * WIDE : (2 - i) * WIDE + n_own, :] for i in range(3)], axis=1)
    rhs = jnp.concatenate([w[:, i * CHANS : (i + 1) * CHANS] for i in range(9)], axis=0)
    y[...] = jnp.dot(lhs, rhs, preferred_element_type=F32)

    def share(j, carry):
        rows = pair_rows(j)
        for k in range(GROUPS):
            outs[k][rows, :] = y[rows, pl.ds(lane_of(t ^ k), LANES)].astype(BF16)
        return carry

    lax.fori_loop(0, n_own // (2 * WIDE), share, 0)


def bwd_step(layer, total, pos, dn, dedge, sums, zc, st, gs, weights, ties):
    n_own = dn.shape[0]
    part = pltpu.VMEM((n_own, LANES), BF16)
    return pl.pallas_call(
        functools.partial(bwd_kernel, layer, total),
        out_shape=(
            part,
            part,
            part,
            part,
            pltpu.VMEM((n_own, 3 * LANES), BF16),
        ),
        in_specs=[SMEM] + [VMEM] * 6 + [ANY] + [FREE] * len(ties),
        out_specs=(VMEM,) * 5,
        scratch_shapes=[
            pltpu.VMEM((n_own + 2 * WIDE, 3 * LANES), BF16),
            pltpu.VMEM((LANES, 9 * CHANS), BF16),
            pltpu.VMEM((n_own, CHANS), F32),
            pltpu.VMEM((8, LANES), F32),
            pltpu.SemaphoreType.DMA,
        ],
        compiler_params=PARAMS,
        cost_estimate=LITTLE,
        name="conv_backward",
    )(pos, dn, dedge, sums, zc, st, gs, in_hbm(weights), *ties)


def last_kernel(t0, t1, t2, t3, *refs):
    out = refs[-1]

    def body(j, carry):
        rows = pair_rows(j)
        out[rows, :] = functools.reduce(jnp.add, [term[rows, :].astype(F32) for term in (t0, t1, t2, t3)])
        return carry

    lax.fori_loop(0, out.shape[0] // (2 * WIDE), body, 0)


def last_step(terms, ties):
    return pl.pallas_call(
        last_kernel,
        out_shape=jax.ShapeDtypeStruct(terms[0].shape, F32),
        in_specs=[VMEM] * 4 + [FREE] * len(ties),
        out_specs=VMEM,
        compiler_params=PARAMS,
        cost_estimate=LITTLE,
        name="add_terms",
    )(*terms, *ties)


def halves_kernel(keep, got, out):
    out[...] = (keep[...].astype(F32) + got[...].astype(F32)).astype(BF16)


def add_halves(keep, got):
    return pl.pallas_call(
        halves_kernel,
        out_shape=jax.ShapeDtypeStruct(keep.shape, BF16),
        in_specs=[VMEM] * 2,
        out_specs=VMEM,
        compiler_params=PARAMS,
        cost_estimate=LITTLE,
        name="add_halves",
    )(keep, got)


def wgrad_kernel(layer, pos, d, hb_hbm, *refs):
    keep, send, hb, grad, sem = refs[-5:]
    load = pltpu.make_async_copy(hb_hbm.at[layer], hb, sem)
    load.start()
    n_own = d.shape[0]
    lhs = d[...]
    load.wait()
    for i in range(3):
        part = lax.dot_general(
            lhs, hb[i * WIDE : i * WIDE + n_own, :], (((0,), (0,)), ((), ())), preferred_element_type=F32
        ).astype(BF16)
        for s in range(3):
            grad[:, (3 * i + s) * CHANS : (3 * i + s + 1) * CHANS] = part[s * LANES : (s + 1) * LANES]
    half = LANES // 2
    keep[...] = grad[pl.ds(pl.multiple_of(pos[1] * half, half), half), :]
    send[...] = grad[pl.ds(pl.multiple_of((1 - pos[1]) * half, half), half), :]


def wgrad_step(layer, pos, d, kept, ties):
    half = pltpu.VMEM((LANES // 2, 9 * CHANS), BF16)
    return pl.pallas_call(
        functools.partial(wgrad_kernel, layer),
        out_shape=(half, half),
        in_specs=[SMEM, VMEM, ANY] + [FREE] * len(ties),
        out_specs=(VMEM, VMEM),
        scratch_shapes=[
            pltpu.VMEM(kept.shape[1:], BF16),
            pltpu.VMEM((LANES, 9 * CHANS), BF16),
            pltpu.SemaphoreType.DMA,
        ],
        compiler_params=PARAMS,
        cost_estimate=LITTLE,
        name="kernel_gradient",
    )(pos, d, in_hbm(kept), *ties)


def place_kernel(layers, fresh, pos, *refs):
    count = 2 * len(layers)
    sources = refs[:count]
    out, held, wide, sem = refs[-4:]
    half = LANES // 2
    r = pos[1]
    loads = [pltpu.make_async_copy(sources[j], held.at[j], sem.at[j]) for j in range(count)]
    for load in loads:
        load.start()
    stores = []
    for j in range(count):
        at = pl.multiple_of((r if j % 2 == 0 else 1 - r) * half, half)
        if j >= 2:
            stores[j - 2].wait()
        loads[j].wait()
        wide[j % 2] = held[j].astype(F32)
        store = pltpu.make_async_copy(wide.at[j % 2], out.at[layers[j // 2], pl.ds(at, half)], sem.at[count + j])
        store.start()
        stores.append(store)
    for store in stores[-2:]:
        store.wait()


def place_step(layers, pos, sources, whole, count):
    half = LANES // 2
    jobs = len(sources)
    return pl.pallas_call(
        functools.partial(place_kernel, layers, whole is None),
        out_shape=pltpu.HBM((count, LANES, 9 * CHANS), F32),
        in_specs=[SMEM] + [ANY] * jobs + ([] if whole is None else [ANY]),
        out_specs=ANY,
        input_output_aliases={} if whole is None else {1 + jobs: 0},
        scratch_shapes=[
            pltpu.VMEM((jobs, half, 9 * CHANS), BF16),
            pltpu.VMEM((2, half, 9 * CHANS), F32),
            pltpu.SemaphoreType.DMA((2 * jobs,)),
        ],
        compiler_params=PARAMS,
        cost_estimate=LITTLE,
        name="place_gradients",
    )(pos, *[in_hbm(v) for v in sources], *(() if whole is None else (in_hbm(whole),)))


def swap_with(value, axis, k):
    return lax.ppermute(value, axis, [(i, i ^ k) for i in range(lax.axis_size(axis))])


def spread(own):
    return (own, *[swap_with(own, "tensor", k) for k in range(1, GROUPS)])


def halo_of_input(x, half):
    n_own = x.shape[0]
    edge = jnp.where(half == 0, x[n_own - WIDE :], x[:WIDE])
    return jnp.concatenate([x, swap_with(edge, "rows", 1)], axis=0)


def fast_local(section_input, conv_weights, norm_gains, norm_shifts, out_grad, out_mask):
    images, rows_here, width = out_mask.shape
    layers = conv_weights.shape[0]
    n_own = rows_here * width
    parts = lax.axis_size("dp") * lax.axis_size("rows")
    total = float(n_own * parts)
    t, half = lax.axis_index("tensor"), lax.axis_index("rows")
    image = lax.axis_index("dp")
    pos = jnp.stack([t, half, 2 * image + half, 2 * image + 1 - half]).astype(jnp.int32)
    middle = layers // 2
    x = to_maps(section_input, width).reshape(n_own, LANES)
    slots = lax.all_gather(halo_of_input(x, half), "tensor", axis=1, tiled=True)
    pad = jnp.zeros((8 - layers, LANES), F32)
    tables = spread(jnp.concatenate([norm_gains, pad, norm_shifts, pad], axis=0))
    top_grad = (to_maps(out_grad, width) * out_mask[..., None].astype(BF16)).reshape(n_own, LANES)

    st, kept = None, None
    halves = ("dp", "rows")
    kept_z, kept_st = [], []
    for layer in range(layers):
        last = layer + 1 == layers
        edge = 2 * WIDE if layer + 1 == middle else WIDE
        everyone = halves if last else (*halves, "tensor")
        devices = parts if last else parts * GROUPS
        kept, zc, rim, local = fwd_step(
            layer,
            layer == middle,
            edge,
            total,
            pos,
            slots,
            st,
            tables,
            conv_weights,
            kept,
            n_own,
            devices,
            (top_grad,) if layer == 2 else (),
        )
        rim = swap_with(rim, "rows", 1)
        st = lax.all_to_all(local, everyone, split_axis=0, concat_axis=0, tiled=True)
        st = st.reshape(parts, devices // parts, 2, LANES)
        zc = lax.dynamic_update_slice_in_dim(zc, rim, n_own, axis=0)
        kept_z.append(zc)
        kept_st.append(st)
        if not last:
            slots = lax.all_gather(zc, "tensor", axis=1, tiled=True)
    top = layers - 1
    h_last, dn, msg = below_step(top, False, total, pos, kept_z[top], kept_st[top], tables[0], (top_grad,))

    def with_other(values):
        return [v for mine in values for v in (mine, swap_with(mine, "rows", 1))]

    sum_list, pairs = [None] * layers, [None] * layers
    ahead, back = [[0, 1, 2, 3]], [[3, 2, 1, 0]]
    urgent = ()
    for layer in range(layers - 1, -1, -1):
        got = swap_with(msg, "rows", 1)
        sums = msg[WIDE:] + got[WIDE:]
        one, two, three = (swap_with(sums, "dp", k) for k in (1, 2, 3))
        sums = (sums + one) + (two + three)
        sum_list[layer] = sums
        *terms, d = bwd_step(
            layer, total, pos, dn, got, sums, kept_z[layer], kept_st[layer], tables[0], conv_weights, urgent
        )
        terms = (terms[0], *[swap_with(terms[k], "tensor", k) for k in range(1, GROUPS)])
        keep, send = wgrad_step(layer, pos, d, kept, ())
        other = swap_with(send, "rows", 1)
        pairs[layer] = add_halves(keep, other)
        urgent = (other,)
        settled = (pairs[layer],) if layer % 2 == 0 else ()
        if layer % 2 == 0 and layer + 1 < layers:
            settled = (pairs[layer + 1], *settled)
        if layer == 4:
            upper = lax.psum((pairs[5], pairs[4]), "dp", axis_index_groups=ahead)
        if layer == 2:
            mid = lax.psum((pairs[3], pairs[2]), "dp", axis_index_groups=back)
        if layer > 0:
            below = layer - 1
            late = (in_hbm(upper[0]),) if layer == 2 else ()
            dn, msg = below_step(
                below, layer == middle, total, pos, kept_z[below], kept_st[below], tables[0], terms, (keep, *settled, *late)
            )
        else:
            grad = last_step(terms, (*settled, in_hbm(mid[0])))
    tied, upper = lax.optimization_barrier(((pairs[1], pairs[0]), upper))
    lower = lax.psum(tied, "dp", axis_index_groups=ahead)
    shape = (images, rows_here, width, LANES)
    outputs = (from_maps(h_last.reshape(shape)), from_maps(grad.reshape(shape)))
    whole = place_step((5, 4, 3, 2), pos, with_other((*upper, *mid)), None, layers)
    sums = jnp.stack(sum_list)
    sums = (sums[:, 1], sums[:, 0])
    lower, whole, outputs, sums = lax.optimization_barrier((lower, whole, outputs, sums))
    whole = place_step((1, 0), pos, with_other(lower), whole, layers)
    return (*outputs, whole, *sums)


def solution(mesh):
    in_specs = (
        P("dp", "rows", "tensor"),
        P(None, "tensor", None),
        P(None, "tensor"),
        P(None, "tensor"),
        P("dp", "rows", "tensor"),
        P("dp", "rows", None),
    )
    out_specs = (
        P("dp", "rows", "tensor"),
        P("dp", "rows", "tensor"),
        P(None, "tensor", None),
        P(None, "tensor"),
        P(None, "tensor"),
    )
    local = fast_local if fits_kernels(mesh) else generic_local
    return jax.shard_map(local, mesh=mesh, in_specs=in_specs, out_specs=out_specs, check_vma=False)
```

```python
import functools

import jax
import jax.numpy as jnp
from jax import lax
from jax.experimental import pallas as pl
from jax.experimental.pallas import tpu as pltpu
from jax.sharding import PartitionSpec as P

EPS = 1e-05


def padded_2(cells, sides, width):
    for axis, dim in sides:
        count = lax.axis_size(axis)
        ends = count - 1
        head = lax.slice_in_dim(cells, 0, width, axis=dim)
        tail = lax.slice_in_dim(cells, cells.shape[dim] - width, cells.shape[dim], axis=dim)
        cells = jnp.concatenate(
            [
                lax.ppermute(tail, axis, [(i, (i + 1) % count) for i in range(ends)]),
                cells,
                lax.ppermute(head, axis, [((i + 1) % count, i) for i in range(ends)]),
            ],
            axis=dim,
        )
    return cells


def to_maps(flat, width):
    count, high, merged = flat.shape
    return flat.reshape(count, high, merged // width, width).transpose(0, 1, 3, 2)


def from_maps(maps):
    count, high, wide, chans = maps.shape
    return maps.transpose(0, 1, 3, 2).reshape(count, high, chans * wide)


def spatial_conv(padded, kernel):
    return lax.conv_general_dilated(
        padded,
        kernel,
        (1, 1),
        ((0, 0), (1, 1)),
        dimension_numbers=("NHWC", "HWIO", "NHWC"),
        preferred_element_type=jnp.float32,
    )


def flipped(kernel):
    return jnp.transpose(kernel[::-1, ::-1], (0, 1, 3, 2))


def pool_unpool(values):
    count, high, wide, chans = values.shape
    blocks = values.reshape(count, high // 2, 2, wide // 2, 2, chans)
    pooled = jax.nn.logsumexp(blocks, axis=(2, 4), keepdims=True)
    return (jnp.exp(blocks - pooled) * pooled).reshape(values.shape)


def moments(conv_out, total_pixels):
    summed = lax.psum(jnp.sum(conv_out, axis=(0, 1, 2)), ("dp", "rows"))
    mean = summed / total_pixels
    spread = lax.psum(jnp.sum(jnp.square(conv_out - mean), axis=(0, 1, 2)), ("dp", "rows"))
    var = spread / total_pixels
    return (mean, lax.rsqrt(var + EPS))


def kernel_grad(whole, dconv):
    images, rows_here, width, chans = dconv.shape
    widened = jnp.pad(whole, ((0, 0), (0, 0), (1, 1), (0, 0)))
    stacked = []
    for row_off in range(3):
        line = []
        for col_off in range(3):
            window = widened[:, row_off : row_off + rows_here, col_off : col_off + width, :]
            line.append(
                jnp.einsum("bhwc,bhwo->co", window, dconv, preferred_element_type=jnp.float32)
            )
        stacked.append(jnp.stack(line))
    return jnp.stack(stacked)


def generic_local(section_input, conv_weights, norm_gains, norm_shifts, out_grad, out_mask):
    width = out_mask.shape[2]
    images, rows_here = (out_mask.shape[0], out_mask.shape[1])
    total_pixels = float(images * rows_here * width * lax.axis_size("dp") * lax.axis_size("rows"))
    layers, out_here, flat_in = conv_weights.shape
    chans_in = flat_in // 9
    kernels_hwio = conv_weights.reshape(layers, out_here, 3, 3, chans_in).transpose(0, 2, 3, 4, 1)
    middle = layers // 2
    kept = []
    acting = to_maps(section_input, width)
    current = acting.astype(jnp.float32)
    pre_pool = current
    for index in range(layers):
        if index == middle:
            pre_pool = current
            acting = pool_unpool(pre_pool).astype(jnp.bfloat16)
        padded = padded_2(acting, (("rows", 1),), 1)
        whole = lax.all_gather(padded, "tensor", axis=3, tiled=True)
        conv_out = spatial_conv(whole, kernels_hwio[index])
        mean, rstd = moments(conv_out, total_pixels)
        normed = (conv_out - mean) * rstd
        shifted = normed * norm_gains[index] + norm_shifts[index]
        current = jax.nn.silu(shifted)
        acting = current.astype(jnp.bfloat16)
        kept.append((whole, normed, shifted, rstd))
    grad = to_maps(out_grad, width).astype(jnp.float32) * out_mask[..., None].astype(jnp.float32)
    kernel_list = [None] * layers
    gain_list = [None] * layers
    shift_list = [None] * layers
    for index in range(layers - 1, -1, -1):
        whole, normed, shifted, rstd = kept[index]
        unused, pull_silu = jax.vjp(jax.nn.silu, shifted)
        dshift = pull_silu(grad)[0]
        gain_sum, shift_sum = lax.psum(
            (jnp.sum(dshift * normed, axis=(0, 1, 2)), jnp.sum(dshift, axis=(0, 1, 2))),
            ("dp", "rows"),
        )
        gain_list[index] = gain_sum
        shift_list[index] = shift_sum
        dconv = (
            norm_gains[index]
            * rstd
            * (dshift - shift_sum / total_pixels - normed * gain_sum / total_pixels)
        ).astype(jnp.bfloat16)
        summed_kernel = lax.psum(
            kernel_grad(whole, dconv).astype(jnp.bfloat16), ("dp", "rows")
        ).astype(jnp.float32)
        kernel_list[index] = summed_kernel.transpose(3, 0, 1, 2).reshape(out_here, flat_in)
        grad_rim = padded_2(dconv, (("rows", 1),), 1)
        partial_terms = spatial_conv(grad_rim, flipped(kernels_hwio[index]))
        grad_in = lax.psum_scatter(
            partial_terms.astype(jnp.bfloat16), "tensor", scatter_dimension=3, tiled=True
        ).astype(jnp.float32)
        if index == middle:
            unused, pull_pool = jax.vjp(pool_unpool, pre_pool)
            grad = pull_pool(grad_in)[0]
        else:
            grad = grad_in
    return (
        from_maps(acting),
        from_maps(grad),
        jnp.stack(kernel_list),
        jnp.stack(gain_list),
        jnp.stack(shift_list),
    )


GROUPS = 4
LANES = 128
WIDE = 48
CHANS = GROUPS * LANES
F32 = jnp.float32
BF16 = jnp.bfloat16
VMEM = pl.BlockSpec(memory_space=pltpu.VMEM)
SMEM = pl.BlockSpec(memory_space=pltpu.SMEM)
ANY = pl.BlockSpec(memory_space=pltpu.HBM)
FREE = pl.BlockSpec(memory_space=pl.ANY)
LITTLE = pl.CostEstimate(flops=1024, bytes_accessed=1024, transcendentals=0)
PARAMS = pltpu.CompilerParams(vmem_limit_bytes=20 * 1024 * 1024)


def in_hbm(value):
    return pltpu.with_memory_space_constraint(value, pltpu.HBM)


def fits_kernels(mesh):
    return mesh.shape["tensor"] == GROUPS and mesh.shape["rows"] == 2 and mesh.shape["dp"] == 4


def sigmoid(v):
    return 0.5 * jnp.tanh(0.5 * v) + 0.5


def swap_columns(v):
    column = lax.broadcasted_iota(jnp.int32, v.shape, 0)
    return jnp.where(column % 2 == 0, pltpu.roll(v, WIDE - 1, 0), pltpu.roll(v, 1, 0))


def soft_parts(h):
    top = jnp.maximum(h[0], h[1])
    top = jnp.maximum(top, swap_columns(top))
    e0, e1 = jnp.exp(h[0] - top), jnp.exp(h[1] - top)
    total = e0 + e1
    total = total + swap_columns(total)
    pooled = top + jnp.log(total)
    inverse = 1.0 / total
    return e0 * inverse, e1 * inverse, pooled


def soft(h):
    h = h.reshape(2, WIDE, LANES)
    q0, q1, pooled = soft_parts(h)
    return jnp.concatenate([q0 * pooled, q1 * pooled], axis=0)


def soft_pull(h, grad):
    h = h.reshape(2, WIDE, LANES)
    grad = grad.reshape(2, WIDE, LANES)
    q0, q1, pooled = soft_parts(h)
    mix = q0 * grad[0] + q1 * grad[1]
    mix = mix + swap_columns(mix)
    return jnp.concatenate(
        [q0 * (pooled * (grad[0] - mix) + mix), q1 * (pooled * (grad[1] - mix) + mix)], axis=0
    )


def norm_tables(st, group, i_own, i_oth, n_local, total):
    parts = st.shape[0]
    group = 0 if st.shape[1] == 1 else group
    blocks = [st[i, group] for i in range(parts)]
    summed = functools.reduce(jnp.add, blocks)
    mean = summed[0:1] / parts
    apart = functools.reduce(jnp.add, [jnp.square(b - mean) for b in blocks])
    rstd = lax.rsqrt((summed[1:2] + n_local * apart[0:1]) / total + EPS)
    return rstd, (st[i_own, group, 0:1] - mean) * rstd, (st[i_oth, group, 0:1] - mean) * rstd


def left_right(y0, y1, y2):
    rows = y0.shape[0]
    column = lax.broadcasted_iota(jnp.int32, y0.shape, 0) % WIDE
    before = jnp.where(column == 0, 0.0, pltpu.roll(y0, 1, 0))
    after = jnp.where(column == WIDE - 1, 0.0, pltpu.roll(y2, rows - 1, 0))
    return before + y1 + after


def lane_of(group):
    return pl.multiple_of(group * LANES, LANES)


def edge_start(n_own, edge, half):
    return pl.multiple_of((1 - half) * (n_own - edge), WIDE)


def pair_rows(j):
    return pl.ds(pl.multiple_of(j * 2 * WIDE, 2 * WIDE), 2 * WIDE)


def fold(v):
    return jnp.sum(v.reshape(v.shape[0] // 8, 8, LANES), axis=0)


def fwd_kernel(first, pool, layer, total, edge_out, *refs):
    pos, zall = refs[0], refs[1]
    if first:
        w_hbm = refs[2]
    else:
        st, gss, w_hbm = refs[2], refs[3:7], refs[7]
    hb_out, zc_out, edge_ref, st_out, hb, w, y, z, tab, hs, sem = refs[-11:]
    load = pltpu.make_async_copy(w_hbm.at[layer], w, sem.at[0])
    load.start()
    save = pltpu.make_async_copy(hb, hb_out.at[layer], sem.at[1])
    t, r = pos[0], pos[1]
    n_own = z.shape[0]
    halo_at = pl.multiple_of((1 - r) * (n_own + WIDE), WIDE)
    zero_at = pl.multiple_of(r * (n_own + WIDE), WIDE)
    hb[pl.ds(zero_at, WIDE), :] = jnp.zeros((WIDE, CHANS), BF16)
    edge = zall.shape[0] - n_own
    if not first:
        for k in range(GROUPS):
            group = t ^ k
            rstd, own, oth = norm_tables(st, group, pos[2], pos[3], float(n_own), total)
            gain, shift = gss[k][layer - 1 : layer, :], gss[k][layer + 7 : layer + 8, :]
            tab[group, 0:1] = rstd * gain
            tab[group, 1:2] = own * gain + shift
            tab[group, 2:3] = oth * gain + shift

    def act(values, group, which):
        if first:
            return values
        n = values.astype(F32) * tab[group, 0:1, :] + tab[group, which : which + 1, :]
        h = n * sigmoid(n)
        return soft(h) if pool else h

    def body(j, carry):
        at = pl.multiple_of(j * 2 * WIDE, 2 * WIDE)
        for group in range(GROUPS):
            lanes = slice(group * LANES, (group + 1) * LANES)
            h = act(zall[pl.ds(at, 2 * WIDE), lanes], group, 1)
            hb[pl.ds(pl.multiple_of(at + WIDE, WIDE), 2 * WIDE), lanes] = h.astype(BF16)
        return carry

    lax.fori_loop(0, n_own // (2 * WIDE), body, 0, unroll=3)
    for group in range(GROUPS):
        lanes = slice(group * LANES, (group + 1) * LANES)
        h = act(zall[n_own : n_own + edge, lanes], group, 2)
        if edge > WIDE:
            hs[...] = h
            h = hs[pl.ds(pl.multiple_of(r * WIDE, WIDE), WIDE), :]
        hb[pl.ds(halo_at, WIDE), lanes] = h.astype(BF16)
    save.start()
    load.wait()
    rhs = jnp.concatenate(
        [
            jnp.concatenate([w[:, (3 * i + s) * CHANS : (3 * i + s + 1) * CHANS] for i in range(3)], axis=1)
            for s in range(3)
        ],
        axis=0,
    )
    block = n_own // 3
    for j in range(3):
        at = j * block
        lhs = jnp.concatenate([hb[at + i * WIDE : at + i * WIDE + block, :] for i in range(3)], axis=1)
        y[at : at + block, :] = lax.dot_general(lhs, rhs, (((1,), (1,)), ((), ())), preferred_element_type=F32)

    def add_up(j, acc):
        rows = pair_rows(j)
        v = left_right(y[rows, 0:128], y[rows, 128:256], y[rows, 256:384])
        z[rows, :] = v
        return acc + fold(v)

    steps = n_own // (2 * WIDE)
    summed = lax.fori_loop(0, steps, add_up, jnp.zeros((8, LANES), F32), unroll=3)
    mean = jnp.sum(summed, axis=0, keepdims=True) / n_own

    def centre(j, acc):
        rows = pair_rows(j)
        v = z[rows, :] - mean
        z[rows, :] = v
        zc_out[rows, :] = v.astype(BF16)
        return acc + fold(jnp.square(v))

    apart = lax.fori_loop(0, steps, centre, jnp.zeros((8, LANES), F32), unroll=3)
    sums = jnp.concatenate([mean, jnp.sum(apart, axis=0, keepdims=True)], axis=0)
    for i in range(st_out.shape[0]):
        st_out[i] = sums
    edge_ref[...] = zc_out[pl.ds(edge_start(n_own, edge_out, r), edge_out), :]
    zc_out[n_own : n_own + edge_out, :] = jnp.zeros((edge_out, LANES), BF16)
    save.wait()


def fwd_step(layer, pool, edge_out, total, pos, slots, st, tables, weights, kept, n_own, devices, ties):
    first = st is None
    layers = weights.shape[0]
    extra = () if first else (st, *tables)
    return pl.pallas_call(
        functools.partial(fwd_kernel, first, pool, layer, total, edge_out),
        out_shape=(
            pltpu.HBM((layers, n_own + 2 * WIDE, CHANS), BF16),
            pltpu.VMEM((n_own + edge_out, LANES), BF16),
            pltpu.VMEM((edge_out, LANES), BF16),
            pltpu.VMEM((devices, 2, LANES), F32),
        ),
        in_specs=[SMEM] + [VMEM] * (1 + len(extra)) + [ANY] * (1 if first else 2) + [FREE] * len(ties),
        out_specs=(ANY, VMEM, VMEM, VMEM),
        input_output_aliases={} if first else {3 + len(extra): 0},
        scratch_shapes=[
            pltpu.VMEM((n_own + 2 * WIDE, CHANS), BF16),
            pltpu.VMEM((LANES, 9 * CHANS), BF16),
            pltpu.VMEM((n_own, 3 * LANES), F32),
            pltpu.VMEM((n_own, LANES), F32),
            pltpu.VMEM((GROUPS, 8, LANES), F32),
            pltpu.VMEM((2 * WIDE, LANES), F32),
            pltpu.SemaphoreType.DMA((2,)),
        ],
        compiler_params=PARAMS,
        cost_estimate=pl.CostEstimate(
            flops=2 * n_own * 9 * CHANS * LANES, bytes_accessed=4 * 1024 * 1024, transcendentals=n_own * CHANS
        ),
        name="conv_forward",
    )(pos, slots, *extra, in_hbm(weights), *(() if first else (in_hbm(kept),)), *ties)


def below_kernel(layer, pool, total, top, *refs):
    pos, zc, st, gs = refs[:4]
    if top:
        terms, h_out, dn_out, msg, tab = refs[4:]
    else:
        terms, (dn_out, msg, tab) = refs[4:8], refs[-3:]
    n_own = dn_out.shape[0]
    rstd, own, oth = norm_tables(st, pos[0], pos[2], pos[3], float(n_own), total)
    tab[0:1], tab[1:2] = rstd, own
    tab[2:3], tab[3:4] = gs[layer : layer + 1, :], gs[layer + 8 : layer + 9, :]

    def body(j, accs):
        rows = pair_rows(j)
        xhat = zc[rows, :].astype(F32) * tab[0:1, :] + tab[1:2, :]
        n = xhat * tab[2:3, :] + tab[3:4, :]
        sig = sigmoid(n)
        h = n * sig
        if top:
            g = terms[rows, :].astype(F32)
            h_out[rows, :] = h.astype(BF16)
        else:
            g = functools.reduce(jnp.add, [term[rows, :].astype(F32) for term in terms])
        if pool:
            g = soft_pull(h, g)
        dn = g * (sig * (1.0 + n - h))
        dn_out[rows, :] = dn
        return accs[0] + fold(dn), accs[1] + fold(dn * xhat)

    zero = jnp.zeros((8, LANES), F32)
    sums = lax.fori_loop(0, n_own // (2 * WIDE), body, (zero, zero), unroll=3)
    sums = [jnp.sum(v, axis=0, keepdims=True) for v in sums]
    msg[0:WIDE, :] = dn_out[pl.ds(edge_start(n_own, WIDE, pos[1]), WIDE), :]
    msg[WIDE : WIDE + 8, :] = jnp.concatenate(sums + [jnp.zeros((6, LANES), F32)], axis=0)


def below_step(layer, pool, total, pos, zc, st, gs, terms, ties=()):
    n_own = terms[0].shape[0]
    top = len(terms) == 1
    out_shape = [
        pltpu.VMEM((n_own, LANES), F32),
        pltpu.VMEM((WIDE + 8, LANES), F32),
    ]
    if top:
        out_shape = [jax.ShapeDtypeStruct((n_own, LANES), BF16)] + out_shape
    return pl.pallas_call(
        functools.partial(below_kernel, layer, pool, total, top),
        out_shape=tuple(out_shape),
        in_specs=[SMEM] + [VMEM] * (3 + len(terms)) + [FREE] * len(ties),
        out_specs=(VMEM,) * len(out_shape),
        scratch_shapes=[pltpu.VMEM((8, LANES), F32)],
        compiler_params=PARAMS,
        cost_estimate=LITTLE,
        name="silu_backward",
    )(pos, zc, st, gs, *terms, *ties)


def bwd_kernel(layer, total, *refs):
    pos, dn, dedge, sums, zc, st, gs, w_hbm = refs[:8]
    outs, d_out, d, w, y, tab, sem = refs[-10:-6], *refs[-6:]
    load = pltpu.make_async_copy(w_hbm.at[layer], w, sem)
    load.start()
    t, r = pos[0], pos[1]
    n_own = dn.shape[0]
    halo_at = pl.multiple_of((1 - r) * (n_own + WIDE), WIDE)
    zero_at = pl.multiple_of(r * (n_own + WIDE), WIDE)
    edge = zc.shape[0] - n_own
    d[pl.ds(zero_at, WIDE), :] = jnp.zeros((WIDE, 3 * LANES), BF16)
    rstd, own, oth = norm_tables(st, t, pos[2], pos[3], float(n_own), total)
    scale = gs[layer : layer + 1, :] * rstd
    shift_sum, gain_sum = sums[0:1, :], sums[1:2, :]
    slope = scale * gain_sum / total
    tab[0:1] = scale
    tab[1:2] = slope * rstd
    tab[2:3] = scale * shift_sum / total + slope * own
    tab[3:4] = scale * shift_sum / total + slope * oth

    def spread_columns(v, at):
        rows = v.shape[0]
        column = lax.broadcasted_iota(jnp.int32, v.shape, 0) % WIDE
        ahead = jnp.where(column == WIDE - 1, 0.0, pltpu.roll(v, rows - 1, 0))
        behind = jnp.where(column == 0, 0.0, pltpu.roll(v, 1, 0))
        d[pl.ds(at, rows), 0:128] = ahead.astype(BF16)
        d[pl.ds(at, rows), 128:256] = v.astype(BF16)
        d[pl.ds(at, rows), 256:384] = behind.astype(BF16)

    def body(j, carry):
        rows = pair_rows(j)
        v = dn[rows, :] * tab[0:1, :] - tab[2:3, :] - zc[rows, :].astype(F32) * tab[1:2, :]
        spread_columns(v, pl.multiple_of(j * 2 * WIDE + WIDE, WIDE))
        return carry

    lax.fori_loop(0, n_own // (2 * WIDE), body, 0, unroll=3)
    near = n_own if edge == WIDE else pl.multiple_of(n_own + r * WIDE, WIDE)
    near = zc[pl.ds(near, WIDE), :].astype(F32)
    spread_columns(dedge[0:WIDE, :] * tab[0:1, :] - tab[3:4, :] - near * tab[1:2, :], halo_at)
    d_out[...] = d[WIDE : WIDE + n_own, :]
    load.wait()
    rhs = jnp.concatenate([w[:, i * CHANS : (i + 1) * CHANS] for i in range(9)], axis=0)
    block = n_own // 2
    for j in range(2):
        at = j * block
        lhs = jnp.concatenate([d[at + (2 - i) * WIDE : at + (2 - i) * WIDE + block, :] for i in range(3)], axis=1)
        y[at : at + block, :] = jnp.dot(lhs, rhs, preferred_element_type=F32)

    def share(j, carry):
        rows = pair_rows(j)
        for k in range(GROUPS):
            outs[k][rows, :] = y[rows, pl.ds(lane_of(t ^ k), LANES)].astype(BF16)
        return carry

    lax.fori_loop(0, n_own // (2 * WIDE), share, 0, unroll=3)


def bwd_step(layer, total, pos, dn, dedge, sums, zc, st, gs, weights, ties):
    n_own = dn.shape[0]
    part = pltpu.VMEM((n_own, LANES), BF16)
    return pl.pallas_call(
        functools.partial(bwd_kernel, layer, total),
        out_shape=(
            part,
            part,
            part,
            part,
            pltpu.VMEM((n_own, 3 * LANES), BF16),
        ),
        in_specs=[SMEM] + [VMEM] * 6 + [ANY] + [FREE] * len(ties),
        out_specs=(VMEM,) * 5,
        scratch_shapes=[
            pltpu.VMEM((n_own + 2 * WIDE, 3 * LANES), BF16),
            pltpu.VMEM((LANES, 9 * CHANS), BF16),
            pltpu.VMEM((n_own, CHANS), F32),
            pltpu.VMEM((8, LANES), F32),
            pltpu.SemaphoreType.DMA,
        ],
        compiler_params=PARAMS,
        cost_estimate=LITTLE,
        name="conv_backward",
    )(pos, dn, dedge, sums, zc, st, gs, in_hbm(weights), *ties)


def last_kernel(t0, t1, t2, t3, *refs):
    out = refs[-1]

    def body(j, carry):
        rows = pair_rows(j)
        out[rows, :] = functools.reduce(jnp.add, [term[rows, :].astype(F32) for term in (t0, t1, t2, t3)])
        return carry

    lax.fori_loop(0, out.shape[0] // (2 * WIDE), body, 0)


def last_step(terms, ties):
    return pl.pallas_call(
        last_kernel,
        out_shape=jax.ShapeDtypeStruct(terms[0].shape, F32),
        in_specs=[VMEM] * 4 + [FREE] * len(ties),
        out_specs=VMEM,
        compiler_params=PARAMS,
        cost_estimate=LITTLE,
        name="add_terms",
    )(*terms, *ties)


def halves_kernel(keep, got, out):
    out[...] = (keep[...].astype(F32) + got[...].astype(F32)).astype(BF16)


def add_halves(keep, got):
    return pl.pallas_call(
        halves_kernel,
        out_shape=jax.ShapeDtypeStruct(keep.shape, BF16),
        in_specs=[VMEM] * 2,
        out_specs=VMEM,
        compiler_params=PARAMS,
        cost_estimate=LITTLE,
        name="add_halves",
    )(keep, got)


def wgrad_kernel(layer, pos, d, hb_hbm, *refs):
    keep, send, hb, grad, sem = refs[-5:]
    load = pltpu.make_async_copy(hb_hbm.at[layer], hb, sem)
    load.start()
    n_own = d.shape[0]
    lhs = d[...]
    load.wait()
    for i in range(3):
        part = lax.dot_general(
            lhs, hb[i * WIDE : i * WIDE + n_own, :], (((0,), (0,)), ((), ())), preferred_element_type=F32
        ).astype(BF16)
        for s in range(3):
            grad[:, (3 * i + s) * CHANS : (3 * i + s + 1) * CHANS] = part[s * LANES : (s + 1) * LANES]
    half = LANES // 2
    keep[...] = grad[pl.ds(pl.multiple_of(pos[1] * half, half), half), :]
    send[...] = grad[pl.ds(pl.multiple_of((1 - pos[1]) * half, half), half), :]


def wgrad_step(layer, pos, d, kept, ties):
    half = pltpu.VMEM((LANES // 2, 9 * CHANS), BF16)
    return pl.pallas_call(
        functools.partial(wgrad_kernel, layer),
        out_shape=(half, half),
        in_specs=[SMEM, VMEM, ANY] + [FREE] * len(ties),
        out_specs=(VMEM, VMEM),
        scratch_shapes=[
            pltpu.VMEM(kept.shape[1:], BF16),
            pltpu.VMEM((LANES, 9 * CHANS), BF16),
            pltpu.SemaphoreType.DMA,
        ],
        compiler_params=PARAMS,
        cost_estimate=LITTLE,
        name="kernel_gradient",
    )(pos, d, in_hbm(kept), *ties)


def place_kernel(layers, fresh, pos, *refs):
    count = 2 * len(layers)
    sources = refs[:count]
    out, held, wide, sem = refs[-4:]
    half = LANES // 2
    r = pos[1]
    loads = [pltpu.make_async_copy(sources[j], held.at[j], sem.at[j]) for j in range(count)]
    for load in loads:
        load.start()
    stores = []
    for j in range(count):
        at = pl.multiple_of((r if j % 2 == 0 else 1 - r) * half, half)
        if j >= 2:
            stores[j - 2].wait()
        loads[j].wait()
        wide[j % 2] = held[j].astype(F32)
        store = pltpu.make_async_copy(wide.at[j % 2], out.at[layers[j // 2], pl.ds(at, half)], sem.at[count + j])
        store.start()
        stores.append(store)
    for store in stores[-2:]:
        store.wait()


def place_step(layers, pos, sources, whole, count):
    half = LANES // 2
    jobs = len(sources)
    return pl.pallas_call(
        functools.partial(place_kernel, layers, whole is None),
        out_shape=pltpu.HBM((count, LANES, 9 * CHANS), F32),
        in_specs=[SMEM] + [ANY] * jobs + ([] if whole is None else [ANY]),
        out_specs=ANY,
        input_output_aliases={} if whole is None else {1 + jobs: 0},
        scratch_shapes=[
            pltpu.VMEM((jobs, half, 9 * CHANS), BF16),
            pltpu.VMEM((2, half, 9 * CHANS), F32),
            pltpu.SemaphoreType.DMA((2 * jobs,)),
        ],
        compiler_params=PARAMS,
        cost_estimate=LITTLE,
        name="place_gradients",
    )(pos, *[in_hbm(v) for v in sources], *(() if whole is None else (in_hbm(whole),)))


def swap_with(value, axis, k):
    return lax.ppermute(value, axis, [(i, i ^ k) for i in range(lax.axis_size(axis))])


def spread(own):
    return (own, *[swap_with(own, "tensor", k) for k in range(1, GROUPS)])


def halo_of_input(x, half):
    n_own = x.shape[0]
    edge = jnp.where(half == 0, x[n_own - WIDE :], x[:WIDE])
    return jnp.concatenate([x, swap_with(edge, "rows", 1)], axis=0)


def fast_local(section_input, conv_weights, norm_gains, norm_shifts, out_grad, out_mask):
    images, rows_here, width = out_mask.shape
    layers = conv_weights.shape[0]
    n_own = rows_here * width
    parts = lax.axis_size("dp") * lax.axis_size("rows")
    total = float(n_own * parts)
    t, half = lax.axis_index("tensor"), lax.axis_index("rows")
    image = lax.axis_index("dp")
    pos = jnp.stack([t, half, 2 * image + half, 2 * image + 1 - half]).astype(jnp.int32)
    middle = layers // 2
    x = to_maps(section_input, width).reshape(n_own, LANES)
    slots = lax.all_gather(halo_of_input(x, half), "tensor", axis=1, tiled=True)
    pad = jnp.zeros((8 - layers, LANES), F32)
    tables = spread(jnp.concatenate([norm_gains, pad, norm_shifts, pad], axis=0))
    top_grad = (to_maps(out_grad, width) * out_mask[..., None].astype(BF16)).reshape(n_own, LANES)

    st, kept = None, None
    halves = ("dp", "rows")
    kept_z, kept_st = [], []
    for layer in range(layers):
        last = layer + 1 == layers
        edge = 2 * WIDE if layer + 1 == middle else WIDE
        everyone = halves if last else (*halves, "tensor")
        devices = parts if last else parts * GROUPS
        kept, zc, rim, local = fwd_step(
            layer,
            layer == middle,
            edge,
            total,
            pos,
            slots,
            st,
            tables,
            conv_weights,
            kept,
            n_own,
            devices,
            (top_grad,) if layer == 2 else (),
        )
        rim = swap_with(rim, "rows", 1)
        st = lax.all_to_all(local, everyone, split_axis=0, concat_axis=0, tiled=True)
        st = st.reshape(parts, devices // parts, 2, LANES)
        zc = lax.dynamic_update_slice_in_dim(zc, rim, n_own, axis=0)
        kept_z.append(zc)
        kept_st.append(st)
        if not last:
            slots = lax.all_gather(zc, "tensor", axis=1, tiled=True)
    top = layers - 1
    h_last, dn, msg = below_step(top, False, total, pos, kept_z[top], kept_st[top], tables[0], (top_grad,))

    def with_other(values):
        return [v for mine in values for v in (mine, swap_with(mine, "rows", 1))]

    sum_list, pairs = [None] * layers, [None] * layers
    ahead, back = [[0, 1, 3, 2]], [[2, 3, 1, 0]]
    urgent = ()
    for layer in range(layers - 1, -1, -1):
        got = swap_with(msg, "rows", 1)
        sums = msg[WIDE:] + got[WIDE:]
        one, two, three = (swap_with(sums, "dp", k) for k in (1, 2, 3))
        sums = (sums + one) + (two + three)
        sum_list[layer] = sums
        *terms, d = bwd_step(
            layer, total, pos, dn, got, sums, kept_z[layer], kept_st[layer], tables[0], conv_weights, urgent
        )
        terms = (terms[0], *[swap_with(terms[k], "tensor", k) for k in range(1, GROUPS)])
        keep, send = wgrad_step(layer, pos, d, kept, ())
        other = swap_with(send, "rows", 1)
        pairs[layer] = add_halves(keep, other)
        urgent, settled = (other,), (() if layer + 1 == layers else (pairs[layer + 1],))
        if layer == 4:
            upper = lax.psum((pairs[5], pairs[4]), "dp", axis_index_groups=ahead)
        if layer == 2:
            mid = lax.psum((pairs[3], pairs[2]), "dp", axis_index_groups=back)
        if layer > 0:
            below = layer - 1
            late = (in_hbm(upper[0]),) if layer == 1 else ()
            dn, msg = below_step(
                below, layer == middle, total, pos, kept_z[below], kept_st[below], tables[0], terms, (keep, *settled, *late)
            )
        else:
            grad = last_step(terms, (pairs[0], pairs[1]))
    tied, upper = lax.optimization_barrier(((pairs[1], pairs[0]), upper))
    lower = lax.psum(tied, "dp", axis_index_groups=ahead)
    shape = (images, rows_here, width, LANES)
    grad, mid = lax.optimization_barrier((grad, mid))
    outputs = (from_maps(h_last.reshape(shape)), from_maps(grad.reshape(shape)))
    whole = place_step((5, 4, 3, 2), pos, with_other((*upper, *mid)), None, layers)
    sums = jnp.stack(sum_list)
    sums = (sums[:, 1], sums[:, 0])
    lower, whole, outputs, sums = lax.optimization_barrier((lower, whole, outputs, sums))
    whole = place_step((1, 0), pos, with_other(lower), whole, layers)
    return (*outputs, whole, *sums)


def solution(mesh):
    in_specs = (
        P("dp", "rows", "tensor"),
        P(None, "tensor", None),
        P(None, "tensor"),
        P(None, "tensor"),
        P("dp", "rows", "tensor"),
        P("dp", "rows", None),
    )
    out_specs = (
        P("dp", "rows", "tensor"),
        P("dp", "rows", "tensor"),
        P(None, "tensor", None),
        P(None, "tensor"),
        P(None, "tensor"),
    )
    local = fast_local if fits_kernels(mesh) else generic_local
    return jax.shard_map(local, mesh=mesh, in_specs=in_specs, out_specs=out_specs, check_vma=False)
```

```python
import functools

import jax
import jax.numpy as jnp
from jax import lax
from jax.experimental import pallas as pl
from jax.experimental.pallas import tpu as pltpu
from jax.sharding import PartitionSpec as P

EPS = 1e-05


def padded_2(cells, sides, width):
    for axis, dim in sides:
        count = lax.axis_size(axis)
        ends = count - 1
        head = lax.slice_in_dim(cells, 0, width, axis=dim)
        tail = lax.slice_in_dim(cells, cells.shape[dim] - width, cells.shape[dim], axis=dim)
        cells = jnp.concatenate(
            [
                lax.ppermute(tail, axis, [(i, (i + 1) % count) for i in range(ends)]),
                cells,
                lax.ppermute(head, axis, [((i + 1) % count, i) for i in range(ends)]),
            ],
            axis=dim,
        )
    return cells


def to_maps(flat, width):
    count, high, merged = flat.shape
    return flat.reshape(count, high, merged // width, width).transpose(0, 1, 3, 2)


def from_maps(maps):
    count, high, wide, chans = maps.shape
    return maps.transpose(0, 1, 3, 2).reshape(count, high, chans * wide)


def spatial_conv(padded, kernel):
    return lax.conv_general_dilated(
        padded,
        kernel,
        (1, 1),
        ((0, 0), (1, 1)),
        dimension_numbers=("NHWC", "HWIO", "NHWC"),
        preferred_element_type=jnp.float32,
    )


def flipped(kernel):
    return jnp.transpose(kernel[::-1, ::-1], (0, 1, 3, 2))


def pool_unpool(values):
    count, high, wide, chans = values.shape
    blocks = values.reshape(count, high // 2, 2, wide // 2, 2, chans)
    pooled = jax.nn.logsumexp(blocks, axis=(2, 4), keepdims=True)
    return (jnp.exp(blocks - pooled) * pooled).reshape(values.shape)


def moments(conv_out, total_pixels):
    summed = lax.psum(jnp.sum(conv_out, axis=(0, 1, 2)), ("dp", "rows"))
    mean = summed / total_pixels
    spread = lax.psum(jnp.sum(jnp.square(conv_out - mean), axis=(0, 1, 2)), ("dp", "rows"))
    var = spread / total_pixels
    return (mean, lax.rsqrt(var + EPS))


def kernel_grad(whole, dconv):
    images, rows_here, width, chans = dconv.shape
    widened = jnp.pad(whole, ((0, 0), (0, 0), (1, 1), (0, 0)))
    stacked = []
    for row_off in range(3):
        line = []
        for col_off in range(3):
            window = widened[:, row_off : row_off + rows_here, col_off : col_off + width, :]
            line.append(
                jnp.einsum("bhwc,bhwo->co", window, dconv, preferred_element_type=jnp.float32)
            )
        stacked.append(jnp.stack(line))
    return jnp.stack(stacked)


def generic_local(section_input, conv_weights, norm_gains, norm_shifts, out_grad, out_mask):
    width = out_mask.shape[2]
    images, rows_here = (out_mask.shape[0], out_mask.shape[1])
    total_pixels = float(images * rows_here * width * lax.axis_size("dp") * lax.axis_size("rows"))
    layers, out_here, flat_in = conv_weights.shape
    chans_in = flat_in // 9
    kernels_hwio = conv_weights.reshape(layers, out_here, 3, 3, chans_in).transpose(0, 2, 3, 4, 1)
    middle = layers // 2
    kept = []
    acting = to_maps(section_input, width)
    current = acting.astype(jnp.float32)
    pre_pool = current
    for index in range(layers):
        if index == middle:
            pre_pool = current
            acting = pool_unpool(pre_pool).astype(jnp.bfloat16)
        padded = padded_2(acting, (("rows", 1),), 1)
        whole = lax.all_gather(padded, "tensor", axis=3, tiled=True)
        conv_out = spatial_conv(whole, kernels_hwio[index])
        mean, rstd = moments(conv_out, total_pixels)
        normed = (conv_out - mean) * rstd
        shifted = normed * norm_gains[index] + norm_shifts[index]
        current = jax.nn.silu(shifted)
        acting = current.astype(jnp.bfloat16)
        kept.append((whole, normed, shifted, rstd))
    grad = to_maps(out_grad, width).astype(jnp.float32) * out_mask[..., None].astype(jnp.float32)
    kernel_list = [None] * layers
    gain_list = [None] * layers
    shift_list = [None] * layers
    for index in range(layers - 1, -1, -1):
        whole, normed, shifted, rstd = kept[index]
        unused, pull_silu = jax.vjp(jax.nn.silu, shifted)
        dshift = pull_silu(grad)[0]
        gain_sum, shift_sum = lax.psum(
            (jnp.sum(dshift * normed, axis=(0, 1, 2)), jnp.sum(dshift, axis=(0, 1, 2))),
            ("dp", "rows"),
        )
        gain_list[index] = gain_sum
        shift_list[index] = shift_sum
        dconv = (
            norm_gains[index]
            * rstd
            * (dshift - shift_sum / total_pixels - normed * gain_sum / total_pixels)
        ).astype(jnp.bfloat16)
        summed_kernel = lax.psum(
            kernel_grad(whole, dconv).astype(jnp.bfloat16), ("dp", "rows")
        ).astype(jnp.float32)
        kernel_list[index] = summed_kernel.transpose(3, 0, 1, 2).reshape(out_here, flat_in)
        grad_rim = padded_2(dconv, (("rows", 1),), 1)
        partial_terms = spatial_conv(grad_rim, flipped(kernels_hwio[index]))
        grad_in = lax.psum_scatter(
            partial_terms.astype(jnp.bfloat16), "tensor", scatter_dimension=3, tiled=True
        ).astype(jnp.float32)
        if index == middle:
            unused, pull_pool = jax.vjp(pool_unpool, pre_pool)
            grad = pull_pool(grad_in)[0]
        else:
            grad = grad_in
    return (
        from_maps(acting),
        from_maps(grad),
        jnp.stack(kernel_list),
        jnp.stack(gain_list),
        jnp.stack(shift_list),
    )


GROUPS = 4
LANES = 128
WIDE = 48
CHANS = GROUPS * LANES
F32 = jnp.float32
BF16 = jnp.bfloat16
VMEM = pl.BlockSpec(memory_space=pltpu.VMEM)
SMEM = pl.BlockSpec(memory_space=pltpu.SMEM)
ANY = pl.BlockSpec(memory_space=pltpu.HBM)
FREE = pl.BlockSpec(memory_space=pl.ANY)
LITTLE = pl.CostEstimate(flops=1024, bytes_accessed=1024, transcendentals=0)
PARAMS = pltpu.CompilerParams(vmem_limit_bytes=20 * 1024 * 1024)


def in_hbm(value):
    return pltpu.with_memory_space_constraint(value, pltpu.HBM)


def fits_kernels(mesh):
    return mesh.shape["tensor"] == GROUPS and mesh.shape["rows"] == 2 and mesh.shape["dp"] == 4


def sigmoid(v):
    return 0.5 * jnp.tanh(0.5 * v) + 0.5


def swap_columns(v):
    column = lax.broadcasted_iota(jnp.int32, v.shape, 0)
    return jnp.where(column % 2 == 0, pltpu.roll(v, WIDE - 1, 0), pltpu.roll(v, 1, 0))


def soft_parts(h):
    top = jnp.maximum(h[0], h[1])
    top = jnp.maximum(top, swap_columns(top))
    e0, e1 = jnp.exp(h[0] - top), jnp.exp(h[1] - top)
    total = e0 + e1
    total = total + swap_columns(total)
    pooled = top + jnp.log(total)
    inverse = 1.0 / total
    return e0 * inverse, e1 * inverse, pooled


def soft(h):
    h = h.reshape(2, WIDE, LANES)
    q0, q1, pooled = soft_parts(h)
    return jnp.concatenate([q0 * pooled, q1 * pooled], axis=0)


def soft_pull(h, grad):
    h = h.reshape(2, WIDE, LANES)
    grad = grad.reshape(2, WIDE, LANES)
    q0, q1, pooled = soft_parts(h)
    mix = q0 * grad[0] + q1 * grad[1]
    mix = mix + swap_columns(mix)
    return jnp.concatenate(
        [q0 * (pooled * (grad[0] - mix) + mix), q1 * (pooled * (grad[1] - mix) + mix)], axis=0
    )


def norm_tables(st, group, i_own, i_oth, n_local, total):
    parts = st.shape[0]
    if parts == 2:
        mean, rstd = st[0, 0, 0:1], lax.rsqrt(st[0, 0, 1:2] / total + EPS)
        return rstd, (st[1, 0, 0:1] - mean) * rstd, (st[1, 0, 1:2] - mean) * rstd
    group = 0 if st.shape[1] == 1 else group
    blocks = [st[i, group] for i in range(parts)]
    summed = functools.reduce(jnp.add, blocks)
    mean = summed[0:1] / parts
    apart = functools.reduce(jnp.add, [jnp.square(b - mean) for b in blocks])
    rstd = lax.rsqrt((summed[1:2] + n_local * apart[0:1]) / total + EPS)
    return rstd, (st[i_own, group, 0:1] - mean) * rstd, (st[i_oth, group, 0:1] - mean) * rstd


def left_right(y0, y1, y2):
    rows = y0.shape[0]
    column = lax.broadcasted_iota(jnp.int32, y0.shape, 0) % WIDE
    before = jnp.where(column == 0, 0.0, pltpu.roll(y0, 1, 0))
    after = jnp.where(column == WIDE - 1, 0.0, pltpu.roll(y2, rows - 1, 0))
    return before + y1 + after


def lane_of(group):
    return pl.multiple_of(group * LANES, LANES)


def edge_start(n_own, edge, half):
    return pl.multiple_of((1 - half) * (n_own - edge), WIDE)


def pair_rows(j):
    return pl.ds(pl.multiple_of(j * 2 * WIDE, 2 * WIDE), 2 * WIDE)


def fold(v):
    return jnp.sum(v.reshape(v.shape[0] // 8, 8, LANES), axis=0)


def fwd_kernel(first, pool, layer, total, edge_out, *refs):
    pos, zall = refs[0], refs[1]
    if first:
        w_hbm = refs[2]
    else:
        st, gss, w_hbm = refs[2], refs[3:7], refs[7]
    hb_out, zc_out, edge_ref, st_out, hb, w, y, z, tab, hs, sem = refs[-11:]
    load = pltpu.make_async_copy(w_hbm.at[layer], w, sem.at[0])
    load.start()
    save = pltpu.make_async_copy(hb, hb_out.at[layer], sem.at[1])
    t, r = pos[0], pos[1]
    n_own = z.shape[0]
    halo_at = pl.multiple_of((1 - r) * (n_own + WIDE), WIDE)
    zero_at = pl.multiple_of(r * (n_own + WIDE), WIDE)
    hb[pl.ds(zero_at, WIDE), :] = jnp.zeros((WIDE, CHANS), BF16)
    edge = zall.shape[0] - n_own
    if not first:
        for k in range(GROUPS):
            group = t ^ k
            rstd, own, oth = norm_tables(st, group, pos[2], pos[3], float(n_own), total)
            gain, shift = gss[k][layer - 1 : layer, :], gss[k][layer + 7 : layer + 8, :]
            tab[group, 0:1] = rstd * gain
            tab[group, 1:2] = own * gain + shift
            tab[group, 2:3] = oth * gain + shift

    def act(values, group, which):
        if first:
            return values
        n = values.astype(F32) * tab[group, 0:1, :] + tab[group, which : which + 1, :]
        h = n * sigmoid(n)
        return soft(h) if pool else h

    for group in range(GROUPS):
        lanes = slice(group * LANES, (group + 1) * LANES)
        h = act(zall[n_own : n_own + edge, lanes], group, 2)
        if edge > WIDE:
            hs[...] = h
            h = hs[pl.ds(pl.multiple_of(r * WIDE, WIDE), WIDE), :]
        hb[pl.ds(halo_at, WIDE), lanes] = h.astype(BF16)
    pair, block = 2 * WIDE, n_own // 3
    steps, made = n_own // pair, 0
    summed = jnp.zeros((8, LANES), F32)
    for part in range(3):
        first_row = part * block
        while made < min(steps, (first_row + block + WIDE + pair - 1) // pair):
            at = made * pair
            for group in range(GROUPS):
                lanes = slice(group * LANES, (group + 1) * LANES)
                h = act(zall[at : at + pair, lanes], group, 1)
                hb[at + WIDE : at + WIDE + pair, lanes] = h.astype(BF16)
            made += 1
        if part == 0:
            load.wait()
            rhs = jnp.concatenate(
                [
                    jnp.concatenate([w[:, (3 * i + s) * CHANS : (3 * i + s + 1) * CHANS] for i in range(3)], axis=1)
                    for s in range(3)
                ],
                axis=0,
            )
        if part == 2:
            save.start()
        lhs = jnp.concatenate([hb[first_row + i * WIDE : first_row + i * WIDE + block, :] for i in range(3)], axis=1)
        rows = slice(first_row, first_row + block)
        y[rows, :] = lax.dot_general(lhs, rhs, (((1,), (1,)), ((), ())), preferred_element_type=F32)
        for j in range(block // pair):
            rows = slice(first_row + j * pair, first_row + (j + 1) * pair)
            v = left_right(y[rows, 0:128], y[rows, 128:256], y[rows, 256:384])
            z[rows, :] = v
            summed = summed + fold(v)
    mean = jnp.sum(summed, axis=0, keepdims=True) / n_own
    apart = jnp.zeros((8, LANES), F32)
    for j in range(steps):
        rows = slice(j * pair, (j + 1) * pair)
        v = z[rows, :] - mean
        zc_out[rows, :] = v.astype(BF16)
        apart = apart + fold(jnp.square(v))
    sums = jnp.concatenate([mean, jnp.sum(apart, axis=0, keepdims=True)], axis=0)
    for i in range(st_out.shape[0]):
        st_out[i] = sums
    edge_ref[...] = zc_out[pl.ds(edge_start(n_own, edge_out, r), edge_out), :]
    zc_out[n_own : n_own + edge_out, :] = jnp.zeros((edge_out, LANES), BF16)
    save.wait()


def fwd_step(layer, pool, edge_out, total, pos, slots, st, tables, weights, kept, n_own, devices, ties):
    first = st is None
    layers = weights.shape[0]
    extra = () if first else (st, *tables)
    return pl.pallas_call(
        functools.partial(fwd_kernel, first, pool, layer, total, edge_out),
        out_shape=(
            pltpu.HBM((layers, n_own + 2 * WIDE, CHANS), BF16),
            pltpu.VMEM((n_own + edge_out, LANES), BF16),
            pltpu.VMEM((edge_out, LANES), BF16),
            pltpu.VMEM((devices, 2, LANES), F32),
        ),
        in_specs=[SMEM] + [VMEM] * (1 + len(extra)) + [ANY] * (1 if first else 2) + [FREE] * len(ties),
        out_specs=(ANY, VMEM, VMEM, VMEM),
        input_output_aliases={} if first else {3 + len(extra): 0},
        scratch_shapes=[
            pltpu.VMEM((n_own + 2 * WIDE, CHANS), BF16),
            pltpu.VMEM((LANES, 9 * CHANS), BF16),
            pltpu.VMEM((n_own, 3 * LANES), F32),
            pltpu.VMEM((n_own, LANES), F32),
            pltpu.VMEM((GROUPS, 8, LANES), F32),
            pltpu.VMEM((2 * WIDE, LANES), F32),
            pltpu.SemaphoreType.DMA((2,)),
        ],
        compiler_params=PARAMS,
        cost_estimate=pl.CostEstimate(
            flops=2 * n_own * 9 * CHANS * LANES, bytes_accessed=4 * 1024 * 1024, transcendentals=n_own * CHANS
        ),
        name="conv_forward",
    )(pos, slots, *extra, in_hbm(weights), *(() if first else (in_hbm(kept),)), *ties)


def below_kernel(layer, pool, total, top, *refs):
    pos, zc, st, gs = refs[:4]
    if top:
        terms, h_out, dn_out, msg, tab = refs[4:]
    else:
        terms, (dn_out, msg, tab) = refs[4:8], refs[-3:]
    n_own = dn_out.shape[0]
    rstd, own, oth = norm_tables(st, pos[0], pos[2], pos[3], float(n_own), total)
    tab[0:1], tab[1:2] = rstd, own
    tab[2:3], tab[3:4] = gs[layer : layer + 1, :], gs[layer + 8 : layer + 9, :]

    def body(j, accs):
        rows = pair_rows(j)
        xhat = zc[rows, :].astype(F32) * tab[0:1, :] + tab[1:2, :]
        n = xhat * tab[2:3, :] + tab[3:4, :]
        sig = sigmoid(n)
        h = n * sig
        if top:
            g = terms[rows, :].astype(F32)
            h_out[rows, :] = h.astype(BF16)
        else:
            g = functools.reduce(jnp.add, [term[rows, :].astype(F32) for term in terms])
        if pool:
            g = soft_pull(h, g)
        dn = g * (sig * (1.0 + n - h))
        dn_out[rows, :] = dn
        return accs[0] + fold(dn), accs[1] + fold(dn * xhat)

    zero = jnp.zeros((8, LANES), F32)
    sums = lax.fori_loop(0, n_own // (2 * WIDE), body, (zero, zero), unroll=3)
    sums = [jnp.sum(v, axis=0, keepdims=True) for v in sums]
    msg[0:WIDE, :] = dn_out[pl.ds(edge_start(n_own, WIDE, pos[1]), WIDE), :]
    msg[WIDE : WIDE + 8, :] = jnp.concatenate(sums + [jnp.zeros((6, LANES), F32)], axis=0)


def below_step(layer, pool, total, pos, zc, st, gs, terms, ties=()):
    n_own = terms[0].shape[0]
    top = len(terms) == 1
    out_shape = [
        pltpu.VMEM((n_own, LANES), F32),
        pltpu.VMEM((WIDE + 8, LANES), F32),
    ]
    if top:
        out_shape = [jax.ShapeDtypeStruct((n_own, LANES), BF16)] + out_shape
    return pl.pallas_call(
        functools.partial(below_kernel, layer, pool, total, top),
        out_shape=tuple(out_shape),
        in_specs=[SMEM] + [VMEM] * (3 + len(terms)) + [FREE] * len(ties),
        out_specs=(VMEM,) * len(out_shape),
        scratch_shapes=[pltpu.VMEM((8, LANES), F32)],
        compiler_params=PARAMS,
        cost_estimate=LITTLE,
        name="silu_backward",
    )(pos, zc, st, gs, *terms, *ties)


def bwd_kernel(layer, total, *refs):
    pos, dn, dedge, sums, zc, st, gs, w_hbm = refs[:8]
    outs, d_out, d, w, y, tab, sem = refs[-10:-6], *refs[-6:]
    load = pltpu.make_async_copy(w_hbm.at[layer], w, sem)
    load.start()
    t, r = pos[0], pos[1]
    n_own = dn.shape[0]
    halo_at = pl.multiple_of((1 - r) * (n_own + WIDE), WIDE)
    zero_at = pl.multiple_of(r * (n_own + WIDE), WIDE)
    edge = zc.shape[0] - n_own
    d[pl.ds(zero_at, WIDE), :] = jnp.zeros((WIDE, 3 * LANES), BF16)
    rstd, own, oth = norm_tables(st, t, pos[2], pos[3], float(n_own), total)
    scale = gs[layer : layer + 1, :] * rstd
    shift_sum, gain_sum = sums[0:1, :], sums[1:2, :]
    slope = scale * gain_sum / total
    tab[0:1] = scale
    tab[1:2] = slope * rstd
    tab[2:3] = scale * shift_sum / total + slope * own
    tab[3:4] = scale * shift_sum / total + slope * oth

    def spread_columns(v):
        rows = v.shape[0]
        column = lax.broadcasted_iota(jnp.int32, v.shape, 0) % WIDE
        ahead = jnp.where(column == WIDE - 1, 0.0, pltpu.roll(v, rows - 1, 0))
        behind = jnp.where(column == 0, 0.0, pltpu.roll(v, 1, 0))
        return jnp.concatenate([ahead.astype(BF16), v.astype(BF16), behind.astype(BF16)], axis=1)

    near = n_own if edge == WIDE else pl.multiple_of(n_own + r * WIDE, WIDE)
    near = zc[pl.ds(near, WIDE), :].astype(F32)
    d[pl.ds(halo_at, WIDE), :] = spread_columns(dedge[0:WIDE, :] * tab[0:1, :] - tab[3:4, :] - near * tab[1:2, :])
    pair, block = 2 * WIDE, n_own // 3
    steps, made = n_own // pair, 0
    for part in range(3):
        first_row = part * block
        while made < min(steps, (first_row + block + WIDE + pair - 1) // pair):
            at = made * pair
            v = dn[at : at + pair, :] * tab[0:1, :] - tab[2:3, :] - zc[at : at + pair, :].astype(F32) * tab[1:2, :]
            v = spread_columns(v)
            d[at + WIDE : at + WIDE + pair, :] = v
            d_out[at : at + pair, :] = v
            made += 1
        if part == 0:
            load.wait()
            rhs = jnp.concatenate([w[:, i * CHANS : (i + 1) * CHANS] for i in range(9)], axis=0)
        windows = [first_row + (2 - i) * WIDE for i in range(3)]
        lhs = jnp.concatenate([d[at : at + block, :] for at in windows], axis=1)
        y[first_row : first_row + block, :] = jnp.dot(lhs, rhs, preferred_element_type=F32)
        for j in range(block // pair):
            rows = slice(first_row + j * pair, first_row + (j + 1) * pair)
            for k in range(GROUPS):
                outs[k][rows, :] = y[rows, pl.ds(lane_of(t ^ k), LANES)].astype(BF16)


def bwd_step(layer, total, pos, dn, dedge, sums, zc, st, gs, weights, ties):
    n_own = dn.shape[0]
    part = pltpu.VMEM((n_own, LANES), BF16)
    return pl.pallas_call(
        functools.partial(bwd_kernel, layer, total),
        out_shape=(
            part,
            part,
            part,
            part,
            pltpu.VMEM((n_own, 3 * LANES), BF16),
        ),
        in_specs=[SMEM] + [VMEM] * 6 + [ANY] + [FREE] * len(ties),
        out_specs=(VMEM,) * 5,
        scratch_shapes=[
            pltpu.VMEM((n_own + 2 * WIDE, 3 * LANES), BF16),
            pltpu.VMEM((LANES, 9 * CHANS), BF16),
            pltpu.VMEM((n_own, CHANS), F32),
            pltpu.VMEM((8, LANES), F32),
            pltpu.SemaphoreType.DMA,
        ],
        compiler_params=PARAMS,
        cost_estimate=LITTLE,
        name="conv_backward",
    )(pos, dn, dedge, sums, zc, st, gs, in_hbm(weights), *ties)


def last_kernel(t0, t1, t2, t3, *refs):
    out = refs[-1]

    def body(j, carry):
        rows = pair_rows(j)
        out[rows, :] = functools.reduce(jnp.add, [term[rows, :].astype(F32) for term in (t0, t1, t2, t3)])
        return carry

    lax.fori_loop(0, out.shape[0] // (2 * WIDE), body, 0)


def last_step(terms, ties):
    return pl.pallas_call(
        last_kernel,
        out_shape=jax.ShapeDtypeStruct(terms[0].shape, F32),
        in_specs=[VMEM] * 4 + [FREE] * len(ties),
        out_specs=VMEM,
        compiler_params=PARAMS,
        cost_estimate=LITTLE,
        name="add_terms",
    )(*terms, *ties)


def halves_kernel(keep, got, out):
    out[...] = (keep[...].astype(F32) + got[...].astype(F32)).astype(BF16)


def add_halves(keep, got):
    return pl.pallas_call(
        halves_kernel,
        out_shape=jax.ShapeDtypeStruct(keep.shape, BF16),
        in_specs=[VMEM] * 2,
        out_specs=VMEM,
        compiler_params=PARAMS,
        cost_estimate=LITTLE,
        name="add_halves",
    )(keep, got)


def wgrad_kernel(layer, pos, d, hb_hbm, *refs):
    keep, send, hb, grad, sem = refs[-5:]
    load = pltpu.make_async_copy(hb_hbm.at[layer], hb, sem)
    load.start()
    n_own = d.shape[0]
    lhs = d[...]
    load.wait()
    for i in range(3):
        part = lax.dot_general(
            lhs, hb[i * WIDE : i * WIDE + n_own, :], (((0,), (0,)), ((), ())), preferred_element_type=F32
        ).astype(BF16)
        for s in range(3):
            grad[:, (3 * i + s) * CHANS : (3 * i + s + 1) * CHANS] = part[s * LANES : (s + 1) * LANES]
    half = LANES // 2
    keep[...] = grad[pl.ds(pl.multiple_of(pos[1] * half, half), half), :]
    send[...] = grad[pl.ds(pl.multiple_of((1 - pos[1]) * half, half), half), :]


def wgrad_step(layer, pos, d, kept, ties):
    half = pltpu.VMEM((LANES // 2, 9 * CHANS), BF16)
    return pl.pallas_call(
        functools.partial(wgrad_kernel, layer),
        out_shape=(half, half),
        in_specs=[SMEM, VMEM, ANY] + [FREE] * len(ties),
        out_specs=(VMEM, VMEM),
        scratch_shapes=[
            pltpu.VMEM(kept.shape[1:], BF16),
            pltpu.VMEM((LANES, 9 * CHANS), BF16),
            pltpu.SemaphoreType.DMA,
        ],
        compiler_params=PARAMS,
        cost_estimate=LITTLE,
        name="kernel_gradient",
    )(pos, d, in_hbm(kept), *ties)


def place_kernel(layers, fresh, pos, *refs):
    count = 2 * len(layers)
    sources = refs[:count]
    out, held, wide, sem = refs[-4:]
    half = LANES // 2
    r = pos[1]
    loads = [pltpu.make_async_copy(sources[j], held.at[j], sem.at[j]) for j in range(count)]
    for load in loads:
        load.start()
    stores = []
    for j in range(count):
        at = pl.multiple_of((r if j % 2 == 0 else 1 - r) * half, half)
        if j >= 2:
            stores[j - 2].wait()
        loads[j].wait()
        wide[j % 2] = held[j].astype(F32)
        store = pltpu.make_async_copy(wide.at[j % 2], out.at[layers[j // 2], pl.ds(at, half)], sem.at[count + j])
        store.start()
        stores.append(store)
    for store in stores[-2:]:
        store.wait()


def place_step(layers, pos, sources, whole, count):
    half = LANES // 2
    jobs = len(sources)
    return pl.pallas_call(
        functools.partial(place_kernel, layers, whole is None),
        out_shape=pltpu.HBM((count, LANES, 9 * CHANS), F32),
        in_specs=[SMEM] + [ANY] * jobs + ([] if whole is None else [ANY]),
        out_specs=ANY,
        input_output_aliases={} if whole is None else {1 + jobs: 0},
        scratch_shapes=[
            pltpu.VMEM((jobs, half, 9 * CHANS), BF16),
            pltpu.VMEM((2, half, 9 * CHANS), F32),
            pltpu.SemaphoreType.DMA((2 * jobs,)),
        ],
        compiler_params=PARAMS,
        cost_estimate=LITTLE,
        name="place_gradients",
    )(pos, *[in_hbm(v) for v in sources], *(() if whole is None else (in_hbm(whole),)))


def swap_with(value, axis, k):
    return lax.ppermute(value, axis, [(i, i ^ k) for i in range(lax.axis_size(axis))])


def spread(own):
    return (own, *[swap_with(own, "tensor", k) for k in range(1, GROUPS)])


def share_moments(mine, count):
    other = swap_with(mine, "rows", 1)
    mean = 0.5 * (mine[0:1] + other[0:1])
    apart = mine[1:2] + other[1:2] + (0.5 * count) * jnp.square(other[0:1] - mine[0:1])
    own = jnp.concatenate([mean, apart], axis=0)
    all_four = [own] + [swap_with(own, "dp", k) for k in (1, 2, 3)]
    mean = 0.25 * functools.reduce(jnp.add, [v[0:1] for v in all_four])
    apart = functools.reduce(jnp.add, [v[1:2] + (2.0 * count) * jnp.square(v[0:1] - mean) for v in all_four])
    return jnp.concatenate([mean, apart, mine[0:1], other[0:1]], axis=0).reshape(2, 1, 2, LANES)


def halo_of_input(x, half):
    n_own = x.shape[0]
    edge = jnp.where(half == 0, x[n_own - WIDE :], x[:WIDE])
    return jnp.concatenate([x, swap_with(edge, "rows", 1)], axis=0)


def fast_local(section_input, conv_weights, norm_gains, norm_shifts, out_grad, out_mask):
    images, rows_here, width = out_mask.shape
    layers = conv_weights.shape[0]
    n_own = rows_here * width
    parts = lax.axis_size("dp") * lax.axis_size("rows")
    total = float(n_own * parts)
    t, half = lax.axis_index("tensor"), lax.axis_index("rows")
    image = lax.axis_index("dp")
    pos = jnp.stack([t, half, 2 * image + half, 2 * image + 1 - half]).astype(jnp.int32)
    middle = layers // 2
    x = to_maps(section_input, width).reshape(n_own, LANES)
    slots = lax.all_gather(halo_of_input(x, half), "tensor", axis=1, tiled=True)
    pad = jnp.zeros((8 - layers, LANES), F32)
    tables = spread(jnp.concatenate([norm_gains, pad, norm_shifts, pad], axis=0))
    top_grad = (to_maps(out_grad, width) * out_mask[..., None].astype(BF16)).reshape(n_own, LANES)

    st, kept = None, None
    halves = ("dp", "rows")
    kept_z, kept_st = [], []
    for layer in range(layers):
        last = layer + 1 == layers
        edge = 2 * WIDE if layer + 1 == middle else WIDE
        everyone = ("dp", "rows", "tensor")
        devices = 1 if last else parts * GROUPS
        kept, zc, rim, local = fwd_step(
            layer,
            layer == middle,
            edge,
            total,
            pos,
            slots,
            st,
            tables,
            conv_weights,
            kept,
            n_own,
            devices,
            (top_grad,) if layer == 2 else (),
        )
        rim = swap_with(rim, "rows", 1)
        if last:
            st = share_moments(local[0], float(n_own))
        else:
            st = lax.all_to_all(local, everyone, split_axis=0, concat_axis=0, tiled=True)
            st = st.reshape(parts, GROUPS, 2, LANES)
        zc = lax.dynamic_update_slice_in_dim(zc, rim, n_own, axis=0)
        kept_z.append(zc)
        kept_st.append(st)
        if not last:
            slots = lax.all_gather(zc, "tensor", axis=1, tiled=True)
    top = layers - 1
    h_last, dn, msg = below_step(top, False, total, pos, kept_z[top], kept_st[top], tables[0], (top_grad,))

    def with_other(values):
        return [v for mine in values for v in (mine, swap_with(mine, "rows", 1))]

    sum_list, pairs = [None] * layers, [None] * layers
    ahead, back = [[0, 1, 3, 2]], [[2, 3, 1, 0]]
    urgent = ()
    for layer in range(layers - 1, -1, -1):
        got = swap_with(msg, "rows", 1)
        sums = msg[WIDE:] + got[WIDE:]
        one, two, three = (swap_with(sums, "dp", k) for k in (1, 2, 3))
        sums = (sums + one) + (two + three)
        sum_list[layer] = sums
        *terms, d = bwd_step(
            layer, total, pos, dn, got, sums, kept_z[layer], kept_st[layer], tables[0], conv_weights, urgent
        )
        terms = (terms[0], *[swap_with(terms[k], "tensor", k) for k in range(1, GROUPS)])
        keep, send = wgrad_step(layer, pos, d, kept, ())
        other = swap_with(send, "rows", 1)
        pairs[layer] = add_halves(keep, other)
        urgent, settled = (other,), (() if layer + 1 == layers else (pairs[layer + 1],))
        if layer == 4:
            upper = lax.psum((pairs[5], pairs[4]), "dp", axis_index_groups=ahead)
        if layer == 2:
            mid = lax.psum((pairs[3], pairs[2]), "dp", axis_index_groups=back)
        if layer > 0:
            below = layer - 1
            late = (in_hbm(upper[0]),) if layer == 1 else ()
            dn, msg = below_step(
                below, layer == middle, total, pos, kept_z[below], kept_st[below], tables[0], terms, (keep, *settled, *late)
            )
        else:
            grad = last_step(terms, (pairs[0], pairs[1]))
    tied, upper = lax.optimization_barrier(((pairs[1], pairs[0]), upper))
    lower = lax.psum(tied, "dp", axis_index_groups=ahead)
    shape = (images, rows_here, width, LANES)
    grad, mid = lax.optimization_barrier((grad, mid))
    outputs = (from_maps(h_last.reshape(shape)), from_maps(grad.reshape(shape)))
    whole = place_step((5, 4, 3, 2), pos, with_other((*upper, *mid)), None, layers)
    sums = jnp.stack(sum_list)
    sums = (sums[:, 1], sums[:, 0])
    lower, whole, outputs, sums = lax.optimization_barrier((lower, whole, outputs, sums))
    whole = place_step((1, 0), pos, with_other(lower), whole, layers)
    return (*outputs, whole, *sums)


def solution(mesh):
    in_specs = (
        P("dp", "rows", "tensor"),
        P(None, "tensor", None),
        P(None, "tensor"),
        P(None, "tensor"),
        P("dp", "rows", "tensor"),
        P("dp", "rows", None),
    )
    out_specs = (
        P("dp", "rows", "tensor"),
        P("dp", "rows", "tensor"),
        P(None, "tensor", None),
        P(None, "tensor"),
        P(None, "tensor"),
    )
    local = fast_local if fits_kernels(mesh) else generic_local
    return jax.shard_map(local, mesh=mesh, in_specs=in_specs, out_specs=out_specs, check_vma=False)
```

```python
import functools

import jax
import jax.numpy as jnp
from jax import lax
from jax.experimental import pallas as pl
from jax.experimental.pallas import tpu as pltpu
from jax.sharding import PartitionSpec as P

EPS = 1e-05


def padded_2(cells, sides, width):
    for axis, dim in sides:
        count = lax.axis_size(axis)
        ends = count - 1
        head = lax.slice_in_dim(cells, 0, width, axis=dim)
        tail = lax.slice_in_dim(cells, cells.shape[dim] - width, cells.shape[dim], axis=dim)
        cells = jnp.concatenate(
            [
                lax.ppermute(tail, axis, [(i, (i + 1) % count) for i in range(ends)]),
                cells,
                lax.ppermute(head, axis, [((i + 1) % count, i) for i in range(ends)]),
            ],
            axis=dim,
        )
    return cells


def to_maps(flat, width):
    count, high, merged = flat.shape
    return flat.reshape(count, high, merged // width, width).transpose(0, 1, 3, 2)


def from_maps(maps):
    count, high, wide, chans = maps.shape
    return maps.transpose(0, 1, 3, 2).reshape(count, high, chans * wide)


def spatial_conv(padded, kernel):
    return lax.conv_general_dilated(
        padded,
        kernel,
        (1, 1),
        ((0, 0), (1, 1)),
        dimension_numbers=("NHWC", "HWIO", "NHWC"),
        preferred_element_type=jnp.float32,
    )


def flipped(kernel):
    return jnp.transpose(kernel[::-1, ::-1], (0, 1, 3, 2))


def pool_unpool(values):
    count, high, wide, chans = values.shape
    blocks = values.reshape(count, high // 2, 2, wide // 2, 2, chans)
    pooled = jax.nn.logsumexp(blocks, axis=(2, 4), keepdims=True)
    return (jnp.exp(blocks - pooled) * pooled).reshape(values.shape)


def moments(conv_out, total_pixels):
    summed = lax.psum(jnp.sum(conv_out, axis=(0, 1, 2)), ("dp", "rows"))
    mean = summed / total_pixels
    spread = lax.psum(jnp.sum(jnp.square(conv_out - mean), axis=(0, 1, 2)), ("dp", "rows"))
    var = spread / total_pixels
    return (mean, lax.rsqrt(var + EPS))


def kernel_grad(whole, dconv):
    images, rows_here, width, chans = dconv.shape
    widened = jnp.pad(whole, ((0, 0), (0, 0), (1, 1), (0, 0)))
    stacked = []
    for row_off in range(3):
        line = []
        for col_off in range(3):
            window = widened[:, row_off : row_off + rows_here, col_off : col_off + width, :]
            line.append(
                jnp.einsum("bhwc,bhwo->co", window, dconv, preferred_element_type=jnp.float32)
            )
        stacked.append(jnp.stack(line))
    return jnp.stack(stacked)


def generic_local(section_input, conv_weights, norm_gains, norm_shifts, out_grad, out_mask):
    width = out_mask.shape[2]
    images, rows_here = (out_mask.shape[0], out_mask.shape[1])
    total_pixels = float(images * rows_here * width * lax.axis_size("dp") * lax.axis_size("rows"))
    layers, out_here, flat_in = conv_weights.shape
    chans_in = flat_in // 9
    kernels_hwio = conv_weights.reshape(layers, out_here, 3, 3, chans_in).transpose(0, 2, 3, 4, 1)
    middle = layers // 2
    kept = []
    acting = to_maps(section_input, width)
    current = acting.astype(jnp.float32)
    pre_pool = current
    for index in range(layers):
        if index == middle:
            pre_pool = current
            acting = pool_unpool(pre_pool).astype(jnp.bfloat16)
        padded = padded_2(acting, (("rows", 1),), 1)
        whole = lax.all_gather(padded, "tensor", axis=3, tiled=True)
        conv_out = spatial_conv(whole, kernels_hwio[index])
        mean, rstd = moments(conv_out, total_pixels)
        normed = (conv_out - mean) * rstd
        shifted = normed * norm_gains[index] + norm_shifts[index]
        current = jax.nn.silu(shifted)
        acting = current.astype(jnp.bfloat16)
        kept.append((whole, normed, shifted, rstd))
    grad = to_maps(out_grad, width).astype(jnp.float32) * out_mask[..., None].astype(jnp.float32)
    kernel_list = [None] * layers
    gain_list = [None] * layers
    shift_list = [None] * layers
    for index in range(layers - 1, -1, -1):
        whole, normed, shifted, rstd = kept[index]
        unused, pull_silu = jax.vjp(jax.nn.silu, shifted)
        dshift = pull_silu(grad)[0]
        gain_sum, shift_sum = lax.psum(
            (jnp.sum(dshift * normed, axis=(0, 1, 2)), jnp.sum(dshift, axis=(0, 1, 2))),
            ("dp", "rows"),
        )
        gain_list[index] = gain_sum
        shift_list[index] = shift_sum
        dconv = (
            norm_gains[index]
            * rstd
            * (dshift - shift_sum / total_pixels - normed * gain_sum / total_pixels)
        ).astype(jnp.bfloat16)
        summed_kernel = lax.psum(
            kernel_grad(whole, dconv).astype(jnp.bfloat16), ("dp", "rows")
        ).astype(jnp.float32)
        kernel_list[index] = summed_kernel.transpose(3, 0, 1, 2).reshape(out_here, flat_in)
        grad_rim = padded_2(dconv, (("rows", 1),), 1)
        partial_terms = spatial_conv(grad_rim, flipped(kernels_hwio[index]))
        grad_in = lax.psum_scatter(
            partial_terms.astype(jnp.bfloat16), "tensor", scatter_dimension=3, tiled=True
        ).astype(jnp.float32)
        if index == middle:
            unused, pull_pool = jax.vjp(pool_unpool, pre_pool)
            grad = pull_pool(grad_in)[0]
        else:
            grad = grad_in
    return (
        from_maps(acting),
        from_maps(grad),
        jnp.stack(kernel_list),
        jnp.stack(gain_list),
        jnp.stack(shift_list),
    )


GROUPS = 4
LANES = 128
WIDE = 48
CHANS = GROUPS * LANES
F32 = jnp.float32
BF16 = jnp.bfloat16
VMEM = pl.BlockSpec(memory_space=pltpu.VMEM)
SMEM = pl.BlockSpec(memory_space=pltpu.SMEM)
ANY = pl.BlockSpec(memory_space=pltpu.HBM)
FREE = pl.BlockSpec(memory_space=pl.ANY)
LITTLE = pl.CostEstimate(flops=1024, bytes_accessed=1024, transcendentals=0)
PARAMS = pltpu.CompilerParams(vmem_limit_bytes=20 * 1024 * 1024)


def in_hbm(value):
    return pltpu.with_memory_space_constraint(value, pltpu.HBM)


def fits_kernels(mesh):
    return mesh.shape["tensor"] == GROUPS and mesh.shape["rows"] == 2 and mesh.shape["dp"] == 4


def sigmoid(v):
    return 0.5 * jnp.tanh(0.5 * v) + 0.5


def swap_columns(v):
    column = lax.broadcasted_iota(jnp.int32, v.shape, 0)
    return jnp.where(column % 2 == 0, pltpu.roll(v, WIDE - 1, 0), pltpu.roll(v, 1, 0))


def soft_parts(h):
    top = jnp.maximum(h[0], h[1])
    top = jnp.maximum(top, swap_columns(top))
    e0, e1 = jnp.exp(h[0] - top), jnp.exp(h[1] - top)
    total = e0 + e1
    total = total + swap_columns(total)
    pooled = top + jnp.log(total)
    inverse = 1.0 / total
    return e0 * inverse, e1 * inverse, pooled


def soft(h):
    h = h.reshape(2, WIDE, LANES)
    q0, q1, pooled = soft_parts(h)
    return jnp.concatenate([q0 * pooled, q1 * pooled], axis=0)


def soft_pull(h, grad):
    h = h.reshape(2, WIDE, LANES)
    grad = grad.reshape(2, WIDE, LANES)
    q0, q1, pooled = soft_parts(h)
    mix = q0 * grad[0] + q1 * grad[1]
    mix = mix + swap_columns(mix)
    return jnp.concatenate(
        [q0 * (pooled * (grad[0] - mix) + mix), q1 * (pooled * (grad[1] - mix) + mix)], axis=0
    )


def norm_tables(st, group, i_own, i_oth, n_local, total):
    parts = st.shape[0]
    if parts == 2:
        mean, rstd = st[0, 0, 0:1], lax.rsqrt(st[0, 0, 1:2] / total + EPS)
        return rstd, (st[1, 0, 0:1] - mean) * rstd, (st[1, 0, 1:2] - mean) * rstd
    group = 0 if st.shape[1] == 1 else group
    blocks = [st[i, group] for i in range(parts)]
    summed = functools.reduce(jnp.add, blocks)
    mean = summed[0:1] / parts
    apart = functools.reduce(jnp.add, [jnp.square(b - mean) for b in blocks])
    rstd = lax.rsqrt((summed[1:2] + n_local * apart[0:1]) / total + EPS)
    return rstd, (st[i_own, group, 0:1] - mean) * rstd, (st[i_oth, group, 0:1] - mean) * rstd


def left_right(y0, y1, y2):
    rows = y0.shape[0]
    column = lax.broadcasted_iota(jnp.int32, y0.shape, 0) % WIDE
    before = jnp.where(column == 0, 0.0, pltpu.roll(y0, 1, 0))
    after = jnp.where(column == WIDE - 1, 0.0, pltpu.roll(y2, rows - 1, 0))
    return before + y1 + after


def lane_of(group):
    return pl.multiple_of(group * LANES, LANES)


def edge_start(n_own, edge, half):
    return pl.multiple_of((1 - half) * (n_own - edge), WIDE)


def pair_rows(j):
    return pl.ds(pl.multiple_of(j * 2 * WIDE, 2 * WIDE), 2 * WIDE)


def fold(v):
    return jnp.sum(v.reshape(v.shape[0] // 8, 8, LANES), axis=0)


def fwd_kernel(first, pool, layer, total, edge_out, *refs):
    pos, zall = refs[0], refs[1]
    if first:
        w_hbm = refs[2]
    else:
        st, gss, w_hbm = refs[2], refs[3:7], refs[7]
    hb_out, zc_out, edge_ref, st_out, hb, w, y, z, tab, hs, sem = refs[-11:]
    load = pltpu.make_async_copy(w_hbm.at[layer], w, sem.at[0])
    load.start()
    saves = []
    t, r = pos[0], pos[1]
    n_own = z.shape[0]
    halo_at = pl.multiple_of((1 - r) * (n_own + WIDE), WIDE)
    zero_at = pl.multiple_of(r * (n_own + WIDE), WIDE)
    hb[pl.ds(zero_at, WIDE), :] = jnp.zeros((WIDE, CHANS), BF16)
    edge = zall.shape[0] - n_own
    if not first:
        for k in range(GROUPS):
            group = t ^ k
            rstd, own, oth = norm_tables(st, group, pos[2], pos[3], float(n_own), total)
            gain, shift = gss[k][layer - 1 : layer, :], gss[k][layer + 7 : layer + 8, :]
            tab[group, 0:1] = rstd * gain
            tab[group, 1:2] = own * gain + shift
            tab[group, 2:3] = oth * gain + shift

    def act(values, group, which):
        if first:
            return values
        n = values.astype(F32) * tab[group, 0:1, :] + tab[group, which : which + 1, :]
        h = n * sigmoid(n)
        return soft(h) if pool else h

    for group in range(GROUPS):
        lanes = slice(group * LANES, (group + 1) * LANES)
        h = act(zall[n_own : n_own + edge, lanes], group, 2)
        if edge > WIDE:
            hs[...] = h
            h = hs[pl.ds(pl.multiple_of(r * WIDE, WIDE), WIDE), :]
        hb[pl.ds(halo_at, WIDE), lanes] = h.astype(BF16)
    pair, block = 2 * WIDE, n_own // 3
    steps, made = n_own // pair, 0
    summed = jnp.zeros((8, LANES), F32)
    for part in range(3):
        first_row = part * block
        while made < min(steps, (first_row + block + WIDE + pair - 1) // pair):
            at = made * pair
            for group in range(GROUPS):
                lanes = slice(group * LANES, (group + 1) * LANES)
                h = act(zall[at : at + pair, lanes], group, 1)
                hb[at + WIDE : at + WIDE + pair, lanes] = h.astype(BF16)
            made += 1
        if part == 0:
            load.wait()
            rhs = jnp.concatenate(
                [
                    jnp.concatenate([w[:, (3 * i + s) * CHANS : (3 * i + s + 1) * CHANS] for i in range(3)], axis=1)
                    for s in range(3)
                ],
                axis=0,
            )
        start, stop = (0 if part == 0 else first_row + 2 * WIDE), first_row + block + 2 * WIDE
        saves.append(
            pltpu.make_async_copy(hb.at[start:stop], hb_out.at[layer, start:stop], sem.at[1 + part])
        )
        saves[-1].start()
        lhs = jnp.concatenate([hb[first_row + i * WIDE : first_row + i * WIDE + block, :] for i in range(3)], axis=1)
        rows = slice(first_row, first_row + block)
        y[rows, :] = lax.dot_general(lhs, rhs, (((1,), (1,)), ((), ())), preferred_element_type=F32)
        for j in range(block // pair):
            rows = slice(first_row + j * pair, first_row + (j + 1) * pair)
            v = left_right(y[rows, 0:128], y[rows, 128:256], y[rows, 256:384])
            z[rows, :] = v
            summed = summed + fold(v)
    mean = jnp.sum(summed, axis=0, keepdims=True) / n_own
    apart = jnp.zeros((8, LANES), F32)
    for j in range(steps):
        rows = slice(j * pair, (j + 1) * pair)
        v = z[rows, :] - mean
        zc_out[rows, :] = v.astype(BF16)
        apart = apart + fold(jnp.square(v))
    sums = jnp.concatenate([mean, jnp.sum(apart, axis=0, keepdims=True)], axis=0)
    for i in range(st_out.shape[0]):
        st_out[i] = sums
    edge_ref[...] = zc_out[pl.ds(edge_start(n_own, edge_out, r), edge_out), :]
    zc_out[n_own : n_own + edge_out, :] = jnp.zeros((edge_out, LANES), BF16)
    for save in saves:
        save.wait()


def fwd_step(layer, pool, edge_out, total, pos, slots, st, tables, weights, kept, n_own, devices, ties):
    first = st is None
    layers = weights.shape[0]
    extra = () if first else (st, *tables)
    return pl.pallas_call(
        functools.partial(fwd_kernel, first, pool, layer, total, edge_out),
        out_shape=(
            pltpu.HBM((layers, n_own + 2 * WIDE, CHANS), BF16),
            pltpu.VMEM((n_own + edge_out, LANES), BF16),
            pltpu.VMEM((edge_out, LANES), BF16),
            pltpu.VMEM((devices, 2, LANES), F32),
        ),
        in_specs=[SMEM] + [VMEM] * (1 + len(extra)) + [ANY] * (1 if first else 2) + [FREE] * len(ties),
        out_specs=(ANY, VMEM, VMEM, VMEM),
        input_output_aliases={} if first else {3 + len(extra): 0},
        scratch_shapes=[
            pltpu.VMEM((n_own + 2 * WIDE, CHANS), BF16),
            pltpu.VMEM((LANES, 9 * CHANS), BF16),
            pltpu.VMEM((n_own, 3 * LANES), F32),
            pltpu.VMEM((n_own, LANES), F32),
            pltpu.VMEM((GROUPS, 8, LANES), F32),
            pltpu.VMEM((2 * WIDE, LANES), F32),
            pltpu.SemaphoreType.DMA((4,)),
        ],
        compiler_params=PARAMS,
        cost_estimate=pl.CostEstimate(
            flops=2 * n_own * 9 * CHANS * LANES, bytes_accessed=4 * 1024 * 1024, transcendentals=n_own * CHANS
        ),
        name="conv_forward",
    )(pos, slots, *extra, in_hbm(weights), *(() if first else (in_hbm(kept),)), *ties)


def below_kernel(layer, pool, total, top, *refs):
    pos, zc, st, gs = refs[:4]
    if top:
        terms, h_out, dn_out, msg, tab = refs[4:]
    else:
        terms, (dn_out, msg, tab) = refs[4:8], refs[-3:]
    n_own = dn_out.shape[0]
    rstd, own, oth = norm_tables(st, pos[0], pos[2], pos[3], float(n_own), total)
    tab[0:1], tab[1:2] = rstd, own
    tab[2:3], tab[3:4] = gs[layer : layer + 1, :], gs[layer + 8 : layer + 9, :]

    def body(j, accs):
        rows = pair_rows(j)
        xhat = zc[rows, :].astype(F32) * tab[0:1, :] + tab[1:2, :]
        n = xhat * tab[2:3, :] + tab[3:4, :]
        sig = sigmoid(n)
        h = n * sig
        if top:
            g = terms[rows, :].astype(F32)
            h_out[rows, :] = h.astype(BF16)
        else:
            g = functools.reduce(jnp.add, [term[rows, :].astype(F32) for term in terms])
        if pool:
            g = soft_pull(h, g)
        dn = g * (sig * (1.0 + n - h))
        dn_out[rows, :] = dn
        return accs[0] + fold(dn), accs[1] + fold(dn * xhat)

    zero = jnp.zeros((8, LANES), F32)
    sums = lax.fori_loop(0, n_own // (2 * WIDE), body, (zero, zero), unroll=3)
    sums = [jnp.sum(v, axis=0, keepdims=True) for v in sums]
    msg[0:WIDE, :] = dn_out[pl.ds(edge_start(n_own, WIDE, pos[1]), WIDE), :]
    msg[WIDE : WIDE + 8, :] = jnp.concatenate(sums + [jnp.zeros((6, LANES), F32)], axis=0)


def below_step(layer, pool, total, pos, zc, st, gs, terms, ties=()):
    n_own = terms[0].shape[0]
    top = len(terms) == 1
    out_shape = [
        pltpu.VMEM((n_own, LANES), F32),
        pltpu.VMEM((WIDE + 8, LANES), F32),
    ]
    if top:
        out_shape = [jax.ShapeDtypeStruct((n_own, LANES), BF16)] + out_shape
    return pl.pallas_call(
        functools.partial(below_kernel, layer, pool, total, top),
        out_shape=tuple(out_shape),
        in_specs=[SMEM] + [VMEM] * (3 + len(terms)) + [FREE] * len(ties),
        out_specs=(VMEM,) * len(out_shape),
        scratch_shapes=[pltpu.VMEM((8, LANES), F32)],
        compiler_params=PARAMS,
        cost_estimate=LITTLE,
        name="silu_backward",
    )(pos, zc, st, gs, *terms, *ties)


def bwd_kernel(layer, total, *refs):
    pos, dn, dedge, sums, zc, st, gs, w_hbm = refs[:8]
    outs, d_out, d, w, y, tab, sem = refs[-10:-6], *refs[-6:]
    load = pltpu.make_async_copy(w_hbm.at[layer], w, sem)
    load.start()
    t, r = pos[0], pos[1]
    n_own = dn.shape[0]
    halo_at = pl.multiple_of((1 - r) * (n_own + WIDE), WIDE)
    zero_at = pl.multiple_of(r * (n_own + WIDE), WIDE)
    edge = zc.shape[0] - n_own
    d[pl.ds(zero_at, WIDE), :] = jnp.zeros((WIDE, 3 * LANES), BF16)
    rstd, own, oth = norm_tables(st, t, pos[2], pos[3], float(n_own), total)
    scale = gs[layer : layer + 1, :] * rstd
    shift_sum, gain_sum = sums[0:1, :], sums[1:2, :]
    slope = scale * gain_sum / total
    tab[0:1] = scale
    tab[1:2] = slope * rstd
    tab[2:3] = scale * shift_sum / total + slope * own
    tab[3:4] = scale * shift_sum / total + slope * oth

    def spread_columns(v):
        rows = v.shape[0]
        column = lax.broadcasted_iota(jnp.int32, v.shape, 0) % WIDE
        ahead = jnp.where(column == WIDE - 1, 0.0, pltpu.roll(v, rows - 1, 0))
        behind = jnp.where(column == 0, 0.0, pltpu.roll(v, 1, 0))
        return jnp.concatenate([ahead.astype(BF16), v.astype(BF16), behind.astype(BF16)], axis=1)

    near = n_own if edge == WIDE else pl.multiple_of(n_own + r * WIDE, WIDE)
    near = zc[pl.ds(near, WIDE), :].astype(F32)
    d[pl.ds(halo_at, WIDE), :] = spread_columns(dedge[0:WIDE, :] * tab[0:1, :] - tab[3:4, :] - near * tab[1:2, :])
    pair, block = 2 * WIDE, n_own // 3
    steps, made = n_own // pair, 0
    for part in range(3):
        first_row = part * block
        while made < min(steps, (first_row + block + WIDE + pair - 1) // pair):
            at = made * pair
            v = dn[at : at + pair, :] * tab[0:1, :] - tab[2:3, :] - zc[at : at + pair, :].astype(F32) * tab[1:2, :]
            v = spread_columns(v)
            d[at + WIDE : at + WIDE + pair, :] = v
            d_out[at : at + pair, :] = v
            made += 1
        if part == 0:
            load.wait()
            rhs = jnp.concatenate([w[:, i * CHANS : (i + 1) * CHANS] for i in range(9)], axis=0)
        windows = [first_row + (2 - i) * WIDE for i in range(3)]
        lhs = jnp.concatenate([d[at : at + block, :] for at in windows], axis=1)
        y[first_row : first_row + block, :] = jnp.dot(lhs, rhs, preferred_element_type=F32)
        for j in range(block // pair):
            rows = slice(first_row + j * pair, first_row + (j + 1) * pair)
            for k in range(GROUPS):
                outs[k][rows, :] = y[rows, pl.ds(lane_of(t ^ k), LANES)].astype(BF16)


def bwd_step(layer, total, pos, dn, dedge, sums, zc, st, gs, weights, ties):
    n_own = dn.shape[0]
    part = pltpu.VMEM((n_own, LANES), BF16)
    return pl.pallas_call(
        functools.partial(bwd_kernel, layer, total),
        out_shape=(
            part,
            part,
            part,
            part,
            pltpu.VMEM((n_own, 3 * LANES), BF16),
        ),
        in_specs=[SMEM] + [VMEM] * 6 + [ANY] + [FREE] * len(ties),
        out_specs=(VMEM,) * 5,
        scratch_shapes=[
            pltpu.VMEM((n_own + 2 * WIDE, 3 * LANES), BF16),
            pltpu.VMEM((LANES, 9 * CHANS), BF16),
            pltpu.VMEM((n_own, CHANS), F32),
            pltpu.VMEM((8, LANES), F32),
            pltpu.SemaphoreType.DMA,
        ],
        compiler_params=PARAMS,
        cost_estimate=LITTLE,
        name="conv_backward",
    )(pos, dn, dedge, sums, zc, st, gs, in_hbm(weights), *ties)


def last_kernel(t0, t1, t2, t3, *refs):
    out = refs[-1]

    def body(j, carry):
        rows = pair_rows(j)
        out[rows, :] = functools.reduce(jnp.add, [term[rows, :].astype(F32) for term in (t0, t1, t2, t3)])
        return carry

    lax.fori_loop(0, out.shape[0] // (2 * WIDE), body, 0)


def last_step(terms, ties):
    return pl.pallas_call(
        last_kernel,
        out_shape=jax.ShapeDtypeStruct(terms[0].shape, F32),
        in_specs=[VMEM] * 4 + [FREE] * len(ties),
        out_specs=VMEM,
        compiler_params=PARAMS,
        cost_estimate=LITTLE,
        name="add_terms",
    )(*terms, *ties)


def halves_kernel(keep, got, out):
    out[...] = (keep[...].astype(F32) + got[...].astype(F32)).astype(BF16)


def add_halves(keep, got):
    return pl.pallas_call(
        halves_kernel,
        out_shape=jax.ShapeDtypeStruct(keep.shape, BF16),
        in_specs=[VMEM] * 2,
        out_specs=VMEM,
        compiler_params=PARAMS,
        cost_estimate=LITTLE,
        name="add_halves",
    )(keep, got)


def wgrad_kernel(layer, pos, d, hb_hbm, *refs):
    keep, send, hb, grad, sem = refs[-5:]
    load = pltpu.make_async_copy(hb_hbm.at[layer], hb, sem)
    load.start()
    n_own = d.shape[0]
    lhs = d[...]
    load.wait()
    for i in range(3):
        part = lax.dot_general(
            lhs, hb[i * WIDE : i * WIDE + n_own, :], (((0,), (0,)), ((), ())), preferred_element_type=F32
        ).astype(BF16)
        for s in range(3):
            grad[:, (3 * i + s) * CHANS : (3 * i + s + 1) * CHANS] = part[s * LANES : (s + 1) * LANES]
    half = LANES // 2
    keep[...] = grad[pl.ds(pl.multiple_of(pos[1] * half, half), half), :]
    send[...] = grad[pl.ds(pl.multiple_of((1 - pos[1]) * half, half), half), :]


def wgrad_step(layer, pos, d, kept, ties):
    half = pltpu.VMEM((LANES // 2, 9 * CHANS), BF16)
    return pl.pallas_call(
        functools.partial(wgrad_kernel, layer),
        out_shape=(half, half),
        in_specs=[SMEM, VMEM, ANY] + [FREE] * len(ties),
        out_specs=(VMEM, VMEM),
        scratch_shapes=[
            pltpu.VMEM(kept.shape[1:], BF16),
            pltpu.VMEM((LANES, 9 * CHANS), BF16),
            pltpu.SemaphoreType.DMA,
        ],
        compiler_params=PARAMS,
        cost_estimate=LITTLE,
        name="kernel_gradient",
    )(pos, d, in_hbm(kept), *ties)


def place_kernel(layers, fresh, pos, *refs):
    count = 2 * len(layers)
    sources = refs[:count]
    out, held, wide, sem = refs[-4:]
    half = LANES // 2
    r = pos[1]
    loads = [pltpu.make_async_copy(sources[j], held.at[j], sem.at[j]) for j in range(count)]
    for load in loads:
        load.start()
    stores = []
    for j in range(count):
        at = pl.multiple_of((r if j % 2 == 0 else 1 - r) * half, half)
        if j >= 2:
            stores[j - 2].wait()
        loads[j].wait()
        wide[j % 2] = held[j].astype(F32)
        store = pltpu.make_async_copy(wide.at[j % 2], out.at[layers[j // 2], pl.ds(at, half)], sem.at[count + j])
        store.start()
        stores.append(store)
    for store in stores[-2:]:
        store.wait()


def place_step(layers, pos, sources, whole, count):
    half = LANES // 2
    jobs = len(sources)
    return pl.pallas_call(
        functools.partial(place_kernel, layers, whole is None),
        out_shape=pltpu.HBM((count, LANES, 9 * CHANS), F32),
        in_specs=[SMEM] + [ANY] * jobs + ([] if whole is None else [ANY]),
        out_specs=ANY,
        input_output_aliases={} if whole is None else {1 + jobs: 0},
        scratch_shapes=[
            pltpu.VMEM((jobs, half, 9 * CHANS), BF16),
            pltpu.VMEM((2, half, 9 * CHANS), F32),
            pltpu.SemaphoreType.DMA((2 * jobs,)),
        ],
        compiler_params=PARAMS,
        cost_estimate=LITTLE,
        name="place_gradients",
    )(pos, *[in_hbm(v) for v in sources], *(() if whole is None else (in_hbm(whole),)))


def swap_with(value, axis, k):
    return lax.ppermute(value, axis, [(i, i ^ k) for i in range(lax.axis_size(axis))])


def spread(own):
    return (own, *[swap_with(own, "tensor", k) for k in range(1, GROUPS)])


def share_moments(mine, count):
    other = swap_with(mine, "rows", 1)
    mean = 0.5 * (mine[0:1] + other[0:1])
    apart = mine[1:2] + other[1:2] + (0.5 * count) * jnp.square(other[0:1] - mine[0:1])
    own = jnp.concatenate([mean, apart], axis=0)
    all_four = [own] + [swap_with(own, "dp", k) for k in (1, 2, 3)]
    mean = 0.25 * functools.reduce(jnp.add, [v[0:1] for v in all_four])
    apart = functools.reduce(jnp.add, [v[1:2] + (2.0 * count) * jnp.square(v[0:1] - mean) for v in all_four])
    return jnp.concatenate([mean, apart, mine[0:1], other[0:1]], axis=0).reshape(2, 1, 2, LANES)


def halo_of_input(x, half):
    n_own = x.shape[0]
    edge = jnp.where(half == 0, x[n_own - WIDE :], x[:WIDE])
    return jnp.concatenate([x, swap_with(edge, "rows", 1)], axis=0)


def fast_local(section_input, conv_weights, norm_gains, norm_shifts, out_grad, out_mask):
    images, rows_here, width = out_mask.shape
    layers = conv_weights.shape[0]
    n_own = rows_here * width
    parts = lax.axis_size("dp") * lax.axis_size("rows")
    total = float(n_own * parts)
    t, half = lax.axis_index("tensor"), lax.axis_index("rows")
    image = lax.axis_index("dp")
    pos = jnp.stack([t, half, 2 * image + half, 2 * image + 1 - half]).astype(jnp.int32)
    middle = layers // 2
    x = to_maps(section_input, width).reshape(n_own, LANES)
    slots = lax.all_gather(halo_of_input(x, half), "tensor", axis=1, tiled=True)
    pad = jnp.zeros((8 - layers, LANES), F32)
    tables = spread(jnp.concatenate([norm_gains, pad, norm_shifts, pad], axis=0))
    top_grad = (to_maps(out_grad, width) * out_mask[..., None].astype(BF16)).reshape(n_own, LANES)

    st, kept = None, None
    halves = ("dp", "rows")
    kept_z, kept_st = [], []
    for layer in range(layers):
        last = layer + 1 == layers
        edge = 2 * WIDE if layer + 1 == middle else WIDE
        everyone = ("dp", "rows", "tensor")
        devices = 1 if last else parts * GROUPS
        kept, zc, rim, local = fwd_step(
            layer,
            layer == middle,
            edge,
            total,
            pos,
            slots,
            st,
            tables,
            conv_weights,
            kept,
            n_own,
            devices,
            (top_grad,) if layer == 2 else (),
        )
        rim = swap_with(rim, "rows", 1)
        if last:
            st = share_moments(local[0], float(n_own))
        else:
            st = lax.all_to_all(local, everyone, split_axis=0, concat_axis=0, tiled=True)
            st = st.reshape(parts, GROUPS, 2, LANES)
        zc = lax.dynamic_update_slice_in_dim(zc, rim, n_own, axis=0)
        kept_z.append(zc)
        kept_st.append(st)
        if not last:
            slots = lax.all_gather(zc, "tensor", axis=1, tiled=True)
    top = layers - 1
    h_last, dn, msg = below_step(top, False, total, pos, kept_z[top], kept_st[top], tables[0], (top_grad,))

    def with_other(values):
        return [v for mine in values for v in (mine, swap_with(mine, "rows", 1))]

    sum_list, pairs = [None] * layers, [None] * layers
    ahead, back = [[0, 1, 3, 2]], [[2, 3, 1, 0]]
    urgent = ()
    for layer in range(layers - 1, -1, -1):
        got = swap_with(msg, "rows", 1)
        sums = msg[WIDE:] + got[WIDE:]
        one, two, three = (swap_with(sums, "dp", k) for k in (1, 2, 3))
        sums = (sums + one) + (two + three)
        sum_list[layer] = sums
        *terms, d = bwd_step(
            layer, total, pos, dn, got, sums, kept_z[layer], kept_st[layer], tables[0], conv_weights, urgent
        )
        terms = (terms[0], *[swap_with(terms[k], "tensor", k) for k in range(1, GROUPS)])
        keep, send = wgrad_step(layer, pos, d, kept, (in_hbm(upper[0]),) if layer == 1 else ())
        other = swap_with(send, "rows", 1)
        pairs[layer] = add_halves(keep, other)
        urgent, settled = (other,), (() if layer + 1 == layers else (pairs[layer + 1],))
        if layer == 4:
            upper = lax.psum((pairs[5], pairs[4]), "dp", axis_index_groups=ahead)
        if layer == 2:
            mid = lax.psum((pairs[3], pairs[2]), "dp", axis_index_groups=back)
        if layer > 0:
            below = layer - 1
            dn, msg = below_step(
                below, layer == middle, total, pos, kept_z[below], kept_st[below], tables[0], terms, (keep, *settled)
            )
        else:
            grad = last_step(terms, (pairs[0], pairs[1]))
    tied, upper = lax.optimization_barrier(((pairs[1], pairs[0]), upper))
    lower = lax.psum(tied, "dp", axis_index_groups=ahead)
    shape = (images, rows_here, width, LANES)
    grad, mid = lax.optimization_barrier((grad, mid))
    outputs = (from_maps(h_last.reshape(shape)), from_maps(grad.reshape(shape)))
    whole = place_step((5, 4, 3, 2), pos, with_other((*upper, *mid)), None, layers)
    sums = jnp.stack(sum_list)
    sums = (sums[:, 1], sums[:, 0])
    lower, whole, outputs, sums = lax.optimization_barrier((lower, whole, outputs, sums))
    whole = place_step((1, 0), pos, with_other(lower), whole, layers)
    return (*outputs, whole, *sums)


def solution(mesh):
    in_specs = (
        P("dp", "rows", "tensor"),
        P(None, "tensor", None),
        P(None, "tensor"),
        P(None, "tensor"),
        P("dp", "rows", "tensor"),
        P("dp", "rows", None),
    )
    out_specs = (
        P("dp", "rows", "tensor"),
        P("dp", "rows", "tensor"),
        P(None, "tensor", None),
        P(None, "tensor"),
        P(None, "tensor"),
    )
    local = fast_local if fits_kernels(mesh) else generic_local
    return jax.shard_map(local, mesh=mesh, in_specs=in_specs, out_specs=out_specs, check_vma=False)
```

```python
import functools

import jax
import jax.numpy as jnp
from jax import lax
from jax.experimental import pallas as pl
from jax.experimental.pallas import tpu as pltpu
from jax.sharding import PartitionSpec as P

EPS = 1e-05


def padded_2(cells, sides, width):
    for axis, dim in sides:
        count = lax.axis_size(axis)
        ends = count - 1
        head = lax.slice_in_dim(cells, 0, width, axis=dim)
        tail = lax.slice_in_dim(cells, cells.shape[dim] - width, cells.shape[dim], axis=dim)
        cells = jnp.concatenate(
            [
                lax.ppermute(tail, axis, [(i, (i + 1) % count) for i in range(ends)]),
                cells,
                lax.ppermute(head, axis, [((i + 1) % count, i) for i in range(ends)]),
            ],
            axis=dim,
        )
    return cells


def to_maps(flat, width):
    count, high, merged = flat.shape
    return flat.reshape(count, high, merged // width, width).transpose(0, 1, 3, 2)


def from_maps(maps):
    count, high, wide, chans = maps.shape
    return maps.transpose(0, 1, 3, 2).reshape(count, high, chans * wide)


def spatial_conv(padded, kernel):
    return lax.conv_general_dilated(
        padded,
        kernel,
        (1, 1),
        ((0, 0), (1, 1)),
        dimension_numbers=("NHWC", "HWIO", "NHWC"),
        preferred_element_type=jnp.float32,
    )


def flipped(kernel):
    return jnp.transpose(kernel[::-1, ::-1], (0, 1, 3, 2))


def pool_unpool(values):
    count, high, wide, chans = values.shape
    blocks = values.reshape(count, high // 2, 2, wide // 2, 2, chans)
    pooled = jax.nn.logsumexp(blocks, axis=(2, 4), keepdims=True)
    return (jnp.exp(blocks - pooled) * pooled).reshape(values.shape)


def moments(conv_out, total_pixels):
    summed = lax.psum(jnp.sum(conv_out, axis=(0, 1, 2)), ("dp", "rows"))
    mean = summed / total_pixels
    spread = lax.psum(jnp.sum(jnp.square(conv_out - mean), axis=(0, 1, 2)), ("dp", "rows"))
    var = spread / total_pixels
    return (mean, lax.rsqrt(var + EPS))


def kernel_grad(whole, dconv):
    images, rows_here, width, chans = dconv.shape
    widened = jnp.pad(whole, ((0, 0), (0, 0), (1, 1), (0, 0)))
    stacked = []
    for row_off in range(3):
        line = []
        for col_off in range(3):
            window = widened[:, row_off : row_off + rows_here, col_off : col_off + width, :]
            line.append(
                jnp.einsum("bhwc,bhwo->co", window, dconv, preferred_element_type=jnp.float32)
            )
        stacked.append(jnp.stack(line))
    return jnp.stack(stacked)


def generic_local(section_input, conv_weights, norm_gains, norm_shifts, out_grad, out_mask):
    width = out_mask.shape[2]
    images, rows_here = (out_mask.shape[0], out_mask.shape[1])
    total_pixels = float(images * rows_here * width * lax.axis_size("dp") * lax.axis_size("rows"))
    layers, out_here, flat_in = conv_weights.shape
    chans_in = flat_in // 9
    kernels_hwio = conv_weights.reshape(layers, out_here, 3, 3, chans_in).transpose(0, 2, 3, 4, 1)
    middle = layers // 2
    kept = []
    acting = to_maps(section_input, width)
    current = acting.astype(jnp.float32)
    pre_pool = current
    for index in range(layers):
        if index == middle:
            pre_pool = current
            acting = pool_unpool(pre_pool).astype(jnp.bfloat16)
        padded = padded_2(acting, (("rows", 1),), 1)
        whole = lax.all_gather(padded, "tensor", axis=3, tiled=True)
        conv_out = spatial_conv(whole, kernels_hwio[index])
        mean, rstd = moments(conv_out, total_pixels)
        normed = (conv_out - mean) * rstd
        shifted = normed * norm_gains[index] + norm_shifts[index]
        current = jax.nn.silu(shifted)
        acting = current.astype(jnp.bfloat16)
        kept.append((whole, normed, shifted, rstd))
    grad = to_maps(out_grad, width).astype(jnp.float32) * out_mask[..., None].astype(jnp.float32)
    kernel_list = [None] * layers
    gain_list = [None] * layers
    shift_list = [None] * layers
    for index in range(layers - 1, -1, -1):
        whole, normed, shifted, rstd = kept[index]
        unused, pull_silu = jax.vjp(jax.nn.silu, shifted)
        dshift = pull_silu(grad)[0]
        gain_sum, shift_sum = lax.psum(
            (jnp.sum(dshift * normed, axis=(0, 1, 2)), jnp.sum(dshift, axis=(0, 1, 2))),
            ("dp", "rows"),
        )
        gain_list[index] = gain_sum
        shift_list[index] = shift_sum
        dconv = (
            norm_gains[index]
            * rstd
            * (dshift - shift_sum / total_pixels - normed * gain_sum / total_pixels)
        ).astype(jnp.bfloat16)
        summed_kernel = lax.psum(
            kernel_grad(whole, dconv).astype(jnp.bfloat16), ("dp", "rows")
        ).astype(jnp.float32)
        kernel_list[index] = summed_kernel.transpose(3, 0, 1, 2).reshape(out_here, flat_in)
        grad_rim = padded_2(dconv, (("rows", 1),), 1)
        partial_terms = spatial_conv(grad_rim, flipped(kernels_hwio[index]))
        grad_in = lax.psum_scatter(
            partial_terms.astype(jnp.bfloat16), "tensor", scatter_dimension=3, tiled=True
        ).astype(jnp.float32)
        if index == middle:
            unused, pull_pool = jax.vjp(pool_unpool, pre_pool)
            grad = pull_pool(grad_in)[0]
        else:
            grad = grad_in
    return (
        from_maps(acting),
        from_maps(grad),
        jnp.stack(kernel_list),
        jnp.stack(gain_list),
        jnp.stack(shift_list),
    )


GROUPS = 4
LANES = 128
WIDE = 48
CHANS = GROUPS * LANES
F32 = jnp.float32
BF16 = jnp.bfloat16
VMEM = pl.BlockSpec(memory_space=pltpu.VMEM)
SMEM = pl.BlockSpec(memory_space=pltpu.SMEM)
ANY = pl.BlockSpec(memory_space=pltpu.HBM)
FREE = pl.BlockSpec(memory_space=pl.ANY)
LITTLE = pl.CostEstimate(flops=1024, bytes_accessed=1024, transcendentals=0)
PARAMS = pltpu.CompilerParams(vmem_limit_bytes=20 * 1024 * 1024)


def in_hbm(value):
    return pltpu.with_memory_space_constraint(value, pltpu.HBM)


def fits_kernels(mesh):
    return mesh.shape["tensor"] == GROUPS and mesh.shape["rows"] == 2 and mesh.shape["dp"] == 4


def sigmoid(v):
    return 0.5 * jnp.tanh(0.5 * v) + 0.5


def swap_columns(v):
    column = lax.broadcasted_iota(jnp.int32, v.shape, 0)
    return jnp.where(column % 2 == 0, pltpu.roll(v, WIDE - 1, 0), pltpu.roll(v, 1, 0))


def soft_parts(h):
    top = jnp.maximum(h[0], h[1])
    top = jnp.maximum(top, swap_columns(top))
    e0, e1 = jnp.exp(h[0] - top), jnp.exp(h[1] - top)
    total = e0 + e1
    total = total + swap_columns(total)
    pooled = top + jnp.log(total)
    inverse = 1.0 / total
    return e0 * inverse, e1 * inverse, pooled


def soft(h):
    h = h.reshape(2, WIDE, LANES)
    q0, q1, pooled = soft_parts(h)
    return jnp.concatenate([q0 * pooled, q1 * pooled], axis=0)


def soft_pull(h, grad):
    h = h.reshape(2, WIDE, LANES)
    grad = grad.reshape(2, WIDE, LANES)
    q0, q1, pooled = soft_parts(h)
    mix = q0 * grad[0] + q1 * grad[1]
    mix = mix + swap_columns(mix)
    return jnp.concatenate(
        [q0 * (pooled * (grad[0] - mix) + mix), q1 * (pooled * (grad[1] - mix) + mix)], axis=0
    )


def norm_tables(st, group, i_own, i_oth, n_local, total):
    parts = st.shape[0]
    if parts == 2:
        mean, rstd = st[0, 0, 0:1], lax.rsqrt(st[0, 0, 1:2] / total + EPS)
        return rstd, (st[1, 0, 0:1] - mean) * rstd, (st[1, 0, 1:2] - mean) * rstd
    group = 0 if st.shape[1] == 1 else group
    blocks = [st[i, group] for i in range(parts)]
    summed = functools.reduce(jnp.add, blocks)
    mean = summed[0:1] / parts
    apart = functools.reduce(jnp.add, [jnp.square(b - mean) for b in blocks])
    rstd = lax.rsqrt((summed[1:2] + n_local * apart[0:1]) / total + EPS)
    return rstd, (st[i_own, group, 0:1] - mean) * rstd, (st[i_oth, group, 0:1] - mean) * rstd


def left_right(y0, y1, y2):
    rows = y0.shape[0]
    column = lax.broadcasted_iota(jnp.int32, y0.shape, 0) % WIDE
    before = jnp.where(column == 0, 0.0, pltpu.roll(y0, 1, 0))
    after = jnp.where(column == WIDE - 1, 0.0, pltpu.roll(y2, rows - 1, 0))
    return before + y1 + after


def lane_of(group):
    return pl.multiple_of(group * LANES, LANES)


def edge_start(n_own, edge, half):
    return pl.multiple_of((1 - half) * (n_own - edge), WIDE)


def pair_rows(j):
    return pl.ds(pl.multiple_of(j * 2 * WIDE, 2 * WIDE), 2 * WIDE)


def fold(v):
    return jnp.sum(v.reshape(v.shape[0] // 8, 8, LANES), axis=0)


def fwd_kernel(first, pool, layer, total, edge_out, *refs):
    pos, zall = refs[0], refs[1]
    if first:
        w_hbm = refs[2]
    else:
        st, gss, w_hbm = refs[2], refs[3:7], refs[7]
    hb_out, zc_out, edge_ref, st_out, hb, w, y, z, tab, hs, sem = refs[-11:]
    load = pltpu.make_async_copy(w_hbm.at[layer], w, sem.at[0])
    load.start()
    saves = []
    t, r = pos[0], pos[1]
    n_own = z.shape[0]
    halo_at = pl.multiple_of((1 - r) * (n_own + WIDE), WIDE)
    zero_at = pl.multiple_of(r * (n_own + WIDE), WIDE)
    hb[pl.ds(zero_at, WIDE), :] = jnp.zeros((WIDE, CHANS), BF16)
    edge = zall.shape[0] - n_own
    if not first:
        for k in range(GROUPS):
            group = t ^ k
            rstd, own, oth = norm_tables(st, group, pos[2], pos[3], float(n_own), total)
            gain, shift = gss[k][layer - 1 : layer, :], gss[k][layer + 7 : layer + 8, :]
            tab[group, 0:1] = rstd * gain
            tab[group, 1:2] = own * gain + shift
            tab[group, 2:3] = oth * gain + shift

    def act(values, group, which):
        if first:
            return values
        n = values.astype(F32) * tab[group, 0:1, :] + tab[group, which : which + 1, :]
        h = n * sigmoid(n)
        return soft(h) if pool else h

    for group in range(GROUPS):
        lanes = slice(group * LANES, (group + 1) * LANES)
        h = act(zall[n_own : n_own + edge, lanes], group, 2)
        if edge > WIDE:
            hs[...] = h
            h = hs[pl.ds(pl.multiple_of(r * WIDE, WIDE), WIDE), :]
        hb[pl.ds(halo_at, WIDE), lanes] = h.astype(BF16)
    pair, block = 2 * WIDE, n_own // 3
    steps, made = n_own // pair, 0
    summed = jnp.zeros((8, LANES), F32)
    for part in range(3):
        first_row = part * block
        while made < min(steps, (first_row + block + WIDE + pair - 1) // pair):
            at = made * pair
            for group in range(GROUPS):
                lanes = slice(group * LANES, (group + 1) * LANES)
                h = act(zall[at : at + pair, lanes], group, 1)
                hb[at + WIDE : at + WIDE + pair, lanes] = h.astype(BF16)
            made += 1
        if part == 0:
            load.wait()
            rhs = jnp.concatenate(
                [
                    jnp.concatenate([w[:, (3 * i + s) * CHANS : (3 * i + s + 1) * CHANS] for i in range(3)], axis=1)
                    for s in range(3)
                ],
                axis=0,
            )
        start, stop = (0 if part == 0 else first_row + 2 * WIDE), first_row + block + 2 * WIDE
        saves.append(
            pltpu.make_async_copy(hb.at[start:stop], hb_out.at[layer, start:stop], sem.at[1 + part])
        )
        saves[-1].start()
        lhs = jnp.concatenate([hb[first_row + i * WIDE : first_row + i * WIDE + block, :] for i in range(3)], axis=1)
        rows = slice(first_row, first_row + block)
        y[rows, :] = lax.dot_general(lhs, rhs, (((1,), (1,)), ((), ())), preferred_element_type=F32)
        for j in range(block // pair):
            rows = slice(first_row + j * pair, first_row + (j + 1) * pair)
            v = left_right(y[rows, 0:128], y[rows, 128:256], y[rows, 256:384])
            z[rows, :] = v
            summed = summed + fold(v)
    mean = jnp.sum(summed, axis=0, keepdims=True) / n_own
    apart = jnp.zeros((8, LANES), F32)
    for j in range(steps):
        rows = slice(j * pair, (j + 1) * pair)
        v = z[rows, :] - mean
        zc_out[rows, :] = v.astype(BF16)
        apart = apart + fold(jnp.square(v))
    sums = jnp.concatenate([mean, jnp.sum(apart, axis=0, keepdims=True)], axis=0)
    for i in range(st_out.shape[0]):
        st_out[i] = sums
    edge_ref[...] = zc_out[pl.ds(edge_start(n_own, edge_out, r), edge_out), :]
    zc_out[n_own : n_own + edge_out, :] = jnp.zeros((edge_out, LANES), BF16)
    for save in saves:
        save.wait()


def fwd_step(layer, pool, edge_out, total, pos, slots, st, tables, weights, kept, n_own, devices, ties):
    first = st is None
    layers = weights.shape[0]
    extra = () if first else (st, *tables)
    return pl.pallas_call(
        functools.partial(fwd_kernel, first, pool, layer, total, edge_out),
        out_shape=(
            pltpu.HBM((layers, n_own + 2 * WIDE, CHANS), BF16),
            pltpu.VMEM((n_own + edge_out, LANES), BF16),
            pltpu.VMEM((edge_out, LANES), BF16),
            pltpu.VMEM((devices, 2, LANES), F32),
        ),
        in_specs=[SMEM] + [VMEM] * (1 + len(extra)) + [ANY] * (1 if first else 2) + [FREE] * len(ties),
        out_specs=(ANY, VMEM, VMEM, VMEM),
        input_output_aliases={} if first else {3 + len(extra): 0},
        scratch_shapes=[
            pltpu.VMEM((n_own + 2 * WIDE, CHANS), BF16),
            pltpu.VMEM((LANES, 9 * CHANS), BF16),
            pltpu.VMEM((n_own, 3 * LANES), F32),
            pltpu.VMEM((n_own, LANES), F32),
            pltpu.VMEM((GROUPS, 8, LANES), F32),
            pltpu.VMEM((2 * WIDE, LANES), F32),
            pltpu.SemaphoreType.DMA((4,)),
        ],
        compiler_params=PARAMS,
        cost_estimate=pl.CostEstimate(
            flops=2 * n_own * 9 * CHANS * LANES, bytes_accessed=4 * 1024 * 1024, transcendentals=n_own * CHANS
        ),
        name="conv_forward",
    )(pos, slots, *extra, in_hbm(weights), *(() if first else (in_hbm(kept),)), *ties)


def below_kernel(layer, pool, total, top, *refs):
    pos, zc, st, gs = refs[:4]
    if top:
        terms, h_out, dn_out, msg, tab = refs[4:]
    else:
        terms, (dn_out, msg, tab) = refs[4:8], refs[-3:]
    n_own = dn_out.shape[0]
    rstd, own, oth = norm_tables(st, pos[0], pos[2], pos[3], float(n_own), total)
    tab[0:1], tab[1:2] = rstd, own
    tab[2:3], tab[3:4] = gs[layer : layer + 1, :], gs[layer + 8 : layer + 9, :]

    def body(j, accs):
        rows = pair_rows(j)
        xhat = zc[rows, :].astype(F32) * tab[0:1, :] + tab[1:2, :]
        n = xhat * tab[2:3, :] + tab[3:4, :]
        sig = sigmoid(n)
        h = n * sig
        if top:
            g = terms[rows, :].astype(F32)
            h_out[rows, :] = h.astype(BF16)
        else:
            g = functools.reduce(jnp.add, [term[rows, :].astype(F32) for term in terms])
        if pool:
            g = soft_pull(h, g)
        dn = g * (sig * (1.0 + n - h))
        dn_out[rows, :] = dn
        return accs[0] + fold(dn), accs[1] + fold(dn * xhat)

    zero = jnp.zeros((8, LANES), F32)
    sums = lax.fori_loop(0, n_own // (2 * WIDE), body, (zero, zero), unroll=3)
    sums = [jnp.sum(v, axis=0, keepdims=True) for v in sums]
    msg[0:WIDE, :] = dn_out[pl.ds(edge_start(n_own, WIDE, pos[1]), WIDE), :]
    msg[WIDE : WIDE + 8, :] = jnp.concatenate(sums + [jnp.zeros((6, LANES), F32)], axis=0)


def below_step(layer, pool, total, pos, zc, st, gs, terms, ties=()):
    n_own = terms[0].shape[0]
    top = len(terms) == 1
    out_shape = [
        pltpu.VMEM((n_own, LANES), F32),
        pltpu.VMEM((WIDE + 8, LANES), F32),
    ]
    if top:
        out_shape = [jax.ShapeDtypeStruct((n_own, LANES), BF16)] + out_shape
    return pl.pallas_call(
        functools.partial(below_kernel, layer, pool, total, top),
        out_shape=tuple(out_shape),
        in_specs=[SMEM] + [VMEM] * (3 + len(terms)) + [FREE] * len(ties),
        out_specs=(VMEM,) * len(out_shape),
        scratch_shapes=[pltpu.VMEM((8, LANES), F32)],
        compiler_params=PARAMS,
        cost_estimate=LITTLE,
        name="silu_backward",
    )(pos, zc, st, gs, *terms, *ties)


def bwd_kernel(layer, total, *refs):
    pos, dn, dedge, sums, zc, st, gs, w_hbm = refs[:8]
    outs, d_out, d, w, y, tab, sem = refs[-10:-6], *refs[-6:]
    load = pltpu.make_async_copy(w_hbm.at[layer], w, sem)
    load.start()
    t, r = pos[0], pos[1]
    n_own = dn.shape[0]
    halo_at = pl.multiple_of((1 - r) * (n_own + WIDE), WIDE)
    zero_at = pl.multiple_of(r * (n_own + WIDE), WIDE)
    edge = zc.shape[0] - n_own
    d[pl.ds(zero_at, WIDE), :] = jnp.zeros((WIDE, 3 * LANES), BF16)
    rstd, own, oth = norm_tables(st, t, pos[2], pos[3], float(n_own), total)
    scale = gs[layer : layer + 1, :] * rstd
    shift_sum, gain_sum = sums[0:1, :], sums[1:2, :]
    slope = scale * gain_sum / total
    tab[0:1] = scale
    tab[1:2] = slope * rstd
    tab[2:3] = scale * shift_sum / total + slope * own
    tab[3:4] = scale * shift_sum / total + slope * oth

    def spread_columns(v):
        rows = v.shape[0]
        column = lax.broadcasted_iota(jnp.int32, v.shape, 0) % WIDE
        ahead = jnp.where(column == WIDE - 1, 0.0, pltpu.roll(v, rows - 1, 0))
        behind = jnp.where(column == 0, 0.0, pltpu.roll(v, 1, 0))
        return jnp.concatenate([ahead.astype(BF16), v.astype(BF16), behind.astype(BF16)], axis=1)

    near = n_own if edge == WIDE else pl.multiple_of(n_own + r * WIDE, WIDE)
    near = zc[pl.ds(near, WIDE), :].astype(F32)
    d[pl.ds(halo_at, WIDE), :] = spread_columns(dedge[0:WIDE, :] * tab[0:1, :] - tab[3:4, :] - near * tab[1:2, :])
    pair, block = 2 * WIDE, n_own // 3
    steps, made = n_own // pair, 0
    for part in range(3):
        first_row = part * block
        while made < min(steps, (first_row + block + WIDE + pair - 1) // pair):
            at = made * pair
            v = dn[at : at + pair, :] * tab[0:1, :] - tab[2:3, :] - zc[at : at + pair, :].astype(F32) * tab[1:2, :]
            v = spread_columns(v)
            d[at + WIDE : at + WIDE + pair, :] = v
            d_out[at : at + pair, :] = v
            made += 1
        if part == 0:
            load.wait()
            rhs = jnp.concatenate([w[:, i * CHANS : (i + 1) * CHANS] for i in range(9)], axis=0)
        windows = [first_row + (2 - i) * WIDE for i in range(3)]
        lhs = jnp.concatenate([d[at : at + block, :] for at in windows], axis=1)
        y[first_row : first_row + block, :] = jnp.dot(lhs, rhs, preferred_element_type=F32)
        for j in range(block // pair):
            rows = slice(first_row + j * pair, first_row + (j + 1) * pair)
            for k in range(GROUPS):
                outs[k][rows, :] = y[rows, pl.ds(lane_of(t ^ k), LANES)].astype(BF16)


def bwd_step(layer, total, pos, dn, dedge, sums, zc, st, gs, weights, ties):
    n_own = dn.shape[0]
    part = pltpu.VMEM((n_own, LANES), BF16)
    return pl.pallas_call(
        functools.partial(bwd_kernel, layer, total),
        out_shape=(
            part,
            part,
            part,
            part,
            pltpu.VMEM((n_own, 3 * LANES), BF16),
        ),
        in_specs=[SMEM] + [VMEM] * 6 + [ANY] + [FREE] * len(ties),
        out_specs=(VMEM,) * 5,
        scratch_shapes=[
            pltpu.VMEM((n_own + 2 * WIDE, 3 * LANES), BF16),
            pltpu.VMEM((LANES, 9 * CHANS), BF16),
            pltpu.VMEM((n_own, CHANS), F32),
            pltpu.VMEM((8, LANES), F32),
            pltpu.SemaphoreType.DMA,
        ],
        compiler_params=PARAMS,
        cost_estimate=LITTLE,
        name="conv_backward",
    )(pos, dn, dedge, sums, zc, st, gs, in_hbm(weights), *ties)


def last_kernel(t0, t1, t2, t3, *refs):
    out = refs[-1]

    def body(j, carry):
        rows = pair_rows(j)
        out[rows, :] = functools.reduce(jnp.add, [term[rows, :].astype(F32) for term in (t0, t1, t2, t3)])
        return carry

    lax.fori_loop(0, out.shape[0] // (2 * WIDE), body, 0)


def last_step(terms, ties):
    return pl.pallas_call(
        last_kernel,
        out_shape=jax.ShapeDtypeStruct(terms[0].shape, F32),
        in_specs=[VMEM] * 4 + [FREE] * len(ties),
        out_specs=VMEM,
        compiler_params=PARAMS,
        cost_estimate=LITTLE,
        name="add_terms",
    )(*terms, *ties)


def halves_kernel(keep, got, out):
    out[...] = (keep[...].astype(F32) + got[...].astype(F32)).astype(BF16)


def add_halves(keep, got):
    return pl.pallas_call(
        halves_kernel,
        out_shape=jax.ShapeDtypeStruct(keep.shape, BF16),
        in_specs=[VMEM] * 2,
        out_specs=VMEM,
        compiler_params=PARAMS,
        cost_estimate=LITTLE,
        name="add_halves",
    )(keep, got)


def bundle_kernel(keep1, got1, keep0, got0, *refs):
    out = refs[-1]
    rows = LANES // 8
    for i in range(4):
        at = slice(i * rows, (i + 1) * rows)
        out[i, 0:rows] = (keep1[at, :].astype(F32) + got1[at, :].astype(F32)).astype(BF16)
        out[i, rows : 2 * rows] = (keep0[at, :].astype(F32) + got0[at, :].astype(F32)).astype(BF16)


def bundle_halves(upper, lower, ties):
    return pl.pallas_call(
        bundle_kernel,
        out_shape=pltpu.VMEM((4, LANES // 4, 9 * CHANS), BF16),
        in_specs=[VMEM] * 4 + [FREE] * len(ties),
        out_specs=VMEM,
        compiler_params=PARAMS,
        cost_estimate=LITTLE,
        name="bundle_halves",
    )(*upper, *lower, *ties)


def quarters_kernel(pieces, *refs):
    out = refs[-1]
    rows = LANES // 8
    for j in range(2):
        at = slice(j * rows, (j + 1) * rows)
        total = functools.reduce(jnp.add, [pieces[i, at].astype(F32) for i in range(4)]).astype(BF16)
        for i in range(4):
            out[i, at] = total


def add_quarters(pieces, ties):
    return pl.pallas_call(
        quarters_kernel,
        out_shape=pltpu.VMEM(pieces.shape, BF16),
        in_specs=[VMEM] + [FREE] * len(ties),
        out_specs=VMEM,
        compiler_params=PARAMS,
        cost_estimate=LITTLE,
        name="add_quarters",
    )(pieces, *ties)


def wgrad_kernel(layer, pos, d, hb_hbm, *refs):
    keep, send, hb, grad, sem = refs[-5:]
    load = pltpu.make_async_copy(hb_hbm.at[layer], hb, sem)
    load.start()
    n_own = d.shape[0]
    lhs = d[...]
    load.wait()
    for i in range(3):
        part = lax.dot_general(
            lhs, hb[i * WIDE : i * WIDE + n_own, :], (((0,), (0,)), ((), ())), preferred_element_type=F32
        ).astype(BF16)
        for s in range(3):
            grad[:, (3 * i + s) * CHANS : (3 * i + s + 1) * CHANS] = part[s * LANES : (s + 1) * LANES]
    half = LANES // 2
    keep[...] = grad[pl.ds(pl.multiple_of(pos[1] * half, half), half), :]
    send[...] = grad[pl.ds(pl.multiple_of((1 - pos[1]) * half, half), half), :]


def wgrad_step(layer, pos, d, kept, ties):
    half = pltpu.VMEM((LANES // 2, 9 * CHANS), BF16)
    return pl.pallas_call(
        functools.partial(wgrad_kernel, layer),
        out_shape=(half, half),
        in_specs=[SMEM, VMEM, ANY] + [FREE] * len(ties),
        out_specs=(VMEM, VMEM),
        scratch_shapes=[
            pltpu.VMEM(kept.shape[1:], BF16),
            pltpu.VMEM((LANES, 9 * CHANS), BF16),
            pltpu.SemaphoreType.DMA,
        ],
        compiler_params=PARAMS,
        cost_estimate=LITTLE,
        name="kernel_gradient",
    )(pos, d, in_hbm(kept), *ties)


def place_kernel(layers, fresh, pos, *refs):
    count = 2 * len(layers)
    sources = refs[:count]
    out, held, wide, sem = refs[-4:]
    half = LANES // 2
    r = pos[1]
    loads = [pltpu.make_async_copy(sources[j], held.at[j], sem.at[j]) for j in range(count)]
    for load in loads:
        load.start()
    stores = []
    for j in range(count):
        at = pl.multiple_of((r if j % 2 == 0 else 1 - r) * half, half)
        if j >= 2:
            stores[j - 2].wait()
        loads[j].wait()
        wide[j % 2] = held[j].astype(F32)
        store = pltpu.make_async_copy(wide.at[j % 2], out.at[layers[j // 2], pl.ds(at, half)], sem.at[count + j])
        store.start()
        stores.append(store)
    for store in stores[-2:]:
        store.wait()


def place_step(layers, pos, sources, whole, count):
    half = LANES // 2
    jobs = len(sources)
    return pl.pallas_call(
        functools.partial(place_kernel, layers, whole is None),
        out_shape=pltpu.HBM((count, LANES, 9 * CHANS), F32),
        in_specs=[SMEM] + [ANY] * jobs + ([] if whole is None else [ANY]),
        out_specs=ANY,
        input_output_aliases={} if whole is None else {1 + jobs: 0},
        scratch_shapes=[
            pltpu.VMEM((jobs, half, 9 * CHANS), BF16),
            pltpu.VMEM((2, half, 9 * CHANS), F32),
            pltpu.SemaphoreType.DMA((2 * jobs,)),
        ],
        compiler_params=PARAMS,
        cost_estimate=LITTLE,
        name="place_gradients",
    )(pos, *[in_hbm(v) for v in sources], *(() if whole is None else (in_hbm(whole),)))


def unbundle_kernel(pos, mine, other, whole, out, held, wide, sem):
    rows, half = LANES // 8, LANES // 2
    r = pos[1]
    loads = [pltpu.make_async_copy(v, held.at[j], sem.at[j]) for j, v in enumerate((mine, other))]
    for load in loads:
        load.start()
    stores = []
    for j in range(2):
        loads[j].wait()
        base = (r if j == 0 else 1 - r) * half
        for layer in (1, 0):
            slot = 2 * j + layer
            for i in range(4):
                at = slice((1 - layer) * rows, (2 - layer) * rows)
                wide[slot, i * rows : (i + 1) * rows] = held[j, i, at].astype(F32)
            store = pltpu.make_async_copy(
                wide.at[slot], out.at[layer, pl.ds(pl.multiple_of(base, half), half)], sem.at[2 + slot]
            )
            store.start()
            stores.append(store)
    for store in stores:
        store.wait()


def unbundle_step(pos, mine, other, whole):
    half = LANES // 2
    return pl.pallas_call(
        unbundle_kernel,
        out_shape=pltpu.HBM(whole.shape, F32),
        in_specs=[SMEM, FREE, FREE, ANY],
        out_specs=ANY,
        input_output_aliases={3: 0},
        scratch_shapes=[
            pltpu.VMEM((2,) + mine.shape, BF16),
            pltpu.VMEM((4, half, 9 * CHANS), F32),
            pltpu.SemaphoreType.DMA((6,)),
        ],
        compiler_params=PARAMS,
        cost_estimate=LITTLE,
        name="unbundle_gradients",
    )(pos, mine, other, in_hbm(whole))


def swap_with(value, axis, k):
    return lax.ppermute(value, axis, [(i, i ^ k) for i in range(lax.axis_size(axis))])


def spread(own):
    return (own, *[swap_with(own, "tensor", k) for k in range(1, GROUPS)])


def share_moments(mine, count):
    other = swap_with(mine, "rows", 1)
    mean = 0.5 * (mine[0:1] + other[0:1])
    apart = mine[1:2] + other[1:2] + (0.5 * count) * jnp.square(other[0:1] - mine[0:1])
    own = jnp.concatenate([mean, apart], axis=0)
    all_four = [own] + [swap_with(own, "dp", k) for k in (1, 2, 3)]
    mean = 0.25 * functools.reduce(jnp.add, [v[0:1] for v in all_four])
    apart = functools.reduce(jnp.add, [v[1:2] + (2.0 * count) * jnp.square(v[0:1] - mean) for v in all_four])
    return jnp.concatenate([mean, apart, mine[0:1], other[0:1]], axis=0).reshape(2, 1, 2, LANES)


def halo_of_input(x, half):
    n_own = x.shape[0]
    edge = jnp.where(half == 0, x[n_own - WIDE :], x[:WIDE])
    return jnp.concatenate([x, swap_with(edge, "rows", 1)], axis=0)


def fast_local(section_input, conv_weights, norm_gains, norm_shifts, out_grad, out_mask):
    images, rows_here, width = out_mask.shape
    layers = conv_weights.shape[0]
    n_own = rows_here * width
    parts = lax.axis_size("dp") * lax.axis_size("rows")
    total = float(n_own * parts)
    t, half = lax.axis_index("tensor"), lax.axis_index("rows")
    image = lax.axis_index("dp")
    pos = jnp.stack([t, half, 2 * image + half, 2 * image + 1 - half]).astype(jnp.int32)
    middle = layers // 2
    x = to_maps(section_input, width).reshape(n_own, LANES)
    slots = lax.all_gather(halo_of_input(x, half), "tensor", axis=1, tiled=True)
    pad = jnp.zeros((8 - layers, LANES), F32)
    tables = spread(jnp.concatenate([norm_gains, pad, norm_shifts, pad], axis=0))
    top_grad = (to_maps(out_grad, width) * out_mask[..., None].astype(BF16)).reshape(n_own, LANES)

    st, kept = None, None
    halves = ("dp", "rows")
    kept_z, kept_st = [], []
    for layer in range(layers):
        last = layer + 1 == layers
        edge = 2 * WIDE if layer + 1 == middle else WIDE
        everyone = ("dp", "rows", "tensor")
        devices = 1 if last else parts * GROUPS
        kept, zc, rim, local = fwd_step(
            layer,
            layer == middle,
            edge,
            total,
            pos,
            slots,
            st,
            tables,
            conv_weights,
            kept,
            n_own,
            devices,
            (top_grad,) if layer == 2 else (),
        )
        rim = swap_with(rim, "rows", 1)
        if last:
            st = share_moments(local[0], float(n_own))
        else:
            st = lax.all_to_all(local, everyone, split_axis=0, concat_axis=0, tiled=True)
            st = st.reshape(parts, GROUPS, 2, LANES)
        zc = lax.dynamic_update_slice_in_dim(zc, rim, n_own, axis=0)
        kept_z.append(zc)
        kept_st.append(st)
        if not last:
            slots = lax.all_gather(zc, "tensor", axis=1, tiled=True)
    top = layers - 1
    h_last, dn, msg = below_step(top, False, total, pos, kept_z[top], kept_st[top], tables[0], (top_grad,))

    def with_other(values):
        return [v for mine in values for v in (mine, swap_with(mine, "rows", 1))]

    sum_list, pairs = [None] * layers, [None] * layers
    ahead, back = [[0, 1, 3, 2]], [[2, 3, 1, 0]]
    urgent, split = (), [None] * layers
    for layer in range(layers - 1, -1, -1):
        got = swap_with(msg, "rows", 1)
        sums = msg[WIDE:] + got[WIDE:]
        one, two, three = (swap_with(sums, "dp", k) for k in (1, 2, 3))
        sums = (sums + one) + (two + three)
        sum_list[layer] = sums
        *terms, d = bwd_step(
            layer, total, pos, dn, got, sums, kept_z[layer], kept_st[layer], tables[0], conv_weights, urgent
        )
        terms = (terms[0], *[swap_with(terms[k], "tensor", k) for k in range(1, GROUPS)])
        keep, send = wgrad_step(layer, pos, d, kept, ())
        other = swap_with(send, "rows", 1)
        split[layer] = (keep, other)
        if layer > 1:
            pairs[layer] = add_halves(keep, other)
        urgent, settled = (other,), (() if layer in (0, layers - 1) else (pairs[layer + 1],))
        if layer == 4:
            upper = lax.psum((pairs[5], pairs[4]), "dp", axis_index_groups=ahead)
        if layer == 2:
            mid = lax.psum((pairs[3], pairs[2]), "dp", axis_index_groups=back)
        if layer > 0:
            below = layer - 1
            late = (in_hbm(upper[0]),) if layer == 1 else ()
            dn, msg = below_step(
                below, layer == middle, total, pos, kept_z[below], kept_st[below], tables[0], terms, (keep, *settled, *late)
            )
        else:
            grad = last_step(terms, (keep,))
    shape = (images, rows_here, width, LANES)
    bundle = bundle_halves(split[1], split[0], (in_hbm(grad),))
    bundle = lax.all_to_all(bundle, "dp", split_axis=0, concat_axis=0, tiled=True)
    grad, mid = lax.optimization_barrier((grad, mid))
    outputs = (from_maps(h_last.reshape(shape)), from_maps(grad.reshape(shape)))
    bundle = add_quarters(bundle, tuple(in_hbm(v) for v in outputs))
    bundle = lax.all_to_all(bundle, "dp", split_axis=0, concat_axis=0, tiled=True)
    whole = place_step((5, 4, 3, 2), pos, with_other((*upper, *mid)), None, layers)
    sums = jnp.stack(sum_list)
    sums = (sums[:, 1], sums[:, 0])
    bundle, whole, outputs, sums = lax.optimization_barrier((bundle, whole, outputs, sums))
    whole = unbundle_step(pos, bundle, swap_with(bundle, "rows", 1), whole)
    return (*outputs, whole, *sums)


def solution(mesh):
    in_specs = (
        P("dp", "rows", "tensor"),
        P(None, "tensor", None),
        P(None, "tensor"),
        P(None, "tensor"),
        P("dp", "rows", "tensor"),
        P("dp", "rows", None),
    )
    out_specs = (
        P("dp", "rows", "tensor"),
        P("dp", "rows", "tensor"),
        P(None, "tensor", None),
        P(None, "tensor"),
        P(None, "tensor"),
    )
    local = fast_local if fits_kernels(mesh) else generic_local
    return jax.shard_map(local, mesh=mesh, in_specs=in_specs, out_specs=out_specs, check_vma=False)
```

```python
import functools

import jax
import jax.numpy as jnp
from jax import lax
from jax.experimental import pallas as pl
from jax.experimental.pallas import tpu as pltpu
from jax.sharding import PartitionSpec as P

EPS = 1e-05


def padded_2(cells, sides, width):
    for axis, dim in sides:
        count = lax.axis_size(axis)
        ends = count - 1
        head = lax.slice_in_dim(cells, 0, width, axis=dim)
        tail = lax.slice_in_dim(cells, cells.shape[dim] - width, cells.shape[dim], axis=dim)
        cells = jnp.concatenate(
            [
                lax.ppermute(tail, axis, [(i, (i + 1) % count) for i in range(ends)]),
                cells,
                lax.ppermute(head, axis, [((i + 1) % count, i) for i in range(ends)]),
            ],
            axis=dim,
        )
    return cells


def to_maps(flat, width):
    count, high, merged = flat.shape
    return flat.reshape(count, high, merged // width, width).transpose(0, 1, 3, 2)


def from_maps(maps):
    count, high, wide, chans = maps.shape
    return maps.transpose(0, 1, 3, 2).reshape(count, high, chans * wide)


def spatial_conv(padded, kernel):
    return lax.conv_general_dilated(
        padded,
        kernel,
        (1, 1),
        ((0, 0), (1, 1)),
        dimension_numbers=("NHWC", "HWIO", "NHWC"),
        preferred_element_type=jnp.float32,
    )


def flipped(kernel):
    return jnp.transpose(kernel[::-1, ::-1], (0, 1, 3, 2))


def pool_unpool(values):
    count, high, wide, chans = values.shape
    blocks = values.reshape(count, high // 2, 2, wide // 2, 2, chans)
    pooled = jax.nn.logsumexp(blocks, axis=(2, 4), keepdims=True)
    return (jnp.exp(blocks - pooled) * pooled).reshape(values.shape)


def moments(conv_out, total_pixels):
    summed = lax.psum(jnp.sum(conv_out, axis=(0, 1, 2)), ("dp", "rows"))
    mean = summed / total_pixels
    spread = lax.psum(jnp.sum(jnp.square(conv_out - mean), axis=(0, 1, 2)), ("dp", "rows"))
    var = spread / total_pixels
    return (mean, lax.rsqrt(var + EPS))


def kernel_grad(whole, dconv):
    images, rows_here, width, chans = dconv.shape
    widened = jnp.pad(whole, ((0, 0), (0, 0), (1, 1), (0, 0)))
    stacked = []
    for row_off in range(3):
        line = []
        for col_off in range(3):
            window = widened[:, row_off : row_off + rows_here, col_off : col_off + width, :]
            line.append(
                jnp.einsum("bhwc,bhwo->co", window, dconv, preferred_element_type=jnp.float32)
            )
        stacked.append(jnp.stack(line))
    return jnp.stack(stacked)


def generic_local(section_input, conv_weights, norm_gains, norm_shifts, out_grad, out_mask):
    width = out_mask.shape[2]
    images, rows_here = (out_mask.shape[0], out_mask.shape[1])
    total_pixels = float(images * rows_here * width * lax.axis_size("dp") * lax.axis_size("rows"))
    layers, out_here, flat_in = conv_weights.shape
    chans_in = flat_in // 9
    kernels_hwio = conv_weights.reshape(layers, out_here, 3, 3, chans_in).transpose(0, 2, 3, 4, 1)
    middle = layers // 2
    kept = []
    acting = to_maps(section_input, width)
    current = acting.astype(jnp.float32)
    pre_pool = current
    for index in range(layers):
        if index == middle:
            pre_pool = current
            acting = pool_unpool(pre_pool).astype(jnp.bfloat16)
        padded = padded_2(acting, (("rows", 1),), 1)
        whole = lax.all_gather(padded, "tensor", axis=3, tiled=True)
        conv_out = spatial_conv(whole, kernels_hwio[index])
        mean, rstd = moments(conv_out, total_pixels)
        normed = (conv_out - mean) * rstd
        shifted = normed * norm_gains[index] + norm_shifts[index]
        current = jax.nn.silu(shifted)
        acting = current.astype(jnp.bfloat16)
        kept.append((whole, normed, shifted, rstd))
    grad = to_maps(out_grad, width).astype(jnp.float32) * out_mask[..., None].astype(jnp.float32)
    kernel_list = [None] * layers
    gain_list = [None] * layers
    shift_list = [None] * layers
    for index in range(layers - 1, -1, -1):
        whole, normed, shifted, rstd = kept[index]
        unused, pull_silu = jax.vjp(jax.nn.silu, shifted)
        dshift = pull_silu(grad)[0]
        gain_sum, shift_sum = lax.psum(
            (jnp.sum(dshift * normed, axis=(0, 1, 2)), jnp.sum(dshift, axis=(0, 1, 2))),
            ("dp", "rows"),
        )
        gain_list[index] = gain_sum
        shift_list[index] = shift_sum
        dconv = (
            norm_gains[index]
            * rstd
            * (dshift - shift_sum / total_pixels - normed * gain_sum / total_pixels)
        ).astype(jnp.bfloat16)
        summed_kernel = lax.psum(
            kernel_grad(whole, dconv).astype(jnp.bfloat16), ("dp", "rows")
        ).astype(jnp.float32)
        kernel_list[index] = summed_kernel.transpose(3, 0, 1, 2).reshape(out_here, flat_in)
        grad_rim = padded_2(dconv, (("rows", 1),), 1)
        partial_terms = spatial_conv(grad_rim, flipped(kernels_hwio[index]))
        grad_in = lax.psum_scatter(
            partial_terms.astype(jnp.bfloat16), "tensor", scatter_dimension=3, tiled=True
        ).astype(jnp.float32)
        if index == middle:
            unused, pull_pool = jax.vjp(pool_unpool, pre_pool)
            grad = pull_pool(grad_in)[0]
        else:
            grad = grad_in
    return (
        from_maps(acting),
        from_maps(grad),
        jnp.stack(kernel_list),
        jnp.stack(gain_list),
        jnp.stack(shift_list),
    )


GROUPS = 4
LANES = 128
WIDE = 48
CHANS = GROUPS * LANES
F32 = jnp.float32
BF16 = jnp.bfloat16
VMEM = pl.BlockSpec(memory_space=pltpu.VMEM)
SMEM = pl.BlockSpec(memory_space=pltpu.SMEM)
ANY = pl.BlockSpec(memory_space=pltpu.HBM)
FREE = pl.BlockSpec(memory_space=pl.ANY)
LITTLE = pl.CostEstimate(flops=1024, bytes_accessed=1024, transcendentals=0)
PARAMS = pltpu.CompilerParams(vmem_limit_bytes=20 * 1024 * 1024)


def in_hbm(value):
    return pltpu.with_memory_space_constraint(value, pltpu.HBM)


def fits_kernels(mesh):
    return mesh.shape["tensor"] == GROUPS and mesh.shape["rows"] == 2 and mesh.shape["dp"] == 4


def sigmoid(v):
    return 0.5 * jnp.tanh(0.5 * v) + 0.5


def swap_columns(v):
    column = lax.broadcasted_iota(jnp.int32, v.shape, 0)
    return jnp.where(column % 2 == 0, pltpu.roll(v, WIDE - 1, 0), pltpu.roll(v, 1, 0))


def soft_parts(h):
    top = jnp.maximum(h[0], h[1])
    top = jnp.maximum(top, swap_columns(top))
    e0, e1 = jnp.exp(h[0] - top), jnp.exp(h[1] - top)
    total = e0 + e1
    total = total + swap_columns(total)
    pooled = top + jnp.log(total)
    inverse = 1.0 / total
    return e0 * inverse, e1 * inverse, pooled


def soft(h):
    h = h.reshape(2, WIDE, LANES)
    q0, q1, pooled = soft_parts(h)
    return jnp.concatenate([q0 * pooled, q1 * pooled], axis=0)


def soft_pull(h, grad):
    h = h.reshape(2, WIDE, LANES)
    grad = grad.reshape(2, WIDE, LANES)
    q0, q1, pooled = soft_parts(h)
    mix = q0 * grad[0] + q1 * grad[1]
    mix = mix + swap_columns(mix)
    return jnp.concatenate(
        [q0 * (pooled * (grad[0] - mix) + mix), q1 * (pooled * (grad[1] - mix) + mix)], axis=0
    )


def norm_tables(st, group, i_own, i_oth, n_local, total):
    parts = st.shape[0]
    if parts == 2:
        mean, rstd = st[0, 0, 0:1], lax.rsqrt(st[0, 0, 1:2] / total + EPS)
        return rstd, (st[1, 0, 0:1] - mean) * rstd, (st[1, 0, 1:2] - mean) * rstd
    group = 0 if st.shape[1] == 1 else group
    blocks = [st[i, group] for i in range(parts)]
    summed = functools.reduce(jnp.add, blocks)
    mean = summed[0:1] / parts
    apart = functools.reduce(jnp.add, [jnp.square(b - mean) for b in blocks])
    rstd = lax.rsqrt((summed[1:2] + n_local * apart[0:1]) / total + EPS)
    return rstd, (st[i_own, group, 0:1] - mean) * rstd, (st[i_oth, group, 0:1] - mean) * rstd


def left_right(y0, y1, y2):
    rows = y0.shape[0]
    column = lax.broadcasted_iota(jnp.int32, y0.shape, 0) % WIDE
    before = jnp.where(column == 0, 0.0, pltpu.roll(y0, 1, 0))
    after = jnp.where(column == WIDE - 1, 0.0, pltpu.roll(y2, rows - 1, 0))
    return before + y1 + after


def lane_of(group):
    return pl.multiple_of(group * LANES, LANES)


def edge_start(n_own, edge, half):
    return pl.multiple_of((1 - half) * (n_own - edge), WIDE)


def pair_rows(j):
    return pl.ds(pl.multiple_of(j * 2 * WIDE, 2 * WIDE), 2 * WIDE)


def fold(v):
    return jnp.sum(v.reshape(v.shape[0] // 8, 8, LANES), axis=0)


def fwd_kernel(first, pool, layer, total, edge_out, *refs):
    pos, zall = refs[0], refs[1]
    if first:
        w_hbm = refs[2]
    else:
        st, gss, w_hbm = refs[2], refs[3:7], refs[7]
    hb_out, zc_out, edge_ref, st_out, hb, w, y, z, tab, hs, sem = refs[-11:]
    load = pltpu.make_async_copy(w_hbm.at[layer], w, sem.at[0])
    load.start()
    saves = []
    t, r = pos[0], pos[1]
    n_own = z.shape[0]
    halo_at = pl.multiple_of((1 - r) * (n_own + WIDE), WIDE)
    zero_at = pl.multiple_of(r * (n_own + WIDE), WIDE)
    hb[pl.ds(zero_at, WIDE), :] = jnp.zeros((WIDE, CHANS), BF16)
    edge = zall.shape[0] - n_own
    if not first:
        for k in range(GROUPS):
            group = t ^ k
            rstd, own, oth = norm_tables(st, group, pos[2], pos[3], float(n_own), total)
            gain, shift = gss[k][layer - 1 : layer, :], gss[k][layer + 7 : layer + 8, :]
            tab[group, 0:1] = rstd * gain
            tab[group, 1:2] = own * gain + shift
            tab[group, 2:3] = oth * gain + shift

    def act(values, group, which):
        if first:
            return values
        n = values.astype(F32) * tab[group, 0:1, :] + tab[group, which : which + 1, :]
        h = n * sigmoid(n)
        return soft(h) if pool else h

    for group in range(GROUPS):
        lanes = slice(group * LANES, (group + 1) * LANES)
        h = act(zall[n_own : n_own + edge, lanes], group, 2)
        if edge > WIDE:
            hs[...] = h
            h = hs[pl.ds(pl.multiple_of(r * WIDE, WIDE), WIDE), :]
        hb[pl.ds(halo_at, WIDE), lanes] = h.astype(BF16)
    pair, block = 2 * WIDE, n_own // 3
    steps, made = n_own // pair, 0
    summed = jnp.zeros((8, LANES), F32)
    for part in range(3):
        first_row = part * block
        while made < min(steps, (first_row + block + WIDE + pair - 1) // pair):
            at = made * pair
            for group in range(GROUPS):
                lanes = slice(group * LANES, (group + 1) * LANES)
                h = act(zall[at : at + pair, lanes], group, 1)
                hb[at + WIDE : at + WIDE + pair, lanes] = h.astype(BF16)
            made += 1
        if part == 0:
            load.wait()
            rhs = jnp.concatenate(
                [
                    jnp.concatenate([w[:, (3 * i + s) * CHANS : (3 * i + s + 1) * CHANS] for i in range(3)], axis=1)
                    for s in range(3)
                ],
                axis=0,
            )
        start, stop = (0 if part == 0 else first_row + 2 * WIDE), first_row + block + 2 * WIDE
        saves.append(
            pltpu.make_async_copy(hb.at[start:stop], hb_out.at[layer, start:stop], sem.at[1 + part])
        )
        saves[-1].start()
        lhs = jnp.concatenate([hb[first_row + i * WIDE : first_row + i * WIDE + block, :] for i in range(3)], axis=1)
        rows = slice(first_row, first_row + block)
        y[rows, :] = lax.dot_general(lhs, rhs, (((1,), (1,)), ((), ())), preferred_element_type=F32)
        for j in range(block // pair):
            rows = slice(first_row + j * pair, first_row + (j + 1) * pair)
            v = left_right(y[rows, 0:128], y[rows, 128:256], y[rows, 256:384])
            z[rows, :] = v
            summed = summed + fold(v)
    mean = jnp.sum(summed, axis=0, keepdims=True) / n_own
    apart = jnp.zeros((8, LANES), F32)
    for j in range(steps):
        rows = slice(j * pair, (j + 1) * pair)
        v = z[rows, :] - mean
        zc_out[rows, :] = v.astype(BF16)
        apart = apart + fold(jnp.square(v))
    sums = jnp.concatenate([mean, jnp.sum(apart, axis=0, keepdims=True)], axis=0)
    for i in range(st_out.shape[0]):
        st_out[i] = sums
    edge_ref[...] = zc_out[pl.ds(edge_start(n_own, edge_out, r), edge_out), :]
    zc_out[n_own : n_own + edge_out, :] = jnp.zeros((edge_out, LANES), BF16)
    for save in saves:
        save.wait()


def fwd_step(layer, pool, edge_out, total, pos, slots, st, tables, weights, kept, n_own, devices, ties):
    first = st is None
    layers = weights.shape[0]
    extra = () if first else (st, *tables)
    return pl.pallas_call(
        functools.partial(fwd_kernel, first, pool, layer, total, edge_out),
        out_shape=(
            pltpu.HBM((layers, n_own + 2 * WIDE, CHANS), BF16),
            pltpu.VMEM((n_own + edge_out, LANES), BF16),
            pltpu.VMEM((edge_out, LANES), BF16),
            pltpu.VMEM((devices, 2, LANES), F32),
        ),
        in_specs=[SMEM] + [VMEM] * (1 + len(extra)) + [ANY] * (1 if first else 2) + [FREE] * len(ties),
        out_specs=(ANY, VMEM, VMEM, VMEM),
        input_output_aliases={} if first else {3 + len(extra): 0},
        scratch_shapes=[
            pltpu.VMEM((n_own + 2 * WIDE, CHANS), BF16),
            pltpu.VMEM((LANES, 9 * CHANS), BF16),
            pltpu.VMEM((n_own, 3 * LANES), F32),
            pltpu.VMEM((n_own, LANES), F32),
            pltpu.VMEM((GROUPS, 8, LANES), F32),
            pltpu.VMEM((2 * WIDE, LANES), F32),
            pltpu.SemaphoreType.DMA((4,)),
        ],
        compiler_params=PARAMS,
        cost_estimate=pl.CostEstimate(
            flops=2 * n_own * 9 * CHANS * LANES, bytes_accessed=4 * 1024 * 1024, transcendentals=n_own * CHANS
        ),
        name="conv_forward",
    )(pos, slots, *extra, in_hbm(weights), *(() if first else (in_hbm(kept),)), *ties)


def below_kernel(layer, pool, total, top, *refs):
    pos, zc, st, gs = refs[:4]
    if top:
        terms, h_out, dn_out, msg, tab = refs[4:]
    else:
        terms, (dn_out, msg, tab) = refs[4:8], refs[-3:]
    n_own = dn_out.shape[0]
    rstd, own, oth = norm_tables(st, pos[0], pos[2], pos[3], float(n_own), total)
    tab[0:1], tab[1:2] = rstd, own
    tab[2:3], tab[3:4] = gs[layer : layer + 1, :], gs[layer + 8 : layer + 9, :]

    def body(j, accs):
        rows = pair_rows(j)
        xhat = zc[rows, :].astype(F32) * tab[0:1, :] + tab[1:2, :]
        n = xhat * tab[2:3, :] + tab[3:4, :]
        sig = sigmoid(n)
        h = n * sig
        if top:
            g = terms[rows, :].astype(F32)
            h_out[rows, :] = h.astype(BF16)
        else:
            g = functools.reduce(jnp.add, [term[rows, :].astype(F32) for term in terms])
        if pool:
            g = soft_pull(h, g)
        dn = g * (sig * (1.0 + n - h))
        dn_out[rows, :] = dn
        return accs[0] + fold(dn), accs[1] + fold(dn * xhat)

    zero = jnp.zeros((8, LANES), F32)
    sums = lax.fori_loop(0, n_own // (2 * WIDE), body, (zero, zero), unroll=3)
    sums = [jnp.sum(v, axis=0, keepdims=True) for v in sums]
    msg[0:WIDE, :] = dn_out[pl.ds(edge_start(n_own, WIDE, pos[1]), WIDE), :]
    msg[WIDE : WIDE + 8, :] = jnp.concatenate(sums + [jnp.zeros((6, LANES), F32)], axis=0)


def below_step(layer, pool, total, pos, zc, st, gs, terms, ties=()):
    n_own = terms[0].shape[0]
    top = len(terms) == 1
    out_shape = [
        pltpu.VMEM((n_own, LANES), F32),
        pltpu.VMEM((WIDE + 8, LANES), F32),
    ]
    if top:
        out_shape = [jax.ShapeDtypeStruct((n_own, LANES), BF16)] + out_shape
    return pl.pallas_call(
        functools.partial(below_kernel, layer, pool, total, top),
        out_shape=tuple(out_shape),
        in_specs=[SMEM] + [VMEM] * (3 + len(terms)) + [FREE] * len(ties),
        out_specs=(VMEM,) * len(out_shape),
        scratch_shapes=[pltpu.VMEM((8, LANES), F32)],
        compiler_params=PARAMS,
        cost_estimate=LITTLE,
        name="silu_backward",
    )(pos, zc, st, gs, *terms, *ties)


def bwd_kernel(layer, total, *refs):
    pos, dn, dedge, sums, zc, st, gs, w_hbm = refs[:8]
    outs, d_out, d, w, y, tab, sem = refs[-10:-6], *refs[-6:]
    load = pltpu.make_async_copy(w_hbm.at[layer], w, sem)
    load.start()
    t, r = pos[0], pos[1]
    n_own = dn.shape[0]
    halo_at = pl.multiple_of((1 - r) * (n_own + WIDE), WIDE)
    zero_at = pl.multiple_of(r * (n_own + WIDE), WIDE)
    edge = zc.shape[0] - n_own
    d[pl.ds(zero_at, WIDE), :] = jnp.zeros((WIDE, 3 * LANES), BF16)
    rstd, own, oth = norm_tables(st, t, pos[2], pos[3], float(n_own), total)
    scale = gs[layer : layer + 1, :] * rstd
    shift_sum, gain_sum = sums[0:1, :], sums[1:2, :]
    slope = scale * gain_sum / total
    tab[0:1] = scale
    tab[1:2] = slope * rstd
    tab[2:3] = scale * shift_sum / total + slope * own
    tab[3:4] = scale * shift_sum / total + slope * oth

    def spread_columns(v):
        rows = v.shape[0]
        column = lax.broadcasted_iota(jnp.int32, v.shape, 0) % WIDE
        ahead = jnp.where(column == WIDE - 1, 0.0, pltpu.roll(v, rows - 1, 0))
        behind = jnp.where(column == 0, 0.0, pltpu.roll(v, 1, 0))
        return jnp.concatenate([ahead.astype(BF16), v.astype(BF16), behind.astype(BF16)], axis=1)

    near = n_own if edge == WIDE else pl.multiple_of(n_own + r * WIDE, WIDE)
    near = zc[pl.ds(near, WIDE), :].astype(F32)
    d[pl.ds(halo_at, WIDE), :] = spread_columns(dedge[0:WIDE, :] * tab[0:1, :] - tab[3:4, :] - near * tab[1:2, :])
    pair, block = 2 * WIDE, n_own // 3
    steps, made = n_own // pair, 0
    for part in range(3):
        first_row = part * block
        while made < min(steps, (first_row + block + WIDE + pair - 1) // pair):
            at = made * pair
            v = dn[at : at + pair, :] * tab[0:1, :] - tab[2:3, :] - zc[at : at + pair, :].astype(F32) * tab[1:2, :]
            v = spread_columns(v)
            d[at + WIDE : at + WIDE + pair, :] = v
            d_out[at : at + pair, :] = v
            made += 1
        if part == 0:
            load.wait()
            rhs = jnp.concatenate([w[:, i * CHANS : (i + 1) * CHANS] for i in range(9)], axis=0)
        windows = [first_row + (2 - i) * WIDE for i in range(3)]
        lhs = jnp.concatenate([d[at : at + block, :] for at in windows], axis=1)
        y[first_row : first_row + block, :] = jnp.dot(lhs, rhs, preferred_element_type=F32)
        for j in range(block // pair):
            rows = slice(first_row + j * pair, first_row + (j + 1) * pair)
            for k in range(GROUPS):
                outs[k][rows, :] = y[rows, pl.ds(lane_of(t ^ k), LANES)].astype(BF16)


def bwd_step(layer, total, pos, dn, dedge, sums, zc, st, gs, weights, ties):
    n_own = dn.shape[0]
    part = pltpu.VMEM((n_own, LANES), BF16)
    return pl.pallas_call(
        functools.partial(bwd_kernel, layer, total),
        out_shape=(
            part,
            part,
            part,
            part,
            pltpu.VMEM((n_own, 3 * LANES), BF16),
        ),
        in_specs=[SMEM] + [VMEM] * 6 + [ANY] + [FREE] * len(ties),
        out_specs=(VMEM,) * 5,
        scratch_shapes=[
            pltpu.VMEM((n_own + 2 * WIDE, 3 * LANES), BF16),
            pltpu.VMEM((LANES, 9 * CHANS), BF16),
            pltpu.VMEM((n_own, CHANS), F32),
            pltpu.VMEM((8, LANES), F32),
            pltpu.SemaphoreType.DMA,
        ],
        compiler_params=PARAMS,
        cost_estimate=LITTLE,
        name="conv_backward",
    )(pos, dn, dedge, sums, zc, st, gs, in_hbm(weights), *ties)


def last_kernel(t0, t1, t2, t3, *refs):
    out = refs[-1]

    def body(j, carry):
        rows = pair_rows(j)
        out[rows, :] = functools.reduce(jnp.add, [term[rows, :].astype(F32) for term in (t0, t1, t2, t3)])
        return carry

    lax.fori_loop(0, out.shape[0] // (2 * WIDE), body, 0)


def last_step(terms, ties):
    return pl.pallas_call(
        last_kernel,
        out_shape=jax.ShapeDtypeStruct(terms[0].shape, F32),
        in_specs=[VMEM] * 4 + [FREE] * len(ties),
        out_specs=VMEM,
        compiler_params=PARAMS,
        cost_estimate=LITTLE,
        name="add_terms",
    )(*terms, *ties)


def halves_kernel(keep, got, out):
    out[...] = (keep[...].astype(F32) + got[...].astype(F32)).astype(BF16)


def add_halves(keep, got):
    return pl.pallas_call(
        halves_kernel,
        out_shape=jax.ShapeDtypeStruct(keep.shape, BF16),
        in_specs=[VMEM] * 2,
        out_specs=VMEM,
        compiler_params=PARAMS,
        cost_estimate=LITTLE,
        name="add_halves",
    )(keep, got)


def quarters_kernel(parts, *refs):
    out = refs[-1]
    total = functools.reduce(jnp.add, [parts[i].astype(F32) for i in range(4)]).astype(BF16)
    for i in range(4):
        out[i] = total


def add_quarters(parts, ties):
    return pl.pallas_call(
        quarters_kernel,
        out_shape=pltpu.VMEM(parts.shape, BF16),
        in_specs=[VMEM] + [FREE] * len(ties),
        out_specs=VMEM,
        compiler_params=PARAMS,
        cost_estimate=pl.CostEstimate(flops=parts.size, bytes_accessed=4 * parts.size, transcendentals=0),
        name="add_quarters",
    )(parts, *ties)


def wgrad_kernel(layer, pos, d, hb_hbm, *refs):
    keep, send, hb, grad, sem = refs[-5:]
    load = pltpu.make_async_copy(hb_hbm.at[layer], hb, sem)
    load.start()
    n_own = d.shape[0]
    lhs = d[...]
    load.wait()
    for i in range(3):
        part = lax.dot_general(
            lhs, hb[i * WIDE : i * WIDE + n_own, :], (((0,), (0,)), ((), ())), preferred_element_type=F32
        ).astype(BF16)
        for s in range(3):
            grad[:, (3 * i + s) * CHANS : (3 * i + s + 1) * CHANS] = part[s * LANES : (s + 1) * LANES]
    half = LANES // 2
    keep[...] = grad[pl.ds(pl.multiple_of(pos[1] * half, half), half), :]
    send[...] = grad[pl.ds(pl.multiple_of((1 - pos[1]) * half, half), half), :]


def wgrad_step(layer, pos, d, kept, ties):
    half = pltpu.VMEM((LANES // 2, 9 * CHANS), BF16)
    return pl.pallas_call(
        functools.partial(wgrad_kernel, layer),
        out_shape=(half, half),
        in_specs=[SMEM, VMEM, ANY] + [FREE] * len(ties),
        out_specs=(VMEM, VMEM),
        scratch_shapes=[
            pltpu.VMEM(kept.shape[1:], BF16),
            pltpu.VMEM((LANES, 9 * CHANS), BF16),
            pltpu.SemaphoreType.DMA,
        ],
        compiler_params=PARAMS,
        cost_estimate=LITTLE,
        name="kernel_gradient",
    )(pos, d, in_hbm(kept), *ties)


def place_kernel(layers, fresh, pos, *refs):
    count = 2 * len(layers)
    sources = refs[:count]
    out, held, wide, sem = refs[-4:]
    half = LANES // 2
    r = pos[1]
    loads = [pltpu.make_async_copy(sources[j], held.at[j], sem.at[j]) for j in range(count)]
    for load in loads:
        load.start()
    stores = []
    for j in range(count):
        at = pl.multiple_of((r if j % 2 == 0 else 1 - r) * half, half)
        if j >= 4:
            stores[j - 4].wait()
        loads[j].wait()
        wide[j % 4] = held[j].astype(F32)
        store = pltpu.make_async_copy(wide.at[j % 4], out.at[layers[j // 2], pl.ds(at, half)], sem.at[count + j])
        store.start()
        stores.append(store)
    for store in stores[-4:]:
        store.wait()


def place_step(layers, pos, sources, whole, count):
    half = LANES // 2
    jobs = len(sources)
    return pl.pallas_call(
        functools.partial(place_kernel, layers, whole is None),
        out_shape=pltpu.HBM((count, LANES, 9 * CHANS), F32),
        in_specs=[SMEM] + [ANY] * jobs + ([] if whole is None else [ANY]),
        out_specs=ANY,
        input_output_aliases={} if whole is None else {1 + jobs: 0},
        scratch_shapes=[
            pltpu.VMEM((jobs, half, 9 * CHANS), BF16),
            pltpu.VMEM((4, half, 9 * CHANS), F32),
            pltpu.SemaphoreType.DMA((2 * jobs,)),
        ],
        compiler_params=PARAMS,
        cost_estimate=LITTLE,
        name="place_gradients",
    )(pos, *[in_hbm(v) for v in sources], *(() if whole is None else (in_hbm(whole),)))


def swap_with(value, axis, k):
    return lax.ppermute(value, axis, [(i, i ^ k) for i in range(lax.axis_size(axis))])


def spread(own):
    return (own, *[swap_with(own, "tensor", k) for k in range(1, GROUPS)])


def share_moments(mine, count):
    other = swap_with(mine, "rows", 1)
    mean = 0.5 * (mine[0:1] + other[0:1])
    apart = mine[1:2] + other[1:2] + (0.5 * count) * jnp.square(other[0:1] - mine[0:1])
    own = jnp.concatenate([mean, apart], axis=0)
    all_four = [own] + [swap_with(own, "dp", k) for k in (1, 2, 3)]
    mean = 0.25 * functools.reduce(jnp.add, [v[0:1] for v in all_four])
    apart = functools.reduce(jnp.add, [v[1:2] + (2.0 * count) * jnp.square(v[0:1] - mean) for v in all_four])
    return jnp.concatenate([mean, apart, mine[0:1], other[0:1]], axis=0).reshape(2, 1, 2, LANES)


def halo_of_input(x, half):
    n_own = x.shape[0]
    edge = jnp.where(half == 0, x[n_own - WIDE :], x[:WIDE])
    return jnp.concatenate([x, swap_with(edge, "rows", 1)], axis=0)


def fast_local(section_input, conv_weights, norm_gains, norm_shifts, out_grad, out_mask):
    images, rows_here, width = out_mask.shape
    layers = conv_weights.shape[0]
    n_own = rows_here * width
    parts = lax.axis_size("dp") * lax.axis_size("rows")
    total = float(n_own * parts)
    t, half = lax.axis_index("tensor"), lax.axis_index("rows")
    image = lax.axis_index("dp")
    pos = jnp.stack([t, half, 2 * image + half, 2 * image + 1 - half]).astype(jnp.int32)
    middle = layers // 2
    x = to_maps(section_input, width).reshape(n_own, LANES)
    slots = lax.all_gather(halo_of_input(x, half), "tensor", axis=1, tiled=True)
    pad = jnp.zeros((8 - layers, LANES), F32)
    tables = spread(jnp.concatenate([norm_gains, pad, norm_shifts, pad], axis=0))
    top_grad = (to_maps(out_grad, width) * out_mask[..., None].astype(BF16)).reshape(n_own, LANES)

    st, kept = None, None
    halves = ("dp", "rows")
    kept_z, kept_st = [], []
    for layer in range(layers):
        last = layer + 1 == layers
        edge = 2 * WIDE if layer + 1 == middle else WIDE
        everyone = ("dp", "rows", "tensor")
        devices = 1 if last else parts * GROUPS
        kept, zc, rim, local = fwd_step(
            layer,
            layer == middle,
            edge,
            total,
            pos,
            slots,
            st,
            tables,
            conv_weights,
            kept,
            n_own,
            devices,
            (top_grad,) if layer == 2 else (),
        )
        rim = swap_with(rim, "rows", 1)
        if last:
            st = share_moments(local[0], float(n_own))
        else:
            st = lax.all_to_all(local, everyone, split_axis=0, concat_axis=0, tiled=True)
            st = st.reshape(parts, GROUPS, 2, LANES)
        zc = lax.dynamic_update_slice_in_dim(zc, rim, n_own, axis=0)
        kept_z.append(zc)
        kept_st.append(st)
        if not last:
            slots = lax.all_gather(zc, "tensor", axis=1, tiled=True)
    top = layers - 1
    h_last, dn, msg = below_step(top, False, total, pos, kept_z[top], kept_st[top], tables[0], (top_grad,))

    def with_other(values):
        return [v for mine in values for v in (mine, swap_with(mine, "rows", 1))]

    sum_list, pairs = [None] * layers, [None] * layers
    ahead, back = [[0, 1, 3, 2]], [[2, 3, 1, 0]]
    urgent = ()
    for layer in range(layers - 1, -1, -1):
        got = swap_with(msg, "rows", 1)
        sums = msg[WIDE:] + got[WIDE:]
        one, two, three = (swap_with(sums, "dp", k) for k in (1, 2, 3))
        sums = (sums + one) + (two + three)
        sum_list[layer] = sums
        *terms, d = bwd_step(
            layer, total, pos, dn, got, sums, kept_z[layer], kept_st[layer], tables[0], conv_weights, urgent
        )
        terms = (terms[0], *[swap_with(terms[k], "tensor", k) for k in range(1, GROUPS)])
        keep, send = wgrad_step(layer, pos, d, kept, ())
        other = swap_with(send, "rows", 1)
        pairs[layer] = add_halves(keep, other)
        urgent, settled = (other,), (() if layer in (0, layers - 1) else (pairs[layer + 1],))
        if layer == 1:
            settled = (*settled, pairs[1])
        if layer == 4:
            upper = lax.psum((pairs[5], pairs[4]), "dp", axis_index_groups=ahead)
        if layer == 1:
            lower = lax.psum((pairs[3], pairs[2], pairs[1]), "dp", axis_index_groups=back)
        if layer > 0:
            below = layer - 1
            late = (in_hbm(upper[0]),) if layer == 1 else ()
            dn, msg = below_step(
                below, layer == middle, total, pos, kept_z[below], kept_st[below], tables[0], terms, (keep, *settled, *late)
            )
        else:
            grad = last_step(terms, (keep,))
    shape = (images, rows_here, width, LANES)
    outputs = (from_maps(h_last.reshape(shape)), from_maps(grad.reshape(shape)))
    pieces = pairs[0].reshape(4, LANES // 8, -1)
    pieces = lax.all_to_all(pieces, "dp", split_axis=0, concat_axis=0, tiled=True)
    pieces = add_quarters(pieces, (in_hbm(lower[0]), *[in_hbm(v) for v in outputs]))
    pieces = lax.all_to_all(pieces, "dp", split_axis=0, concat_axis=0, tiled=True)
    whole = place_step((5, 4, 3, 2, 1), pos, with_other((*upper, *lower)), None, layers)
    sums = jnp.stack(sum_list)
    sums = (sums[:, 1], sums[:, 0])
    pieces, whole, outputs, sums = lax.optimization_barrier((pieces, whole, outputs, sums))
    whole = place_step((0,), pos, with_other((pieces.reshape(pairs[0].shape),)), whole, layers)
    return (*outputs, whole, *sums)


def solution(mesh):
    in_specs = (
        P("dp", "rows", "tensor"),
        P(None, "tensor", None),
        P(None, "tensor"),
        P(None, "tensor"),
        P("dp", "rows", "tensor"),
        P("dp", "rows", None),
    )
    out_specs = (
        P("dp", "rows", "tensor"),
        P("dp", "rows", "tensor"),
        P(None, "tensor", None),
        P(None, "tensor"),
        P(None, "tensor"),
    )
    local = fast_local if fits_kernels(mesh) else generic_local
    return jax.shard_map(local, mesh=mesh, in_specs=in_specs, out_specs=out_specs, check_vma=False)
```

```python
import functools

import jax
import jax.numpy as jnp
from jax import lax
from jax.experimental import pallas as pl
from jax.experimental.pallas import tpu as pltpu
from jax.sharding import PartitionSpec as P

EPS = 1e-05


def padded_2(cells, sides, width):
    for axis, dim in sides:
        count = lax.axis_size(axis)
        ends = count - 1
        head = lax.slice_in_dim(cells, 0, width, axis=dim)
        tail = lax.slice_in_dim(cells, cells.shape[dim] - width, cells.shape[dim], axis=dim)
        cells = jnp.concatenate(
            [
                lax.ppermute(tail, axis, [(i, (i + 1) % count) for i in range(ends)]),
                cells,
                lax.ppermute(head, axis, [((i + 1) % count, i) for i in range(ends)]),
            ],
            axis=dim,
        )
    return cells


def to_maps(flat, width):
    count, high, merged = flat.shape
    return flat.reshape(count, high, merged // width, width).transpose(0, 1, 3, 2)


def from_maps(maps):
    count, high, wide, chans = maps.shape
    return maps.transpose(0, 1, 3, 2).reshape(count, high, chans * wide)


def spatial_conv(padded, kernel):
    return lax.conv_general_dilated(
        padded,
        kernel,
        (1, 1),
        ((0, 0), (1, 1)),
        dimension_numbers=("NHWC", "HWIO", "NHWC"),
        preferred_element_type=jnp.float32,
    )


def flipped(kernel):
    return jnp.transpose(kernel[::-1, ::-1], (0, 1, 3, 2))


def pool_unpool(values):
    count, high, wide, chans = values.shape
    blocks = values.reshape(count, high // 2, 2, wide // 2, 2, chans)
    pooled = jax.nn.logsumexp(blocks, axis=(2, 4), keepdims=True)
    return (jnp.exp(blocks - pooled) * pooled).reshape(values.shape)


def moments(conv_out, total_pixels):
    summed = lax.psum(jnp.sum(conv_out, axis=(0, 1, 2)), ("dp", "rows"))
    mean = summed / total_pixels
    spread = lax.psum(jnp.sum(jnp.square(conv_out - mean), axis=(0, 1, 2)), ("dp", "rows"))
    var = spread / total_pixels
    return (mean, lax.rsqrt(var + EPS))


def kernel_grad(whole, dconv):
    images, rows_here, width, chans = dconv.shape
    widened = jnp.pad(whole, ((0, 0), (0, 0), (1, 1), (0, 0)))
    stacked = []
    for row_off in range(3):
        line = []
        for col_off in range(3):
            window = widened[:, row_off : row_off + rows_here, col_off : col_off + width, :]
            line.append(
                jnp.einsum("bhwc,bhwo->co", window, dconv, preferred_element_type=jnp.float32)
            )
        stacked.append(jnp.stack(line))
    return jnp.stack(stacked)


def generic_local(section_input, conv_weights, norm_gains, norm_shifts, out_grad, out_mask):
    width = out_mask.shape[2]
    images, rows_here = (out_mask.shape[0], out_mask.shape[1])
    total_pixels = float(images * rows_here * width * lax.axis_size("dp") * lax.axis_size("rows"))
    layers, out_here, flat_in = conv_weights.shape
    chans_in = flat_in // 9
    kernels_hwio = conv_weights.reshape(layers, out_here, 3, 3, chans_in).transpose(0, 2, 3, 4, 1)
    middle = layers // 2
    kept = []
    acting = to_maps(section_input, width)
    current = acting.astype(jnp.float32)
    pre_pool = current
    for index in range(layers):
        if index == middle:
            pre_pool = current
            acting = pool_unpool(pre_pool).astype(jnp.bfloat16)
        padded = padded_2(acting, (("rows", 1),), 1)
        whole = lax.all_gather(padded, "tensor", axis=3, tiled=True)
        conv_out = spatial_conv(whole, kernels_hwio[index])
        mean, rstd = moments(conv_out, total_pixels)
        normed = (conv_out - mean) * rstd
        shifted = normed * norm_gains[index] + norm_shifts[index]
        current = jax.nn.silu(shifted)
        acting = current.astype(jnp.bfloat16)
        kept.append((whole, normed, shifted, rstd))
    grad = to_maps(out_grad, width).astype(jnp.float32) * out_mask[..., None].astype(jnp.float32)
    kernel_list = [None] * layers
    gain_list = [None] * layers
    shift_list = [None] * layers
    for index in range(layers - 1, -1, -1):
        whole, normed, shifted, rstd = kept[index]
        unused, pull_silu = jax.vjp(jax.nn.silu, shifted)
        dshift = pull_silu(grad)[0]
        gain_sum, shift_sum = lax.psum(
            (jnp.sum(dshift * normed, axis=(0, 1, 2)), jnp.sum(dshift, axis=(0, 1, 2))),
            ("dp", "rows"),
        )
        gain_list[index] = gain_sum
        shift_list[index] = shift_sum
        dconv = (
            norm_gains[index]
            * rstd
            * (dshift - shift_sum / total_pixels - normed * gain_sum / total_pixels)
        ).astype(jnp.bfloat16)
        summed_kernel = lax.psum(
            kernel_grad(whole, dconv).astype(jnp.bfloat16), ("dp", "rows")
        ).astype(jnp.float32)
        kernel_list[index] = summed_kernel.transpose(3, 0, 1, 2).reshape(out_here, flat_in)
        grad_rim = padded_2(dconv, (("rows", 1),), 1)
        partial_terms = spatial_conv(grad_rim, flipped(kernels_hwio[index]))
        grad_in = lax.psum_scatter(
            partial_terms.astype(jnp.bfloat16), "tensor", scatter_dimension=3, tiled=True
        ).astype(jnp.float32)
        if index == middle:
            unused, pull_pool = jax.vjp(pool_unpool, pre_pool)
            grad = pull_pool(grad_in)[0]
        else:
            grad = grad_in
    return (
        from_maps(acting),
        from_maps(grad),
        jnp.stack(kernel_list),
        jnp.stack(gain_list),
        jnp.stack(shift_list),
    )


GROUPS = 4
LANES = 128
WIDE = 48
CHANS = GROUPS * LANES
F32 = jnp.float32
BF16 = jnp.bfloat16
VMEM = pl.BlockSpec(memory_space=pltpu.VMEM)
SMEM = pl.BlockSpec(memory_space=pltpu.SMEM)
ANY = pl.BlockSpec(memory_space=pltpu.HBM)
FREE = pl.BlockSpec(memory_space=pl.ANY)
LITTLE = pl.CostEstimate(flops=1024, bytes_accessed=1024, transcendentals=0)
PARAMS = pltpu.CompilerParams(vmem_limit_bytes=20 * 1024 * 1024)


def in_hbm(value):
    return pltpu.with_memory_space_constraint(value, pltpu.HBM)


def fits_kernels(mesh):
    return mesh.shape["tensor"] == GROUPS and mesh.shape["rows"] == 2 and mesh.shape["dp"] == 4


def sigmoid(v):
    return 0.5 * jnp.tanh(0.5 * v) + 0.5


def swap_columns(v):
    column = lax.broadcasted_iota(jnp.int32, v.shape, 0)
    return jnp.where(column % 2 == 0, pltpu.roll(v, WIDE - 1, 0), pltpu.roll(v, 1, 0))


def soft_parts(h):
    top = jnp.maximum(h[0], h[1])
    top = jnp.maximum(top, swap_columns(top))
    e0, e1 = jnp.exp(h[0] - top), jnp.exp(h[1] - top)
    total = e0 + e1
    total = total + swap_columns(total)
    pooled = top + jnp.log(total)
    inverse = 1.0 / total
    return e0 * inverse, e1 * inverse, pooled


def soft(h):
    h = h.reshape(2, WIDE, LANES)
    q0, q1, pooled = soft_parts(h)
    return jnp.concatenate([q0 * pooled, q1 * pooled], axis=0)


def soft_pull(h, grad):
    h = h.reshape(2, WIDE, LANES)
    grad = grad.reshape(2, WIDE, LANES)
    q0, q1, pooled = soft_parts(h)
    mix = q0 * grad[0] + q1 * grad[1]
    mix = mix + swap_columns(mix)
    return jnp.concatenate(
        [q0 * (pooled * (grad[0] - mix) + mix), q1 * (pooled * (grad[1] - mix) + mix)], axis=0
    )


def norm_tables(st, group, i_own, i_oth, n_local, total):
    parts = st.shape[0]
    if parts == 2:
        mean, rstd = st[0, 0, 0:1], lax.rsqrt(st[0, 0, 1:2] / total + EPS)
        return rstd, (st[1, 0, 0:1] - mean) * rstd, (st[1, 0, 1:2] - mean) * rstd
    group = 0 if st.shape[1] == 1 else group
    blocks = [st[i, group] for i in range(parts)]
    summed = functools.reduce(jnp.add, blocks)
    mean = summed[0:1] / parts
    apart = functools.reduce(jnp.add, [jnp.square(b - mean) for b in blocks])
    rstd = lax.rsqrt((summed[1:2] + n_local * apart[0:1]) / total + EPS)
    return rstd, (st[i_own, group, 0:1] - mean) * rstd, (st[i_oth, group, 0:1] - mean) * rstd


def left_right(y0, y1, y2):
    rows = y0.shape[0]
    column = lax.broadcasted_iota(jnp.int32, y0.shape, 0) % WIDE
    before = jnp.where(column == 0, 0.0, pltpu.roll(y0, 1, 0))
    after = jnp.where(column == WIDE - 1, 0.0, pltpu.roll(y2, rows - 1, 0))
    return before + y1 + after


def lane_of(group):
    return pl.multiple_of(group * LANES, LANES)


def edge_start(n_own, edge, half):
    return pl.multiple_of((1 - half) * (n_own - edge), WIDE)


def pair_rows(j):
    return pl.ds(pl.multiple_of(j * 2 * WIDE, 2 * WIDE), 2 * WIDE)


def fold(v):
    return jnp.sum(v.reshape(v.shape[0] // 8, 8, LANES), axis=0)


def fwd_kernel(first, pool, layer, total, edge_out, *refs):
    pos, zall = refs[0], refs[1]
    if first:
        w_hbm = refs[2]
    else:
        st, gss, w_hbm = refs[2], refs[3:7], refs[7]
    hb_out, zc_out, edge_ref, st_out, hb, w, y, z, tab, hs, sem = refs[-11:]
    load = pltpu.make_async_copy(w_hbm.at[layer], w, sem.at[0])
    load.start()
    saves = []
    t, r = pos[0], pos[1]
    n_own = z.shape[0]
    halo_at = pl.multiple_of((1 - r) * (n_own + WIDE), WIDE)
    zero_at = pl.multiple_of(r * (n_own + WIDE), WIDE)
    hb[pl.ds(zero_at, WIDE), :] = jnp.zeros((WIDE, CHANS), BF16)
    edge = zall.shape[0] - n_own
    if not first:
        for k in range(GROUPS):
            group = t ^ k
            rstd, own, oth = norm_tables(st, group, pos[2], pos[3], float(n_own), total)
            gain, shift = gss[k][layer - 1 : layer, :], gss[k][layer + 7 : layer + 8, :]
            tab[group, 0:1] = rstd * gain
            tab[group, 1:2] = own * gain + shift
            tab[group, 2:3] = oth * gain + shift

    def act(values, group, which):
        if first:
            return values
        n = values.astype(F32) * tab[group, 0:1, :] + tab[group, which : which + 1, :]
        h = n * sigmoid(n)
        return soft(h) if pool else h

    for group in range(GROUPS):
        lanes = slice(group * LANES, (group + 1) * LANES)
        h = act(zall[n_own : n_own + edge, lanes], group, 2)
        if edge > WIDE:
            hs[...] = h
            h = hs[pl.ds(pl.multiple_of(r * WIDE, WIDE), WIDE), :]
        hb[pl.ds(halo_at, WIDE), lanes] = h.astype(BF16)
    pair, block = 2 * WIDE, n_own // 3
    steps, made = n_own // pair, 0
    summed = jnp.zeros((8, LANES), F32)
    for part in range(3):
        first_row = part * block
        while made < min(steps, (first_row + block + WIDE + pair - 1) // pair):
            at = made * pair
            for group in range(GROUPS):
                lanes = slice(group * LANES, (group + 1) * LANES)
                h = act(zall[at : at + pair, lanes], group, 1)
                hb[at + WIDE : at + WIDE + pair, lanes] = h.astype(BF16)
            made += 1
        if part == 0:
            load.wait()
            rhs = jnp.concatenate(
                [
                    jnp.concatenate([w[:, (3 * i + s) * CHANS : (3 * i + s + 1) * CHANS] for i in range(3)], axis=1)
                    for s in range(3)
                ],
                axis=0,
            )
        start, stop = (0 if part == 0 else first_row + 2 * WIDE), first_row + block + 2 * WIDE
        saves.append(
            pltpu.make_async_copy(hb.at[start:stop], hb_out.at[layer, start:stop], sem.at[1 + part])
        )
        saves[-1].start()
        lhs = jnp.concatenate([hb[first_row + i * WIDE : first_row + i * WIDE + block, :] for i in range(3)], axis=1)
        rows = slice(first_row, first_row + block)
        y[rows, :] = lax.dot_general(lhs, rhs, (((1,), (1,)), ((), ())), preferred_element_type=F32)
        for j in range(block // pair):
            rows = slice(first_row + j * pair, first_row + (j + 1) * pair)
            v = left_right(y[rows, 0:128], y[rows, 128:256], y[rows, 256:384])
            z[rows, :] = v
            summed = summed + fold(v)
    mean = jnp.sum(summed, axis=0, keepdims=True) / n_own
    apart = jnp.zeros((8, LANES), F32)
    for j in range(steps):
        rows = slice(j * pair, (j + 1) * pair)
        v = z[rows, :] - mean
        zc_out[rows, :] = v.astype(BF16)
        apart = apart + fold(jnp.square(v))
    sums = jnp.concatenate([mean, jnp.sum(apart, axis=0, keepdims=True)], axis=0)
    st_out[...] = sums
    edge_ref[...] = zc_out[pl.ds(edge_start(n_own, edge_out, r), edge_out), :]
    zc_out[n_own : n_own + edge_out, :] = jnp.zeros((edge_out, LANES), BF16)
    for save in saves:
        save.wait()


def fwd_step(layer, pool, edge_out, total, pos, slots, st, tables, weights, kept, n_own, ties):
    first = st is None
    layers = weights.shape[0]
    extra = () if first else (st, *tables)
    return pl.pallas_call(
        functools.partial(fwd_kernel, first, pool, layer, total, edge_out),
        out_shape=(
            pltpu.HBM((layers, n_own + 2 * WIDE, CHANS), BF16),
            pltpu.VMEM((n_own + edge_out, LANES), BF16),
            pltpu.VMEM((edge_out, LANES), BF16),
            pltpu.VMEM((2, LANES), F32),
        ),
        in_specs=[SMEM] + [VMEM] * (1 + len(extra)) + [ANY] * (1 if first else 2) + [FREE] * len(ties),
        out_specs=(ANY, VMEM, VMEM, VMEM),
        input_output_aliases={} if first else {3 + len(extra): 0},
        scratch_shapes=[
            pltpu.VMEM((n_own + 2 * WIDE, CHANS), BF16),
            pltpu.VMEM((LANES, 9 * CHANS), BF16),
            pltpu.VMEM((n_own, 3 * LANES), F32),
            pltpu.VMEM((n_own, LANES), F32),
            pltpu.VMEM((GROUPS, 8, LANES), F32),
            pltpu.VMEM((2 * WIDE, LANES), F32),
            pltpu.SemaphoreType.DMA((4,)),
        ],
        compiler_params=PARAMS,
        cost_estimate=pl.CostEstimate(
            flops=2 * n_own * 9 * CHANS * LANES, bytes_accessed=4 * 1024 * 1024, transcendentals=n_own * CHANS
        ),
        name="conv_forward",
    )(pos, slots, *extra, in_hbm(weights), *(() if first else (in_hbm(kept),)), *ties)


def below_kernel(layer, pool, total, top, *refs):
    pos, zc, st, gs = refs[:4]
    if top:
        terms, w_hbm, h_out, dn_out, msg, w, tab, sem = refs[4:]
        fetch = pltpu.make_async_copy(w_hbm.at[layer], w, sem)
        fetch.start()
    else:
        terms, (dn_out, msg, tab) = refs[4:8], refs[-3:]
    n_own = dn_out.shape[0]
    rstd, own, oth = norm_tables(st, pos[0], pos[2], pos[3], float(n_own), total)
    tab[0:1], tab[1:2] = rstd, own
    tab[2:3], tab[3:4] = gs[layer : layer + 1, :], gs[layer + 8 : layer + 9, :]

    def body(j, accs):
        rows = pair_rows(j)
        xhat = zc[rows, :].astype(F32) * tab[0:1, :] + tab[1:2, :]
        n = xhat * tab[2:3, :] + tab[3:4, :]
        sig = sigmoid(n)
        h = n * sig
        if top:
            g = terms[rows, :].astype(F32)
            h_out[rows, :] = h.astype(BF16)
        else:
            g = functools.reduce(jnp.add, [term[rows, :].astype(F32) for term in terms])
        if pool:
            g = soft_pull(h, g)
        dn = g * (sig * (1.0 + n - h))
        dn_out[rows, :] = dn
        return accs[0] + fold(dn), accs[1] + fold(dn * xhat)

    zero = jnp.zeros((8, LANES), F32)
    sums = lax.fori_loop(0, n_own // (2 * WIDE), body, (zero, zero), unroll=3)
    sums = [jnp.sum(v, axis=0, keepdims=True) for v in sums]
    msg[0:WIDE, :] = dn_out[pl.ds(edge_start(n_own, WIDE, pos[1]), WIDE), :]
    msg[WIDE : WIDE + 8, :] = jnp.concatenate(sums + [jnp.zeros((6, LANES), F32)], axis=0)
    if top:
        fetch.wait()


def below_step(layer, pool, total, pos, zc, st, gs, terms, ties=(), weights=None):
    n_own = terms[0].shape[0]
    top = weights is not None
    ties = (in_hbm(weights),) if top else ties
    out_shape = [
        pltpu.VMEM((n_own, LANES), F32),
        pltpu.VMEM((WIDE + 8, LANES), F32),
    ]
    if top:
        out_shape = [jax.ShapeDtypeStruct((n_own, LANES), BF16), *out_shape, pltpu.VMEM(weights.shape[1:], BF16)]
    return pl.pallas_call(
        functools.partial(below_kernel, layer, pool, total, top),
        out_shape=tuple(out_shape),
        in_specs=[SMEM] + [VMEM] * (3 + len(terms)) + [ANY if top else FREE] * len(ties),
        out_specs=(VMEM,) * len(out_shape),
        scratch_shapes=[pltpu.VMEM((8, LANES), F32)] + ([pltpu.SemaphoreType.DMA] if top else []),
        compiler_params=PARAMS,
        cost_estimate=LITTLE,
        name="silu_backward",
    )(pos, zc, st, gs, *terms, *ties)


def bwd_kernel(layer, total, *refs):
    pos, dn, dedge, sums, zc, st, gs, w = refs[:8]
    outs, d_out, d, y, tab = refs[-8:-4], *refs[-4:]
    t, r = pos[0], pos[1]
    n_own = dn.shape[0]
    halo_at = pl.multiple_of((1 - r) * (n_own + WIDE), WIDE)
    zero_at = pl.multiple_of(r * (n_own + WIDE), WIDE)
    edge = zc.shape[0] - n_own
    d[pl.ds(zero_at, WIDE), :] = jnp.zeros((WIDE, 3 * LANES), BF16)
    rstd, own, oth = norm_tables(st, t, pos[2], pos[3], float(n_own), total)
    scale = gs[layer : layer + 1, :] * rstd
    shift_sum, gain_sum = sums[0:1, :], sums[1:2, :]
    slope = scale * gain_sum / total
    tab[0:1] = scale
    tab[1:2] = slope * rstd
    tab[2:3] = scale * shift_sum / total + slope * own
    tab[3:4] = scale * shift_sum / total + slope * oth

    def spread_columns(v):
        rows = v.shape[0]
        column = lax.broadcasted_iota(jnp.int32, v.shape, 0) % WIDE
        ahead = jnp.where(column == WIDE - 1, 0.0, pltpu.roll(v, rows - 1, 0))
        behind = jnp.where(column == 0, 0.0, pltpu.roll(v, 1, 0))
        return jnp.concatenate([ahead.astype(BF16), v.astype(BF16), behind.astype(BF16)], axis=1)

    near = n_own if edge == WIDE else pl.multiple_of(n_own + r * WIDE, WIDE)
    near = zc[pl.ds(near, WIDE), :].astype(F32)
    d[pl.ds(halo_at, WIDE), :] = spread_columns(dedge[0:WIDE, :] * tab[0:1, :] - tab[3:4, :] - near * tab[1:2, :])
    pair, block = 2 * WIDE, n_own // 3
    steps, made = n_own // pair, 0
    for part in range(3):
        first_row = part * block
        while made < min(steps, (first_row + block + WIDE + pair - 1) // pair):
            at = made * pair
            v = dn[at : at + pair, :] * tab[0:1, :] - tab[2:3, :] - zc[at : at + pair, :].astype(F32) * tab[1:2, :]
            v = spread_columns(v)
            d[at + WIDE : at + WIDE + pair, :] = v
            d_out[at : at + pair, :] = v
            made += 1
        if part == 0:
            rhs = jnp.concatenate([w[:, i * CHANS : (i + 1) * CHANS] for i in range(9)], axis=0)
        windows = [first_row + (2 - i) * WIDE for i in range(3)]
        lhs = jnp.concatenate([d[at : at + block, :] for at in windows], axis=1)
        y[first_row : first_row + block, :] = jnp.dot(lhs, rhs, preferred_element_type=F32)
        for j in range(block // pair):
            rows = slice(first_row + j * pair, first_row + (j + 1) * pair)
            for k in range(GROUPS):
                outs[k][rows, :] = y[rows, pl.ds(lane_of(t ^ k), LANES)].astype(BF16)


def bwd_step(layer, total, pos, dn, dedge, sums, zc, st, gs, w, ties):
    n_own = dn.shape[0]
    part = pltpu.VMEM((n_own, LANES), BF16)
    return pl.pallas_call(
        functools.partial(bwd_kernel, layer, total),
        out_shape=(part, part, part, part, pltpu.VMEM((n_own, 3 * LANES), BF16)),
        in_specs=[SMEM] + [VMEM] * 7 + [FREE] * len(ties),
        out_specs=(VMEM,) * 5,
        scratch_shapes=[
            pltpu.VMEM((n_own + 2 * WIDE, 3 * LANES), BF16),
            pltpu.VMEM((n_own, CHANS), F32),
            pltpu.VMEM((8, LANES), F32),
        ],
        compiler_params=PARAMS,
        cost_estimate=LITTLE,
        name="conv_backward",
    )(pos, dn, dedge, sums, zc, st, gs, pltpu.with_memory_space_constraint(w, pltpu.VMEM), *ties)


def last_kernel(t0, t1, t2, t3, *refs):
    out = refs[-1]

    def body(j, carry):
        rows = pair_rows(j)
        out[rows, :] = functools.reduce(jnp.add, [term[rows, :].astype(F32) for term in (t0, t1, t2, t3)])
        return carry

    lax.fori_loop(0, out.shape[0] // (2 * WIDE), body, 0)


def last_step(terms, ties):
    return pl.pallas_call(
        last_kernel,
        out_shape=jax.ShapeDtypeStruct(terms[0].shape, F32),
        in_specs=[VMEM] * 4 + [FREE] * len(ties),
        out_specs=VMEM,
        compiler_params=PARAMS,
        cost_estimate=LITTLE,
        name="add_terms",
    )(*terms, *ties)


def halves_kernel(keep, got, out):
    out[...] = (keep[...].astype(F32) + got[...].astype(F32)).astype(BF16)


def add_halves(keep, got):
    return pl.pallas_call(
        halves_kernel,
        out_shape=jax.ShapeDtypeStruct(keep.shape, BF16),
        in_specs=[VMEM] * 2,
        out_specs=VMEM,
        compiler_params=PARAMS,
        cost_estimate=LITTLE,
        name="add_halves",
    )(keep, got)


def wgrad_kernel(layer, pos, d, hb_hbm, *refs):
    if layer > 0:
        w_hbm, keep, send, w, hb, grad, sem = refs
        fetch = pltpu.make_async_copy(w_hbm.at[layer - 1], w, sem.at[1])
    else:
        keep, send, hb, grad, sem = refs
    load = pltpu.make_async_copy(hb_hbm.at[layer], hb, sem.at[0])
    load.start()
    if layer > 0:
        fetch.start()
    n_own = d.shape[0]
    lhs = d[...]
    load.wait()
    for i in range(3):
        part = lax.dot_general(
            lhs, hb[i * WIDE : i * WIDE + n_own, :], (((0,), (0,)), ((), ())), preferred_element_type=F32
        ).astype(BF16)
        for s in range(3):
            grad[:, (3 * i + s) * CHANS : (3 * i + s + 1) * CHANS] = part[s * LANES : (s + 1) * LANES]
    half = LANES // 2
    keep[...] = grad[pl.ds(pl.multiple_of(pos[1] * half, half), half), :]
    send[...] = grad[pl.ds(pl.multiple_of((1 - pos[1]) * half, half), half), :]
    if layer > 0:
        fetch.wait()


def wgrad_step(layer, pos, d, kept, weights):
    half = pltpu.VMEM((LANES // 2, 9 * CHANS), BF16)
    more = layer > 0
    return pl.pallas_call(
        functools.partial(wgrad_kernel, layer),
        out_shape=(half, half) + ((pltpu.VMEM((LANES, 9 * CHANS), BF16),) if more else ()),
        in_specs=[SMEM, VMEM, ANY] + ([ANY] if more else []),
        out_specs=(VMEM,) * (3 if more else 2),
        scratch_shapes=[
            pltpu.VMEM(kept.shape[1:], BF16),
            pltpu.VMEM((LANES, 9 * CHANS), BF16),
            pltpu.SemaphoreType.DMA((2,)),
        ],
        compiler_params=PARAMS,
        cost_estimate=LITTLE,
        name="kernel_gradient",
    )(pos, d, in_hbm(kept), *((in_hbm(weights),) if more else ()))


def place_kernel(layers, fresh, pos, *refs):
    count = 2 * len(layers)
    sources = refs[:count]
    out, held, wide, sem = refs[-4:]
    half = LANES // 2
    r = pos[1]
    loads = [pltpu.make_async_copy(sources[j], held.at[j], sem.at[j]) for j in range(count)]
    for load in loads:
        load.start()
    stores = []
    for j in range(count):
        at = pl.multiple_of((r if j % 2 == 0 else 1 - r) * half, half)
        if j >= 4:
            stores[j - 4].wait()
        loads[j].wait()
        wide[j % 4] = held[j].astype(F32)
        store = pltpu.make_async_copy(wide.at[j % 4], out.at[layers[j // 2], pl.ds(at, half)], sem.at[count + j])
        store.start()
        stores.append(store)
    for store in stores[-4:]:
        store.wait()


def place_step(layers, pos, sources, whole, count):
    half = LANES // 2
    jobs = len(sources)
    return pl.pallas_call(
        functools.partial(place_kernel, layers, whole is None),
        out_shape=pltpu.HBM((count, LANES, 9 * CHANS), F32),
        in_specs=[SMEM] + [FREE] * jobs + ([] if whole is None else [ANY]),
        out_specs=ANY,
        input_output_aliases={} if whole is None else {1 + jobs: 0},
        scratch_shapes=[
            pltpu.VMEM((jobs, half, 9 * CHANS), BF16),
            pltpu.VMEM((4, half, 9 * CHANS), F32),
            pltpu.SemaphoreType.DMA((2 * jobs,)),
        ],
        compiler_params=PARAMS,
        cost_estimate=LITTLE,
        name="place_gradients",
    )(pos, *sources, *(() if whole is None else (in_hbm(whole),)))


def swap_with(value, axis, k):
    return lax.ppermute(value, axis, [(i, i ^ k) for i in range(lax.axis_size(axis))])


def spread(own):
    return (own, *[swap_with(own, "tensor", k) for k in range(1, GROUPS)])


def share_moments(mine, count):
    other = swap_with(mine, "rows", 1)
    mean = 0.5 * (mine[0:1] + other[0:1])
    apart = mine[1:2] + other[1:2] + (0.5 * count) * jnp.square(other[0:1] - mine[0:1])
    own = jnp.concatenate([mean, apart], axis=0)
    all_four = [own] + [swap_with(own, "dp", k) for k in (1, 2, 3)]
    mean = 0.25 * functools.reduce(jnp.add, [v[0:1] for v in all_four])
    apart = functools.reduce(jnp.add, [v[1:2] + (2.0 * count) * jnp.square(v[0:1] - mean) for v in all_four])
    return jnp.concatenate([mean, apart, mine[0:1], other[0:1]], axis=0).reshape(2, 1, 2, LANES)


def halo_of_input(x, half):
    n_own = x.shape[0]
    edge = jnp.where(half == 0, x[n_own - WIDE :], x[:WIDE])
    return jnp.concatenate([x, swap_with(edge, "rows", 1)], axis=0)


def fast_local(section_input, conv_weights, norm_gains, norm_shifts, out_grad, out_mask):
    images, rows_here, width = out_mask.shape
    layers = conv_weights.shape[0]
    n_own = rows_here * width
    parts = lax.axis_size("dp") * lax.axis_size("rows")
    total = float(n_own * parts)
    t, half = lax.axis_index("tensor"), lax.axis_index("rows")
    image = lax.axis_index("dp")
    pos = jnp.stack([t, half, 2 * image + half, 2 * image + 1 - half]).astype(jnp.int32)
    middle = layers // 2
    x = to_maps(section_input, width).reshape(n_own, LANES)
    slots = lax.all_gather(halo_of_input(x, half), "tensor", axis=1, tiled=True)
    pad = jnp.zeros((8 - layers, LANES), F32)
    tables = spread(jnp.concatenate([norm_gains, pad, norm_shifts, pad], axis=0))
    top_grad = (to_maps(out_grad, width) * out_mask[..., None].astype(BF16)).reshape(n_own, LANES)

    st, kept = None, None
    halves = ("dp", "rows")
    kept_z, kept_st = [], []
    for layer in range(layers):
        last = layer + 1 == layers
        edge = 2 * WIDE if layer + 1 == middle else WIDE
        everyone = ("dp", "rows", "tensor")
        kept, zc, rim, local = fwd_step(
            layer,
            layer == middle,
            edge,
            total,
            pos,
            slots,
            st,
            tables,
            conv_weights,
            kept,
            n_own,
            (top_grad,) if layer == 2 else (),
        )
        rim = swap_with(rim, "rows", 1)
        if last:
            st = share_moments(local, float(n_own))
        else:
            local = jnp.broadcast_to(local, (parts * GROUPS, 2, LANES))
            st = lax.all_to_all(local, everyone, split_axis=0, concat_axis=0, tiled=True)
            st = st.reshape(parts, GROUPS, 2, LANES)
        zc = lax.dynamic_update_slice_in_dim(zc, rim, n_own, axis=0)
        kept_z.append(zc)
        kept_st.append(st)
        if not last:
            slots = lax.all_gather(zc, "tensor", axis=1, tiled=True)
    top = layers - 1
    h_last, dn, msg, w = below_step(
        top, False, total, pos, kept_z[top], kept_st[top], tables[0], (top_grad,), weights=conv_weights
    )

    def with_other(values):
        return [v for mine in values for v in (mine, swap_with(mine, "rows", 1))]

    sum_list, pairs = [None] * layers, [None] * layers
    ahead, back = [[0, 1, 3, 2]], [[2, 3, 1, 0]]
    urgent = ()
    for layer in range(layers - 1, -1, -1):
        got = swap_with(msg, "rows", 1)
        sums = msg[WIDE:] + got[WIDE:]
        one, two, three = (swap_with(sums, "dp", k) for k in (1, 2, 3))
        sums = (sums + one) + (two + three)
        sum_list[layer] = sums
        *terms, d = bwd_step(
            layer, total, pos, dn, got, sums, kept_z[layer], kept_st[layer], tables[0], w, urgent
        )
        terms = (terms[0], *[swap_with(terms[k], "tensor", k) for k in range(1, GROUPS)])
        keep, send, *w = wgrad_step(layer, pos, d, kept, conv_weights)
        w = w[0] if w else None
        other = swap_with(send, "rows", 1)
        pairs[layer] = add_halves(keep, other)
        urgent, settled = (other,), (() if layer + 1 == layers else (pairs[layer + 1],))
        if layer == 4:
            upper = lax.psum((pairs[5], pairs[4]), "dp", axis_index_groups=ahead)
        if layer == 2:
            mid = lax.psum((pairs[3], pairs[2]), "dp", axis_index_groups=back)
        if layer > 0:
            below = layer - 1
            late = (in_hbm(upper[0]),) if layer == 1 else ()
            dn, msg = below_step(
                below, layer == middle, total, pos, kept_z[below], kept_st[below], tables[0], terms, (keep, *settled, *late)
            )
        else:
            grad = last_step(terms, (pairs[0], pairs[1]))
    tied, upper = lax.optimization_barrier(((pairs[1], pairs[0]), upper))
    lower = lax.psum(tied, "dp", axis_index_groups=ahead)
    shape = (images, rows_here, width, LANES)
    grad, mid = lax.optimization_barrier((grad, mid))
    outputs = (from_maps(h_last.reshape(shape)), from_maps(grad.reshape(shape)))
    whole = place_step((5, 4, 3, 2), pos, with_other((*upper, *mid)), None, layers)
    sums = jnp.stack(sum_list)
    sums = (sums[:, 1], sums[:, 0])
    lower, whole, outputs, sums = lax.optimization_barrier((lower, whole, outputs, sums))
    whole = place_step((1, 0), pos, with_other(lower), whole, layers)
    return (*outputs, whole, *sums)


def solution(mesh):
    in_specs = (
        P("dp", "rows", "tensor"),
        P(None, "tensor", None),
        P(None, "tensor"),
        P(None, "tensor"),
        P("dp", "rows", "tensor"),
        P("dp", "rows", None),
    )
    out_specs = (
        P("dp", "rows", "tensor"),
        P("dp", "rows", "tensor"),
        P(None, "tensor", None),
        P(None, "tensor"),
        P(None, "tensor"),
    )
    local = fast_local if fits_kernels(mesh) else generic_local
    return jax.shard_map(local, mesh=mesh, in_specs=in_specs, out_specs=out_specs, check_vma=False)
```

```python
import functools

import jax
import jax.numpy as jnp
from jax import lax
from jax.experimental import pallas as pl
from jax.experimental.pallas import tpu as pltpu
from jax.sharding import PartitionSpec as P

EPS = 1e-05


def padded_2(cells, sides, width):
    for axis, dim in sides:
        count = lax.axis_size(axis)
        ends = count - 1
        head = lax.slice_in_dim(cells, 0, width, axis=dim)
        tail = lax.slice_in_dim(cells, cells.shape[dim] - width, cells.shape[dim], axis=dim)
        cells = jnp.concatenate(
            [
                lax.ppermute(tail, axis, [(i, (i + 1) % count) for i in range(ends)]),
                cells,
                lax.ppermute(head, axis, [((i + 1) % count, i) for i in range(ends)]),
            ],
            axis=dim,
        )
    return cells


def to_maps(flat, width):
    count, high, merged = flat.shape
    return flat.reshape(count, high, merged // width, width).transpose(0, 1, 3, 2)


def from_maps(maps):
    count, high, wide, chans = maps.shape
    return maps.transpose(0, 1, 3, 2).reshape(count, high, chans * wide)


def spatial_conv(padded, kernel):
    return lax.conv_general_dilated(
        padded,
        kernel,
        (1, 1),
        ((0, 0), (1, 1)),
        dimension_numbers=("NHWC", "HWIO", "NHWC"),
        preferred_element_type=jnp.float32,
    )


def flipped(kernel):
    return jnp.transpose(kernel[::-1, ::-1], (0, 1, 3, 2))


def pool_unpool(values):
    count, high, wide, chans = values.shape
    blocks = values.reshape(count, high // 2, 2, wide // 2, 2, chans)
    pooled = jax.nn.logsumexp(blocks, axis=(2, 4), keepdims=True)
    return (jnp.exp(blocks - pooled) * pooled).reshape(values.shape)


def moments(conv_out, total_pixels):
    summed = lax.psum(jnp.sum(conv_out, axis=(0, 1, 2)), ("dp", "rows"))
    mean = summed / total_pixels
    spread = lax.psum(jnp.sum(jnp.square(conv_out - mean), axis=(0, 1, 2)), ("dp", "rows"))
    var = spread / total_pixels
    return (mean, lax.rsqrt(var + EPS))


def kernel_grad(whole, dconv):
    images, rows_here, width, chans = dconv.shape
    widened = jnp.pad(whole, ((0, 0), (0, 0), (1, 1), (0, 0)))
    stacked = []
    for row_off in range(3):
        line = []
        for col_off in range(3):
            window = widened[:, row_off : row_off + rows_here, col_off : col_off + width, :]
            line.append(
                jnp.einsum("bhwc,bhwo->co", window, dconv, preferred_element_type=jnp.float32)
            )
        stacked.append(jnp.stack(line))
    return jnp.stack(stacked)


def generic_local(section_input, conv_weights, norm_gains, norm_shifts, out_grad, out_mask):
    width = out_mask.shape[2]
    images, rows_here = (out_mask.shape[0], out_mask.shape[1])
    total_pixels = float(images * rows_here * width * lax.axis_size("dp") * lax.axis_size("rows"))
    layers, out_here, flat_in = conv_weights.shape
    chans_in = flat_in // 9
    kernels_hwio = conv_weights.reshape(layers, out_here, 3, 3, chans_in).transpose(0, 2, 3, 4, 1)
    middle = layers // 2
    kept = []
    acting = to_maps(section_input, width)
    current = acting.astype(jnp.float32)
    pre_pool = current
    for index in range(layers):
        if index == middle:
            pre_pool = current
            acting = pool_unpool(pre_pool).astype(jnp.bfloat16)
        padded = padded_2(acting, (("rows", 1),), 1)
        whole = lax.all_gather(padded, "tensor", axis=3, tiled=True)
        conv_out = spatial_conv(whole, kernels_hwio[index])
        mean, rstd = moments(conv_out, total_pixels)
        normed = (conv_out - mean) * rstd
        shifted = normed * norm_gains[index] + norm_shifts[index]
        current = jax.nn.silu(shifted)
        acting = current.astype(jnp.bfloat16)
        kept.append((whole, normed, shifted, rstd))
    grad = to_maps(out_grad, width).astype(jnp.float32) * out_mask[..., None].astype(jnp.float32)
    kernel_list = [None] * layers
    gain_list = [None] * layers
    shift_list = [None] * layers
    for index in range(layers - 1, -1, -1):
        whole, normed, shifted, rstd = kept[index]
        unused, pull_silu = jax.vjp(jax.nn.silu, shifted)
        dshift = pull_silu(grad)[0]
        gain_sum, shift_sum = lax.psum(
            (jnp.sum(dshift * normed, axis=(0, 1, 2)), jnp.sum(dshift, axis=(0, 1, 2))),
            ("dp", "rows"),
        )
        gain_list[index] = gain_sum
        shift_list[index] = shift_sum
        dconv = (
            norm_gains[index]
            * rstd
            * (dshift - shift_sum / total_pixels - normed * gain_sum / total_pixels)
        ).astype(jnp.bfloat16)
        summed_kernel = lax.psum(
            kernel_grad(whole, dconv).astype(jnp.bfloat16), ("dp", "rows")
        ).astype(jnp.float32)
        kernel_list[index] = summed_kernel.transpose(3, 0, 1, 2).reshape(out_here, flat_in)
        grad_rim = padded_2(dconv, (("rows", 1),), 1)
        partial_terms = spatial_conv(grad_rim, flipped(kernels_hwio[index]))
        grad_in = lax.psum_scatter(
            partial_terms.astype(jnp.bfloat16), "tensor", scatter_dimension=3, tiled=True
        ).astype(jnp.float32)
        if index == middle:
            unused, pull_pool = jax.vjp(pool_unpool, pre_pool)
            grad = pull_pool(grad_in)[0]
        else:
            grad = grad_in
    return (
        from_maps(acting),
        from_maps(grad),
        jnp.stack(kernel_list),
        jnp.stack(gain_list),
        jnp.stack(shift_list),
    )


GROUPS = 4
LANES = 128
WIDE = 48
CHANS = GROUPS * LANES
F32 = jnp.float32
BF16 = jnp.bfloat16
VMEM = pl.BlockSpec(memory_space=pltpu.VMEM)
SMEM = pl.BlockSpec(memory_space=pltpu.SMEM)
ANY = pl.BlockSpec(memory_space=pltpu.HBM)
FREE = pl.BlockSpec(memory_space=pl.ANY)
LITTLE = pl.CostEstimate(flops=1024, bytes_accessed=1024, transcendentals=0)
PARAMS = pltpu.CompilerParams(vmem_limit_bytes=20 * 1024 * 1024)


def in_hbm(value):
    return pltpu.with_memory_space_constraint(value, pltpu.HBM)


def fits_kernels(mesh):
    return mesh.shape["tensor"] == GROUPS and mesh.shape["rows"] == 2 and mesh.shape["dp"] == 4


def sigmoid(v):
    return 0.5 * jnp.tanh(0.5 * v) + 0.5


def swap_columns(v):
    column = lax.broadcasted_iota(jnp.int32, v.shape, 0)
    return jnp.where(column % 2 == 0, pltpu.roll(v, WIDE - 1, 0), pltpu.roll(v, 1, 0))


def soft_parts(h):
    top = jnp.maximum(h[0], h[1])
    top = jnp.maximum(top, swap_columns(top))
    e0, e1 = jnp.exp(h[0] - top), jnp.exp(h[1] - top)
    total = e0 + e1
    total = total + swap_columns(total)
    pooled = top + jnp.log(total)
    inverse = 1.0 / total
    return e0 * inverse, e1 * inverse, pooled


def soft(h):
    h = h.reshape(2, WIDE, LANES)
    q0, q1, pooled = soft_parts(h)
    return jnp.concatenate([q0 * pooled, q1 * pooled], axis=0)


def soft_pull(h, grad):
    h = h.reshape(2, WIDE, LANES)
    grad = grad.reshape(2, WIDE, LANES)
    q0, q1, pooled = soft_parts(h)
    mix = q0 * grad[0] + q1 * grad[1]
    mix = mix + swap_columns(mix)
    return jnp.concatenate(
        [q0 * (pooled * (grad[0] - mix) + mix), q1 * (pooled * (grad[1] - mix) + mix)], axis=0
    )


def norm_tables(st, group, i_own, i_oth, n_local, total):
    parts = st.shape[0]
    if parts == 2:
        mean, rstd = st[0, 0, 0:1], lax.rsqrt(st[0, 0, 1:2] / total + EPS)
        return rstd, (st[1, 0, 0:1] - mean) * rstd, (st[1, 0, 1:2] - mean) * rstd
    group = 0 if st.shape[1] == 1 else group
    blocks = [st[i, group] for i in range(parts)]
    summed = functools.reduce(jnp.add, blocks)
    mean = summed[0:1] / parts
    apart = functools.reduce(jnp.add, [jnp.square(b - mean) for b in blocks])
    rstd = lax.rsqrt((summed[1:2] + n_local * apart[0:1]) / total + EPS)
    return rstd, (st[i_own, group, 0:1] - mean) * rstd, (st[i_oth, group, 0:1] - mean) * rstd


def left_right(y0, y1, y2):
    rows = y0.shape[0]
    column = lax.broadcasted_iota(jnp.int32, y0.shape, 0) % WIDE
    before = jnp.where(column == 0, 0.0, pltpu.roll(y0, 1, 0))
    after = jnp.where(column == WIDE - 1, 0.0, pltpu.roll(y2, rows - 1, 0))
    return before + y1 + after


def lane_of(group):
    return pl.multiple_of(group * LANES, LANES)


def edge_start(n_own, edge, half):
    return pl.multiple_of((1 - half) * (n_own - edge), WIDE)


def pair_rows(j):
    return pl.ds(pl.multiple_of(j * 2 * WIDE, 2 * WIDE), 2 * WIDE)


def fold(v):
    return jnp.sum(v.reshape(v.shape[0] // 8, 8, LANES), axis=0)


def fwd_kernel(first, last, pool, layer, total, edge_out, *refs):
    pos, zall = refs[0], refs[1]
    if first:
        w_hbm = refs[2]
    else:
        st, gss, w_hbm = refs[2], refs[3:7], refs[7]
    if last:
        hb_out, zc_out, edge_ref, st_out, w, hb, y, z, tab, hs, sem = refs[-11:]
    else:
        hb_out, zc_out, edge_ref, st_out, hb, w, y, z, tab, hs, sem = refs[-11:]
    load = pltpu.make_async_copy(w_hbm.at[layer], w, sem.at[0])
    load.start()
    saves = []
    t, r = pos[0], pos[1]
    n_own = z.shape[0]
    halo_at = pl.multiple_of((1 - r) * (n_own + WIDE), WIDE)
    zero_at = pl.multiple_of(r * (n_own + WIDE), WIDE)
    hb[pl.ds(zero_at, WIDE), :] = jnp.zeros((WIDE, CHANS), BF16)
    edge = zall.shape[0] - n_own
    if not first:
        for k in range(GROUPS):
            group = t ^ k
            rstd, own, oth = norm_tables(st, group, pos[2], pos[3], float(n_own), total)
            gain, shift = gss[k][layer - 1 : layer, :], gss[k][layer + 7 : layer + 8, :]
            tab[group, 0:1] = rstd * gain
            tab[group, 1:2] = own * gain + shift
            tab[group, 2:3] = oth * gain + shift

    def act(values, group, which):
        if first:
            return values
        n = values.astype(F32) * tab[group, 0:1, :] + tab[group, which : which + 1, :]
        h = n * sigmoid(n)
        return soft(h) if pool else h

    for group in range(GROUPS):
        lanes = slice(group * LANES, (group + 1) * LANES)
        h = act(zall[n_own : n_own + edge, lanes], group, 2)
        if edge > WIDE:
            hs[...] = h
            h = hs[pl.ds(pl.multiple_of(r * WIDE, WIDE), WIDE), :]
        hb[pl.ds(halo_at, WIDE), lanes] = h.astype(BF16)
    pair, block = 2 * WIDE, n_own // 3
    steps, made = n_own // pair, 0
    summed = jnp.zeros((8, LANES), F32)
    for part in range(3):
        first_row = part * block
        while made < min(steps, (first_row + block + WIDE + pair - 1) // pair):
            at = made * pair
            for group in range(GROUPS):
                lanes = slice(group * LANES, (group + 1) * LANES)
                h = act(zall[at : at + pair, lanes], group, 1)
                hb[at + WIDE : at + WIDE + pair, lanes] = h.astype(BF16)
            made += 1
        if part == 0:
            load.wait()
            rhs = jnp.concatenate(
                [
                    jnp.concatenate([w[:, (3 * i + s) * CHANS : (3 * i + s + 1) * CHANS] for i in range(3)], axis=1)
                    for s in range(3)
                ],
                axis=0,
            )
        start, stop = (0 if part == 0 else first_row + 2 * WIDE), first_row + block + 2 * WIDE
        saves.append(
            pltpu.make_async_copy(hb.at[start:stop], hb_out.at[layer, start:stop], sem.at[1 + part])
        )
        saves[-1].start()
        lhs = jnp.concatenate([hb[first_row + i * WIDE : first_row + i * WIDE + block, :] for i in range(3)], axis=1)
        rows = slice(first_row, first_row + block)
        y[rows, :] = lax.dot_general(lhs, rhs, (((1,), (1,)), ((), ())), preferred_element_type=F32)
        for j in range(block // pair):
            rows = slice(first_row + j * pair, first_row + (j + 1) * pair)
            v = left_right(y[rows, 0:128], y[rows, 128:256], y[rows, 256:384])
            z[rows, :] = v
            summed = summed + fold(v)
    mean = jnp.sum(summed, axis=0, keepdims=True) / n_own
    apart = jnp.zeros((8, LANES), F32)
    for j in range(steps):
        rows = slice(j * pair, (j + 1) * pair)
        v = z[rows, :] - mean
        zc_out[rows, :] = v.astype(BF16)
        apart = apart + fold(jnp.square(v))
    sums = jnp.concatenate([mean, jnp.sum(apart, axis=0, keepdims=True)], axis=0)
    st_out[...] = sums
    edge_ref[...] = zc_out[pl.ds(edge_start(n_own, edge_out, r), edge_out), :]
    zc_out[n_own : n_own + edge_out, :] = jnp.zeros((edge_out, LANES), BF16)
    for save in saves:
        save.wait()


def fwd_step(layer, pool, edge_out, total, pos, slots, st, tables, weights, kept, n_own, ties):
    first = st is None
    layers = weights.shape[0]
    extra = () if first else (st, *tables)
    last = layer + 1 == layers
    kernels = pltpu.VMEM((LANES, 9 * CHANS), BF16)
    return pl.pallas_call(
        functools.partial(fwd_kernel, first, last, pool, layer, total, edge_out),
        out_shape=(
            pltpu.HBM((layers, n_own + 2 * WIDE, CHANS), BF16),
            pltpu.VMEM((n_own + edge_out, LANES), BF16),
            pltpu.VMEM((edge_out, LANES), BF16),
            pltpu.VMEM((2, LANES), F32),
            *((kernels,) if last else ()),
        ),
        in_specs=[SMEM] + [VMEM] * (1 + len(extra)) + [ANY] * (1 if first else 2) + [FREE] * len(ties),
        out_specs=(ANY, VMEM, VMEM, VMEM) + ((VMEM,) if last else ()),
        input_output_aliases={} if first else {3 + len(extra): 0},
        scratch_shapes=[
            pltpu.VMEM((n_own + 2 * WIDE, CHANS), BF16),
            *(() if last else (kernels,)),
            pltpu.VMEM((n_own, 3 * LANES), F32),
            pltpu.VMEM((n_own, LANES), F32),
            pltpu.VMEM((GROUPS, 8, LANES), F32),
            pltpu.VMEM((2 * WIDE, LANES), F32),
            pltpu.SemaphoreType.DMA((4,)),
        ],
        compiler_params=PARAMS,
        cost_estimate=pl.CostEstimate(
            flops=2 * n_own * 9 * CHANS * LANES, bytes_accessed=4 * 1024 * 1024, transcendentals=n_own * CHANS
        ),
        name="conv_forward",
    )(pos, slots, *extra, in_hbm(weights), *(() if first else (in_hbm(kept),)), *ties)


def below_kernel(layer, pool, total, top, *refs):
    pos, zc, st, gs = refs[:4]
    if top:
        terms, h_out, dn_out, msg, tab = refs[4:]
    else:
        terms, (dn_out, msg, tab) = refs[4:8], refs[-3:]
    n_own = dn_out.shape[0]
    rstd, own, oth = norm_tables(st, pos[0], pos[2], pos[3], float(n_own), total)
    tab[0:1], tab[1:2] = rstd, own
    tab[2:3], tab[3:4] = gs[layer : layer + 1, :], gs[layer + 8 : layer + 9, :]

    def body(j, accs):
        rows = pair_rows(j)
        xhat = zc[rows, :].astype(F32) * tab[0:1, :] + tab[1:2, :]
        n = xhat * tab[2:3, :] + tab[3:4, :]
        sig = sigmoid(n)
        h = n * sig
        if top:
            g = terms[rows, :].astype(F32)
            h_out[rows, :] = h.astype(BF16)
        else:
            g = functools.reduce(jnp.add, [term[rows, :].astype(F32) for term in terms])
        if pool:
            g = soft_pull(h, g)
        dn = g * (sig * (1.0 + n - h))
        dn_out[rows, :] = dn
        return accs[0] + fold(dn), accs[1] + fold(dn * xhat)

    zero = jnp.zeros((8, LANES), F32)
    sums = lax.fori_loop(0, n_own // (2 * WIDE), body, (zero, zero), unroll=3)
    sums = [jnp.sum(v, axis=0, keepdims=True) for v in sums]
    msg[0:WIDE, :] = dn_out[pl.ds(edge_start(n_own, WIDE, pos[1]), WIDE), :]
    msg[WIDE : WIDE + 8, :] = jnp.concatenate(sums + [jnp.zeros((6, LANES), F32)], axis=0)


def below_step(layer, pool, total, pos, zc, st, gs, terms, ties=()):
    n_own = terms[0].shape[0]
    top = len(terms) == 1
    out_shape = [
        pltpu.VMEM((n_own, LANES), F32),
        pltpu.VMEM((WIDE + 8, LANES), F32),
    ]
    if top:
        out_shape = [jax.ShapeDtypeStruct((n_own, LANES), BF16)] + out_shape
    return pl.pallas_call(
        functools.partial(below_kernel, layer, pool, total, top),
        out_shape=tuple(out_shape),
        in_specs=[SMEM] + [VMEM] * (3 + len(terms)) + [FREE] * len(ties),
        out_specs=(VMEM,) * len(out_shape),
        scratch_shapes=[pltpu.VMEM((8, LANES), F32)],
        compiler_params=PARAMS,
        cost_estimate=LITTLE,
        name="silu_backward",
    )(pos, zc, st, gs, *terms, *ties)


def bwd_kernel(layer, total, *refs):
    pos, dn, dedge, sums, zc, st, gs, w = refs[:8]
    outs, d_out, d, y, tab = refs[-8:-4], *refs[-4:]
    t, r = pos[0], pos[1]
    n_own = dn.shape[0]
    halo_at = pl.multiple_of((1 - r) * (n_own + WIDE), WIDE)
    zero_at = pl.multiple_of(r * (n_own + WIDE), WIDE)
    edge = zc.shape[0] - n_own
    d[pl.ds(zero_at, WIDE), :] = jnp.zeros((WIDE, 3 * LANES), BF16)
    rstd, own, oth = norm_tables(st, t, pos[2], pos[3], float(n_own), total)
    scale = gs[layer : layer + 1, :] * rstd
    shift_sum, gain_sum = sums[0:1, :], sums[1:2, :]
    slope = scale * gain_sum / total
    tab[0:1] = scale
    tab[1:2] = slope * rstd
    tab[2:3] = scale * shift_sum / total + slope * own
    tab[3:4] = scale * shift_sum / total + slope * oth

    def spread_columns(v):
        rows = v.shape[0]
        column = lax.broadcasted_iota(jnp.int32, v.shape, 0) % WIDE
        ahead = jnp.where(column == WIDE - 1, 0.0, pltpu.roll(v, rows - 1, 0))
        behind = jnp.where(column == 0, 0.0, pltpu.roll(v, 1, 0))
        return jnp.concatenate([ahead.astype(BF16), v.astype(BF16), behind.astype(BF16)], axis=1)

    near = n_own if edge == WIDE else pl.multiple_of(n_own + r * WIDE, WIDE)
    near = zc[pl.ds(near, WIDE), :].astype(F32)
    d[pl.ds(halo_at, WIDE), :] = spread_columns(dedge[0:WIDE, :] * tab[0:1, :] - tab[3:4, :] - near * tab[1:2, :])
    pair, block = 2 * WIDE, n_own // 3
    steps, made = n_own // pair, 0
    for part in range(3):
        first_row = part * block
        while made < min(steps, (first_row + block + WIDE + pair - 1) // pair):
            at = made * pair
            v = dn[at : at + pair, :] * tab[0:1, :] - tab[2:3, :] - zc[at : at + pair, :].astype(F32) * tab[1:2, :]
            v = spread_columns(v)
            d[at + WIDE : at + WIDE + pair, :] = v
            d_out[at : at + pair, :] = v
            made += 1
        if part == 0:
            rhs = jnp.concatenate([w[:, i * CHANS : (i + 1) * CHANS] for i in range(9)], axis=0)
        windows = [first_row + (2 - i) * WIDE for i in range(3)]
        lhs = jnp.concatenate([d[at : at + block, :] for at in windows], axis=1)
        y[first_row : first_row + block, :] = jnp.dot(lhs, rhs, preferred_element_type=F32)
        for j in range(block // pair):
            rows = slice(first_row + j * pair, first_row + (j + 1) * pair)
            for k in range(GROUPS):
                outs[k][rows, :] = y[rows, pl.ds(lane_of(t ^ k), LANES)].astype(BF16)


def bwd_step(layer, total, pos, dn, dedge, sums, zc, st, gs, w, ties):
    n_own = dn.shape[0]
    part = pltpu.VMEM((n_own, LANES), BF16)
    return pl.pallas_call(
        functools.partial(bwd_kernel, layer, total),
        out_shape=(part, part, part, part, pltpu.VMEM((n_own, 3 * LANES), BF16)),
        in_specs=[SMEM] + [VMEM] * 7 + [FREE] * len(ties),
        out_specs=(VMEM,) * 5,
        scratch_shapes=[
            pltpu.VMEM((n_own + 2 * WIDE, 3 * LANES), BF16),
            pltpu.VMEM((n_own, CHANS), F32),
            pltpu.VMEM((8, LANES), F32),
        ],
        compiler_params=PARAMS,
        cost_estimate=LITTLE,
        name="conv_backward",
    )(pos, dn, dedge, sums, zc, st, gs, pltpu.with_memory_space_constraint(w, pltpu.VMEM), *ties)


def last_kernel(t0, t1, t2, t3, *refs):
    out = refs[-1]

    def body(j, carry):
        rows = pair_rows(j)
        out[rows, :] = functools.reduce(jnp.add, [term[rows, :].astype(F32) for term in (t0, t1, t2, t3)])
        return carry

    lax.fori_loop(0, out.shape[0] // (2 * WIDE), body, 0)


def last_step(terms, ties):
    return pl.pallas_call(
        last_kernel,
        out_shape=jax.ShapeDtypeStruct(terms[0].shape, F32),
        in_specs=[VMEM] * 4 + [FREE] * len(ties),
        out_specs=VMEM,
        compiler_params=PARAMS,
        cost_estimate=LITTLE,
        name="add_terms",
    )(*terms, *ties)


def halves_kernel(keep, got, out):
    out[...] = (keep[...].astype(F32) + got[...].astype(F32)).astype(BF16)


def add_halves(keep, got):
    return pl.pallas_call(
        halves_kernel,
        out_shape=jax.ShapeDtypeStruct(keep.shape, BF16),
        in_specs=[VMEM] * 2,
        out_specs=VMEM,
        compiler_params=PARAMS,
        cost_estimate=LITTLE,
        name="add_halves",
    )(keep, got)


def wgrad_kernel(layer, pos, d, hb_hbm, *refs):
    if layer > 0:
        w_hbm, keep, send, w, hb, grad, sem = refs
        fetch = pltpu.make_async_copy(w_hbm.at[layer - 1], w, sem.at[1])
    else:
        keep, send, hb, grad, sem = refs
    load = pltpu.make_async_copy(hb_hbm.at[layer], hb, sem.at[0])
    load.start()
    if layer > 0:
        fetch.start()
    n_own = d.shape[0]
    lhs = d[...]
    load.wait()
    for i in range(3):
        part = lax.dot_general(
            lhs, hb[i * WIDE : i * WIDE + n_own, :], (((0,), (0,)), ((), ())), preferred_element_type=F32
        ).astype(BF16)
        for s in range(3):
            grad[:, (3 * i + s) * CHANS : (3 * i + s + 1) * CHANS] = part[s * LANES : (s + 1) * LANES]
    half = LANES // 2
    keep[...] = grad[pl.ds(pl.multiple_of(pos[1] * half, half), half), :]
    send[...] = grad[pl.ds(pl.multiple_of((1 - pos[1]) * half, half), half), :]
    if layer > 0:
        fetch.wait()


def wgrad_step(layer, pos, d, kept, weights):
    half = pltpu.VMEM((LANES // 2, 9 * CHANS), BF16)
    more = layer > 0
    return pl.pallas_call(
        functools.partial(wgrad_kernel, layer),
        out_shape=(half, half) + ((pltpu.VMEM((LANES, 9 * CHANS), BF16),) if more else ()),
        in_specs=[SMEM, VMEM, ANY] + ([ANY] if more else []),
        out_specs=(VMEM,) * (3 if more else 2),
        scratch_shapes=[
            pltpu.VMEM(kept.shape[1:], BF16),
            pltpu.VMEM((LANES, 9 * CHANS), BF16),
            pltpu.SemaphoreType.DMA((2,)),
        ],
        compiler_params=PARAMS,
        cost_estimate=LITTLE,
        name="kernel_gradient",
    )(pos, d, in_hbm(kept), *((in_hbm(weights),) if more else ()))


def place_kernel(layers, fresh, pos, *refs):
    count = 2 * len(layers)
    sources = refs[:count]
    out, held, wide, sem = refs[-4:]
    half = LANES // 2
    r = pos[1]
    loads = [pltpu.make_async_copy(sources[j], held.at[j], sem.at[j]) for j in range(count)]
    for load in loads:
        load.start()
    stores = []
    for j in range(count):
        at = pl.multiple_of((r if j % 2 == 0 else 1 - r) * half, half)
        if j >= 4:
            stores[j - 4].wait()
        loads[j].wait()
        wide[j % 4] = held[j].astype(F32)
        store = pltpu.make_async_copy(wide.at[j % 4], out.at[layers[j // 2], pl.ds(at, half)], sem.at[count + j])
        store.start()
        stores.append(store)
    for store in stores[-4:]:
        store.wait()


def place_step(layers, pos, sources, whole, count):
    half = LANES // 2
    jobs = len(sources)
    return pl.pallas_call(
        functools.partial(place_kernel, layers, whole is None),
        out_shape=pltpu.HBM((count, LANES, 9 * CHANS), F32),
        in_specs=[SMEM] + [FREE] * jobs + ([] if whole is None else [ANY]),
        out_specs=ANY,
        input_output_aliases={} if whole is None else {1 + jobs: 0},
        scratch_shapes=[
            pltpu.VMEM((jobs, half, 9 * CHANS), BF16),
            pltpu.VMEM((4, half, 9 * CHANS), F32),
            pltpu.SemaphoreType.DMA((2 * jobs,)),
        ],
        compiler_params=PARAMS,
        cost_estimate=LITTLE,
        name="place_gradients",
    )(pos, *sources, *(() if whole is None else (in_hbm(whole),)))


def swap_with(value, axis, k):
    return lax.ppermute(value, axis, [(i, i ^ k) for i in range(lax.axis_size(axis))])


def spread(own):
    return (own, *[swap_with(own, "tensor", k) for k in range(1, GROUPS)])


def share_moments(mine, count):
    other = swap_with(mine, "rows", 1)
    mean = 0.5 * (mine[0:1] + other[0:1])
    apart = mine[1:2] + other[1:2] + (0.5 * count) * jnp.square(other[0:1] - mine[0:1])
    own = jnp.concatenate([mean, apart], axis=0)
    all_four = [own] + [swap_with(own, "dp", k) for k in (1, 2, 3)]
    mean = 0.25 * functools.reduce(jnp.add, [v[0:1] for v in all_four])
    apart = functools.reduce(jnp.add, [v[1:2] + (2.0 * count) * jnp.square(v[0:1] - mean) for v in all_four])
    return jnp.concatenate([mean, apart, mine[0:1], other[0:1]], axis=0).reshape(2, 1, 2, LANES)


def halo_of_input(x, half):
    n_own = x.shape[0]
    edge = jnp.where(half == 0, x[n_own - WIDE :], x[:WIDE])
    return jnp.concatenate([x, swap_with(edge, "rows", 1)], axis=0)


def fast_local(section_input, conv_weights, norm_gains, norm_shifts, out_grad, out_mask):
    images, rows_here, width = out_mask.shape
    layers = conv_weights.shape[0]
    n_own = rows_here * width
    parts = lax.axis_size("dp") * lax.axis_size("rows")
    total = float(n_own * parts)
    t, half = lax.axis_index("tensor"), lax.axis_index("rows")
    image = lax.axis_index("dp")
    pos = jnp.stack([t, half, 2 * image + half, 2 * image + 1 - half]).astype(jnp.int32)
    middle = layers // 2
    x = to_maps(section_input, width).reshape(n_own, LANES)
    slots = lax.all_gather(halo_of_input(x, half), "tensor", axis=1, tiled=True)
    pad = jnp.zeros((8 - layers, LANES), F32)
    tables = spread(jnp.concatenate([norm_gains, pad, norm_shifts, pad], axis=0))
    top_grad = (to_maps(out_grad, width) * out_mask[..., None].astype(BF16)).reshape(n_own, LANES)

    st, kept = None, None
    halves = ("dp", "rows")
    kept_z, kept_st = [], []
    for layer in range(layers):
        last = layer + 1 == layers
        edge = 2 * WIDE if layer + 1 == middle else WIDE
        everyone = ("dp", "rows", "tensor")
        kept, zc, rim, local, *w = fwd_step(
            layer,
            layer == middle,
            edge,
            total,
            pos,
            slots,
            st,
            tables,
            conv_weights,
            kept,
            n_own,
            (top_grad,) if layer == 2 else (),
        )
        rim = swap_with(rim, "rows", 1)
        if last:
            st = share_moments(local, float(n_own))
        else:
            local = jnp.broadcast_to(local, (parts * GROUPS, 2, LANES))
            st = lax.all_to_all(local, everyone, split_axis=0, concat_axis=0, tiled=True)
            st = st.reshape(parts, GROUPS, 2, LANES)
        zc = lax.dynamic_update_slice_in_dim(zc, rim, n_own, axis=0)
        kept_z.append(zc)
        kept_st.append(st)
        if not last:
            slots = lax.all_gather(zc, "tensor", axis=1, tiled=True)
    top = layers - 1
    w = w[0]
    h_last, dn, msg = below_step(top, False, total, pos, kept_z[top], kept_st[top], tables[0], (top_grad,))

    def with_other(values):
        return [v for mine in values for v in (in_hbm(mine), swap_with(mine, "rows", 1))]

    sum_list, pairs = [None] * layers, [None] * layers
    ahead, back = [[0, 1, 3, 2]], [[2, 3, 1, 0]]
    urgent = ()
    for layer in range(layers - 1, -1, -1):
        got = swap_with(msg, "rows", 1)
        sums = msg[WIDE:] + got[WIDE:]
        one, two, three = (swap_with(sums, "dp", k) for k in (1, 2, 3))
        sums = (sums + one) + (two + three)
        sum_list[layer] = sums
        *terms, d = bwd_step(
            layer, total, pos, dn, got, sums, kept_z[layer], kept_st[layer], tables[0], w, urgent
        )
        terms = (terms[0], *[swap_with(terms[k], "tensor", k) for k in range(1, GROUPS)])
        keep, send, *w = wgrad_step(layer, pos, d, kept, conv_weights)
        w = w[0] if w else None
        other = swap_with(send, "rows", 1)
        pairs[layer] = add_halves(keep, other)
        urgent, settled = (other,), (() if layer + 1 == layers else (pairs[layer + 1],))
        if layer == 4:
            upper = lax.psum((pairs[5], pairs[4]), "dp", axis_index_groups=ahead)
        if layer == 2:
            mid = lax.psum((pairs[3], pairs[2]), "dp", axis_index_groups=back)
        if layer > 0:
            below = layer - 1
            late = (in_hbm(upper[0]),) if layer == 1 else ()
            dn, msg = below_step(
                below, layer == middle, total, pos, kept_z[below], kept_st[below], tables[0], terms, (keep, *settled, *late)
            )
        else:
            grad = last_step(terms, (pairs[0], pairs[1]))
    tied, upper = lax.optimization_barrier(((pairs[1], pairs[0]), upper))
    lower = lax.psum(tied, "dp", axis_index_groups=ahead)
    shape = (images, rows_here, width, LANES)
    grad, mid = lax.optimization_barrier((grad, mid))
    outputs = (from_maps(h_last.reshape(shape)), from_maps(grad.reshape(shape)))
    whole = place_step((5, 4, 3, 2), pos, with_other((*upper, *mid)), None, layers)
    sums = jnp.stack(sum_list)
    sums = (sums[:, 1], sums[:, 0])
    lower, whole, outputs, sums = lax.optimization_barrier((lower, whole, outputs, sums))
    whole = place_step((1, 0), pos, with_other(lower), whole, layers)
    return (*outputs, whole, *sums)


def solution(mesh):
    in_specs = (
        P("dp", "rows", "tensor"),
        P(None, "tensor", None),
        P(None, "tensor"),
        P(None, "tensor"),
        P("dp", "rows", "tensor"),
        P("dp", "rows", None),
    )
    out_specs = (
        P("dp", "rows", "tensor"),
        P("dp", "rows", "tensor"),
        P(None, "tensor", None),
        P(None, "tensor"),
        P(None, "tensor"),
    )
    local = fast_local if fits_kernels(mesh) else generic_local
    return jax.shard_map(local, mesh=mesh, in_specs=in_specs, out_specs=out_specs, check_vma=False)
```

```python
import functools

import jax
import jax.numpy as jnp
from jax import lax
from jax.experimental import pallas as pl
from jax.experimental.pallas import tpu as pltpu
from jax.sharding import PartitionSpec as P

EPS = 1e-05


def padded_2(cells, sides, width):
    for axis, dim in sides:
        count = lax.axis_size(axis)
        ends = count - 1
        head = lax.slice_in_dim(cells, 0, width, axis=dim)
        tail = lax.slice_in_dim(cells, cells.shape[dim] - width, cells.shape[dim], axis=dim)
        cells = jnp.concatenate(
            [
                lax.ppermute(tail, axis, [(i, (i + 1) % count) for i in range(ends)]),
                cells,
                lax.ppermute(head, axis, [((i + 1) % count, i) for i in range(ends)]),
            ],
            axis=dim,
        )
    return cells


def to_maps(flat, width):
    count, high, merged = flat.shape
    return flat.reshape(count, high, merged // width, width).transpose(0, 1, 3, 2)


def from_maps(maps):
    count, high, wide, chans = maps.shape
    return maps.transpose(0, 1, 3, 2).reshape(count, high, chans * wide)


def spatial_conv(padded, kernel):
    return lax.conv_general_dilated(
        padded,
        kernel,
        (1, 1),
        ((0, 0), (1, 1)),
        dimension_numbers=("NHWC", "HWIO", "NHWC"),
        preferred_element_type=jnp.float32,
    )


def flipped(kernel):
    return jnp.transpose(kernel[::-1, ::-1], (0, 1, 3, 2))


def pool_unpool(values):
    count, high, wide, chans = values.shape
    blocks = values.reshape(count, high // 2, 2, wide // 2, 2, chans)
    pooled = jax.nn.logsumexp(blocks, axis=(2, 4), keepdims=True)
    return (jnp.exp(blocks - pooled) * pooled).reshape(values.shape)


def moments(conv_out, total_pixels):
    summed = lax.psum(jnp.sum(conv_out, axis=(0, 1, 2)), ("dp", "rows"))
    mean = summed / total_pixels
    spread = lax.psum(jnp.sum(jnp.square(conv_out - mean), axis=(0, 1, 2)), ("dp", "rows"))
    var = spread / total_pixels
    return (mean, lax.rsqrt(var + EPS))


def kernel_grad(whole, dconv):
    images, rows_here, width, chans = dconv.shape
    widened = jnp.pad(whole, ((0, 0), (0, 0), (1, 1), (0, 0)))
    stacked = []
    for row_off in range(3):
        line = []
        for col_off in range(3):
            window = widened[:, row_off : row_off + rows_here, col_off : col_off + width, :]
            line.append(
                jnp.einsum("bhwc,bhwo->co", window, dconv, preferred_element_type=jnp.float32)
            )
        stacked.append(jnp.stack(line))
    return jnp.stack(stacked)


def generic_local(section_input, conv_weights, norm_gains, norm_shifts, out_grad, out_mask):
    width = out_mask.shape[2]
    images, rows_here = (out_mask.shape[0], out_mask.shape[1])
    total_pixels = float(images * rows_here * width * lax.axis_size("dp") * lax.axis_size("rows"))
    layers, out_here, flat_in = conv_weights.shape
    chans_in = flat_in // 9
    kernels_hwio = conv_weights.reshape(layers, out_here, 3, 3, chans_in).transpose(0, 2, 3, 4, 1)
    middle = layers // 2
    kept = []
    acting = to_maps(section_input, width)
    current = acting.astype(jnp.float32)
    pre_pool = current
    for index in range(layers):
        if index == middle:
            pre_pool = current
            acting = pool_unpool(pre_pool).astype(jnp.bfloat16)
        padded = padded_2(acting, (("rows", 1),), 1)
        whole = lax.all_gather(padded, "tensor", axis=3, tiled=True)
        conv_out = spatial_conv(whole, kernels_hwio[index])
        mean, rstd = moments(conv_out, total_pixels)
        normed = (conv_out - mean) * rstd
        shifted = normed * norm_gains[index] + norm_shifts[index]
        current = jax.nn.silu(shifted)
        acting = current.astype(jnp.bfloat16)
        kept.append((whole, normed, shifted, rstd))
    grad = to_maps(out_grad, width).astype(jnp.float32) * out_mask[..., None].astype(jnp.float32)
    kernel_list = [None] * layers
    gain_list = [None] * layers
    shift_list = [None] * layers
    for index in range(layers - 1, -1, -1):
        whole, normed, shifted, rstd = kept[index]
        unused, pull_silu = jax.vjp(jax.nn.silu, shifted)
        dshift = pull_silu(grad)[0]
        gain_sum, shift_sum = lax.psum(
            (jnp.sum(dshift * normed, axis=(0, 1, 2)), jnp.sum(dshift, axis=(0, 1, 2))),
            ("dp", "rows"),
        )
        gain_list[index] = gain_sum
        shift_list[index] = shift_sum
        dconv = (
            norm_gains[index]
            * rstd
            * (dshift - shift_sum / total_pixels - normed * gain_sum / total_pixels)
        ).astype(jnp.bfloat16)
        summed_kernel = lax.psum(
            kernel_grad(whole, dconv).astype(jnp.bfloat16), ("dp", "rows")
        ).astype(jnp.float32)
        kernel_list[index] = summed_kernel.transpose(3, 0, 1, 2).reshape(out_here, flat_in)
        grad_rim = padded_2(dconv, (("rows", 1),), 1)
        partial_terms = spatial_conv(grad_rim, flipped(kernels_hwio[index]))
        grad_in = lax.psum_scatter(
            partial_terms.astype(jnp.bfloat16), "tensor", scatter_dimension=3, tiled=True
        ).astype(jnp.float32)
        if index == middle:
            unused, pull_pool = jax.vjp(pool_unpool, pre_pool)
            grad = pull_pool(grad_in)[0]
        else:
            grad = grad_in
    return (
        from_maps(acting),
        from_maps(grad),
        jnp.stack(kernel_list),
        jnp.stack(gain_list),
        jnp.stack(shift_list),
    )


GROUPS = 4
LANES = 128
WIDE = 48
CHANS = GROUPS * LANES
F32 = jnp.float32
BF16 = jnp.bfloat16
VMEM = pl.BlockSpec(memory_space=pltpu.VMEM)
SMEM = pl.BlockSpec(memory_space=pltpu.SMEM)
ANY = pl.BlockSpec(memory_space=pltpu.HBM)
FREE = pl.BlockSpec(memory_space=pl.ANY)
LITTLE = pl.CostEstimate(flops=1024, bytes_accessed=1024, transcendentals=0)
PARAMS = pltpu.CompilerParams(vmem_limit_bytes=20 * 1024 * 1024)


def in_hbm(value):
    return pltpu.with_memory_space_constraint(value, pltpu.HBM)


def fits_kernels(mesh):
    return mesh.shape["tensor"] == GROUPS and mesh.shape["rows"] == 2 and mesh.shape["dp"] == 4


def sigmoid(v):
    return 0.5 * jnp.tanh(0.5 * v) + 0.5


def swap_columns(v):
    column = lax.broadcasted_iota(jnp.int32, v.shape, 0)
    return jnp.where(column % 2 == 0, pltpu.roll(v, WIDE - 1, 0), pltpu.roll(v, 1, 0))


def soft_parts(h):
    top = jnp.maximum(h[0], h[1])
    top = jnp.maximum(top, swap_columns(top))
    e0, e1 = jnp.exp(h[0] - top), jnp.exp(h[1] - top)
    total = e0 + e1
    total = total + swap_columns(total)
    pooled = top + jnp.log(total)
    inverse = 1.0 / total
    return e0 * inverse, e1 * inverse, pooled


def soft(h):
    h = h.reshape(2, WIDE, LANES)
    q0, q1, pooled = soft_parts(h)
    return jnp.concatenate([q0 * pooled, q1 * pooled], axis=0)


def soft_pull(h, grad):
    h = h.reshape(2, WIDE, LANES)
    grad = grad.reshape(2, WIDE, LANES)
    q0, q1, pooled = soft_parts(h)
    mix = q0 * grad[0] + q1 * grad[1]
    mix = mix + swap_columns(mix)
    return jnp.concatenate(
        [q0 * (pooled * (grad[0] - mix) + mix), q1 * (pooled * (grad[1] - mix) + mix)], axis=0
    )


def norm_tables(st, group, i_own, i_oth, n_local, total):
    parts = st.shape[0]
    if parts == 2:
        mean, rstd = st[0, 0, 0:1], lax.rsqrt(st[0, 0, 1:2] / total + EPS)
        return rstd, (st[1, 0, 0:1] - mean) * rstd, (st[1, 0, 1:2] - mean) * rstd
    group = 0 if st.shape[1] == 1 else group
    blocks = [st[i, group] for i in range(parts)]
    summed = functools.reduce(jnp.add, blocks)
    mean = summed[0:1] / parts
    apart = functools.reduce(jnp.add, [jnp.square(b - mean) for b in blocks])
    rstd = lax.rsqrt((summed[1:2] + n_local * apart[0:1]) / total + EPS)
    return rstd, (st[i_own, group, 0:1] - mean) * rstd, (st[i_oth, group, 0:1] - mean) * rstd


def left_right(y0, y1, y2):
    rows = y0.shape[0]
    column = lax.broadcasted_iota(jnp.int32, y0.shape, 0) % WIDE
    before = jnp.where(column == 0, 0.0, pltpu.roll(y0, 1, 0))
    after = jnp.where(column == WIDE - 1, 0.0, pltpu.roll(y2, rows - 1, 0))
    return before + y1 + after


def lane_of(group):
    return pl.multiple_of(group * LANES, LANES)


def edge_start(n_own, edge, half):
    return pl.multiple_of((1 - half) * (n_own - edge), WIDE)


def pair_rows(j):
    return pl.ds(pl.multiple_of(j * 2 * WIDE, 2 * WIDE), 2 * WIDE)


def fold(v):
    return jnp.sum(v.reshape(v.shape[0] // 8, 8, LANES), axis=0)


def fwd_kernel(first, last, pool, layer, total, edge_out, *refs):
    pos, zall = refs[0], refs[1]
    if first:
        w_hbm = refs[2]
    else:
        st, gss, w_hbm = refs[2], refs[3:7], refs[7]
    if last:
        hb_out, zc_out, edge_ref, st_out, w, hb, y, z, tab, hs, sem = refs[-11:]
    else:
        hb_out, zc_out, edge_ref, st_out, hb, w, y, z, tab, hs, sem = refs[-11:]
    load = pltpu.make_async_copy(w_hbm.at[layer], w, sem.at[0])
    load.start()
    saves = []
    t, r = pos[0], pos[1]
    n_own = z.shape[0]
    halo_at = pl.multiple_of((1 - r) * (n_own + WIDE), WIDE)
    zero_at = pl.multiple_of(r * (n_own + WIDE), WIDE)
    hb[pl.ds(zero_at, WIDE), :] = jnp.zeros((WIDE, CHANS), BF16)
    edge = zall.shape[0] - n_own
    if not first:
        for k in range(GROUPS):
            group = t ^ k
            rstd, own, oth = norm_tables(st, group, pos[2], pos[3], float(n_own), total)
            gain, shift = gss[k][layer - 1 : layer, :], gss[k][layer + 7 : layer + 8, :]
            tab[group, 0:1] = rstd * gain
            tab[group, 1:2] = own * gain + shift
            tab[group, 2:3] = oth * gain + shift

    def act(values, group, which):
        if first:
            return values
        n = values.astype(F32) * tab[group, 0:1, :] + tab[group, which : which + 1, :]
        h = n * sigmoid(n)
        return soft(h) if pool else h

    for group in range(GROUPS):
        lanes = slice(group * LANES, (group + 1) * LANES)
        h = act(zall[n_own : n_own + edge, lanes], group, 2)
        if edge > WIDE:
            hs[...] = h
            h = hs[pl.ds(pl.multiple_of(r * WIDE, WIDE), WIDE), :]
        hb[pl.ds(halo_at, WIDE), lanes] = h.astype(BF16)
    pair, block = 2 * WIDE, n_own // 3
    steps, made = n_own // pair, 0
    summed = jnp.zeros((8, LANES), F32)
    for part in range(3):
        first_row = part * block
        while made < min(steps, (first_row + block + WIDE + pair - 1) // pair):
            at = made * pair
            for group in range(GROUPS):
                lanes = slice(group * LANES, (group + 1) * LANES)
                h = act(zall[at : at + pair, lanes], group, 1)
                hb[at + WIDE : at + WIDE + pair, lanes] = h.astype(BF16)
            made += 1
        if part == 0:
            load.wait()
            rhs = jnp.concatenate(
                [
                    jnp.concatenate([w[:, (3 * i + s) * CHANS : (3 * i + s + 1) * CHANS] for i in range(3)], axis=1)
                    for s in range(3)
                ],
                axis=0,
            )
        start, stop = (0 if part == 0 else first_row + 2 * WIDE), first_row + block + 2 * WIDE
        saves.append(
            pltpu.make_async_copy(hb.at[start:stop], hb_out.at[layer, start:stop], sem.at[1 + part])
        )
        saves[-1].start()
        lhs = jnp.concatenate([hb[first_row + i * WIDE : first_row + i * WIDE + block, :] for i in range(3)], axis=1)
        rows = slice(first_row, first_row + block)
        y[rows, :] = lax.dot_general(lhs, rhs, (((1,), (1,)), ((), ())), preferred_element_type=F32)
        for j in range(block // pair):
            rows = slice(first_row + j * pair, first_row + (j + 1) * pair)
            v = left_right(y[rows, 0:128], y[rows, 128:256], y[rows, 256:384])
            z[rows, :] = v
            summed = summed + fold(v)
    mean = jnp.sum(summed, axis=0, keepdims=True) / n_own
    apart = jnp.zeros((8, LANES), F32)
    for j in range(steps):
        rows = slice(j * pair, (j + 1) * pair)
        v = z[rows, :] - mean
        zc_out[rows, :] = v.astype(BF16)
        apart = apart + fold(jnp.square(v))
    sums = jnp.concatenate([mean, jnp.sum(apart, axis=0, keepdims=True)], axis=0)
    st_out[...] = sums
    edge_ref[...] = zc_out[pl.ds(edge_start(n_own, edge_out, r), edge_out), :]
    zc_out[n_own : n_own + edge_out, :] = jnp.zeros((edge_out, LANES), BF16)
    for save in saves:
        save.wait()


def fwd_step(layer, pool, edge_out, total, pos, slots, st, tables, weights, kept, n_own, ties):
    first = st is None
    layers = weights.shape[0]
    extra = () if first else (st, *tables)
    last = layer + 1 == layers
    kernels = pltpu.VMEM((LANES, 9 * CHANS), BF16)
    return pl.pallas_call(
        functools.partial(fwd_kernel, first, last, pool, layer, total, edge_out),
        out_shape=(
            pltpu.HBM((layers, n_own + 2 * WIDE, CHANS), BF16),
            pltpu.VMEM((n_own + edge_out, LANES), BF16),
            pltpu.VMEM((edge_out, LANES), BF16),
            pltpu.VMEM((2, LANES), F32),
            *((kernels,) if last else ()),
        ),
        in_specs=[SMEM] + [VMEM] * (1 + len(extra)) + [ANY] * (1 if first else 2) + [FREE] * len(ties),
        out_specs=(ANY, VMEM, VMEM, VMEM) + ((VMEM,) if last else ()),
        input_output_aliases={} if first else {3 + len(extra): 0},
        scratch_shapes=[
            pltpu.VMEM((n_own + 2 * WIDE, CHANS), BF16),
            *(() if last else (kernels,)),
            pltpu.VMEM((n_own, 3 * LANES), F32),
            pltpu.VMEM((n_own, LANES), F32),
            pltpu.VMEM((GROUPS, 8, LANES), F32),
            pltpu.VMEM((2 * WIDE, LANES), F32),
            pltpu.SemaphoreType.DMA((4,)),
        ],
        compiler_params=PARAMS,
        cost_estimate=pl.CostEstimate(
            flops=2 * n_own * 9 * CHANS * LANES, bytes_accessed=4 * 1024 * 1024, transcendentals=n_own * CHANS
        ),
        name="conv_forward",
    )(pos, slots, *extra, in_hbm(weights), *(() if first else (in_hbm(kept),)), *ties)


def below_kernel(layer, pool, total, top, *refs):
    pos, zc, st, gs = refs[:4]
    if top:
        terms, h_out, dn_out, msg, tab = refs[4:]
    else:
        terms, (dn_out, msg, tab) = refs[4:8], refs[-3:]
    n_own = dn_out.shape[0]
    rstd, own, oth = norm_tables(st, pos[0], pos[2], pos[3], float(n_own), total)
    tab[0:1], tab[1:2] = rstd, own
    tab[2:3], tab[3:4] = gs[layer : layer + 1, :], gs[layer + 8 : layer + 9, :]

    def body(j, accs):
        rows = pair_rows(j)
        xhat = zc[rows, :].astype(F32) * tab[0:1, :] + tab[1:2, :]
        n = xhat * tab[2:3, :] + tab[3:4, :]
        sig = sigmoid(n)
        h = n * sig
        if top:
            g = terms[rows, :].astype(F32)
            h_out[rows, :] = h.astype(BF16)
        else:
            g = functools.reduce(jnp.add, [term[rows, :].astype(F32) for term in terms])
        if pool:
            g = soft_pull(h, g)
        dn = g * (sig * (1.0 + n - h))
        dn_out[rows, :] = dn
        return accs[0] + fold(dn), accs[1] + fold(dn * xhat)

    zero = jnp.zeros((8, LANES), F32)
    sums = lax.fori_loop(0, n_own // (2 * WIDE), body, (zero, zero), unroll=3)
    sums = [jnp.sum(v, axis=0, keepdims=True) for v in sums]
    msg[0:WIDE, :] = dn_out[pl.ds(edge_start(n_own, WIDE, pos[1]), WIDE), :]
    msg[WIDE : WIDE + 8, :] = jnp.concatenate(sums + [jnp.zeros((6, LANES), F32)], axis=0)


def below_step(layer, pool, total, pos, zc, st, gs, terms, ties=()):
    n_own = terms[0].shape[0]
    top = len(terms) == 1
    out_shape = [
        pltpu.VMEM((n_own, LANES), F32),
        pltpu.VMEM((WIDE + 8, LANES), F32),
    ]
    if top:
        out_shape = [jax.ShapeDtypeStruct((n_own, LANES), BF16)] + out_shape
    return pl.pallas_call(
        functools.partial(below_kernel, layer, pool, total, top),
        out_shape=tuple(out_shape),
        in_specs=[SMEM] + [VMEM] * (3 + len(terms)) + [FREE] * len(ties),
        out_specs=(VMEM,) * len(out_shape),
        scratch_shapes=[pltpu.VMEM((8, LANES), F32)],
        compiler_params=PARAMS,
        cost_estimate=LITTLE,
        name="silu_backward",
    )(pos, zc, st, gs, *terms, *ties)


def bwd_kernel(layer, total, *refs):
    pos, dn, dedge, sums, zc, st, gs, w = refs[:8]
    outs, d_out, d, y, tab = refs[-8:-4], *refs[-4:]
    t, r = pos[0], pos[1]
    n_own = dn.shape[0]
    halo_at = pl.multiple_of((1 - r) * (n_own + WIDE), WIDE)
    zero_at = pl.multiple_of(r * (n_own + WIDE), WIDE)
    edge = zc.shape[0] - n_own
    d[pl.ds(zero_at, WIDE), :] = jnp.zeros((WIDE, 3 * LANES), BF16)
    rstd, own, oth = norm_tables(st, t, pos[2], pos[3], float(n_own), total)
    scale = gs[layer : layer + 1, :] * rstd
    shift_sum, gain_sum = sums[0:1, :], sums[1:2, :]
    slope = scale * gain_sum / total
    tab[0:1] = scale
    tab[1:2] = slope * rstd
    tab[2:3] = scale * shift_sum / total + slope * own
    tab[3:4] = scale * shift_sum / total + slope * oth

    def spread_columns(v):
        rows = v.shape[0]
        column = lax.broadcasted_iota(jnp.int32, v.shape, 0) % WIDE
        ahead = jnp.where(column == WIDE - 1, 0.0, pltpu.roll(v, rows - 1, 0))
        behind = jnp.where(column == 0, 0.0, pltpu.roll(v, 1, 0))
        return jnp.concatenate([ahead.astype(BF16), v.astype(BF16), behind.astype(BF16)], axis=1)

    near = n_own if edge == WIDE else pl.multiple_of(n_own + r * WIDE, WIDE)
    near = zc[pl.ds(near, WIDE), :].astype(F32)
    d[pl.ds(halo_at, WIDE), :] = spread_columns(dedge[0:WIDE, :] * tab[0:1, :] - tab[3:4, :] - near * tab[1:2, :])
    pair, block = 2 * WIDE, n_own // 3
    steps, made = n_own // pair, 0
    for part in range(3):
        first_row = part * block
        while made < min(steps, (first_row + block + WIDE + pair - 1) // pair):
            at = made * pair
            v = dn[at : at + pair, :] * tab[0:1, :] - tab[2:3, :] - zc[at : at + pair, :].astype(F32) * tab[1:2, :]
            v = spread_columns(v)
            d[at + WIDE : at + WIDE + pair, :] = v
            d_out[at : at + pair, :] = v
            made += 1
        if part == 0:
            rhs = jnp.concatenate([w[:, i * CHANS : (i + 1) * CHANS] for i in range(9)], axis=0)
        windows = [first_row + (2 - i) * WIDE for i in range(3)]
        lhs = jnp.concatenate([d[at : at + block, :] for at in windows], axis=1)
        y[first_row : first_row + block, :] = jnp.dot(lhs, rhs, preferred_element_type=F32)
        for j in range(block // pair):
            rows = slice(first_row + j * pair, first_row + (j + 1) * pair)
            for k in range(GROUPS):
                outs[k][rows, :] = y[rows, pl.ds(lane_of(t ^ k), LANES)].astype(BF16)


def bwd_step(layer, total, pos, dn, dedge, sums, zc, st, gs, w, ties):
    n_own = dn.shape[0]
    part = pltpu.VMEM((n_own, LANES), BF16)
    return pl.pallas_call(
        functools.partial(bwd_kernel, layer, total),
        out_shape=(part, part, part, part, pltpu.VMEM((n_own, 3 * LANES), BF16)),
        in_specs=[SMEM] + [VMEM] * 7 + [FREE] * len(ties),
        out_specs=(VMEM,) * 5,
        scratch_shapes=[
            pltpu.VMEM((n_own + 2 * WIDE, 3 * LANES), BF16),
            pltpu.VMEM((n_own, CHANS), F32),
            pltpu.VMEM((8, LANES), F32),
        ],
        compiler_params=PARAMS,
        cost_estimate=LITTLE,
        name="conv_backward",
    )(pos, dn, dedge, sums, zc, st, gs, pltpu.with_memory_space_constraint(w, pltpu.VMEM), *ties)


def last_kernel(t0, t1, t2, t3, *refs):
    out = refs[-1]

    def body(j, carry):
        rows = pair_rows(j)
        out[rows, :] = functools.reduce(jnp.add, [term[rows, :].astype(F32) for term in (t0, t1, t2, t3)])
        return carry

    lax.fori_loop(0, out.shape[0] // (2 * WIDE), body, 0)


def last_step(terms, ties):
    return pl.pallas_call(
        last_kernel,
        out_shape=jax.ShapeDtypeStruct(terms[0].shape, F32),
        in_specs=[VMEM] * 4 + [FREE] * len(ties),
        out_specs=VMEM,
        compiler_params=PARAMS,
        cost_estimate=LITTLE,
        name="add_terms",
    )(*terms, *ties)


def halves_kernel(keep, got, out):
    out[...] = (keep[...].astype(F32) + got[...].astype(F32)).astype(BF16)


def add_halves(keep, got):
    return pl.pallas_call(
        halves_kernel,
        out_shape=jax.ShapeDtypeStruct(keep.shape, BF16),
        in_specs=[VMEM] * 2,
        out_specs=VMEM,
        compiler_params=PARAMS,
        cost_estimate=LITTLE,
        name="add_halves",
    )(keep, got)


def quarters_kernel(parts, *refs):
    out = refs[-1]
    total = functools.reduce(jnp.add, [parts[i].astype(F32) for i in range(4)]).astype(BF16)
    for i in range(4):
        out[i] = total


def add_quarters(parts, ties):
    return pl.pallas_call(
        quarters_kernel,
        out_shape=pltpu.VMEM(parts.shape, BF16),
        in_specs=[VMEM] + [FREE] * len(ties),
        out_specs=VMEM,
        compiler_params=PARAMS,
        cost_estimate=LITTLE,
        name="add_quarters",
    )(parts, *ties)


def wgrad_kernel(layer, pos, d, hb_hbm, *refs):
    if layer > 0:
        w_hbm, keep, send, w, hb, grad, sem = refs
        fetch = pltpu.make_async_copy(w_hbm.at[layer - 1], w, sem.at[1])
    else:
        keep, send, hb, grad, sem = refs
    load = pltpu.make_async_copy(hb_hbm.at[layer], hb, sem.at[0])
    load.start()
    if layer > 0:
        fetch.start()
    n_own = d.shape[0]
    lhs = d[...]
    load.wait()
    for i in range(3):
        part = lax.dot_general(
            lhs, hb[i * WIDE : i * WIDE + n_own, :], (((0,), (0,)), ((), ())), preferred_element_type=F32
        ).astype(BF16)
        for s in range(3):
            grad[:, (3 * i + s) * CHANS : (3 * i + s + 1) * CHANS] = part[s * LANES : (s + 1) * LANES]
    half = LANES // 2
    keep[...] = grad[pl.ds(pl.multiple_of(pos[1] * half, half), half), :]
    send[...] = grad[pl.ds(pl.multiple_of((1 - pos[1]) * half, half), half), :]
    if layer > 0:
        fetch.wait()


def wgrad_step(layer, pos, d, kept, weights):
    half = pltpu.VMEM((LANES // 2, 9 * CHANS), BF16)
    more = layer > 0
    return pl.pallas_call(
        functools.partial(wgrad_kernel, layer),
        out_shape=(half, half) + ((pltpu.VMEM((LANES, 9 * CHANS), BF16),) if more else ()),
        in_specs=[SMEM, VMEM, ANY] + ([ANY] if more else []),
        out_specs=(VMEM,) * (3 if more else 2),
        scratch_shapes=[
            pltpu.VMEM(kept.shape[1:], BF16),
            pltpu.VMEM((LANES, 9 * CHANS), BF16),
            pltpu.SemaphoreType.DMA((2,)),
        ],
        compiler_params=PARAMS,
        cost_estimate=LITTLE,
        name="kernel_gradient",
    )(pos, d, in_hbm(kept), *((in_hbm(weights),) if more else ()))


def place_kernel(layers, fresh, pos, *refs):
    count = 2 * len(layers)
    sources = refs[:count]
    out, held, wide, sem = refs[-4:]
    half = LANES // 2
    r = pos[1]
    loads = [pltpu.make_async_copy(sources[j], held.at[j], sem.at[j]) for j in range(count)]
    for load in loads:
        load.start()
    stores = []
    for j in range(count):
        at = pl.multiple_of((r if j % 2 == 0 else 1 - r) * half, half)
        if j >= 4:
            stores[j - 4].wait()
        loads[j].wait()
        wide[j % 4] = held[j].astype(F32)
        store = pltpu.make_async_copy(wide.at[j % 4], out.at[layers[j // 2], pl.ds(at, half)], sem.at[count + j])
        store.start()
        stores.append(store)
    for store in stores[-4:]:
        store.wait()


def place_step(layers, pos, sources, whole, count):
    half = LANES // 2
    jobs = len(sources)
    return pl.pallas_call(
        functools.partial(place_kernel, layers, whole is None),
        out_shape=pltpu.HBM((count, LANES, 9 * CHANS), F32),
        in_specs=[SMEM] + [FREE] * jobs + ([] if whole is None else [ANY]),
        out_specs=ANY,
        input_output_aliases={} if whole is None else {1 + jobs: 0},
        scratch_shapes=[
            pltpu.VMEM((jobs, half, 9 * CHANS), BF16),
            pltpu.VMEM((4, half, 9 * CHANS), F32),
            pltpu.SemaphoreType.DMA((2 * jobs,)),
        ],
        compiler_params=PARAMS,
        cost_estimate=LITTLE,
        name="place_gradients",
    )(pos, *sources, *(() if whole is None else (in_hbm(whole),)))


def swap_with(value, axis, k):
    return lax.ppermute(value, axis, [(i, i ^ k) for i in range(lax.axis_size(axis))])


def spread(own):
    return (own, *[swap_with(own, "tensor", k) for k in range(1, GROUPS)])


def share_moments(mine, count):
    other = swap_with(mine, "rows", 1)
    mean = 0.5 * (mine[0:1] + other[0:1])
    apart = mine[1:2] + other[1:2] + (0.5 * count) * jnp.square(other[0:1] - mine[0:1])
    own = jnp.concatenate([mean, apart], axis=0)
    all_four = [own] + [swap_with(own, "dp", k) for k in (1, 2, 3)]
    mean = 0.25 * functools.reduce(jnp.add, [v[0:1] for v in all_four])
    apart = functools.reduce(jnp.add, [v[1:2] + (2.0 * count) * jnp.square(v[0:1] - mean) for v in all_four])
    return jnp.concatenate([mean, apart, mine[0:1], other[0:1]], axis=0).reshape(2, 1, 2, LANES)


def halo_of_input(x, half):
    n_own = x.shape[0]
    edge = jnp.where(half == 0, x[n_own - WIDE :], x[:WIDE])
    return jnp.concatenate([x, swap_with(edge, "rows", 1)], axis=0)


def fast_local(section_input, conv_weights, norm_gains, norm_shifts, out_grad, out_mask):
    images, rows_here, width = out_mask.shape
    layers = conv_weights.shape[0]
    n_own = rows_here * width
    parts = lax.axis_size("dp") * lax.axis_size("rows")
    total = float(n_own * parts)
    t, half = lax.axis_index("tensor"), lax.axis_index("rows")
    image = lax.axis_index("dp")
    pos = jnp.stack([t, half, 2 * image + half, 2 * image + 1 - half]).astype(jnp.int32)
    middle = layers // 2
    x = to_maps(section_input, width).reshape(n_own, LANES)
    slots = lax.all_gather(halo_of_input(x, half), "tensor", axis=1, tiled=True)
    pad = jnp.zeros((8 - layers, LANES), F32)
    tables = spread(jnp.concatenate([norm_gains, pad, norm_shifts, pad], axis=0))
    top_grad = (to_maps(out_grad, width) * out_mask[..., None].astype(BF16)).reshape(n_own, LANES)

    st, kept = None, None
    halves = ("dp", "rows")
    kept_z, kept_st = [], []
    for layer in range(layers):
        last = layer + 1 == layers
        edge = 2 * WIDE if layer + 1 == middle else WIDE
        everyone = ("dp", "rows", "tensor")
        kept, zc, rim, local, *w = fwd_step(
            layer,
            layer == middle,
            edge,
            total,
            pos,
            slots,
            st,
            tables,
            conv_weights,
            kept,
            n_own,
            (top_grad,) if layer == 2 else (),
        )
        rim = swap_with(rim, "rows", 1)
        if last:
            st = share_moments(local, float(n_own))
        else:
            local = jnp.broadcast_to(local, (parts * GROUPS, 2, LANES))
            st = lax.all_to_all(local, everyone, split_axis=0, concat_axis=0, tiled=True)
            st = st.reshape(parts, GROUPS, 2, LANES)
        zc = lax.dynamic_update_slice_in_dim(zc, rim, n_own, axis=0)
        kept_z.append(zc)
        kept_st.append(st)
        if not last:
            slots = lax.all_gather(zc, "tensor", axis=1, tiled=True)
    top = layers - 1
    w = w[0]
    h_last, dn, msg = below_step(top, False, total, pos, kept_z[top], kept_st[top], tables[0], (top_grad,))

    def with_other(values):
        return [v for mine in values for v in (in_hbm(mine), swap_with(mine, "rows", 1))]

    sum_list, pairs = [None] * layers, [None] * layers
    ahead, back = [[0, 1, 3, 2]], [[2, 3, 1, 0]]
    urgent = ()
    for layer in range(layers - 1, -1, -1):
        got = swap_with(msg, "rows", 1)
        sums = msg[WIDE:] + got[WIDE:]
        one, two, three = (swap_with(sums, "dp", k) for k in (1, 2, 3))
        sums = (sums + one) + (two + three)
        sum_list[layer] = sums
        *terms, d = bwd_step(
            layer, total, pos, dn, got, sums, kept_z[layer], kept_st[layer], tables[0], w, urgent
        )
        terms = (terms[0], *[swap_with(terms[k], "tensor", k) for k in range(1, GROUPS)])
        keep, send, *w = wgrad_step(layer, pos, d, kept, conv_weights)
        w = w[0] if w else None
        other = swap_with(send, "rows", 1)
        pairs[layer] = add_halves(keep, other)
        urgent, settled = (other,), (() if layer + 1 == layers else (pairs[layer + 1],))
        if layer == 4:
            upper = lax.psum((pairs[5], pairs[4]), "dp", axis_index_groups=ahead)
        if layer == 2:
            mid = lax.psum((pairs[3], pairs[2]), "dp", axis_index_groups=back)
        if layer > 0:
            below = layer - 1
            late = (in_hbm(upper[0]),) if layer == 1 else ()
            dn, msg = below_step(
                below, layer == middle, total, pos, kept_z[below], kept_st[below], tables[0], terms, (keep, *settled, *late)
            )
        else:
            grad = last_step(terms, (pairs[0], pairs[1]))
    pieces = pairs[0].reshape(4, LANES // 8, -1)
    pieces = lax.all_to_all(pieces, "dp", split_axis=0, concat_axis=0, tiled=True)
    tied, upper = lax.optimization_barrier((pairs[1], upper))
    lower = lax.psum(tied, "dp", axis_index_groups=ahead)
    shape = (images, rows_here, width, LANES)
    grad, mid = lax.optimization_barrier((grad, mid))
    outputs = (from_maps(h_last.reshape(shape)), from_maps(grad.reshape(shape)))
    pieces = lax.all_to_all(add_quarters(pieces, ()), "dp", split_axis=0, concat_axis=0, tiled=True)
    whole = place_step((5, 4, 3, 2), pos, with_other((*upper, *mid)), None, layers)
    sums = jnp.stack(sum_list)
    sums = (sums[:, 1], sums[:, 0])
    pieces, lower, whole, outputs, sums = lax.optimization_barrier((pieces, lower, whole, outputs, sums))
    whole = place_step((1, 0), pos, with_other((lower, pieces.reshape(pairs[0].shape))), whole, layers)
    return (*outputs, whole, *sums)


def solution(mesh):
    in_specs = (
        P("dp", "rows", "tensor"),
        P(None, "tensor", None),
        P(None, "tensor"),
        P(None, "tensor"),
        P("dp", "rows", "tensor"),
        P("dp", "rows", None),
    )
    out_specs = (
        P("dp", "rows", "tensor"),
        P("dp", "rows", "tensor"),
        P(None, "tensor", None),
        P(None, "tensor"),
        P(None, "tensor"),
    )
    local = fast_local if fits_kernels(mesh) else generic_local
    return jax.shard_map(local, mesh=mesh, in_specs=in_specs, out_specs=out_specs, check_vma=False)
```

```python
import functools

import jax
import jax.numpy as jnp
from jax import lax
from jax.experimental import pallas as pl
from jax.experimental.pallas import tpu as pltpu
from jax.sharding import PartitionSpec as P

EPS = 1e-05


def padded_2(cells, sides, width):
    for axis, dim in sides:
        count = lax.axis_size(axis)
        ends = count - 1
        head = lax.slice_in_dim(cells, 0, width, axis=dim)
        tail = lax.slice_in_dim(cells, cells.shape[dim] - width, cells.shape[dim], axis=dim)
        cells = jnp.concatenate(
            [
                lax.ppermute(tail, axis, [(i, (i + 1) % count) for i in range(ends)]),
                cells,
                lax.ppermute(head, axis, [((i + 1) % count, i) for i in range(ends)]),
            ],
            axis=dim,
        )
    return cells


def to_maps(flat, width):
    count, high, merged = flat.shape
    return flat.reshape(count, high, merged // width, width).transpose(0, 1, 3, 2)


def from_maps(maps):
    count, high, wide, chans = maps.shape
    return maps.transpose(0, 1, 3, 2).reshape(count, high, chans * wide)


def spatial_conv(padded, kernel):
    return lax.conv_general_dilated(
        padded,
        kernel,
        (1, 1),
        ((0, 0), (1, 1)),
        dimension_numbers=("NHWC", "HWIO", "NHWC"),
        preferred_element_type=jnp.float32,
    )


def flipped(kernel):
    return jnp.transpose(kernel[::-1, ::-1], (0, 1, 3, 2))


def pool_unpool(values):
    count, high, wide, chans = values.shape
    blocks = values.reshape(count, high // 2, 2, wide // 2, 2, chans)
    pooled = jax.nn.logsumexp(blocks, axis=(2, 4), keepdims=True)
    return (jnp.exp(blocks - pooled) * pooled).reshape(values.shape)


def moments(conv_out, total_pixels):
    summed = lax.psum(jnp.sum(conv_out, axis=(0, 1, 2)), ("dp", "rows"))
    mean = summed / total_pixels
    spread = lax.psum(jnp.sum(jnp.square(conv_out - mean), axis=(0, 1, 2)), ("dp", "rows"))
    var = spread / total_pixels
    return (mean, lax.rsqrt(var + EPS))


def kernel_grad(whole, dconv):
    images, rows_here, width, chans = dconv.shape
    widened = jnp.pad(whole, ((0, 0), (0, 0), (1, 1), (0, 0)))
    stacked = []
    for row_off in range(3):
        line = []
        for col_off in range(3):
            window = widened[:, row_off : row_off + rows_here, col_off : col_off + width, :]
            line.append(
                jnp.einsum("bhwc,bhwo->co", window, dconv, preferred_element_type=jnp.float32)
            )
        stacked.append(jnp.stack(line))
    return jnp.stack(stacked)


def generic_local(section_input, conv_weights, norm_gains, norm_shifts, out_grad, out_mask):
    width = out_mask.shape[2]
    images, rows_here = (out_mask.shape[0], out_mask.shape[1])
    total_pixels = float(images * rows_here * width * lax.axis_size("dp") * lax.axis_size("rows"))
    layers, out_here, flat_in = conv_weights.shape
    chans_in = flat_in // 9
    kernels_hwio = conv_weights.reshape(layers, out_here, 3, 3, chans_in).transpose(0, 2, 3, 4, 1)
    middle = layers // 2
    kept = []
    acting = to_maps(section_input, width)
    current = acting.astype(jnp.float32)
    pre_pool = current
    for index in range(layers):
        if index == middle:
            pre_pool = current
            acting = pool_unpool(pre_pool).astype(jnp.bfloat16)
        padded = padded_2(acting, (("rows", 1),), 1)
        whole = lax.all_gather(padded, "tensor", axis=3, tiled=True)
        conv_out = spatial_conv(whole, kernels_hwio[index])
        mean, rstd = moments(conv_out, total_pixels)
        normed = (conv_out - mean) * rstd
        shifted = normed * norm_gains[index] + norm_shifts[index]
        current = jax.nn.silu(shifted)
        acting = current.astype(jnp.bfloat16)
        kept.append((whole, normed, shifted, rstd))
    grad = to_maps(out_grad, width).astype(jnp.float32) * out_mask[..., None].astype(jnp.float32)
    kernel_list = [None] * layers
    gain_list = [None] * layers
    shift_list = [None] * layers
    for index in range(layers - 1, -1, -1):
        whole, normed, shifted, rstd = kept[index]
        unused, pull_silu = jax.vjp(jax.nn.silu, shifted)
        dshift = pull_silu(grad)[0]
        gain_sum, shift_sum = lax.psum(
            (jnp.sum(dshift * normed, axis=(0, 1, 2)), jnp.sum(dshift, axis=(0, 1, 2))),
            ("dp", "rows"),
        )
        gain_list[index] = gain_sum
        shift_list[index] = shift_sum
        dconv = (
            norm_gains[index]
            * rstd
            * (dshift - shift_sum / total_pixels - normed * gain_sum / total_pixels)
        ).astype(jnp.bfloat16)
        summed_kernel = lax.psum(
            kernel_grad(whole, dconv).astype(jnp.bfloat16), ("dp", "rows")
        ).astype(jnp.float32)
        kernel_list[index] = summed_kernel.transpose(3, 0, 1, 2).reshape(out_here, flat_in)
        grad_rim = padded_2(dconv, (("rows", 1),), 1)
        partial_terms = spatial_conv(grad_rim, flipped(kernels_hwio[index]))
        grad_in = lax.psum_scatter(
            partial_terms.astype(jnp.bfloat16), "tensor", scatter_dimension=3, tiled=True
        ).astype(jnp.float32)
        if index == middle:
            unused, pull_pool = jax.vjp(pool_unpool, pre_pool)
            grad = pull_pool(grad_in)[0]
        else:
            grad = grad_in
    return (
        from_maps(acting),
        from_maps(grad),
        jnp.stack(kernel_list),
        jnp.stack(gain_list),
        jnp.stack(shift_list),
    )


GROUPS = 4
LANES = 128
WIDE = 48
CHANS = GROUPS * LANES
F32 = jnp.float32
BF16 = jnp.bfloat16
VMEM = pl.BlockSpec(memory_space=pltpu.VMEM)
SMEM = pl.BlockSpec(memory_space=pltpu.SMEM)
ANY = pl.BlockSpec(memory_space=pltpu.HBM)
FREE = pl.BlockSpec(memory_space=pl.ANY)
LITTLE = pl.CostEstimate(flops=1024, bytes_accessed=1024, transcendentals=0)
PARAMS = pltpu.CompilerParams(vmem_limit_bytes=20 * 1024 * 1024)


def in_hbm(value):
    return pltpu.with_memory_space_constraint(value, pltpu.HBM)


def fits_kernels(mesh):
    return mesh.shape["tensor"] == GROUPS and mesh.shape["rows"] == 2 and mesh.shape["dp"] == 4


def sigmoid(v):
    return 0.5 * jnp.tanh(0.5 * v) + 0.5


def swap_columns(v):
    column = lax.broadcasted_iota(jnp.int32, v.shape, 0)
    return jnp.where(column % 2 == 0, pltpu.roll(v, WIDE - 1, 0), pltpu.roll(v, 1, 0))


def soft_parts(h):
    top = jnp.maximum(h[0], h[1])
    top = jnp.maximum(top, swap_columns(top))
    e0, e1 = jnp.exp(h[0] - top), jnp.exp(h[1] - top)
    total = e0 + e1
    total = total + swap_columns(total)
    pooled = top + jnp.log(total)
    inverse = 1.0 / total
    return e0 * inverse, e1 * inverse, pooled


def soft(h):
    h = h.reshape(2, WIDE, LANES)
    q0, q1, pooled = soft_parts(h)
    return jnp.concatenate([q0 * pooled, q1 * pooled], axis=0)


def soft_pull(h, grad):
    h = h.reshape(2, WIDE, LANES)
    grad = grad.reshape(2, WIDE, LANES)
    q0, q1, pooled = soft_parts(h)
    mix = q0 * grad[0] + q1 * grad[1]
    mix = mix + swap_columns(mix)
    return jnp.concatenate(
        [q0 * (pooled * (grad[0] - mix) + mix), q1 * (pooled * (grad[1] - mix) + mix)], axis=0
    )


def norm_tables(st, group, i_own, i_oth, n_local, total):
    parts = st.shape[0]
    if parts == 2:
        mean, rstd = st[0, 0, 0:1], lax.rsqrt(st[0, 0, 1:2] / total + EPS)
        return rstd, (st[1, 0, 0:1] - mean) * rstd, (st[1, 0, 1:2] - mean) * rstd
    group = 0 if st.shape[1] == 1 else group
    blocks = [st[i, group] for i in range(parts)]
    summed = functools.reduce(jnp.add, blocks)
    mean = summed[0:1] / parts
    apart = functools.reduce(jnp.add, [jnp.square(b - mean) for b in blocks])
    rstd = lax.rsqrt((summed[1:2] + n_local * apart[0:1]) / total + EPS)
    return rstd, (st[i_own, group, 0:1] - mean) * rstd, (st[i_oth, group, 0:1] - mean) * rstd


def left_right(y0, y1, y2):
    rows = y0.shape[0]
    column = lax.broadcasted_iota(jnp.int32, y0.shape, 0) % WIDE
    before = jnp.where(column == 0, 0.0, pltpu.roll(y0, 1, 0))
    after = jnp.where(column == WIDE - 1, 0.0, pltpu.roll(y2, rows - 1, 0))
    return before + y1 + after


def lane_of(group):
    return pl.multiple_of(group * LANES, LANES)


def edge_start(n_own, edge, half):
    return pl.multiple_of((1 - half) * (n_own - edge), WIDE)


def pair_rows(j):
    return pl.ds(pl.multiple_of(j * 2 * WIDE, 2 * WIDE), 2 * WIDE)


def fold(v):
    return jnp.sum(v.reshape(v.shape[0] // 8, 8, LANES), axis=0)


def fwd_kernel(first, last, pool, layer, total, edge_out, *refs):
    pos, zall = refs[0], refs[1]
    if first:
        w_hbm = refs[2]
    else:
        st, gss, w_hbm = refs[2], refs[3:7], refs[7]
    if last:
        hb_out, zc_out, edge_ref, st_out, w, hb, y, z, tab, hs, sem = refs[-11:]
    else:
        hb_out, zc_out, edge_ref, st_out, hb, w, y, z, tab, hs, sem = refs[-11:]
    load = pltpu.make_async_copy(w_hbm.at[layer], w, sem.at[0])
    load.start()
    saves = []
    t, r = pos[0], pos[1]
    n_own = z.shape[0]
    halo_at = pl.multiple_of((1 - r) * (n_own + WIDE), WIDE)
    zero_at = pl.multiple_of(r * (n_own + WIDE), WIDE)
    hb[pl.ds(zero_at, WIDE), :] = jnp.zeros((WIDE, CHANS), BF16)
    edge = zall.shape[0] - n_own
    if not first:
        for k in range(GROUPS):
            group = t ^ k
            rstd, own, oth = norm_tables(st, group, pos[2], pos[3], float(n_own), total)
            gain, shift = gss[k][layer - 1 : layer, :], gss[k][layer + 7 : layer + 8, :]
            tab[group, 0:1] = rstd * gain
            tab[group, 1:2] = own * gain + shift
            tab[group, 2:3] = oth * gain + shift

    def act(values, group, which):
        if first:
            return values
        n = values.astype(F32) * tab[group, 0:1, :] + tab[group, which : which + 1, :]
        h = n * sigmoid(n)
        return soft(h) if pool else h

    for group in range(GROUPS):
        lanes = slice(group * LANES, (group + 1) * LANES)
        h = act(zall[n_own : n_own + edge, lanes], group, 2)
        if edge > WIDE:
            hs[...] = h
            h = hs[pl.ds(pl.multiple_of(r * WIDE, WIDE), WIDE), :]
        hb[pl.ds(halo_at, WIDE), lanes] = h.astype(BF16)
    pair, block = 2 * WIDE, n_own // 3
    steps, made = n_own // pair, 0
    summed = jnp.zeros((8, LANES), F32)
    for part in range(3):
        first_row = part * block
        while made < min(steps, (first_row + block + WIDE + pair - 1) // pair):
            at = made * pair
            for group in range(GROUPS):
                lanes = slice(group * LANES, (group + 1) * LANES)
                h = act(zall[at : at + pair, lanes], group, 1)
                hb[at + WIDE : at + WIDE + pair, lanes] = h.astype(BF16)
            made += 1
        if part == 0:
            load.wait()
            rhs = jnp.concatenate(
                [
                    jnp.concatenate([w[:, (3 * i + s) * CHANS : (3 * i + s + 1) * CHANS] for i in range(3)], axis=1)
                    for s in range(3)
                ],
                axis=0,
            )
        start, stop = (0 if part == 0 else first_row + 2 * WIDE), first_row + block + 2 * WIDE
        saves.append(
            pltpu.make_async_copy(hb.at[start:stop], hb_out.at[layer, start:stop], sem.at[1 + part])
        )
        saves[-1].start()
        lhs = jnp.concatenate([hb[first_row + i * WIDE : first_row + i * WIDE + block, :] for i in range(3)], axis=1)
        rows = slice(first_row, first_row + block)
        y[rows, :] = lax.dot_general(lhs, rhs, (((1,), (1,)), ((), ())), preferred_element_type=F32)
        for j in range(block // pair):
            rows = slice(first_row + j * pair, first_row + (j + 1) * pair)
            v = left_right(y[rows, 0:128], y[rows, 128:256], y[rows, 256:384])
            z[rows, :] = v
            summed = summed + fold(v)
    mean = jnp.sum(summed, axis=0, keepdims=True) / n_own
    apart = jnp.zeros((8, LANES), F32)
    for j in range(steps):
        rows = slice(j * pair, (j + 1) * pair)
        v = z[rows, :] - mean
        zc_out[rows, :] = v.astype(BF16)
        apart = apart + fold(jnp.square(v))
    sums = jnp.concatenate([mean, jnp.sum(apart, axis=0, keepdims=True)], axis=0)
    st_out[...] = sums
    edge_ref[...] = zc_out[pl.ds(edge_start(n_own, edge_out, r), edge_out), :]
    zc_out[n_own : n_own + edge_out, :] = jnp.zeros((edge_out, LANES), BF16)
    for save in saves:
        save.wait()


def fwd_step(layer, pool, edge_out, total, pos, slots, st, tables, weights, kept, n_own, ties):
    first = st is None
    layers = weights.shape[0]
    extra = () if first else (st, *tables)
    last = layer + 1 == layers
    kernels = pltpu.VMEM((LANES, 9 * CHANS), BF16)
    return pl.pallas_call(
        functools.partial(fwd_kernel, first, last, pool, layer, total, edge_out),
        out_shape=(
            pltpu.HBM((layers, n_own + 2 * WIDE, CHANS), BF16),
            pltpu.VMEM((n_own + edge_out, LANES), BF16),
            pltpu.VMEM((edge_out, LANES), BF16),
            pltpu.VMEM((2, LANES), F32),
            *((kernels,) if last else ()),
        ),
        in_specs=[SMEM] + [VMEM] * (1 + len(extra)) + [ANY] * (1 if first else 2) + [FREE] * len(ties),
        out_specs=(ANY, VMEM, VMEM, VMEM) + ((VMEM,) if last else ()),
        input_output_aliases={} if first else {3 + len(extra): 0},
        scratch_shapes=[
            pltpu.VMEM((n_own + 2 * WIDE, CHANS), BF16),
            *(() if last else (kernels,)),
            pltpu.VMEM((n_own, 3 * LANES), F32),
            pltpu.VMEM((n_own, LANES), F32),
            pltpu.VMEM((GROUPS, 8, LANES), F32),
            pltpu.VMEM((2 * WIDE, LANES), F32),
            pltpu.SemaphoreType.DMA((4,)),
        ],
        compiler_params=PARAMS,
        cost_estimate=pl.CostEstimate(
            flops=2 * n_own * 9 * CHANS * LANES, bytes_accessed=4 * 1024 * 1024, transcendentals=n_own * CHANS
        ),
        name="conv_forward",
    )(pos, slots, *extra, in_hbm(weights), *(() if first else (in_hbm(kept),)), *ties)


def below_kernel(layer, pool, total, top, *refs):
    pos, zc, st, gs = refs[:4]
    if top:
        terms, h_out, dn_out, msg, tab = refs[4:]
    else:
        terms, (dn_out, msg, tab) = refs[4:8], refs[-3:]
    n_own = dn_out.shape[0]
    rstd, own, oth = norm_tables(st, pos[0], pos[2], pos[3], float(n_own), total)
    tab[0:1], tab[1:2] = rstd, own
    tab[2:3], tab[3:4] = gs[layer : layer + 1, :], gs[layer + 8 : layer + 9, :]

    def body(j, accs):
        rows = pair_rows(j)
        xhat = zc[rows, :].astype(F32) * tab[0:1, :] + tab[1:2, :]
        n = xhat * tab[2:3, :] + tab[3:4, :]
        sig = sigmoid(n)
        h = n * sig
        if top:
            g = terms[rows, :].astype(F32)
            h_out[rows, :] = h.astype(BF16)
        else:
            g = functools.reduce(jnp.add, [term[rows, :].astype(F32) for term in terms])
        if pool:
            g = soft_pull(h, g)
        dn = g * (sig * (1.0 + n - h))
        dn_out[rows, :] = dn
        return accs[0] + fold(dn), accs[1] + fold(dn * xhat)

    zero = jnp.zeros((8, LANES), F32)
    sums = lax.fori_loop(0, n_own // (2 * WIDE), body, (zero, zero), unroll=3)
    sums = [jnp.sum(v, axis=0, keepdims=True) for v in sums]
    msg[0:WIDE, :] = dn_out[pl.ds(edge_start(n_own, WIDE, pos[1]), WIDE), :]
    msg[WIDE : WIDE + 8, :] = jnp.concatenate(sums + [jnp.zeros((6, LANES), F32)], axis=0)


def below_step(layer, pool, total, pos, zc, st, gs, terms, ties=()):
    n_own = terms[0].shape[0]
    top = len(terms) == 1
    out_shape = [
        pltpu.VMEM((n_own, LANES), F32),
        pltpu.VMEM((WIDE + 8, LANES), F32),
    ]
    if top:
        out_shape = [jax.ShapeDtypeStruct((n_own, LANES), BF16)] + out_shape
    return pl.pallas_call(
        functools.partial(below_kernel, layer, pool, total, top),
        out_shape=tuple(out_shape),
        in_specs=[SMEM] + [VMEM] * (3 + len(terms)) + [FREE] * len(ties),
        out_specs=(VMEM,) * len(out_shape),
        scratch_shapes=[pltpu.VMEM((8, LANES), F32)],
        compiler_params=PARAMS,
        cost_estimate=LITTLE,
        name="silu_backward",
    )(pos, zc, st, gs, *terms, *ties)


def bwd_kernel(layer, total, *refs):
    pos, dn, dedge, sums, zc, st, gs, w = refs[:8]
    outs, d_out, d, y, tab = refs[-8:-4], *refs[-4:]
    t, r = pos[0], pos[1]
    n_own = dn.shape[0]
    halo_at = pl.multiple_of((1 - r) * (n_own + WIDE), WIDE)
    zero_at = pl.multiple_of(r * (n_own + WIDE), WIDE)
    edge = zc.shape[0] - n_own
    d[pl.ds(zero_at, WIDE), :] = jnp.zeros((WIDE, 3 * LANES), BF16)
    rstd, own, oth = norm_tables(st, t, pos[2], pos[3], float(n_own), total)
    scale = gs[layer : layer + 1, :] * rstd
    shift_sum, gain_sum = sums[0:1, :], sums[1:2, :]
    slope = scale * gain_sum / total
    tab[0:1] = scale
    tab[1:2] = slope * rstd
    tab[2:3] = scale * shift_sum / total + slope * own
    tab[3:4] = scale * shift_sum / total + slope * oth

    def spread_columns(v):
        rows = v.shape[0]
        column = lax.broadcasted_iota(jnp.int32, v.shape, 0) % WIDE
        ahead = jnp.where(column == WIDE - 1, 0.0, pltpu.roll(v, rows - 1, 0))
        behind = jnp.where(column == 0, 0.0, pltpu.roll(v, 1, 0))
        return jnp.concatenate([ahead.astype(BF16), v.astype(BF16), behind.astype(BF16)], axis=1)

    near = n_own if edge == WIDE else pl.multiple_of(n_own + r * WIDE, WIDE)
    near = zc[pl.ds(near, WIDE), :].astype(F32)
    d[pl.ds(halo_at, WIDE), :] = spread_columns(dedge[0:WIDE, :] * tab[0:1, :] - tab[3:4, :] - near * tab[1:2, :])
    pair, block = 2 * WIDE, n_own // 3
    steps, made = n_own // pair, 0
    for part in range(3):
        first_row = part * block
        while made < min(steps, (first_row + block + WIDE + pair - 1) // pair):
            at = made * pair
            v = dn[at : at + pair, :] * tab[0:1, :] - tab[2:3, :] - zc[at : at + pair, :].astype(F32) * tab[1:2, :]
            v = spread_columns(v)
            d[at + WIDE : at + WIDE + pair, :] = v
            d_out[at : at + pair, :] = v
            made += 1
        if part == 0:
            rhs = jnp.concatenate([w[:, i * CHANS : (i + 1) * CHANS] for i in range(9)], axis=0)
        windows = [first_row + (2 - i) * WIDE for i in range(3)]
        lhs = jnp.concatenate([d[at : at + block, :] for at in windows], axis=1)
        y[first_row : first_row + block, :] = jnp.dot(lhs, rhs, preferred_element_type=F32)
        for j in range(block // pair):
            rows = slice(first_row + j * pair, first_row + (j + 1) * pair)
            for k in range(GROUPS):
                outs[k][rows, :] = y[rows, pl.ds(lane_of(t ^ k), LANES)].astype(BF16)


def bwd_step(layer, total, pos, dn, dedge, sums, zc, st, gs, w, ties):
    n_own = dn.shape[0]
    part = pltpu.VMEM((n_own, LANES), BF16)
    return pl.pallas_call(
        functools.partial(bwd_kernel, layer, total),
        out_shape=(part, part, part, part, pltpu.VMEM((n_own, 3 * LANES), BF16)),
        in_specs=[SMEM] + [VMEM] * 7 + [FREE] * len(ties),
        out_specs=(VMEM,) * 5,
        scratch_shapes=[
            pltpu.VMEM((n_own + 2 * WIDE, 3 * LANES), BF16),
            pltpu.VMEM((n_own, CHANS), F32),
            pltpu.VMEM((8, LANES), F32),
        ],
        compiler_params=PARAMS,
        cost_estimate=LITTLE,
        name="conv_backward",
    )(pos, dn, dedge, sums, zc, st, gs, pltpu.with_memory_space_constraint(w, pltpu.VMEM), *ties)


def last_kernel(t0, t1, t2, t3, *refs):
    out = refs[-1]

    def body(j, carry):
        rows = pair_rows(j)
        out[rows, :] = functools.reduce(jnp.add, [term[rows, :].astype(F32) for term in (t0, t1, t2, t3)])
        return carry

    lax.fori_loop(0, out.shape[0] // (2 * WIDE), body, 0)


def last_step(terms, ties):
    return pl.pallas_call(
        last_kernel,
        out_shape=jax.ShapeDtypeStruct(terms[0].shape, F32),
        in_specs=[VMEM] * 4 + [FREE] * len(ties),
        out_specs=VMEM,
        compiler_params=PARAMS,
        cost_estimate=LITTLE,
        name="add_terms",
    )(*terms, *ties)


def halves_kernel(keep, got, out, total, sem):
    total[...] = (keep[...].astype(F32) + got[...].astype(F32)).astype(BF16)
    save = pltpu.make_async_copy(total, out, sem)
    save.start()
    save.wait()


def add_halves(keep, got):
    return pl.pallas_call(
        halves_kernel,
        out_shape=pltpu.HBM(keep.shape, BF16),
        in_specs=[VMEM] * 2,
        out_specs=ANY,
        scratch_shapes=[pltpu.VMEM(keep.shape, BF16), pltpu.SemaphoreType.DMA],
        compiler_params=PARAMS,
        cost_estimate=LITTLE,
        name="add_halves",
    )(keep, got)


def wgrad_kernel(layer, pos, d, hb_hbm, *refs):
    if layer > 0:
        w_hbm, keep, send, w, hb, grad, sem = refs
        fetch = pltpu.make_async_copy(w_hbm.at[layer - 1], w, sem.at[1])
    else:
        keep, send, hb, grad, sem = refs
    load = pltpu.make_async_copy(hb_hbm.at[layer], hb, sem.at[0])
    load.start()
    if layer > 0:
        fetch.start()
    n_own = d.shape[0]
    lhs = d[...]
    load.wait()
    for i in range(3):
        part = lax.dot_general(
            lhs, hb[i * WIDE : i * WIDE + n_own, :], (((0,), (0,)), ((), ())), preferred_element_type=F32
        ).astype(BF16)
        for s in range(3):
            grad[:, (3 * i + s) * CHANS : (3 * i + s + 1) * CHANS] = part[s * LANES : (s + 1) * LANES]
    half = LANES // 2
    keep[...] = grad[pl.ds(pl.multiple_of(pos[1] * half, half), half), :]
    send[...] = grad[pl.ds(pl.multiple_of((1 - pos[1]) * half, half), half), :]
    if layer > 0:
        fetch.wait()


def wgrad_step(layer, pos, d, kept, weights):
    half = pltpu.VMEM((LANES // 2, 9 * CHANS), BF16)
    more = layer > 0
    return pl.pallas_call(
        functools.partial(wgrad_kernel, layer),
        out_shape=(half, half) + ((pltpu.VMEM((LANES, 9 * CHANS), BF16),) if more else ()),
        in_specs=[SMEM, VMEM, ANY] + ([ANY] if more else []),
        out_specs=(VMEM,) * (3 if more else 2),
        scratch_shapes=[
            pltpu.VMEM(kept.shape[1:], BF16),
            pltpu.VMEM((LANES, 9 * CHANS), BF16),
            pltpu.SemaphoreType.DMA((2,)),
        ],
        compiler_params=PARAMS,
        cost_estimate=LITTLE,
        name="kernel_gradient",
    )(pos, d, in_hbm(kept), *((in_hbm(weights),) if more else ()))


def place_kernel(layers, fresh, pos, *refs):
    count = 2 * len(layers)
    sources = refs[:count]
    out, held, wide, sem = refs[-4:]
    half = LANES // 2
    r = pos[1]
    loads = [pltpu.make_async_copy(sources[j], held.at[j], sem.at[j]) for j in range(count)]
    for load in loads:
        load.start()
    stores = []
    for j in range(count):
        at = pl.multiple_of((r if j % 2 == 0 else 1 - r) * half, half)
        if j >= 4:
            stores[j - 4].wait()
        loads[j].wait()
        wide[j % 4] = held[j].astype(F32)
        store = pltpu.make_async_copy(wide.at[j % 4], out.at[layers[j // 2], pl.ds(at, half)], sem.at[count + j])
        store.start()
        stores.append(store)
    for store in stores[-4:]:
        store.wait()


def place_step(layers, pos, sources, whole, count):
    half = LANES // 2
    jobs = len(sources)
    return pl.pallas_call(
        functools.partial(place_kernel, layers, whole is None),
        out_shape=pltpu.HBM((count, LANES, 9 * CHANS), F32),
        in_specs=[SMEM] + [FREE] * jobs + ([] if whole is None else [ANY]),
        out_specs=ANY,
        input_output_aliases={} if whole is None else {1 + jobs: 0},
        scratch_shapes=[
            pltpu.VMEM((jobs, half, 9 * CHANS), BF16),
            pltpu.VMEM((4, half, 9 * CHANS), F32),
            pltpu.SemaphoreType.DMA((2 * jobs,)),
        ],
        compiler_params=PARAMS,
        cost_estimate=LITTLE,
        name="place_gradients",
    )(pos, *sources, *(() if whole is None else (in_hbm(whole),)))


def swap_with(value, axis, k):
    return lax.ppermute(value, axis, [(i, i ^ k) for i in range(lax.axis_size(axis))])


def spread(own):
    return (own, *[swap_with(own, "tensor", k) for k in range(1, GROUPS)])


def share_moments(mine, count):
    other = swap_with(mine, "rows", 1)
    mean = 0.5 * (mine[0:1] + other[0:1])
    apart = mine[1:2] + other[1:2] + (0.5 * count) * jnp.square(other[0:1] - mine[0:1])
    own = jnp.concatenate([mean, apart], axis=0)
    all_four = [own] + [swap_with(own, "dp", k) for k in (1, 2, 3)]
    mean = 0.25 * functools.reduce(jnp.add, [v[0:1] for v in all_four])
    apart = functools.reduce(jnp.add, [v[1:2] + (2.0 * count) * jnp.square(v[0:1] - mean) for v in all_four])
    return jnp.concatenate([mean, apart, mine[0:1], other[0:1]], axis=0).reshape(2, 1, 2, LANES)


def halo_of_input(x, half):
    n_own = x.shape[0]
    edge = jnp.where(half == 0, x[n_own - WIDE :], x[:WIDE])
    return jnp.concatenate([x, swap_with(edge, "rows", 1)], axis=0)


def fast_local(section_input, conv_weights, norm_gains, norm_shifts, out_grad, out_mask):
    images, rows_here, width = out_mask.shape
    layers = conv_weights.shape[0]
    n_own = rows_here * width
    parts = lax.axis_size("dp") * lax.axis_size("rows")
    total = float(n_own * parts)
    t, half = lax.axis_index("tensor"), lax.axis_index("rows")
    image = lax.axis_index("dp")
    pos = jnp.stack([t, half, 2 * image + half, 2 * image + 1 - half]).astype(jnp.int32)
    middle = layers // 2
    x = to_maps(section_input, width).reshape(n_own, LANES)
    slots = lax.all_gather(halo_of_input(x, half), "tensor", axis=1, tiled=True)
    pad = jnp.zeros((8 - layers, LANES), F32)
    tables = spread(jnp.concatenate([norm_gains, pad, norm_shifts, pad], axis=0))
    top_grad = (to_maps(out_grad, width) * out_mask[..., None].astype(BF16)).reshape(n_own, LANES)

    st, kept = None, None
    halves = ("dp", "rows")
    kept_z, kept_st = [], []
    for layer in range(layers):
        last = layer + 1 == layers
        edge = 2 * WIDE if layer + 1 == middle else WIDE
        everyone = ("dp", "rows", "tensor")
        kept, zc, rim, local, *w = fwd_step(
            layer,
            layer == middle,
            edge,
            total,
            pos,
            slots,
            st,
            tables,
            conv_weights,
            kept,
            n_own,
            (top_grad,) if layer == 2 else (),
        )
        rim = swap_with(rim, "rows", 1)
        if last:
            st = share_moments(local, float(n_own))
        else:
            local = jnp.broadcast_to(local, (parts * GROUPS, 2, LANES))
            st = lax.all_to_all(local, everyone, split_axis=0, concat_axis=0, tiled=True)
            st = st.reshape(parts, GROUPS, 2, LANES)
        zc = lax.dynamic_update_slice_in_dim(zc, rim, n_own, axis=0)
        kept_z.append(zc)
        kept_st.append(st)
        if not last:
            slots = lax.all_gather(zc, "tensor", axis=1, tiled=True)
    top = layers - 1
    w = w[0]
    h_last, dn, msg = below_step(top, False, total, pos, kept_z[top], kept_st[top], tables[0], (top_grad,))

    def with_other(values):
        return [v for mine in values for v in (in_hbm(mine), swap_with(mine, "rows", 1))]

    sum_list, pairs = [None] * layers, [None] * layers
    ahead, back = [[0, 1, 3, 2]], [[2, 3, 1, 0]]
    urgent = ()
    for layer in range(layers - 1, -1, -1):
        got = swap_with(msg, "rows", 1)
        sums = msg[WIDE:] + got[WIDE:]
        one, two, three = (swap_with(sums, "dp", k) for k in (1, 2, 3))
        sums = (sums + one) + (two + three)
        sum_list[layer] = sums
        *terms, d = bwd_step(
            layer, total, pos, dn, got, sums, kept_z[layer], kept_st[layer], tables[0], w, urgent
        )
        terms = (terms[0], *[swap_with(terms[k], "tensor", k) for k in range(1, GROUPS)])
        keep, send, *w = wgrad_step(layer, pos, d, kept, conv_weights)
        w = w[0] if w else None
        other = swap_with(send, "rows", 1)
        pairs[layer] = add_halves(keep, other)
        urgent, settled = (other,), (() if layer + 1 == layers else (pairs[layer + 1],))
        if layer == 4:
            upper = lax.psum((pairs[5], pairs[4]), "dp", axis_index_groups=ahead)
        if layer == 2:
            mid = lax.psum((pairs[3], pairs[2]), "dp", axis_index_groups=back)
        if layer > 0:
            below = layer - 1
            late = (in_hbm(upper[0]),) if layer == 1 else ()
            dn, msg = below_step(
                below, layer == middle, total, pos, kept_z[below], kept_st[below], tables[0], terms, (keep, *settled, *late)
            )
        else:
            grad = last_step(terms, (pairs[0], pairs[1]))
    tied, upper = lax.optimization_barrier(((pairs[1], pairs[0]), upper))
    lower = lax.psum(tied, "dp", axis_index_groups=ahead)
    shape = (images, rows_here, width, LANES)
    grad, mid = lax.optimization_barrier((grad, mid))
    outputs = (from_maps(h_last.reshape(shape)), from_maps(grad.reshape(shape)))
    whole = place_step((5, 4, 3, 2), pos, with_other((*upper, *mid)), None, layers)
    sums = jnp.stack(sum_list)
    sums = (sums[:, 1], sums[:, 0])
    lower, whole, outputs, sums = lax.optimization_barrier((lower, whole, outputs, sums))
    whole = place_step((1, 0), pos, with_other(lower), whole, layers)
    return (*outputs, whole, *sums)


def solution(mesh):
    in_specs = (
        P("dp", "rows", "tensor"),
        P(None, "tensor", None),
        P(None, "tensor"),
        P(None, "tensor"),
        P("dp", "rows", "tensor"),
        P("dp", "rows", None),
    )
    out_specs = (
        P("dp", "rows", "tensor"),
        P("dp", "rows", "tensor"),
        P(None, "tensor", None),
        P(None, "tensor"),
        P(None, "tensor"),
    )
    local = fast_local if fits_kernels(mesh) else generic_local
    return jax.shard_map(local, mesh=mesh, in_specs=in_specs, out_specs=out_specs, check_vma=False)
```

```python
import functools

import jax
import jax.numpy as jnp
from jax import lax
from jax.experimental import pallas as pl
from jax.experimental.pallas import tpu as pltpu
from jax.sharding import PartitionSpec as P

EPS = 1e-05


def padded_2(cells, sides, width):
    for axis, dim in sides:
        count = lax.axis_size(axis)
        ends = count - 1
        head = lax.slice_in_dim(cells, 0, width, axis=dim)
        tail = lax.slice_in_dim(cells, cells.shape[dim] - width, cells.shape[dim], axis=dim)
        cells = jnp.concatenate(
            [
                lax.ppermute(tail, axis, [(i, (i + 1) % count) for i in range(ends)]),
                cells,
                lax.ppermute(head, axis, [((i + 1) % count, i) for i in range(ends)]),
            ],
            axis=dim,
        )
    return cells


def to_maps(flat, width):
    count, high, merged = flat.shape
    return flat.reshape(count, high, merged // width, width).transpose(0, 1, 3, 2)


def from_maps(maps):
    count, high, wide, chans = maps.shape
    return maps.transpose(0, 1, 3, 2).reshape(count, high, chans * wide)


def spatial_conv(padded, kernel):
    return lax.conv_general_dilated(
        padded,
        kernel,
        (1, 1),
        ((0, 0), (1, 1)),
        dimension_numbers=("NHWC", "HWIO", "NHWC"),
        preferred_element_type=jnp.float32,
    )


def flipped(kernel):
    return jnp.transpose(kernel[::-1, ::-1], (0, 1, 3, 2))


def pool_unpool(values):
    count, high, wide, chans = values.shape
    blocks = values.reshape(count, high // 2, 2, wide // 2, 2, chans)
    pooled = jax.nn.logsumexp(blocks, axis=(2, 4), keepdims=True)
    return (jnp.exp(blocks - pooled) * pooled).reshape(values.shape)


def moments(conv_out, total_pixels):
    summed = lax.psum(jnp.sum(conv_out, axis=(0, 1, 2)), ("dp", "rows"))
    mean = summed / total_pixels
    spread = lax.psum(jnp.sum(jnp.square(conv_out - mean), axis=(0, 1, 2)), ("dp", "rows"))
    var = spread / total_pixels
    return (mean, lax.rsqrt(var + EPS))


def kernel_grad(whole, dconv):
    images, rows_here, width, chans = dconv.shape
    widened = jnp.pad(whole, ((0, 0), (0, 0), (1, 1), (0, 0)))
    stacked = []
    for row_off in range(3):
        line = []
        for col_off in range(3):
            window = widened[:, row_off : row_off + rows_here, col_off : col_off + width, :]
            line.append(
                jnp.einsum("bhwc,bhwo->co", window, dconv, preferred_element_type=jnp.float32)
            )
        stacked.append(jnp.stack(line))
    return jnp.stack(stacked)


def generic_local(section_input, conv_weights, norm_gains, norm_shifts, out_grad, out_mask):
    width = out_mask.shape[2]
    images, rows_here = (out_mask.shape[0], out_mask.shape[1])
    total_pixels = float(images * rows_here * width * lax.axis_size("dp") * lax.axis_size("rows"))
    layers, out_here, flat_in = conv_weights.shape
    chans_in = flat_in // 9
    kernels_hwio = conv_weights.reshape(layers, out_here, 3, 3, chans_in).transpose(0, 2, 3, 4, 1)
    middle = layers // 2
    kept = []
    acting = to_maps(section_input, width)
    current = acting.astype(jnp.float32)
    pre_pool = current
    for index in range(layers):
        if index == middle:
            pre_pool = current
            acting = pool_unpool(pre_pool).astype(jnp.bfloat16)
        padded = padded_2(acting, (("rows", 1),), 1)
        whole = lax.all_gather(padded, "tensor", axis=3, tiled=True)
        conv_out = spatial_conv(whole, kernels_hwio[index])
        mean, rstd = moments(conv_out, total_pixels)
        normed = (conv_out - mean) * rstd
        shifted = normed * norm_gains[index] + norm_shifts[index]
        current = jax.nn.silu(shifted)
        acting = current.astype(jnp.bfloat16)
        kept.append((whole, normed, shifted, rstd))
    grad = to_maps(out_grad, width).astype(jnp.float32) * out_mask[..., None].astype(jnp.float32)
    kernel_list = [None] * layers
    gain_list = [None] * layers
    shift_list = [None] * layers
    for index in range(layers - 1, -1, -1):
        whole, normed, shifted, rstd = kept[index]
        unused, pull_silu = jax.vjp(jax.nn.silu, shifted)
        dshift = pull_silu(grad)[0]
        gain_sum, shift_sum = lax.psum(
            (jnp.sum(dshift * normed, axis=(0, 1, 2)), jnp.sum(dshift, axis=(0, 1, 2))),
            ("dp", "rows"),
        )
        gain_list[index] = gain_sum
        shift_list[index] = shift_sum
        dconv = (
            norm_gains[index]
            * rstd
            * (dshift - shift_sum / total_pixels - normed * gain_sum / total_pixels)
        ).astype(jnp.bfloat16)
        summed_kernel = lax.psum(
            kernel_grad(whole, dconv).astype(jnp.bfloat16), ("dp", "rows")
        ).astype(jnp.float32)
        kernel_list[index] = summed_kernel.transpose(3, 0, 1, 2).reshape(out_here, flat_in)
        grad_rim = padded_2(dconv, (("rows", 1),), 1)
        partial_terms = spatial_conv(grad_rim, flipped(kernels_hwio[index]))
        grad_in = lax.psum_scatter(
            partial_terms.astype(jnp.bfloat16), "tensor", scatter_dimension=3, tiled=True
        ).astype(jnp.float32)
        if index == middle:
            unused, pull_pool = jax.vjp(pool_unpool, pre_pool)
            grad = pull_pool(grad_in)[0]
        else:
            grad = grad_in
    return (
        from_maps(acting),
        from_maps(grad),
        jnp.stack(kernel_list),
        jnp.stack(gain_list),
        jnp.stack(shift_list),
    )


GROUPS = 4
LANES = 128
WIDE = 48
CHANS = GROUPS * LANES
F32 = jnp.float32
BF16 = jnp.bfloat16
VMEM = pl.BlockSpec(memory_space=pltpu.VMEM)
SMEM = pl.BlockSpec(memory_space=pltpu.SMEM)
ANY = pl.BlockSpec(memory_space=pltpu.HBM)
FREE = pl.BlockSpec(memory_space=pl.ANY)
LITTLE = pl.CostEstimate(flops=1024, bytes_accessed=1024, transcendentals=0)
PARAMS = pltpu.CompilerParams(vmem_limit_bytes=20 * 1024 * 1024)


def in_hbm(value):
    return pltpu.with_memory_space_constraint(value, pltpu.HBM)


def fits_kernels(mesh):
    return mesh.shape["tensor"] == GROUPS and mesh.shape["rows"] == 2 and mesh.shape["dp"] == 4


def sigmoid(v):
    return 0.5 * jnp.tanh(0.5 * v) + 0.5


def swap_columns(v):
    column = lax.broadcasted_iota(jnp.int32, v.shape, 0)
    return jnp.where(column % 2 == 0, pltpu.roll(v, WIDE - 1, 0), pltpu.roll(v, 1, 0))


def soft_parts(h):
    top = jnp.maximum(h[0], h[1])
    top = jnp.maximum(top, swap_columns(top))
    e0, e1 = jnp.exp(h[0] - top), jnp.exp(h[1] - top)
    total = e0 + e1
    total = total + swap_columns(total)
    pooled = top + jnp.log(total)
    inverse = 1.0 / total
    return e0 * inverse, e1 * inverse, pooled


def soft(h):
    h = h.reshape(2, WIDE, LANES)
    q0, q1, pooled = soft_parts(h)
    return jnp.concatenate([q0 * pooled, q1 * pooled], axis=0)


def soft_pull(h, grad):
    h = h.reshape(2, WIDE, LANES)
    grad = grad.reshape(2, WIDE, LANES)
    q0, q1, pooled = soft_parts(h)
    mix = q0 * grad[0] + q1 * grad[1]
    mix = mix + swap_columns(mix)
    return jnp.concatenate(
        [q0 * (pooled * (grad[0] - mix) + mix), q1 * (pooled * (grad[1] - mix) + mix)], axis=0
    )


def norm_tables(st, group, i_own, i_oth, n_local, total):
    parts = st.shape[0]
    if parts == 2:
        mean, rstd = st[0, 0, 0:1], lax.rsqrt(st[0, 0, 1:2] / total + EPS)
        return rstd, (st[1, 0, 0:1] - mean) * rstd, (st[1, 0, 1:2] - mean) * rstd
    group = 0 if st.shape[1] == 1 else group
    blocks = [st[i, group] for i in range(parts)]
    summed = functools.reduce(jnp.add, blocks)
    mean = summed[0:1] / parts
    apart = functools.reduce(jnp.add, [jnp.square(b - mean) for b in blocks])
    rstd = lax.rsqrt((summed[1:2] + n_local * apart[0:1]) / total + EPS)
    return rstd, (st[i_own, group, 0:1] - mean) * rstd, (st[i_oth, group, 0:1] - mean) * rstd


def left_right(y0, y1, y2):
    rows = y0.shape[0]
    column = lax.broadcasted_iota(jnp.int32, y0.shape, 0) % WIDE
    before = jnp.where(column == 0, 0.0, pltpu.roll(y0, 1, 0))
    after = jnp.where(column == WIDE - 1, 0.0, pltpu.roll(y2, rows - 1, 0))
    return before + y1 + after


def lane_of(group):
    return pl.multiple_of(group * LANES, LANES)


def edge_start(n_own, edge, half):
    return pl.multiple_of((1 - half) * (n_own - edge), WIDE)


def pair_rows(j):
    return pl.ds(pl.multiple_of(j * 2 * WIDE, 2 * WIDE), 2 * WIDE)


def fold(v):
    return jnp.sum(v.reshape(v.shape[0] // 8, 8, LANES), axis=0)


def fwd_kernel(first, last, pool, layer, total, edge_out, *refs):
    pos, zall = refs[0], refs[1]
    if first:
        w_hbm = refs[2]
    else:
        st, gss, w_hbm = refs[2], refs[3:7], refs[7]
    if last:
        hb_out, zc_out, edge_ref, st_out, w, hb, y, z, tab, hs, sem = refs[-11:]
    else:
        hb_out, zc_out, edge_ref, st_out, hb, w, y, z, tab, hs, sem = refs[-11:]
    load = pltpu.make_async_copy(w_hbm.at[layer], w, sem.at[0])
    load.start()
    saves = []
    t, r = pos[0], pos[1]
    n_own = z.shape[0]
    halo_at = pl.multiple_of((1 - r) * (n_own + WIDE), WIDE)
    zero_at = pl.multiple_of(r * (n_own + WIDE), WIDE)
    hb[pl.ds(zero_at, WIDE), :] = jnp.zeros((WIDE, CHANS), BF16)
    edge = zall.shape[0] - n_own
    if not first:
        for k in range(GROUPS):
            group = t ^ k
            rstd, own, oth = norm_tables(st, group, pos[2], pos[3], float(n_own), total)
            gain, shift = gss[k][layer - 1 : layer, :], gss[k][layer + 7 : layer + 8, :]
            tab[group, 0:1] = rstd * gain
            tab[group, 1:2] = own * gain + shift
            tab[group, 2:3] = oth * gain + shift

    def act(values, group, which):
        if first:
            return values
        n = values.astype(F32) * tab[group, 0:1, :] + tab[group, which : which + 1, :]
        h = n * sigmoid(n)
        return soft(h) if pool else h

    for group in range(GROUPS):
        lanes = slice(group * LANES, (group + 1) * LANES)
        h = act(zall[n_own : n_own + edge, lanes], group, 2)
        if edge > WIDE:
            hs[...] = h
            h = hs[pl.ds(pl.multiple_of(r * WIDE, WIDE), WIDE), :]
        hb[pl.ds(halo_at, WIDE), lanes] = h.astype(BF16)
    pair, block = 2 * WIDE, n_own // 3
    steps, made = n_own // pair, 0
    summed = jnp.zeros((8, LANES), F32)
    for part in range(3):
        first_row = part * block
        while made < min(steps, (first_row + block + WIDE + pair - 1) // pair):
            at = made * pair
            for group in range(GROUPS):
                lanes = slice(group * LANES, (group + 1) * LANES)
                h = act(zall[at : at + pair, lanes], group, 1)
                hb[at + WIDE : at + WIDE + pair, lanes] = h.astype(BF16)
            made += 1
        if part == 0:
            load.wait()
            rhs = jnp.concatenate(
                [
                    jnp.concatenate([w[:, (3 * i + s) * CHANS : (3 * i + s + 1) * CHANS] for i in range(3)], axis=1)
                    for s in range(3)
                ],
                axis=0,
            )
        start, stop = (0 if part == 0 else first_row + 2 * WIDE), first_row + block + 2 * WIDE
        saves.append(
            pltpu.make_async_copy(hb.at[start:stop], hb_out.at[layer, start:stop], sem.at[1 + part])
        )
        saves[-1].start()
        lhs = jnp.concatenate([hb[first_row + i * WIDE : first_row + i * WIDE + block, :] for i in range(3)], axis=1)
        rows = slice(first_row, first_row + block)
        y[rows, :] = lax.dot_general(lhs, rhs, (((1,), (1,)), ((), ())), preferred_element_type=F32)
        for j in range(block // pair):
            rows = slice(first_row + j * pair, first_row + (j + 1) * pair)
            v = left_right(y[rows, 0:128], y[rows, 128:256], y[rows, 256:384])
            z[rows, :] = v
            summed = summed + fold(v)
    mean = jnp.sum(summed, axis=0, keepdims=True) / n_own
    apart = jnp.zeros((8, LANES), F32)
    for j in range(steps):
        rows = slice(j * pair, (j + 1) * pair)
        v = z[rows, :] - mean
        zc_out[rows, :] = v.astype(BF16)
        apart = apart + fold(jnp.square(v))
    sums = jnp.concatenate([mean, jnp.sum(apart, axis=0, keepdims=True)], axis=0)
    st_out[...] = sums
    edge_ref[...] = zc_out[pl.ds(edge_start(n_own, edge_out, r), edge_out), :]
    zc_out[n_own : n_own + edge_out, :] = jnp.zeros((edge_out, LANES), BF16)
    for save in saves:
        save.wait()


def fwd_step(layer, pool, edge_out, total, pos, slots, st, tables, weights, kept, n_own, ties):
    first = st is None
    layers = weights.shape[0]
    extra = () if first else (st, *tables)
    last = layer + 1 == layers
    kernels = pltpu.VMEM((LANES, 9 * CHANS), BF16)
    return pl.pallas_call(
        functools.partial(fwd_kernel, first, last, pool, layer, total, edge_out),
        out_shape=(
            pltpu.HBM((layers, n_own + 2 * WIDE, CHANS), BF16),
            pltpu.VMEM((n_own + edge_out, LANES), BF16),
            pltpu.VMEM((edge_out, LANES), BF16),
            pltpu.VMEM((2, LANES), F32),
            *((kernels,) if last else ()),
        ),
        in_specs=[SMEM] + [VMEM] * (1 + len(extra)) + [ANY] * (1 if first else 2) + [FREE] * len(ties),
        out_specs=(ANY, VMEM, VMEM, VMEM) + ((VMEM,) if last else ()),
        input_output_aliases={} if first else {3 + len(extra): 0},
        scratch_shapes=[
            pltpu.VMEM((n_own + 2 * WIDE, CHANS), BF16),
            *(() if last else (kernels,)),
            pltpu.VMEM((n_own, 3 * LANES), F32),
            pltpu.VMEM((n_own, LANES), F32),
            pltpu.VMEM((GROUPS, 8, LANES), F32),
            pltpu.VMEM((2 * WIDE, LANES), F32),
            pltpu.SemaphoreType.DMA((4,)),
        ],
        compiler_params=PARAMS,
        cost_estimate=pl.CostEstimate(
            flops=2 * n_own * 9 * CHANS * LANES, bytes_accessed=4 * 1024 * 1024, transcendentals=n_own * CHANS
        ),
        name="conv_forward",
    )(pos, slots, *extra, in_hbm(weights), *(() if first else (in_hbm(kept),)), *ties)


def below_kernel(layer, pool, total, top, *refs):
    pos, zc, st, gs = refs[:4]
    if top:
        terms, h_out, dn_out, msg, tab = refs[4:]
    else:
        terms, (dn_out, msg, tab) = refs[4:8], refs[-3:]
    n_own = dn_out.shape[0]
    rstd, own, oth = norm_tables(st, pos[0], pos[2], pos[3], float(n_own), total)
    tab[0:1], tab[1:2] = rstd, own
    tab[2:3], tab[3:4] = gs[layer : layer + 1, :], gs[layer + 8 : layer + 9, :]

    def body(j, accs):
        rows = pair_rows(j)
        xhat = zc[rows, :].astype(F32) * tab[0:1, :] + tab[1:2, :]
        n = xhat * tab[2:3, :] + tab[3:4, :]
        sig = sigmoid(n)
        h = n * sig
        if top:
            g = terms[rows, :].astype(F32)
            h_out[rows, :] = h.astype(BF16)
        else:
            g = functools.reduce(jnp.add, [term[rows, :].astype(F32) for term in terms])
        if pool:
            g = soft_pull(h, g)
        dn = g * (sig * (1.0 + n - h))
        dn_out[rows, :] = dn
        return accs[0] + fold(dn), accs[1] + fold(dn * xhat)

    zero = jnp.zeros((8, LANES), F32)
    sums = lax.fori_loop(0, n_own // (2 * WIDE), body, (zero, zero), unroll=3)
    sums = [jnp.sum(v, axis=0, keepdims=True) for v in sums]
    msg[0:WIDE, :] = dn_out[pl.ds(edge_start(n_own, WIDE, pos[1]), WIDE), :]
    msg[WIDE : WIDE + 8, :] = jnp.concatenate(sums + [jnp.zeros((6, LANES), F32)], axis=0)


def below_step(layer, pool, total, pos, zc, st, gs, terms, ties=()):
    n_own = terms[0].shape[0]
    top = len(terms) == 1
    out_shape = [
        pltpu.VMEM((n_own, LANES), F32),
        pltpu.VMEM((WIDE + 8, LANES), F32),
    ]
    if top:
        out_shape = [jax.ShapeDtypeStruct((n_own, LANES), BF16)] + out_shape
    return pl.pallas_call(
        functools.partial(below_kernel, layer, pool, total, top),
        out_shape=tuple(out_shape),
        in_specs=[SMEM] + [VMEM] * (3 + len(terms)) + [FREE] * len(ties),
        out_specs=(VMEM,) * len(out_shape),
        scratch_shapes=[pltpu.VMEM((8, LANES), F32)],
        compiler_params=PARAMS,
        cost_estimate=LITTLE,
        name="silu_backward",
    )(pos, zc, st, gs, *terms, *ties)


def bwd_kernel(layer, total, *refs):
    pos, dn, dedge, sums, zc, st, gs, w = refs[:8]
    outs, d_out, d, y, tab = refs[-8:-4], *refs[-4:]
    t, r = pos[0], pos[1]
    n_own = dn.shape[0]
    halo_at = pl.multiple_of((1 - r) * (n_own + WIDE), WIDE)
    zero_at = pl.multiple_of(r * (n_own + WIDE), WIDE)
    edge = zc.shape[0] - n_own
    d[pl.ds(zero_at, WIDE), :] = jnp.zeros((WIDE, 3 * LANES), BF16)
    rstd, own, oth = norm_tables(st, t, pos[2], pos[3], float(n_own), total)
    scale = gs[layer : layer + 1, :] * rstd
    shift_sum, gain_sum = sums[0:1, :], sums[1:2, :]
    slope = scale * gain_sum / total
    tab[0:1] = scale
    tab[1:2] = slope * rstd
    tab[2:3] = scale * shift_sum / total + slope * own
    tab[3:4] = scale * shift_sum / total + slope * oth

    def spread_columns(v):
        rows = v.shape[0]
        column = lax.broadcasted_iota(jnp.int32, v.shape, 0) % WIDE
        ahead = jnp.where(column == WIDE - 1, 0.0, pltpu.roll(v, rows - 1, 0))
        behind = jnp.where(column == 0, 0.0, pltpu.roll(v, 1, 0))
        return jnp.concatenate([ahead.astype(BF16), v.astype(BF16), behind.astype(BF16)], axis=1)

    near = n_own if edge == WIDE else pl.multiple_of(n_own + r * WIDE, WIDE)
    near = zc[pl.ds(near, WIDE), :].astype(F32)
    d[pl.ds(halo_at, WIDE), :] = spread_columns(dedge[0:WIDE, :] * tab[0:1, :] - tab[3:4, :] - near * tab[1:2, :])
    pair, block = 2 * WIDE, n_own // 3
    steps, made = n_own // pair, 0
    for part in range(3):
        first_row = part * block
        while made < min(steps, (first_row + block + WIDE + pair - 1) // pair):
            at = made * pair
            v = dn[at : at + pair, :] * tab[0:1, :] - tab[2:3, :] - zc[at : at + pair, :].astype(F32) * tab[1:2, :]
            v = spread_columns(v)
            d[at + WIDE : at + WIDE + pair, :] = v
            d_out[at : at + pair, :] = v
            made += 1
        if part == 0:
            rhs = jnp.concatenate([w[:, i * CHANS : (i + 1) * CHANS] for i in range(9)], axis=0)
        windows = [first_row + (2 - i) * WIDE for i in range(3)]
        lhs = jnp.concatenate([d[at : at + block, :] for at in windows], axis=1)
        y[first_row : first_row + block, :] = jnp.dot(lhs, rhs, preferred_element_type=F32)
        for j in range(block // pair):
            rows = slice(first_row + j * pair, first_row + (j + 1) * pair)
            for k in range(GROUPS):
                outs[k][rows, :] = y[rows, pl.ds(lane_of(t ^ k), LANES)].astype(BF16)


def bwd_step(layer, total, pos, dn, dedge, sums, zc, st, gs, w, ties):
    n_own = dn.shape[0]
    part = pltpu.VMEM((n_own, LANES), BF16)
    return pl.pallas_call(
        functools.partial(bwd_kernel, layer, total),
        out_shape=(part, part, part, part, pltpu.VMEM((n_own, 3 * LANES), BF16)),
        in_specs=[SMEM] + [VMEM] * 7 + [FREE] * len(ties),
        out_specs=(VMEM,) * 5,
        scratch_shapes=[
            pltpu.VMEM((n_own + 2 * WIDE, 3 * LANES), BF16),
            pltpu.VMEM((n_own, CHANS), F32),
            pltpu.VMEM((8, LANES), F32),
        ],
        compiler_params=PARAMS,
        cost_estimate=LITTLE,
        name="conv_backward",
    )(pos, dn, dedge, sums, zc, st, gs, pltpu.with_memory_space_constraint(w, pltpu.VMEM), *ties)


def last_kernel(t0, t1, t2, t3, *refs):
    out = refs[-1]

    def body(j, carry):
        rows = pair_rows(j)
        out[rows, :] = functools.reduce(jnp.add, [term[rows, :].astype(F32) for term in (t0, t1, t2, t3)])
        return carry

    lax.fori_loop(0, out.shape[0] // (2 * WIDE), body, 0)


def last_step(terms, ties):
    return pl.pallas_call(
        last_kernel,
        out_shape=jax.ShapeDtypeStruct(terms[0].shape, F32),
        in_specs=[VMEM] * 4 + [FREE] * len(ties),
        out_specs=VMEM,
        compiler_params=PARAMS,
        cost_estimate=LITTLE,
        name="add_terms",
    )(*terms, *ties)


def halves_kernel(keep, got, out, total, sem):
    total[...] = (keep[...].astype(F32) + got[...].astype(F32)).astype(BF16)
    save = pltpu.make_async_copy(total, out, sem)
    save.start()
    save.wait()


def add_halves(keep, got):
    return pl.pallas_call(
        halves_kernel,
        out_shape=pltpu.HBM(keep.shape, BF16),
        in_specs=[VMEM] * 2,
        out_specs=ANY,
        scratch_shapes=[pltpu.VMEM(keep.shape, BF16), pltpu.SemaphoreType.DMA],
        compiler_params=PARAMS,
        cost_estimate=LITTLE,
        name="add_halves",
    )(keep, got)


def wgrad_kernel(layer, pos, d, hb_hbm, *refs):
    if layer > 0:
        w_hbm, keep, send, w, hb, grad, sem = refs
        fetch = pltpu.make_async_copy(w_hbm.at[layer - 1], w, sem.at[1])
    else:
        keep, send, hb, grad, sem = refs
    load = pltpu.make_async_copy(hb_hbm.at[layer], hb, sem.at[0])
    load.start()
    if layer > 0:
        fetch.start()
    n_own = d.shape[0]
    lhs = d[...]
    load.wait()
    for i in range(3):
        part = lax.dot_general(
            lhs, hb[i * WIDE : i * WIDE + n_own, :], (((0,), (0,)), ((), ())), preferred_element_type=F32
        ).astype(BF16)
        for s in range(3):
            grad[:, (3 * i + s) * CHANS : (3 * i + s + 1) * CHANS] = part[s * LANES : (s + 1) * LANES]
    half = LANES // 2
    keep[...] = grad[pl.ds(pl.multiple_of(pos[1] * half, half), half), :]
    send[...] = grad[pl.ds(pl.multiple_of((1 - pos[1]) * half, half), half), :]
    if layer > 0:
        fetch.wait()


def wgrad_step(layer, pos, d, kept, weights):
    half = pltpu.VMEM((LANES // 2, 9 * CHANS), BF16)
    more = layer > 0
    return pl.pallas_call(
        functools.partial(wgrad_kernel, layer),
        out_shape=(half, half) + ((pltpu.VMEM((LANES, 9 * CHANS), BF16),) if more else ()),
        in_specs=[SMEM, VMEM, ANY] + ([ANY] if more else []),
        out_specs=(VMEM,) * (3 if more else 2),
        scratch_shapes=[
            pltpu.VMEM(kept.shape[1:], BF16),
            pltpu.VMEM((LANES, 9 * CHANS), BF16),
            pltpu.SemaphoreType.DMA((2,)),
        ],
        compiler_params=PARAMS,
        cost_estimate=LITTLE,
        name="kernel_gradient",
    )(pos, d, in_hbm(kept), *((in_hbm(weights),) if more else ()))


def place_kernel(layers, fresh, pos, *refs):
    count = 2 * len(layers)
    sources = refs[:count]
    out, held, wide, sem = refs[-4:]
    half = LANES // 2
    r = pos[1]
    loads = [pltpu.make_async_copy(sources[j], held.at[j], sem.at[j]) for j in range(count)]
    for load in loads:
        load.start()
    stores = []
    for j in range(count):
        at = pl.multiple_of((r if j % 2 == 0 else 1 - r) * half, half)
        if j >= 4:
            stores[j - 4].wait()
        loads[j].wait()
        wide[j % 4] = held[j].astype(F32)
        store = pltpu.make_async_copy(wide.at[j % 4], out.at[layers[j // 2], pl.ds(at, half)], sem.at[count + j])
        store.start()
        stores.append(store)
    for store in stores[-4:]:
        store.wait()


def place_step(layers, pos, sources, whole, count):
    half = LANES // 2
    jobs = len(sources)
    return pl.pallas_call(
        functools.partial(place_kernel, layers, whole is None),
        out_shape=pltpu.HBM((count, LANES, 9 * CHANS), F32),
        in_specs=[SMEM] + [FREE] * jobs + ([] if whole is None else [ANY]),
        out_specs=ANY,
        input_output_aliases={} if whole is None else {1 + jobs: 0},
        scratch_shapes=[
            pltpu.VMEM((jobs, half, 9 * CHANS), BF16),
            pltpu.VMEM((4, half, 9 * CHANS), F32),
            pltpu.SemaphoreType.DMA((2 * jobs,)),
        ],
        compiler_params=PARAMS,
        cost_estimate=LITTLE,
        name="place_gradients",
    )(pos, *sources, *(() if whole is None else (in_hbm(whole),)))


def swap_with(value, axis, k):
    return lax.ppermute(value, axis, [(i, i ^ k) for i in range(lax.axis_size(axis))])


def spread(own):
    return (own, *[swap_with(own, "tensor", k) for k in range(1, GROUPS)])


def share_moments(mine, count):
    other = swap_with(mine, "rows", 1)
    mean = 0.5 * (mine[0:1] + other[0:1])
    apart = mine[1:2] + other[1:2] + (0.5 * count) * jnp.square(other[0:1] - mine[0:1])
    own = jnp.concatenate([mean, apart], axis=0)
    all_four = [own] + [swap_with(own, "dp", k) for k in (1, 2, 3)]
    mean = 0.25 * functools.reduce(jnp.add, [v[0:1] for v in all_four])
    apart = functools.reduce(jnp.add, [v[1:2] + (2.0 * count) * jnp.square(v[0:1] - mean) for v in all_four])
    return jnp.concatenate([mean, apart, mine[0:1], other[0:1]], axis=0).reshape(2, 1, 2, LANES)


def halo_of_input(x, half):
    n_own = x.shape[0]
    edge = jnp.where(half == 0, x[n_own - WIDE :], x[:WIDE])
    return jnp.concatenate([x, swap_with(edge, "rows", 1)], axis=0)


def fast_local(section_input, conv_weights, norm_gains, norm_shifts, out_grad, out_mask):
    images, rows_here, width = out_mask.shape
    layers = conv_weights.shape[0]
    n_own = rows_here * width
    parts = lax.axis_size("dp") * lax.axis_size("rows")
    total = float(n_own * parts)
    t, half = lax.axis_index("tensor"), lax.axis_index("rows")
    image = lax.axis_index("dp")
    pos = jnp.stack([t, half, 2 * image + half, 2 * image + 1 - half]).astype(jnp.int32)
    middle = layers // 2
    x = to_maps(section_input, width).reshape(n_own, LANES)
    slots = lax.all_gather(halo_of_input(x, half), "tensor", axis=1, tiled=True)
    pad = jnp.zeros((8 - layers, LANES), F32)
    tables = spread(jnp.concatenate([norm_gains, pad, norm_shifts, pad], axis=0))
    top_grad = (to_maps(out_grad, width) * out_mask[..., None].astype(BF16)).reshape(n_own, LANES)

    st, kept = None, None
    halves = ("dp", "rows")
    kept_z, kept_st = [], []
    for layer in range(layers):
        last = layer + 1 == layers
        edge = 2 * WIDE if layer + 1 == middle else WIDE
        everyone = ("dp", "rows", "tensor")
        kept, zc, rim, local, *w = fwd_step(
            layer,
            layer == middle,
            edge,
            total,
            pos,
            slots,
            st,
            tables,
            conv_weights,
            kept,
            n_own,
            (top_grad,) if layer == 2 else (),
        )
        rim = swap_with(rim, "rows", 1)
        if last:
            st = share_moments(local, float(n_own))
        else:
            local = jnp.broadcast_to(local, (parts * GROUPS, 2, LANES))
            st = lax.all_to_all(local, everyone, split_axis=0, concat_axis=0, tiled=True)
            st = st.reshape(parts, GROUPS, 2, LANES)
        zc = lax.dynamic_update_slice_in_dim(zc, rim, n_own, axis=0)
        kept_z.append(zc)
        kept_st.append(st)
        if not last:
            slots = lax.all_gather(zc, "tensor", axis=1, tiled=True)
    top = layers - 1
    w = w[0]
    h_last, dn, msg = below_step(top, False, total, pos, kept_z[top], kept_st[top], tables[0], (top_grad,))

    def with_other(values):
        return [v for mine in values for v in (in_hbm(mine), swap_with(mine, "rows", 1))]

    sum_list, pairs = [None] * layers, [None] * layers
    ahead, back = [[0, 1, 3, 2]], [[2, 3, 1, 0]]
    urgent = ()
    for layer in range(layers - 1, -1, -1):
        got = swap_with(msg, "rows", 1)
        sums = msg[WIDE:] + got[WIDE:]
        one, two, three = (swap_with(sums, "dp", k) for k in (1, 2, 3))
        sums = (sums + one) + (two + three)
        sum_list[layer] = sums
        *terms, d = bwd_step(
            layer, total, pos, dn, got, sums, kept_z[layer], kept_st[layer], tables[0], w, urgent
        )
        terms = (terms[0], *[swap_with(terms[k], "tensor", k) for k in range(1, GROUPS)])
        keep, send, *w = wgrad_step(layer, pos, d, kept, conv_weights)
        w = w[0] if w else None
        other = swap_with(send, "rows", 1)
        pairs[layer] = add_halves(keep, other)
        urgent, settled = (other,), (() if layer + 1 == layers else (in_hbm(pairs[layer + 1]),))
        if layer == 4:
            upper = lax.psum((pairs[5], pairs[4]), "dp", axis_index_groups=ahead)
        if layer == 2:
            mid = lax.psum((pairs[3], pairs[2]), "dp", axis_index_groups=back)
        if layer > 0:
            below = layer - 1
            late = (in_hbm(upper[0]),) if layer == 1 else ()
            dn, msg = below_step(
                below, layer == middle, total, pos, kept_z[below], kept_st[below], tables[0], terms, (keep, *settled, *late)
            )
        else:
            grad = last_step(terms, (in_hbm(pairs[0]), in_hbm(pairs[1])))
    tied, upper = lax.optimization_barrier(((pairs[1], pairs[0]), upper))
    lower = lax.psum(tied, "dp", axis_index_groups=ahead)
    shape = (images, rows_here, width, LANES)
    grad, mid = lax.optimization_barrier((grad, mid))
    outputs = (from_maps(h_last.reshape(shape)), from_maps(grad.reshape(shape)))
    whole = place_step((5, 4, 3, 2), pos, with_other((*upper, *mid)), None, layers)
    sums = jnp.stack(sum_list)
    sums = (sums[:, 1], sums[:, 0])
    lower, whole, outputs, sums = lax.optimization_barrier((lower, whole, outputs, sums))
    whole = place_step((1, 0), pos, with_other(lower), whole, layers)
    return (*outputs, whole, *sums)


def solution(mesh):
    in_specs = (
        P("dp", "rows", "tensor"),
        P(None, "tensor", None),
        P(None, "tensor"),
        P(None, "tensor"),
        P("dp", "rows", "tensor"),
        P("dp", "rows", None),
    )
    out_specs = (
        P("dp", "rows", "tensor"),
        P("dp", "rows", "tensor"),
        P(None, "tensor", None),
        P(None, "tensor"),
        P(None, "tensor"),
    )
    local = fast_local if fits_kernels(mesh) else generic_local
    return jax.shard_map(local, mesh=mesh, in_specs=in_specs, out_specs=out_specs, check_vma=False)
```
